32 devices in a mesh: rows: 8 (over z, core), seq: 4 (over y, x).
Axes of the slice: x: 2, y: 2, z: 4, core: 2. Of those that a mesh axis runs over, the one named last changes fastest.
Arguments:
- tokens: bfloat16 [16, 1024, 1152], P('rows', 'seq'), may hold values from -6 to 6
- conditioning: bfloat16 [128, 1152], P('rows'), may hold values from -6 to 6
- segment_ids: int32 [16, 1024], P('rows'), may hold values from 0 to 7, as said below
- image_index: int32 [16, 8], P('rows'), may hold values from 0 to 15
- row_fill: int32 [16], P('rows'), may hold values from 512 to 1024, as said below
- ada_weight: bfloat16 [1152, 6912], P(None, 'seq'), may hold values from -0.1875 to 0.1875
- ada_bias: bfloat16 [6912], replicated, may hold values from -1.796875 to 1.796875
- qkv_weight: bfloat16 [1152, 3456], replicated, may hold values from -0.1875 to 0.1875
- qv_bias: bfloat16 [2, 1152], replicated, may hold values from -1.796875 to 1.796875
- proj_weight: bfloat16 [1152, 1152], replicated, may hold values from -2 to 2
- proj_bias: bfloat16 [1152], replicated, may hold values from -1.796875 to 1.796875
- up_weight: bfloat16 [1152, 4608], replicated, may hold values from -0.1875 to 0.1875
- up_bias: bfloat16 [4608], replicated, may hold values from -1.796875 to 1.796875
- down_weight: bfloat16 [4608, 1152], replicated, may hold values from -0.09375 to 0.09375
- down_bias: bfloat16 [1152], replicated, may hold values from -1.796875 to 1.796875
- cotangent: bfloat16 [16, 1024, 1152], P('rows', 'seq'), may hold values from -6 to 6
Outputs:
- block_out: bfloat16 [16, 1024, 1152], P('rows', 'seq')
- grad_tokens: float32 [16, 1024, 1152], P('rows', 'seq')
- grad_cond: float32 [128, 1152], P('rows')
- grad_ada_weight: float32 [1152, 6912], P('rows', 'seq')
- grad_ada_bias: float32 [6912], replicated
- grad_qkv_weight: float32 [1152, 3456], P('rows', 'seq')
- grad_qv_bias: float32 [2, 1152], replicated
- grad_proj_weight: float32 [1152, 1152], P('rows', 'seq')
- grad_proj_bias: float32 [1152], replicated
- grad_up_weight: float32 [1152, 4608], P('rows', 'seq')
- grad_up_bias: float32 [4608], replicated
- grad_down_weight: float32 [4608, 1152], P('rows', 'seq')
- grad_down_bias: float32 [1152], replicated
The draws below stay inside these ranges and needn't reach their ends.
Inputs may be any that keep to these rules, and one draw needn't show every extreme that they name: `segment_ids`: never falls along a row; in every aligned block of 2 rows one row has a segment that holds every position from 1024 // (2 * 4) to 1024 - 1024 // (2 * 4). `row_fill`: that row's fill is above 1024 - 1024 // (2 * 4).
All inputs are finite; a program needn't handle non-finite values.
Results may differ from the reference program's by a relative error of at most 0.012.
The reference program's roundings to bfloat16 on the way count: a program that leaves them out, or rounds other values in their place, can miss the bound.
Values may be sent and summed in bfloat16 or wider, within the bound.
A program may use at most 256 MiB of HBM per device.

```python
import jax
import jax.numpy as jnp
from jax import lax

D = 1152
HEADS = 16
FF = 4608
ROW_LEN = 1024
SEGS = 8
ROWS_DEV = 2
ROWS = 16
IMG_DEV = 16
IMAGES = 128
N_SEQ = 4


def long_rows(key):
    chosen = jax.random.randint(key, (ROWS // ROWS_DEV,), 0, ROWS_DEV)
    row_ids = jnp.arange(ROWS)
    return row_ids % ROWS_DEV == chosen[row_ids // ROWS_DEV]


def edge_width():
    return max(ROW_LEN // (2 * N_SEQ), 1)


def draw_segment_ids(key, part):
    single = long_rows(key)
    key = jax.random.fold_in(key, 11)
    free_key, chosen_key, lower_key, upper_key = jax.random.split(key, 4)
    boundary = jax.random.randint(free_key, (ROWS, SEGS - 1), 1, ROW_LEN)
    edge = edge_width()
    chosen_seg = jax.random.randint(chosen_key, (ROWS, 1), 0, SEGS)
    lower = jax.random.randint(lower_key, (ROWS, SEGS - 1), 1, edge + 1)
    upper = jax.random.randint(upper_key, (ROWS, SEGS - 1), ROW_LEN - edge + 1, ROW_LEN + 1)
    slot_ids = jnp.arange(SEGS - 1)[None, :]
    long_boundary = jnp.where(slot_ids < chosen_seg, lower, upper)
    boundary = jnp.where(single[:, None], long_boundary, boundary)
    positions = jnp.arange(ROW_LEN)
    return jnp.sum((boundary[:, None, :] <= positions[None, :, None]).astype(jnp.int32), axis=-1).astype(jnp.int32)


def draw_row_fill(key, part):
    single = long_rows(key)
    key = jax.random.fold_in(key, 12)
    free_key, long_key = jax.random.split(key)
    edge = edge_width()
    filled = jax.random.randint(free_key, (ROWS,), ROW_LEN // 2, ROW_LEN + 1)
    long_fill = jax.random.randint(long_key, (ROWS,), ROW_LEN - edge + 1, ROW_LEN + 1)
    return jnp.where(single, long_fill, filled).astype(jnp.int32)


def with_ends(drawn, rng, low, largest):
    index_at = [jax.random.randint(jax.random.fold_in(rng, axis), (), 0, length) for axis, length in enumerate(drawn.shape)]
    widest = drawn.shape.index(max(drawn.shape))
    next_to = index_at[:widest] + [(index_at[widest] + 1) % drawn.shape[widest]] + index_at[widest + 1:]
    return drawn.at[tuple(index_at)].set(low).at[tuple(next_to)].set(largest)


def level_of(stream_key, shape, cuts, least, largest):
    factor_of, own = 1.0, jax.random.fold_in(stream_key, 6)
    for position, parts in cuts:
        draws = jnp.exp(jax.random.uniform(jax.random.fold_in(own, position), (parts,), jnp.float32, least / len(cuts), largest / len(cuts)))
        factor_of = factor_of * jnp.repeat(draws, shape[position] // parts).reshape([-1 if axis == position else 1 for axis in range(len(shape))])
    return factor_of


def bell_draw(key, shape, scale, bound, cuts=(), held_as=jnp.bfloat16):
    level = level_of(key, shape, cuts, -0.22, 0.18) if cuts else 1.0
    values = jax.random.normal(key, shape, jnp.float32) * scale * level
    return jnp.minimum(jnp.maximum(values, -bound), bound).astype(held_as)


def setup_inputs(seed: int = 0) -> dict:
    arg_keys = jax.random.split(jax.random.key(seed), 17)
    return {
        "tokens": bell_draw(arg_keys[0], (ROWS, ROW_LEN, D), 1.0, 6.0, ((0, 8), (1, 4))),
        "conditioning": bell_draw(arg_keys[1], (IMAGES, D), 1.0, 6.0, ((0, 8),)),
        "segment_ids": draw_segment_ids(jax.random.fold_in(arg_keys[16], 71), 0),
        "image_index": with_ends(jax.random.randint(arg_keys[3], (ROWS, SEGS), 0, IMG_DEV), jax.random.fold_in(arg_keys[3], 1), 0, IMG_DEV - 1).astype(jnp.int32),
        "row_fill": draw_row_fill(jax.random.fold_in(arg_keys[16], 71), 0),
        "ada_weight": bell_draw(arg_keys[5], (D, 6 * D), D ** -0.5, 0.1875, ((1, 4),)),
        "ada_bias": bell_draw(arg_keys[6], (6 * D,), 0.3, 1.796875),
        "qkv_weight": bell_draw(arg_keys[7], (D, 3 * D), D ** -0.5, 0.1875),
        "qv_bias": bell_draw(arg_keys[8], (2, D), 0.3, 1.796875),
        "proj_weight": bell_draw(arg_keys[9], (D, D), (max(8 * D // ROW_LEN, 1)) ** -0.5, 2.0),
        "proj_bias": bell_draw(arg_keys[10], (D,), 0.3, 1.796875),
        "up_weight": bell_draw(arg_keys[11], (D, FF), D ** -0.5, 0.1875),
        "up_bias": bell_draw(arg_keys[12], (FF,), 0.3, 1.796875),
        "down_weight": bell_draw(arg_keys[13], (FF, D), FF ** -0.5, 0.09375),
        "down_bias": bell_draw(arg_keys[14], (D,), 0.3, 1.796875),
        "cotangent": bell_draw(arg_keys[15], (ROWS, ROW_LEN, D), 1.0, 6.0, ((0, 8), (1, 4))),
    }


@jax.custom_vjp
def low(v):
    return lax.optimization_barrier(v.astype(jnp.bfloat16)).astype(jnp.float32)

@jax.custom_vjp
def low_back(v):
    return v

def low_keep(v):
    return (low(v), None)

def low_pass(kept, grad):
    return (grad,)

def back_keep(v):
    return (v, None)

def back_low(kept, grad):
    return (low(grad),)
low.defvjp(low_keep, low_pass)
low_back.defvjp(back_keep, back_low)
norm_eps = 1e-06

def matmul(left, right):
    return jnp.dot(left, right, precision=lax.Precision.HIGHEST, preferred_element_type=jnp.float32)

def modulate(values, offset, factor):
    center = values - lax.optimization_barrier(jnp.mean(values, axis=-1, keepdims=True))
    spread = lax.optimization_barrier(jnp.mean(center * center, axis=-1, keepdims=True))
    return center * lax.rsqrt(spread + norm_eps) * (1.0 + factor) + offset

def gelu_tanh(values):
    return jax.nn.gelu(values, approximate=True)

def allowed_pairs(segments, filled):
    places = jnp.arange(segments.shape[0]).astype(jnp.int32)
    inside = places < filled
    same_segment = (segments[:, None] == segments[None, :]) & inside[:, None] & inside[None, :]
    return same_segment | (places[:, None] == places[None, :])

def head_forward(query_block, key_block, value_block, allowed):
    raw_scores = low_back(matmul(query_block, key_block.T))
    scores = jnp.where(allowed, raw_scores * query_block.shape[1] ** (-0.5), -1e+30)
    row_peak = lax.optimization_barrier(jnp.max(scores, axis=-1, keepdims=True))
    raised = jnp.exp(scores - row_peak)
    soft_weights = raised / lax.optimization_barrier(jnp.sum(raised, axis=-1, keepdims=True))
    return matmul(low(soft_weights), value_block)

def row_block(row_tokens, mod_tok, allowed, params):
    qkv_weight, qv_bias, proj_weight, proj_bias, up_weight, up_bias, down_weight, down_bias = params
    length = row_tokens.shape[0]
    width = row_tokens.shape[1]
    shift_a, scale_a, gate_a, shift_b, scale_b, gate_b = jnp.split(mod_tok, 6, axis=-1)
    normed_a = low(modulate(row_tokens, shift_a, scale_a))
    bias_qkv = jnp.concatenate([qv_bias[0], jnp.zeros((width,), jnp.float32), qv_bias[1]])
    packed = low(low_back(matmul(normed_a, qkv_weight) + bias_qkv))
    split_heads = packed.reshape(length, 3, HEADS, width // HEADS).transpose(1, 2, 0, 3)

    def one_head(blocks):
        return head_forward(blocks[0], blocks[1], blocks[2], allowed)
    heads_out = lax.map(jax.checkpoint(one_head), (split_heads[0], split_heads[1], split_heads[2]))
    attended = low(low_back(heads_out.transpose(1, 0, 2).reshape(length, width)))
    branch_a = low_back(matmul(attended, proj_weight) + proj_bias)
    middle = row_tokens + gate_a * branch_a
    normed_b = low(modulate(middle, shift_b, scale_b))
    hidden_pre = low_back(matmul(normed_b, up_weight) + up_bias)
    activated = low(gelu_tanh(hidden_pre))
    branch_b = low_back(matmul(activated, down_weight) + down_bias)
    return middle + gate_b * branch_b

def reference(tokens, conditioning, segment_ids, image_index, row_fill, ada_weight, ada_bias, qkv_weight, qv_bias, proj_weight, proj_bias, up_weight, up_bias, down_weight, down_bias, cotangent):

    def make_mod(cond_in, weight_in, bias_in):
        return low_back(matmul(low(jax.nn.silu(cond_in)), weight_in)) + bias_in
    modulation, mod_back = jax.vjp(make_mod, conditioning.astype(jnp.float32), ada_weight.astype(jnp.float32), ada_bias.astype(jnp.float32))
    params = tuple((weight.astype(jnp.float32) for weight in (qkv_weight, qv_bias, proj_weight, proj_bias, up_weight, up_bias, down_weight, down_bias)))
    group_of = (jnp.arange(ROWS) // ROWS_DEV).astype(jnp.int32)

    def row_step(carry, inputs):
        mod_grad, param_grad = carry
        row_tokens, segments, images, filled, row_cot, group = inputs
        picked = (group * IMG_DEV + images[segments]).astype(jnp.int32)
        mod_tok = modulation[picked]
        allowed = allowed_pairs(segments, filled)

        def inner(row_in, mod_in, param_in):
            return row_block(row_in, mod_in, allowed, param_in)
        out_row, row_back = jax.vjp(inner, row_tokens, mod_tok, params)
        grad_row, grad_mod, grad_params = row_back(row_cot)
        mod_grad = mod_grad.at[picked].add(grad_mod)
        param_grad = jax.tree.map(jnp.add, param_grad, grad_params)
        return ((mod_grad, param_grad), (out_row.astype(jnp.bfloat16), grad_row))
    start = (jnp.zeros_like(modulation), jax.tree.map(jnp.zeros_like, params))
    carried, stacked = lax.scan(row_step, start, (tokens.astype(jnp.float32), segment_ids, image_index, row_fill, cotangent.astype(jnp.float32), group_of))
    mod_grad, param_grad = carried
    block_out, grad_tokens = stacked
    grad_cond, grad_ada_weight, grad_ada_bias = mod_back(mod_grad)
    return (block_out, grad_tokens, grad_cond, grad_ada_weight, grad_ada_bias, param_grad[0], param_grad[1], param_grad[2], param_grad[3], param_grad[4], param_grad[5], param_grad[6], param_grad[7])
```

```python
from functools import partial
import math

import jax
import jax.numpy as jnp
from jax import lax
from jax.experimental import pallas as pl
from jax.experimental.pallas import tpu as pltpu
from jax.sharding import PartitionSpec as P

HEADS = 16
LOG2E = math.log2(math.e)
VMEM_LIMIT = 48 << 20
BF16 = jnp.bfloat16
F32 = jnp.float32

norm_eps = 1e-06


def modulate(values, offset, factor):
    center = values - jnp.mean(values, axis=-1, keepdims=True)
    spread = jnp.mean(center * center, axis=-1, keepdims=True)
    return center * lax.rsqrt(spread + norm_eps) * (1.0 + factor) + offset


def gelu_tanh(values):
    return jax.nn.gelu(values, approximate=True)


def swap(values, axis, mask):
    count = lax.axis_size(axis)
    return lax.ppermute(values, axis, [(i, i ^ mask) for i in range(count)])


def flip_blocks(values, axis, mask):
    return jnp.take(values, lax.iota(jnp.int32, values.shape[axis]) ^ mask, axis=axis)


def qkv_kernel(slot_row, seg, mod, tokens, weight, bias, normed_ref, qkv_ref):
    width = tokens.shape[-1]
    values = tokens[0].astype(F32)
    picked = (seg[0] == slot_row[...]).astype(BF16)
    table = mod[0]
    high = table.astype(BF16)
    rest = table - high.astype(F32)
    middle = rest.astype(BF16)
    last = (rest - middle.astype(F32)).astype(BF16)
    stacked = jnp.concatenate([high, middle, last], axis=0)
    per_token = jnp.dot(picked, stacked, preferred_element_type=F32)
    normed = modulate(values, per_token[:, :width], per_token[:, width:]).astype(BF16)
    normed_ref[0] = normed
    mixed = lax.dot_general(weight[...], normed, (((1,), (1,)), ((), ())), preferred_element_type=F32)
    mixed = (mixed + bias[...]).astype(BF16)
    _, parts, heads, size, _ = qkv_ref.shape
    for part in range(parts):
        for head in range(heads):
            start = (part * heads + head) * size
            qkv_ref[0, part, head] = mixed[start : start + size]


def project_qkv(tokens, seg, slot_mod, weight, bias, heads, block):
    rows, length, width = tokens.shape
    slots = slot_mod.shape[1]
    features = weight.shape[0]
    size = features // (3 * heads)
    slot_row = jnp.tile(lax.iota(jnp.int32, slots), 3)[None]
    return pl.pallas_call(
        qkv_kernel,
        grid=(rows, length // block),
        in_specs=[
            pl.BlockSpec((1, 3 * slots), lambda r, t: (0, 0)),
            pl.BlockSpec((1, block, 1), lambda r, t: (r, t, 0)),
            pl.BlockSpec((1, slots, 2 * width), lambda r, t: (r, 0, 0)),
            pl.BlockSpec((1, block, width), lambda r, t: (r, t, 0)),
            pl.BlockSpec((features, width), lambda r, t: (0, 0)),
            pl.BlockSpec((features, 1), lambda r, t: (0, 0)),
        ],
        out_specs=[
            pl.BlockSpec((1, block, width), lambda r, t: (r, t, 0)),
            pl.BlockSpec((1, 3, heads, size, block), lambda r, t: (r, 0, 0, 0, t)),
        ],
        out_shape=[
            jax.ShapeDtypeStruct((rows, length, width), BF16),
            jax.ShapeDtypeStruct((rows, 3, heads, size, length), BF16),
        ],
        compiler_params=pltpu.CompilerParams(vmem_limit_bytes=VMEM_LIMIT),
        cost_estimate=pl.CostEstimate(
            flops=2 * rows * length * width * features,
            bytes_accessed=2 * rows * length * (2 * width + features),
            transcendentals=0,
        ),
    )(slot_row, seg[:, :, None], slot_mod, tokens, weight, bias[:, None])


def attend_kernel(block, scale, code_col, code_row, query, key, value, out_ref, lse_ref):
    length = query.shape[-1]
    keys = key[0, 0].astype(F32).T.astype(BF16)
    values = value[0, 0]
    codes = code_col[0]
    for step in range(length // block):
        here = pl.ds(step * block, block)
        scores = jnp.dot(keys, query[0, 0, :, here], preferred_element_type=F32)
        scores = jnp.where(codes == code_row[0, :, here], scores * scale, -1e30)
        peak = jnp.max(scores, axis=0, keepdims=True)
        raised = jnp.exp2(scores - peak)
        total = jnp.sum(raised, axis=0, keepdims=True)
        probs = (raised * (1.0 / total)).astype(BF16)
        out_ref[0, 0, :, here] = jnp.dot(values, probs, preferred_element_type=F32).astype(BF16)
        lse_ref[0, 0, :, here] = peak + jnp.log2(total)


def attend(packed, col, row, block):
    rows, _, heads, size, length = packed.shape
    part = lambda j: pl.BlockSpec((1, None, 1, size, length), lambda r, h: (r, j, h, 0, 0))
    return pl.pallas_call(
        partial(attend_kernel, block, size**-0.5 * LOG2E),
        grid=(rows, heads),
        in_specs=[
            pl.BlockSpec((1, length, 1), lambda r, h: (r, 0, 0)),
            pl.BlockSpec((1, 1, length), lambda r, h: (r, 0, 0)),
            part(0),
            part(1),
            part(2),
        ],
        out_specs=[
            pl.BlockSpec((1, 1, size, length), lambda r, h: (r, h, 0, 0)),
            pl.BlockSpec((1, 1, 1, length), lambda r, h: (r, h, 0, 0)),
        ],
        out_shape=[
            jax.ShapeDtypeStruct((rows, heads, size, length), BF16),
            jax.ShapeDtypeStruct((rows, heads, 1, length), F32),
        ],
        compiler_params=pltpu.CompilerParams(vmem_limit_bytes=VMEM_LIMIT),
        cost_estimate=pl.CostEstimate(
            flops=8 * rows * heads * length * length * 128,
            bytes_accessed=8 * rows * heads * length * size,
            transcendentals=rows * heads * length * length,
        ),
    )(col, row, packed, packed, packed)


def attend_back_kernel(
    block, inner, scale, code_col, code_row, query, key, value, out, grad_out, lse, grad_ref, key_sum, value_sum, keys, values
):
    length = query.shape[-1]
    size = query.shape[-2]
    keys[...] = key[0, 0].astype(F32).T.astype(BF16)
    values[...] = value[0, 0].astype(F32).T.astype(BF16)
    for step in range(length // block):
        here = pl.ds(step * block, block)
        query_low = query[0, 0, :, here]
        grad_low = grad_out[0, 0, :, here]
        query_rows = query_low.astype(F32).T.astype(BF16)
        grad_rows = grad_low.astype(F32).T.astype(BF16)
        row_dot = jnp.sum(grad_low.astype(F32) * out[0, 0, :, here].astype(F32), axis=0, keepdims=True)
        grad_query = jnp.zeros((size, block), F32)
        for part in range(length // inner):
            there = pl.ds(part * inner, inner)
            scores = jnp.dot(keys[there, :], query_low, preferred_element_type=F32)
            scores = jnp.where(code_col[0, there, :] == code_row[0, :, here], scores * (scale * LOG2E), -1e30)
            probs = jnp.exp2(scores - lse[0, 0, :, here])
            grad_probs = jnp.dot(values[there, :], grad_low, preferred_element_type=F32)
            grad_raw = (probs * (grad_probs - row_dot) * scale).astype(BF16)
            value_part = jnp.dot(probs.astype(BF16), grad_rows, preferred_element_type=F32)
            key_part = jnp.dot(grad_raw, query_rows, preferred_element_type=F32)
            if step == 0:
                value_sum[there, :] = value_part
                key_sum[there, :] = key_part
            else:
                value_sum[there, :] += value_part
                key_sum[there, :] += key_part
            grad_query += jnp.dot(key[0, 0, :, there], grad_raw, preferred_element_type=F32)
        grad_ref[0, 0, 0, :, here] = grad_query.astype(BF16)
    grad_ref[0, 1, 0] = key_sum[...].T.astype(BF16)
    grad_ref[0, 2, 0] = value_sum[...].T.astype(BF16)


def attend_back(packed, out, grad_out, lse, col, row, block, inner):
    rows, _, heads, size, length = packed.shape
    part = lambda j: pl.BlockSpec((1, None, 1, size, length), lambda r, h: (r, j, h, 0, 0))
    whole = pl.BlockSpec((1, 1, size, length), lambda r, h: (r, h, 0, 0))
    return pl.pallas_call(
        partial(attend_back_kernel, block, inner, size**-0.5),
        grid=(rows, heads),
        in_specs=[
            pl.BlockSpec((1, length, 1), lambda r, h: (r, 0, 0)),
            pl.BlockSpec((1, 1, length), lambda r, h: (r, 0, 0)),
            part(0),
            part(1),
            part(2),
            whole,
            whole,
            pl.BlockSpec((1, 1, 1, length), lambda r, h: (r, h, 0, 0)),
        ],
        out_specs=pl.BlockSpec((1, 3, 1, size, length), lambda r, h: (r, 0, h, 0, 0)),
        out_shape=jax.ShapeDtypeStruct((rows, 3, heads, size, length), BF16),
        scratch_shapes=[
            pltpu.VMEM((length, size), F32),
            pltpu.VMEM((length, size), F32),
            pltpu.VMEM((length, size), BF16),
            pltpu.VMEM((length, size), BF16),
        ],
        compiler_params=pltpu.CompilerParams(vmem_limit_bytes=VMEM_LIMIT),
        cost_estimate=pl.CostEstimate(
            flops=20 * rows * heads * length * length * 128,
            bytes_accessed=16 * rows * heads * length * size,
            transcendentals=rows * heads * length * length,
        ),
    )(col, row, packed, packed, packed, out, grad_out, lse)


def gather_seq(values):
    count = lax.axis_size("seq")
    if count == 4:
        first, second = swap(values, "seq", 1), swap(values, "seq", 2)
        half = values.shape[0] // 2
        third = jnp.concatenate([swap(second[:half], "seq", 1), swap(first[half:], "seq", 2)], axis=0)
        return [values, first, second, third]
    return [values] + [swap(values, "seq", m) for m in range(1, count)]


def exchange_seq(blocks):
    return [blocks[0]] + [swap(blocks[m], "seq", m) for m in range(1, len(blocks))]


def sum_seq(values):
    total = values
    for m in range(1, lax.axis_size("seq")):
        total = total + swap(values, "seq", m)
    return total


def halve_seq(parts, order):
    index = lax.axis_index("seq")
    count = lax.axis_size("seq")
    shape = parts.shape[1:]
    bits = [count >> (k + 1) for k in range(count.bit_length() - 1)]
    current = parts.reshape((2,) * len(bits) + shape)
    left = list(bits)
    for bit in [bits[k] for k in order]:
        axis = left.index(bit)
        mine = (index // bit) % 2
        keep = lax.dynamic_index_in_dim(current, mine, axis, keepdims=False)
        send = lax.dynamic_index_in_dim(current, 1 - mine, axis, keepdims=False).astype(BF16)
        current = keep + swap(send, "seq", bit).astype(F32)
        left.pop(axis)
    return current


def reduce_weight(part):
    groups, index, count = lax.axis_size("rows"), lax.axis_index("rows"), lax.axis_size("seq")
    chips = groups // 2
    core = index % 2
    depth, width = part.shape[0] // groups, part.shape[1] // count
    view = part.reshape(chips, 2, depth, part.shape[1])
    keep = lax.dynamic_index_in_dim(view, core, 1, keepdims=False)
    send = lax.dynamic_index_in_dim(view, 1 - core, 1, keepdims=False).astype(BF16)
    both = keep + swap(send, "rows", 1).astype(F32)
    blocks = both.reshape(chips * depth, count, width).transpose(1, 0, 2)
    half = chips * depth // 2
    levels = count.bit_length() - 1
    up = halve_seq(blocks[:, :half], list(range(levels)))
    down = halve_seq(blocks[:, half:], list(range(levels))[::-1])
    summed = jnp.concatenate([up, down], axis=0).reshape(chips, depth, width)
    return spread_rows(summed)


def spread_rows(summed):
    chip = lax.axis_index("rows") // 2
    chips = summed.shape[0]
    total = lax.dynamic_index_in_dim(summed, chip, 0, keepdims=False)
    for m in range(1, chips):
        send = lax.dynamic_index_in_dim(summed, chip ^ m, 0, keepdims=False).astype(BF16)
        total = total + swap(send, "rows", 2 * m).astype(F32)
    return total


def on_device(
    tokens,
    conditioning,
    segment_ids,
    image_index,
    row_fill,
    ada_weight,
    ada_bias,
    qkv_weight,
    qv_bias,
    proj_weight,
    proj_bias,
    up_weight,
    up_bias,
    down_weight,
    down_bias,
    cotangent,
):
    row_count, local_len, width = tokens.shape
    seq_count = lax.axis_size("seq")
    seq_index = lax.axis_index("seq")
    row_index = lax.axis_index("rows")
    full_len = local_len * seq_count
    heads_dev = HEADS // seq_count
    head_size = width // HEADS
    own = heads_dev * head_size
    image_count = conditioning.shape[0]

    tokens_all = jnp.concatenate(gather_seq(tokens), axis=1)
    seg_blocks = flip_blocks(segment_ids.reshape(row_count, seq_count, local_len), 1, seq_index)
    seg_all = seg_blocks.reshape(row_count, full_len)
    places = (lax.iota(jnp.int32, seq_count) ^ seq_index)[:, None] * local_len + lax.iota(jnp.int32, local_len)
    places = places.reshape(1, full_len)
    codes = jnp.where(places < row_fill[:, None], seg_all, -1 - places)
    code_col, code_row = codes[:, :, None], codes[:, None, :]

    qkv_turned = qkv_weight.T.reshape(3, seq_count, own, width)
    qkv_order = flip_blocks(qkv_turned, 1, seq_index).transpose(1, 0, 2, 3)
    qkv_own = qkv_order[0].reshape(3 * own, width)
    qkv_back = qkv_order.reshape(3 * width, width)
    proj_order = flip_blocks(proj_weight.reshape(seq_count, own, width), 0, seq_index).reshape(width, width)
    bias_own = lax.dynamic_slice_in_dim(qv_bias.astype(F32), seq_index * own, own, 1)
    bias_own = jnp.concatenate([bias_own[0], jnp.zeros((own,), F32), bias_own[1]])

    cond_wide = conditioning.astype(F32)
    cond_low = jax.nn.silu(cond_wide).astype(BF16)
    cond_all = lax.all_gather(cond_low, "rows", axis=0, tiled=True)
    mod_part = jnp.dot(cond_low, ada_weight, preferred_element_type=F32)
    modulation = lax.all_gather(mod_part, "seq", axis=1, tiled=True) + ada_bias.astype(F32)
    local_seg = lax.dynamic_slice_in_dim(segment_ids, seq_index * local_len, local_len, 1)
    slot_ids = lax.iota(jnp.int32, image_index.shape[1])
    slot_mod = jnp.take(modulation, image_index, axis=0)

    normed_all, packed = project_qkv(
        tokens_all, seg_all, slot_mod[:, :, : 2 * width], qkv_own, bias_own, heads_dev, min(256, full_len)
    )
    attended, log_totals = attend(packed, code_col, code_row, 512)

    slot_pick = (local_seg[:, :, None] == slot_ids).astype(F32)
    mod_tok = jnp.einsum("rts,rse->rte", slot_pick, slot_mod, precision=lax.Precision.HIGHEST)
    shift_a, scale_a, gate_a, shift_b, scale_b, gate_b = jnp.split(mod_tok, 6, axis=-1)
    tokens_wide = tokens.astype(F32)

    def by_block(values):
        return [values[..., m * local_len : (m + 1) * local_len] for m in range(seq_count)]

    attended_tok = jnp.concatenate(
        exchange_seq(by_block(attended.reshape(row_count, own, full_len))), axis=1
    )
    branch_a = jnp.einsum(
        "rft,fe->rte", attended_tok, proj_order, preferred_element_type=F32
    ) + proj_bias.astype(F32)
    middle = tokens_wide + gate_a * branch_a
    normed_b = modulate(middle, shift_b, scale_b).astype(BF16)
    hidden_pre = jnp.einsum(
        "rtd,df->rtf", normed_b, up_weight, preferred_element_type=F32
    ) + up_bias.astype(F32)
    activated = gelu_tanh(hidden_pre).astype(BF16)
    branch_b = jnp.einsum(
        "rtf,fe->rte", activated, down_weight, preferred_element_type=F32
    ) + down_bias.astype(F32)
    block_out = (middle + gate_b * branch_b).astype(BF16)
    upstream = cotangent.astype(F32)
    grad_branch_b = (upstream * gate_b).astype(BF16)
    grad_gate_b = upstream * branch_b
    part_down_bias = jnp.sum(grad_branch_b.astype(F32), axis=(0, 1))
    grad_act = jnp.einsum("rte,fe->rtf", grad_branch_b, down_weight, preferred_element_type=F32)
    _, gelu_back = jax.vjp(gelu_tanh, hidden_pre)
    grad_pre = gelu_back(grad_act)[0].astype(BF16)
    part_up_bias = jnp.sum(grad_pre.astype(F32), axis=(0, 1))
    grad_normed_b = jnp.einsum("rtf,df->rtd", grad_pre, up_weight, preferred_element_type=F32)
    _, norm_back_b = jax.vjp(modulate, middle, shift_b, scale_b)
    grad_mid_norm, grad_shift_b, grad_scale_b = norm_back_b(grad_normed_b)
    grad_middle = upstream + grad_mid_norm
    grad_branch_a = (grad_middle * gate_a).astype(BF16)
    grad_gate_a = grad_middle * branch_a
    part_proj_bias = jnp.sum(grad_branch_a.astype(F32), axis=(0, 1))
    grad_attended = jnp.einsum(
        "fe,rte->rft", proj_order, grad_branch_a, preferred_element_type=F32
    ).astype(BF16)
    grad_heads_in = jnp.concatenate(
        exchange_seq([grad_attended[:, m * own : (m + 1) * own] for m in range(seq_count)]), axis=2
    )
    grad_view = grad_heads_in.reshape(row_count, heads_dev, head_size, full_len)

    part_down = jnp.einsum("rtf,rte->fe", activated, grad_branch_b, preferred_element_type=F32)
    part_up = jnp.einsum("rtd,rtf->df", normed_b, grad_pre, preferred_element_type=F32)
    attended_plain = flip_blocks(
        attended_tok.reshape(row_count, seq_count, own, local_len), 1, seq_index
    ).reshape(row_count, width, local_len)
    part_proj = jnp.einsum("rft,rte->fe", attended_plain, grad_branch_a, preferred_element_type=F32)
    grad_down_weight = reduce_weight(part_down)
    grad_up_weight = reduce_weight(part_up)
    grad_proj_weight = reduce_weight(part_proj)

    grad_heads = attend_back(packed, attended, grad_view, log_totals, code_col, code_row, 256, 512)
    grad_own = grad_heads.reshape(row_count, 3 * own, full_len)
    grad_flat = jnp.concatenate(exchange_seq(by_block(grad_own)), axis=1)
    grad_normed_a = jnp.einsum("rft,fd->rtd", grad_flat, qkv_back, preferred_element_type=F32)

    part_qkv = jnp.einsum("rft,rtd->fd", grad_own, normed_all, preferred_element_type=F32)
    own_sums = jnp.sum(grad_own.astype(F32), axis=(0, 2)).reshape(3, own)
    groups = lax.axis_size("rows")
    chips = groups // 2
    core = row_index % 2
    turned = part_qkv.T.reshape(chips, 2, width // groups, 3 * own)
    keep = lax.dynamic_index_in_dim(turned, core, 1, keepdims=False)
    send = lax.dynamic_index_in_dim(turned, 1 - core, 1, keepdims=False).astype(BF16)
    qkv_sum = spread_rows(keep + swap(send, "rows", 1).astype(F32))
    qkv_blocks = lax.all_gather(qkv_sum.astype(BF16), "seq", axis=0).reshape(seq_count, width // groups, 3, own)
    qkv_cols = qkv_blocks.transpose(1, 2, 0, 3).reshape(width // groups, 3 * width)
    grad_qkv_weight = lax.dynamic_slice_in_dim(
        qkv_cols, seq_index * (3 * width // seq_count), 3 * width // seq_count, 1
    ).astype(F32)

    _, norm_back_a = jax.vjp(modulate, tokens_wide, shift_a, scale_a)
    grad_tok_norm, grad_shift_a, grad_scale_a = norm_back_a(grad_normed_a)
    grad_tokens = grad_middle + grad_tok_norm
    grad_mod_tok = jnp.concatenate(
        [grad_shift_a, grad_scale_a, grad_gate_a, grad_shift_b, grad_scale_b, grad_gate_b], axis=-1
    )
    slot_grads = jnp.einsum("rts,rte->rse", slot_pick, grad_mod_tok, precision=lax.Precision.HIGHEST)
    image_pick = (image_index[:, :, None] == lax.iota(jnp.int32, image_count)).astype(F32)
    grad_modulation = jnp.einsum("rsi,rse->ie", image_pick, slot_grads, precision=lax.Precision.HIGHEST)
    part_ada_bias = jnp.sum(grad_modulation, axis=0)
    mod_view = grad_modulation.reshape(image_count, seq_count, -1)
    mod_blocks = [
        lax.dynamic_index_in_dim(mod_view, seq_index ^ m, 1, keepdims=False) for m in range(seq_count)
    ]
    mod_columns = sum(exchange_seq(mod_blocks))
    grad_mod_low = mod_columns.astype(BF16)
    grad_mod_all = lax.all_gather(grad_mod_low, "rows", axis=0, tiled=True)
    cond_cols = lax.dynamic_slice_in_dim(cond_all, row_index * (width // groups), width // groups, 1)
    grad_ada_weight = jnp.einsum("id,ie->de", cond_cols, grad_mod_all, preferred_element_type=F32)
    cond_term = jnp.einsum("ie,de->id", grad_mod_low, ada_weight, preferred_element_type=F32)
    grad_cond_low = sum_seq(cond_term)
    _, silu_back = jax.vjp(jax.nn.silu, cond_wide)
    grad_cond = silu_back(grad_cond_low)[0]

    part_qv_bias = jnp.zeros((2, seq_count, own), F32)
    part_qv_bias = lax.dynamic_update_slice(
        part_qv_bias, jnp.stack([own_sums[0], own_sums[2]])[:, None], (0, seq_index, 0)
    ).reshape(2, width)
    grad_proj_bias, grad_up_bias, grad_down_bias = lax.psum(
        (part_proj_bias, part_up_bias, part_down_bias), ("rows", "seq")
    )
    grad_qv_bias, grad_ada_bias = lax.psum((part_qv_bias, part_ada_bias), ("rows", "seq"))
    return (
        block_out,
        grad_tokens,
        grad_cond,
        grad_ada_weight,
        grad_ada_bias,
        grad_qkv_weight,
        grad_qv_bias,
        grad_proj_weight,
        grad_proj_bias,
        grad_up_weight,
        grad_up_bias,
        grad_down_weight,
        grad_down_bias,
    )


def solution(mesh):
    in_specs = (
        P("rows", "seq", None),
        P("rows", None),
        P("rows", None),
        P("rows", None),
        P("rows"),
        P(None, "seq"),
        P(),
        P(),
        P(),
        P(),
        P(),
        P(),
        P(),
        P(),
        P(),
        P("rows", "seq", None),
    )
    out_specs = (
        P("rows", "seq", None),
        P("rows", "seq", None),
        P("rows", None),
        P("rows", "seq"),
        P(),
        P("rows", "seq"),
        P(),
        P("rows", "seq"),
        P(),
        P("rows", "seq"),
        P(),
        P("rows", "seq"),
        P(),
    )
    return jax.shard_map(
        on_device, mesh=mesh, in_specs=in_specs, out_specs=out_specs, check_vma=False
    )
```

```python
from functools import partial
import math

import jax
import jax.numpy as jnp
from jax import lax
from jax.experimental import pallas as pl
from jax.experimental.pallas import tpu as pltpu
from jax.sharding import PartitionSpec as P

HEADS = 16
LOG2E = math.log2(math.e)
VMEM_LIMIT = 48 << 20
BF16 = jnp.bfloat16
F32 = jnp.float32

norm_eps = 1e-06


def modulate(values, offset, factor):
    center = values - jnp.mean(values, axis=-1, keepdims=True)
    spread = jnp.mean(center * center, axis=-1, keepdims=True)
    return center * lax.rsqrt(spread + norm_eps) * (1.0 + factor) + offset


def gelu_tanh(values):
    return jax.nn.gelu(values, approximate=True)


def swap(values, axis, mask):
    count = lax.axis_size(axis)
    return lax.ppermute(values, axis, [(i, i ^ mask) for i in range(count)])


def flip_blocks(values, axis, mask):
    return jnp.take(values, lax.iota(jnp.int32, values.shape[axis]) ^ mask, axis=axis)


def qkv_kernel(slot_row, seg, mod, tokens, weight, bias, normed_ref, qkv_ref):
    width = tokens.shape[-1]
    values = tokens[0].astype(F32)
    picked = (seg[0] == slot_row[...]).astype(BF16)
    table = mod[0]
    high = table.astype(BF16)
    rest = table - high.astype(F32)
    middle = rest.astype(BF16)
    last = (rest - middle.astype(F32)).astype(BF16)
    stacked = jnp.concatenate([high, middle, last], axis=0)
    per_token = jnp.dot(picked, stacked, preferred_element_type=F32)
    normed = modulate(values, per_token[:, :width], per_token[:, width:]).astype(BF16)
    normed_ref[0] = normed
    mixed = lax.dot_general(weight[...], normed, (((1,), (1,)), ((), ())), preferred_element_type=F32)
    mixed = (mixed + bias[...]).astype(BF16)
    _, parts, heads, size, _ = qkv_ref.shape
    for part in range(parts):
        for head in range(heads):
            start = (part * heads + head) * size
            qkv_ref[0, part, head] = mixed[start : start + size]


def project_qkv(tokens, seg, slot_mod, weight, bias, heads, block):
    rows, length, width = tokens.shape
    slots = slot_mod.shape[1]
    features = weight.shape[0]
    size = features // (3 * heads)
    slot_row = jnp.tile(lax.iota(jnp.int32, slots), 3)[None]
    return pl.pallas_call(
        qkv_kernel,
        grid=(rows, length // block),
        in_specs=[
            pl.BlockSpec((1, 3 * slots), lambda r, t: (0, 0)),
            pl.BlockSpec((1, block, 1), lambda r, t: (r, t, 0)),
            pl.BlockSpec((1, slots, 2 * width), lambda r, t: (r, 0, 0)),
            pl.BlockSpec((1, block, width), lambda r, t: (r, t, 0)),
            pl.BlockSpec((features, width), lambda r, t: (0, 0)),
            pl.BlockSpec((features, 1), lambda r, t: (0, 0)),
        ],
        out_specs=[
            pl.BlockSpec((1, block, width), lambda r, t: (r, t, 0)),
            pl.BlockSpec((1, 3, heads, size, block), lambda r, t: (r, 0, 0, 0, t)),
        ],
        out_shape=[
            jax.ShapeDtypeStruct((rows, length, width), BF16),
            jax.ShapeDtypeStruct((rows, 3, heads, size, length), BF16),
        ],
        compiler_params=pltpu.CompilerParams(vmem_limit_bytes=VMEM_LIMIT),
        cost_estimate=pl.CostEstimate(
            flops=2 * rows * length * width * features,
            bytes_accessed=2 * rows * length * (2 * width + features),
            transcendentals=0,
        ),
    )(slot_row, seg[:, :, None], slot_mod, tokens, weight, bias[:, None])


def peers_of(seq):
    x, y = lax.rem(seq, 2), lax.div(seq, 2)
    return [seq + 1 - 2 * x, seq + 2 - 4 * y, 3 - seq]


def greet(devices):
    barrier = pltpu.get_barrier_semaphore()
    for device in devices:
        pl.semaphore_signal(barrier, inc=1, device_id={"seq": device}, device_id_type=pl.DeviceIdType.MESH)
    pl.semaphore_wait(barrier, len(devices))


def send_block(source, target, sent, came, index, device):
    return pltpu.make_async_remote_copy(
        src_ref=source,
        dst_ref=target,
        send_sem=sent.at[index],
        recv_sem=came.at[index],
        device_id={"seq": device},
        device_id_type=pl.DeviceIdType.MESH,
    )


def attend_kernel(block, scale, code_col, code_row, query, key, value, out_ref, lse_ref, token_ref=None, sent=None, came=None, kept=None):
    length = query.shape[-1]
    keys = key[0, 0].astype(F32).T.astype(BF16)
    values = value[0, 0]
    codes = code_col[0]
    row, head = (pl.program_id(0), pl.program_id(1)) if sent is not None else (0, 0)
    rows, heads = out_ref.shape[:2]
    if sent is not None:
        seq = lax.axis_index("seq")
        peers = peers_of(seq)
        size = length // 4

        @pl.when((row == 0) & (head == 0))
        def _():
            greet(peers)

        def to_peer(r, h, m):
            lanes = pl.ds(m * size, size)
            place = (r * heads + h) * 3 + m - 1
            return send_block(out_ref.at[r, h, :, lanes], token_ref.at[r, seq, h], sent, came, place, peers[m - 1])

        def to_self(r, h):
            return pltpu.make_async_copy(out_ref.at[r, h, :, pl.ds(0, size)], token_ref.at[r, seq, h], kept.at[r * heads + h])

    for step in range(length // block):
        here = pl.ds(step * block, block)
        scores = jnp.dot(keys, query[0, 0, :, here], preferred_element_type=F32)
        scores = jnp.where(codes == code_row[0, :, here], scores * scale, -1e30)
        peak = jnp.max(scores, axis=0, keepdims=True)
        raised = jnp.exp2(scores - peak)
        total = jnp.sum(raised, axis=0, keepdims=True)
        probs = (raised * (1.0 / total)).astype(BF16)
        out_ref[row, head, :, here] = jnp.dot(values, probs, preferred_element_type=F32).astype(BF16)
        lse_ref[0, 0, :, here] = peak + jnp.log2(total)

    if sent is not None:
        to_self(row, head).start()
        for m in range(1, 4):
            to_peer(row, head, m).start()

        @pl.when((row == rows - 1) & (head == heads - 1))
        def _():
            for r in range(rows):
                for h in range(heads):
                    to_self(r, h).wait()
                    for m in range(1, 4):
                        to_peer(r, h, m).wait()


def attend(packed, col, row, block, exchange):
    rows, _, heads, size, length = packed.shape
    part = lambda j: pl.BlockSpec((1, None, 1, size, length), lambda r, h: (r, j, h, 0, 0))
    out_specs = [
        pl.BlockSpec((1, 1, size, length), lambda r, h: (r, h, 0, 0)),
        pl.BlockSpec((1, 1, 1, length), lambda r, h: (r, h, 0, 0)),
    ]
    out_shape = [
        jax.ShapeDtypeStruct((rows, heads, size, length), BF16),
        jax.ShapeDtypeStruct((rows, heads, 1, length), F32),
    ]
    scratch = []
    extra = {}
    if exchange:
        out_specs[0] = pl.BlockSpec((rows, heads, size, length), lambda r, h: (0, 0, 0, 0))
        out_specs.append(pl.BlockSpec(memory_space=pl.ANY))
        out_shape.append(jax.ShapeDtypeStruct((rows, 4, heads, size, length // 4), BF16))
        count = rows * heads
        scratch = [pltpu.SemaphoreType.DMA((3 * count,)), pltpu.SemaphoreType.DMA((3 * count,)), pltpu.SemaphoreType.DMA((count,))]
        extra = dict(collective_id=2, has_side_effects=True)
    return pl.pallas_call(
        partial(attend_kernel, block, size**-0.5 * LOG2E),
        grid=(rows, heads),
        in_specs=[
            pl.BlockSpec((1, length, 1), lambda r, h: (r, 0, 0)),
            pl.BlockSpec((1, 1, length), lambda r, h: (r, 0, 0)),
            part(0),
            part(1),
            part(2),
        ],
        out_specs=out_specs,
        out_shape=out_shape,
        scratch_shapes=scratch,
        compiler_params=pltpu.CompilerParams(vmem_limit_bytes=VMEM_LIMIT, **extra),
        cost_estimate=pl.CostEstimate(
            flops=8 * rows * heads * length * length * 128,
            bytes_accessed=8 * rows * heads * length * size,
            transcendentals=rows * heads * length * length,
        ),
    )(col, row, packed, packed, packed)


def attend_back_kernel(
    block,
    inner,
    scale,
    exchange,
    code_col,
    code_row,
    query,
    key,
    value,
    out,
    grad_out,
    lse,
    grad_ref,
    *rest,
):
    length = query.shape[-1]
    size = query.shape[-2]
    row, head = (pl.program_id(0), pl.program_id(1)) if exchange else (0, 0)
    rows, _, heads = grad_ref.shape[:3]
    if exchange:
        token_ref, key_sum, value_sum, keys, values, sent, came, kept = rest
        seq = lax.axis_index("seq")
        peers = peers_of(seq)
        local = length // 4

        @pl.when((row == 0) & (head == 0))
        def _():
            greet(peers)

        def to_peer(r, h, m):
            lanes = pl.ds(m * local, local)
            place = (r * heads + h) * 3 + m - 1
            return send_block(grad_ref.at[r, :, h, :, lanes], token_ref.at[r, :, seq, h], sent, came, place, peers[m - 1])

        def to_self(r, h):
            lanes = pl.ds(0, local)
            return pltpu.make_async_copy(grad_ref.at[r, :, h, :, lanes], token_ref.at[r, :, seq, h], kept.at[r * heads + h])

    else:
        key_sum, value_sum, keys, values = rest
    keys[...] = key[0, 0].astype(F32).T.astype(BF16)
    values[...] = value[0, 0].astype(F32).T.astype(BF16)
    for step in range(length // block):
        here = pl.ds(step * block, block)
        query_low = query[0, 0, :, here]
        grad_low = grad_out[0, 0, :, here]
        query_rows = query_low.astype(F32).T.astype(BF16)
        grad_rows = grad_low.astype(F32).T.astype(BF16)
        row_dot = jnp.sum(grad_low.astype(F32) * out[0, 0, :, here].astype(F32), axis=0, keepdims=True)
        grad_query = jnp.zeros((size, block), F32)
        for part in range(length // inner):
            there = pl.ds(part * inner, inner)
            scores = jnp.dot(keys[there, :], query_low, preferred_element_type=F32)
            scores = jnp.where(code_col[0, there, :] == code_row[0, :, here], scores * (scale * LOG2E), -1e30)
            probs = jnp.exp2(scores - lse[0, 0, :, here])
            grad_probs = jnp.dot(values[there, :], grad_low, preferred_element_type=F32)
            grad_raw = (probs * (grad_probs - row_dot) * scale).astype(BF16)
            value_part = jnp.dot(probs.astype(BF16), grad_rows, preferred_element_type=F32)
            key_part = jnp.dot(grad_raw, query_rows, preferred_element_type=F32)
            if step == 0:
                value_sum[there, :] = value_part
                key_sum[there, :] = key_part
            else:
                value_sum[there, :] += value_part
                key_sum[there, :] += key_part
            grad_query += jnp.dot(key[0, 0, :, there], grad_raw, preferred_element_type=F32)
        grad_ref[row, 0, head, :, here] = grad_query.astype(BF16)
    grad_ref[row, 1, head] = key_sum[...].T.astype(BF16)
    grad_ref[row, 2, head] = value_sum[...].T.astype(BF16)

    if exchange:
        to_self(row, head).start()
        for m in range(1, 4):
            to_peer(row, head, m).start()

        @pl.when((row == rows - 1) & (head == heads - 1))
        def _():
            for r in range(rows):
                for h in range(heads):
                    to_self(r, h).wait()
                    for m in range(1, 4):
                        to_peer(r, h, m).wait()


def attend_back(packed, out, grad_out, lse, col, row, block, inner, exchange):
    rows, _, heads, size, length = packed.shape
    part = lambda j: pl.BlockSpec((1, None, 1, size, length), lambda r, h: (r, j, h, 0, 0))
    whole = pl.BlockSpec((1, 1, size, length), lambda r, h: (r, h, 0, 0))
    out_specs = [pl.BlockSpec((1, 3, 1, size, length), lambda r, h: (r, 0, h, 0, 0))]
    out_shape = [jax.ShapeDtypeStruct((rows, 3, heads, size, length), BF16)]
    scratch = []
    extra = {}
    if exchange:
        out_specs = [
            pl.BlockSpec((rows, 3, heads, size, length), lambda r, h: (0, 0, 0, 0, 0)),
            pl.BlockSpec(memory_space=pl.ANY),
        ]
        out_shape.append(jax.ShapeDtypeStruct((rows, 3, 4, heads, size, length // 4), BF16))
        count = rows * heads
        scratch = [pltpu.SemaphoreType.DMA((3 * count,)), pltpu.SemaphoreType.DMA((3 * count,)), pltpu.SemaphoreType.DMA((count,))]
        extra = dict(collective_id=3, has_side_effects=True)
    return pl.pallas_call(
        partial(attend_back_kernel, block, inner, size**-0.5, exchange),
        grid=(rows, heads),
        in_specs=[
            pl.BlockSpec((1, length, 1), lambda r, h: (r, 0, 0)),
            pl.BlockSpec((1, 1, length), lambda r, h: (r, 0, 0)),
            part(0),
            part(1),
            part(2),
            whole,
            whole,
            pl.BlockSpec((1, 1, 1, length), lambda r, h: (r, h, 0, 0)),
        ],
        out_specs=out_specs,
        out_shape=out_shape,
        scratch_shapes=[
            pltpu.VMEM((length, size), F32),
            pltpu.VMEM((length, size), F32),
            pltpu.VMEM((length, size), BF16),
            pltpu.VMEM((length, size), BF16),
        ]
        + scratch,
        compiler_params=pltpu.CompilerParams(vmem_limit_bytes=VMEM_LIMIT, **extra),
        cost_estimate=pl.CostEstimate(
            flops=20 * rows * heads * length * length * 128,
            bytes_accessed=16 * rows * heads * length * size,
            transcendentals=rows * heads * length * length,
        ),
    )(col, row, packed, packed, packed, out, grad_out, lse)


def mlp_kernel(
    normed, grad_out, normed_turned, grad_turned, up, down, bias, out_sum, grad_sum, up_keep, up_send, down_keep, down_send, bias_sum
):
    step = pl.program_id(0)
    half = up_keep.shape[0]
    c0 = math.sqrt(2 / math.pi)
    c1 = c0 * 0.044715
    hidden = jnp.dot(normed[...], up[...], preferred_element_type=F32) + bias[...]
    square = hidden * hidden
    gate = 0.5 + 0.5 * jnp.tanh(hidden * (c0 + c1 * square))
    raised = hidden * gate
    slope = gate + raised * (1.0 - gate) * (2 * c0 + 6 * c1 * square)
    active = raised.astype(BF16)
    back = (((1,), (1,)), ((), ()))
    grad_active = lax.dot_general(grad_out[...], down[...], back, preferred_element_type=F32)
    grad_wide = (grad_active * slope).astype(BF16)
    out_part = jnp.dot(active, down[...], preferred_element_type=F32)
    grad_part = lax.dot_general(grad_wide, up[...], back, preferred_element_type=F32)

    @pl.when(step == 0)
    def _():
        out_sum[...] = out_part
        grad_sum[...] = grad_part

    @pl.when(step > 0)
    def _():
        out_sum[...] += out_part
        grad_sum[...] += grad_part

    bias_sum[...] = jnp.sum(grad_wide.astype(F32), axis=0, keepdims=True)
    up_keep[...] = jnp.dot(normed_turned[:half], grad_wide, preferred_element_type=F32)
    up_send[...] = jnp.dot(normed_turned[half:], grad_wide, preferred_element_type=F32).astype(BF16)
    down_keep[...] = jnp.dot(grad_turned[:half], active, preferred_element_type=F32)
    down_send[...] = jnp.dot(grad_turned[half:], active, preferred_element_type=F32).astype(BF16)


def feed_forward(normed, grad_out, normed_turned, grad_turned, up, down, bias, tile):
    count, width = normed.shape
    hidden = up.shape[1]
    half = width // 2
    fixed = lambda *shape: pl.BlockSpec(shape, lambda t: (0, 0))
    across = lambda rows: pl.BlockSpec((rows, tile), lambda t: (0, t))
    shape = jax.ShapeDtypeStruct
    return pl.pallas_call(
        mlp_kernel,
        grid=(hidden // tile,),
        in_specs=[
            fixed(count, width),
            fixed(count, width),
            fixed(width, count),
            fixed(width, count),
            across(width),
            pl.BlockSpec((tile, width), lambda t: (t, 0)),
            across(1),
        ],
        out_specs=[fixed(count, width), fixed(count, width), across(half), across(half), across(half), across(half), across(1)],
        out_shape=[
            shape((count, width), F32),
            shape((count, width), F32),
            shape((half, hidden), F32),
            shape((half, hidden), BF16),
            shape((half, hidden), F32),
            shape((half, hidden), BF16),
            shape((1, hidden), F32),
        ],
        compiler_params=pltpu.CompilerParams(vmem_limit_bytes=56 << 20),
        cost_estimate=pl.CostEstimate(
            flops=12 * count * width * hidden,
            bytes_accessed=10 * width * hidden,
            transcendentals=count * hidden,
        ),
    )(normed, grad_out, normed_turned, grad_turned, up, down, bias)


def turn_halves(values, groups, mine):
    count, width = values.shape
    view = values.T.reshape(groups, 2, width // (2 * groups), count)
    keep = lax.dynamic_index_in_dim(view, mine, 1, keepdims=False).reshape(width // 2, count)
    send = lax.dynamic_index_in_dim(view, 1 - mine, 1, keepdims=False).reshape(width // 2, count)
    return jnp.concatenate([keep, send], axis=0)


STAGES = 4


def mlp_reduce_kernel(
    tiles,
    normed,
    grad_out,
    normed_turned,
    grad_turned,
    up0,
    up1,
    up2,
    up3,
    down0,
    down1,
    down2,
    down3,
    bias,
    out_sum,
    grad_sum,
    bias_sum,
    up_total,
    down_total,
    up_mine,
    down_mine,
    up_core,
    down_core,
    up_core_got,
    down_core_got,
    up_half,
    down_half,
    up_out,
    down_out,
    up_got,
    down_got,
    up_quarter,
    down_quarter,
    up_last,
    down_last,
    up_last_got,
    down_last_got,
    chip_full,
    chip_out,
    chip_got,
    core_sent,
    core_came,
    seq_sent,
    seq_came,
    last_sent,
    last_came,
    chip_sent,
    chip_came,
):
    step = pl.program_id(0)
    seq, row = lax.axis_index("seq"), lax.axis_index("rows")
    half = normed_turned.shape[0] // 2
    x, y = lax.rem(seq, 2), lax.div(seq, 2)
    core_peer = {"rows": row + 1 - 2 * lax.rem(row, 2)}
    x_peer = {"seq": seq + 1 - 2 * x}
    y_peer = {"seq": seq + 2 - 4 * y}
    chip, core = lax.div(row, 2), lax.rem(row, 2)
    to_chip = [lax.rem(chip + k, 4) for k in range(4)]
    chip_peers = [{"rows": 2 * to_chip[k] + core} for k in range(4)]

    @pl.when(step == 0)
    def _():
        barrier = pltpu.get_barrier_semaphore()
        for peer in (core_peer, x_peer, y_peer, *chip_peers[1:]):
            pl.semaphore_signal(barrier, inc=1, device_id=peer, device_id_type=pl.DeviceIdType.MESH)
        pl.semaphore_wait(barrier, 6)

    def copies(source, target, sent, came, slot, kind, device):
        return pltpu.make_async_remote_copy(
            src_ref=source.at[slot],
            dst_ref=target.at[slot],
            send_sem=sent.at[kind, slot],
            recv_sem=came.at[kind, slot],
            device_id=device,
            device_id_type=pl.DeviceIdType.MESH,
        )

    def to_core(slot):
        return (
            copies(up_core, up_core_got, core_sent, core_came, slot, 0, core_peer),
            copies(down_core, down_core_got, core_sent, core_came, slot, 1, core_peer),
        )

    def to_seq(slot):
        return (
            copies(up_out, up_got, seq_sent, seq_came, slot, 0, x_peer),
            copies(down_out, down_got, seq_sent, seq_came, slot, 1, y_peer),
        )

    def to_last(slot):
        return (
            copies(up_last, up_last_got, last_sent, last_came, slot, 0, y_peer),
            copies(down_last, down_last_got, last_sent, last_came, slot, 1, x_peer),
        )

    def to_chips(slot):
        return [
            pltpu.make_async_remote_copy(
                src_ref=chip_out.at[slot, to_chip[k]],
                dst_ref=chip_got.at[slot, k - 1],
                send_sem=chip_sent.at[k - 1, slot],
                recv_sem=chip_came.at[k - 1, slot],
                device_id=chip_peers[k],
                device_id_type=pl.DeviceIdType.MESH,
            )
            for k in range(1, 4)
        ]

    @pl.when(step >= 4)
    def _():
        slot = lax.rem(step, 2)
        for copy in to_chips(slot):
            copy.wait()
        for kind, total in enumerate((up_total, down_total)):
            value = chip_full[slot, chip, kind]
            for k in range(3):
                value = value + chip_got[slot, k, kind].astype(F32)
            total[...] = value

    @pl.when((step >= 3) & (step < tiles + 3))
    def _():
        slot = lax.rem(step + 1, 2)
        for copy in to_last(slot):
            copy.wait()
        size = half // 4
        ups = up_quarter[slot] + up_last_got[slot].astype(F32)
        downs = down_quarter[slot] + down_last_got[slot].astype(F32)
        for place in range(4):
            up_block = ups[place * size : (place + 1) * size]
            down_block = downs[:, place * 128 : (place + 1) * 128]
            chip_full[slot, place, 0] = up_block
            chip_full[slot, place, 1] = down_block
            chip_out[slot, place, 0] = up_block.astype(BF16)
            chip_out[slot, place, 1] = down_block.astype(BF16)
        for copy in to_chips(slot):
            copy.start()

    @pl.when((step >= 2) & (step < tiles + 2))
    def _():
        slot = lax.rem(step, 2)
        for copy in to_seq(slot):
            copy.wait()
        up_quarter[slot] = up_half[slot, y] + up_got[slot, y].astype(F32)
        up_last[slot] = (up_half[slot, 1 - y] + up_got[slot, 1 - y].astype(F32)).astype(BF16)
        down_quarter[slot] = down_half[slot, x] + down_got[slot, x].astype(F32)
        down_last[slot] = (down_half[slot, 1 - x] + down_got[slot, 1 - x].astype(F32)).astype(BF16)
        for copy in to_last(slot):
            copy.start()

    @pl.when((step >= 1) & (step <= tiles))
    def _():
        slot = lax.rem(step + 1, 2)
        for copy in to_core(slot):
            copy.wait()
        for other in range(2):
            kept, gone = 2 * other + x, 2 * other + 1 - x
            up_half[slot, other] = up_mine[slot, kept] + up_core_got[slot, kept].astype(F32)
            up_out[slot, other] = (up_mine[slot, gone] + up_core_got[slot, gone].astype(F32)).astype(BF16)
            kept, gone = 2 * y + other, 2 * (1 - y) + other
            down_half[slot, other] = down_mine[slot, kept] + down_core_got[slot, kept].astype(F32)
            down_out[slot, other] = (down_mine[slot, gone] + down_core_got[slot, gone].astype(F32)).astype(BF16)
        for copy in to_seq(slot):
            copy.start()

    @pl.when(step < tiles)
    def _():
        slot = lax.rem(step, 2)
        up = jnp.concatenate([up0[...], up1[...], up2[...], up3[...]], axis=1)
        down = jnp.concatenate([down0[...], down1[...], down2[...], down3[...]], axis=0)
        biases = jnp.concatenate([bias[owner] for owner in range(4)], axis=1)
        c0 = math.sqrt(2 / math.pi)
        c1 = c0 * 0.044715
        hidden = jnp.dot(normed[...], up, preferred_element_type=F32) + biases
        square = hidden * hidden
        gate = 0.5 + 0.5 * jnp.tanh(hidden * (c0 + c1 * square))
        raised = hidden * gate
        slope = gate + raised * (1.0 - gate) * (2 * c0 + 6 * c1 * square)
        active = raised.astype(BF16)
        down_part = jnp.dot(grad_turned[...], active, preferred_element_type=F32)
        for owner in range(4):
            size = half // 4
            down_mine[slot, owner] = down_part[owner * size : (owner + 1) * size]
            down_core[slot, owner] = down_part[half + owner * size : half + (owner + 1) * size].astype(BF16)
        to_core(slot)[1].start()
        back = (((1,), (1,)), ((), ()))
        grad_active = lax.dot_general(grad_out[...], down, back, preferred_element_type=F32)
        grad_wide = (grad_active * slope).astype(BF16)
        up_part = jnp.dot(normed_turned[...], grad_wide, preferred_element_type=F32)
        for owner in range(4):
            columns = slice(owner * 128, (owner + 1) * 128)
            up_mine[slot, owner] = up_part[:half, columns]
            up_core[slot, owner] = up_part[half:, columns].astype(BF16)
        to_core(slot)[0].start()
        sums = jnp.sum(grad_wide.astype(F32), axis=0, keepdims=True)
        for owner in range(4):
            bias_sum[owner] = sums[:, owner * 128 : (owner + 1) * 128]
        out_part = jnp.dot(active, down, preferred_element_type=F32)
        grad_part = lax.dot_general(grad_wide, up, back, preferred_element_type=F32)

        @pl.when(step == 0)
        def _():
            out_sum[...] = out_part
            grad_sum[...] = grad_part

        @pl.when(step > 0)
        def _():
            out_sum[...] += out_part
            grad_sum[...] += grad_part


def feed_forward_reduce(normed, grad_out, normed_turned, grad_turned, up, down, bias):
    count, width = normed.shape
    hidden = up.shape[1]
    part = hidden // 4
    tiles = part // 128
    half, quarter = width // 2, width // 8
    last = tiles - 1
    shape = jax.ShapeDtypeStruct
    fixed = lambda *dims: pl.BlockSpec(dims, lambda t: (0, 0), pipeline_mode=pl.Buffered(buffer_count=1))
    result = lambda *dims: pl.BlockSpec(dims, lambda t: (0, 0))
    done = lambda t: jnp.maximum(t - STAGES, 0)

    def up_block(owner):
        return pl.BlockSpec((width, 128), lambda t: (0, owner * tiles + jnp.minimum(t, last)))

    def down_block(owner):
        return pl.BlockSpec((128, width), lambda t: (owner * tiles + jnp.minimum(t, last), 0))

    bias_block = pl.BlockSpec((4, 1, 128), lambda t: (0, 0, jnp.minimum(t, last)))
    pair = lambda dtype, *dims: pltpu.VMEM((2,) + dims, dtype)
    return pl.pallas_call(
        partial(mlp_reduce_kernel, tiles),
        grid=(tiles + STAGES,),
        in_specs=[fixed(count, width), fixed(count, width), fixed(width, count), fixed(width, count)]
        + [up_block(owner) for owner in range(4)]
        + [down_block(owner) for owner in range(4)]
        + [bias_block],
        out_specs=[
            result(count, width),
            result(count, width),
            bias_block,
            pl.BlockSpec((quarter, 128), lambda t: (0, done(t))),
            pl.BlockSpec((quarter, 128), lambda t: (0, done(t))),
        ],
        out_shape=[
            shape((count, width), F32),
            shape((count, width), F32),
            shape((4, 1, part), F32),
            shape((quarter, part), F32),
            shape((quarter, part), F32),
        ],
        scratch_shapes=[
            pair(F32, 4, half, 128),
            pair(F32, 4, quarter, 512),
            pair(BF16, 4, half, 128),
            pair(BF16, 4, quarter, 512),
            pair(BF16, 4, half, 128),
            pair(BF16, 4, quarter, 512),
            pair(F32, 2, half, 128),
            pair(F32, 2, quarter, 512),
            pair(BF16, 2, half, 128),
            pair(BF16, 2, quarter, 512),
            pair(BF16, 2, half, 128),
            pair(BF16, 2, quarter, 512),
            pair(F32, half, 128),
            pair(F32, quarter, 512),
            pair(BF16, half, 128),
            pair(BF16, quarter, 512),
            pair(BF16, half, 128),
            pair(BF16, quarter, 512),
            pair(F32, 4, 2, quarter, 128),
            pair(BF16, 4, 2, quarter, 128),
            pair(BF16, 3, 2, quarter, 128),
        ]
        + [pltpu.SemaphoreType.DMA((2, 2))] * 6
        + [pltpu.SemaphoreType.DMA((3, 2))] * 2,
        compiler_params=pltpu.CompilerParams(collective_id=1, has_side_effects=True, vmem_limit_bytes=56 << 20),
        cost_estimate=pl.CostEstimate(
            flops=12 * count * width * hidden,
            bytes_accessed=6 * width * hidden,
            transcendentals=count * hidden,
        ),
    )(normed, grad_out, normed_turned, grad_turned, up, up, up, up, down, down, down, down, bias.reshape(4, 1, part))


def qkv_weight_kernel(grad, normed, keep_ref, send_ref, sum_ref, total, turned):
    step = pl.program_id(0)
    chips, depth = lax.axis_size("rows") // 2, total.shape[1] // lax.axis_size("rows")
    mine = lax.rem(lax.axis_index("rows"), 2)
    part = jnp.dot(grad[0], normed[0], preferred_element_type=F32)
    sums = jnp.sum(grad[0].astype(F32), axis=1, keepdims=True)

    @pl.when(step == 0)
    def _():
        total[...] = part
        sum_ref[...] = sums

    @pl.when(step > 0)
    def _():
        total[...] += part
        sum_ref[...] += sums

    @pl.when(step == pl.num_programs(0) - 1)
    def _():
        turned[...] = total[...].T
        for chip in range(chips):
            first = pl.multiple_of((2 * chip + mine) * depth, 8)
            other = pl.multiple_of((2 * chip + 1 - mine) * depth, 8)
            keep_ref[chip] = turned[pl.ds(first, depth), :]
            send_ref[chip] = turned[pl.ds(other, depth), :].astype(BF16)


def qkv_weight_grad(grad, normed):
    rows, features, length = grad.shape
    width = normed.shape[2]
    groups = lax.axis_size("rows")
    shape = (groups // 2, width // groups, features)
    return pl.pallas_call(
        qkv_weight_kernel,
        grid=(rows,),
        in_specs=[
            pl.BlockSpec((1, features, length), lambda r: (r, 0, 0)),
            pl.BlockSpec((1, length, width), lambda r: (r, 0, 0)),
        ],
        out_specs=[
            pl.BlockSpec(shape, lambda r: (0, 0, 0)),
            pl.BlockSpec(shape, lambda r: (0, 0, 0)),
            pl.BlockSpec((features, 1), lambda r: (0, 0)),
        ],
        out_shape=[
            jax.ShapeDtypeStruct(shape, F32),
            jax.ShapeDtypeStruct(shape, BF16),
            jax.ShapeDtypeStruct((features, 1), F32),
        ],
        scratch_shapes=[pltpu.VMEM((features, width), F32), pltpu.VMEM((width, features), F32)],
        compiler_params=pltpu.CompilerParams(vmem_limit_bytes=VMEM_LIMIT),
        cost_estimate=pl.CostEstimate(
            flops=2 * rows * length * width * features,
            bytes_accessed=2 * rows * length * (width + features) + 6 * width * features // 2,
            transcendentals=0,
        ),
    )(grad, normed)


def tail_kernel(
    images,
    mod,
    weight,
    cond,
    ada_ref,
    cond_ref,
    bias_ref,
    got,
    low_mine,
    low_got,
    row_mine,
    row_got,
    cond_mine,
    cond_got,
    column_got,
    sent,
    arrived,
):
    seq_count, row_total = lax.axis_size("seq"), lax.axis_size("rows")
    seq, row = lax.axis_index("seq"), lax.axis_index("rows")
    to_seq = [lax.rem(seq + m, seq_count) for m in range(seq_count)]
    to_row = [lax.rem(row + m, row_total) for m in range(row_total)]
    barrier = pltpu.get_barrier_semaphore()
    for m in range(1, seq_count):
        pl.semaphore_signal(barrier, inc=1, device_id={"seq": to_seq[m]}, device_id_type=pl.DeviceIdType.MESH)
    for m in range(1, row_total):
        pl.semaphore_signal(barrier, inc=1, device_id={"rows": to_row[m]}, device_id_type=pl.DeviceIdType.MESH)
    pl.semaphore_wait(barrier, seq_count + row_total - 2)

    used = [0]

    def start(source, target, device):
        copy = pltpu.make_async_remote_copy(
            src_ref=source,
            dst_ref=target,
            send_sem=sent.at[used[0]],
            recv_sem=arrived.at[used[0]],
            device_id=device,
            device_id_type=pl.DeviceIdType.MESH,
        )
        used[0] += 1
        copy.start()
        return copy

    copies = [start(mod.at[to_seq[m]], got.at[m], {"seq": to_seq[m]}) for m in range(1, seq_count)]
    column_got[0] = cond[row]
    column_copies = [start(cond.at[to_row[m]], column_got.at[m], {"rows": to_row[m]}) for m in range(1, row_total)]
    total = mod[seq]
    for m, copy in enumerate(copies):
        copy.wait()
        total = total + got[m + 1]
    low = total[:images].astype(BF16)
    low_mine[...] = low
    row_mine[...] = total[images:]
    row_mine[0:1] = jnp.sum(total[:images], axis=0, keepdims=True)
    low_got[0] = low
    copies = [start(low_mine, low_got.at[m], {"rows": to_row[m]}) for m in range(1, row_total)]
    copies += [start(row_mine, row_got.at[m], {"rows": to_row[m]}) for m in range(1, row_total)]
    term = lax.dot_general(low, weight[...], (((1,), (1,)), ((), ())), preferred_element_type=F32)
    cond_mine[...] = term
    cond_copies = [start(cond_mine, cond_got.at[m], {"seq": to_seq[m]}) for m in range(1, seq_count)]
    for copy in copies:
        copy.wait()
    sums = row_mine[...]
    for m in range(1, row_total):
        sums = sums + row_got[m]
    bias_ref[seq] = sums
    copies = [start(bias_ref.at[seq], bias_ref.at[seq], {"seq": to_seq[m]}) for m in range(1, seq_count)]
    for copy in column_copies:
        copy.wait()
    gathered = jnp.concatenate([low_got[m] for m in range(row_total)], axis=0)
    columns = jnp.concatenate([column_got[m] for m in range(row_total)], axis=0)
    ada_ref[...] = lax.dot_general(columns, gathered, (((0,), (0,)), ((), ())), preferred_element_type=F32)
    for m, copy in enumerate(cond_copies):
        copy.wait()
        term = term + cond_got[m + 1]
    cond_ref[...] = term
    for copy in copies:
        copy.wait()


def finish(mod, weight, cond, images):
    seq_count, lines, columns = mod.shape
    width, depth = weight.shape[0], cond.shape[2]
    row_total = lax.axis_size("rows")
    extra = lines - images
    copies = 3 * (seq_count - 1) + 3 * (row_total - 1)
    return pl.pallas_call(
        partial(tail_kernel, images),
        in_specs=[pl.BlockSpec(memory_space=pltpu.VMEM)] * 3,
        out_specs=[pl.BlockSpec(memory_space=pltpu.VMEM)] * 3,
        out_shape=[
            jax.ShapeDtypeStruct((depth, columns), F32),
            jax.ShapeDtypeStruct((images, width), F32),
            jax.ShapeDtypeStruct((seq_count, extra, columns), F32),
        ],
        scratch_shapes=[
            pltpu.VMEM((seq_count, lines, columns), F32),
            pltpu.VMEM((images, columns), BF16),
            pltpu.VMEM((row_total, images, columns), BF16),
            pltpu.VMEM((extra, columns), F32),
            pltpu.VMEM((row_total, extra, columns), F32),
            pltpu.VMEM((images, width), F32),
            pltpu.VMEM((seq_count, images, width), F32),
            pltpu.VMEM((row_total, images, depth), BF16),
            pltpu.SemaphoreType.DMA((copies,)),
            pltpu.SemaphoreType.DMA((copies,)),
        ],
        compiler_params=pltpu.CompilerParams(collective_id=0, has_side_effects=True, vmem_limit_bytes=VMEM_LIMIT),
        cost_estimate=pl.CostEstimate(flops=10**9, bytes_accessed=10**7, transcendentals=0),
    )(mod, weight, cond)


def gather_seq(values):
    count = lax.axis_size("seq")
    if count == 4:
        first, second = swap(values, "seq", 1), swap(values, "seq", 2)
        half = values.shape[0] // 2
        third = jnp.concatenate([swap(second[:half], "seq", 1), swap(first[half:], "seq", 2)], axis=0)
        return [values, first, second, third]
    return [values] + [swap(values, "seq", m) for m in range(1, count)]


def exchange_seq(blocks):
    return [blocks[0]] + [swap(blocks[m], "seq", m) for m in range(1, len(blocks))]


def in_order(blocks, axis):
    index = lax.axis_index("seq")
    stacked = jnp.stack(blocks, axis=axis)
    return flip_blocks(stacked, axis, index)


class Halving:
    def __init__(self, blocks, low_first):
        self.blocks = dict(enumerate(blocks))
        bits = [1 << k for k in range(len(blocks).bit_length() - 1)]
        self.bits = bits if low_first else bits[::-1]

    def send(self):
        self.bit = self.bits.pop(0)
        self.kept = [m for m in self.blocks if not m & self.bit]
        return jnp.stack([self.blocks[m | self.bit] for m in self.kept]).astype(BF16)

    def move(self, sent):
        return swap(sent, "seq", self.bit)

    def add(self, came):
        self.blocks = {m: self.blocks[m] + came[k].astype(F32) for k, m in enumerate(self.kept)}


class Spreading:
    def __init__(self, pick):
        chip, chips = lax.axis_index("rows") // 2, lax.axis_size("rows") // 2
        self.own = pick(chip)
        self.sent = [pick(chip ^ m).astype(BF16) for m in range(1, chips)]

    def move(self):
        self.came = [swap(block, "rows", 2 * (m + 1)) for m, block in enumerate(self.sent)]

    def total(self):
        total = self.own
        for block in self.came:
            total = total + block.astype(F32)
        return total


def columns_of(values, index, size):
    return lax.dynamic_slice_in_dim(values, index * size, size, values.ndim - 1)


def lines_of(values, index, size):
    return lax.dynamic_slice_in_dim(values, index * size, size, 0)


def tied(*values):
    return lax.optimization_barrier(values)


def on_device(
    tokens,
    conditioning,
    segment_ids,
    image_index,
    row_fill,
    ada_weight,
    ada_bias,
    qkv_weight,
    qv_bias,
    proj_weight,
    proj_bias,
    up_weight,
    up_bias,
    down_weight,
    down_bias,
    cotangent,
):
    row_count, local_len, width = tokens.shape
    seq_count, groups = lax.axis_size("seq"), lax.axis_size("rows")
    seq_index, row_index = lax.axis_index("seq"), lax.axis_index("rows")
    chips, core = groups // 2, row_index % 2
    full_len = local_len * seq_count
    token_count = row_count * local_len
    heads_dev = HEADS // seq_count
    head_size = width // HEADS
    own = heads_dev * head_size
    image_count = conditioning.shape[0]
    hidden_size = up_weight.shape[1]
    depth = width // groups

    tokens_all = jnp.concatenate(gather_seq(tokens), axis=1)
    order = lax.iota(jnp.int32, seq_count) ^ seq_index
    seg_blocks = flip_blocks(segment_ids.reshape(row_count, seq_count, local_len), 1, seq_index)
    seg_all = seg_blocks.reshape(row_count, full_len)
    places = (order[:, None] * local_len + lax.iota(jnp.int32, local_len)).reshape(1, full_len)
    codes = jnp.where(places < row_fill[:, None], seg_all, -1 - places)
    code_col, code_row = codes[:, :, None], codes[:, None, :]

    qkv_own = jnp.concatenate(
        [lax.dynamic_slice_in_dim(qkv_weight, part * width + seq_index * own, own, 1).T for part in range(3)], axis=0
    )
    bias_own = lax.dynamic_slice_in_dim(qv_bias.astype(F32), seq_index * own, own, 1)
    bias_own = jnp.concatenate([bias_own[0], jnp.zeros((own,), F32), bias_own[1]])

    cond_wide = conditioning.astype(F32)
    cond_low = jax.nn.silu(cond_wide).astype(BF16)
    mod_part = jnp.dot(cond_low, ada_weight, preferred_element_type=F32)
    modulation = lax.all_gather(mod_part, "seq", axis=1, tiled=True) + ada_bias.astype(F32)
    cond_cols = cond_low.reshape(image_count, groups, depth).transpose(1, 0, 2)
    local_seg = lax.dynamic_slice_in_dim(segment_ids, seq_index * local_len, local_len, 1)
    slot_ids = lax.iota(jnp.int32, image_index.shape[1])
    slot_mod = jnp.take(modulation, image_index, axis=0)

    normed_all, packed = project_qkv(
        tokens_all, seg_all, slot_mod[:, :, : 2 * width], qkv_own, bias_own, heads_dev, min(256, full_len)
    )
    square = seq_count == 4 and chips == 4
    attended, log_totals, *attended_sent = attend(packed, code_col, code_row, 512, square)

    slot_pick = (local_seg[:, :, None] == slot_ids).astype(F32)
    mod_tok = jnp.einsum("rts,rse->rte", slot_pick, slot_mod, precision=lax.Precision.HIGHEST)
    shift_a, scale_a, gate_a, shift_b, scale_b, gate_b = jnp.split(mod_tok, 6, axis=-1)
    tokens_wide = tokens.astype(F32)
    upstream = cotangent.astype(F32)
    grad_branch_b = (upstream * gate_b).astype(BF16)
    part_down_bias = jnp.sum(grad_branch_b.astype(F32), axis=(0, 1))
    grad_out = grad_branch_b.reshape(token_count, width)
    grad_turned = turn_halves(grad_out, seq_count, core)

    def by_block(values):
        return [values[..., m * local_len : (m + 1) * local_len] for m in range(seq_count)]

    if square:
        attended_tok = attended_sent[0]
    else:
        attended_tok = in_order(exchange_seq(by_block(attended.reshape(row_count, own, full_len))), 1)
    attended_tok = attended_tok.reshape(row_count, width, local_len)
    branch_a = jnp.einsum(
        "rft,fe->rte", attended_tok, proj_weight, preferred_element_type=F32
    ) + proj_bias.astype(F32)
    middle = tokens_wide + gate_a * branch_a
    normed_b = modulate(middle, shift_b, scale_b).astype(BF16).reshape(token_count, width)
    normed_turned = turn_halves(normed_b, chips, core)

    if square:
        out_sum, grad_sum, part_up_bias, grad_up_weight, down_turned = feed_forward_reduce(
            normed_b, grad_out, normed_turned, grad_turned, up_weight, down_weight, up_bias.astype(F32)
        )
        part_up_bias = part_up_bias.reshape(1, hidden_size)
    else:
        out_sum, grad_sum, up_keep, up_send, down_keep, down_send, part_up_bias = feed_forward(
            normed_b, grad_out, normed_turned, grad_turned, up_weight, down_weight, up_bias.astype(F32)[None], 512
        )
        up_came, down_came = swap(up_send, "rows", 1), swap(down_send, "rows", 1)
    branch_b = out_sum.reshape(row_count, local_len, width) + down_bias.astype(F32)
    grad_normed_b = grad_sum.reshape(row_count, local_len, width)
    block_out = (middle + gate_b * branch_b).astype(BF16)
    grad_gate_b = upstream * branch_b
    _, norm_back_b = jax.vjp(modulate, middle, shift_b, scale_b)
    grad_mid_norm, grad_shift_b, grad_scale_b = norm_back_b(grad_normed_b)
    grad_middle = upstream + grad_mid_norm
    grad_branch_a = (grad_middle * gate_a).astype(BF16)
    grad_gate_a = grad_middle * branch_a
    part_proj_bias = jnp.sum(grad_branch_a.astype(F32), axis=(0, 1))
    grad_attended = jnp.einsum(
        "fe,rte->rft", proj_weight, grad_branch_a, preferred_element_type=F32
    ).astype(BF16)
    heads_blocks = [lax.dynamic_slice_in_dim(grad_attended, (seq_index ^ m) * own, own, 1) for m in range(seq_count)]
    grad_heads_in = jnp.concatenate(exchange_seq(heads_blocks), axis=2)
    grad_view = grad_heads_in.reshape(row_count, heads_dev, head_size, full_len)

    part_proj = jnp.einsum("rte,rft->ef", grad_branch_a, attended_tok, preferred_element_type=F32)
    proj_view = part_proj.reshape(seq_count, 2, depth * groups // (2 * seq_count), width)
    proj_keep = lax.dynamic_index_in_dim(proj_view, core, 1, keepdims=False)
    proj_send = lax.dynamic_index_in_dim(proj_view, 1 - core, 1, keepdims=False).astype(BF16)
    proj_came = swap(proj_send, "rows", 1).reshape(width // 2, width)
    proj_keep = proj_keep.reshape(width // 2, width)
    up_size, down_size = hidden_size // seq_count, width // (2 * seq_count)
    proj_blocks = [
        lines_of(proj_keep, seq_index ^ m, down_size) + lines_of(proj_came, seq_index ^ m, down_size).astype(F32)
        for m in range(seq_count)
    ]
    if square:
        proj_sent = [block.astype(BF16) for block in proj_blocks[1:]]
        grad_view, *proj_sent = tied(grad_view, *proj_sent)
        proj_total = proj_blocks[0]
        for m in range(1, seq_count):
            proj_total = proj_total + swap(proj_sent[m - 1], "seq", m).astype(F32)
    else:
        ups = Halving(
            [
                columns_of(up_keep, seq_index ^ m, up_size) + columns_of(up_came, seq_index ^ m, up_size).astype(F32)
                for m in range(seq_count)
            ],
            True,
        )
        downs = Halving(
            [
                jnp.concatenate(
                    [
                        lines_of(down_keep, seq_index ^ m, down_size)
                        + lines_of(down_came, seq_index ^ m, down_size).astype(F32),
                        proj_blocks[m],
                    ],
                    axis=1,
                )
                for m in range(seq_count)
            ],
            False,
        )
        up_sent, down_sent = ups.send(), downs.send()
        up_came, down_came = ups.move(up_sent), downs.move(down_sent)

    grad_heads, *grad_sent = attend_back(
        packed, attended, grad_view, log_totals, code_col, code_row, 256, 512, square
    )
    grad_own = grad_heads.reshape(row_count, 3 * own, full_len)
    if square:
        grad_flat = grad_sent[0]
    else:
        grad_blocks = exchange_seq(by_block(grad_own))
        grad_flat = in_order([block.reshape(row_count, 3, own, local_len) for block in grad_blocks], 2)
    grad_flat = grad_flat.reshape(row_count, 3 * width, local_len)

    qkv_keep, qkv_send, own_sums = qkv_weight_grad(grad_own, normed_all)
    down_part, proj_part = hidden_size // chips, width // chips
    if square:
        proj_spread = Spreading(lambda chip: columns_of(proj_total, chip, proj_part))
        grad_flat, qkv_send, *proj_spread.sent = tied(grad_flat, qkv_send, *proj_spread.sent)
        proj_spread.move()
    else:
        while ups.bits:
            ups.add(up_came)
            downs.add(down_came)
            up_came, down_came = ups.move(ups.send()), downs.move(downs.send())
        ups.add(up_came)
        downs.add(down_came)
        up_total, down_total = ups.blocks[0], downs.blocks[0][:, :hidden_size]
        proj_total = downs.blocks[0][:, hidden_size:]
        up_spread = Spreading(lambda chip: lines_of(up_total, chip, depth))
        down_spread = Spreading(
            lambda chip: jnp.concatenate(
                [columns_of(down_total, chip, down_part), columns_of(proj_total, chip, proj_part)], axis=1
            )
        )
        up_spread.move()
        down_spread.move()
    qkv_came = swap(qkv_send, "rows", 1)
    grad_normed_a = jnp.einsum("rft,df->rtd", grad_flat, qkv_weight, preferred_element_type=F32)
    _, norm_back_a = jax.vjp(modulate, tokens_wide, shift_a, scale_a)
    grad_tok_norm, grad_shift_a, grad_scale_a = norm_back_a(grad_normed_a)
    grad_tokens = grad_middle + grad_tok_norm
    grad_mod_tok = jnp.concatenate(
        [grad_shift_a, grad_scale_a, grad_gate_a, grad_shift_b, grad_scale_b, grad_gate_b], axis=-1
    )
    slot_grads = jnp.einsum("rts,rte->rse", slot_pick, grad_mod_tok, precision=lax.Precision.HIGHEST)
    image_pick = (image_index[:, :, None] == lax.iota(jnp.int32, image_count)).astype(F32)
    grad_modulation = jnp.einsum("rsi,rse->ie", image_pick, slot_grads, precision=lax.Precision.HIGHEST)

    own_sums = own_sums.reshape(3, own)
    part_qv = lax.dynamic_update_slice(
        jnp.zeros((2, width), F32), jnp.stack([own_sums[0], own_sums[2]]), (0, seq_index * own)
    )
    small = jnp.concatenate([part_qv.reshape(-1), part_proj_bias, part_up_bias[0], part_down_bias])
    columns = ada_weight.shape[1]
    lines = -(-small.size // (seq_count * columns))
    room = seq_count * columns * lines
    small = jnp.pad(small, (0, room - small.size)).reshape(seq_count, lines, columns)
    mod_view = grad_modulation.reshape(image_count, seq_count, columns).transpose(1, 0, 2)
    joined = jnp.concatenate(
        [mod_view, jnp.zeros((seq_count, 1, columns), F32), small, jnp.zeros((seq_count, 7 - lines, columns), F32)], axis=1
    )
    qkv_both = qkv_keep + qkv_came.astype(F32)
    qkv_spread = Spreading(lambda chip: lax.dynamic_index_in_dim(qkv_both, chip, 0, keepdims=False))
    joined, *qkv_spread.sent = tied(joined, *qkv_spread.sent)
    qkv_spread.move()
    if square:
        turned = jnp.concatenate([down_turned, proj_spread.total()], axis=1)
    else:
        grad_up_weight, turned = up_spread.total(), down_spread.total()
    half = down_part // 2
    cut = lambda index: jnp.concatenate(
        [columns_of(turned[:, :down_part], index, half), columns_of(turned[:, down_part:], index, proj_part // 2)], axis=1
    )
    core_keep, core_sent = cut(core), cut(1 - core)
    joined, core_sent = tied(joined, core_sent)
    core_came = swap(core_sent, "rows", 1)
    grad_ada_weight, cond_sum, bias_sums = finish(joined, ada_weight, cond_cols, image_count)
    _, silu_back = jax.vjp(jax.nn.silu, cond_wide)
    grad_cond = silu_back(cond_sum)[0]
    grad_ada_bias = bias_sums[:, 0].reshape(-1)
    small = bias_sums[:, 1 : 1 + lines].reshape(-1)
    grad_qv_bias = small[: 2 * width].reshape(2, width)
    grad_proj_bias = small[2 * width : 3 * width]
    grad_up_bias = small[3 * width : 3 * width + hidden_size]
    grad_down_bias = small[3 * width + hidden_size : 4 * width + hidden_size]

    pair = flip_blocks(jnp.stack([core_keep, core_came]), 0, core).reshape(-1, core_keep.shape[1])
    grad_down_weight, grad_proj_weight = pair[:, :half].T, pair[:, half:].T

    qkv_total = qkv_spread.total()
    pieces = []
    for place in range(3):
        pairs = [((3 * target + place) % seq_count, target) for target in range(seq_count)]
        part_of = [0] * seq_count
        for source, target in pairs:
            part_of[source] = (3 * target + place) // seq_count
        chosen = columns_of(qkv_total, jnp.array(part_of, jnp.int32)[seq_index], own)
        pieces.append(lax.ppermute(chosen, "seq", pairs))
    grad_qkv_weight = jnp.concatenate(pieces, axis=1)
    return (
        block_out,
        grad_tokens,
        grad_cond,
        grad_ada_weight,
        grad_ada_bias,
        grad_qkv_weight,
        grad_qv_bias,
        grad_proj_weight,
        grad_proj_bias,
        grad_up_weight,
        grad_up_bias,
        grad_down_weight,
        grad_down_bias,
    )


def solution(mesh):
    in_specs = (
        P("rows", "seq", None),
        P("rows", None),
        P("rows", None),
        P("rows", None),
        P("rows"),
        P(None, "seq"),
        P(),
        P(),
        P(),
        P(),
        P(),
        P(),
        P(),
        P(),
        P(),
        P("rows", "seq", None),
    )
    out_specs = (
        P("rows", "seq", None),
        P("rows", "seq", None),
        P("rows", None),
        P("rows", "seq"),
        P(),
        P("rows", "seq"),
        P(),
        P("rows", "seq"),
        P(),
        P("rows", "seq"),
        P(),
        P("rows", "seq"),
        P(),
    )
    return jax.shard_map(
        on_device, mesh=mesh, in_specs=in_specs, out_specs=out_specs, check_vma=False
    )
```

```python
from functools import partial
import math

import jax
import jax.numpy as jnp
from jax import lax
from jax.experimental import pallas as pl
from jax.experimental.pallas import tpu as pltpu
from jax.sharding import PartitionSpec as P

HEADS = 16
LOG2E = math.log2(math.e)
VMEM_LIMIT = 48 << 20
BF16 = jnp.bfloat16
F32 = jnp.float32

norm_eps = 1e-06


def modulate(values, offset, factor):
    center = values - jnp.mean(values, axis=-1, keepdims=True)
    spread = jnp.mean(center * center, axis=-1, keepdims=True)
    return center * lax.rsqrt(spread + norm_eps) * (1.0 + factor) + offset


def gelu_tanh(values):
    return jax.nn.gelu(values, approximate=True)


def swap(values, axis, mask):
    count = lax.axis_size(axis)
    return lax.ppermute(values, axis, [(i, i ^ mask) for i in range(count)])


def flip_blocks(values, axis, mask):
    return jnp.take(values, lax.iota(jnp.int32, values.shape[axis]) ^ mask, axis=axis)


def qkv_kernel(slot_row, seg, mod, tokens, weight, bias, normed_ref, qkv_ref):
    width = tokens.shape[-1]
    values = tokens[0].astype(F32)
    picked = (seg[0] == slot_row[...]).astype(BF16)
    table = mod[0]
    high = table.astype(BF16)
    rest = table - high.astype(F32)
    middle = rest.astype(BF16)
    last = (rest - middle.astype(F32)).astype(BF16)
    stacked = jnp.concatenate([high, middle, last], axis=0)
    per_token = jnp.dot(picked, stacked, preferred_element_type=F32)
    normed = modulate(values, per_token[:, :width], per_token[:, width:]).astype(BF16)
    normed_ref[0] = normed
    mixed = lax.dot_general(weight[...], normed, (((1,), (1,)), ((), ())), preferred_element_type=F32)
    mixed = (mixed + bias[...]).astype(BF16)
    _, parts, heads, size, _ = qkv_ref.shape
    for part in range(parts):
        for head in range(heads):
            start = (part * heads + head) * size
            qkv_ref[0, part, head] = mixed[start : start + size]


def project_qkv(tokens, seg, slot_mod, weight, bias, heads, block):
    rows, length, width = tokens.shape
    slots = slot_mod.shape[1]
    features = weight.shape[0]
    size = features // (3 * heads)
    slot_row = jnp.tile(lax.iota(jnp.int32, slots), 3)[None]
    return pl.pallas_call(
        qkv_kernel,
        grid=(rows, length // block),
        in_specs=[
            pl.BlockSpec((1, 3 * slots), lambda r, t: (0, 0)),
            pl.BlockSpec((1, block, 1), lambda r, t: (r, t, 0)),
            pl.BlockSpec((1, slots, 2 * width), lambda r, t: (r, 0, 0)),
            pl.BlockSpec((1, block, width), lambda r, t: (r, t, 0)),
            pl.BlockSpec((features, width), lambda r, t: (0, 0)),
            pl.BlockSpec((features, 1), lambda r, t: (0, 0)),
        ],
        out_specs=[
            pl.BlockSpec((1, block, width), lambda r, t: (r, t, 0)),
            pl.BlockSpec((1, 3, heads, size, block), lambda r, t: (r, 0, 0, 0, t)),
        ],
        out_shape=[
            jax.ShapeDtypeStruct((rows, length, width), BF16),
            jax.ShapeDtypeStruct((rows, 3, heads, size, length), BF16),
        ],
        compiler_params=pltpu.CompilerParams(vmem_limit_bytes=VMEM_LIMIT),
        cost_estimate=pl.CostEstimate(
            flops=2 * rows * length * width * features,
            bytes_accessed=2 * rows * length * (2 * width + features),
            transcendentals=0,
        ),
    )(slot_row, seg[:, :, None], slot_mod, tokens, weight, bias[:, None])


def peers_of(seq):
    x, y = lax.rem(seq, 2), lax.div(seq, 2)
    return [seq + 1 - 2 * x, seq + 2 - 4 * y, 3 - seq]


def greet(devices):
    barrier = pltpu.get_barrier_semaphore()
    for device in devices:
        pl.semaphore_signal(barrier, inc=1, device_id=device, device_id_type=pl.DeviceIdType.MESH)
    pl.semaphore_wait(barrier, len(devices))


def send_block(source, target, sent, came, index, device):
    return pltpu.make_async_remote_copy(
        src_ref=source,
        dst_ref=target,
        send_sem=sent.at[index],
        recv_sem=came.at[index],
        device_id=device,
        device_id_type=pl.DeviceIdType.MESH,
    )


def attend_kernel(block, scale, code_col, code_row, query, key, value, out_ref, lse_ref, token_ref=None, sent=None, came=None, kept=None):
    length = query.shape[-1]
    keys = key[0, 0].astype(F32).T.astype(BF16)
    values = value[0, 0]
    codes = code_col[0]
    row, head = (pl.program_id(0), pl.program_id(1)) if sent is not None else (0, 0)
    rows, heads = out_ref.shape[:2]
    if sent is not None:
        seq = lax.axis_index("seq")
        peers = peers_of(seq)
        size = length // 4

        @pl.when((row == 0) & (head == 0))
        def _():
            greet([{"seq": peer} for peer in peers])

        def to_peer(r, h, m):
            lanes = pl.ds(m * size, size)
            place = (r * heads + h) * 3 + m - 1
            return send_block(out_ref.at[r, h, :, lanes], token_ref.at[r, seq, h], sent, came, place, {"seq": peers[m - 1]})

        def to_self(r, h):
            return pltpu.make_async_copy(out_ref.at[r, h, :, pl.ds(0, size)], token_ref.at[r, seq, h], kept.at[r * heads + h])

    for step in range(length // block):
        here = pl.ds(step * block, block)
        scores = jnp.dot(keys, query[0, 0, :, here], preferred_element_type=F32)
        scores = jnp.where(codes == code_row[0, :, here], scores * scale, -1e30)
        peak = jnp.max(scores, axis=0, keepdims=True)
        raised = jnp.exp2(scores - peak)
        total = jnp.sum(raised, axis=0, keepdims=True)
        probs = (raised * (1.0 / total)).astype(BF16)
        out_ref[row, head, :, here] = jnp.dot(values, probs, preferred_element_type=F32).astype(BF16)
        lse_ref[0, 0, :, here] = peak + jnp.log2(total)

    if sent is not None:
        to_self(row, head).start()
        for m in range(1, 4):
            to_peer(row, head, m).start()

        @pl.when((row == rows - 1) & (head == heads - 1))
        def _():
            for r in range(rows):
                for h in range(heads):
                    to_self(r, h).wait()
                    for m in range(1, 4):
                        to_peer(r, h, m).wait()


def attend(packed, col, row, block, exchange):
    rows, _, heads, size, length = packed.shape
    part = lambda j: pl.BlockSpec((1, None, 1, size, length), lambda r, h: (r, j, h, 0, 0))
    out_specs = [
        pl.BlockSpec((1, 1, size, length), lambda r, h: (r, h, 0, 0)),
        pl.BlockSpec((1, 1, 1, length), lambda r, h: (r, h, 0, 0)),
    ]
    out_shape = [
        jax.ShapeDtypeStruct((rows, heads, size, length), BF16),
        jax.ShapeDtypeStruct((rows, heads, 1, length), F32),
    ]
    scratch = []
    extra = {}
    if exchange:
        out_specs[0] = pl.BlockSpec((rows, heads, size, length), lambda r, h: (0, 0, 0, 0))
        out_specs.append(pl.BlockSpec(memory_space=pl.ANY))
        out_shape.append(jax.ShapeDtypeStruct((rows, 4, heads, size, length // 4), BF16))
        count = rows * heads
        scratch = [pltpu.SemaphoreType.DMA((3 * count,)), pltpu.SemaphoreType.DMA((3 * count,)), pltpu.SemaphoreType.DMA((count,))]
        extra = dict(collective_id=2, has_side_effects=True)
    return pl.pallas_call(
        partial(attend_kernel, block, size**-0.5 * LOG2E),
        grid=(rows, heads),
        in_specs=[
            pl.BlockSpec((1, length, 1), lambda r, h: (r, 0, 0)),
            pl.BlockSpec((1, 1, length), lambda r, h: (r, 0, 0)),
            part(0),
            part(1),
            part(2),
        ],
        out_specs=out_specs,
        out_shape=out_shape,
        scratch_shapes=scratch,
        compiler_params=pltpu.CompilerParams(vmem_limit_bytes=VMEM_LIMIT, **extra),
        cost_estimate=pl.CostEstimate(
            flops=8 * rows * heads * length * length * 128,
            bytes_accessed=8 * rows * heads * length * size,
            transcendentals=rows * heads * length * length,
        ),
    )(col, row, packed, packed, packed)


def attend_back_kernel(
    block,
    inner,
    scale,
    exchange,
    code_col,
    code_row,
    query,
    key,
    value,
    out,
    grad_out,
    lse,
    grad_ref,
    *rest,
):
    length = query.shape[-1]
    size = query.shape[-2]
    row, head = (pl.program_id(0), pl.program_id(1)) if exchange else (0, 0)
    rows, _, heads = grad_ref.shape[:3]
    if exchange:
        token_ref, key_sum, value_sum, keys, values, sent, came, kept = rest
        seq = lax.axis_index("seq")
        peers = peers_of(seq)
        local = length // 4

        @pl.when((row == 0) & (head == 0))
        def _():
            greet([{"seq": peer} for peer in peers])

        def to_peer(r, h, m):
            lanes = pl.ds(m * local, local)
            place = (r * heads + h) * 3 + m - 1
            return send_block(grad_ref.at[r, :, h, :, lanes], token_ref.at[r, :, seq, h], sent, came, place, {"seq": peers[m - 1]})

        def to_self(r, h):
            lanes = pl.ds(0, local)
            return pltpu.make_async_copy(grad_ref.at[r, :, h, :, lanes], token_ref.at[r, :, seq, h], kept.at[r * heads + h])

    else:
        key_sum, value_sum, keys, values = rest
    keys[...] = key[0, 0].astype(F32).T.astype(BF16)
    values[...] = value[0, 0].astype(F32).T.astype(BF16)
    for step in range(length // block):
        here = pl.ds(step * block, block)
        query_low = query[0, 0, :, here]
        grad_low = grad_out[0, 0, :, here]
        query_rows = query_low.astype(F32).T.astype(BF16)
        grad_rows = grad_low.astype(F32).T.astype(BF16)
        row_dot = jnp.sum(grad_low.astype(F32) * out[0, 0, :, here].astype(F32), axis=0, keepdims=True)
        grad_query = jnp.zeros((size, block), F32)
        for part in range(length // inner):
            there = pl.ds(part * inner, inner)
            scores = jnp.dot(keys[there, :], query_low, preferred_element_type=F32)
            scores = jnp.where(code_col[0, there, :] == code_row[0, :, here], scores * (scale * LOG2E), -1e30)
            probs = jnp.exp2(scores - lse[0, 0, :, here])
            grad_probs = jnp.dot(values[there, :], grad_low, preferred_element_type=F32)
            grad_raw = (probs * (grad_probs - row_dot) * scale).astype(BF16)
            value_part = jnp.dot(probs.astype(BF16), grad_rows, preferred_element_type=F32)
            key_part = jnp.dot(grad_raw, query_rows, preferred_element_type=F32)
            if step == 0:
                value_sum[there, :] = value_part
                key_sum[there, :] = key_part
            else:
                value_sum[there, :] += value_part
                key_sum[there, :] += key_part
            grad_query += jnp.dot(key[0, 0, :, there], grad_raw, preferred_element_type=F32)
        grad_ref[row, 0, head, :, here] = grad_query.astype(BF16)
    grad_ref[row, 1, head] = key_sum[...].T.astype(BF16)
    grad_ref[row, 2, head] = value_sum[...].T.astype(BF16)

    if exchange:
        to_self(row, head).start()
        for m in range(1, 4):
            to_peer(row, head, m).start()

        @pl.when((row == rows - 1) & (head == heads - 1))
        def _():
            for r in range(rows):
                for h in range(heads):
                    to_self(r, h).wait()
                    for m in range(1, 4):
                        to_peer(r, h, m).wait()


def attend_back(packed, out, grad_out, lse, col, row, block, inner, exchange):
    rows, _, heads, size, length = packed.shape
    part = lambda j: pl.BlockSpec((1, None, 1, size, length), lambda r, h: (r, j, h, 0, 0))
    whole = pl.BlockSpec((1, 1, size, length), lambda r, h: (r, h, 0, 0))
    out_specs = [pl.BlockSpec((1, 3, 1, size, length), lambda r, h: (r, 0, h, 0, 0))]
    out_shape = [jax.ShapeDtypeStruct((rows, 3, heads, size, length), BF16)]
    scratch = []
    extra = {}
    if exchange:
        out_specs = [
            pl.BlockSpec((rows, 3, heads, size, length), lambda r, h: (0, 0, 0, 0, 0)),
            pl.BlockSpec(memory_space=pl.ANY),
        ]
        out_shape.append(jax.ShapeDtypeStruct((rows, 3, 4, heads, size, length // 4), BF16))
        count = rows * heads
        scratch = [pltpu.SemaphoreType.DMA((3 * count,)), pltpu.SemaphoreType.DMA((3 * count,)), pltpu.SemaphoreType.DMA((count,))]
        extra = dict(collective_id=3, has_side_effects=True)
    return pl.pallas_call(
        partial(attend_back_kernel, block, inner, size**-0.5, exchange),
        grid=(rows, heads),
        in_specs=[
            pl.BlockSpec((1, length, 1), lambda r, h: (r, 0, 0)),
            pl.BlockSpec((1, 1, length), lambda r, h: (r, 0, 0)),
            part(0),
            part(1),
            part(2),
            whole,
            whole,
            pl.BlockSpec((1, 1, 1, length), lambda r, h: (r, h, 0, 0)),
        ],
        out_specs=out_specs,
        out_shape=out_shape,
        scratch_shapes=[
            pltpu.VMEM((length, size), F32),
            pltpu.VMEM((length, size), F32),
            pltpu.VMEM((length, size), BF16),
            pltpu.VMEM((length, size), BF16),
        ]
        + scratch,
        compiler_params=pltpu.CompilerParams(vmem_limit_bytes=VMEM_LIMIT, **extra),
        cost_estimate=pl.CostEstimate(
            flops=20 * rows * heads * length * length * 128,
            bytes_accessed=16 * rows * heads * length * size,
            transcendentals=rows * heads * length * length,
        ),
    )(col, row, packed, packed, packed, out, grad_out, lse)


def mlp_kernel(
    normed, grad_out, normed_turned, grad_turned, up, down, bias, out_sum, grad_sum, up_keep, up_send, down_keep, down_send, bias_sum
):
    step = pl.program_id(0)
    half = up_keep.shape[0]
    c0 = math.sqrt(2 / math.pi)
    c1 = c0 * 0.044715
    hidden = jnp.dot(normed[...], up[...], preferred_element_type=F32) + bias[...]
    square = hidden * hidden
    gate = 0.5 + 0.5 * jnp.tanh(hidden * (c0 + c1 * square))
    raised = hidden * gate
    slope = gate + raised * (1.0 - gate) * (2 * c0 + 6 * c1 * square)
    active = raised.astype(BF16)
    back = (((1,), (1,)), ((), ()))
    grad_active = lax.dot_general(grad_out[...], down[...], back, preferred_element_type=F32)
    grad_wide = (grad_active * slope).astype(BF16)
    out_part = jnp.dot(active, down[...], preferred_element_type=F32)
    grad_part = lax.dot_general(grad_wide, up[...], back, preferred_element_type=F32)

    @pl.when(step == 0)
    def _():
        out_sum[...] = out_part
        grad_sum[...] = grad_part

    @pl.when(step > 0)
    def _():
        out_sum[...] += out_part
        grad_sum[...] += grad_part

    bias_sum[...] = jnp.sum(grad_wide.astype(F32), axis=0, keepdims=True)
    up_keep[...] = jnp.dot(normed_turned[:half], grad_wide, preferred_element_type=F32)
    up_send[...] = jnp.dot(normed_turned[half:], grad_wide, preferred_element_type=F32).astype(BF16)
    down_keep[...] = jnp.dot(grad_turned[:half], active, preferred_element_type=F32)
    down_send[...] = jnp.dot(grad_turned[half:], active, preferred_element_type=F32).astype(BF16)


def feed_forward(normed, grad_out, normed_turned, grad_turned, up, down, bias, tile):
    count, width = normed.shape
    hidden = up.shape[1]
    half = width // 2
    fixed = lambda *shape: pl.BlockSpec(shape, lambda t: (0, 0))
    across = lambda rows: pl.BlockSpec((rows, tile), lambda t: (0, t))
    shape = jax.ShapeDtypeStruct
    return pl.pallas_call(
        mlp_kernel,
        grid=(hidden // tile,),
        in_specs=[
            fixed(count, width),
            fixed(count, width),
            fixed(width, count),
            fixed(width, count),
            across(width),
            pl.BlockSpec((tile, width), lambda t: (t, 0)),
            across(1),
        ],
        out_specs=[fixed(count, width), fixed(count, width), across(half), across(half), across(half), across(half), across(1)],
        out_shape=[
            shape((count, width), F32),
            shape((count, width), F32),
            shape((half, hidden), F32),
            shape((half, hidden), BF16),
            shape((half, hidden), F32),
            shape((half, hidden), BF16),
            shape((1, hidden), F32),
        ],
        compiler_params=pltpu.CompilerParams(vmem_limit_bytes=56 << 20),
        cost_estimate=pl.CostEstimate(
            flops=12 * count * width * hidden,
            bytes_accessed=10 * width * hidden,
            transcendentals=count * hidden,
        ),
    )(normed, grad_out, normed_turned, grad_turned, up, down, bias)


def turn_halves(values, groups, mine):
    count, width = values.shape
    view = values.T.reshape(groups, 2, width // (2 * groups), count)
    keep = lax.dynamic_index_in_dim(view, mine, 1, keepdims=False).reshape(width // 2, count)
    send = lax.dynamic_index_in_dim(view, 1 - mine, 1, keepdims=False).reshape(width // 2, count)
    return jnp.concatenate([keep, send], axis=0)


STAGES = 4


def mlp_reduce_kernel(
    tiles,
    normed,
    grad_out,
    normed_turned,
    grad_turned,
    up0,
    up1,
    up2,
    up3,
    down0,
    down1,
    down2,
    down3,
    bias,
    out_sum,
    grad_sum,
    bias_sum,
    up_total,
    down_total,
    up_mine,
    down_mine,
    up_core,
    down_core,
    up_core_got,
    down_core_got,
    up_half,
    down_half,
    up_out,
    down_out,
    up_got,
    down_got,
    up_quarter,
    down_quarter,
    up_last,
    down_last,
    up_last_got,
    down_last_got,
    chip_full,
    chip_out,
    chip_got,
    core_sent,
    core_came,
    seq_sent,
    seq_came,
    last_sent,
    last_came,
    chip_sent,
    chip_came,
):
    step = pl.program_id(0)
    seq, row = lax.axis_index("seq"), lax.axis_index("rows")
    half = normed_turned.shape[0] // 2
    x, y = lax.rem(seq, 2), lax.div(seq, 2)
    core_peer = {"rows": row + 1 - 2 * lax.rem(row, 2)}
    x_peer = {"seq": seq + 1 - 2 * x}
    y_peer = {"seq": seq + 2 - 4 * y}
    chip, core = lax.div(row, 2), lax.rem(row, 2)
    to_chip = [lax.rem(chip + k, 4) for k in range(4)]
    chip_peers = [{"rows": 2 * to_chip[k] + core} for k in range(4)]

    @pl.when(step == 0)
    def _():
        barrier = pltpu.get_barrier_semaphore()
        for peer in (core_peer, x_peer, y_peer, *chip_peers[1:]):
            pl.semaphore_signal(barrier, inc=1, device_id=peer, device_id_type=pl.DeviceIdType.MESH)
        pl.semaphore_wait(barrier, 6)

    def copies(source, target, sent, came, slot, kind, device):
        return pltpu.make_async_remote_copy(
            src_ref=source.at[slot],
            dst_ref=target.at[slot],
            send_sem=sent.at[kind, slot],
            recv_sem=came.at[kind, slot],
            device_id=device,
            device_id_type=pl.DeviceIdType.MESH,
        )

    def to_core(slot):
        return (
            copies(up_core, up_core_got, core_sent, core_came, slot, 0, core_peer),
            copies(down_core, down_core_got, core_sent, core_came, slot, 1, core_peer),
        )

    def to_seq(slot):
        return (
            copies(up_out, up_got, seq_sent, seq_came, slot, 0, x_peer),
            copies(down_out, down_got, seq_sent, seq_came, slot, 1, y_peer),
        )

    def to_last(slot):
        return (
            copies(up_last, up_last_got, last_sent, last_came, slot, 0, y_peer),
            copies(down_last, down_last_got, last_sent, last_came, slot, 1, x_peer),
        )

    def to_chips(slot):
        return [
            pltpu.make_async_remote_copy(
                src_ref=chip_out.at[slot, to_chip[k]],
                dst_ref=chip_got.at[slot, k - 1],
                send_sem=chip_sent.at[k - 1, slot],
                recv_sem=chip_came.at[k - 1, slot],
                device_id=chip_peers[k],
                device_id_type=pl.DeviceIdType.MESH,
            )
            for k in range(1, 4)
        ]

    @pl.when(step >= 4)
    def _():
        slot = lax.rem(step, 2)
        for copy in to_chips(slot):
            copy.wait()
        for kind, total in enumerate((up_total, down_total)):
            value = chip_full[slot, chip, kind]
            for k in range(3):
                value = value + chip_got[slot, k, kind].astype(F32)
            total[...] = value

    @pl.when((step >= 3) & (step < tiles + 3))
    def _():
        slot = lax.rem(step + 1, 2)
        for copy in to_last(slot):
            copy.wait()
        size = half // 4
        ups = up_quarter[slot] + up_last_got[slot].astype(F32)
        downs = down_quarter[slot] + down_last_got[slot].astype(F32)
        for place in range(4):
            up_block = ups[place * size : (place + 1) * size]
            down_block = downs[:, place * 128 : (place + 1) * 128]
            chip_full[slot, place, 0] = up_block
            chip_full[slot, place, 1] = down_block
            chip_out[slot, place, 0] = up_block.astype(BF16)
            chip_out[slot, place, 1] = down_block.astype(BF16)
        for copy in to_chips(slot):
            copy.start()

    @pl.when((step >= 2) & (step < tiles + 2))
    def _():
        slot = lax.rem(step, 2)
        for copy in to_seq(slot):
            copy.wait()
        up_quarter[slot] = up_half[slot, y] + up_got[slot, y].astype(F32)
        up_last[slot] = (up_half[slot, 1 - y] + up_got[slot, 1 - y].astype(F32)).astype(BF16)
        down_quarter[slot] = down_half[slot, x] + down_got[slot, x].astype(F32)
        down_last[slot] = (down_half[slot, 1 - x] + down_got[slot, 1 - x].astype(F32)).astype(BF16)
        for copy in to_last(slot):
            copy.start()

    @pl.when((step >= 1) & (step <= tiles))
    def _():
        slot = lax.rem(step + 1, 2)
        for copy in to_core(slot):
            copy.wait()
        for other in range(2):
            kept, gone = 2 * other + x, 2 * other + 1 - x
            up_half[slot, other] = up_mine[slot, kept] + up_core_got[slot, kept].astype(F32)
            up_out[slot, other] = (up_mine[slot, gone] + up_core_got[slot, gone].astype(F32)).astype(BF16)
            kept, gone = 2 * y + other, 2 * (1 - y) + other
            down_half[slot, other] = down_mine[slot, kept] + down_core_got[slot, kept].astype(F32)
            down_out[slot, other] = (down_mine[slot, gone] + down_core_got[slot, gone].astype(F32)).astype(BF16)
        for copy in to_seq(slot):
            copy.start()

    @pl.when(step < tiles)
    def _():
        slot = lax.rem(step, 2)
        up = jnp.concatenate([up0[...], up1[...], up2[...], up3[...]], axis=1)
        down = jnp.concatenate([down0[...], down1[...], down2[...], down3[...]], axis=0)
        biases = jnp.concatenate([bias[owner] for owner in range(4)], axis=1)
        c0 = math.sqrt(2 / math.pi)
        c1 = c0 * 0.044715
        hidden = jnp.dot(normed[...], up, preferred_element_type=F32) + biases
        square = hidden * hidden
        gate = 0.5 + 0.5 * jnp.tanh(hidden * (c0 + c1 * square))
        raised = hidden * gate
        slope = gate + raised * (1.0 - gate) * (2 * c0 + 6 * c1 * square)
        active = raised.astype(BF16)
        down_part = jnp.dot(grad_turned[...], active, preferred_element_type=F32)
        for owner in range(4):
            size = half // 4
            down_mine[slot, owner] = down_part[owner * size : (owner + 1) * size]
            down_core[slot, owner] = down_part[half + owner * size : half + (owner + 1) * size].astype(BF16)
        to_core(slot)[1].start()
        back = (((1,), (1,)), ((), ()))
        grad_active = lax.dot_general(grad_out[...], down, back, preferred_element_type=F32)
        grad_wide = (grad_active * slope).astype(BF16)
        up_part = jnp.dot(normed_turned[...], grad_wide, preferred_element_type=F32)
        for owner in range(4):
            columns = slice(owner * 128, (owner + 1) * 128)
            up_mine[slot, owner] = up_part[:half, columns]
            up_core[slot, owner] = up_part[half:, columns].astype(BF16)
        to_core(slot)[0].start()
        sums = jnp.sum(grad_wide.astype(F32), axis=0, keepdims=True)
        for owner in range(4):
            bias_sum[owner] = sums[:, owner * 128 : (owner + 1) * 128]
        out_part = jnp.dot(active, down, preferred_element_type=F32)
        grad_part = lax.dot_general(grad_wide, up, back, preferred_element_type=F32)

        @pl.when(step == 0)
        def _():
            out_sum[...] = out_part
            grad_sum[...] = grad_part

        @pl.when(step > 0)
        def _():
            out_sum[...] += out_part
            grad_sum[...] += grad_part


def feed_forward_reduce(normed, grad_out, normed_turned, grad_turned, up, down, bias):
    count, width = normed.shape
    hidden = up.shape[1]
    part = hidden // 4
    tiles = part // 128
    half, quarter = width // 2, width // 8
    last = tiles - 1
    shape = jax.ShapeDtypeStruct
    fixed = lambda *dims: pl.BlockSpec(dims, lambda t: (0, 0), pipeline_mode=pl.Buffered(buffer_count=1))
    result = lambda *dims: pl.BlockSpec(dims, lambda t: (0, 0))
    done = lambda t: jnp.maximum(t - STAGES, 0)

    def up_block(owner):
        return pl.BlockSpec((width, 128), lambda t: (0, owner * tiles + jnp.minimum(t, last)))

    def down_block(owner):
        return pl.BlockSpec((128, width), lambda t: (owner * tiles + jnp.minimum(t, last), 0))

    bias_block = pl.BlockSpec((4, 1, 128), lambda t: (0, 0, jnp.minimum(t, last)))
    pair = lambda dtype, *dims: pltpu.VMEM((2,) + dims, dtype)
    return pl.pallas_call(
        partial(mlp_reduce_kernel, tiles),
        grid=(tiles + STAGES,),
        in_specs=[fixed(count, width), fixed(count, width), fixed(width, count), fixed(width, count)]
        + [up_block(owner) for owner in range(4)]
        + [down_block(owner) for owner in range(4)]
        + [bias_block],
        out_specs=[
            result(count, width),
            result(count, width),
            bias_block,
            pl.BlockSpec((quarter, 128), lambda t: (0, done(t))),
            pl.BlockSpec((quarter, 128), lambda t: (0, done(t))),
        ],
        out_shape=[
            shape((count, width), F32),
            shape((count, width), F32),
            shape((4, 1, part), F32),
            shape((quarter, part), F32),
            shape((quarter, part), F32),
        ],
        scratch_shapes=[
            pair(F32, 4, half, 128),
            pair(F32, 4, quarter, 512),
            pair(BF16, 4, half, 128),
            pair(BF16, 4, quarter, 512),
            pair(BF16, 4, half, 128),
            pair(BF16, 4, quarter, 512),
            pair(F32, 2, half, 128),
            pair(F32, 2, quarter, 512),
            pair(BF16, 2, half, 128),
            pair(BF16, 2, quarter, 512),
            pair(BF16, 2, half, 128),
            pair(BF16, 2, quarter, 512),
            pair(F32, half, 128),
            pair(F32, quarter, 512),
            pair(BF16, half, 128),
            pair(BF16, quarter, 512),
            pair(BF16, half, 128),
            pair(BF16, quarter, 512),
            pair(F32, 4, 2, quarter, 128),
            pair(BF16, 4, 2, quarter, 128),
            pair(BF16, 3, 2, quarter, 128),
        ]
        + [pltpu.SemaphoreType.DMA((2, 2))] * 6
        + [pltpu.SemaphoreType.DMA((3, 2))] * 2,
        compiler_params=pltpu.CompilerParams(collective_id=1, has_side_effects=True, vmem_limit_bytes=56 << 20),
        cost_estimate=pl.CostEstimate(
            flops=12 * count * width * hidden,
            bytes_accessed=6 * width * hidden,
            transcendentals=count * hidden,
        ),
    )(normed, grad_out, normed_turned, grad_turned, up, up, up, up, down, down, down, down, bias.reshape(4, 1, part))


def split_low(values):
    high = values.astype(BF16)
    rest = values - high.astype(F32)
    middle = rest.astype(BF16)
    return high, middle, (rest - middle.astype(F32)).astype(BF16)


def per_token(slot_col, seg_row, table):
    picked = (slot_col == seg_row).astype(BF16)
    return lax.dot_general(
        picked, jnp.concatenate(split_low(table), axis=0), (((0,), (0,)), ((), ())), preferred_element_type=F32
    )


def per_slot(slot_col, seg_row, values):
    slots = slot_col.shape[0] // 3
    picked = (slot_col[:slots] == seg_row).astype(BF16)
    return sum(jnp.dot(picked, part, preferred_element_type=F32) for part in split_low(values))


def normalize(values):
    center = values - jnp.mean(values, axis=-1, keepdims=True)
    inverse = lax.rsqrt(jnp.mean(center * center, axis=-1, keepdims=True) + norm_eps)
    return center * inverse, inverse


def normalize_back(normal, inverse, grad):
    return inverse * (grad - jnp.mean(grad, axis=-1, keepdims=True) - normal * jnp.mean(grad * normal, axis=-1, keepdims=True))


def before_kernel(
    slot_col,
    seg,
    table,
    attended,
    weight,
    bias,
    tokens,
    cotangent,
    branch_ref,
    middle_ref,
    normed_ref,
    grad_ref,
    normed_turned,
    grad_turned,
    bias_sum,
    turned,
):
    width = tokens.shape[-1]
    depth = width // 8
    core = lax.rem(lax.axis_index("rows"), 2)
    mods = per_token(slot_col[...], seg[0], table[0, :, 2 * width :])
    gate_a, shift_b, scale_b, gate_b = (mods[:, k * width : (k + 1) * width] for k in range(4))
    branch = lax.dot_general(attended[0], weight[...], (((0,), (0,)), ((), ())), preferred_element_type=F32) + bias[...]
    middle = tokens[0].astype(F32) + gate_a * branch
    branch_ref[0] = branch
    middle_ref[0] = middle
    normed = normalize(middle)[0] * (1.0 + scale_b) + shift_b
    grad = cotangent[0].astype(F32) * gate_b
    normed_ref[...] = normed.astype(BF16)
    grad_ref[...] = grad.astype(BF16)
    for values, target in ((normed, normed_turned), (grad, grad_turned)):
        turned[...] = values.T
        for place in range(4):
            for order in range(2):
                first = pl.multiple_of((2 * place + (core if order == 0 else 1 - core)) * depth, 8)
                start = (4 * order + place) * depth
                target[start : start + depth] = turned[pl.ds(first, depth), :].astype(BF16)
    sums = jnp.sum(grad.astype(BF16).astype(F32), axis=0, keepdims=True)

    @pl.when(pl.program_id(0) == 0)
    def _():
        bias_sum[...] = sums

    @pl.when(pl.program_id(0) > 0)
    def _():
        bias_sum[...] += sums


def before_feed_forward(slot_col, seg, table, attended, weight, bias, tokens, cotangent):
    rows, length, width = tokens.shape
    fixed = lambda *dims: pl.BlockSpec(dims, lambda r: (0,) * len(dims))
    row = lambda *dims: pl.BlockSpec((1,) + dims, lambda r: (r, 0, 0))
    shape = jax.ShapeDtypeStruct
    return pl.pallas_call(
        before_kernel,
        grid=(rows,),
        in_specs=[
            fixed(*slot_col.shape),
            row(1, length),
            row(*table.shape[1:]),
            row(width, length),
            fixed(width, width),
            fixed(1, width),
            row(length, width),
            row(length, width),
        ],
        out_specs=[
            row(length, width),
            row(length, width),
            pl.BlockSpec((length, width), lambda r: (r, 0)),
            pl.BlockSpec((length, width), lambda r: (r, 0)),
            pl.BlockSpec((width, length), lambda r: (0, r)),
            pl.BlockSpec((width, length), lambda r: (0, r)),
            fixed(1, width),
        ],
        out_shape=[
            shape((rows, length, width), F32),
            shape((rows, length, width), F32),
            shape((rows * length, width), BF16),
            shape((rows * length, width), BF16),
            shape((width, rows * length), BF16),
            shape((width, rows * length), BF16),
            shape((1, width), F32),
        ],
        scratch_shapes=[pltpu.VMEM((width, length), F32)],
        compiler_params=pltpu.CompilerParams(vmem_limit_bytes=VMEM_LIMIT),
        cost_estimate=pl.CostEstimate(flops=4 * 10**9, bytes_accessed=2 * 10**7, transcendentals=0),
    )(slot_col, seg, table, attended, weight, bias, tokens, cotangent)


def after_kernel(
    slot_col,
    seg,
    table,
    attended,
    weight,
    bias,
    out_sum,
    grad_sum,
    middle_ref,
    branch_ref,
    cotangent,
    block_out,
    grad_middle_ref,
    slot_sums,
    bias_sum,
    view_ref,
    proj_ref,
    heads_out,
    total,
    core_out,
    core_got,
    sent,
    came,
    kept,
    core_sent,
    core_came,
):
    step = pl.program_id(0)
    rows = pl.num_programs(0)
    width = cotangent.shape[-1]
    length = cotangent.shape[-2]
    depth, own = width // 8, width // 4
    seq, row = lax.axis_index("seq"), lax.axis_index("rows")
    core = lax.rem(row, 2)
    core_peer = {"rows": row + 1 - 2 * core}
    peers = peers_of(seq)

    @pl.when(step == 0)
    def _():
        greet([{"seq": peer} for peer in peers] + [core_peer])

    def to_peer(r, m):
        lanes = pl.ds(m * length, length)
        return send_block(
            heads_out.at[r, peers[m - 1]], view_ref.at[r, :, lanes], sent, came, r * 3 + m - 1, {"seq": peers[m - 1]}
        )

    def to_self(r):
        return pltpu.make_async_copy(heads_out.at[r, seq], view_ref.at[r, :, pl.ds(0, length)], kept.at[r])

    mods = per_token(slot_col[...], seg[0], table[0, :, 2 * width :])
    gate_a, scale_b, gate_b = (mods[:, k * width : (k + 1) * width] for k in (0, 2, 3))
    middle, branch = middle_ref[0], branch_ref[0]
    upstream = cotangent[0].astype(F32)
    normal, inverse = normalize(middle)
    grad_normed = grad_sum[...]
    grad_middle = upstream + normalize_back(normal, inverse, grad_normed * (1.0 + scale_b))
    grad_middle_ref[0] = grad_middle
    grad_branch = (grad_middle * gate_a).astype(BF16)
    grad_heads = lax.dot_general(weight[...], grad_branch, (((1,), (1,)), ((), ())), preferred_element_type=F32)
    for owner in range(4):
        heads_out[step, owner] = grad_heads[owner * own : (owner + 1) * own].astype(BF16)
    to_self(step).start()
    for m in range(1, 4):
        to_peer(step, m).start()

    part = jnp.dot(attended[0], grad_branch, preferred_element_type=F32)
    sums = jnp.sum(grad_branch.astype(F32), axis=0, keepdims=True)

    @pl.when(step == 0)
    def _():
        total[...] = part
        bias_sum[...] = sums

    @pl.when(step > 0)
    def _():
        total[...] += part
        bias_sum[...] += sums

    to_core = pltpu.make_async_remote_copy(
        src_ref=core_out,
        dst_ref=core_got,
        send_sem=core_sent,
        recv_sem=core_came,
        device_id=core_peer,
        device_id_type=pl.DeviceIdType.MESH,
    )

    @pl.when(step == rows - 1)
    def _():
        for chip in range(4):
            other = pl.multiple_of((2 * chip + 1 - core) * depth, 8)
            core_out[chip] = total[pl.ds(other, depth), :].astype(BF16)
        to_core.start()

    branch_b = out_sum[...] + bias[...]
    block_out[0] = (middle + gate_b * branch_b).astype(BF16)
    pieces = (grad_middle * branch, grad_normed, grad_normed * normal, upstream * branch_b)
    for k, piece in enumerate(pieces):
        slot_sums[0, :, k * width : (k + 1) * width] = per_slot(slot_col[...], seg[0], piece)

    @pl.when(step == rows - 1)
    def _():
        to_core.wait()
        for chip in range(4):
            mine = pl.multiple_of((2 * chip + core) * depth, 8)
            proj_ref[chip] = total[pl.ds(mine, depth), :] + core_got[chip].astype(F32)
        for r in range(heads_out.shape[0]):
            to_self(r).wait()
            for m in range(1, 4):
                to_peer(r, m).wait()


def after_feed_forward(slot_col, seg, table, attended, weight, bias, out_sum, grad_sum, middle, branch, cotangent):
    rows, length, width = cotangent.shape
    slots = table.shape[1]
    depth = width // 8
    fixed = lambda *dims: pl.BlockSpec(dims, lambda r: (0,) * len(dims))
    row = lambda *dims: pl.BlockSpec((1,) + dims, lambda r: (r, 0, 0))
    shape = jax.ShapeDtypeStruct
    return pl.pallas_call(
        after_kernel,
        grid=(rows,),
        in_specs=[
            fixed(*slot_col.shape),
            row(1, length),
            row(*table.shape[1:]),
            row(width, length),
            fixed(width, width),
            fixed(1, width),
            pl.BlockSpec((length, width), lambda r: (r, 0)),
            pl.BlockSpec((length, width), lambda r: (r, 0)),
            row(length, width),
            row(length, width),
            row(length, width),
        ],
        out_specs=[
            row(length, width),
            row(length, width),
            row(slots, 4 * width),
            fixed(1, width),
            pl.BlockSpec(memory_space=pl.ANY),
            fixed(4, depth, width),
        ],
        out_shape=[
            shape((rows, length, width), BF16),
            shape((rows, length, width), F32),
            shape((rows, slots, 4 * width), F32),
            shape((1, width), F32),
            shape((rows, width // 4, 4 * length), BF16),
            shape((4, depth, width), F32),
        ],
        scratch_shapes=[
            pltpu.VMEM((rows, 4, width // 4, length), BF16),
            pltpu.VMEM((width, width), F32),
            pltpu.VMEM((4, depth, width), BF16),
            pltpu.VMEM((4, depth, width), BF16),
            pltpu.SemaphoreType.DMA((3 * rows,)),
            pltpu.SemaphoreType.DMA((3 * rows,)),
            pltpu.SemaphoreType.DMA((rows,)),
            pltpu.SemaphoreType.DMA,
            pltpu.SemaphoreType.DMA,
        ],
        compiler_params=pltpu.CompilerParams(vmem_limit_bytes=56 << 20, collective_id=4, has_side_effects=True),
        cost_estimate=pl.CostEstimate(flops=8 * 10**9, bytes_accessed=3 * 10**7, transcendentals=0),
    )(slot_col, seg, table, attended, weight, bias, out_sum, grad_sum, middle, branch, cotangent)


def qkv_weight_kernel(grad, normed, keep_ref, send_ref, sum_ref, total, turned):
    step = pl.program_id(0)
    chips, depth = lax.axis_size("rows") // 2, total.shape[1] // lax.axis_size("rows")
    mine = lax.rem(lax.axis_index("rows"), 2)
    part = jnp.dot(grad[0], normed[0], preferred_element_type=F32)
    sums = jnp.sum(grad[0].astype(F32), axis=1, keepdims=True)

    @pl.when(step == 0)
    def _():
        total[...] = part
        sum_ref[...] = sums

    @pl.when(step > 0)
    def _():
        total[...] += part
        sum_ref[...] += sums

    @pl.when(step == pl.num_programs(0) - 1)
    def _():
        turned[...] = total[...].T
        for chip in range(chips):
            first = pl.multiple_of((2 * chip + mine) * depth, 8)
            other = pl.multiple_of((2 * chip + 1 - mine) * depth, 8)
            keep_ref[chip] = turned[pl.ds(first, depth), :]
            send_ref[chip] = turned[pl.ds(other, depth), :].astype(BF16)


def qkv_weight_grad(grad, normed):
    rows, features, length = grad.shape
    width = normed.shape[2]
    groups = lax.axis_size("rows")
    shape = (groups // 2, width // groups, features)
    return pl.pallas_call(
        qkv_weight_kernel,
        grid=(rows,),
        in_specs=[
            pl.BlockSpec((1, features, length), lambda r: (r, 0, 0)),
            pl.BlockSpec((1, length, width), lambda r: (r, 0, 0)),
        ],
        out_specs=[
            pl.BlockSpec(shape, lambda r: (0, 0, 0)),
            pl.BlockSpec(shape, lambda r: (0, 0, 0)),
            pl.BlockSpec((features, 1), lambda r: (0, 0)),
        ],
        out_shape=[
            jax.ShapeDtypeStruct(shape, F32),
            jax.ShapeDtypeStruct(shape, BF16),
            jax.ShapeDtypeStruct((features, 1), F32),
        ],
        scratch_shapes=[pltpu.VMEM((features, width), F32), pltpu.VMEM((width, features), F32)],
        compiler_params=pltpu.CompilerParams(vmem_limit_bytes=VMEM_LIMIT),
        cost_estimate=pl.CostEstimate(
            flops=2 * rows * length * width * features,
            bytes_accessed=2 * rows * length * (width + features) + 6 * width * features // 2,
            transcendentals=0,
        ),
    )(grad, normed)


def tail_kernel(
    images,
    mod,
    weight,
    cond,
    ada_ref,
    cond_ref,
    bias_ref,
    got,
    low_mine,
    low_got,
    row_mine,
    row_got,
    cond_mine,
    cond_got,
    column_got,
    sent,
    arrived,
):
    seq_count, row_total = lax.axis_size("seq"), lax.axis_size("rows")
    seq, row = lax.axis_index("seq"), lax.axis_index("rows")
    to_seq = [lax.rem(seq + m, seq_count) for m in range(seq_count)]
    to_row = [lax.rem(row + m, row_total) for m in range(row_total)]
    barrier = pltpu.get_barrier_semaphore()
    for m in range(1, seq_count):
        pl.semaphore_signal(barrier, inc=1, device_id={"seq": to_seq[m]}, device_id_type=pl.DeviceIdType.MESH)
    for m in range(1, row_total):
        pl.semaphore_signal(barrier, inc=1, device_id={"rows": to_row[m]}, device_id_type=pl.DeviceIdType.MESH)
    pl.semaphore_wait(barrier, seq_count + row_total - 2)

    used = [0]

    def start(source, target, device):
        copy = pltpu.make_async_remote_copy(
            src_ref=source,
            dst_ref=target,
            send_sem=sent.at[used[0]],
            recv_sem=arrived.at[used[0]],
            device_id=device,
            device_id_type=pl.DeviceIdType.MESH,
        )
        used[0] += 1
        copy.start()
        return copy

    copies = [start(mod.at[to_seq[m]], got.at[m], {"seq": to_seq[m]}) for m in range(1, seq_count)]
    column_got[0] = cond[row]
    column_copies = [start(cond.at[to_row[m]], column_got.at[m], {"rows": to_row[m]}) for m in range(1, row_total)]
    total = mod[seq]
    for m, copy in enumerate(copies):
        copy.wait()
        total = total + got[m + 1]
    low = total[:images].astype(BF16)
    low_mine[...] = low
    row_mine[...] = total[images:]
    row_mine[0:1] = jnp.sum(total[:images], axis=0, keepdims=True)
    low_got[0] = low
    copies = [start(low_mine, low_got.at[m], {"rows": to_row[m]}) for m in range(1, row_total)]
    copies += [start(row_mine, row_got.at[m], {"rows": to_row[m]}) for m in range(1, row_total)]
    term = lax.dot_general(low, weight[...], (((1,), (1,)), ((), ())), preferred_element_type=F32)
    cond_mine[...] = term
    cond_copies = [start(cond_mine, cond_got.at[m], {"seq": to_seq[m]}) for m in range(1, seq_count)]
    for copy in copies:
        copy.wait()
    sums = row_mine[...]
    for m in range(1, row_total):
        sums = sums + row_got[m]
    bias_ref[seq] = sums
    copies = [start(bias_ref.at[seq], bias_ref.at[seq], {"seq": to_seq[m]}) for m in range(1, seq_count)]
    for copy in column_copies:
        copy.wait()
    gathered = jnp.concatenate([low_got[m] for m in range(row_total)], axis=0)
    columns = jnp.concatenate([column_got[m] for m in range(row_total)], axis=0)
    ada_ref[...] = lax.dot_general(columns, gathered, (((0,), (0,)), ((), ())), preferred_element_type=F32)
    for m, copy in enumerate(cond_copies):
        copy.wait()
        term = term + cond_got[m + 1]
    cond_ref[...] = term
    for copy in copies:
        copy.wait()


def finish(mod, weight, cond, images):
    seq_count, lines, columns = mod.shape
    width, depth = weight.shape[0], cond.shape[2]
    row_total = lax.axis_size("rows")
    extra = lines - images
    copies = 3 * (seq_count - 1) + 3 * (row_total - 1)
    return pl.pallas_call(
        partial(tail_kernel, images),
        in_specs=[pl.BlockSpec(memory_space=pltpu.VMEM)] * 3,
        out_specs=[pl.BlockSpec(memory_space=pltpu.VMEM)] * 3,
        out_shape=[
            jax.ShapeDtypeStruct((depth, columns), F32),
            jax.ShapeDtypeStruct((images, width), F32),
            jax.ShapeDtypeStruct((seq_count, extra, columns), F32),
        ],
        scratch_shapes=[
            pltpu.VMEM((seq_count, lines, columns), F32),
            pltpu.VMEM((images, columns), BF16),
            pltpu.VMEM((row_total, images, columns), BF16),
            pltpu.VMEM((extra, columns), F32),
            pltpu.VMEM((row_total, extra, columns), F32),
            pltpu.VMEM((images, width), F32),
            pltpu.VMEM((seq_count, images, width), F32),
            pltpu.VMEM((row_total, images, depth), BF16),
            pltpu.SemaphoreType.DMA((copies,)),
            pltpu.SemaphoreType.DMA((copies,)),
        ],
        compiler_params=pltpu.CompilerParams(collective_id=0, has_side_effects=True, vmem_limit_bytes=VMEM_LIMIT),
        cost_estimate=pl.CostEstimate(flops=10**9, bytes_accessed=10**7, transcendentals=0),
    )(mod, weight, cond)


def send_to(source, target, sent, came, device):
    return pltpu.make_async_remote_copy(
        src_ref=source,
        dst_ref=target,
        send_sem=sent,
        recv_sem=came,
        device_id=device,
        device_id_type=pl.DeviceIdType.MESH,
    )


def attend_back_reduce_kernel(
    block,
    inner,
    scale,
    code_col,
    code_row,
    query,
    key,
    value,
    out,
    grad_out,
    lse,
    normed,
    proj,
    down,
    token_ref,
    qkv_ref,
    proj_ref,
    down_ref,
    grads,
    key_sum,
    value_sum,
    keys,
    values,
    flat,
    total,
    turned,
    core_out,
    core_got,
    proj_out,
    proj_got,
    seq_out,
    seq_got,
    down_out,
    down_got,
    sent,
    came,
    kept,
    proj_sent,
    proj_came,
    seq_sent,
    seq_came,
    core_sent,
    core_came,
):
    length, size = query.shape[-1], query.shape[-2]
    row, head = pl.program_id(0), pl.program_id(1)
    rows, _, heads = grads.shape[:3]
    width = normed.shape[-1]
    depth, own, local = width // 8, width // 4, length // 4
    seq, group = lax.axis_index("seq"), lax.axis_index("rows")
    chip, core = lax.div(group, 2), lax.rem(group, 2)
    peers = [{"seq": peer} for peer in peers_of(seq)]
    core_peer = {"rows": group + 1 - 2 * core}
    to_chip = [lax.rem(chip + k, 4) for k in range(4)]
    chip_peers = [{"rows": 2 * to_chip[k] + core} for k in range(4)]
    first = (row == 0) & (head == 0)
    last = (row == rows - 1) & (head == heads - 1)

    def to_peer(r, h, m):
        place = (r * heads + h) * 3 + m - 1
        source = grads.at[r, :, h, :, pl.ds(m * local, local)]
        return send_to(source, token_ref.at[r, :, seq, h], sent.at[place], came.at[place], peers[m - 1])

    def to_self(r, h):
        source = grads.at[r, :, h, :, pl.ds(0, local)]
        return pltpu.make_async_copy(source, token_ref.at[r, :, seq, h], kept.at[r * heads + h])

    proj_copies = [
        send_to(proj_out.at[to_chip[k]], proj_got.at[k - 1], proj_sent.at[k - 1], proj_came.at[k - 1], chip_peers[k])
        for k in range(1, 4)
    ]
    seq_copies = [
        send_to(seq_out.at[target], seq_got.at[m], seq_sent.at[m], seq_came.at[m], peers[m])
        for m, target in enumerate(peers_of(seq))
    ]
    core_copy = send_to(core_out, core_got, core_sent.at[0], core_came.at[0], core_peer)
    down_copy = send_to(down_out.at[1 - core], down_got, core_sent.at[1], core_came.at[1], core_peer)

    @pl.when(first)
    def _():
        greet(peers + [core_peer] + chip_peers[1:])
        proj_out[...] = proj[...].astype(BF16)
        for copy in proj_copies:
            copy.start()
        half = down.shape[1] // 2
        for place in range(2):
            down_out[place] = down[:, place * half : (place + 1) * half]
        down_copy.start()

    keys[...] = key[0, 0].astype(F32).T.astype(BF16)
    values[...] = value[0, 0].astype(F32).T.astype(BF16)

    def place_of(part):
        return pl.ds(pl.multiple_of((part * heads + head) * size, 8), size)

    for step in range(length // block):
        here = pl.ds(step * block, block)
        query_low = query[0, 0, :, here]
        grad_low = grad_out[0, 0, :, here]
        query_rows = query_low.astype(F32).T.astype(BF16)
        grad_rows = grad_low.astype(F32).T.astype(BF16)
        row_dot = jnp.sum(grad_low.astype(F32) * out[0, 0, :, here].astype(F32), axis=0, keepdims=True)
        grad_query = jnp.zeros((size, block), F32)
        for part in range(length // inner):
            there = pl.ds(part * inner, inner)
            scores = jnp.dot(keys[there, :], query_low, preferred_element_type=F32)
            scores = jnp.where(code_col[0, there, :] == code_row[0, :, here], scores * (scale * LOG2E), -1e30)
            probs = jnp.exp2(scores - lse[0, 0, :, here])
            grad_probs = jnp.dot(values[there, :], grad_low, preferred_element_type=F32)
            grad_raw = (probs * (grad_probs - row_dot) * scale).astype(BF16)
            value_part = jnp.dot(probs.astype(BF16), grad_rows, preferred_element_type=F32)
            key_part = jnp.dot(grad_raw, query_rows, preferred_element_type=F32)
            if step == 0:
                value_sum[there, :] = value_part
                key_sum[there, :] = key_part
            else:
                value_sum[there, :] += value_part
                key_sum[there, :] += key_part
            grad_query += jnp.dot(key[0, 0, :, there], grad_raw, preferred_element_type=F32)
        low = grad_query.astype(BF16)
        grads[row, 0, head, :, here] = low
        flat[place_of(0), here] = low.astype(F32)
    for part, sums in ((1, key_sum), (2, value_sum)):
        low = sums[...].T.astype(BF16)
        grads[row, part, head] = low
        flat[place_of(part), :] = low.astype(F32)

    to_self(row, head).start()
    for m in range(1, 4):
        to_peer(row, head, m).start()

    @pl.when((head == heads - 1) & (row == 0))
    def _():
        total[...] = jnp.dot(flat[...].astype(BF16), normed[0], preferred_element_type=F32)

    @pl.when((head == heads - 1) & (row > 0))
    def _():
        total[...] += jnp.dot(flat[...].astype(BF16), normed[0], preferred_element_type=F32)

    @pl.when(last)
    def _():
        turned[...] = total[...].T
        for place in range(4):
            other = pl.multiple_of((2 * place + 1 - core) * depth, 8)
            core_out[place] = turned[pl.ds(other, depth), :].astype(BF16)
        core_copy.start()
        for copy in proj_copies:
            copy.wait()
        mine = proj[chip]
        for k in range(3):
            mine = mine + proj_got[k].astype(F32)
        for place in range(4):
            seq_out[place] = mine[:, place * own : (place + 1) * own].astype(BF16)
        for copy in seq_copies:
            copy.start()
        down_copy.wait()
        left, right = down_out[core], down_got[...]
        left, right = jnp.where(core == 0, left, right), jnp.where(core == 0, right, left)
        down_ref[:, :depth] = left.T
        down_ref[:, depth:] = right.T
        core_copy.wait()
        for place in range(4):
            same = pl.multiple_of((2 * place + core) * depth, 8)
            qkv_ref[place] = turned[pl.ds(same, depth), :] + core_got[place].astype(F32)
        for place in range(4):

            @pl.when(seq == place)
            def _():
                proj_ref[...] = mine[:, place * own : (place + 1) * own]

        for m, copy in enumerate(seq_copies):
            copy.wait()
            proj_ref[...] += seq_got[m].astype(F32)
        for r in range(rows):
            for h in range(heads):
                to_self(r, h).wait()
                for m in range(1, 4):
                    to_peer(r, h, m).wait()


def attend_back_reduce(packed, out, grad_out, lse, col, row, normed, proj, down, block, inner):
    rows, _, heads, size, length = packed.shape
    width = normed.shape[2]
    depth, own, features = width // 8, width // 4, 3 * heads * size
    half = down.shape[1] // 2
    part = lambda j: pl.BlockSpec((1, None, 1, size, length), lambda r, h: (r, j, h, 0, 0))
    whole = pl.BlockSpec((1, 1, size, length), lambda r, h: (r, h, 0, 0))
    fixed = lambda *dims: pl.BlockSpec(dims, lambda r, h: (0,) * len(dims))
    shape = jax.ShapeDtypeStruct
    count = rows * heads
    dma = lambda n: pltpu.SemaphoreType.DMA((n,))
    return pl.pallas_call(
        partial(attend_back_reduce_kernel, block, inner, size**-0.5),
        grid=(rows, heads),
        in_specs=[
            pl.BlockSpec((1, length, 1), lambda r, h: (r, 0, 0)),
            pl.BlockSpec((1, 1, length), lambda r, h: (r, 0, 0)),
            part(0),
            part(1),
            part(2),
            whole,
            whole,
            pl.BlockSpec((1, 1, 1, length), lambda r, h: (r, h, 0, 0)),
            pl.BlockSpec((1, length, width), lambda r, h: (r, 0, 0)),
            fixed(4, depth, width),
            fixed(depth, 2 * half),
        ],
        out_specs=[pl.BlockSpec(memory_space=pl.ANY), fixed(4, depth, features), fixed(depth, own), fixed(half, own)],
        out_shape=[
            shape((rows, 3, 4, heads, size, length // 4), BF16),
            shape((4, depth, features), F32),
            shape((depth, own), F32),
            shape((half, own), F32),
        ],
        scratch_shapes=[
            pltpu.VMEM((rows, 3, heads, size, length), BF16),
            pltpu.VMEM((length, size), F32),
            pltpu.VMEM((length, size), F32),
            pltpu.VMEM((length, size), BF16),
            pltpu.VMEM((length, size), BF16),
            pltpu.VMEM((features, length), F32),
            pltpu.VMEM((features, width), F32),
            pltpu.VMEM((width, features), F32),
            pltpu.VMEM((4, depth, features), BF16),
            pltpu.VMEM((4, depth, features), BF16),
            pltpu.VMEM((4, depth, width), BF16),
            pltpu.VMEM((3, depth, width), BF16),
            pltpu.VMEM((4, depth, own), BF16),
            pltpu.VMEM((3, depth, own), BF16),
            pltpu.VMEM((2, depth, half), F32),
            pltpu.VMEM((depth, half), F32),
            dma(3 * count),
            dma(3 * count),
            dma(count),
            dma(3),
            dma(3),
            dma(3),
            dma(3),
            dma(2),
            dma(2),
        ],
        compiler_params=pltpu.CompilerParams(vmem_limit_bytes=56 << 20, collective_id=3, has_side_effects=True),
        cost_estimate=pl.CostEstimate(
            flops=20 * rows * heads * length * length * 128,
            bytes_accessed=16 * rows * heads * length * size,
            transcendentals=rows * heads * length * length,
        ),
    )(col, row, packed, packed, packed, out, grad_out, lse, normed, proj, down)


def last_kernel(
    slot_col,
    seg,
    table,
    grads,
    weight,
    tokens,
    grad_middle,
    slot_sums,
    pick,
    conditioning,
    biases,
    qkv,
    cond,
    ada,
    grad_tokens,
    ada_ref,
    cond_ref,
    ada_bias_ref,
    qv_bias_ref,
    proj_bias_ref,
    up_bias_ref,
    down_bias_ref,
    qkv_ref,
    ada_here,
    image_sums,
    feature_sums,
    mod,
    got,
    lines,
    lines_got,
    low_all,
    small_core,
    small_chip,
    small_seq,
    cond_all,
    column_got,
    chip_out,
    chip_got,
    piece_out,
    piece_got,
    ada_came,
    sent,
    came,
):
    step, rows = pl.program_id(0), pl.num_programs(0)
    seq, group = lax.axis_index("seq"), lax.axis_index("rows")
    width = tokens.shape[-1]
    images = image_sums.shape[0]
    columns = mod.shape[2]
    own = width // 4
    chip, core = lax.div(group, 2), lax.rem(group, 2)
    seq_peers = peers_of(seq)
    to_seq = [{"seq": peer} for peer in seq_peers]
    rows_peers = [lax.rem(group + m, 8) for m in range(8)]
    to_row = [{"rows": peer} for peer in rows_peers]
    chips = [lax.rem(chip + k, 4) for k in range(4)]
    load_ada = pltpu.make_async_copy(ada, ada_here, ada_came)
    used = [0]

    def copy_to(source, target, device):
        used[0] += 1
        return send_to(source, target, sent.at[used[0] - 1], came.at[used[0] - 1], device)

    chip_copies = [copy_to(chip_out.at[chips[k]], chip_got.at[k - 1], {"rows": 2 * chips[k] + core}) for k in range(1, 4)]
    column_copies = [copy_to(cond.at[rows_peers[m]], column_got.at[group], to_row[m]) for m in range(1, 8)]
    mod_copies = [copy_to(mod.at[seq_peers[m]], got.at[m], to_seq[m]) for m in range(3)]
    line_copies = [copy_to(lines.at[seq_peers[m]], lines_got.at[m], to_seq[m]) for m in range(3)]
    core_peer = {"rows": group + 1 - 2 * core}
    chip_peers = [{"rows": 2 * chips[k] + core} for k in range(4)]
    low_core = copy_to(low_all.at[chip, core], low_all.at[chip, core], core_peer)
    low_chips = [copy_to(low_all.at[chip, core], low_all.at[chip, core], chip_peers[k]) for k in range(1, 4)]
    before = [lax.rem(chip + 4 - k, 4) for k in range(4)]
    low_on = [copy_to(low_all.at[before[k], core], low_all.at[before[k], core], core_peer) for k in range(1, 4)]
    small_over = copy_to(small_core.at[core], small_core.at[core], core_peer)
    small_chips = [copy_to(small_chip.at[chip], small_chip.at[chip], chip_peers[k]) for k in range(1, 4)]
    small_copies = [copy_to(small_seq.at[seq], small_seq.at[seq], to_seq[m]) for m in range(3)]
    cond_copies = [copy_to(cond_all.at[seq], cond_all.at[seq], to_seq[m]) for m in range(3)]
    base = used[0]

    @pl.when(step == 0)
    def _():
        load_ada.start()
        greet(to_seq + to_row[1:])
        chip_out[...] = qkv[...].astype(BF16)
        for copy in chip_copies + column_copies:
            copy.start()
        column_got[group] = cond[group]
        image_sums[...] = jnp.zeros_like(image_sums)
        feature_sums[...] = jnp.zeros_like(feature_sums)

    grad_low = grads[0]
    grad_normed = jnp.dot(weight[...], grad_low, preferred_element_type=F32).T
    ones = jnp.ones((8, grad_low.shape[1]), BF16)
    feature_sums[...] += lax.dot_general(ones, grad_low, (((1,), (1,)), ((), ())), preferred_element_type=F32)
    normal, inverse = normalize(tokens[0].astype(F32))
    scale_a = per_token(slot_col[...], seg[0], table[0, :, width : 2 * width])
    grad_tokens[0] = grad_middle[0] + normalize_back(normal, inverse, grad_normed * (1.0 + scale_a))
    late = [per_slot(slot_col[...], seg[0], piece) for piece in (grad_normed, grad_normed * normal)]
    slots = jnp.concatenate(late + [slot_sums[0]], axis=1)
    image_sums[...] += jnp.dot(pick[0], slots, precision=lax.Precision.HIGHEST, preferred_element_type=F32)

    @pl.when(step == rows - 1)
    def _():
        for place in range(4):
            mod[place] = image_sums[:, place * columns : (place + 1) * columns]
        lines[...] = jnp.zeros_like(lines)
        for line in range(8):
            value = biases[line : line + 1]
            if line < 2:
                value = feature_sums[0:1, 2 * line * width : (2 * line + 1) * width]
            lines[line // 2, line % 2 : line % 2 + 1, :width] = value
        for copy in mod_copies + line_copies:
            copy.start()
        for copy in chip_copies:
            copy.wait()
        for copy in column_copies:
            copy.wait()
        mine = qkv[chip]
        for k in range(3):
            mine = mine + chip_got[k].astype(F32)
        for part in range(3):
            piece_out[part] = mine[:, part * own : (part + 1) * own]

        def piece(part):
            index = part * 4 + seq
            target, place = lax.div(index, 3), lax.rem(index, 3)
            copy = send_to(piece_out.at[part], piece_got.at[place], sent.at[base + part], came.at[base + place], {"seq": target})
            return copy, target, place

        def arriving(place):
            source = lax.rem(3 * seq + place, 4)
            copy = send_to(piece_out.at[0], piece_got.at[place], sent.at[base], came.at[base + place], {"seq": source})
            return copy, source

        for part in range(3):
            copy, target, place = piece(part)

            @pl.when(target != seq)
            def _():
                copy.start()

            @pl.when(target == seq)
            def _():
                piece_got[place] = piece_out[part]

        total = mod[seq]
        for m, copy in enumerate(mod_copies):
            copy.wait()
            total = total + got[m]
        low = total.astype(BF16)
        low_all[chip, core] = low
        low_core.start()
        for copy in low_chips:
            copy.start()
        small = lines[seq]
        for m, copy in enumerate(line_copies):
            copy.wait()
            small = small + lines_got[m]
        small_core[core] = small
        small_core[core, 2:3] = jnp.sum(total, axis=0, keepdims=True)
        small_over.start()
        load_ada.wait()
        cond_all[seq] = lax.dot_general(low, ada_here[...], (((1,), (1,)), ((), ())), preferred_element_type=F32)
        for copy in cond_copies:
            copy.start()
        small_over.wait()
        small_chip[chip] = small_core[0] + small_core[1]
        for copy in small_chips:
            copy.start()
        for came_in, going_on in zip(low_chips, low_on):
            came_in.wait()
            going_on.start()
        for copy in small_chips:
            copy.wait()
        small_seq[seq] = (small_chip[0] + small_chip[1]) + (small_chip[2] + small_chip[3])
        for copy in small_copies:
            copy.start()
        low_core.wait()
        for copy in low_on:
            copy.wait()
        gathered = jnp.concatenate([low_all[m // 2, m % 2] for m in range(8)], axis=0)
        blocks = jnp.concatenate([column_got[m] for m in range(8)], axis=0)
        ada_ref[...] = lax.dot_general(blocks, gathered, (((0,), (0,)), ((), ())), preferred_element_type=F32)
        for part in range(3):
            copy, target, place = piece(part)

            @pl.when(target != seq)
            def _():
                copy.wait_send()

        for place in range(3):
            copy, source = arriving(place)

            @pl.when(source != seq)
            def _():
                copy.wait_recv()

        for place in range(3):
            qkv_ref[:, place * own : (place + 1) * own] = piece_got[place]
        for copy in cond_copies:
            copy.wait()
        term = (cond_all[0] + cond_all[1]) + (cond_all[2] + cond_all[3])
        value = conditioning[...]
        gate = 1.0 / (1.0 + jnp.exp(-value))
        cond_ref[...] = term * gate * (1.0 + value * (1.0 - gate))
        for copy in small_copies:
            copy.wait()
        for place in range(4):
            ada_bias_ref[:, place * columns : (place + 1) * columns] = small_seq[place, 2:3]
        qv_bias_ref[...] = small_seq[0, 0:2, :width]
        proj_bias_ref[...] = small_seq[1, 0:1, :width]
        for line in range(3, 7):
            up_bias_ref[:, (line - 3) * width : (line - 2) * width] = small_seq[line // 2, line % 2 : line % 2 + 1, :width]
        down_bias_ref[...] = small_seq[3, 1:2, :width]


def finish_all(slot_col, seg, table, grads, weight, tokens, grad_middle, slot_sums, pick, conditioning, biases, qkv, cond, ada):
    rows, length, width = tokens.shape
    images, columns = conditioning.shape[0], ada.shape[1]
    depth, own = width // 8, width // 4
    fixed = lambda *dims: pl.BlockSpec(dims, lambda r: (0,) * len(dims), pipeline_mode=pl.Buffered(buffer_count=1))
    result = lambda *dims: pl.BlockSpec(dims, lambda r: (0,) * len(dims))
    row = lambda *dims: pl.BlockSpec((1,) + dims, lambda r: (r, 0, 0))
    shape = jax.ShapeDtypeStruct
    vmem = lambda dtype, *dims: pltpu.VMEM(dims, dtype)
    copies = 3 + 7 + 3 + 3 + 1 + 3 + 3 + 1 + 3 + 3 + 3 + 3
    return pl.pallas_call(
        last_kernel,
        grid=(rows,),
        in_specs=[
            fixed(*slot_col.shape),
            row(1, length),
            row(*table.shape[1:]),
            row(3 * width, length),
            fixed(width, 3 * width),
            row(length, width),
            row(length, width),
            row(*slot_sums.shape[1:]),
            row(*pick.shape[1:]),
            fixed(images, width),
            fixed(8, width),
            fixed(4, depth, 3 * own),
            fixed(8, images, depth),
            pl.BlockSpec(memory_space=pl.ANY),
        ],
        out_specs=[
            row(length, width),
            result(depth, columns),
            result(images, width),
            result(1, 4 * columns),
            result(2, width),
            result(1, width),
            result(1, 4 * width),
            result(1, width),
            result(depth, 3 * own),
        ],
        out_shape=[
            shape((rows, length, width), F32),
            shape((depth, columns), F32),
            shape((images, width), F32),
            shape((1, 4 * columns), F32),
            shape((2, width), F32),
            shape((1, width), F32),
            shape((1, 4 * width), F32),
            shape((1, width), F32),
            shape((depth, 3 * own), F32),
        ],
        scratch_shapes=[
            vmem(BF16, width, columns),
            vmem(F32, images, 6 * width),
            vmem(F32, 8, 3 * width),
            vmem(F32, 4, images, columns),
            vmem(F32, 3, images, columns),
            vmem(F32, 4, 8, columns),
            vmem(F32, 3, 8, columns),
            vmem(BF16, 4, 2, images, columns),
            vmem(F32, 2, 8, columns),
            vmem(F32, 4, 8, columns),
            vmem(F32, 4, 8, columns),
            vmem(F32, 4, images, width),
            vmem(BF16, 8, images, depth),
            vmem(BF16, 4, depth, 3 * own),
            vmem(BF16, 3, depth, 3 * own),
            vmem(F32, 3, depth, own),
            vmem(F32, 3, depth, own),
            pltpu.SemaphoreType.DMA,
            pltpu.SemaphoreType.DMA((copies,)),
            pltpu.SemaphoreType.DMA((copies,)),
        ],
        compiler_params=pltpu.CompilerParams(vmem_limit_bytes=56 << 20, collective_id=5, has_side_effects=True),
        cost_estimate=pl.CostEstimate(flops=5 * 10**9, bytes_accessed=3 * 10**7, transcendentals=0),
    )(slot_col, seg, table, grads, weight, tokens, grad_middle, slot_sums, pick, conditioning, biases, qkv, cond, ada)


def first_kernel(
    slot_col,
    image_col,
    seg,
    fill,
    conditioning,
    ada_bias,
    qv_bias,
    tokens,
    ada,
    weight,
    normed_ref,
    packed_ref,
    table_ref,
    code_row,
    code_col,
    here,
    normed_all,
    packed_all,
    ada_here,
    windows,
    turned,
    own_weight,
    bias_turned,
    mod_all,
    table,
    seg_all,
    load_sem,
    own_sem,
    mod_sent,
    mod_came,
    sent,
    came,
    forward_sent,
    forward_came,
    store_sem,
):
    rows, _, local, width = here.shape
    _, parts, heads, size, _ = packed_all.shape
    own = heads * size
    columns = ada_here.shape[1]
    seq = lax.axis_index("seq")
    places = [seq] + peers_of(seq)
    peers = [{"seq": place} for place in places]
    forward_rows = rows // 2

    greet(peers[1:])

    def direct(r, m):
        index = r * 2 + m - 1
        return send_to(tokens.at[r], here.at[r, m], sent.at[index], came.at[index], peers[m])

    def forward(r):
        source, target = (2, 1) if r < forward_rows else (1, 2)
        return send_to(here.at[r, source], here.at[r, 3], forward_sent.at[r], forward_came.at[r], peers[target])

    for r in range(rows):
        for m in (1, 2):
            direct(r, m).start()
    own_copies = [pltpu.make_async_copy(tokens.at[r], here.at[r, 0], own_sem.at[r]) for r in range(rows)]
    load_ada = pltpu.make_async_copy(ada, ada_here, load_sem.at[0])
    load_ada.start()
    load_windows = []
    for part in range(3):
        lanes = pl.ds(pl.multiple_of(part * width + seq * 256, 128), 384)
        load_windows.append(pltpu.make_async_copy(weight.at[:, lanes], windows.at[part], load_sem.at[1 + part]))
    for copy in load_windows + own_copies:
        copy.start()

    value = conditioning[...].astype(F32)
    low = (value / (1.0 + jnp.exp(-value))).astype(BF16)
    load_ada.wait()
    mod_all[seq] = jnp.dot(low, ada_here[...], preferred_element_type=F32)
    mod_copies = [
        send_to(mod_all.at[seq], mod_all.at[seq], mod_sent.at[m - 1], mod_came.at[m - 1], peers[m]) for m in range(1, 4)
    ]
    for copy in mod_copies:
        copy.start()

    for m in range(4):
        lanes = pl.ds(pl.multiple_of(places[m] * local, 128), local)
        found = seg[:, lanes]
        where = places[m] * local + lax.broadcasted_iota(jnp.int32, (rows, local), 1)
        code = jnp.where(where < fill[...], found, -1 - where)
        for r in range(rows):
            seg_all[r, m] = found[r : r + 1]
            code_row[r, :, m * local : (m + 1) * local] = code[r : r + 1]
            column = jnp.broadcast_to(code[r : r + 1].astype(F32), (128, local)).T[:, :1]
            code_col[r, m * local : (m + 1) * local] = column.astype(jnp.int32)

    for part in range(3):
        load_windows[part].wait()
        turned[...] = windows[part].astype(F32).T
        own_weight[part * own : (part + 1) * own] = turned[pl.ds(pl.multiple_of(seq * 32, 8), own), :].astype(BF16)
    window = qv_bias[:, pl.ds(pl.multiple_of(seq * 256, 128), 384)].astype(F32)
    bias_turned[...] = jnp.concatenate([window, jnp.zeros((6, 384), F32)], axis=0).T
    bias = bias_turned[pl.ds(pl.multiple_of(seq * 32, 8), own), :]
    bias = jnp.concatenate([bias[:, 0:1], jnp.zeros((own, 1), F32), bias[:, 1:2]], axis=0)

    for copy in mod_copies:
        copy.wait()
    images = conditioning.shape[0]
    slots = image_col.shape[1]
    for place in range(4):
        lanes = slice(place * columns, (place + 1) * columns)
        table[:, lanes] = mod_all[place] + ada_bias[:, lanes].astype(F32)
    stacked = jnp.concatenate(split_low(table[...]), axis=0)
    image_row = lax.rem(lax.broadcasted_iota(jnp.int32, (slots, 3 * images), 1), images)
    for r in range(rows):
        picked = (image_col[r] == image_row).astype(BF16)
        table_ref[r] = jnp.dot(picked, stacked, preferred_element_type=F32)

    def stores(r, m):
        index = r * 4 + m
        lanes = pl.ds(m * local, local)
        return (
            pltpu.make_async_copy(normed_all.at[r, m], normed_ref.at[r, m], store_sem.at[0, index]),
            pltpu.make_async_copy(packed_all.at[r, :, :, :, lanes], packed_ref.at[r, :, :, :, lanes], store_sem.at[1, index]),
        )

    def work(r, m):
        mods = per_token(slot_col[...], seg_all[r, m], table_ref[r, :, : 2 * width])
        normal, _ = normalize(here[r, m].astype(F32))
        normed = (normal * (1.0 + mods[:, width:]) + mods[:, :width]).astype(BF16)
        normed_all[r, m] = normed
        mixed = lax.dot_general(own_weight[...], normed, (((1,), (1,)), ((), ())), preferred_element_type=F32)
        mixed = (mixed + bias).astype(BF16)
        for part in range(parts):
            for head in range(heads):
                start = (part * heads + head) * size
                packed_all[r, part, head, :, m * local : (m + 1) * local] = mixed[start : start + size]
        for copy in stores(r, m):
            copy.start()

    for r in range(rows):
        own_copies[r].wait()
        work(r, 0)
    for r in range(rows):
        for m in (2, 1) if r < forward_rows else (1, 2):
            direct(r, m).wait()
            if m == (2 if r < forward_rows else 1):
                forward(r).start()
    for r in range(rows):
        for m in (1, 2):
            work(r, m)
    for r in range(rows):
        forward(r).wait()
        work(r, 3)
    for r in range(rows):
        for m in range(4):
            for copy in stores(r, m):
                copy.wait()


def start_rows(slot_col, image_col, seg, fill, conditioning, ada_bias, qv_bias, tokens, ada, weight):
    rows, local, width = tokens.shape
    length = 4 * local
    images, slots = conditioning.shape[0], image_col.shape[1]
    heads, size = HEADS // 4, width // HEADS
    columns = ada.shape[1]
    shape = jax.ShapeDtypeStruct
    vmem = lambda dtype, *dims: pltpu.VMEM(dims, dtype)
    near, far = pl.BlockSpec(memory_space=pltpu.VMEM), pl.BlockSpec(memory_space=pl.ANY)
    dma = lambda *dims: pltpu.SemaphoreType.DMA(dims)
    return pl.pallas_call(
        first_kernel,
        in_specs=[near] * 7 + [far] * 3,
        out_specs=[far, far, near, near, near],
        out_shape=[
            shape((rows, 4, local, width), BF16),
            shape((rows, 3, heads, size, length), BF16),
            shape((rows, slots, 6 * width), F32),
            shape((rows, 1, length), jnp.int32),
            shape((rows, length, 1), jnp.int32),
        ],
        scratch_shapes=[
            vmem(BF16, rows, 4, local, width),
            vmem(BF16, rows, 4, local, width),
            vmem(BF16, rows, 3, heads, size, length),
            vmem(BF16, width, columns),
            vmem(BF16, 3, width, 384),
            vmem(F32, 384, width),
            vmem(BF16, 3 * heads * size, width),
            vmem(F32, 384, 8),
            vmem(F32, 4, images, columns),
            vmem(F32, images, 6 * width),
            vmem(jnp.int32, rows, 4, 1, local),
            dma(4),
            dma(rows),
            dma(3),
            dma(3),
            dma(2 * rows),
            dma(2 * rows),
            dma(rows),
            dma(rows),
            dma(2, 4 * rows),
        ],
        compiler_params=pltpu.CompilerParams(vmem_limit_bytes=56 << 20, collective_id=6, has_side_effects=True),
        cost_estimate=pl.CostEstimate(flops=5 * 10**9, bytes_accessed=3 * 10**7, transcendentals=0),
    )(slot_col, image_col, seg, fill, conditioning, ada_bias, qv_bias, tokens, ada, weight)


def gather_seq(values):
    count = lax.axis_size("seq")
    if count == 4:
        first, second = swap(values, "seq", 1), swap(values, "seq", 2)
        half = values.shape[0] // 2
        third = jnp.concatenate([swap(second[:half], "seq", 1), swap(first[half:], "seq", 2)], axis=0)
        return [values, first, second, third]
    return [values] + [swap(values, "seq", m) for m in range(1, count)]


def exchange_seq(blocks):
    return [blocks[0]] + [swap(blocks[m], "seq", m) for m in range(1, len(blocks))]


def in_order(blocks, axis):
    index = lax.axis_index("seq")
    stacked = jnp.stack(blocks, axis=axis)
    return flip_blocks(stacked, axis, index)


class Halving:
    def __init__(self, blocks, low_first):
        self.blocks = dict(enumerate(blocks))
        bits = [1 << k for k in range(len(blocks).bit_length() - 1)]
        self.bits = bits if low_first else bits[::-1]

    def send(self):
        self.bit = self.bits.pop(0)
        self.kept = [m for m in self.blocks if not m & self.bit]
        return jnp.stack([self.blocks[m | self.bit] for m in self.kept]).astype(BF16)

    def move(self, sent):
        return swap(sent, "seq", self.bit)

    def add(self, came):
        self.blocks = {m: self.blocks[m] + came[k].astype(F32) for k, m in enumerate(self.kept)}


class Spreading:
    def __init__(self, pick):
        chip, chips = lax.axis_index("rows") // 2, lax.axis_size("rows") // 2
        self.own = pick(chip)
        self.sent = [pick(chip ^ m).astype(BF16) for m in range(1, chips)]

    def move(self):
        self.came = [swap(block, "rows", 2 * (m + 1)) for m, block in enumerate(self.sent)]

    def total(self):
        total = self.own
        for block in self.came:
            total = total + block.astype(F32)
        return total


def columns_of(values, index, size):
    return lax.dynamic_slice_in_dim(values, index * size, size, values.ndim - 1)


def lines_of(values, index, size):
    return lax.dynamic_slice_in_dim(values, index * size, size, 0)


def tied(*values):
    return lax.optimization_barrier(values)


def on_square(
    tokens,
    conditioning,
    segment_ids,
    image_index,
    row_fill,
    ada_weight,
    ada_bias,
    qkv_weight,
    qv_bias,
    proj_weight,
    proj_bias,
    up_weight,
    up_bias,
    down_weight,
    down_bias,
    cotangent,
):
    row_count, local_len, width = tokens.shape
    seq_count, groups = lax.axis_size("seq"), lax.axis_size("rows")
    seq_index, row_index = lax.axis_index("seq"), lax.axis_index("rows")
    chips, core = groups // 2, row_index % 2
    full_len = local_len * seq_count
    token_count = row_count * local_len
    heads_dev = HEADS // seq_count
    head_size = width // HEADS
    own = heads_dev * head_size
    image_count = conditioning.shape[0]
    hidden_size = up_weight.shape[1]
    depth = width // groups

    slot_ids = lax.iota(jnp.int32, image_index.shape[1])
    slot_col = jnp.tile(slot_ids, 3)[:, None]
    normed_all, packed, slot_mod, code_row, code_col = start_rows(
        slot_col,
        image_index[:, :, None],
        segment_ids,
        row_fill[:, None],
        conditioning,
        ada_bias[None],
        qv_bias,
        tokens,
        ada_weight,
        qkv_weight,
    )
    normed_all = normed_all.reshape(row_count, full_len, width)
    cond_wide = conditioning.astype(F32)
    cond_cols = jax.nn.silu(cond_wide).astype(BF16).reshape(image_count, groups, depth).transpose(1, 0, 2)
    local_seg = lax.dynamic_slice_in_dim(segment_ids, seq_index * local_len, local_len, 1)

    attended, log_totals, attended_sent = attend(packed, code_col, code_row, 512, True)
    seg_row = local_seg[:, None, :]
    attended_tok = attended_sent.reshape(row_count, width, local_len)
    branch_a, middle, normed_b, grad_out, normed_turned, grad_turned, part_down_bias = before_feed_forward(
        slot_col, seg_row, slot_mod, attended_tok, proj_weight, proj_bias.astype(F32)[None], tokens, cotangent
    )
    out_sum, grad_sum, part_up_bias, grad_up_weight, down_turned = feed_forward_reduce(
        normed_b, grad_out, normed_turned, grad_turned, up_weight, down_weight, up_bias.astype(F32)
    )
    block_out, grad_middle, slot_sums, part_proj_bias, grad_view, proj_both = after_feed_forward(
        slot_col,
        seg_row,
        slot_mod,
        attended_tok,
        proj_weight,
        down_bias.astype(F32)[None],
        out_sum,
        grad_sum,
        middle,
        branch_a,
        cotangent,
    )
    grad_view = grad_view.reshape(row_count, heads_dev, head_size, full_len)
    grad_sent, qkv_both, grad_proj_weight, grad_down_weight = attend_back_reduce(
        packed, attended, grad_view, log_totals, code_col, code_row, normed_all, proj_both, down_turned, 256, 512
    )
    grad_flat = grad_sent.reshape(row_count, 3 * width, local_len)
    pick = (image_index[:, None, :] == lax.iota(jnp.int32, image_count)[None, :, None]).astype(F32)
    biases = jnp.concatenate(
        [jnp.zeros((2, width), F32), part_proj_bias, part_up_bias.reshape(4, width), part_down_bias], axis=0
    )
    (
        grad_tokens,
        grad_ada_weight,
        grad_cond,
        grad_ada_bias,
        grad_qv_bias,
        grad_proj_bias,
        grad_up_bias,
        grad_down_bias,
        grad_qkv_weight,
    ) = finish_all(
        slot_col,
        seg_row,
        slot_mod,
        grad_flat,
        qkv_weight,
        tokens,
        grad_middle,
        slot_sums,
        pick,
        cond_wide,
        biases,
        qkv_both,
        cond_cols,
        ada_weight,
    )
    return (
        block_out,
        grad_tokens,
        grad_cond,
        grad_ada_weight,
        grad_ada_bias[0],
        grad_qkv_weight,
        grad_qv_bias,
        grad_proj_weight,
        grad_proj_bias[0],
        grad_up_weight,
        grad_up_bias[0],
        grad_down_weight,
        grad_down_bias[0],
    )


def on_device(
    tokens,
    conditioning,
    segment_ids,
    image_index,
    row_fill,
    ada_weight,
    ada_bias,
    qkv_weight,
    qv_bias,
    proj_weight,
    proj_bias,
    up_weight,
    up_bias,
    down_weight,
    down_bias,
    cotangent,
):
    row_count, local_len, width = tokens.shape
    seq_count, groups = lax.axis_size("seq"), lax.axis_size("rows")
    seq_index, row_index = lax.axis_index("seq"), lax.axis_index("rows")
    chips, core = groups // 2, row_index % 2
    full_len = local_len * seq_count
    token_count = row_count * local_len
    heads_dev = HEADS // seq_count
    head_size = width // HEADS
    own = heads_dev * head_size
    image_count = conditioning.shape[0]
    hidden_size = up_weight.shape[1]
    depth = width // groups

    tokens_all = jnp.concatenate(gather_seq(tokens), axis=1)
    order = lax.iota(jnp.int32, seq_count) ^ seq_index
    seg_blocks = flip_blocks(segment_ids.reshape(row_count, seq_count, local_len), 1, seq_index)
    seg_all = seg_blocks.reshape(row_count, full_len)
    places = (order[:, None] * local_len + lax.iota(jnp.int32, local_len)).reshape(1, full_len)
    codes = jnp.where(places < row_fill[:, None], seg_all, -1 - places)
    code_col, code_row = codes[:, :, None], codes[:, None, :]

    qkv_own = jnp.concatenate(
        [lax.dynamic_slice_in_dim(qkv_weight, part * width + seq_index * own, own, 1).T for part in range(3)], axis=0
    )
    bias_own = lax.dynamic_slice_in_dim(qv_bias.astype(F32), seq_index * own, own, 1)
    bias_own = jnp.concatenate([bias_own[0], jnp.zeros((own,), F32), bias_own[1]])

    cond_wide = conditioning.astype(F32)
    cond_low = jax.nn.silu(cond_wide).astype(BF16)
    mod_part = jnp.dot(cond_low, ada_weight, preferred_element_type=F32)
    modulation = lax.all_gather(mod_part, "seq", axis=1, tiled=True) + ada_bias.astype(F32)
    cond_cols = cond_low.reshape(image_count, groups, depth).transpose(1, 0, 2)
    local_seg = lax.dynamic_slice_in_dim(segment_ids, seq_index * local_len, local_len, 1)
    slot_ids = lax.iota(jnp.int32, image_index.shape[1])
    slot_mod = jnp.take(modulation, image_index, axis=0)

    normed_all, packed = project_qkv(
        tokens_all, seg_all, slot_mod[:, :, : 2 * width], qkv_own, bias_own, heads_dev, min(256, full_len)
    )
    square = seq_count == 4 and chips == 4
    attended, log_totals, *attended_sent = attend(packed, code_col, code_row, 512, square)

    slot_pick = (local_seg[:, :, None] == slot_ids).astype(F32)
    mod_tok = jnp.einsum("rts,rse->rte", slot_pick, slot_mod, precision=lax.Precision.HIGHEST)
    shift_a, scale_a, gate_a, shift_b, scale_b, gate_b = jnp.split(mod_tok, 6, axis=-1)
    tokens_wide = tokens.astype(F32)
    upstream = cotangent.astype(F32)
    grad_branch_b = (upstream * gate_b).astype(BF16)
    part_down_bias = jnp.sum(grad_branch_b.astype(F32), axis=(0, 1))
    grad_out = grad_branch_b.reshape(token_count, width)
    grad_turned = turn_halves(grad_out, seq_count, core)

    def by_block(values):
        return [values[..., m * local_len : (m + 1) * local_len] for m in range(seq_count)]

    if square:
        attended_tok = attended_sent[0]
    else:
        attended_tok = in_order(exchange_seq(by_block(attended.reshape(row_count, own, full_len))), 1)
    attended_tok = attended_tok.reshape(row_count, width, local_len)
    branch_a = jnp.einsum(
        "rft,fe->rte", attended_tok, proj_weight, preferred_element_type=F32
    ) + proj_bias.astype(F32)
    middle = tokens_wide + gate_a * branch_a
    normed_b = modulate(middle, shift_b, scale_b).astype(BF16).reshape(token_count, width)
    normed_turned = turn_halves(normed_b, chips, core)

    if square:
        out_sum, grad_sum, part_up_bias, grad_up_weight, down_turned = feed_forward_reduce(
            normed_b, grad_out, normed_turned, grad_turned, up_weight, down_weight, up_bias.astype(F32)
        )
        part_up_bias = part_up_bias.reshape(1, hidden_size)
    else:
        out_sum, grad_sum, up_keep, up_send, down_keep, down_send, part_up_bias = feed_forward(
            normed_b, grad_out, normed_turned, grad_turned, up_weight, down_weight, up_bias.astype(F32)[None], 512
        )
        up_came, down_came = swap(up_send, "rows", 1), swap(down_send, "rows", 1)
    branch_b = out_sum.reshape(row_count, local_len, width) + down_bias.astype(F32)
    grad_normed_b = grad_sum.reshape(row_count, local_len, width)
    block_out = (middle + gate_b * branch_b).astype(BF16)
    grad_gate_b = upstream * branch_b
    _, norm_back_b = jax.vjp(modulate, middle, shift_b, scale_b)
    grad_mid_norm, grad_shift_b, grad_scale_b = norm_back_b(grad_normed_b)
    grad_middle = upstream + grad_mid_norm
    grad_branch_a = (grad_middle * gate_a).astype(BF16)
    grad_gate_a = grad_middle * branch_a
    part_proj_bias = jnp.sum(grad_branch_a.astype(F32), axis=(0, 1))
    grad_attended = jnp.einsum(
        "fe,rte->rft", proj_weight, grad_branch_a, preferred_element_type=F32
    ).astype(BF16)
    heads_blocks = [lax.dynamic_slice_in_dim(grad_attended, (seq_index ^ m) * own, own, 1) for m in range(seq_count)]
    grad_heads_in = jnp.concatenate(exchange_seq(heads_blocks), axis=2)
    grad_view = grad_heads_in.reshape(row_count, heads_dev, head_size, full_len)

    part_proj = jnp.einsum("rte,rft->ef", grad_branch_a, attended_tok, preferred_element_type=F32)
    proj_view = part_proj.reshape(seq_count, 2, depth * groups // (2 * seq_count), width)
    proj_keep = lax.dynamic_index_in_dim(proj_view, core, 1, keepdims=False)
    proj_send = lax.dynamic_index_in_dim(proj_view, 1 - core, 1, keepdims=False).astype(BF16)
    proj_came = swap(proj_send, "rows", 1).reshape(width // 2, width)
    proj_keep = proj_keep.reshape(width // 2, width)
    up_size, down_size = hidden_size // seq_count, width // (2 * seq_count)
    proj_blocks = [
        lines_of(proj_keep, seq_index ^ m, down_size) + lines_of(proj_came, seq_index ^ m, down_size).astype(F32)
        for m in range(seq_count)
    ]
    if square:
        proj_sent = [block.astype(BF16) for block in proj_blocks[1:]]
        grad_view, *proj_sent = tied(grad_view, *proj_sent)
        proj_total = proj_blocks[0]
        for m in range(1, seq_count):
            proj_total = proj_total + swap(proj_sent[m - 1], "seq", m).astype(F32)
    else:
        ups = Halving(
            [
                columns_of(up_keep, seq_index ^ m, up_size) + columns_of(up_came, seq_index ^ m, up_size).astype(F32)
                for m in range(seq_count)
            ],
            True,
        )
        downs = Halving(
            [
                jnp.concatenate(
                    [
                        lines_of(down_keep, seq_index ^ m, down_size)
                        + lines_of(down_came, seq_index ^ m, down_size).astype(F32),
                        proj_blocks[m],
                    ],
                    axis=1,
                )
                for m in range(seq_count)
            ],
            False,
        )
        up_sent, down_sent = ups.send(), downs.send()
        up_came, down_came = ups.move(up_sent), downs.move(down_sent)

    grad_heads, *grad_sent = attend_back(
        packed, attended, grad_view, log_totals, code_col, code_row, 256, 512, square
    )
    grad_own = grad_heads.reshape(row_count, 3 * own, full_len)
    if square:
        grad_flat = grad_sent[0]
    else:
        grad_blocks = exchange_seq(by_block(grad_own))
        grad_flat = in_order([block.reshape(row_count, 3, own, local_len) for block in grad_blocks], 2)
    grad_flat = grad_flat.reshape(row_count, 3 * width, local_len)

    qkv_keep, qkv_send, own_sums = qkv_weight_grad(grad_own, normed_all)
    down_part, proj_part = hidden_size // chips, width // chips
    if square:
        proj_spread = Spreading(lambda chip: columns_of(proj_total, chip, proj_part))
        grad_flat, qkv_send, *proj_spread.sent = tied(grad_flat, qkv_send, *proj_spread.sent)
        proj_spread.move()
    else:
        while ups.bits:
            ups.add(up_came)
            downs.add(down_came)
            up_came, down_came = ups.move(ups.send()), downs.move(downs.send())
        ups.add(up_came)
        downs.add(down_came)
        up_total, down_total = ups.blocks[0], downs.blocks[0][:, :hidden_size]
        proj_total = downs.blocks[0][:, hidden_size:]
        up_spread = Spreading(lambda chip: lines_of(up_total, chip, depth))
        down_spread = Spreading(
            lambda chip: jnp.concatenate(
                [columns_of(down_total, chip, down_part), columns_of(proj_total, chip, proj_part)], axis=1
            )
        )
        up_spread.move()
        down_spread.move()
    qkv_came = swap(qkv_send, "rows", 1)
    grad_normed_a = jnp.einsum("rft,df->rtd", grad_flat, qkv_weight, preferred_element_type=F32)
    _, norm_back_a = jax.vjp(modulate, tokens_wide, shift_a, scale_a)
    grad_tok_norm, grad_shift_a, grad_scale_a = norm_back_a(grad_normed_a)
    grad_tokens = grad_middle + grad_tok_norm
    grad_mod_tok = jnp.concatenate(
        [grad_shift_a, grad_scale_a, grad_gate_a, grad_shift_b, grad_scale_b, grad_gate_b], axis=-1
    )
    slot_grads = jnp.einsum("rts,rte->rse", slot_pick, grad_mod_tok, precision=lax.Precision.HIGHEST)
    image_pick = (image_index[:, :, None] == lax.iota(jnp.int32, image_count)).astype(F32)
    grad_modulation = jnp.einsum("rsi,rse->ie", image_pick, slot_grads, precision=lax.Precision.HIGHEST)

    own_sums = own_sums.reshape(3, own)
    part_qv = lax.dynamic_update_slice(
        jnp.zeros((2, width), F32), jnp.stack([own_sums[0], own_sums[2]]), (0, seq_index * own)
    )
    small = jnp.concatenate([part_qv.reshape(-1), part_proj_bias, part_up_bias[0], part_down_bias])
    columns = ada_weight.shape[1]
    lines = -(-small.size // (seq_count * columns))
    room = seq_count * columns * lines
    small = jnp.pad(small, (0, room - small.size)).reshape(seq_count, lines, columns)
    mod_view = grad_modulation.reshape(image_count, seq_count, columns).transpose(1, 0, 2)
    joined = jnp.concatenate(
        [mod_view, jnp.zeros((seq_count, 1, columns), F32), small, jnp.zeros((seq_count, 7 - lines, columns), F32)], axis=1
    )
    qkv_both = qkv_keep + qkv_came.astype(F32)
    qkv_spread = Spreading(lambda chip: lax.dynamic_index_in_dim(qkv_both, chip, 0, keepdims=False))
    joined, *qkv_spread.sent = tied(joined, *qkv_spread.sent)
    qkv_spread.move()
    if square:
        turned = jnp.concatenate([down_turned, proj_spread.total()], axis=1)
    else:
        grad_up_weight, turned = up_spread.total(), down_spread.total()
    half = down_part // 2
    cut = lambda index: jnp.concatenate(
        [columns_of(turned[:, :down_part], index, half), columns_of(turned[:, down_part:], index, proj_part // 2)], axis=1
    )
    core_keep, core_sent = cut(core), cut(1 - core)
    joined, core_sent = tied(joined, core_sent)
    core_came = swap(core_sent, "rows", 1)
    grad_ada_weight, cond_sum, bias_sums = finish(joined, ada_weight, cond_cols, image_count)
    _, silu_back = jax.vjp(jax.nn.silu, cond_wide)
    grad_cond = silu_back(cond_sum)[0]
    grad_ada_bias = bias_sums[:, 0].reshape(-1)
    small = bias_sums[:, 1 : 1 + lines].reshape(-1)
    grad_qv_bias = small[: 2 * width].reshape(2, width)
    grad_proj_bias = small[2 * width : 3 * width]
    grad_up_bias = small[3 * width : 3 * width + hidden_size]
    grad_down_bias = small[3 * width + hidden_size : 4 * width + hidden_size]

    pair = flip_blocks(jnp.stack([core_keep, core_came]), 0, core).reshape(-1, core_keep.shape[1])
    grad_down_weight, grad_proj_weight = pair[:, :half].T, pair[:, half:].T

    qkv_total = qkv_spread.total()
    pieces = []
    for place in range(3):
        pairs = [((3 * target + place) % seq_count, target) for target in range(seq_count)]
        part_of = [0] * seq_count
        for source, target in pairs:
            part_of[source] = (3 * target + place) // seq_count
        chosen = columns_of(qkv_total, jnp.array(part_of, jnp.int32)[seq_index], own)
        pieces.append(lax.ppermute(chosen, "seq", pairs))
    grad_qkv_weight = jnp.concatenate(pieces, axis=1)
    return (
        block_out,
        grad_tokens,
        grad_cond,
        grad_ada_weight,
        grad_ada_bias,
        grad_qkv_weight,
        grad_qv_bias,
        grad_proj_weight,
        grad_proj_bias,
        grad_up_weight,
        grad_up_bias,
        grad_down_weight,
        grad_down_bias,
    )


def solution(mesh):
    in_specs = (
        P("rows", "seq", None),
        P("rows", None),
        P("rows", None),
        P("rows", None),
        P("rows"),
        P(None, "seq"),
        P(),
        P(),
        P(),
        P(),
        P(),
        P(),
        P(),
        P(),
        P(),
        P("rows", "seq", None),
    )
    out_specs = (
        P("rows", "seq", None),
        P("rows", "seq", None),
        P("rows", None),
        P("rows", "seq"),
        P(),
        P("rows", "seq"),
        P(),
        P("rows", "seq"),
        P(),
        P("rows", "seq"),
        P(),
        P("rows", "seq"),
        P(),
    )
    square = mesh.shape["seq"] == 4 and mesh.shape["rows"] == 8
    return jax.shard_map(
        on_square if square else on_device, mesh=mesh, in_specs=in_specs, out_specs=out_specs, check_vma=False
    )
```

```python
from functools import partial
import math

import jax
import jax.numpy as jnp
from jax import lax
from jax.experimental import pallas as pl
from jax.experimental.pallas import tpu as pltpu
from jax.sharding import PartitionSpec as P

HEADS = 16
LOG2E = math.log2(math.e)
VMEM_LIMIT = 60 << 20
BF16 = jnp.bfloat16
F32 = jnp.float32

norm_eps = 1e-06


def modulate(values, offset, factor):
    center = values - jnp.mean(values, axis=-1, keepdims=True)
    spread = jnp.mean(center * center, axis=-1, keepdims=True)
    return center * lax.rsqrt(spread + norm_eps) * (1.0 + factor) + offset


def gelu_tanh(values):
    return jax.nn.gelu(values, approximate=True)


def swap(values, axis, mask):
    count = lax.axis_size(axis)
    return lax.ppermute(values, axis, [(i, i ^ mask) for i in range(count)])


def flip_blocks(values, axis, mask):
    return jnp.take(values, lax.iota(jnp.int32, values.shape[axis]) ^ mask, axis=axis)


def qkv_kernel(slot_row, seg, mod, tokens, weight, bias, normed_ref, qkv_ref):
    width = tokens.shape[-1]
    values = tokens[0].astype(F32)
    picked = (seg[0] == slot_row[...]).astype(BF16)
    table = mod[0]
    high = table.astype(BF16)
    rest = table - high.astype(F32)
    middle = rest.astype(BF16)
    last = (rest - middle.astype(F32)).astype(BF16)
    stacked = jnp.concatenate([high, middle, last], axis=0)
    per_token = jnp.dot(picked, stacked, preferred_element_type=F32)
    normed = modulate(values, per_token[:, :width], per_token[:, width:]).astype(BF16)
    normed_ref[0] = normed
    mixed = lax.dot_general(weight[...], normed, (((1,), (1,)), ((), ())), preferred_element_type=F32)
    mixed = (mixed + bias[...]).astype(BF16)
    _, parts, heads, size, _ = qkv_ref.shape
    for part in range(parts):
        for head in range(heads):
            start = (part * heads + head) * size
            qkv_ref[0, part, head] = mixed[start : start + size]


def project_qkv(tokens, seg, slot_mod, weight, bias, heads, block):
    rows, length, width = tokens.shape
    slots = slot_mod.shape[1]
    features = weight.shape[0]
    size = features // (3 * heads)
    slot_row = jnp.tile(lax.iota(jnp.int32, slots), 3)[None]
    return pl.pallas_call(
        qkv_kernel,
        grid=(rows, length // block),
        in_specs=[
            pl.BlockSpec((1, 3 * slots), lambda r, t: (0, 0)),
            pl.BlockSpec((1, block, 1), lambda r, t: (r, t, 0)),
            pl.BlockSpec((1, slots, 2 * width), lambda r, t: (r, 0, 0)),
            pl.BlockSpec((1, block, width), lambda r, t: (r, t, 0)),
            pl.BlockSpec((features, width), lambda r, t: (0, 0)),
            pl.BlockSpec((features, 1), lambda r, t: (0, 0)),
        ],
        out_specs=[
            pl.BlockSpec((1, block, width), lambda r, t: (r, t, 0)),
            pl.BlockSpec((1, 3, heads, size, block), lambda r, t: (r, 0, 0, 0, t)),
        ],
        out_shape=[
            jax.ShapeDtypeStruct((rows, length, width), BF16),
            jax.ShapeDtypeStruct((rows, 3, heads, size, length), BF16),
        ],
        compiler_params=pltpu.CompilerParams(vmem_limit_bytes=VMEM_LIMIT),
        cost_estimate=pl.CostEstimate(
            flops=2 * rows * length * width * features,
            bytes_accessed=2 * rows * length * (2 * width + features),
            transcendentals=0,
        ),
    )(slot_row, seg[:, :, None], slot_mod, tokens, weight, bias[:, None])


def peers_of(seq):
    x, y = lax.rem(seq, 2), lax.div(seq, 2)
    return [seq + 1 - 2 * x, seq + 2 - 4 * y, 3 - seq]


def greet(devices):
    barrier = pltpu.get_barrier_semaphore()
    for device in devices:
        pl.semaphore_signal(barrier, inc=1, device_id=device, device_id_type=pl.DeviceIdType.MESH)
    pl.semaphore_wait(barrier, len(devices))


def send_block(source, target, sent, came, index, device):
    return pltpu.make_async_remote_copy(
        src_ref=source,
        dst_ref=target,
        send_sem=sent.at[index],
        recv_sem=came.at[index],
        device_id=device,
        device_id_type=pl.DeviceIdType.MESH,
    )


def attend_kernel(block, scale, code_col, code_row, query, key, value, out_ref, lse_ref, token_ref=None, sent=None, came=None, kept=None):
    length = query.shape[-1]
    keys = key[0, 0].astype(F32).T.astype(BF16)
    values = value[0, 0]
    codes = code_col[0]
    row, head = (pl.program_id(0), pl.program_id(1)) if sent is not None else (0, 0)
    rows, heads = out_ref.shape[:2]
    if sent is not None:
        seq = lax.axis_index("seq")
        peers = peers_of(seq)
        size = length // 4

        @pl.when((row == 0) & (head == 0))
        def _():
            greet([{"seq": peer} for peer in peers])

        def to_peer(r, h, m):
            lanes = pl.ds(m * size, size)
            place = (r * heads + h) * 3 + m - 1
            return send_block(out_ref.at[r, h, :, lanes], token_ref.at[r, seq, h], sent, came, place, {"seq": peers[m - 1]})

        def to_self(r, h):
            return pltpu.make_async_copy(out_ref.at[r, h, :, pl.ds(0, size)], token_ref.at[r, seq, h], kept.at[r * heads + h])

    for step in range(length // block):
        here = pl.ds(step * block, block)
        scores = jnp.dot(keys, query[0, 0, :, here], preferred_element_type=F32)
        scores = jnp.where(codes == code_row[0, :, here], scores * scale, -1e30)
        peak = jnp.max(scores, axis=0, keepdims=True)
        raised = jnp.exp2(scores - peak)
        total = jnp.sum(raised, axis=0, keepdims=True)
        probs = (raised * (1.0 / total)).astype(BF16)
        out_ref[row, head, :, here] = jnp.dot(values, probs, preferred_element_type=F32).astype(BF16)
        lse_ref[0, 0, :, here] = peak + jnp.log2(total)

    if sent is not None:
        to_self(row, head).start()
        for m in range(1, 4):
            to_peer(row, head, m).start()

        @pl.when((row == rows - 1) & (head == heads - 1))
        def _():
            for r in range(rows):
                for h in range(heads):
                    to_self(r, h).wait()
                    for m in range(1, 4):
                        to_peer(r, h, m).wait()


def attend(packed, col, row, block, exchange):
    rows, _, heads, size, length = packed.shape
    part = lambda j: pl.BlockSpec((1, None, 1, size, length), lambda r, h: (r, j, h, 0, 0))
    out_specs = [
        pl.BlockSpec((1, 1, size, length), lambda r, h: (r, h, 0, 0)),
        pl.BlockSpec((1, 1, 1, length), lambda r, h: (r, h, 0, 0)),
    ]
    out_shape = [
        jax.ShapeDtypeStruct((rows, heads, size, length), BF16),
        jax.ShapeDtypeStruct((rows, heads, 1, length), F32),
    ]
    scratch = []
    extra = {}
    if exchange:
        out_specs[0] = pl.BlockSpec((rows, heads, size, length), lambda r, h: (0, 0, 0, 0))
        out_specs.append(pl.BlockSpec(memory_space=pl.ANY))
        out_shape.append(jax.ShapeDtypeStruct((rows, 4, heads, size, length // 4), BF16))
        count = rows * heads
        scratch = [pltpu.SemaphoreType.DMA((3 * count,)), pltpu.SemaphoreType.DMA((3 * count,)), pltpu.SemaphoreType.DMA((count,))]
        extra = dict(collective_id=2, has_side_effects=True)
    return pl.pallas_call(
        partial(attend_kernel, block, size**-0.5 * LOG2E),
        grid=(rows, heads),
        in_specs=[
            pl.BlockSpec((1, length, 1), lambda r, h: (r, 0, 0)),
            pl.BlockSpec((1, 1, length), lambda r, h: (r, 0, 0)),
            part(0),
            part(1),
            part(2),
        ],
        out_specs=out_specs,
        out_shape=out_shape,
        scratch_shapes=scratch,
        compiler_params=pltpu.CompilerParams(vmem_limit_bytes=VMEM_LIMIT, **extra),
        cost_estimate=pl.CostEstimate(
            flops=8 * rows * heads * length * length * 128,
            bytes_accessed=8 * rows * heads * length * size,
            transcendentals=rows * heads * length * length,
        ),
    )(col, row, packed, packed, packed)


def attend_back_kernel(
    block,
    inner,
    scale,
    exchange,
    code_col,
    code_row,
    query,
    key,
    value,
    out,
    grad_out,
    lse,
    grad_ref,
    *rest,
):
    length = query.shape[-1]
    size = query.shape[-2]
    row, head = (pl.program_id(0), pl.program_id(1)) if exchange else (0, 0)
    rows, _, heads = grad_ref.shape[:3]
    if exchange:
        token_ref, key_sum, value_sum, keys, values, sent, came, kept = rest
        seq = lax.axis_index("seq")
        peers = peers_of(seq)
        local = length // 4

        @pl.when((row == 0) & (head == 0))
        def _():
            greet([{"seq": peer} for peer in peers])

        def to_peer(r, h, m):
            lanes = pl.ds(m * local, local)
            place = (r * heads + h) * 3 + m - 1
            return send_block(grad_ref.at[r, :, h, :, lanes], token_ref.at[r, :, seq, h], sent, came, place, {"seq": peers[m - 1]})

        def to_self(r, h):
            lanes = pl.ds(0, local)
            return pltpu.make_async_copy(grad_ref.at[r, :, h, :, lanes], token_ref.at[r, :, seq, h], kept.at[r * heads + h])

    else:
        key_sum, value_sum, keys, values = rest
    keys[...] = key[0, 0].astype(F32).T.astype(BF16)
    values[...] = value[0, 0].astype(F32).T.astype(BF16)
    for step in range(length // block):
        here = pl.ds(step * block, block)
        query_low = query[0, 0, :, here]
        grad_low = grad_out[0, 0, :, here]
        query_rows = query_low.astype(F32).T.astype(BF16)
        grad_rows = grad_low.astype(F32).T.astype(BF16)
        row_dot = jnp.sum(grad_low.astype(F32) * out[0, 0, :, here].astype(F32), axis=0, keepdims=True)
        grad_query = jnp.zeros((size, block), F32)
        for part in range(length // inner):
            there = pl.ds(part * inner, inner)
            scores = jnp.dot(keys[there, :], query_low, preferred_element_type=F32)
            scores = jnp.where(code_col[0, there, :] == code_row[0, :, here], scores * (scale * LOG2E), -1e30)
            probs = jnp.exp2(scores - lse[0, 0, :, here])
            grad_probs = jnp.dot(values[there, :], grad_low, preferred_element_type=F32)
            grad_raw = (probs * (grad_probs - row_dot) * scale).astype(BF16)
            value_part = jnp.dot(probs.astype(BF16), grad_rows, preferred_element_type=F32)
            key_part = jnp.dot(grad_raw, query_rows, preferred_element_type=F32)
            if step == 0:
                value_sum[there, :] = value_part
                key_sum[there, :] = key_part
            else:
                value_sum[there, :] += value_part
                key_sum[there, :] += key_part
            grad_query += jnp.dot(key[0, 0, :, there], grad_raw, preferred_element_type=F32)
        grad_ref[row, 0, head, :, here] = grad_query.astype(BF16)
    grad_ref[row, 1, head] = key_sum[...].T.astype(BF16)
    grad_ref[row, 2, head] = value_sum[...].T.astype(BF16)

    if exchange:
        to_self(row, head).start()
        for m in range(1, 4):
            to_peer(row, head, m).start()

        @pl.when((row == rows - 1) & (head == heads - 1))
        def _():
            for r in range(rows):
                for h in range(heads):
                    to_self(r, h).wait()
                    for m in range(1, 4):
                        to_peer(r, h, m).wait()


def attend_back(packed, out, grad_out, lse, col, row, block, inner, exchange):
    rows, _, heads, size, length = packed.shape
    part = lambda j: pl.BlockSpec((1, None, 1, size, length), lambda r, h: (r, j, h, 0, 0))
    whole = pl.BlockSpec((1, 1, size, length), lambda r, h: (r, h, 0, 0))
    out_specs = [pl.BlockSpec((1, 3, 1, size, length), lambda r, h: (r, 0, h, 0, 0))]
    out_shape = [jax.ShapeDtypeStruct((rows, 3, heads, size, length), BF16)]
    scratch = []
    extra = {}
    if exchange:
        out_specs = [
            pl.BlockSpec((rows, 3, heads, size, length), lambda r, h: (0, 0, 0, 0, 0)),
            pl.BlockSpec(memory_space=pl.ANY),
        ]
        out_shape.append(jax.ShapeDtypeStruct((rows, 3, 4, heads, size, length // 4), BF16))
        count = rows * heads
        scratch = [pltpu.SemaphoreType.DMA((3 * count,)), pltpu.SemaphoreType.DMA((3 * count,)), pltpu.SemaphoreType.DMA((count,))]
        extra = dict(collective_id=3, has_side_effects=True)
    return pl.pallas_call(
        partial(attend_back_kernel, block, inner, size**-0.5, exchange),
        grid=(rows, heads),
        in_specs=[
            pl.BlockSpec((1, length, 1), lambda r, h: (r, 0, 0)),
            pl.BlockSpec((1, 1, length), lambda r, h: (r, 0, 0)),
            part(0),
            part(1),
            part(2),
            whole,
            whole,
            pl.BlockSpec((1, 1, 1, length), lambda r, h: (r, h, 0, 0)),
        ],
        out_specs=out_specs,
        out_shape=out_shape,
        scratch_shapes=[
            pltpu.VMEM((length, size), F32),
            pltpu.VMEM((length, size), F32),
            pltpu.VMEM((length, size), BF16),
            pltpu.VMEM((length, size), BF16),
        ]
        + scratch,
        compiler_params=pltpu.CompilerParams(vmem_limit_bytes=VMEM_LIMIT, **extra),
        cost_estimate=pl.CostEstimate(
            flops=20 * rows * heads * length * length * 128,
            bytes_accessed=16 * rows * heads * length * size,
            transcendentals=rows * heads * length * length,
        ),
    )(col, row, packed, packed, packed, out, grad_out, lse)


def mlp_kernel(
    normed, grad_out, normed_turned, grad_turned, up, down, bias, out_sum, grad_sum, up_keep, up_send, down_keep, down_send, bias_sum
):
    step = pl.program_id(0)
    half = up_keep.shape[0]
    c0 = math.sqrt(2 / math.pi)
    c1 = c0 * 0.044715
    hidden = jnp.dot(normed[...], up[...], preferred_element_type=F32) + bias[...]
    square = hidden * hidden
    gate = 0.5 + 0.5 * jnp.tanh(hidden * (c0 + c1 * square))
    raised = hidden * gate
    slope = gate + raised * (1.0 - gate) * (2 * c0 + 6 * c1 * square)
    active = raised.astype(BF16)
    back = (((1,), (1,)), ((), ()))
    grad_active = lax.dot_general(grad_out[...], down[...], back, preferred_element_type=F32)
    grad_wide = (grad_active * slope).astype(BF16)
    out_part = jnp.dot(active, down[...], preferred_element_type=F32)
    grad_part = lax.dot_general(grad_wide, up[...], back, preferred_element_type=F32)

    @pl.when(step == 0)
    def _():
        out_sum[...] = out_part
        grad_sum[...] = grad_part

    @pl.when(step > 0)
    def _():
        out_sum[...] += out_part
        grad_sum[...] += grad_part

    bias_sum[...] = jnp.sum(grad_wide.astype(F32), axis=0, keepdims=True)
    up_keep[...] = jnp.dot(normed_turned[:half], grad_wide, preferred_element_type=F32)
    up_send[...] = jnp.dot(normed_turned[half:], grad_wide, preferred_element_type=F32).astype(BF16)
    down_keep[...] = jnp.dot(grad_turned[:half], active, preferred_element_type=F32)
    down_send[...] = jnp.dot(grad_turned[half:], active, preferred_element_type=F32).astype(BF16)


def feed_forward(normed, grad_out, normed_turned, grad_turned, up, down, bias, tile):
    count, width = normed.shape
    hidden = up.shape[1]
    half = width // 2
    fixed = lambda *shape: pl.BlockSpec(shape, lambda t: (0, 0))
    across = lambda rows: pl.BlockSpec((rows, tile), lambda t: (0, t))
    shape = jax.ShapeDtypeStruct
    return pl.pallas_call(
        mlp_kernel,
        grid=(hidden // tile,),
        in_specs=[
            fixed(count, width),
            fixed(count, width),
            fixed(width, count),
            fixed(width, count),
            across(width),
            pl.BlockSpec((tile, width), lambda t: (t, 0)),
            across(1),
        ],
        out_specs=[fixed(count, width), fixed(count, width), across(half), across(half), across(half), across(half), across(1)],
        out_shape=[
            shape((count, width), F32),
            shape((count, width), F32),
            shape((half, hidden), F32),
            shape((half, hidden), BF16),
            shape((half, hidden), F32),
            shape((half, hidden), BF16),
            shape((1, hidden), F32),
        ],
        compiler_params=pltpu.CompilerParams(vmem_limit_bytes=VMEM_LIMIT),
        cost_estimate=pl.CostEstimate(
            flops=12 * count * width * hidden,
            bytes_accessed=10 * width * hidden,
            transcendentals=count * hidden,
        ),
    )(normed, grad_out, normed_turned, grad_turned, up, down, bias)


def turn_halves(values, groups, mine):
    count, width = values.shape
    view = values.T.reshape(groups, 2, width // (2 * groups), count)
    keep = lax.dynamic_index_in_dim(view, mine, 1, keepdims=False).reshape(width // 2, count)
    send = lax.dynamic_index_in_dim(view, 1 - mine, 1, keepdims=False).reshape(width // 2, count)
    return jnp.concatenate([keep, send], axis=0)


STAGES = 4


def mlp_reduce_kernel(
    tiles,
    normed,
    grad_out,
    normed_turned,
    grad_turned,
    up0,
    up1,
    up2,
    up3,
    down0,
    down1,
    down2,
    down3,
    bias,
    out_sum,
    grad_sum,
    bias_sum,
    up_total,
    down_total,
    up_mine,
    down_mine,
    up_core,
    down_core,
    up_core_got,
    down_core_got,
    up_half,
    down_half,
    up_out,
    down_out,
    up_got,
    down_got,
    up_quarter,
    down_quarter,
    up_last,
    down_last,
    up_last_got,
    down_last_got,
    chip_full,
    chip_out,
    chip_got,
    core_sent,
    core_came,
    seq_sent,
    seq_came,
    last_sent,
    last_came,
    chip_sent,
    chip_came,
):
    step = pl.program_id(0)
    seq, row = lax.axis_index("seq"), lax.axis_index("rows")
    half = normed_turned.shape[0] // 2
    x, y = lax.rem(seq, 2), lax.div(seq, 2)
    core_peer = {"rows": row + 1 - 2 * lax.rem(row, 2)}
    x_peer = {"seq": seq + 1 - 2 * x}
    y_peer = {"seq": seq + 2 - 4 * y}
    chip, core = lax.div(row, 2), lax.rem(row, 2)
    to_chip = [lax.rem(chip + k, 4) for k in range(4)]
    chip_peers = [{"rows": 2 * to_chip[k] + core} for k in range(4)]

    @pl.when(step == 0)
    def _():
        barrier = pltpu.get_barrier_semaphore()
        for peer in (core_peer, x_peer, y_peer, *chip_peers[1:]):
            pl.semaphore_signal(barrier, inc=1, device_id=peer, device_id_type=pl.DeviceIdType.MESH)
        pl.semaphore_wait(barrier, 6)

    def copies(source, target, sent, came, slot, kind, device):
        return pltpu.make_async_remote_copy(
            src_ref=source.at[slot],
            dst_ref=target.at[slot],
            send_sem=sent.at[kind, slot],
            recv_sem=came.at[kind, slot],
            device_id=device,
            device_id_type=pl.DeviceIdType.MESH,
        )

    def to_core(slot):
        return (
            copies(up_core, up_core_got, core_sent, core_came, slot, 0, core_peer),
            copies(down_core, down_core_got, core_sent, core_came, slot, 1, core_peer),
        )

    def to_seq(slot):
        return (
            copies(up_out, up_got, seq_sent, seq_came, slot, 0, x_peer),
            copies(down_out, down_got, seq_sent, seq_came, slot, 1, y_peer),
        )

    def to_last(slot):
        return (
            copies(up_last, up_last_got, last_sent, last_came, slot, 0, y_peer),
            copies(down_last, down_last_got, last_sent, last_came, slot, 1, x_peer),
        )

    def to_chips(slot):
        return [
            pltpu.make_async_remote_copy(
                src_ref=chip_out.at[slot, to_chip[k]],
                dst_ref=chip_got.at[slot, k - 1],
                send_sem=chip_sent.at[k - 1, slot],
                recv_sem=chip_came.at[k - 1, slot],
                device_id=chip_peers[k],
                device_id_type=pl.DeviceIdType.MESH,
            )
            for k in range(1, 4)
        ]

    @pl.when(step >= 4)
    def _():
        slot = lax.rem(step, 2)
        for copy in to_chips(slot):
            copy.wait()
        for kind, total in enumerate((up_total, down_total)):
            value = chip_full[slot, chip, kind]
            for k in range(3):
                value = value + chip_got[slot, k, kind].astype(F32)
            total[...] = value

    @pl.when((step >= 3) & (step < tiles + 3))
    def _():
        slot = lax.rem(step + 1, 2)
        for copy in to_last(slot):
            copy.wait()
        size = half // 4
        ups = up_quarter[slot] + up_last_got[slot].astype(F32)
        downs = down_quarter[slot] + down_last_got[slot].astype(F32)
        for place in range(4):
            up_block = ups[place * size : (place + 1) * size]
            down_block = downs[:, place * 128 : (place + 1) * 128]
            chip_full[slot, place, 0] = up_block
            chip_full[slot, place, 1] = down_block
            chip_out[slot, place, 0] = up_block.astype(BF16)
            chip_out[slot, place, 1] = down_block.astype(BF16)
        for copy in to_chips(slot):
            copy.start()

    @pl.when((step >= 2) & (step < tiles + 2))
    def _():
        slot = lax.rem(step, 2)
        for copy in to_seq(slot):
            copy.wait()
        up_quarter[slot] = up_half[slot, y] + up_got[slot, y].astype(F32)
        up_last[slot] = (up_half[slot, 1 - y] + up_got[slot, 1 - y].astype(F32)).astype(BF16)
        down_quarter[slot] = down_half[slot, x] + down_got[slot, x].astype(F32)
        down_last[slot] = (down_half[slot, 1 - x] + down_got[slot, 1 - x].astype(F32)).astype(BF16)
        for copy in to_last(slot):
            copy.start()

    @pl.when((step >= 1) & (step <= tiles))
    def _():
        slot = lax.rem(step + 1, 2)
        for copy in to_core(slot):
            copy.wait()
        for other in range(2):
            kept, gone = 2 * other + x, 2 * other + 1 - x
            up_half[slot, other] = up_mine[slot, kept] + up_core_got[slot, kept].astype(F32)
            up_out[slot, other] = (up_mine[slot, gone] + up_core_got[slot, gone].astype(F32)).astype(BF16)
            kept, gone = 2 * y + other, 2 * (1 - y) + other
            down_half[slot, other] = down_mine[slot, kept] + down_core_got[slot, kept].astype(F32)
            down_out[slot, other] = (down_mine[slot, gone] + down_core_got[slot, gone].astype(F32)).astype(BF16)
        for copy in to_seq(slot):
            copy.start()

    @pl.when(step < tiles)
    def _():
        slot = lax.rem(step, 2)
        up = jnp.concatenate([up0[...], up1[...], up2[...], up3[...]], axis=1)
        down = jnp.concatenate([down0[...], down1[...], down2[...], down3[...]], axis=0)
        biases = jnp.concatenate([bias[owner] for owner in range(4)], axis=1)
        c0 = math.sqrt(2 / math.pi)
        c1 = c0 * 0.044715
        hidden = jnp.dot(normed[...], up, preferred_element_type=F32) + biases
        square = hidden * hidden
        gate = 0.5 + 0.5 * jnp.tanh(hidden * (c0 + c1 * square))
        raised = hidden * gate
        slope = gate + raised * (1.0 - gate) * (2 * c0 + 6 * c1 * square)
        active = raised.astype(BF16)
        down_part = jnp.dot(grad_turned[...], active, preferred_element_type=F32)
        for owner in range(4):
            size = half // 4
            down_mine[slot, owner] = down_part[owner * size : (owner + 1) * size]
            down_core[slot, owner] = down_part[half + owner * size : half + (owner + 1) * size].astype(BF16)
        to_core(slot)[1].start()
        back = (((1,), (1,)), ((), ()))
        grad_active = lax.dot_general(grad_out[...], down, back, preferred_element_type=F32)
        grad_wide = (grad_active * slope).astype(BF16)
        up_part = jnp.dot(normed_turned[...], grad_wide, preferred_element_type=F32)
        for owner in range(4):
            columns = slice(owner * 128, (owner + 1) * 128)
            up_mine[slot, owner] = up_part[:half, columns]
            up_core[slot, owner] = up_part[half:, columns].astype(BF16)
        to_core(slot)[0].start()
        sums = jnp.sum(grad_wide.astype(F32), axis=0, keepdims=True)
        for owner in range(4):
            bias_sum[owner] = sums[:, owner * 128 : (owner + 1) * 128]
        out_part = jnp.dot(active, down, preferred_element_type=F32)
        grad_part = lax.dot_general(grad_wide, up, back, preferred_element_type=F32)

        @pl.when(step == 0)
        def _():
            out_sum[...] = out_part
            grad_sum[...] = grad_part

        @pl.when(step > 0)
        def _():
            out_sum[...] += out_part
            grad_sum[...] += grad_part


def feed_forward_reduce(normed, grad_out, normed_turned, grad_turned, up, down, bias):
    count, width = normed.shape
    hidden = up.shape[1]
    part = hidden // 4
    tiles = part // 128
    half, quarter = width // 2, width // 8
    last = tiles - 1
    shape = jax.ShapeDtypeStruct
    fixed = lambda *dims: pl.BlockSpec(dims, lambda t: (0, 0), pipeline_mode=pl.Buffered(buffer_count=1))
    result = lambda *dims: pl.BlockSpec(dims, lambda t: (0, 0))
    done = lambda t: jnp.maximum(t - STAGES, 0)

    def up_block(owner):
        return pl.BlockSpec((width, 128), lambda t: (0, owner * tiles + jnp.minimum(t, last)))

    def down_block(owner):
        return pl.BlockSpec((128, width), lambda t: (owner * tiles + jnp.minimum(t, last), 0))

    bias_block = pl.BlockSpec((4, 1, 128), lambda t: (0, 0, jnp.minimum(t, last)))
    pair = lambda dtype, *dims: pltpu.VMEM((2,) + dims, dtype)
    return pl.pallas_call(
        partial(mlp_reduce_kernel, tiles),
        grid=(tiles + STAGES,),
        in_specs=[fixed(count, width), fixed(count, width), fixed(width, count), fixed(width, count)]
        + [up_block(owner) for owner in range(4)]
        + [down_block(owner) for owner in range(4)]
        + [bias_block],
        out_specs=[
            result(count, width),
            result(count, width),
            bias_block,
            pl.BlockSpec((quarter, 128), lambda t: (0, done(t))),
            pl.BlockSpec((quarter, 128), lambda t: (0, done(t))),
        ],
        out_shape=[
            shape((count, width), F32),
            shape((count, width), F32),
            shape((4, 1, part), F32),
            shape((quarter, part), F32),
            shape((quarter, part), F32),
        ],
        scratch_shapes=[
            pair(F32, 4, half, 128),
            pair(F32, 4, quarter, 512),
            pair(BF16, 4, half, 128),
            pair(BF16, 4, quarter, 512),
            pair(BF16, 4, half, 128),
            pair(BF16, 4, quarter, 512),
            pair(F32, 2, half, 128),
            pair(F32, 2, quarter, 512),
            pair(BF16, 2, half, 128),
            pair(BF16, 2, quarter, 512),
            pair(BF16, 2, half, 128),
            pair(BF16, 2, quarter, 512),
            pair(F32, half, 128),
            pair(F32, quarter, 512),
            pair(BF16, half, 128),
            pair(BF16, quarter, 512),
            pair(BF16, half, 128),
            pair(BF16, quarter, 512),
            pair(F32, 4, 2, quarter, 128),
            pair(BF16, 4, 2, quarter, 128),
            pair(BF16, 3, 2, quarter, 128),
        ]
        + [pltpu.SemaphoreType.DMA((2, 2))] * 6
        + [pltpu.SemaphoreType.DMA((3, 2))] * 2,
        compiler_params=pltpu.CompilerParams(collective_id=1, has_side_effects=True, vmem_limit_bytes=VMEM_LIMIT),
        cost_estimate=pl.CostEstimate(
            flops=12 * count * width * hidden,
            bytes_accessed=6 * width * hidden,
            transcendentals=count * hidden,
        ),
    )(normed, grad_out, normed_turned, grad_turned, up, up, up, up, down, down, down, down, bias.reshape(4, 1, part))


def split_low(values):
    high = values.astype(BF16)
    rest = values - high.astype(F32)
    middle = rest.astype(BF16)
    return high, middle, (rest - middle.astype(F32)).astype(BF16)


def per_token(slot_col, seg_row, table):
    picked = (slot_col == seg_row).astype(BF16)
    return lax.dot_general(
        picked, jnp.concatenate(split_low(table), axis=0), (((0,), (0,)), ((), ())), preferred_element_type=F32
    )


def per_slot(slot_col, seg_row, values):
    slots = slot_col.shape[0] // 3
    picked = (slot_col[:slots] == seg_row).astype(BF16)
    return sum(jnp.dot(picked, part, preferred_element_type=F32) for part in split_low(values))


def normalize(values):
    center = values - jnp.mean(values, axis=-1, keepdims=True)
    inverse = lax.rsqrt(jnp.mean(center * center, axis=-1, keepdims=True) + norm_eps)
    return center * inverse, inverse


def normalize_back(normal, inverse, grad):
    return inverse * (grad - jnp.mean(grad, axis=-1, keepdims=True) - normal * jnp.mean(grad * normal, axis=-1, keepdims=True))


def after_kernel(
    slot_col,
    seg,
    table,
    attended,
    weight,
    bias,
    out_sum,
    grad_sum,
    middle_ref,
    branch_ref,
    cotangent,
    block_out,
    grad_middle_ref,
    slot_sums,
    bias_sum,
    view_ref,
    proj_ref,
    heads_out,
    total,
    core_out,
    core_got,
    sent,
    came,
    kept,
    core_sent,
    core_came,
):
    step = pl.program_id(0)
    rows = pl.num_programs(0)
    width = cotangent.shape[-1]
    length = cotangent.shape[-2]
    depth, own = width // 8, width // 4
    seq, row = lax.axis_index("seq"), lax.axis_index("rows")
    core = lax.rem(row, 2)
    core_peer = {"rows": row + 1 - 2 * core}
    peers = peers_of(seq)

    @pl.when(step == 0)
    def _():
        greet([{"seq": peer} for peer in peers] + [core_peer])

    def to_peer(r, m):
        lanes = pl.ds(m * length, length)
        return send_block(
            heads_out.at[r, peers[m - 1]], view_ref.at[r, :, lanes], sent, came, r * 3 + m - 1, {"seq": peers[m - 1]}
        )

    def to_self(r):
        return pltpu.make_async_copy(heads_out.at[r, seq], view_ref.at[r, :, pl.ds(0, length)], kept.at[r])

    mods = per_token(slot_col[...], seg[0], table[0, :, 2 * width :])
    gate_a, scale_b, gate_b = (mods[:, k * width : (k + 1) * width] for k in (0, 2, 3))
    middle, branch = middle_ref[0], branch_ref[0]
    upstream = cotangent[0].astype(F32)
    normal, inverse = normalize(middle)
    grad_normed = grad_sum[...]
    grad_middle = upstream + normalize_back(normal, inverse, grad_normed * (1.0 + scale_b))
    grad_middle_ref[0] = grad_middle
    grad_branch = (grad_middle * gate_a).astype(BF16)
    grad_heads = lax.dot_general(weight[...], grad_branch, (((1,), (1,)), ((), ())), preferred_element_type=F32)
    for owner in range(4):
        heads_out[step, owner] = grad_heads[owner * own : (owner + 1) * own].astype(BF16)
    to_self(step).start()
    for m in range(1, 4):
        to_peer(step, m).start()

    part = jnp.dot(attended[0], grad_branch, preferred_element_type=F32)
    sums = jnp.sum(grad_branch.astype(F32), axis=0, keepdims=True)

    @pl.when(step == 0)
    def _():
        total[...] = part
        bias_sum[...] = sums

    @pl.when(step > 0)
    def _():
        total[...] += part
        bias_sum[...] += sums

    to_core = pltpu.make_async_remote_copy(
        src_ref=core_out,
        dst_ref=core_got,
        send_sem=core_sent,
        recv_sem=core_came,
        device_id=core_peer,
        device_id_type=pl.DeviceIdType.MESH,
    )

    @pl.when(step == rows - 1)
    def _():
        for chip in range(4):
            other = pl.multiple_of((2 * chip + 1 - core) * depth, 8)
            core_out[chip] = total[pl.ds(other, depth), :].astype(BF16)
        to_core.start()

    branch_b = out_sum[...] + bias[...]
    block_out[0] = (middle + gate_b * branch_b).astype(BF16)
    pieces = (grad_middle * branch, grad_normed, grad_normed * normal, upstream * branch_b)
    for k, piece in enumerate(pieces):
        slot_sums[0, :, k * width : (k + 1) * width] = per_slot(slot_col[...], seg[0], piece)

    @pl.when(step == rows - 1)
    def _():
        to_core.wait()
        for chip in range(4):
            mine = pl.multiple_of((2 * chip + core) * depth, 8)
            proj_ref[chip] = total[pl.ds(mine, depth), :] + core_got[chip].astype(F32)
        for r in range(heads_out.shape[0]):
            to_self(r).wait()
            for m in range(1, 4):
                to_peer(r, m).wait()


def after_feed_forward(slot_col, seg, table, attended, weight, bias, out_sum, grad_sum, middle, branch, cotangent):
    rows, length, width = cotangent.shape
    slots = table.shape[1]
    depth = width // 8
    fixed = lambda *dims: pl.BlockSpec(dims, lambda r: (0,) * len(dims))
    row = lambda *dims: pl.BlockSpec((1,) + dims, lambda r: (r, 0, 0))
    shape = jax.ShapeDtypeStruct
    return pl.pallas_call(
        after_kernel,
        grid=(rows,),
        in_specs=[
            fixed(*slot_col.shape),
            row(1, length),
            row(*table.shape[1:]),
            row(width, length),
            fixed(width, width),
            fixed(1, width),
            pl.BlockSpec((length, width), lambda r: (r, 0)),
            pl.BlockSpec((length, width), lambda r: (r, 0)),
            row(length, width),
            row(length, width),
            row(length, width),
        ],
        out_specs=[
            row(length, width),
            row(length, width),
            row(slots, 4 * width),
            fixed(1, width),
            pl.BlockSpec(memory_space=pl.ANY),
            fixed(4, depth, width),
        ],
        out_shape=[
            shape((rows, length, width), BF16),
            shape((rows, length, width), F32),
            shape((rows, slots, 4 * width), F32),
            shape((1, width), F32),
            shape((rows, width // 4, 4 * length), BF16),
            shape((4, depth, width), F32),
        ],
        scratch_shapes=[
            pltpu.VMEM((rows, 4, width // 4, length), BF16),
            pltpu.VMEM((width, width), F32),
            pltpu.VMEM((4, depth, width), BF16),
            pltpu.VMEM((4, depth, width), BF16),
            pltpu.SemaphoreType.DMA((3 * rows,)),
            pltpu.SemaphoreType.DMA((3 * rows,)),
            pltpu.SemaphoreType.DMA((rows,)),
            pltpu.SemaphoreType.DMA,
            pltpu.SemaphoreType.DMA,
        ],
        compiler_params=pltpu.CompilerParams(vmem_limit_bytes=VMEM_LIMIT, collective_id=4, has_side_effects=True),
        cost_estimate=pl.CostEstimate(flops=8 * 10**9, bytes_accessed=3 * 10**7, transcendentals=0),
    )(slot_col, seg, table, attended, weight, bias, out_sum, grad_sum, middle, branch, cotangent)


def qkv_weight_kernel(grad, normed, keep_ref, send_ref, sum_ref, total, turned):
    step = pl.program_id(0)
    chips, depth = lax.axis_size("rows") // 2, total.shape[1] // lax.axis_size("rows")
    mine = lax.rem(lax.axis_index("rows"), 2)
    part = jnp.dot(grad[0], normed[0], preferred_element_type=F32)
    sums = jnp.sum(grad[0].astype(F32), axis=1, keepdims=True)

    @pl.when(step == 0)
    def _():
        total[...] = part
        sum_ref[...] = sums

    @pl.when(step > 0)
    def _():
        total[...] += part
        sum_ref[...] += sums

    @pl.when(step == pl.num_programs(0) - 1)
    def _():
        turned[...] = total[...].T
        for chip in range(chips):
            first = pl.multiple_of((2 * chip + mine) * depth, 8)
            other = pl.multiple_of((2 * chip + 1 - mine) * depth, 8)
            keep_ref[chip] = turned[pl.ds(first, depth), :]
            send_ref[chip] = turned[pl.ds(other, depth), :].astype(BF16)


def qkv_weight_grad(grad, normed):
    rows, features, length = grad.shape
    width = normed.shape[2]
    groups = lax.axis_size("rows")
    shape = (groups // 2, width // groups, features)
    return pl.pallas_call(
        qkv_weight_kernel,
        grid=(rows,),
        in_specs=[
            pl.BlockSpec((1, features, length), lambda r: (r, 0, 0)),
            pl.BlockSpec((1, length, width), lambda r: (r, 0, 0)),
        ],
        out_specs=[
            pl.BlockSpec(shape, lambda r: (0, 0, 0)),
            pl.BlockSpec(shape, lambda r: (0, 0, 0)),
            pl.BlockSpec((features, 1), lambda r: (0, 0)),
        ],
        out_shape=[
            jax.ShapeDtypeStruct(shape, F32),
            jax.ShapeDtypeStruct(shape, BF16),
            jax.ShapeDtypeStruct((features, 1), F32),
        ],
        scratch_shapes=[pltpu.VMEM((features, width), F32), pltpu.VMEM((width, features), F32)],
        compiler_params=pltpu.CompilerParams(vmem_limit_bytes=VMEM_LIMIT),
        cost_estimate=pl.CostEstimate(
            flops=2 * rows * length * width * features,
            bytes_accessed=2 * rows * length * (width + features) + 6 * width * features // 2,
            transcendentals=0,
        ),
    )(grad, normed)


def tail_kernel(
    images,
    mod,
    weight,
    cond,
    ada_ref,
    cond_ref,
    bias_ref,
    got,
    low_mine,
    low_got,
    row_mine,
    row_got,
    cond_mine,
    cond_got,
    column_got,
    sent,
    arrived,
):
    seq_count, row_total = lax.axis_size("seq"), lax.axis_size("rows")
    seq, row = lax.axis_index("seq"), lax.axis_index("rows")
    to_seq = [lax.rem(seq + m, seq_count) for m in range(seq_count)]
    to_row = [lax.rem(row + m, row_total) for m in range(row_total)]
    barrier = pltpu.get_barrier_semaphore()
    for m in range(1, seq_count):
        pl.semaphore_signal(barrier, inc=1, device_id={"seq": to_seq[m]}, device_id_type=pl.DeviceIdType.MESH)
    for m in range(1, row_total):
        pl.semaphore_signal(barrier, inc=1, device_id={"rows": to_row[m]}, device_id_type=pl.DeviceIdType.MESH)
    pl.semaphore_wait(barrier, seq_count + row_total - 2)

    used = [0]

    def start(source, target, device):
        copy = pltpu.make_async_remote_copy(
            src_ref=source,
            dst_ref=target,
            send_sem=sent.at[used[0]],
            recv_sem=arrived.at[used[0]],
            device_id=device,
            device_id_type=pl.DeviceIdType.MESH,
        )
        used[0] += 1
        copy.start()
        return copy

    copies = [start(mod.at[to_seq[m]], got.at[m], {"seq": to_seq[m]}) for m in range(1, seq_count)]
    column_got[0] = cond[row]
    column_copies = [start(cond.at[to_row[m]], column_got.at[m], {"rows": to_row[m]}) for m in range(1, row_total)]
    total = mod[seq]
    for m, copy in enumerate(copies):
        copy.wait()
        total = total + got[m + 1]
    low = total[:images].astype(BF16)
    low_mine[...] = low
    row_mine[...] = total[images:]
    row_mine[0:1] = jnp.sum(total[:images], axis=0, keepdims=True)
    low_got[0] = low
    copies = [start(low_mine, low_got.at[m], {"rows": to_row[m]}) for m in range(1, row_total)]
    copies += [start(row_mine, row_got.at[m], {"rows": to_row[m]}) for m in range(1, row_total)]
    term = lax.dot_general(low, weight[...], (((1,), (1,)), ((), ())), preferred_element_type=F32)
    cond_mine[...] = term
    cond_copies = [start(cond_mine, cond_got.at[m], {"seq": to_seq[m]}) for m in range(1, seq_count)]
    for copy in copies:
        copy.wait()
    sums = row_mine[...]
    for m in range(1, row_total):
        sums = sums + row_got[m]
    bias_ref[seq] = sums
    copies = [start(bias_ref.at[seq], bias_ref.at[seq], {"seq": to_seq[m]}) for m in range(1, seq_count)]
    for copy in column_copies:
        copy.wait()
    gathered = jnp.concatenate([low_got[m] for m in range(row_total)], axis=0)
    columns = jnp.concatenate([column_got[m] for m in range(row_total)], axis=0)
    ada_ref[...] = lax.dot_general(columns, gathered, (((0,), (0,)), ((), ())), preferred_element_type=F32)
    for m, copy in enumerate(cond_copies):
        copy.wait()
        term = term + cond_got[m + 1]
    cond_ref[...] = term
    for copy in copies:
        copy.wait()


def finish(mod, weight, cond, images):
    seq_count, lines, columns = mod.shape
    width, depth = weight.shape[0], cond.shape[2]
    row_total = lax.axis_size("rows")
    extra = lines - images
    copies = 3 * (seq_count - 1) + 3 * (row_total - 1)
    return pl.pallas_call(
        partial(tail_kernel, images),
        in_specs=[pl.BlockSpec(memory_space=pltpu.VMEM)] * 3,
        out_specs=[pl.BlockSpec(memory_space=pltpu.VMEM)] * 3,
        out_shape=[
            jax.ShapeDtypeStruct((depth, columns), F32),
            jax.ShapeDtypeStruct((images, width), F32),
            jax.ShapeDtypeStruct((seq_count, extra, columns), F32),
        ],
        scratch_shapes=[
            pltpu.VMEM((seq_count, lines, columns), F32),
            pltpu.VMEM((images, columns), BF16),
            pltpu.VMEM((row_total, images, columns), BF16),
            pltpu.VMEM((extra, columns), F32),
            pltpu.VMEM((row_total, extra, columns), F32),
            pltpu.VMEM((images, width), F32),
            pltpu.VMEM((seq_count, images, width), F32),
            pltpu.VMEM((row_total, images, depth), BF16),
            pltpu.SemaphoreType.DMA((copies,)),
            pltpu.SemaphoreType.DMA((copies,)),
        ],
        compiler_params=pltpu.CompilerParams(collective_id=0, has_side_effects=True, vmem_limit_bytes=VMEM_LIMIT),
        cost_estimate=pl.CostEstimate(flops=10**9, bytes_accessed=10**7, transcendentals=0),
    )(mod, weight, cond)


def send_to(source, target, sent, came, device):
    return pltpu.make_async_remote_copy(
        src_ref=source,
        dst_ref=target,
        send_sem=sent,
        recv_sem=came,
        device_id=device,
        device_id_type=pl.DeviceIdType.MESH,
    )


def attend_back_reduce_kernel(
    block,
    inner,
    scale,
    code_col,
    code_row,
    query,
    key,
    value,
    out,
    grad_out,
    lse,
    normed,
    proj,
    down,
    token_ref,
    qkv_ref,
    proj_ref,
    down_ref,
    grads,
    key_sum,
    value_sum,
    keys,
    values,
    flat,
    total,
    turned,
    core_out,
    core_got,
    proj_out,
    proj_got,
    seq_out,
    seq_got,
    down_out,
    down_got,
    sent,
    came,
    kept,
    proj_sent,
    proj_came,
    seq_sent,
    seq_came,
    core_sent,
    core_came,
):
    length, size = query.shape[-1], query.shape[-2]
    row, head = pl.program_id(0), pl.program_id(1)
    rows, _, heads = grads.shape[:3]
    width = normed.shape[-1]
    depth, own, local = width // 8, width // 4, length // 4
    seq, group = lax.axis_index("seq"), lax.axis_index("rows")
    chip, core = lax.div(group, 2), lax.rem(group, 2)
    peers = [{"seq": peer} for peer in peers_of(seq)]
    core_peer = {"rows": group + 1 - 2 * core}
    to_chip = [lax.rem(chip + k, 4) for k in range(4)]
    chip_peers = [{"rows": 2 * to_chip[k] + core} for k in range(4)]
    first = (row == 0) & (head == 0)
    last = (row == rows - 1) & (head == heads - 1)

    def to_peer(r, h, m):
        place = (r * heads + h) * 3 + m - 1
        source = grads.at[r, :, h, :, pl.ds(m * local, local)]
        return send_to(source, token_ref.at[r, :, seq, h], sent.at[place], came.at[place], peers[m - 1])

    def to_self(r, h):
        source = grads.at[r, :, h, :, pl.ds(0, local)]
        return pltpu.make_async_copy(source, token_ref.at[r, :, seq, h], kept.at[r * heads + h])

    proj_copies = [
        send_to(proj_out.at[to_chip[k]], proj_got.at[k - 1], proj_sent.at[k - 1], proj_came.at[k - 1], chip_peers[k])
        for k in range(1, 4)
    ]
    seq_copies = [
        send_to(seq_out.at[target], seq_got.at[m], seq_sent.at[m], seq_came.at[m], peers[m])
        for m, target in enumerate(peers_of(seq))
    ]
    core_copy = send_to(core_out, core_got, core_sent.at[0], core_came.at[0], core_peer)
    down_copy = send_to(down_out.at[1 - core], down_got, core_sent.at[1], core_came.at[1], core_peer)

    @pl.when(first)
    def _():
        greet(peers + [core_peer] + chip_peers[1:])
        proj_out[...] = proj[...].astype(BF16)
        for copy in proj_copies:
            copy.start()
        half = down.shape[1] // 2
        for place in range(2):
            down_out[place] = down[:, place * half : (place + 1) * half]
        down_copy.start()

    keys[...] = key[0, 0].astype(F32).T.astype(BF16)
    values[...] = value[0, 0].astype(F32).T.astype(BF16)

    def place_of(part):
        return pl.ds(pl.multiple_of((part * heads + head) * size, 8), size)

    for step in range(length // block):
        here = pl.ds(step * block, block)
        query_low = query[0, 0, :, here]
        grad_low = grad_out[0, 0, :, here]
        query_rows = query_low.astype(F32).T.astype(BF16)
        grad_rows = grad_low.astype(F32).T.astype(BF16)
        row_dot = jnp.sum(grad_low.astype(F32) * out[0, 0, :, here].astype(F32), axis=0, keepdims=True)
        grad_query = jnp.zeros((size, block), F32)
        for part in range(length // inner):
            there = pl.ds(part * inner, inner)
            scores = jnp.dot(keys[there, :], query_low, preferred_element_type=F32)
            scores = jnp.where(code_col[0, there, :] == code_row[0, :, here], scores * (scale * LOG2E), -1e30)
            probs = jnp.exp2(scores - lse[0, 0, :, here])
            grad_probs = jnp.dot(values[there, :], grad_low, preferred_element_type=F32)
            grad_raw = (probs * (grad_probs - row_dot) * scale).astype(BF16)
            value_part = jnp.dot(probs.astype(BF16), grad_rows, preferred_element_type=F32)
            key_part = jnp.dot(grad_raw, query_rows, preferred_element_type=F32)
            if step == 0:
                value_sum[there, :] = value_part
                key_sum[there, :] = key_part
            else:
                value_sum[there, :] += value_part
                key_sum[there, :] += key_part
            grad_query += jnp.dot(key[0, 0, :, there], grad_raw, preferred_element_type=F32)
        low = grad_query.astype(BF16)
        grads[row, 0, head, :, here] = low
        flat[place_of(0), here] = low.astype(F32)
    for part, sums in ((1, key_sum), (2, value_sum)):
        low = sums[...].T.astype(BF16)
        grads[row, part, head] = low
        flat[place_of(part), :] = low.astype(F32)

    to_self(row, head).start()
    for m in range(1, 4):
        to_peer(row, head, m).start()

    @pl.when((head == heads - 1) & (row == 0))
    def _():
        total[...] = jnp.dot(flat[...].astype(BF16), normed[0], preferred_element_type=F32)

    @pl.when((head == heads - 1) & (row > 0))
    def _():
        total[...] += jnp.dot(flat[...].astype(BF16), normed[0], preferred_element_type=F32)

    @pl.when(last)
    def _():
        turned[...] = total[...].T
        for place in range(4):
            other = pl.multiple_of((2 * place + 1 - core) * depth, 8)
            core_out[place] = turned[pl.ds(other, depth), :].astype(BF16)
        core_copy.start()
        for copy in proj_copies:
            copy.wait()
        mine = proj[chip]
        for k in range(3):
            mine = mine + proj_got[k].astype(F32)
        for place in range(4):
            seq_out[place] = mine[:, place * own : (place + 1) * own].astype(BF16)
        for copy in seq_copies:
            copy.start()
        down_copy.wait()
        left, right = down_out[core], down_got[...]
        left, right = jnp.where(core == 0, left, right), jnp.where(core == 0, right, left)
        down_ref[:depth] = left
        down_ref[depth:] = right
        core_copy.wait()
        for place in range(4):
            same = pl.multiple_of((2 * place + core) * depth, 8)
            qkv_ref[place] = turned[pl.ds(same, depth), :] + core_got[place].astype(F32)
        for place in range(4):

            @pl.when(seq == place)
            def _():
                proj_ref[...] = mine[:, place * own : (place + 1) * own]

        for m, copy in enumerate(seq_copies):
            copy.wait()
            proj_ref[...] += seq_got[m].astype(F32)
        for r in range(rows):
            for h in range(heads):
                to_self(r, h).wait()
                for m in range(1, 4):
                    to_peer(r, h, m).wait()


def attend_back_reduce(packed, out, grad_out, lse, col, row, normed, proj, down, block, inner):
    rows, _, heads, size, length = packed.shape
    width = normed.shape[2]
    depth, own, features = width // 8, width // 4, 3 * heads * size
    half = down.shape[1] // 2
    part = lambda j: pl.BlockSpec((1, None, 1, size, length), lambda r, h: (r, j, h, 0, 0))
    whole = pl.BlockSpec((1, 1, size, length), lambda r, h: (r, h, 0, 0))
    fixed = lambda *dims: pl.BlockSpec(dims, lambda r, h: (0,) * len(dims))
    shape = jax.ShapeDtypeStruct
    count = rows * heads
    dma = lambda n: pltpu.SemaphoreType.DMA((n,))
    return pl.pallas_call(
        partial(attend_back_reduce_kernel, block, inner, size**-0.5),
        grid=(rows, heads),
        in_specs=[
            pl.BlockSpec((1, length, 1), lambda r, h: (r, 0, 0)),
            pl.BlockSpec((1, 1, length), lambda r, h: (r, 0, 0)),
            part(0),
            part(1),
            part(2),
            whole,
            whole,
            pl.BlockSpec((1, 1, 1, length), lambda r, h: (r, h, 0, 0)),
            pl.BlockSpec((1, length, width), lambda r, h: (r, 0, 0)),
            fixed(4, depth, width),
            fixed(depth, 2 * half),
        ],
        out_specs=[pl.BlockSpec(memory_space=pl.ANY), fixed(4, depth, features), fixed(depth, own), fixed(own, half)],
        out_shape=[
            shape((rows, 3, 4, heads, size, length // 4), BF16),
            shape((4, depth, features), F32),
            shape((depth, own), F32),
            shape((own, half), F32),
        ],
        scratch_shapes=[
            pltpu.VMEM((rows, 3, heads, size, length), BF16),
            pltpu.VMEM((length, size), F32),
            pltpu.VMEM((length, size), F32),
            pltpu.VMEM((length, size), BF16),
            pltpu.VMEM((length, size), BF16),
            pltpu.VMEM((features, length), F32),
            pltpu.VMEM((features, width), F32),
            pltpu.VMEM((width, features), F32),
            pltpu.VMEM((4, depth, features), BF16),
            pltpu.VMEM((4, depth, features), BF16),
            pltpu.VMEM((4, depth, width), BF16),
            pltpu.VMEM((3, depth, width), BF16),
            pltpu.VMEM((4, depth, own), BF16),
            pltpu.VMEM((3, depth, own), BF16),
            pltpu.VMEM((2, depth, half), F32),
            pltpu.VMEM((depth, half), F32),
            dma(3 * count),
            dma(3 * count),
            dma(count),
            dma(3),
            dma(3),
            dma(3),
            dma(3),
            dma(2),
            dma(2),
        ],
        compiler_params=pltpu.CompilerParams(vmem_limit_bytes=VMEM_LIMIT, collective_id=3, has_side_effects=True),
        cost_estimate=pl.CostEstimate(
            flops=20 * rows * heads * length * length * 128,
            bytes_accessed=16 * rows * heads * length * size,
            transcendentals=rows * heads * length * length,
        ),
    )(col, row, packed, packed, packed, out, grad_out, lse, normed, proj, down)


def last_kernel(
    slot_col,
    seg,
    table,
    grads,
    weight,
    tokens,
    grad_middle,
    slot_sums,
    pick,
    conditioning,
    biases,
    qkv,
    cond,
    ada,
    grad_tokens,
    ada_ref,
    cond_ref,
    ada_bias_ref,
    qv_bias_ref,
    proj_bias_ref,
    up_bias_ref,
    down_bias_ref,
    qkv_ref,
    ada_here,
    image_sums,
    feature_sums,
    mod,
    got,
    lines,
    lines_got,
    low_all,
    small_core,
    small_chip,
    small_seq,
    cond_all,
    column_got,
    chip_out,
    chip_got,
    piece_out,
    piece_got,
    ada_came,
    sent,
    came,
):
    step, rows = pl.program_id(0), pl.num_programs(0)
    seq, group = lax.axis_index("seq"), lax.axis_index("rows")
    width = tokens.shape[-1]
    images = image_sums.shape[0]
    columns = mod.shape[2]
    own = width // 4
    chip, core = lax.div(group, 2), lax.rem(group, 2)
    seq_peers = peers_of(seq)
    to_seq = [{"seq": peer} for peer in seq_peers]
    rows_peers = [lax.rem(group + m, 8) for m in range(8)]
    to_row = [{"rows": peer} for peer in rows_peers]
    chips = [lax.rem(chip + k, 4) for k in range(4)]
    load_ada = pltpu.make_async_copy(ada, ada_here, ada_came)
    used = [0]

    def copy_to(source, target, device):
        used[0] += 1
        return send_to(source, target, sent.at[used[0] - 1], came.at[used[0] - 1], device)

    chip_copies = [copy_to(chip_out.at[chips[k]], chip_got.at[k - 1], {"rows": 2 * chips[k] + core}) for k in range(1, 4)]
    column_copies = [copy_to(cond.at[rows_peers[m]], column_got.at[group], to_row[m]) for m in range(1, 8)]
    mod_copies = [copy_to(mod.at[seq_peers[m]], got.at[m], to_seq[m]) for m in range(3)]
    line_copies = [copy_to(lines.at[seq_peers[m]], lines_got.at[m], to_seq[m]) for m in range(3)]
    core_peer = {"rows": group + 1 - 2 * core}
    chip_peers = [{"rows": 2 * chips[k] + core} for k in range(4)]
    low_core = copy_to(low_all.at[chip, core], low_all.at[chip, core], core_peer)
    low_chips = [copy_to(low_all.at[chip, core], low_all.at[chip, core], chip_peers[k]) for k in range(1, 4)]
    before = [lax.rem(chip + 4 - k, 4) for k in range(4)]
    low_on = [copy_to(low_all.at[before[k], core], low_all.at[before[k], core], core_peer) for k in range(1, 4)]
    small_over = copy_to(small_core.at[core], small_core.at[core], core_peer)
    small_chips = [copy_to(small_chip.at[chip], small_chip.at[chip], chip_peers[k]) for k in range(1, 4)]
    small_copies = [copy_to(small_seq.at[seq], small_seq.at[seq], to_seq[m]) for m in range(3)]
    cond_copies = [copy_to(cond_all.at[seq], cond_all.at[seq], to_seq[m]) for m in range(3)]
    base = used[0]

    @pl.when(step == 0)
    def _():
        load_ada.start()
        greet(to_seq + to_row[1:])
        chip_out[...] = qkv[...].astype(BF16)
        for copy in chip_copies + column_copies:
            copy.start()
        column_got[group] = cond[group]
        image_sums[...] = jnp.zeros_like(image_sums)
        feature_sums[...] = jnp.zeros_like(feature_sums)

    grad_low = grads[0]
    grad_normed = jnp.dot(weight[...], grad_low, preferred_element_type=F32).T
    ones = jnp.ones((8, grad_low.shape[1]), BF16)
    feature_sums[...] += lax.dot_general(ones, grad_low, (((1,), (1,)), ((), ())), preferred_element_type=F32)
    normal, inverse = normalize(tokens[0].astype(F32))
    scale_a = per_token(slot_col[...], seg[0], table[0, :, width : 2 * width])
    grad_tokens[0] = grad_middle[0] + normalize_back(normal, inverse, grad_normed * (1.0 + scale_a))
    late = [per_slot(slot_col[...], seg[0], piece) for piece in (grad_normed, grad_normed * normal)]
    slots = jnp.concatenate(late + [slot_sums[0]], axis=1)
    image_sums[...] += jnp.dot(pick[0], slots, precision=lax.Precision.HIGHEST, preferred_element_type=F32)

    @pl.when(step == rows - 1)
    def _():
        for place in range(4):
            mod[place] = image_sums[:, place * columns : (place + 1) * columns]
        lines[...] = jnp.zeros_like(lines)
        for line in range(8):
            value = biases[line : line + 1]
            if line < 2:
                value = feature_sums[0:1, 2 * line * width : (2 * line + 1) * width]
            lines[line // 2, line % 2 : line % 2 + 1, :width] = value
        for copy in mod_copies + line_copies:
            copy.start()
        total = mod[seq]
        for m, copy in enumerate(mod_copies):
            copy.wait()
            total = total + got[m]
        low = total.astype(BF16)
        low_all[chip, core] = low
        low_core.start()
        for copy in low_chips:
            copy.start()
        small = lines[seq]
        for m, copy in enumerate(line_copies):
            copy.wait()
            small = small + lines_got[m]
        small_core[core] = small
        small_core[core, 2:3] = jnp.sum(total, axis=0, keepdims=True)
        small_over.start()
        load_ada.wait()
        cond_all[seq] = jnp.dot(low, ada_here[...], preferred_element_type=F32)
        for copy in cond_copies:
            copy.start()
        for copy in chip_copies:
            copy.wait()
        for copy in column_copies:
            copy.wait()
        mine = qkv[chip]
        for k in range(3):
            mine = mine + chip_got[k].astype(F32)
        for part in range(3):
            piece_out[part] = mine[:, part * own : (part + 1) * own]

        def piece(part):
            index = part * 4 + seq
            target, place = lax.div(index, 3), lax.rem(index, 3)
            copy = send_to(piece_out.at[part], piece_got.at[place], sent.at[base + part], came.at[base + place], {"seq": target})
            return copy, target, place

        def arriving(place):
            source = lax.rem(3 * seq + place, 4)
            copy = send_to(piece_out.at[0], piece_got.at[place], sent.at[base], came.at[base + place], {"seq": source})
            return copy, source

        for part in range(3):
            copy, target, place = piece(part)

            @pl.when(target != seq)
            def _():
                copy.start()

            @pl.when(target == seq)
            def _():
                piece_got[place] = piece_out[part]

        small_over.wait()
        small_chip[chip] = small_core[0] + small_core[1]
        for copy in small_chips:
            copy.start()
        for came_in, going_on in zip(low_chips, low_on):
            came_in.wait()
            going_on.start()
        for copy in small_chips:
            copy.wait()
        small_seq[seq] = (small_chip[0] + small_chip[1]) + (small_chip[2] + small_chip[3])
        for copy in small_copies:
            copy.start()
        low_core.wait()
        for copy in low_on:
            copy.wait()
        gathered = jnp.concatenate([low_all[m // 2, m % 2] for m in range(8)], axis=0)
        blocks = jnp.concatenate([column_got[m] for m in range(8)], axis=0)
        ada_ref[...] = lax.dot_general(blocks, gathered, (((0,), (0,)), ((), ())), preferred_element_type=F32)
        for part in range(3):
            copy, target, place = piece(part)

            @pl.when(target != seq)
            def _():
                copy.wait_send()

        for place in range(3):
            copy, source = arriving(place)

            @pl.when(source != seq)
            def _():
                copy.wait_recv()

        for place in range(3):
            qkv_ref[:, place * own : (place + 1) * own] = piece_got[place]
        for copy in cond_copies:
            copy.wait()
        term = (cond_all[0] + cond_all[1]) + (cond_all[2] + cond_all[3])
        value = conditioning[...]
        gate = 1.0 / (1.0 + jnp.exp(-value))
        cond_ref[...] = term * gate * (1.0 + value * (1.0 - gate))
        for copy in small_copies:
            copy.wait()
        for place in range(4):
            ada_bias_ref[:, place * columns : (place + 1) * columns] = small_seq[place, 2:3]
        qv_bias_ref[...] = small_seq[0, 0:2, :width]
        proj_bias_ref[...] = small_seq[1, 0:1, :width]
        for line in range(3, 7):
            up_bias_ref[:, (line - 3) * width : (line - 2) * width] = small_seq[line // 2, line % 2 : line % 2 + 1, :width]
        down_bias_ref[...] = small_seq[3, 1:2, :width]


def finish_all(slot_col, seg, table, grads, weight, tokens, grad_middle, slot_sums, pick, conditioning, biases, qkv, cond, ada):
    rows, length, width = tokens.shape
    images, columns = conditioning.shape[0], ada.shape[0]
    depth, own = width // 8, width // 4
    fixed = lambda *dims: pl.BlockSpec(dims, lambda r: (0,) * len(dims), pipeline_mode=pl.Buffered(buffer_count=1))
    result = lambda *dims: pl.BlockSpec(dims, lambda r: (0,) * len(dims))
    row = lambda *dims: pl.BlockSpec((1,) + dims, lambda r: (r, 0, 0))
    shape = jax.ShapeDtypeStruct
    vmem = lambda dtype, *dims: pltpu.VMEM(dims, dtype)
    copies = 3 + 7 + 3 + 3 + 1 + 3 + 3 + 1 + 3 + 3 + 3 + 3
    return pl.pallas_call(
        last_kernel,
        grid=(rows,),
        in_specs=[
            fixed(*slot_col.shape),
            row(1, length),
            row(*table.shape[1:]),
            row(3 * width, length),
            fixed(width, 3 * width),
            row(length, width),
            row(length, width),
            row(*slot_sums.shape[1:]),
            row(*pick.shape[1:]),
            fixed(images, width),
            fixed(8, width),
            fixed(4, depth, 3 * own),
            fixed(8, images, depth),
            pl.BlockSpec(memory_space=pl.ANY),
        ],
        out_specs=[
            row(length, width),
            result(depth, columns),
            result(images, width),
            result(1, 4 * columns),
            result(2, width),
            result(1, width),
            result(1, 4 * width),
            result(1, width),
            result(depth, 3 * own),
        ],
        out_shape=[
            shape((rows, length, width), F32),
            shape((depth, columns), F32),
            shape((images, width), F32),
            shape((1, 4 * columns), F32),
            shape((2, width), F32),
            shape((1, width), F32),
            shape((1, 4 * width), F32),
            shape((1, width), F32),
            shape((depth, 3 * own), F32),
        ],
        scratch_shapes=[
            vmem(BF16, columns, width),
            vmem(F32, images, 6 * width),
            vmem(F32, 8, 3 * width),
            vmem(F32, 4, images, columns),
            vmem(F32, 3, images, columns),
            vmem(F32, 4, 8, columns),
            vmem(F32, 3, 8, columns),
            vmem(BF16, 4, 2, images, columns),
            vmem(F32, 2, 8, columns),
            vmem(F32, 4, 8, columns),
            vmem(F32, 4, 8, columns),
            vmem(F32, 4, images, width),
            vmem(BF16, 8, images, depth),
            vmem(BF16, 4, depth, 3 * own),
            vmem(BF16, 3, depth, 3 * own),
            vmem(F32, 3, depth, own),
            vmem(F32, 3, depth, own),
            pltpu.SemaphoreType.DMA,
            pltpu.SemaphoreType.DMA((copies,)),
            pltpu.SemaphoreType.DMA((copies,)),
        ],
        compiler_params=pltpu.CompilerParams(vmem_limit_bytes=VMEM_LIMIT, collective_id=5, has_side_effects=True),
        cost_estimate=pl.CostEstimate(flops=5 * 10**9, bytes_accessed=3 * 10**7, transcendentals=0),
    )(slot_col, seg, table, grads, weight, tokens, grad_middle, slot_sums, pick, conditioning, biases, qkv, cond, ada)


def forward_kernel(
    block,
    slot_col,
    image_col,
    seg,
    fill,
    conditioning,
    ada_bias,
    qv_bias,
    proj_bias,
    tokens,
    ada,
    weight,
    proj,
    cotangent,
    normed_ref,
    packed_ref,
    attended_ref,
    features_ref,
    branch_ref,
    middle_ref,
    inner_ref,
    grad_ref,
    inner_turned_ref,
    grad_turned_ref,
    table_ref,
    code_row,
    code_col,
    lse_ref,
    bias_sum,
    here,
    normed_all,
    packed_all,
    ada_here,
    windows,
    turned,
    own_weight,
    bias_turned,
    mod_all,
    table,
    seg_all,
    attended_all,
    attended_got,
    flat,
    features_all,
    proj_here,
    cotangent_here,
    branch_all,
    middle_all,
    inner_all,
    grad_all,
    inner_turned,
    grad_turned,
    rows_turned,
    load_sem,
    own_sem,
    mod_sent,
    mod_came,
    sent,
    came,
    forward_sent,
    forward_came,
    heads_sent,
    heads_came,
    heads_kept,
    store_sem,
    last_sem,
):
    rows, _, local, width = here.shape
    _, parts, heads, size, length = packed_all.shape
    own, depth, half = heads * size, width // 8, local // 2
    columns = ada_here.shape[0]
    images, slots = conditioning.shape[0], image_col.shape[1]
    scale = size**-0.5 * LOG2E
    seq = lax.axis_index("seq")
    core = lax.rem(lax.axis_index("rows"), 2)
    places = [seq] + peers_of(seq)
    peers = [{"seq": place} for place in places]

    greet(peers[1:])

    def direct(r, m):
        index = r * 2 + m - 1
        return send_to(tokens.at[r], here.at[r, m], sent.at[index], came.at[index], peers[m])

    def forward(r, m):
        part = pl.ds(0, half) if m == 1 else pl.ds(half, half)
        index = r * 2 + m - 1
        return send_to(
            here.at[r, 3 - m, part], here.at[r, 3, part], forward_sent.at[index], forward_came.at[index], peers[m]
        )

    def go(copies):
        for copy in copies:
            copy.start()

    def end(copies):
        for copy in copies:
            copy.wait()

    go([direct(0, m) for m in (1, 2)])
    own_copies = [pltpu.make_async_copy(tokens.at[r], here.at[r, 0], own_sem.at[r]) for r in range(rows)]
    load_ada = pltpu.make_async_copy(ada, ada_here, load_sem.at[0])
    load_windows = []
    for part in range(3):
        lanes = pl.ds(pl.multiple_of(part * width + seq * 256, 128), 384)
        load_windows.append(pltpu.make_async_copy(weight.at[:, lanes], windows.at[part], load_sem.at[1 + part]))
    load_proj = pltpu.make_async_copy(proj, proj_here, load_sem.at[4])
    load_cotangent = pltpu.make_async_copy(cotangent, cotangent_here, load_sem.at[5])
    go([load_ada] + load_windows + own_copies + [load_proj, load_cotangent])

    value = conditioning[...].astype(F32)
    low = (value / (1.0 + jnp.exp(-value))).astype(BF16)
    load_ada.wait()
    mod_all[seq] = lax.dot_general(low, ada_here[...], (((1,), (1,)), ((), ())), preferred_element_type=F32)
    mod_copies = [
        send_to(mod_all.at[seq], mod_all.at[seq], mod_sent.at[m - 1], mod_came.at[m - 1], peers[m]) for m in range(1, 4)
    ]
    go(mod_copies)

    for m in range(4):
        lanes = pl.ds(pl.multiple_of(places[m] * local, 128), local)
        found = seg[:, lanes]
        where = places[m] * local + lax.broadcasted_iota(jnp.int32, (rows, local), 1)
        code = jnp.where(where < fill[...], found, -1 - where)
        for r in range(rows):
            seg_all[r, m] = found[r : r + 1]
            code_row[r, :, m * local : (m + 1) * local] = code[r : r + 1]
            column = jnp.broadcast_to(code[r : r + 1].astype(F32), (128, local)).T[:, :1]
            code_col[r, m * local : (m + 1) * local] = column.astype(jnp.int32)

    for part in range(3):
        load_windows[part].wait()
        turned[...] = windows[part].astype(F32).T
        own_weight[part * own : (part + 1) * own] = turned[pl.ds(pl.multiple_of(seq * 32, 8), own), :].astype(BF16)
    window = qv_bias[:, pl.ds(pl.multiple_of(seq * 256, 128), 384)].astype(F32)
    bias_turned[...] = jnp.concatenate([window, jnp.zeros((6, 384), F32)], axis=0).T
    bias = bias_turned[pl.ds(pl.multiple_of(seq * 32, 8), own), :]
    bias = jnp.concatenate([bias[:, 0:1], jnp.zeros((own, 1), F32), bias[:, 1:2]], axis=0)

    end([direct(0, m) for m in (1, 2)])
    go([forward(0, m) for m in (1, 2)] + [direct(1, m) for m in (1, 2)])

    end(mod_copies)
    for place in range(4):
        lanes = slice(place * columns, (place + 1) * columns)
        table[:, lanes] = mod_all[place] + ada_bias[:, lanes].astype(F32)
    stacked = jnp.concatenate(split_low(table[...]), axis=0)
    image_row = lax.rem(lax.broadcasted_iota(jnp.int32, (slots, 3 * images), 1), images)
    for r in range(rows):
        picked = (image_col[r] == image_row).astype(BF16)
        table_ref[r] = jnp.dot(picked, stacked, preferred_element_type=F32)

    def stores(r, m):
        index = r * 4 + m
        lanes = pl.ds(m * local, local)
        return (
            pltpu.make_async_copy(normed_all.at[r, m], normed_ref.at[r, m], store_sem.at[0, index]),
            pltpu.make_async_copy(packed_all.at[r, :, :, :, lanes], packed_ref.at[r, :, :, :, lanes], store_sem.at[1, index]),
        )

    def work(r, m):
        mods = per_token(slot_col[...], seg_all[r, m], table_ref[r, :, : 2 * width])
        normal, _ = normalize(here[r, m].astype(F32))
        normed = (normal * (1.0 + mods[:, width:]) + mods[:, :width]).astype(BF16)
        normed_all[r, m] = normed
        mixed = lax.dot_general(own_weight[...], normed, (((1,), (1,)), ((), ())), preferred_element_type=F32)
        mixed = (mixed + bias).astype(BF16)
        for part in range(parts):
            for head in range(heads):
                start = (part * heads + head) * size
                packed_all[r, part, head, :, m * local : (m + 1) * local] = mixed[start : start + size]
        go(stores(r, m))

    def to_peer(r, h, m):
        source = attended_all.at[r, h, :, pl.ds(m * local, local)]
        place = (r * heads + h) * 3 + m - 1
        return send_to(source, attended_got.at[r, seq, h], heads_sent.at[place], heads_came.at[place], peers[m])

    def to_self(r, h):
        source = attended_all.at[r, h, :, pl.ds(0, local)]
        return pltpu.make_async_copy(source, attended_got.at[r, seq, h], heads_kept.at[r * heads + h])

    def attend_head(r, h):
        keys = packed_all[r, 1, h].astype(F32).T.astype(BF16)
        values = packed_all[r, 2, h]
        codes = code_col[r]
        for step in range(length // block):
            lanes = pl.ds(step * block, block)
            scores = jnp.dot(keys, packed_all[r, 0, h, :, lanes], preferred_element_type=F32)
            scores = jnp.where(codes == code_row[r, :, lanes], scores * scale, -1e30)
            peak = jnp.max(scores, axis=0, keepdims=True)
            raised = jnp.exp2(scores - peak)
            total = jnp.sum(raised, axis=0, keepdims=True)
            probs = (raised * (1.0 / total)).astype(BF16)
            attended_all[r, h, :, lanes] = jnp.dot(values, probs, preferred_element_type=F32).astype(BF16)
            lse_ref[r, h, :, lanes] = peak + jnp.log2(total)
        to_self(r, h).start()
        for m in range(1, 4):
            to_peer(r, h, m).start()

    def attend_row(r, first, last):
        @pl.loop(first, last)
        def _(h):
            attend_head(r, h)

    end(own_copies)
    for m in range(3):
        work(0, m)
    end([forward(0, m) for m in (1, 2)])
    work(0, 3)
    attend_row(0, 0, heads // 2)
    end([direct(1, m) for m in (1, 2)])
    go([forward(1, m) for m in (1, 2)])
    attend_row(0, heads // 2, heads)
    for m in range(3):
        work(1, m)
    end([forward(1, m) for m in (1, 2)])
    work(1, 3)
    attend_row(1, 0, heads)
    end([load_proj, load_cotangent])

    def last_stores(r):
        lines, lanes = pl.ds(r * local, local), pl.ds(r * local, local)
        pairs = (
            (attended_all.at[r], attended_ref.at[r]),
            (features_all.at[r], features_ref.at[r]),
            (branch_all.at[r], branch_ref.at[r]),
            (middle_all.at[r], middle_ref.at[r]),
            (inner_all.at[r], inner_ref.at[lines]),
            (grad_all.at[r], grad_ref.at[lines]),
            (inner_turned.at[r], inner_turned_ref.at[:, lanes]),
            (grad_turned.at[r], grad_turned_ref.at[:, lanes]),
        )
        return [pltpu.make_async_copy(source, target, last_sem.at[r, k]) for k, (source, target) in enumerate(pairs)]

    for r in range(rows):
        for h in range(heads):
            to_self(r, h).wait()
            for m in range(1, 4):
                to_peer(r, h, m).wait()
        for place in range(4):
            for h in range(heads):
                start = (place * heads + h) * size
                flat[start : start + size] = attended_got[r, place, h].astype(F32)
        features = flat[...].astype(BF16)
        features_all[r] = features
        mods = per_token(slot_col[...], seg_all[r, 0], table_ref[r, :, 2 * width :])
        gate_a, shift_b, scale_b, gate_b = (mods[:, k * width : (k + 1) * width] for k in range(4))
        branch = lax.dot_general(features, proj_here[...], (((0,), (0,)), ((), ())), preferred_element_type=F32) + proj_bias[...]
        middle = here[r, 0].astype(F32) + gate_a * branch
        branch_all[r] = branch
        middle_all[r] = middle
        normed = normalize(middle)[0] * (1.0 + scale_b) + shift_b
        grad = cotangent_here[r].astype(F32) * gate_b
        inner_all[r] = normed.astype(BF16)
        grad_all[r] = grad.astype(BF16)
        for values, target in ((normed, inner_turned), (grad, grad_turned)):
            rows_turned[...] = values.T
            for place in range(4):
                for order in range(2):
                    first = pl.multiple_of((2 * place + (core if order == 0 else 1 - core)) * depth, 8)
                    start = (4 * order + place) * depth
                    target[r, start : start + depth] = rows_turned[pl.ds(first, depth), :].astype(BF16)
        sums = jnp.sum(grad.astype(BF16).astype(F32), axis=0, keepdims=True)
        if r == 0:
            bias_sum[...] = sums
        else:
            bias_sum[...] += sums
        go(last_stores(r))
    for r in range(rows):
        for m in range(4):
            end(stores(r, m))
        end(last_stores(r))


def before_feed_forward(slot_col, image_col, seg, fill, conditioning, ada_bias, qv_bias, proj_bias, tokens, ada, weight, proj, cotangent):
    rows, local, width = tokens.shape
    length = 4 * local
    images, slots = conditioning.shape[0], image_col.shape[1]
    heads, size = HEADS // 4, width // HEADS
    columns = ada.shape[0]
    shape = jax.ShapeDtypeStruct
    vmem = lambda dtype, *dims: pltpu.VMEM(dims, dtype)
    near, far = pl.BlockSpec(memory_space=pltpu.VMEM), pl.BlockSpec(memory_space=pl.ANY)
    dma = lambda *dims: pltpu.SemaphoreType.DMA(dims)
    return pl.pallas_call(
        partial(forward_kernel, 512),
        in_specs=[near] * 8 + [far] * 5,
        out_specs=[far] * 10 + [near] * 5,
        out_shape=[
            shape((rows, 4, local, width), BF16),
            shape((rows, 3, heads, size, length), BF16),
            shape((rows, heads, size, length), BF16),
            shape((rows, width, local), BF16),
            shape((rows, local, width), F32),
            shape((rows, local, width), F32),
            shape((rows * local, width), BF16),
            shape((rows * local, width), BF16),
            shape((width, rows * local), BF16),
            shape((width, rows * local), BF16),
            shape((rows, slots, 6 * width), F32),
            shape((rows, 1, length), jnp.int32),
            shape((rows, length, 1), jnp.int32),
            shape((rows, heads, 1, length), F32),
            shape((1, width), F32),
        ],
        scratch_shapes=[
            vmem(BF16, rows, 4, local, width),
            vmem(BF16, rows, 4, local, width),
            vmem(BF16, rows, 3, heads, size, length),
            vmem(BF16, columns, width),
            vmem(BF16, 3, width, 384),
            vmem(F32, 384, width),
            vmem(BF16, 3 * heads * size, width),
            vmem(F32, 384, 8),
            vmem(F32, 4, images, columns),
            vmem(F32, images, 6 * width),
            vmem(jnp.int32, rows, 4, 1, local),
            vmem(BF16, rows, heads, size, length),
            vmem(BF16, rows, 4, heads, size, local),
            vmem(F32, width, local),
            vmem(BF16, rows, width, local),
            vmem(BF16, width, width),
            vmem(BF16, rows, local, width),
            vmem(F32, rows, local, width),
            vmem(F32, rows, local, width),
            vmem(BF16, rows, local, width),
            vmem(BF16, rows, local, width),
            vmem(BF16, rows, width, local),
            vmem(BF16, rows, width, local),
            vmem(F32, width, local),
            dma(6),
            dma(rows),
            dma(3),
            dma(3),
            dma(2 * rows),
            dma(2 * rows),
            dma(2 * rows),
            dma(2 * rows),
            dma(3 * rows * heads),
            dma(3 * rows * heads),
            dma(rows * heads),
            dma(2, 4 * rows),
            dma(rows, 8),
        ],
        compiler_params=pltpu.CompilerParams(vmem_limit_bytes=VMEM_LIMIT, collective_id=6, has_side_effects=True),
        cost_estimate=pl.CostEstimate(flops=2 * 10**10, bytes_accessed=4 * 10**7, transcendentals=0),
    )(slot_col, image_col, seg, fill, conditioning, ada_bias, qv_bias, proj_bias, tokens, ada, weight, proj, cotangent)


def gather_seq(values):
    count = lax.axis_size("seq")
    if count == 4:
        first, second = swap(values, "seq", 1), swap(values, "seq", 2)
        half = values.shape[0] // 2
        third = jnp.concatenate([swap(second[:half], "seq", 1), swap(first[half:], "seq", 2)], axis=0)
        return [values, first, second, third]
    return [values] + [swap(values, "seq", m) for m in range(1, count)]


def exchange_seq(blocks):
    return [blocks[0]] + [swap(blocks[m], "seq", m) for m in range(1, len(blocks))]


def in_order(blocks, axis):
    index = lax.axis_index("seq")
    stacked = jnp.stack(blocks, axis=axis)
    return flip_blocks(stacked, axis, index)


class Halving:
    def __init__(self, blocks, low_first):
        self.blocks = dict(enumerate(blocks))
        bits = [1 << k for k in range(len(blocks).bit_length() - 1)]
        self.bits = bits if low_first else bits[::-1]

    def send(self):
        self.bit = self.bits.pop(0)
        self.kept = [m for m in self.blocks if not m & self.bit]
        return jnp.stack([self.blocks[m | self.bit] for m in self.kept]).astype(BF16)

    def move(self, sent):
        return swap(sent, "seq", self.bit)

    def add(self, came):
        self.blocks = {m: self.blocks[m] + came[k].astype(F32) for k, m in enumerate(self.kept)}


class Spreading:
    def __init__(self, pick):
        chip, chips = lax.axis_index("rows") // 2, lax.axis_size("rows") // 2
        self.own = pick(chip)
        self.sent = [pick(chip ^ m).astype(BF16) for m in range(1, chips)]

    def move(self):
        self.came = [swap(block, "rows", 2 * (m + 1)) for m, block in enumerate(self.sent)]

    def total(self):
        total = self.own
        for block in self.came:
            total = total + block.astype(F32)
        return total


def columns_of(values, index, size):
    return lax.dynamic_slice_in_dim(values, index * size, size, values.ndim - 1)


def lines_of(values, index, size):
    return lax.dynamic_slice_in_dim(values, index * size, size, 0)


def tied(*values):
    return lax.optimization_barrier(values)


def on_square(
    tokens,
    conditioning,
    segment_ids,
    image_index,
    row_fill,
    ada_weight,
    ada_bias,
    qkv_weight,
    qv_bias,
    proj_weight,
    proj_bias,
    up_weight,
    up_bias,
    down_weight,
    down_bias,
    cotangent,
):
    row_count, local_len, width = tokens.shape
    seq_count, groups = lax.axis_size("seq"), lax.axis_size("rows")
    seq_index, row_index = lax.axis_index("seq"), lax.axis_index("rows")
    chips, core = groups // 2, row_index % 2
    full_len = local_len * seq_count
    token_count = row_count * local_len
    heads_dev = HEADS // seq_count
    head_size = width // HEADS
    own = heads_dev * head_size
    image_count = conditioning.shape[0]
    hidden_size = up_weight.shape[1]
    depth = width // groups

    slot_ids = lax.iota(jnp.int32, image_index.shape[1])
    slot_col = jnp.tile(slot_ids, 3)[:, None]
    (
        normed_all,
        packed,
        attended,
        attended_tok,
        branch_a,
        middle,
        normed_b,
        grad_out,
        normed_turned,
        grad_turned,
        slot_mod,
        code_row,
        code_col,
        log_totals,
        part_down_bias,
    ) = before_feed_forward(
        slot_col,
        image_index[:, :, None],
        segment_ids,
        row_fill[:, None],
        conditioning,
        ada_bias[None],
        qv_bias,
        proj_bias.astype(F32)[None],
        tokens,
        ada_weight.T,
        qkv_weight,
        proj_weight,
        cotangent,
    )
    normed_all = normed_all.reshape(row_count, full_len, width)
    cond_wide = conditioning.astype(F32)
    cond_cols = jax.nn.silu(cond_wide).astype(BF16).reshape(image_count, groups, depth).transpose(1, 0, 2)
    seg_row = lax.dynamic_slice_in_dim(segment_ids, seq_index * local_len, local_len, 1)[:, None, :]
    out_sum, grad_sum, part_up_bias, grad_up_weight, down_turned = feed_forward_reduce(
        normed_b, grad_out, normed_turned, grad_turned, up_weight, down_weight, up_bias.astype(F32)
    )
    block_out, grad_middle, slot_sums, part_proj_bias, grad_view, proj_both = after_feed_forward(
        slot_col,
        seg_row,
        slot_mod,
        attended_tok,
        proj_weight,
        down_bias.astype(F32)[None],
        out_sum,
        grad_sum,
        middle,
        branch_a,
        cotangent,
    )
    grad_view = grad_view.reshape(row_count, heads_dev, head_size, full_len)
    grad_sent, qkv_both, grad_proj_weight, grad_down_weight = attend_back_reduce(
        packed, attended, grad_view, log_totals, code_col, code_row, normed_all, proj_both, down_turned, 256, 512
    )
    grad_flat = grad_sent.reshape(row_count, 3 * width, local_len)
    pick = (image_index[:, None, :] == lax.iota(jnp.int32, image_count)[None, :, None]).astype(F32)
    biases = jnp.concatenate(
        [jnp.zeros((2, width), F32), part_proj_bias, part_up_bias.reshape(4, width), part_down_bias], axis=0
    )
    (
        grad_tokens,
        grad_ada_weight,
        grad_cond,
        grad_ada_bias,
        grad_qv_bias,
        grad_proj_bias,
        grad_up_bias,
        grad_down_bias,
        grad_qkv_weight,
    ) = finish_all(
        slot_col,
        seg_row,
        slot_mod,
        grad_flat,
        qkv_weight,
        tokens,
        grad_middle,
        slot_sums,
        pick,
        cond_wide,
        biases,
        qkv_both,
        cond_cols,
        ada_weight.T,
    )
    return (
        block_out,
        grad_tokens,
        grad_cond,
        grad_ada_weight,
        grad_ada_bias[0],
        grad_qkv_weight,
        grad_qv_bias,
        grad_proj_weight,
        grad_proj_bias[0],
        grad_up_weight,
        grad_up_bias[0],
        grad_down_weight.T,
        grad_down_bias[0],
    )


def on_device(
    tokens,
    conditioning,
    segment_ids,
    image_index,
    row_fill,
    ada_weight,
    ada_bias,
    qkv_weight,
    qv_bias,
    proj_weight,
    proj_bias,
    up_weight,
    up_bias,
    down_weight,
    down_bias,
    cotangent,
):
    row_count, local_len, width = tokens.shape
    seq_count, groups = lax.axis_size("seq"), lax.axis_size("rows")
    seq_index, row_index = lax.axis_index("seq"), lax.axis_index("rows")
    chips, core = groups // 2, row_index % 2
    full_len = local_len * seq_count
    token_count = row_count * local_len
    heads_dev = HEADS // seq_count
    head_size = width // HEADS
    own = heads_dev * head_size
    image_count = conditioning.shape[0]
    hidden_size = up_weight.shape[1]
    depth = width // groups

    tokens_all = jnp.concatenate(gather_seq(tokens), axis=1)
    order = lax.iota(jnp.int32, seq_count) ^ seq_index
    seg_blocks = flip_blocks(segment_ids.reshape(row_count, seq_count, local_len), 1, seq_index)
    seg_all = seg_blocks.reshape(row_count, full_len)
    places = (order[:, None] * local_len + lax.iota(jnp.int32, local_len)).reshape(1, full_len)
    codes = jnp.where(places < row_fill[:, None], seg_all, -1 - places)
    code_col, code_row = codes[:, :, None], codes[:, None, :]

    qkv_own = jnp.concatenate(
        [lax.dynamic_slice_in_dim(qkv_weight, part * width + seq_index * own, own, 1).T for part in range(3)], axis=0
    )
    bias_own = lax.dynamic_slice_in_dim(qv_bias.astype(F32), seq_index * own, own, 1)
    bias_own = jnp.concatenate([bias_own[0], jnp.zeros((own,), F32), bias_own[1]])

    cond_wide = conditioning.astype(F32)
    cond_low = jax.nn.silu(cond_wide).astype(BF16)
    mod_part = jnp.dot(cond_low, ada_weight, preferred_element_type=F32)
    modulation = lax.all_gather(mod_part, "seq", axis=1, tiled=True) + ada_bias.astype(F32)
    cond_cols = cond_low.reshape(image_count, groups, depth).transpose(1, 0, 2)
    local_seg = lax.dynamic_slice_in_dim(segment_ids, seq_index * local_len, local_len, 1)
    slot_ids = lax.iota(jnp.int32, image_index.shape[1])
    slot_mod = jnp.take(modulation, image_index, axis=0)

    normed_all, packed = project_qkv(
        tokens_all, seg_all, slot_mod[:, :, : 2 * width], qkv_own, bias_own, heads_dev, min(256, full_len)
    )
    square = seq_count == 4 and chips == 4
    attended, log_totals, *attended_sent = attend(packed, code_col, code_row, 512, square)

    slot_pick = (local_seg[:, :, None] == slot_ids).astype(F32)
    mod_tok = jnp.einsum("rts,rse->rte", slot_pick, slot_mod, precision=lax.Precision.HIGHEST)
    shift_a, scale_a, gate_a, shift_b, scale_b, gate_b = jnp.split(mod_tok, 6, axis=-1)
    tokens_wide = tokens.astype(F32)
    upstream = cotangent.astype(F32)
    grad_branch_b = (upstream * gate_b).astype(BF16)
    part_down_bias = jnp.sum(grad_branch_b.astype(F32), axis=(0, 1))
    grad_out = grad_branch_b.reshape(token_count, width)
    grad_turned = turn_halves(grad_out, seq_count, core)

    def by_block(values):
        return [values[..., m * local_len : (m + 1) * local_len] for m in range(seq_count)]

    if square:
        attended_tok = attended_sent[0]
    else:
        attended_tok = in_order(exchange_seq(by_block(attended.reshape(row_count, own, full_len))), 1)
    attended_tok = attended_tok.reshape(row_count, width, local_len)
    branch_a = jnp.einsum(
        "rft,fe->rte", attended_tok, proj_weight, preferred_element_type=F32
    ) + proj_bias.astype(F32)
    middle = tokens_wide + gate_a * branch_a
    normed_b = modulate(middle, shift_b, scale_b).astype(BF16).reshape(token_count, width)
    normed_turned = turn_halves(normed_b, chips, core)

    if square:
        out_sum, grad_sum, part_up_bias, grad_up_weight, down_turned = feed_forward_reduce(
            normed_b, grad_out, normed_turned, grad_turned, up_weight, down_weight, up_bias.astype(F32)
        )
        part_up_bias = part_up_bias.reshape(1, hidden_size)
    else:
        out_sum, grad_sum, up_keep, up_send, down_keep, down_send, part_up_bias = feed_forward(
            normed_b, grad_out, normed_turned, grad_turned, up_weight, down_weight, up_bias.astype(F32)[None], 512
        )
        up_came, down_came = swap(up_send, "rows", 1), swap(down_send, "rows", 1)
    branch_b = out_sum.reshape(row_count, local_len, width) + down_bias.astype(F32)
    grad_normed_b = grad_sum.reshape(row_count, local_len, width)
    block_out = (middle + gate_b * branch_b).astype(BF16)
    grad_gate_b = upstream * branch_b
    _, norm_back_b = jax.vjp(modulate, middle, shift_b, scale_b)
    grad_mid_norm, grad_shift_b, grad_scale_b = norm_back_b(grad_normed_b)
    grad_middle = upstream + grad_mid_norm
    grad_branch_a = (grad_middle * gate_a).astype(BF16)
    grad_gate_a = grad_middle * branch_a
    part_proj_bias = jnp.sum(grad_branch_a.astype(F32), axis=(0, 1))
    grad_attended = jnp.einsum(
        "fe,rte->rft", proj_weight, grad_branch_a, preferred_element_type=F32
    ).astype(BF16)
    heads_blocks = [lax.dynamic_slice_in_dim(grad_attended, (seq_index ^ m) * own, own, 1) for m in range(seq_count)]
    grad_heads_in = jnp.concatenate(exchange_seq(heads_blocks), axis=2)
    grad_view = grad_heads_in.reshape(row_count, heads_dev, head_size, full_len)

    part_proj = jnp.einsum("rte,rft->ef", grad_branch_a, attended_tok, preferred_element_type=F32)
    proj_view = part_proj.reshape(seq_count, 2, depth * groups // (2 * seq_count), width)
    proj_keep = lax.dynamic_index_in_dim(proj_view, core, 1, keepdims=False)
    proj_send = lax.dynamic_index_in_dim(proj_view, 1 - core, 1, keepdims=False).astype(BF16)
    proj_came = swap(proj_send, "rows", 1).reshape(width // 2, width)
    proj_keep = proj_keep.reshape(width // 2, width)
    up_size, down_size = hidden_size // seq_count, width // (2 * seq_count)
    proj_blocks = [
        lines_of(proj_keep, seq_index ^ m, down_size) + lines_of(proj_came, seq_index ^ m, down_size).astype(F32)
        for m in range(seq_count)
    ]
    if square:
        proj_sent = [block.astype(BF16) for block in proj_blocks[1:]]
        grad_view, *proj_sent = tied(grad_view, *proj_sent)
        proj_total = proj_blocks[0]
        for m in range(1, seq_count):
            proj_total = proj_total + swap(proj_sent[m - 1], "seq", m).astype(F32)
    else:
        ups = Halving(
            [
                columns_of(up_keep, seq_index ^ m, up_size) + columns_of(up_came, seq_index ^ m, up_size).astype(F32)
                for m in range(seq_count)
            ],
            True,
        )
        downs = Halving(
            [
                jnp.concatenate(
                    [
                        lines_of(down_keep, seq_index ^ m, down_size)
                        + lines_of(down_came, seq_index ^ m, down_size).astype(F32),
                        proj_blocks[m],
                    ],
                    axis=1,
                )
                for m in range(seq_count)
            ],
            False,
        )
        up_sent, down_sent = ups.send(), downs.send()
        up_came, down_came = ups.move(up_sent), downs.move(down_sent)

    grad_heads, *grad_sent = attend_back(
        packed, attended, grad_view, log_totals, code_col, code_row, 256, 512, square
    )
    grad_own = grad_heads.reshape(row_count, 3 * own, full_len)
    if square:
        grad_flat = grad_sent[0]
    else:
        grad_blocks = exchange_seq(by_block(grad_own))
        grad_flat = in_order([block.reshape(row_count, 3, own, local_len) for block in grad_blocks], 2)
    grad_flat = grad_flat.reshape(row_count, 3 * width, local_len)

    qkv_keep, qkv_send, own_sums = qkv_weight_grad(grad_own, normed_all)
    down_part, proj_part = hidden_size // chips, width // chips
    if square:
        proj_spread = Spreading(lambda chip: columns_of(proj_total, chip, proj_part))
        grad_flat, qkv_send, *proj_spread.sent = tied(grad_flat, qkv_send, *proj_spread.sent)
        proj_spread.move()
    else:
        while ups.bits:
            ups.add(up_came)
            downs.add(down_came)
            up_came, down_came = ups.move(ups.send()), downs.move(downs.send())
        ups.add(up_came)
        downs.add(down_came)
        up_total, down_total = ups.blocks[0], downs.blocks[0][:, :hidden_size]
        proj_total = downs.blocks[0][:, hidden_size:]
        up_spread = Spreading(lambda chip: lines_of(up_total, chip, depth))
        down_spread = Spreading(
            lambda chip: jnp.concatenate(
                [columns_of(down_total, chip, down_part), columns_of(proj_total, chip, proj_part)], axis=1
            )
        )
        up_spread.move()
        down_spread.move()
    qkv_came = swap(qkv_send, "rows", 1)
    grad_normed_a = jnp.einsum("rft,df->rtd", grad_flat, qkv_weight, preferred_element_type=F32)
    _, norm_back_a = jax.vjp(modulate, tokens_wide, shift_a, scale_a)
    grad_tok_norm, grad_shift_a, grad_scale_a = norm_back_a(grad_normed_a)
    grad_tokens = grad_middle + grad_tok_norm
    grad_mod_tok = jnp.concatenate(
        [grad_shift_a, grad_scale_a, grad_gate_a, grad_shift_b, grad_scale_b, grad_gate_b], axis=-1
    )
    slot_grads = jnp.einsum("rts,rte->rse", slot_pick, grad_mod_tok, precision=lax.Precision.HIGHEST)
    image_pick = (image_index[:, :, None] == lax.iota(jnp.int32, image_count)).astype(F32)
    grad_modulation = jnp.einsum("rsi,rse->ie", image_pick, slot_grads, precision=lax.Precision.HIGHEST)

    own_sums = own_sums.reshape(3, own)
    part_qv = lax.dynamic_update_slice(
        jnp.zeros((2, width), F32), jnp.stack([own_sums[0], own_sums[2]]), (0, seq_index * own)
    )
    small = jnp.concatenate([part_qv.reshape(-1), part_proj_bias, part_up_bias[0], part_down_bias])
    columns = ada_weight.shape[1]
    lines = -(-small.size // (seq_count * columns))
    room = seq_count * columns * lines
    small = jnp.pad(small, (0, room - small.size)).reshape(seq_count, lines, columns)
    mod_view = grad_modulation.reshape(image_count, seq_count, columns).transpose(1, 0, 2)
    joined = jnp.concatenate(
        [mod_view, jnp.zeros((seq_count, 1, columns), F32), small, jnp.zeros((seq_count, 7 - lines, columns), F32)], axis=1
    )
    qkv_both = qkv_keep + qkv_came.astype(F32)
    qkv_spread = Spreading(lambda chip: lax.dynamic_index_in_dim(qkv_both, chip, 0, keepdims=False))
    joined, *qkv_spread.sent = tied(joined, *qkv_spread.sent)
    qkv_spread.move()
    if square:
        turned = jnp.concatenate([down_turned, proj_spread.total()], axis=1)
    else:
        grad_up_weight, turned = up_spread.total(), down_spread.total()
    half = down_part // 2
    cut = lambda index: jnp.concatenate(
        [columns_of(turned[:, :down_part], index, half), columns_of(turned[:, down_part:], index, proj_part // 2)], axis=1
    )
    core_keep, core_sent = cut(core), cut(1 - core)
    joined, core_sent = tied(joined, core_sent)
    core_came = swap(core_sent, "rows", 1)
    grad_ada_weight, cond_sum, bias_sums = finish(joined, ada_weight, cond_cols, image_count)
    _, silu_back = jax.vjp(jax.nn.silu, cond_wide)
    grad_cond = silu_back(cond_sum)[0]
    grad_ada_bias = bias_sums[:, 0].reshape(-1)
    small = bias_sums[:, 1 : 1 + lines].reshape(-1)
    grad_qv_bias = small[: 2 * width].reshape(2, width)
    grad_proj_bias = small[2 * width : 3 * width]
    grad_up_bias = small[3 * width : 3 * width + hidden_size]
    grad_down_bias = small[3 * width + hidden_size : 4 * width + hidden_size]

    pair = flip_blocks(jnp.stack([core_keep, core_came]), 0, core).reshape(-1, core_keep.shape[1])
    grad_down_weight, grad_proj_weight = pair[:, :half].T, pair[:, half:].T

    qkv_total = qkv_spread.total()
    pieces = []
    for place in range(3):
        pairs = [((3 * target + place) % seq_count, target) for target in range(seq_count)]
        part_of = [0] * seq_count
        for source, target in pairs:
            part_of[source] = (3 * target + place) // seq_count
        chosen = columns_of(qkv_total, jnp.array(part_of, jnp.int32)[seq_index], own)
        pieces.append(lax.ppermute(chosen, "seq", pairs))
    grad_qkv_weight = jnp.concatenate(pieces, axis=1)
    return (
        block_out,
        grad_tokens,
        grad_cond,
        grad_ada_weight,
        grad_ada_bias,
        grad_qkv_weight,
        grad_qv_bias,
        grad_proj_weight,
        grad_proj_bias,
        grad_up_weight,
        grad_up_bias,
        grad_down_weight,
        grad_down_bias,
    )


def solution(mesh):
    in_specs = (
        P("rows", "seq", None),
        P("rows", None),
        P("rows", None),
        P("rows", None),
        P("rows"),
        P(None, "seq"),
        P(),
        P(),
        P(),
        P(),
        P(),
        P(),
        P(),
        P(),
        P(),
        P("rows", "seq", None),
    )
    out_specs = (
        P("rows", "seq", None),
        P("rows", "seq", None),
        P("rows", None),
        P("rows", "seq"),
        P(),
        P("rows", "seq"),
        P(),
        P("rows", "seq"),
        P(),
        P("rows", "seq"),
        P(),
        P("rows", "seq"),
        P(),
    )
    square = mesh.shape["seq"] == 4 and mesh.shape["rows"] == 8
    return jax.shard_map(
        on_square if square else on_device, mesh=mesh, in_specs=in_specs, out_specs=out_specs, check_vma=False
    )
```

```python
from functools import partial
import math

import jax
import jax.numpy as jnp
from jax import lax
from jax.experimental import pallas as pl
from jax.experimental.pallas import tpu as pltpu
from jax.sharding import PartitionSpec as P

HEADS = 16
LOG2E = math.log2(math.e)
VMEM_LIMIT = 60 << 20
BF16 = jnp.bfloat16
F32 = jnp.float32

norm_eps = 1e-06


def modulate(values, offset, factor):
    center = values - jnp.mean(values, axis=-1, keepdims=True)
    spread = jnp.mean(center * center, axis=-1, keepdims=True)
    return center * lax.rsqrt(spread + norm_eps) * (1.0 + factor) + offset


def gelu_tanh(values):
    return jax.nn.gelu(values, approximate=True)


def swap(values, axis, mask):
    count = lax.axis_size(axis)
    return lax.ppermute(values, axis, [(i, i ^ mask) for i in range(count)])


def flip_blocks(values, axis, mask):
    return jnp.take(values, lax.iota(jnp.int32, values.shape[axis]) ^ mask, axis=axis)


def qkv_kernel(slot_row, seg, mod, tokens, weight, bias, normed_ref, qkv_ref):
    width = tokens.shape[-1]
    values = tokens[0].astype(F32)
    picked = (seg[0] == slot_row[...]).astype(BF16)
    table = mod[0]
    high = table.astype(BF16)
    rest = table - high.astype(F32)
    middle = rest.astype(BF16)
    last = (rest - middle.astype(F32)).astype(BF16)
    stacked = jnp.concatenate([high, middle, last], axis=0)
    per_token = jnp.dot(picked, stacked, preferred_element_type=F32)
    normed = modulate(values, per_token[:, :width], per_token[:, width:]).astype(BF16)
    normed_ref[0] = normed
    mixed = lax.dot_general(weight[...], normed, (((1,), (1,)), ((), ())), preferred_element_type=F32)
    mixed = (mixed + bias[...]).astype(BF16)
    _, parts, heads, size, _ = qkv_ref.shape
    for part in range(parts):
        for head in range(heads):
            start = (part * heads + head) * size
            qkv_ref[0, part, head] = mixed[start : start + size]


def project_qkv(tokens, seg, slot_mod, weight, bias, heads, block):
    rows, length, width = tokens.shape
    slots = slot_mod.shape[1]
    features = weight.shape[0]
    size = features // (3 * heads)
    slot_row = jnp.tile(lax.iota(jnp.int32, slots), 3)[None]
    return pl.pallas_call(
        qkv_kernel,
        grid=(rows, length // block),
        in_specs=[
            pl.BlockSpec((1, 3 * slots), lambda r, t: (0, 0)),
            pl.BlockSpec((1, block, 1), lambda r, t: (r, t, 0)),
            pl.BlockSpec((1, slots, 2 * width), lambda r, t: (r, 0, 0)),
            pl.BlockSpec((1, block, width), lambda r, t: (r, t, 0)),
            pl.BlockSpec((features, width), lambda r, t: (0, 0)),
            pl.BlockSpec((features, 1), lambda r, t: (0, 0)),
        ],
        out_specs=[
            pl.BlockSpec((1, block, width), lambda r, t: (r, t, 0)),
            pl.BlockSpec((1, 3, heads, size, block), lambda r, t: (r, 0, 0, 0, t)),
        ],
        out_shape=[
            jax.ShapeDtypeStruct((rows, length, width), BF16),
            jax.ShapeDtypeStruct((rows, 3, heads, size, length), BF16),
        ],
        compiler_params=pltpu.CompilerParams(vmem_limit_bytes=VMEM_LIMIT),
        cost_estimate=pl.CostEstimate(
            flops=2 * rows * length * width * features,
            bytes_accessed=2 * rows * length * (2 * width + features),
            transcendentals=0,
        ),
    )(slot_row, seg[:, :, None], slot_mod, tokens, weight, bias[:, None])


def peers_of(seq):
    x, y = lax.rem(seq, 2), lax.div(seq, 2)
    return [seq + 1 - 2 * x, seq + 2 - 4 * y, 3 - seq]


def greet(devices):
    barrier = pltpu.get_barrier_semaphore()
    for device in devices:
        pl.semaphore_signal(barrier, inc=1, device_id=device, device_id_type=pl.DeviceIdType.MESH)
    pl.semaphore_wait(barrier, len(devices))


def send_block(source, target, sent, came, index, device):
    return pltpu.make_async_remote_copy(
        src_ref=source,
        dst_ref=target,
        send_sem=sent.at[index],
        recv_sem=came.at[index],
        device_id=device,
        device_id_type=pl.DeviceIdType.MESH,
    )


def attend_kernel(block, scale, code_col, code_row, query, key, value, out_ref, lse_ref, token_ref=None, sent=None, came=None, kept=None):
    length = query.shape[-1]
    keys = key[0, 0].astype(F32).T.astype(BF16)
    values = value[0, 0]
    codes = code_col[0]
    row, head = (pl.program_id(0), pl.program_id(1)) if sent is not None else (0, 0)
    rows, heads = out_ref.shape[:2]
    if sent is not None:
        seq = lax.axis_index("seq")
        peers = peers_of(seq)
        size = length // 4

        @pl.when((row == 0) & (head == 0))
        def _():
            greet([{"seq": peer} for peer in peers])

        def to_peer(r, h, m):
            lanes = pl.ds(m * size, size)
            place = (r * heads + h) * 3 + m - 1
            return send_block(out_ref.at[r, h, :, lanes], token_ref.at[r, seq, h], sent, came, place, {"seq": peers[m - 1]})

        def to_self(r, h):
            return pltpu.make_async_copy(out_ref.at[r, h, :, pl.ds(0, size)], token_ref.at[r, seq, h], kept.at[r * heads + h])

    for step in range(length // block):
        here = pl.ds(step * block, block)
        scores = jnp.dot(keys, query[0, 0, :, here], preferred_element_type=F32)
        scores = jnp.where(codes == code_row[0, :, here], scores * scale, -1e30)
        peak = jnp.max(scores, axis=0, keepdims=True)
        raised = jnp.exp2(scores - peak)
        total = jnp.sum(raised, axis=0, keepdims=True)
        probs = (raised * (1.0 / total)).astype(BF16)
        out_ref[row, head, :, here] = jnp.dot(values, probs, preferred_element_type=F32).astype(BF16)
        lse_ref[0, 0, :, here] = peak + jnp.log2(total)

    if sent is not None:
        to_self(row, head).start()
        for m in range(1, 4):
            to_peer(row, head, m).start()

        @pl.when((row == rows - 1) & (head == heads - 1))
        def _():
            for r in range(rows):
                for h in range(heads):
                    to_self(r, h).wait()
                    for m in range(1, 4):
                        to_peer(r, h, m).wait()


def attend(packed, col, row, block, exchange):
    rows, _, heads, size, length = packed.shape
    part = lambda j: pl.BlockSpec((1, None, 1, size, length), lambda r, h: (r, j, h, 0, 0))
    out_specs = [
        pl.BlockSpec((1, 1, size, length), lambda r, h: (r, h, 0, 0)),
        pl.BlockSpec((1, 1, 1, length), lambda r, h: (r, h, 0, 0)),
    ]
    out_shape = [
        jax.ShapeDtypeStruct((rows, heads, size, length), BF16),
        jax.ShapeDtypeStruct((rows, heads, 1, length), F32),
    ]
    scratch = []
    extra = {}
    if exchange:
        out_specs[0] = pl.BlockSpec((rows, heads, size, length), lambda r, h: (0, 0, 0, 0))
        out_specs.append(pl.BlockSpec(memory_space=pl.ANY))
        out_shape.append(jax.ShapeDtypeStruct((rows, 4, heads, size, length // 4), BF16))
        count = rows * heads
        scratch = [pltpu.SemaphoreType.DMA((3 * count,)), pltpu.SemaphoreType.DMA((3 * count,)), pltpu.SemaphoreType.DMA((count,))]
        extra = dict(collective_id=2, has_side_effects=True)
    return pl.pallas_call(
        partial(attend_kernel, block, size**-0.5 * LOG2E),
        grid=(rows, heads),
        in_specs=[
            pl.BlockSpec((1, length, 1), lambda r, h: (r, 0, 0)),
            pl.BlockSpec((1, 1, length), lambda r, h: (r, 0, 0)),
            part(0),
            part(1),
            part(2),
        ],
        out_specs=out_specs,
        out_shape=out_shape,
        scratch_shapes=scratch,
        compiler_params=pltpu.CompilerParams(vmem_limit_bytes=VMEM_LIMIT, **extra),
        cost_estimate=pl.CostEstimate(
            flops=8 * rows * heads * length * length * 128,
            bytes_accessed=8 * rows * heads * length * size,
            transcendentals=rows * heads * length * length,
        ),
    )(col, row, packed, packed, packed)


def attend_back_kernel(
    block,
    inner,
    scale,
    exchange,
    code_col,
    code_row,
    query,
    key,
    value,
    out,
    grad_out,
    lse,
    grad_ref,
    *rest,
):
    length = query.shape[-1]
    size = query.shape[-2]
    row, head = (pl.program_id(0), pl.program_id(1)) if exchange else (0, 0)
    rows, _, heads = grad_ref.shape[:3]
    if exchange:
        token_ref, key_sum, value_sum, keys, values, sent, came, kept = rest
        seq = lax.axis_index("seq")
        peers = peers_of(seq)
        local = length // 4

        @pl.when((row == 0) & (head == 0))
        def _():
            greet([{"seq": peer} for peer in peers])

        def to_peer(r, h, m):
            lanes = pl.ds(m * local, local)
            place = (r * heads + h) * 3 + m - 1
            return send_block(grad_ref.at[r, :, h, :, lanes], token_ref.at[r, :, seq, h], sent, came, place, {"seq": peers[m - 1]})

        def to_self(r, h):
            lanes = pl.ds(0, local)
            return pltpu.make_async_copy(grad_ref.at[r, :, h, :, lanes], token_ref.at[r, :, seq, h], kept.at[r * heads + h])

    else:
        key_sum, value_sum, keys, values = rest
    keys[...] = key[0, 0].astype(F32).T.astype(BF16)
    values[...] = value[0, 0].astype(F32).T.astype(BF16)
    for step in range(length // block):
        here = pl.ds(step * block, block)
        query_low = query[0, 0, :, here]
        grad_low = grad_out[0, 0, :, here]
        query_rows = query_low.astype(F32).T.astype(BF16)
        grad_rows = grad_low.astype(F32).T.astype(BF16)
        row_dot = jnp.sum(grad_low.astype(F32) * out[0, 0, :, here].astype(F32), axis=0, keepdims=True)
        grad_query = jnp.zeros((size, block), F32)
        for part in range(length // inner):
            there = pl.ds(part * inner, inner)
            scores = jnp.dot(keys[there, :], query_low, preferred_element_type=F32)
            scores = jnp.where(code_col[0, there, :] == code_row[0, :, here], scores * (scale * LOG2E), -1e30)
            probs = jnp.exp2(scores - lse[0, 0, :, here])
            grad_probs = jnp.dot(values[there, :], grad_low, preferred_element_type=F32)
            grad_raw = (probs * (grad_probs - row_dot) * scale).astype(BF16)
            value_part = jnp.dot(probs.astype(BF16), grad_rows, preferred_element_type=F32)
            key_part = jnp.dot(grad_raw, query_rows, preferred_element_type=F32)
            if step == 0:
                value_sum[there, :] = value_part
                key_sum[there, :] = key_part
            else:
                value_sum[there, :] += value_part
                key_sum[there, :] += key_part
            grad_query += jnp.dot(key[0, 0, :, there], grad_raw, preferred_element_type=F32)
        grad_ref[row, 0, head, :, here] = grad_query.astype(BF16)
    grad_ref[row, 1, head] = key_sum[...].T.astype(BF16)
    grad_ref[row, 2, head] = value_sum[...].T.astype(BF16)

    if exchange:
        to_self(row, head).start()
        for m in range(1, 4):
            to_peer(row, head, m).start()

        @pl.when((row == rows - 1) & (head == heads - 1))
        def _():
            for r in range(rows):
                for h in range(heads):
                    to_self(r, h).wait()
                    for m in range(1, 4):
                        to_peer(r, h, m).wait()


def attend_back(packed, out, grad_out, lse, col, row, block, inner, exchange):
    rows, _, heads, size, length = packed.shape
    part = lambda j: pl.BlockSpec((1, None, 1, size, length), lambda r, h: (r, j, h, 0, 0))
    whole = pl.BlockSpec((1, 1, size, length), lambda r, h: (r, h, 0, 0))
    out_specs = [pl.BlockSpec((1, 3, 1, size, length), lambda r, h: (r, 0, h, 0, 0))]
    out_shape = [jax.ShapeDtypeStruct((rows, 3, heads, size, length), BF16)]
    scratch = []
    extra = {}
    if exchange:
        out_specs = [
            pl.BlockSpec((rows, 3, heads, size, length), lambda r, h: (0, 0, 0, 0, 0)),
            pl.BlockSpec(memory_space=pl.ANY),
        ]
        out_shape.append(jax.ShapeDtypeStruct((rows, 3, 4, heads, size, length // 4), BF16))
        count = rows * heads
        scratch = [pltpu.SemaphoreType.DMA((3 * count,)), pltpu.SemaphoreType.DMA((3 * count,)), pltpu.SemaphoreType.DMA((count,))]
        extra = dict(collective_id=3, has_side_effects=True)
    return pl.pallas_call(
        partial(attend_back_kernel, block, inner, size**-0.5, exchange),
        grid=(rows, heads),
        in_specs=[
            pl.BlockSpec((1, length, 1), lambda r, h: (r, 0, 0)),
            pl.BlockSpec((1, 1, length), lambda r, h: (r, 0, 0)),
            part(0),
            part(1),
            part(2),
            whole,
            whole,
            pl.BlockSpec((1, 1, 1, length), lambda r, h: (r, h, 0, 0)),
        ],
        out_specs=out_specs,
        out_shape=out_shape,
        scratch_shapes=[
            pltpu.VMEM((length, size), F32),
            pltpu.VMEM((length, size), F32),
            pltpu.VMEM((length, size), BF16),
            pltpu.VMEM((length, size), BF16),
        ]
        + scratch,
        compiler_params=pltpu.CompilerParams(vmem_limit_bytes=VMEM_LIMIT, **extra),
        cost_estimate=pl.CostEstimate(
            flops=20 * rows * heads * length * length * 128,
            bytes_accessed=16 * rows * heads * length * size,
            transcendentals=rows * heads * length * length,
        ),
    )(col, row, packed, packed, packed, out, grad_out, lse)


def mlp_kernel(
    normed, grad_out, normed_turned, grad_turned, up, down, bias, out_sum, grad_sum, up_keep, up_send, down_keep, down_send, bias_sum
):
    step = pl.program_id(0)
    half = up_keep.shape[0]
    c0 = math.sqrt(2 / math.pi)
    c1 = c0 * 0.044715
    hidden = jnp.dot(normed[...], up[...], preferred_element_type=F32) + bias[...]
    square = hidden * hidden
    gate = 0.5 + 0.5 * jnp.tanh(hidden * (c0 + c1 * square))
    raised = hidden * gate
    slope = gate + raised * (1.0 - gate) * (2 * c0 + 6 * c1 * square)
    active = raised.astype(BF16)
    back = (((1,), (1,)), ((), ()))
    grad_active = lax.dot_general(grad_out[...], down[...], back, preferred_element_type=F32)
    grad_wide = (grad_active * slope).astype(BF16)
    out_part = jnp.dot(active, down[...], preferred_element_type=F32)
    grad_part = lax.dot_general(grad_wide, up[...], back, preferred_element_type=F32)

    @pl.when(step == 0)
    def _():
        out_sum[...] = out_part
        grad_sum[...] = grad_part

    @pl.when(step > 0)
    def _():
        out_sum[...] += out_part
        grad_sum[...] += grad_part

    bias_sum[...] = jnp.sum(grad_wide.astype(F32), axis=0, keepdims=True)
    up_keep[...] = jnp.dot(normed_turned[:half], grad_wide, preferred_element_type=F32)
    up_send[...] = jnp.dot(normed_turned[half:], grad_wide, preferred_element_type=F32).astype(BF16)
    down_keep[...] = jnp.dot(grad_turned[:half], active, preferred_element_type=F32)
    down_send[...] = jnp.dot(grad_turned[half:], active, preferred_element_type=F32).astype(BF16)


def feed_forward(normed, grad_out, normed_turned, grad_turned, up, down, bias, tile):
    count, width = normed.shape
    hidden = up.shape[1]
    half = width // 2
    fixed = lambda *shape: pl.BlockSpec(shape, lambda t: (0, 0))
    across = lambda rows: pl.BlockSpec((rows, tile), lambda t: (0, t))
    shape = jax.ShapeDtypeStruct
    return pl.pallas_call(
        mlp_kernel,
        grid=(hidden // tile,),
        in_specs=[
            fixed(count, width),
            fixed(count, width),
            fixed(width, count),
            fixed(width, count),
            across(width),
            pl.BlockSpec((tile, width), lambda t: (t, 0)),
            across(1),
        ],
        out_specs=[fixed(count, width), fixed(count, width), across(half), across(half), across(half), across(half), across(1)],
        out_shape=[
            shape((count, width), F32),
            shape((count, width), F32),
            shape((half, hidden), F32),
            shape((half, hidden), BF16),
            shape((half, hidden), F32),
            shape((half, hidden), BF16),
            shape((1, hidden), F32),
        ],
        compiler_params=pltpu.CompilerParams(vmem_limit_bytes=VMEM_LIMIT),
        cost_estimate=pl.CostEstimate(
            flops=12 * count * width * hidden,
            bytes_accessed=10 * width * hidden,
            transcendentals=count * hidden,
        ),
    )(normed, grad_out, normed_turned, grad_turned, up, down, bias)


def turn_halves(values, groups, mine):
    count, width = values.shape
    view = values.T.reshape(groups, 2, width // (2 * groups), count)
    keep = lax.dynamic_index_in_dim(view, mine, 1, keepdims=False).reshape(width // 2, count)
    send = lax.dynamic_index_in_dim(view, 1 - mine, 1, keepdims=False).reshape(width // 2, count)
    return jnp.concatenate([keep, send], axis=0)


STAGES = 4


def mlp_reduce_kernel(
    tiles,
    normed,
    grad_out,
    normed_turned,
    grad_turned,
    up0,
    up1,
    up2,
    up3,
    down0,
    down1,
    down2,
    down3,
    bias,
    out_sum,
    grad_sum,
    bias_sum,
    up_total,
    down_total,
    up_mine,
    down_mine,
    up_core,
    down_core,
    up_core_got,
    down_core_got,
    up_half,
    down_half,
    up_out,
    down_out,
    up_got,
    down_got,
    up_quarter,
    down_quarter,
    up_last,
    down_last,
    up_last_got,
    down_last_got,
    chip_full,
    chip_out,
    chip_got,
    core_sent,
    core_came,
    seq_sent,
    seq_came,
    last_sent,
    last_came,
    chip_sent,
    chip_came,
    bias_line,
):
    step = pl.program_id(0)
    seq, row = lax.axis_index("seq"), lax.axis_index("rows")
    half = normed_turned.shape[0] // 2
    x, y = lax.rem(seq, 2), lax.div(seq, 2)
    core_peer = {"rows": row + 1 - 2 * lax.rem(row, 2)}
    x_peer = {"seq": seq + 1 - 2 * x}
    y_peer = {"seq": seq + 2 - 4 * y}
    chip, core = lax.div(row, 2), lax.rem(row, 2)
    to_chip = [lax.rem(chip + k, 4) for k in range(4)]
    chip_peers = [{"rows": 2 * to_chip[k] + core} for k in range(4)]

    @pl.when(step == 0)
    def _():
        bias_line[...] = bias[...].astype(F32).reshape(1, bias.shape[0])
        barrier = pltpu.get_barrier_semaphore()
        for peer in (core_peer, x_peer, y_peer, *chip_peers[1:]):
            pl.semaphore_signal(barrier, inc=1, device_id=peer, device_id_type=pl.DeviceIdType.MESH)
        pl.semaphore_wait(barrier, 6)

    def copies(source, target, sent, came, slot, kind, device):
        return pltpu.make_async_remote_copy(
            src_ref=source.at[slot],
            dst_ref=target.at[slot],
            send_sem=sent.at[kind, slot],
            recv_sem=came.at[kind, slot],
            device_id=device,
            device_id_type=pl.DeviceIdType.MESH,
        )

    def to_core(slot):
        return (
            copies(up_core, up_core_got, core_sent, core_came, slot, 0, core_peer),
            copies(down_core, down_core_got, core_sent, core_came, slot, 1, core_peer),
        )

    def to_seq(slot):
        return (
            copies(up_out, up_got, seq_sent, seq_came, slot, 0, x_peer),
            copies(down_out, down_got, seq_sent, seq_came, slot, 1, y_peer),
        )

    def to_last(slot):
        return (
            copies(up_last, up_last_got, last_sent, last_came, slot, 0, y_peer),
            copies(down_last, down_last_got, last_sent, last_came, slot, 1, x_peer),
        )

    def to_chips(slot):
        return [
            pltpu.make_async_remote_copy(
                src_ref=chip_out.at[slot, to_chip[k]],
                dst_ref=chip_got.at[slot, k - 1],
                send_sem=chip_sent.at[k - 1, slot],
                recv_sem=chip_came.at[k - 1, slot],
                device_id=chip_peers[k],
                device_id_type=pl.DeviceIdType.MESH,
            )
            for k in range(1, 4)
        ]

    @pl.when(step >= 4)
    def _():
        slot = lax.rem(step, 2)
        for copy in to_chips(slot):
            copy.wait()
        for kind, total in enumerate((up_total, down_total)):
            value = chip_full[slot, chip, kind]
            for k in range(3):
                value = value + chip_got[slot, k, kind].astype(F32)
            total[...] = value

    @pl.when((step >= 3) & (step < tiles + 3))
    def _():
        slot = lax.rem(step + 1, 2)
        for copy in to_last(slot):
            copy.wait()
        size = half // 4
        ups = up_quarter[slot] + up_last_got[slot].astype(F32)
        downs = down_quarter[slot] + down_last_got[slot].astype(F32)
        for place in range(4):
            up_block = ups[place * size : (place + 1) * size]
            down_block = downs[:, place * 128 : (place + 1) * 128]
            chip_full[slot, place, 0] = up_block
            chip_full[slot, place, 1] = down_block
            chip_out[slot, place, 0] = up_block.astype(BF16)
            chip_out[slot, place, 1] = down_block.astype(BF16)
        for copy in to_chips(slot):
            copy.start()

    @pl.when((step >= 2) & (step < tiles + 2))
    def _():
        slot = lax.rem(step, 2)
        for copy in to_seq(slot):
            copy.wait()
        up_quarter[slot] = up_half[slot, y] + up_got[slot, y].astype(F32)
        up_last[slot] = (up_half[slot, 1 - y] + up_got[slot, 1 - y].astype(F32)).astype(BF16)
        down_quarter[slot] = down_half[slot, x] + down_got[slot, x].astype(F32)
        down_last[slot] = (down_half[slot, 1 - x] + down_got[slot, 1 - x].astype(F32)).astype(BF16)
        for copy in to_last(slot):
            copy.start()

    @pl.when((step >= 1) & (step <= tiles))
    def _():
        slot = lax.rem(step + 1, 2)
        for copy in to_core(slot):
            copy.wait()
        for other in range(2):
            kept, gone = 2 * other + x, 2 * other + 1 - x
            up_half[slot, other] = up_mine[slot, kept] + up_core_got[slot, kept].astype(F32)
            up_out[slot, other] = (up_mine[slot, gone] + up_core_got[slot, gone].astype(F32)).astype(BF16)
            kept, gone = 2 * y + other, 2 * (1 - y) + other
            down_half[slot, other] = down_mine[slot, kept] + down_core_got[slot, kept].astype(F32)
            down_out[slot, other] = (down_mine[slot, gone] + down_core_got[slot, gone].astype(F32)).astype(BF16)
        for copy in to_seq(slot):
            copy.start()

    @pl.when(step < tiles)
    def _():
        slot = lax.rem(step, 2)
        up = jnp.concatenate([up0[...], up1[...], up2[...], up3[...]], axis=1)
        down = jnp.concatenate([down0[...], down1[...], down2[...], down3[...]], axis=0)
        hidden_part = bias.shape[0] // 4
        biases = jnp.concatenate(
            [
                bias_line[:, pl.ds(pl.multiple_of(owner * hidden_part + step * 128, 128), 128)]
                for owner in range(4)
            ],
            axis=1,
        )
        c0 = math.sqrt(2 / math.pi)
        c1 = c0 * 0.044715
        hidden = jnp.dot(normed[...], up, preferred_element_type=F32) + biases
        square = hidden * hidden
        gate = 0.5 + 0.5 * jnp.tanh(hidden * (c0 + c1 * square))
        raised = hidden * gate
        slope = gate + raised * (1.0 - gate) * (2 * c0 + 6 * c1 * square)
        active = raised.astype(BF16)
        down_part = jnp.dot(grad_turned[...], active, preferred_element_type=F32)
        for owner in range(4):
            size = half // 4
            down_mine[slot, owner] = down_part[owner * size : (owner + 1) * size]
            down_core[slot, owner] = down_part[half + owner * size : half + (owner + 1) * size].astype(BF16)
        to_core(slot)[1].start()
        back = (((1,), (1,)), ((), ()))
        grad_active = lax.dot_general(grad_out[...], down, back, preferred_element_type=F32)
        grad_wide = (grad_active * slope).astype(BF16)
        up_part = jnp.dot(normed_turned[...], grad_wide, preferred_element_type=F32)
        for owner in range(4):
            columns = slice(owner * 128, (owner + 1) * 128)
            up_mine[slot, owner] = up_part[:half, columns]
            up_core[slot, owner] = up_part[half:, columns].astype(BF16)
        to_core(slot)[0].start()
        sums = jnp.sum(grad_wide.astype(F32), axis=0, keepdims=True)
        for owner in range(4):
            bias_sum[owner] = sums[:, owner * 128 : (owner + 1) * 128]
        out_part = jnp.dot(active, down, preferred_element_type=F32)
        grad_part = lax.dot_general(grad_wide, up, back, preferred_element_type=F32)

        @pl.when(step == 0)
        def _():
            out_sum[...] = out_part
            grad_sum[...] = grad_part

        @pl.when(step > 0)
        def _():
            out_sum[...] += out_part
            grad_sum[...] += grad_part


def feed_forward_reduce(normed, grad_out, normed_turned, grad_turned, up, down, bias):
    count, width = normed.shape
    hidden = up.shape[1]
    part = hidden // 4
    tiles = part // 128
    half, quarter = width // 2, width // 8
    last = tiles - 1
    shape = jax.ShapeDtypeStruct
    fixed = lambda *dims: pl.BlockSpec(dims, lambda t: (0, 0), pipeline_mode=pl.Buffered(buffer_count=1))
    result = lambda *dims: pl.BlockSpec(dims, lambda t: (0, 0))
    done = lambda t: jnp.maximum(t - STAGES, 0)

    def up_block(owner):
        return pl.BlockSpec((width, 128), lambda t: (0, owner * tiles + jnp.minimum(t, last)))

    def down_block(owner):
        return pl.BlockSpec((128, width), lambda t: (owner * tiles + jnp.minimum(t, last), 0))

    bias_block = pl.BlockSpec((4, 1, 128), lambda t: (0, 0, jnp.minimum(t, last)))
    pair = lambda dtype, *dims: pltpu.VMEM((2,) + dims, dtype)
    return pl.pallas_call(
        partial(mlp_reduce_kernel, tiles),
        grid=(tiles + STAGES,),
        in_specs=[fixed(count, width), fixed(count, width), fixed(width, count), fixed(width, count)]
        + [up_block(owner) for owner in range(4)]
        + [down_block(owner) for owner in range(4)]
        + [pl.BlockSpec((hidden,), lambda t: (0,))],
        out_specs=[
            result(count, width),
            result(count, width),
            bias_block,
            pl.BlockSpec((quarter, 128), lambda t: (0, done(t))),
            pl.BlockSpec((quarter, 128), lambda t: (0, done(t))),
        ],
        out_shape=[
            shape((count, width), F32),
            shape((count, width), F32),
            shape((4, 1, part), F32),
            shape((quarter, part), F32),
            shape((quarter, part), F32),
        ],
        scratch_shapes=[
            pair(F32, 4, half, 128),
            pair(F32, 4, quarter, 512),
            pair(BF16, 4, half, 128),
            pair(BF16, 4, quarter, 512),
            pair(BF16, 4, half, 128),
            pair(BF16, 4, quarter, 512),
            pair(F32, 2, half, 128),
            pair(F32, 2, quarter, 512),
            pair(BF16, 2, half, 128),
            pair(BF16, 2, quarter, 512),
            pair(BF16, 2, half, 128),
            pair(BF16, 2, quarter, 512),
            pair(F32, half, 128),
            pair(F32, quarter, 512),
            pair(BF16, half, 128),
            pair(BF16, quarter, 512),
            pair(BF16, half, 128),
            pair(BF16, quarter, 512),
            pair(F32, 4, 2, quarter, 128),
            pair(BF16, 4, 2, quarter, 128),
            pair(BF16, 3, 2, quarter, 128),
        ]
        + [pltpu.SemaphoreType.DMA((2, 2))] * 6
        + [pltpu.SemaphoreType.DMA((3, 2))] * 2
        + [pltpu.VMEM((1, hidden), F32)],
        compiler_params=pltpu.CompilerParams(collective_id=1, has_side_effects=True, vmem_limit_bytes=VMEM_LIMIT),
        cost_estimate=pl.CostEstimate(
            flops=12 * count * width * hidden,
            bytes_accessed=6 * width * hidden,
            transcendentals=count * hidden,
        ),
    )(normed, grad_out, normed_turned, grad_turned, up, up, up, up, down, down, down, down, bias)


def slot_column(slots):
    return lax.rem(lax.broadcasted_iota(jnp.int32, (3 * slots, 1), 0), slots)


def split_low(values):
    high = values.astype(BF16)
    rest = values - high.astype(F32)
    middle = rest.astype(BF16)
    return high, middle, (rest - middle.astype(F32)).astype(BF16)


def per_token(slot_col, seg_row, table):
    picked = (slot_col == seg_row).astype(BF16)
    return lax.dot_general(
        picked, jnp.concatenate(split_low(table), axis=0), (((0,), (0,)), ((), ())), preferred_element_type=F32
    )


def per_slot(slot_col, seg_row, values):
    slots = slot_col.shape[0] // 3
    picked = (slot_col[:slots] == seg_row).astype(BF16)
    return sum(jnp.dot(picked, part, preferred_element_type=F32) for part in split_low(values))


def normalize(values):
    center = values - jnp.mean(values, axis=-1, keepdims=True)
    inverse = lax.rsqrt(jnp.mean(center * center, axis=-1, keepdims=True) + norm_eps)
    return center * inverse, inverse


def normalize_back(normal, inverse, grad):
    return inverse * (grad - jnp.mean(grad, axis=-1, keepdims=True) - normal * jnp.mean(grad * normal, axis=-1, keepdims=True))


def after_kernel(
    seg,
    table,
    attended,
    weight,
    bias,
    out_sum,
    grad_sum,
    middle_ref,
    branch_ref,
    cotangent,
    block_out,
    grad_middle_ref,
    slot_sums,
    bias_sum,
    view_ref,
    proj_own,
    proj_low,
    heads_out,
    total,
    core_out,
    core_got,
    sent,
    came,
    kept,
    core_sent,
    core_came,
):
    step = pl.program_id(0)
    rows = pl.num_programs(0)
    width = cotangent.shape[-1]
    length = cotangent.shape[-2]
    depth, own = width // 8, width // 4
    seq, row = lax.axis_index("seq"), lax.axis_index("rows")
    core = lax.rem(row, 2)
    core_peer = {"rows": row + 1 - 2 * core}
    peers = peers_of(seq)

    @pl.when(step == 0)
    def _():
        greet([{"seq": peer} for peer in peers] + [core_peer])

    def to_peer(r, m):
        lanes = pl.ds(m * length, length)
        return send_block(
            heads_out.at[r, peers[m - 1]], view_ref.at[r, :, lanes], sent, came, r * 3 + m - 1, {"seq": peers[m - 1]}
        )

    def to_self(r):
        return pltpu.make_async_copy(heads_out.at[r, seq], view_ref.at[r, :, pl.ds(0, length)], kept.at[r])

    slot_col = slot_column(table.shape[1])
    seg_row = seg[pl.ds(step, 1), pl.ds(pl.multiple_of(seq * length, 128), length)]
    mods = per_token(slot_col, seg_row, table[0, :, 2 * width :])
    gate_a, scale_b, gate_b = (mods[:, k * width : (k + 1) * width] for k in (0, 2, 3))
    middle, branch = middle_ref[0], branch_ref[0]
    upstream = cotangent[0].astype(F32)
    normal, inverse = normalize(middle)
    grad_normed = grad_sum[...]
    grad_middle = upstream + normalize_back(normal, inverse, grad_normed * (1.0 + scale_b))
    grad_middle_ref[0] = grad_middle
    grad_branch = (grad_middle * gate_a).astype(BF16)
    grad_heads = lax.dot_general(weight[...], grad_branch, (((1,), (1,)), ((), ())), preferred_element_type=F32)
    for owner in range(4):
        heads_out[step, owner] = grad_heads[owner * own : (owner + 1) * own].astype(BF16)
    to_self(step).start()
    for m in range(1, 4):
        to_peer(step, m).start()

    part = jnp.dot(attended[0], grad_branch, preferred_element_type=F32)
    sums = jnp.sum(grad_branch.astype(F32), axis=0, keepdims=True)

    @pl.when(step == 0)
    def _():
        total[...] = part
        bias_sum[...] = sums

    @pl.when(step > 0)
    def _():
        total[...] += part
        bias_sum[...] += sums

    to_core = pltpu.make_async_remote_copy(
        src_ref=core_out,
        dst_ref=core_got,
        send_sem=core_sent,
        recv_sem=core_came,
        device_id=core_peer,
        device_id_type=pl.DeviceIdType.MESH,
    )

    @pl.when(step == rows - 1)
    def _():
        for chip in range(4):
            other = pl.multiple_of((2 * chip + 1 - core) * depth, 8)
            core_out[chip] = total[pl.ds(other, depth), :].astype(BF16)
        to_core.start()

    branch_b = out_sum[...] + bias[...].astype(F32).reshape(1, width)
    block_out[0] = (middle + gate_b * branch_b).astype(BF16)
    pieces = (grad_middle * branch, grad_normed, grad_normed * normal, upstream * branch_b)
    for k, piece in enumerate(pieces):
        slot_sums[0, :, k * width : (k + 1) * width] = per_slot(slot_col, seg_row, piece)

    @pl.when(step == rows - 1)
    def _():
        to_core.wait()
        for chip in range(4):
            mine = pl.multiple_of((2 * chip + core) * depth, 8)
            proj_low[chip] = (total[pl.ds(mine, depth), :] + core_got[chip].astype(F32)).astype(BF16)
        chip = lax.div(row, 2)
        mine = pl.multiple_of(row * depth, 8)
        proj_own[...] = total[pl.ds(mine, depth), :] + core_got[chip].astype(F32)
        for r in range(heads_out.shape[0]):
            to_self(r).wait()
            for m in range(1, 4):
                to_peer(r, m).wait()


def after_feed_forward(seg, table, attended, weight, bias, out_sum, grad_sum, middle, branch, cotangent):
    rows, length, width = cotangent.shape
    slots = table.shape[1]
    depth = width // 8
    fixed = lambda *dims: pl.BlockSpec(dims, lambda r: (0,) * len(dims))
    row = lambda *dims: pl.BlockSpec((1,) + dims, lambda r: (r, 0, 0))
    shape = jax.ShapeDtypeStruct
    return pl.pallas_call(
        after_kernel,
        grid=(rows,),
        in_specs=[
            fixed(*seg.shape),
            row(*table.shape[1:]),
            row(width, length),
            fixed(width, width),
            fixed(width),
            pl.BlockSpec((length, width), lambda r: (r, 0)),
            pl.BlockSpec((length, width), lambda r: (r, 0)),
            row(length, width),
            row(length, width),
            row(length, width),
        ],
        out_specs=[
            row(length, width),
            row(length, width),
            row(slots, 4 * width),
            fixed(1, width),
            pl.BlockSpec(memory_space=pl.ANY),
            fixed(depth, width),
            fixed(4, depth, width),
        ],
        out_shape=[
            shape((rows, length, width), BF16),
            shape((rows, length, width), F32),
            shape((rows, slots, 4 * width), F32),
            shape((1, width), F32),
            shape((rows, width // 4, 4 * length), BF16),
            shape((depth, width), F32),
            shape((4, depth, width), BF16),
        ],
        scratch_shapes=[
            pltpu.VMEM((rows, 4, width // 4, length), BF16),
            pltpu.VMEM((width, width), F32),
            pltpu.VMEM((4, depth, width), BF16),
            pltpu.VMEM((4, depth, width), BF16),
            pltpu.SemaphoreType.DMA((3 * rows,)),
            pltpu.SemaphoreType.DMA((3 * rows,)),
            pltpu.SemaphoreType.DMA((rows,)),
            pltpu.SemaphoreType.DMA,
            pltpu.SemaphoreType.DMA,
        ],
        compiler_params=pltpu.CompilerParams(vmem_limit_bytes=VMEM_LIMIT, collective_id=4, has_side_effects=True),
        cost_estimate=pl.CostEstimate(flops=8 * 10**9, bytes_accessed=3 * 10**7, transcendentals=0),
    )(seg, table, attended, weight, bias, out_sum, grad_sum, middle, branch, cotangent)


def qkv_weight_kernel(grad, normed, keep_ref, send_ref, sum_ref, total, turned):
    step = pl.program_id(0)
    chips, depth = lax.axis_size("rows") // 2, total.shape[1] // lax.axis_size("rows")
    mine = lax.rem(lax.axis_index("rows"), 2)
    part = jnp.dot(grad[0], normed[0], preferred_element_type=F32)
    sums = jnp.sum(grad[0].astype(F32), axis=1, keepdims=True)

    @pl.when(step == 0)
    def _():
        total[...] = part
        sum_ref[...] = sums

    @pl.when(step > 0)
    def _():
        total[...] += part
        sum_ref[...] += sums

    @pl.when(step == pl.num_programs(0) - 1)
    def _():
        turned[...] = total[...].T
        for chip in range(chips):
            first = pl.multiple_of((2 * chip + mine) * depth, 8)
            other = pl.multiple_of((2 * chip + 1 - mine) * depth, 8)
            keep_ref[chip] = turned[pl.ds(first, depth), :]
            send_ref[chip] = turned[pl.ds(other, depth), :].astype(BF16)


def qkv_weight_grad(grad, normed):
    rows, features, length = grad.shape
    width = normed.shape[2]
    groups = lax.axis_size("rows")
    shape = (groups // 2, width // groups, features)
    return pl.pallas_call(
        qkv_weight_kernel,
        grid=(rows,),
        in_specs=[
            pl.BlockSpec((1, features, length), lambda r: (r, 0, 0)),
            pl.BlockSpec((1, length, width), lambda r: (r, 0, 0)),
        ],
        out_specs=[
            pl.BlockSpec(shape, lambda r: (0, 0, 0)),
            pl.BlockSpec(shape, lambda r: (0, 0, 0)),
            pl.BlockSpec((features, 1), lambda r: (0, 0)),
        ],
        out_shape=[
            jax.ShapeDtypeStruct(shape, F32),
            jax.ShapeDtypeStruct(shape, BF16),
            jax.ShapeDtypeStruct((features, 1), F32),
        ],
        scratch_shapes=[pltpu.VMEM((features, width), F32), pltpu.VMEM((width, features), F32)],
        compiler_params=pltpu.CompilerParams(vmem_limit_bytes=VMEM_LIMIT),
        cost_estimate=pl.CostEstimate(
            flops=2 * rows * length * width * features,
            bytes_accessed=2 * rows * length * (width + features) + 6 * width * features // 2,
            transcendentals=0,
        ),
    )(grad, normed)


def tail_kernel(
    images,
    mod,
    weight,
    cond,
    ada_ref,
    cond_ref,
    bias_ref,
    got,
    low_mine,
    low_got,
    row_mine,
    row_got,
    cond_mine,
    cond_got,
    column_got,
    sent,
    arrived,
):
    seq_count, row_total = lax.axis_size("seq"), lax.axis_size("rows")
    seq, row = lax.axis_index("seq"), lax.axis_index("rows")
    to_seq = [lax.rem(seq + m, seq_count) for m in range(seq_count)]
    to_row = [lax.rem(row + m, row_total) for m in range(row_total)]
    barrier = pltpu.get_barrier_semaphore()
    for m in range(1, seq_count):
        pl.semaphore_signal(barrier, inc=1, device_id={"seq": to_seq[m]}, device_id_type=pl.DeviceIdType.MESH)
    for m in range(1, row_total):
        pl.semaphore_signal(barrier, inc=1, device_id={"rows": to_row[m]}, device_id_type=pl.DeviceIdType.MESH)
    pl.semaphore_wait(barrier, seq_count + row_total - 2)

    used = [0]

    def start(source, target, device):
        copy = pltpu.make_async_remote_copy(
            src_ref=source,
            dst_ref=target,
            send_sem=sent.at[used[0]],
            recv_sem=arrived.at[used[0]],
            device_id=device,
            device_id_type=pl.DeviceIdType.MESH,
        )
        used[0] += 1
        copy.start()
        return copy

    copies = [start(mod.at[to_seq[m]], got.at[m], {"seq": to_seq[m]}) for m in range(1, seq_count)]
    column_got[0] = cond[row]
    column_copies = [start(cond.at[to_row[m]], column_got.at[m], {"rows": to_row[m]}) for m in range(1, row_total)]
    total = mod[seq]
    for m, copy in enumerate(copies):
        copy.wait()
        total = total + got[m + 1]
    low = total[:images].astype(BF16)
    low_mine[...] = low
    row_mine[...] = total[images:]
    row_mine[0:1] = jnp.sum(total[:images], axis=0, keepdims=True)
    low_got[0] = low
    copies = [start(low_mine, low_got.at[m], {"rows": to_row[m]}) for m in range(1, row_total)]
    copies += [start(row_mine, row_got.at[m], {"rows": to_row[m]}) for m in range(1, row_total)]
    term = lax.dot_general(low, weight[...], (((1,), (1,)), ((), ())), preferred_element_type=F32)
    cond_mine[...] = term
    cond_copies = [start(cond_mine, cond_got.at[m], {"seq": to_seq[m]}) for m in range(1, seq_count)]
    for copy in copies:
        copy.wait()
    sums = row_mine[...]
    for m in range(1, row_total):
        sums = sums + row_got[m]
    bias_ref[seq] = sums
    copies = [start(bias_ref.at[seq], bias_ref.at[seq], {"seq": to_seq[m]}) for m in range(1, seq_count)]
    for copy in column_copies:
        copy.wait()
    gathered = jnp.concatenate([low_got[m] for m in range(row_total)], axis=0)
    columns = jnp.concatenate([column_got[m] for m in range(row_total)], axis=0)
    ada_ref[...] = lax.dot_general(columns, gathered, (((0,), (0,)), ((), ())), preferred_element_type=F32)
    for m, copy in enumerate(cond_copies):
        copy.wait()
        term = term + cond_got[m + 1]
    cond_ref[...] = term
    for copy in copies:
        copy.wait()


def finish(mod, weight, cond, images):
    seq_count, lines, columns = mod.shape
    width, depth = weight.shape[0], cond.shape[2]
    row_total = lax.axis_size("rows")
    extra = lines - images
    copies = 3 * (seq_count - 1) + 3 * (row_total - 1)
    return pl.pallas_call(
        partial(tail_kernel, images),
        in_specs=[pl.BlockSpec(memory_space=pltpu.VMEM)] * 3,
        out_specs=[pl.BlockSpec(memory_space=pltpu.VMEM)] * 3,
        out_shape=[
            jax.ShapeDtypeStruct((depth, columns), F32),
            jax.ShapeDtypeStruct((images, width), F32),
            jax.ShapeDtypeStruct((seq_count, extra, columns), F32),
        ],
        scratch_shapes=[
            pltpu.VMEM((seq_count, lines, columns), F32),
            pltpu.VMEM((images, columns), BF16),
            pltpu.VMEM((row_total, images, columns), BF16),
            pltpu.VMEM((extra, columns), F32),
            pltpu.VMEM((row_total, extra, columns), F32),
            pltpu.VMEM((images, width), F32),
            pltpu.VMEM((seq_count, images, width), F32),
            pltpu.VMEM((row_total, images, depth), BF16),
            pltpu.SemaphoreType.DMA((copies,)),
            pltpu.SemaphoreType.DMA((copies,)),
        ],
        compiler_params=pltpu.CompilerParams(collective_id=0, has_side_effects=True, vmem_limit_bytes=VMEM_LIMIT),
        cost_estimate=pl.CostEstimate(flops=10**9, bytes_accessed=10**7, transcendentals=0),
    )(mod, weight, cond)


def send_to(source, target, sent, came, device):
    return pltpu.make_async_remote_copy(
        src_ref=source,
        dst_ref=target,
        send_sem=sent,
        recv_sem=came,
        device_id=device,
        device_id_type=pl.DeviceIdType.MESH,
    )


def back_kernel(
    block,
    inner,
    scale,
    code_col,
    code_row,
    query,
    key,
    value,
    out,
    grad_out,
    lse,
    normed,
    proj_own,
    proj_low,
    down,
    seg,
    table,
    slot_sums,
    image_index,
    conditioning,
    proj_bias,
    up_bias,
    down_bias,
    tokens,
    grad_middle,
    weight,
    ada,
    grad_tokens,
    proj_ref,
    down_ref,
    ada_ref,
    cond_ref,
    ada_bias_ref,
    qv_bias_ref,
    proj_bias_ref,
    up_bias_ref,
    down_bias_ref,
    qkv_ref,
    grads,
    token_got,
    key_sum,
    value_sum,
    keys,
    values,
    total,
    spare,
    core_out,
    core_got,
    proj_got,
    seq_out,
    seq_got,
    down_out,
    down_got,
    qkv_own,
    chip_got,
    weights,
    tokens_here,
    middle_here,
    grad_here,
    features,
    image_sums,
    feature_sums,
    mod,
    got,
    lines,
    lines_got,
    low_all,
    small_core,
    small_chip,
    small_seq,
    cond_all,
    cond,
    column_got,
    piece_out,
    piece_got,
    sent,
    came,
    kept,
    load_sem,
    store_sem,
    other_sent,
    other_came,
):
    length, size = query.shape[-1], query.shape[-2]
    row, head = pl.program_id(0), pl.program_id(1)
    rows, _, heads = grads.shape[:3]
    width = normed.shape[-1]
    images, columns = mod.shape[1:]
    depth, own, local = width // 8, width // 4, length // 4
    seq, group = lax.axis_index("seq"), lax.axis_index("rows")
    chip, core = lax.div(group, 2), lax.rem(group, 2)
    seq_places = peers_of(seq)
    peers = [{"seq": place} for place in seq_places]
    row_places = [lax.rem(group + m, 8) for m in range(8)]
    row_peers = [{"rows": place} for place in row_places]
    core_peer = {"rows": group + 1 - 2 * core}
    to_chip = [lax.rem(chip + k, 4) for k in range(4)]
    from_chip = [lax.rem(chip + 4 - k, 4) for k in range(4)]
    chip_peers = [{"rows": 2 * to_chip[k] + core} for k in range(4)]
    first = (row == 0) & (head == 0)
    last = (row == rows - 1) & (head == heads - 1)
    slot_col = slot_column(table.shape[1])
    used = [0]

    def copy_to(source, target, device):
        used[0] += 1
        return send_to(source, target, other_sent.at[used[0] - 1], other_came.at[used[0] - 1], device)

    def go(copies):
        for copy in copies:
            copy.start()

    def end(copies):
        for copy in copies:
            copy.wait()

    def to_peer(r, h, m):
        place = (r * heads + h) * 3 + m - 1
        source = grads.at[r, :, h, :, pl.ds(m * local, local)]
        return send_to(source, token_got.at[r, :, seq, h], sent.at[place], came.at[place], peers[m - 1])

    def to_self(r, h):
        source = grads.at[r, :, h, :, pl.ds(0, local)]
        return pltpu.make_async_copy(source, token_got.at[r, :, seq, h], kept.at[r * heads + h])

    proj_copies = [copy_to(proj_low.at[to_chip[k]], proj_got.at[k - 1], chip_peers[k]) for k in range(1, 4)]
    seq_copies = [copy_to(seq_out.at[place], seq_got.at[m], peers[m]) for m, place in enumerate(seq_places)]
    core_copy = copy_to(core_out, core_got, core_peer)
    down_copy = copy_to(down_out.at[1 - core], down_got, core_peer)
    chip_copies = [copy_to(core_out.at[to_chip[k]], chip_got.at[k - 1], chip_peers[k]) for k in range(1, 4)]
    column_copies = [copy_to(cond.at[row_places[m]], column_got.at[group], row_peers[m]) for m in range(1, 8)]
    mod_copies = [copy_to(mod.at[place], got.at[m], peers[m]) for m, place in enumerate(seq_places)]
    line_copies = [copy_to(lines.at[place], lines_got.at[m], peers[m]) for m, place in enumerate(seq_places)]
    low_core = copy_to(low_all.at[chip, core], low_all.at[chip, core], core_peer)
    low_chips = [copy_to(low_all.at[chip, core], low_all.at[chip, core], chip_peers[k]) for k in range(1, 4)]
    low_on = [copy_to(low_all.at[from_chip[k], core], low_all.at[from_chip[k], core], core_peer) for k in range(1, 4)]
    small_over = copy_to(small_core.at[core], small_core.at[core], core_peer)
    small_chips = [copy_to(small_chip.at[chip], small_chip.at[chip], chip_peers[k]) for k in range(1, 4)]
    small_copies = [copy_to(small_seq.at[seq], small_seq.at[seq], peers[m]) for m in range(3)]
    cond_copies = [copy_to(cond_all.at[seq], cond_all.at[seq], peers[m]) for m in range(3)]
    base = used[0]

    load_weights = [
        pltpu.make_async_copy(weight.at[:, pl.ds(part * width, width)], weights.at[part], load_sem.at[part])
        for part in range(3)
    ]
    load_tokens = pltpu.make_async_copy(tokens, tokens_here, load_sem.at[3])
    load_middle = pltpu.make_async_copy(grad_middle, middle_here, load_sem.at[4])
    load_ada = [
        pltpu.make_async_copy(ada.at[pl.ds(0, width)], weights.at[0], load_sem.at[5]),
        pltpu.make_async_copy(ada.at[pl.ds(width, columns - width)], weights.at[1, pl.ds(0, columns - width)], load_sem.at[6]),
    ]

    @pl.when(first)
    def _():
        greet(peers + row_peers[1:])
        go(proj_copies)
        half = down.shape[1] // 2
        for place in range(2):
            down_out[place] = down[:, place * half : (place + 1) * half]
        down_copy.start()
        go(load_weights + [load_tokens, load_middle])
        value = conditioning[...].astype(F32)
        low = (value / (1.0 + jnp.exp(-value))).astype(BF16)
        for place in range(8):
            cond[place] = low[:, place * depth : (place + 1) * depth]
        column_got[group] = cond[group]
        go(column_copies)
        image_sums[...] = jnp.zeros_like(image_sums)
        feature_sums[...] = jnp.zeros_like(feature_sums)

    keys[...] = key[0, 0].astype(F32).T.astype(BF16)
    values[...] = value[0, 0].astype(F32).T.astype(BF16)

    def place_of(part):
        return pl.ds(pl.multiple_of((part * heads + head) * size, 8), size)

    for step in range(length // block):
        here = pl.ds(step * block, block)
        query_low = query[0, 0, :, here]
        grad_low = grad_out[0, 0, :, here]
        query_rows = query_low.astype(F32).T.astype(BF16)
        grad_rows = grad_low.astype(F32).T.astype(BF16)
        row_dot = jnp.sum(grad_low.astype(F32) * out[0, 0, :, here].astype(F32), axis=0, keepdims=True)
        grad_query = jnp.zeros((size, block), F32)
        for part in range(length // inner):
            there = pl.ds(part * inner, inner)
            scores = jnp.dot(keys[there, :], query_low, preferred_element_type=F32)
            scores = jnp.where(code_col[0, there, :] == code_row[0, :, here], scores * (scale * LOG2E), -1e30)
            probs = jnp.exp2(scores - lse[0, 0, :, here])
            grad_probs = jnp.dot(values[there, :], grad_low, preferred_element_type=F32)
            grad_raw = (probs * (grad_probs - row_dot) * scale).astype(BF16)
            value_part = jnp.dot(probs.astype(BF16), grad_rows, preferred_element_type=F32)
            key_part = jnp.dot(grad_raw, query_rows, preferred_element_type=F32)
            if step == 0:
                value_sum[there, :] = value_part
                key_sum[there, :] = key_part
            else:
                value_sum[there, :] += value_part
                key_sum[there, :] += key_part
            grad_query += jnp.dot(key[0, 0, :, there], grad_raw, preferred_element_type=F32)
        low = grad_query.astype(BF16)
        grads[row, 0, head, :, here] = low
        spare[place_of(0), here] = low.astype(F32)
    for part, sums in ((1, key_sum), (2, value_sum)):
        low = sums[...].T.astype(BF16)
        grads[row, part, head] = low
        spare[place_of(part), :] = low.astype(F32)

    to_self(row, head).start()
    for m in range(1, 4):
        to_peer(row, head, m).start()

    own_features = 3 * own

    @pl.when((head == heads - 1) & (row == 0))
    def _():
        total[...] = jnp.dot(spare[:own_features].astype(BF16), normed[0], preferred_element_type=F32)

    @pl.when((head == heads - 1) & (row > 0))
    def _():
        total[...] += jnp.dot(spare[:own_features].astype(BF16), normed[0], preferred_element_type=F32)

    def store_tokens(r):
        return pltpu.make_async_copy(grad_here.at[r], grad_tokens.at[r], store_sem.at[r])

    def input_grad(r):
        for h in range(heads):
            to_self(r, h).wait()
            for m in range(1, 4):
                to_peer(r, h, m).wait()
        grad_normed = jnp.zeros((width, local), F32)
        for part in range(3):
            for place in range(4):
                for h in range(heads):
                    start = (place * heads + h) * size
                    features[start : start + size] = token_got[r, part, place, h].astype(F32)
            low = features[...].astype(BF16)
            grad_normed += jnp.dot(weights[part], low, preferred_element_type=F32)
            if part != 1:
                lanes = slice(part * width, (part + 1) * width)
                ones = jnp.ones((8, local), BF16)
                feature_sums[:, lanes] += lax.dot_general(ones, low, (((1,), (1,)), ((), ())), preferred_element_type=F32)
        grad_normed = grad_normed.T
        normal, inverse = normalize(tokens_here[r].astype(F32))
        seg_row = seg[r : r + 1, pl.ds(pl.multiple_of(seq * local, 128), local)]
        scale_a = per_token(slot_col, seg_row, table[r, :, width : 2 * width])
        grad_here[r] = middle_here[r] + normalize_back(normal, inverse, grad_normed * (1.0 + scale_a))
        store_tokens(r).start()
        late = [per_slot(slot_col, seg_row, piece) for piece in (grad_normed, grad_normed * normal)]
        slots = jnp.concatenate(late + [slot_sums[r]], axis=1)
        pick = lax.broadcasted_iota(jnp.int32, (images, slots.shape[0]), 0) == image_index[r : r + 1, :]
        image_sums[...] += jnp.dot(pick.astype(F32), slots, precision=lax.Precision.HIGHEST, preferred_element_type=F32)

    @pl.when(last)
    def _():
        spare[:, :own_features] = total[...].T
        for place in range(4):
            other = pl.multiple_of((2 * place + 1 - core) * depth, 8)
            core_out[place] = spare[pl.ds(other, depth), :own_features].astype(BF16)
        core_copy.start()
        end(proj_copies)
        mine = proj_own[...]
        for k in range(3):
            mine = mine + proj_got[k].astype(F32)
        for place in range(4):
            seq_out[place] = mine[:, place * own : (place + 1) * own].astype(BF16)
        go(seq_copies)
        for place in range(4):

            @pl.when(seq == place)
            def _():
                proj_ref[...] = mine[:, place * own : (place + 1) * own]

        down_copy.wait()
        left, right = down_out[core], down_got[...]
        left, right = jnp.where(core == 0, left, right), jnp.where(core == 0, right, left)
        down_ref[:depth] = left
        down_ref[depth:] = right
        core_copy.wait()
        for place in range(4):
            same = pl.multiple_of((2 * place + core) * depth, 8)
            core_out[place] = (spare[pl.ds(same, depth), :own_features] + core_got[place].astype(F32)).astype(BF16)
        same = pl.multiple_of(group * depth, 8)
        qkv_own[...] = spare[pl.ds(same, depth), :own_features] + core_got[chip].astype(F32)
        go(chip_copies)

        end(load_weights + [load_tokens, load_middle])
        for r in range(rows):
            input_grad(r)
        go(load_ada)

        for place in range(4):
            mod[place] = image_sums[:, place * columns : (place + 1) * columns]
        lines[...] = jnp.zeros_like(lines)
        for line in range(8):
            if line < 2:
                value = feature_sums[0:1, 2 * line * width : (2 * line + 1) * width]
            else:
                value = (proj_bias[...], *(up_bias[k] for k in range(4)), down_bias[...])[line - 2]
            lines[line // 2, line % 2 : line % 2 + 1, :width] = value
        go(mod_copies + line_copies)
        for m, copy in enumerate(seq_copies):
            copy.wait()
            proj_ref[...] += seq_got[m].astype(F32)
        sums = mod[seq]
        for m, copy in enumerate(mod_copies):
            copy.wait()
            sums = sums + got[m]
        low = sums.astype(BF16)
        low_all[chip, core] = low
        go([low_core] + low_chips)
        small = lines[seq]
        for m, copy in enumerate(line_copies):
            copy.wait()
            small = small + lines_got[m]
        small_core[core] = small
        small_core[core, 2:3] = jnp.sum(sums, axis=0, keepdims=True)
        small_over.start()
        end(load_ada)
        term = jnp.dot(low[:, :width], weights[0], preferred_element_type=F32)
        term += jnp.dot(low[:, width:], weights[1, : columns - width], preferred_element_type=F32)
        cond_all[seq] = term
        go(cond_copies)
        end(chip_copies + column_copies)
        mine = qkv_own[...]
        for k in range(3):
            mine = mine + chip_got[k].astype(F32)
        for part in range(3):
            piece_out[part] = mine[:, part * own : (part + 1) * own]

        def piece(part):
            index = part * 4 + seq
            target, place = lax.div(index, 3), lax.rem(index, 3)
            copy = send_to(
                piece_out.at[part], piece_got.at[place], other_sent.at[base + part], other_came.at[base + place], {"seq": target}
            )
            return copy, target, place

        def arriving(place):
            source = lax.rem(3 * seq + place, 4)
            copy = send_to(
                piece_out.at[0], piece_got.at[place], other_sent.at[base], other_came.at[base + place], {"seq": source}
            )
            return copy, source

        for part in range(3):
            copy, target, place = piece(part)

            @pl.when(target != seq)
            def _():
                copy.start()

            @pl.when(target == seq)
            def _():
                piece_got[place] = piece_out[part]

        small_over.wait()
        small_chip[chip] = small_core[0] + small_core[1]
        go(small_chips)
        for came_in, going_on in zip(low_chips, low_on):
            came_in.wait()
            going_on.start()
        end(small_chips)
        small_seq[seq] = (small_chip[0] + small_chip[1]) + (small_chip[2] + small_chip[3])
        go(small_copies)
        end([low_core] + low_on)
        gathered = jnp.concatenate([low_all[m // 2, m % 2] for m in range(8)], axis=0)
        blocks = jnp.concatenate([column_got[m] for m in range(8)], axis=0)
        ada_ref[...] = lax.dot_general(blocks, gathered, (((0,), (0,)), ((), ())), preferred_element_type=F32)
        for part in range(3):
            copy, target, place = piece(part)

            @pl.when(target != seq)
            def _():
                copy.wait_send()

        for place in range(3):
            copy, source = arriving(place)

            @pl.when(source != seq)
            def _():
                copy.wait_recv()

        for place in range(3):
            qkv_ref[:, place * own : (place + 1) * own] = piece_got[place]
        end(cond_copies)
        value = conditioning[...].astype(F32)
        gate = 1.0 / (1.0 + jnp.exp(-value))
        sums = (cond_all[0] + cond_all[1]) + (cond_all[2] + cond_all[3])
        cond_ref[...] = sums * gate * (1.0 + value * (1.0 - gate))
        end(small_copies)
        for place in range(4):
            ada_bias_ref[pl.ds(place * columns, columns)] = small_seq[place, 2]
        qv_bias_ref[...] = small_seq[0, 0:2, :width]
        proj_bias_ref[...] = small_seq[1, 0, :width]
        for line in range(3, 7):
            up_bias_ref[pl.ds((line - 3) * width, width)] = small_seq[line // 2, line % 2, :width]
        down_bias_ref[...] = small_seq[3, 1, :width]
        for r in range(rows):
            store_tokens(r).wait()


def attend_back_and_finish(packed, out, grad_out, lse, col, row, normed, *rest):
    proj_own, proj_low, down, seg, table, slot_sums, image_index, conditioning, biases, tokens, grad_middle, weight, ada = rest
    rows, _, heads, size, length = packed.shape
    width = normed.shape[2]
    depth, own, features, local = width // 8, width // 4, 3 * heads * size, length // 4
    half = down.shape[1] // 2
    images, columns = conditioning.shape[0], ada.shape[0]
    part = lambda j: pl.BlockSpec((1, None, 1, size, length), lambda r, h: (r, j, h, 0, 0))
    whole = pl.BlockSpec((1, 1, size, length), lambda r, h: (r, h, 0, 0))
    single = pl.Buffered(buffer_count=1)
    fixed = lambda *dims: pl.BlockSpec(dims, lambda r, h: (0,) * len(dims), pipeline_mode=single)
    result = lambda *dims: pl.BlockSpec(dims, lambda r, h: (0,) * len(dims))
    far = pl.BlockSpec(memory_space=pl.ANY)
    shape = jax.ShapeDtypeStruct
    vmem = lambda dtype, *dims: pltpu.VMEM(dims, dtype)
    count = rows * heads
    copies = 3 + 3 + 1 + 1 + 3 + 7 + 3 + 3 + 1 + 3 + 3 + 1 + 3 + 3 + 3 + 3
    dma = lambda n: pltpu.SemaphoreType.DMA((n,))
    return pl.pallas_call(
        partial(back_kernel, 256, 512, size**-0.5),
        grid=(rows, heads),
        in_specs=[
            pl.BlockSpec((1, length, 1), lambda r, h: (r, 0, 0)),
            pl.BlockSpec((1, 1, length), lambda r, h: (r, 0, 0)),
            part(0),
            part(1),
            part(2),
            whole,
            whole,
            pl.BlockSpec((1, 1, 1, length), lambda r, h: (r, h, 0, 0)),
            pl.BlockSpec((1, length, width), lambda r, h: (r, 0, 0), pipeline_mode=single),
            fixed(depth, width),
            fixed(4, depth, width),
            fixed(depth, 2 * half),
            fixed(*seg.shape),
            fixed(*table.shape),
            fixed(*slot_sums.shape),
            fixed(*image_index.shape),
            fixed(images, width),
            fixed(1, width),
            fixed(4, 1, width),
            fixed(1, width),
            far,
            far,
            far,
            far,
        ],
        out_specs=[
            far,
            result(depth, own),
            result(own, half),
            result(depth, columns),
            result(images, width),
            result(4 * columns),
            result(2, width),
            result(width),
            result(4 * width),
            result(width),
            result(depth, features),
        ],
        out_shape=[
            shape((rows, local, width), F32),
            shape((depth, own), F32),
            shape((own, half), F32),
            shape((depth, columns), F32),
            shape((images, width), F32),
            shape((4 * columns,), F32),
            shape((2, width), F32),
            shape((width,), F32),
            shape((4 * width,), F32),
            shape((width,), F32),
            shape((depth, features), F32),
        ],
        scratch_shapes=[
            vmem(BF16, rows, 3, heads, size, length),
            vmem(BF16, rows, 3, 4, heads, size, local),
            vmem(F32, length, size),
            vmem(F32, length, size),
            vmem(BF16, length, size),
            vmem(BF16, length, size),
            vmem(F32, features, width),
            vmem(F32, width, length),
            vmem(BF16, 4, depth, features),
            vmem(BF16, 4, depth, features),
            vmem(BF16, 3, depth, width),
            vmem(BF16, 4, depth, own),
            vmem(BF16, 3, depth, own),
            vmem(F32, 2, depth, half),
            vmem(F32, depth, half),
            vmem(F32, depth, features),
            vmem(BF16, 3, depth, features),
            vmem(BF16, 3, width, width),
            vmem(BF16, rows, local, width),
            vmem(F32, rows, local, width),
            vmem(F32, rows, local, width),
            vmem(F32, width, local),
            vmem(F32, images, 6 * width),
            vmem(F32, 8, 3 * width),
            vmem(F32, 4, images, columns),
            vmem(F32, 3, images, columns),
            vmem(F32, 4, 8, columns),
            vmem(F32, 3, 8, columns),
            vmem(BF16, 4, 2, images, columns),
            vmem(F32, 2, 8, columns),
            vmem(F32, 4, 8, columns),
            vmem(F32, 4, 8, columns),
            vmem(F32, 4, images, width),
            vmem(BF16, 8, images, depth),
            vmem(BF16, 8, images, depth),
            vmem(F32, 3, depth, own),
            vmem(F32, 3, depth, own),
            dma(3 * count),
            dma(3 * count),
            dma(count),
            dma(7),
            dma(rows),
            dma(copies),
            dma(copies),
        ],
        compiler_params=pltpu.CompilerParams(vmem_limit_bytes=VMEM_LIMIT, collective_id=3, has_side_effects=True),
        cost_estimate=pl.CostEstimate(
            flops=20 * rows * heads * length * length * 128,
            bytes_accessed=16 * rows * heads * length * size,
            transcendentals=rows * heads * length * length,
        ),
    )(
        col,
        row,
        packed,
        packed,
        packed,
        out,
        grad_out,
        lse,
        normed,
        proj_own,
        proj_low,
        down,
        seg,
        table,
        slot_sums,
        image_index,
        conditioning,
        *biases,
        tokens,
        grad_middle,
        weight,
        ada,
    )


def forward_kernel(
    block,
    image_index,
    seg,
    fill,
    conditioning,
    ada_bias,
    qv_bias,
    proj_bias,
    tokens,
    ada,
    weight,
    proj,
    cotangent,
    normed_ref,
    packed_ref,
    attended_ref,
    features_ref,
    branch_ref,
    middle_ref,
    inner_ref,
    grad_ref,
    inner_turned_ref,
    grad_turned_ref,
    table_ref,
    code_row,
    code_col,
    lse_ref,
    bias_sum,
    here,
    normed_all,
    packed_all,
    ada_here,
    windows,
    turned,
    own_weight,
    bias_turned,
    mod_all,
    table,
    seg_all,
    attended_all,
    attended_got,
    flat,
    features_all,
    proj_here,
    cotangent_here,
    branch_all,
    middle_all,
    inner_all,
    grad_all,
    inner_turned,
    grad_turned,
    rows_turned,
    load_sem,
    own_sem,
    mod_sent,
    mod_came,
    sent,
    came,
    forward_sent,
    forward_came,
    heads_sent,
    heads_came,
    heads_kept,
    store_sem,
    last_sem,
):
    rows, _, local, width = here.shape
    _, parts, heads, size, length = packed_all.shape
    own, depth, half = heads * size, width // 8, local // 2
    columns = ada_here.shape[0]
    images, slots = conditioning.shape[0], image_index.shape[1]
    slot_col = slot_column(slots)
    scale = size**-0.5 * LOG2E
    seq = lax.axis_index("seq")
    core = lax.rem(lax.axis_index("rows"), 2)
    places = [seq] + peers_of(seq)
    peers = [{"seq": place} for place in places]

    greet(peers[1:])

    def direct(r, m):
        index = r * 2 + m - 1
        return send_to(tokens.at[r], here.at[r, m], sent.at[index], came.at[index], peers[m])

    def forward(r, m):
        part = pl.ds(0, half) if m == 1 else pl.ds(half, half)
        index = r * 2 + m - 1
        return send_to(
            here.at[r, 3 - m, part], here.at[r, 3, part], forward_sent.at[index], forward_came.at[index], peers[m]
        )

    def go(copies):
        for copy in copies:
            copy.start()

    def end(copies):
        for copy in copies:
            copy.wait()

    go([direct(0, m) for m in (1, 2)])
    own_copies = [pltpu.make_async_copy(tokens.at[r], here.at[r, 0], own_sem.at[r]) for r in range(rows)]
    load_ada = pltpu.make_async_copy(ada, ada_here, load_sem.at[0])
    load_windows = []
    for part in range(3):
        lanes = pl.ds(pl.multiple_of(part * width + seq * 256, 128), 384)
        load_windows.append(pltpu.make_async_copy(weight.at[:, lanes], windows.at[part], load_sem.at[1 + part]))
    load_proj = pltpu.make_async_copy(proj, proj_here, load_sem.at[4])
    load_cotangent = pltpu.make_async_copy(cotangent, cotangent_here, load_sem.at[5])
    go([load_ada] + load_windows + own_copies + [load_proj, load_cotangent])

    value = conditioning[...].astype(F32)
    low = (value / (1.0 + jnp.exp(-value))).astype(BF16)
    load_ada.wait()
    mod_all[seq] = lax.dot_general(low, ada_here[...], (((1,), (1,)), ((), ())), preferred_element_type=F32)
    mod_copies = [
        send_to(mod_all.at[seq], mod_all.at[seq], mod_sent.at[m - 1], mod_came.at[m - 1], peers[m]) for m in range(1, 4)
    ]
    go(mod_copies)

    for m in range(4):
        lanes = pl.ds(pl.multiple_of(places[m] * local, 128), local)
        found = seg[:, lanes]
        where = places[m] * local + lax.broadcasted_iota(jnp.int32, (1, local), 1)
        for r in range(rows):
            code = jnp.where(where < fill[r], found[r : r + 1], -1 - where)
            seg_all[r, m] = found[r : r + 1]
            code_row[r, :, m * local : (m + 1) * local] = code
            column = jnp.broadcast_to(code.astype(F32), (128, local)).T[:, :1]
            code_col[r, m * local : (m + 1) * local] = column.astype(jnp.int32)

    for part in range(3):
        load_windows[part].wait()
        turned[...] = windows[part].astype(F32).T
        own_weight[part * own : (part + 1) * own] = turned[pl.ds(pl.multiple_of(seq * 32, 8), own), :].astype(BF16)
    window = qv_bias[:, pl.ds(pl.multiple_of(seq * 256, 128), 384)].astype(F32)
    bias_turned[...] = jnp.concatenate([window, jnp.zeros((6, 384), F32)], axis=0).T
    bias = bias_turned[pl.ds(pl.multiple_of(seq * 32, 8), own), :]
    bias = jnp.concatenate([bias[:, 0:1], jnp.zeros((own, 1), F32), bias[:, 1:2]], axis=0)

    end([direct(0, m) for m in (1, 2)])
    go([forward(0, m) for m in (1, 2)] + [direct(1, m) for m in (1, 2)])

    end(mod_copies)
    bias_all = ada_bias[...].astype(F32).reshape(1, 4 * columns)
    proj_line = proj_bias[...].astype(F32).reshape(1, width)
    for place in range(4):
        lanes = slice(place * columns, (place + 1) * columns)
        table[:, lanes] = mod_all[place] + bias_all[:, lanes]
    stacked = jnp.concatenate(split_low(table[...]), axis=0)
    image_col = lax.rem(lax.broadcasted_iota(jnp.int32, (3 * images, slots), 0), images)
    for r in range(rows):
        picked = (image_col == image_index[r : r + 1]).astype(BF16)
        table_ref[r] = lax.dot_general(picked, stacked, (((0,), (0,)), ((), ())), preferred_element_type=F32)

    def stores(r, m):
        index = r * 4 + m
        lanes = pl.ds(m * local, local)
        return (
            pltpu.make_async_copy(normed_all.at[r, m], normed_ref.at[r, m], store_sem.at[0, index]),
            pltpu.make_async_copy(packed_all.at[r, :, :, :, lanes], packed_ref.at[r, :, :, :, lanes], store_sem.at[1, index]),
        )

    def work(r, m):
        mods = per_token(slot_col, seg_all[r, m], table_ref[r, :, : 2 * width])
        normal, _ = normalize(here[r, m].astype(F32))
        normed = (normal * (1.0 + mods[:, width:]) + mods[:, :width]).astype(BF16)
        normed_all[r, m] = normed
        mixed = lax.dot_general(own_weight[...], normed, (((1,), (1,)), ((), ())), preferred_element_type=F32)
        mixed = (mixed + bias).astype(BF16)
        for part in range(parts):
            for head in range(heads):
                start = (part * heads + head) * size
                packed_all[r, part, head, :, m * local : (m + 1) * local] = mixed[start : start + size]
        go(stores(r, m))

    def to_peer(r, h, m):
        source = attended_all.at[r, h, :, pl.ds(m * local, local)]
        place = (r * heads + h) * 3 + m - 1
        return send_to(source, attended_got.at[r, seq, h], heads_sent.at[place], heads_came.at[place], peers[m])

    def to_self(r, h):
        source = attended_all.at[r, h, :, pl.ds(0, local)]
        return pltpu.make_async_copy(source, attended_got.at[r, seq, h], heads_kept.at[r * heads + h])

    def attend_head(r, h):
        keys = packed_all[r, 1, h].astype(F32).T.astype(BF16)
        values = packed_all[r, 2, h]
        codes = code_col[r]
        for step in range(length // block):
            lanes = pl.ds(step * block, block)
            scores = jnp.dot(keys, packed_all[r, 0, h, :, lanes], preferred_element_type=F32)
            scores = jnp.where(codes == code_row[r, :, lanes], scores * scale, -1e30)
            peak = jnp.max(scores, axis=0, keepdims=True)
            raised = jnp.exp2(scores - peak)
            total = jnp.sum(raised, axis=0, keepdims=True)
            probs = (raised * (1.0 / total)).astype(BF16)
            attended_all[r, h, :, lanes] = jnp.dot(values, probs, preferred_element_type=F32).astype(BF16)
            lse_ref[r, h, :, lanes] = peak + jnp.log2(total)
        to_self(r, h).start()
        for m in range(1, 4):
            to_peer(r, h, m).start()

    def attend_row(r, first, last):
        @pl.loop(first, last)
        def _(h):
            attend_head(r, h)

    end(own_copies)
    for m in range(3):
        work(0, m)
    end([forward(0, m) for m in (1, 2)])
    work(0, 3)
    attend_row(0, 0, heads // 2)
    end([direct(1, m) for m in (1, 2)])
    go([forward(1, m) for m in (1, 2)])
    attend_row(0, heads // 2, heads)
    for m in range(3):
        work(1, m)
    end([forward(1, m) for m in (1, 2)])
    work(1, 3)
    attend_row(1, 0, heads)
    end([load_proj, load_cotangent])

    def last_stores(r):
        lines, lanes = pl.ds(r * local, local), pl.ds(r * local, local)
        pairs = (
            (attended_all.at[r], attended_ref.at[r]),
            (features_all.at[r], features_ref.at[r]),
            (branch_all.at[r], branch_ref.at[r]),
            (middle_all.at[r], middle_ref.at[r]),
            (inner_all.at[r], inner_ref.at[lines]),
            (grad_all.at[r], grad_ref.at[lines]),
            (inner_turned.at[r], inner_turned_ref.at[:, lanes]),
            (grad_turned.at[r], grad_turned_ref.at[:, lanes]),
        )
        return [pltpu.make_async_copy(source, target, last_sem.at[r, k]) for k, (source, target) in enumerate(pairs)]

    for r in range(rows):
        for h in range(heads):
            to_self(r, h).wait()
            for m in range(1, 4):
                to_peer(r, h, m).wait()
        for place in range(4):
            for h in range(heads):
                start = (place * heads + h) * size
                flat[start : start + size] = attended_got[r, place, h].astype(F32)
        features = flat[...].astype(BF16)
        features_all[r] = features
        mods = per_token(slot_col, seg_all[r, 0], table_ref[r, :, 2 * width :])
        gate_a, shift_b, scale_b, gate_b = (mods[:, k * width : (k + 1) * width] for k in range(4))
        branch = lax.dot_general(features, proj_here[...], (((0,), (0,)), ((), ())), preferred_element_type=F32) + proj_line
        middle = here[r, 0].astype(F32) + gate_a * branch
        branch_all[r] = branch
        middle_all[r] = middle
        normed = normalize(middle)[0] * (1.0 + scale_b) + shift_b
        grad = cotangent_here[r].astype(F32) * gate_b
        inner_all[r] = normed.astype(BF16)
        grad_all[r] = grad.astype(BF16)
        for values, target in ((normed, inner_turned), (grad, grad_turned)):
            rows_turned[...] = values.T
            for place in range(4):
                for order in range(2):
                    first = pl.multiple_of((2 * place + (core if order == 0 else 1 - core)) * depth, 8)
                    start = (4 * order + place) * depth
                    target[r, start : start + depth] = rows_turned[pl.ds(first, depth), :].astype(BF16)
        sums = jnp.sum(grad.astype(BF16).astype(F32), axis=0, keepdims=True)
        if r == 0:
            bias_sum[...] = sums
        else:
            bias_sum[...] += sums
        go(last_stores(r))
    for r in range(rows):
        for m in range(4):
            end(stores(r, m))
        end(last_stores(r))


def before_feed_forward(image_index, seg, fill, conditioning, ada_bias, qv_bias, proj_bias, tokens, ada, weight, proj, cotangent):
    rows, local, width = tokens.shape
    length = 4 * local
    images, slots = conditioning.shape[0], image_index.shape[1]
    heads, size = HEADS // 4, width // HEADS
    columns = ada.shape[0]
    shape = jax.ShapeDtypeStruct
    vmem = lambda dtype, *dims: pltpu.VMEM(dims, dtype)
    near, far = pl.BlockSpec(memory_space=pltpu.VMEM), pl.BlockSpec(memory_space=pl.ANY)
    dma = lambda *dims: pltpu.SemaphoreType.DMA(dims)
    return pl.pallas_call(
        partial(forward_kernel, 512),
        in_specs=[near] * 2 + [pl.BlockSpec(memory_space=pltpu.SMEM)] + [near] * 4 + [far] * 5,
        out_specs=[far] * 10 + [near] * 5,
        out_shape=[
            shape((rows, 4, local, width), BF16),
            shape((rows, 3, heads, size, length), BF16),
            shape((rows, heads, size, length), BF16),
            shape((rows, width, local), BF16),
            shape((rows, local, width), F32),
            shape((rows, local, width), F32),
            shape((rows * local, width), BF16),
            shape((rows * local, width), BF16),
            shape((width, rows * local), BF16),
            shape((width, rows * local), BF16),
            shape((rows, slots, 6 * width), F32),
            shape((rows, 1, length), jnp.int32),
            shape((rows, length, 1), jnp.int32),
            shape((rows, heads, 1, length), F32),
            shape((1, width), F32),
        ],
        scratch_shapes=[
            vmem(BF16, rows, 4, local, width),
            vmem(BF16, rows, 4, local, width),
            vmem(BF16, rows, 3, heads, size, length),
            vmem(BF16, columns, width),
            vmem(BF16, 3, width, 384),
            vmem(F32, 384, width),
            vmem(BF16, 3 * heads * size, width),
            vmem(F32, 384, 8),
            vmem(F32, 4, images, columns),
            vmem(F32, images, 6 * width),
            vmem(jnp.int32, rows, 4, 1, local),
            vmem(BF16, rows, heads, size, length),
            vmem(BF16, rows, 4, heads, size, local),
            vmem(F32, width, local),
            vmem(BF16, rows, width, local),
            vmem(BF16, width, width),
            vmem(BF16, rows, local, width),
            vmem(F32, rows, local, width),
            vmem(F32, rows, local, width),
            vmem(BF16, rows, local, width),
            vmem(BF16, rows, local, width),
            vmem(BF16, rows, width, local),
            vmem(BF16, rows, width, local),
            vmem(F32, width, local),
            dma(6),
            dma(rows),
            dma(3),
            dma(3),
            dma(2 * rows),
            dma(2 * rows),
            dma(2 * rows),
            dma(2 * rows),
            dma(3 * rows * heads),
            dma(3 * rows * heads),
            dma(rows * heads),
            dma(2, 4 * rows),
            dma(rows, 8),
        ],
        compiler_params=pltpu.CompilerParams(vmem_limit_bytes=VMEM_LIMIT, collective_id=6, has_side_effects=True),
        cost_estimate=pl.CostEstimate(flops=2 * 10**10, bytes_accessed=4 * 10**7, transcendentals=0),
    )(image_index, seg, fill, conditioning, ada_bias, qv_bias, proj_bias, tokens, ada, weight, proj, cotangent)


def gather_seq(values):
    count = lax.axis_size("seq")
    if count == 4:
        first, second = swap(values, "seq", 1), swap(values, "seq", 2)
        half = values.shape[0] // 2
        third = jnp.concatenate([swap(second[:half], "seq", 1), swap(first[half:], "seq", 2)], axis=0)
        return [values, first, second, third]
    return [values] + [swap(values, "seq", m) for m in range(1, count)]


def exchange_seq(blocks):
    return [blocks[0]] + [swap(blocks[m], "seq", m) for m in range(1, len(blocks))]


def in_order(blocks, axis):
    index = lax.axis_index("seq")
    stacked = jnp.stack(blocks, axis=axis)
    return flip_blocks(stacked, axis, index)


class Halving:
    def __init__(self, blocks, low_first):
        self.blocks = dict(enumerate(blocks))
        bits = [1 << k for k in range(len(blocks).bit_length() - 1)]
        self.bits = bits if low_first else bits[::-1]

    def send(self):
        self.bit = self.bits.pop(0)
        self.kept = [m for m in self.blocks if not m & self.bit]
        return jnp.stack([self.blocks[m | self.bit] for m in self.kept]).astype(BF16)

    def move(self, sent):
        return swap(sent, "seq", self.bit)

    def add(self, came):
        self.blocks = {m: self.blocks[m] + came[k].astype(F32) for k, m in enumerate(self.kept)}


class Spreading:
    def __init__(self, pick):
        chip, chips = lax.axis_index("rows") // 2, lax.axis_size("rows") // 2
        self.own = pick(chip)
        self.sent = [pick(chip ^ m).astype(BF16) for m in range(1, chips)]

    def move(self):
        self.came = [swap(block, "rows", 2 * (m + 1)) for m, block in enumerate(self.sent)]

    def total(self):
        total = self.own
        for block in self.came:
            total = total + block.astype(F32)
        return total


def columns_of(values, index, size):
    return lax.dynamic_slice_in_dim(values, index * size, size, values.ndim - 1)


def lines_of(values, index, size):
    return lax.dynamic_slice_in_dim(values, index * size, size, 0)


def tied(*values):
    return lax.optimization_barrier(values)


def on_square(
    tokens,
    conditioning,
    segment_ids,
    image_index,
    row_fill,
    ada_weight,
    ada_bias,
    qkv_weight,
    qv_bias,
    proj_weight,
    proj_bias,
    up_weight,
    up_bias,
    down_weight,
    down_bias,
    cotangent,
):
    row_count, local_len, width = tokens.shape
    seq_count, groups = lax.axis_size("seq"), lax.axis_size("rows")
    seq_index, row_index = lax.axis_index("seq"), lax.axis_index("rows")
    chips, core = groups // 2, row_index % 2
    full_len = local_len * seq_count
    token_count = row_count * local_len
    heads_dev = HEADS // seq_count
    head_size = width // HEADS
    own = heads_dev * head_size
    image_count = conditioning.shape[0]
    hidden_size = up_weight.shape[1]
    depth = width // groups

    (
        normed_all,
        packed,
        attended,
        attended_tok,
        branch_a,
        middle,
        normed_b,
        grad_out,
        normed_turned,
        grad_turned,
        slot_mod,
        code_row,
        code_col,
        log_totals,
        part_down_bias,
    ) = before_feed_forward(
        image_index,
        segment_ids,
        row_fill,
        conditioning,
        ada_bias,
        qv_bias,
        proj_bias,
        tokens,
        ada_weight.T,
        qkv_weight,
        proj_weight,
        cotangent,
    )
    normed_all = normed_all.reshape(row_count, full_len, width)
    out_sum, grad_sum, part_up_bias, grad_up_weight, down_turned = feed_forward_reduce(
        normed_b, grad_out, normed_turned, grad_turned, up_weight, down_weight, up_bias
    )
    block_out, grad_middle, slot_sums, part_proj_bias, grad_view, proj_own, proj_low = after_feed_forward(
        segment_ids,
        slot_mod,
        attended_tok,
        proj_weight,
        down_bias,
        out_sum,
        grad_sum,
        middle,
        branch_a,
        cotangent,
    )
    grad_view = grad_view.reshape(row_count, heads_dev, head_size, full_len)
    (
        grad_tokens,
        grad_proj_weight,
        grad_down_weight,
        grad_ada_weight,
        grad_cond,
        grad_ada_bias,
        grad_qv_bias,
        grad_proj_bias,
        grad_up_bias,
        grad_down_bias,
        grad_qkv_weight,
    ) = attend_back_and_finish(
        packed,
        attended,
        grad_view,
        log_totals,
        code_col,
        code_row,
        normed_all,
        proj_own,
        proj_low,
        down_turned,
        segment_ids,
        slot_mod,
        slot_sums,
        image_index,
        conditioning,
        (part_proj_bias, part_up_bias, part_down_bias),
        tokens,
        grad_middle,
        qkv_weight,
        ada_weight.T,
    )
    return (
        block_out,
        grad_tokens,
        grad_cond,
        grad_ada_weight,
        grad_ada_bias,
        grad_qkv_weight,
        grad_qv_bias,
        grad_proj_weight,
        grad_proj_bias,
        grad_up_weight,
        grad_up_bias,
        grad_down_weight.T,
        grad_down_bias,
    )


def on_device(
    tokens,
    conditioning,
    segment_ids,
    image_index,
    row_fill,
    ada_weight,
    ada_bias,
    qkv_weight,
    qv_bias,
    proj_weight,
    proj_bias,
    up_weight,
    up_bias,
    down_weight,
    down_bias,
    cotangent,
):
    row_count, local_len, width = tokens.shape
    seq_count, groups = lax.axis_size("seq"), lax.axis_size("rows")
    seq_index, row_index = lax.axis_index("seq"), lax.axis_index("rows")
    chips, core = groups // 2, row_index % 2
    full_len = local_len * seq_count
    token_count = row_count * local_len
    heads_dev = HEADS // seq_count
    head_size = width // HEADS
    own = heads_dev * head_size
    image_count = conditioning.shape[0]
    hidden_size = up_weight.shape[1]
    depth = width // groups

    tokens_all = jnp.concatenate(gather_seq(tokens), axis=1)
    order = lax.iota(jnp.int32, seq_count) ^ seq_index
    seg_blocks = flip_blocks(segment_ids.reshape(row_count, seq_count, local_len), 1, seq_index)
    seg_all = seg_blocks.reshape(row_count, full_len)
    places = (order[:, None] * local_len + lax.iota(jnp.int32, local_len)).reshape(1, full_len)
    codes = jnp.where(places < row_fill[:, None], seg_all, -1 - places)
    code_col, code_row = codes[:, :, None], codes[:, None, :]

    qkv_own = jnp.concatenate(
        [lax.dynamic_slice_in_dim(qkv_weight, part * width + seq_index * own, own, 1).T for part in range(3)], axis=0
    )
    bias_own = lax.dynamic_slice_in_dim(qv_bias.astype(F32), seq_index * own, own, 1)
    bias_own = jnp.concatenate([bias_own[0], jnp.zeros((own,), F32), bias_own[1]])

    cond_wide = conditioning.astype(F32)
    cond_low = jax.nn.silu(cond_wide).astype(BF16)
    mod_part = jnp.dot(cond_low, ada_weight, preferred_element_type=F32)
    modulation = lax.all_gather(mod_part, "seq", axis=1, tiled=True) + ada_bias.astype(F32)
    cond_cols = cond_low.reshape(image_count, groups, depth).transpose(1, 0, 2)
    local_seg = lax.dynamic_slice_in_dim(segment_ids, seq_index * local_len, local_len, 1)
    slot_ids = lax.iota(jnp.int32, image_index.shape[1])
    slot_mod = jnp.take(modulation, image_index, axis=0)

    normed_all, packed = project_qkv(
        tokens_all, seg_all, slot_mod[:, :, : 2 * width], qkv_own, bias_own, heads_dev, min(256, full_len)
    )
    square = seq_count == 4 and chips == 4
    attended, log_totals, *attended_sent = attend(packed, code_col, code_row, 512, square)

    slot_pick = (local_seg[:, :, None] == slot_ids).astype(F32)
    mod_tok = jnp.einsum("rts,rse->rte", slot_pick, slot_mod, precision=lax.Precision.HIGHEST)
    shift_a, scale_a, gate_a, shift_b, scale_b, gate_b = jnp.split(mod_tok, 6, axis=-1)
    tokens_wide = tokens.astype(F32)
    upstream = cotangent.astype(F32)
    grad_branch_b = (upstream * gate_b).astype(BF16)
    part_down_bias = jnp.sum(grad_branch_b.astype(F32), axis=(0, 1))
    grad_out = grad_branch_b.reshape(token_count, width)
    grad_turned = turn_halves(grad_out, seq_count, core)

    def by_block(values):
        return [values[..., m * local_len : (m + 1) * local_len] for m in range(seq_count)]

    if square:
        attended_tok = attended_sent[0]
    else:
        attended_tok = in_order(exchange_seq(by_block(attended.reshape(row_count, own, full_len))), 1)
    attended_tok = attended_tok.reshape(row_count, width, local_len)
    branch_a = jnp.einsum(
        "rft,fe->rte", attended_tok, proj_weight, preferred_element_type=F32
    ) + proj_bias.astype(F32)
    middle = tokens_wide + gate_a * branch_a
    normed_b = modulate(middle, shift_b, scale_b).astype(BF16).reshape(token_count, width)
    normed_turned = turn_halves(normed_b, chips, core)

    if square:
        out_sum, grad_sum, part_up_bias, grad_up_weight, down_turned = feed_forward_reduce(
            normed_b, grad_out, normed_turned, grad_turned, up_weight, down_weight, up_bias.astype(F32)
        )
        part_up_bias = part_up_bias.reshape(1, hidden_size)
    else:
        out_sum, grad_sum, up_keep, up_send, down_keep, down_send, part_up_bias = feed_forward(
            normed_b, grad_out, normed_turned, grad_turned, up_weight, down_weight, up_bias.astype(F32)[None], 512
        )
        up_came, down_came = swap(up_send, "rows", 1), swap(down_send, "rows", 1)
    branch_b = out_sum.reshape(row_count, local_len, width) + down_bias.astype(F32)
    grad_normed_b = grad_sum.reshape(row_count, local_len, width)
    block_out = (middle + gate_b * branch_b).astype(BF16)
    grad_gate_b = upstream * branch_b
    _, norm_back_b = jax.vjp(modulate, middle, shift_b, scale_b)
    grad_mid_norm, grad_shift_b, grad_scale_b = norm_back_b(grad_normed_b)
    grad_middle = upstream + grad_mid_norm
    grad_branch_a = (grad_middle * gate_a).astype(BF16)
    grad_gate_a = grad_middle * branch_a
    part_proj_bias = jnp.sum(grad_branch_a.astype(F32), axis=(0, 1))
    grad_attended = jnp.einsum(
        "fe,rte->rft", proj_weight, grad_branch_a, preferred_element_type=F32
    ).astype(BF16)
    heads_blocks = [lax.dynamic_slice_in_dim(grad_attended, (seq_index ^ m) * own, own, 1) for m in range(seq_count)]
    grad_heads_in = jnp.concatenate(exchange_seq(heads_blocks), axis=2)
    grad_view = grad_heads_in.reshape(row_count, heads_dev, head_size, full_len)

    part_proj = jnp.einsum("rte,rft->ef", grad_branch_a, attended_tok, preferred_element_type=F32)
    proj_view = part_proj.reshape(seq_count, 2, depth * groups // (2 * seq_count), width)
    proj_keep = lax.dynamic_index_in_dim(proj_view, core, 1, keepdims=False)
    proj_send = lax.dynamic_index_in_dim(proj_view, 1 - core, 1, keepdims=False).astype(BF16)
    proj_came = swap(proj_send, "rows", 1).reshape(width // 2, width)
    proj_keep = proj_keep.reshape(width // 2, width)
    up_size, down_size = hidden_size // seq_count, width // (2 * seq_count)
    proj_blocks = [
        lines_of(proj_keep, seq_index ^ m, down_size) + lines_of(proj_came, seq_index ^ m, down_size).astype(F32)
        for m in range(seq_count)
    ]
    if square:
        proj_sent = [block.astype(BF16) for block in proj_blocks[1:]]
        grad_view, *proj_sent = tied(grad_view, *proj_sent)
        proj_total = proj_blocks[0]
        for m in range(1, seq_count):
            proj_total = proj_total + swap(proj_sent[m - 1], "seq", m).astype(F32)
    else:
        ups = Halving(
            [
                columns_of(up_keep, seq_index ^ m, up_size) + columns_of(up_came, seq_index ^ m, up_size).astype(F32)
                for m in range(seq_count)
            ],
            True,
        )
        downs = Halving(
            [
                jnp.concatenate(
                    [
                        lines_of(down_keep, seq_index ^ m, down_size)
                        + lines_of(down_came, seq_index ^ m, down_size).astype(F32),
                        proj_blocks[m],
                    ],
                    axis=1,
                )
                for m in range(seq_count)
            ],
            False,
        )
        up_sent, down_sent = ups.send(), downs.send()
        up_came, down_came = ups.move(up_sent), downs.move(down_sent)

    grad_heads, *grad_sent = attend_back(
        packed, attended, grad_view, log_totals, code_col, code_row, 256, 512, square
    )
    grad_own = grad_heads.reshape(row_count, 3 * own, full_len)
    if square:
        grad_flat = grad_sent[0]
    else:
        grad_blocks = exchange_seq(by_block(grad_own))
        grad_flat = in_order([block.reshape(row_count, 3, own, local_len) for block in grad_blocks], 2)
    grad_flat = grad_flat.reshape(row_count, 3 * width, local_len)

    qkv_keep, qkv_send, own_sums = qkv_weight_grad(grad_own, normed_all)
    down_part, proj_part = hidden_size // chips, width // chips
    if square:
        proj_spread = Spreading(lambda chip: columns_of(proj_total, chip, proj_part))
        grad_flat, qkv_send, *proj_spread.sent = tied(grad_flat, qkv_send, *proj_spread.sent)
        proj_spread.move()
    else:
        while ups.bits:
            ups.add(up_came)
            downs.add(down_came)
            up_came, down_came = ups.move(ups.send()), downs.move(downs.send())
        ups.add(up_came)
        downs.add(down_came)
        up_total, down_total = ups.blocks[0], downs.blocks[0][:, :hidden_size]
        proj_total = downs.blocks[0][:, hidden_size:]
        up_spread = Spreading(lambda chip: lines_of(up_total, chip, depth))
        down_spread = Spreading(
            lambda chip: jnp.concatenate(
                [columns_of(down_total, chip, down_part), columns_of(proj_total, chip, proj_part)], axis=1
            )
        )
        up_spread.move()
        down_spread.move()
    qkv_came = swap(qkv_send, "rows", 1)
    grad_normed_a = jnp.einsum("rft,df->rtd", grad_flat, qkv_weight, preferred_element_type=F32)
    _, norm_back_a = jax.vjp(modulate, tokens_wide, shift_a, scale_a)
    grad_tok_norm, grad_shift_a, grad_scale_a = norm_back_a(grad_normed_a)
    grad_tokens = grad_middle + grad_tok_norm
    grad_mod_tok = jnp.concatenate(
        [grad_shift_a, grad_scale_a, grad_gate_a, grad_shift_b, grad_scale_b, grad_gate_b], axis=-1
    )
    slot_grads = jnp.einsum("rts,rte->rse", slot_pick, grad_mod_tok, precision=lax.Precision.HIGHEST)
    image_pick = (image_index[:, :, None] == lax.iota(jnp.int32, image_count)).astype(F32)
    grad_modulation = jnp.einsum("rsi,rse->ie", image_pick, slot_grads, precision=lax.Precision.HIGHEST)

    own_sums = own_sums.reshape(3, own)
    part_qv = lax.dynamic_update_slice(
        jnp.zeros((2, width), F32), jnp.stack([own_sums[0], own_sums[2]]), (0, seq_index * own)
    )
    small = jnp.concatenate([part_qv.reshape(-1), part_proj_bias, part_up_bias[0], part_down_bias])
    columns = ada_weight.shape[1]
    lines = -(-small.size // (seq_count * columns))
    room = seq_count * columns * lines
    small = jnp.pad(small, (0, room - small.size)).reshape(seq_count, lines, columns)
    mod_view = grad_modulation.reshape(image_count, seq_count, columns).transpose(1, 0, 2)
    joined = jnp.concatenate(
        [mod_view, jnp.zeros((seq_count, 1, columns), F32), small, jnp.zeros((seq_count, 7 - lines, columns), F32)], axis=1
    )
    qkv_both = qkv_keep + qkv_came.astype(F32)
    qkv_spread = Spreading(lambda chip: lax.dynamic_index_in_dim(qkv_both, chip, 0, keepdims=False))
    joined, *qkv_spread.sent = tied(joined, *qkv_spread.sent)
    qkv_spread.move()
    if square:
        turned = jnp.concatenate([down_turned, proj_spread.total()], axis=1)
    else:
        grad_up_weight, turned = up_spread.total(), down_spread.total()
    half = down_part // 2
    cut = lambda index: jnp.concatenate(
        [columns_of(turned[:, :down_part], index, half), columns_of(turned[:, down_part:], index, proj_part // 2)], axis=1
    )
    core_keep, core_sent = cut(core), cut(1 - core)
    joined, core_sent = tied(joined, core_sent)
    core_came = swap(core_sent, "rows", 1)
    grad_ada_weight, cond_sum, bias_sums = finish(joined, ada_weight, cond_cols, image_count)
    _, silu_back = jax.vjp(jax.nn.silu, cond_wide)
    grad_cond = silu_back(cond_sum)[0]
    grad_ada_bias = bias_sums[:, 0].reshape(-1)
    small = bias_sums[:, 1 : 1 + lines].reshape(-1)
    grad_qv_bias = small[: 2 * width].reshape(2, width)
    grad_proj_bias = small[2 * width : 3 * width]
    grad_up_bias = small[3 * width : 3 * width + hidden_size]
    grad_down_bias = small[3 * width + hidden_size : 4 * width + hidden_size]

    pair = flip_blocks(jnp.stack([core_keep, core_came]), 0, core).reshape(-1, core_keep.shape[1])
    grad_down_weight, grad_proj_weight = pair[:, :half].T, pair[:, half:].T

    qkv_total = qkv_spread.total()
    pieces = []
    for place in range(3):
        pairs = [((3 * target + place) % seq_count, target) for target in range(seq_count)]
        part_of = [0] * seq_count
        for source, target in pairs:
            part_of[source] = (3 * target + place) // seq_count
        chosen = columns_of(qkv_total, jnp.array(part_of, jnp.int32)[seq_index], own)
        pieces.append(lax.ppermute(chosen, "seq", pairs))
    grad_qkv_weight = jnp.concatenate(pieces, axis=1)
    return (
        block_out,
        grad_tokens,
        grad_cond,
        grad_ada_weight,
        grad_ada_bias,
        grad_qkv_weight,
        grad_qv_bias,
        grad_proj_weight,
        grad_proj_bias,
        grad_up_weight,
        grad_up_bias,
        grad_down_weight,
        grad_down_bias,
    )


def solution(mesh):
    in_specs = (
        P("rows", "seq", None),
        P("rows", None),
        P("rows", None),
        P("rows", None),
        P("rows"),
        P(None, "seq"),
        P(),
        P(),
        P(),
        P(),
        P(),
        P(),
        P(),
        P(),
        P(),
        P("rows", "seq", None),
    )
    out_specs = (
        P("rows", "seq", None),
        P("rows", "seq", None),
        P("rows", None),
        P("rows", "seq"),
        P(),
        P("rows", "seq"),
        P(),
        P("rows", "seq"),
        P(),
        P("rows", "seq"),
        P(),
        P("rows", "seq"),
        P(),
    )
    square = mesh.shape["seq"] == 4 and mesh.shape["rows"] == 8
    return jax.shard_map(
        on_square if square else on_device, mesh=mesh, in_specs=in_specs, out_specs=out_specs, check_vma=False
    )
```

```python
from functools import partial
import math

import jax
import jax.numpy as jnp
from jax import lax
from jax.experimental import pallas as pl
from jax.experimental.pallas import tpu as pltpu
from jax.sharding import PartitionSpec as P

HEADS = 16
LOG2E = math.log2(math.e)
VMEM_LIMIT = 60 << 20
BF16 = jnp.bfloat16
F32 = jnp.float32

norm_eps = 1e-06


def modulate(values, offset, factor):
    center = values - jnp.mean(values, axis=-1, keepdims=True)
    spread = jnp.mean(center * center, axis=-1, keepdims=True)
    return center * lax.rsqrt(spread + norm_eps) * (1.0 + factor) + offset


def gelu_tanh(values):
    return jax.nn.gelu(values, approximate=True)


def swap(values, axis, mask):
    count = lax.axis_size(axis)
    return lax.ppermute(values, axis, [(i, i ^ mask) for i in range(count)])


def flip_blocks(values, axis, mask):
    return jnp.take(values, lax.iota(jnp.int32, values.shape[axis]) ^ mask, axis=axis)


def qkv_kernel(slot_row, seg, mod, tokens, weight, bias, normed_ref, qkv_ref):
    width = tokens.shape[-1]
    values = tokens[0].astype(F32)
    picked = (seg[0] == slot_row[...]).astype(BF16)
    table = mod[0]
    high = table.astype(BF16)
    rest = table - high.astype(F32)
    middle = rest.astype(BF16)
    last = (rest - middle.astype(F32)).astype(BF16)
    stacked = jnp.concatenate([high, middle, last], axis=0)
    per_token = jnp.dot(picked, stacked, preferred_element_type=F32)
    normed = modulate(values, per_token[:, :width], per_token[:, width:]).astype(BF16)
    normed_ref[0] = normed
    mixed = lax.dot_general(weight[...], normed, (((1,), (1,)), ((), ())), preferred_element_type=F32)
    mixed = (mixed + bias[...]).astype(BF16)
    _, parts, heads, size, _ = qkv_ref.shape
    for part in range(parts):
        for head in range(heads):
            start = (part * heads + head) * size
            qkv_ref[0, part, head] = mixed[start : start + size]


def project_qkv(tokens, seg, slot_mod, weight, bias, heads, block):
    rows, length, width = tokens.shape
    slots = slot_mod.shape[1]
    features = weight.shape[0]
    size = features // (3 * heads)
    slot_row = jnp.tile(lax.iota(jnp.int32, slots), 3)[None]
    return pl.pallas_call(
        qkv_kernel,
        grid=(rows, length // block),
        in_specs=[
            pl.BlockSpec((1, 3 * slots), lambda r, t: (0, 0)),
            pl.BlockSpec((1, block, 1), lambda r, t: (r, t, 0)),
            pl.BlockSpec((1, slots, 2 * width), lambda r, t: (r, 0, 0)),
            pl.BlockSpec((1, block, width), lambda r, t: (r, t, 0)),
            pl.BlockSpec((features, width), lambda r, t: (0, 0)),
            pl.BlockSpec((features, 1), lambda r, t: (0, 0)),
        ],
        out_specs=[
            pl.BlockSpec((1, block, width), lambda r, t: (r, t, 0)),
            pl.BlockSpec((1, 3, heads, size, block), lambda r, t: (r, 0, 0, 0, t)),
        ],
        out_shape=[
            jax.ShapeDtypeStruct((rows, length, width), BF16),
            jax.ShapeDtypeStruct((rows, 3, heads, size, length), BF16),
        ],
        compiler_params=pltpu.CompilerParams(vmem_limit_bytes=VMEM_LIMIT),
        cost_estimate=pl.CostEstimate(
            flops=2 * rows * length * width * features,
            bytes_accessed=2 * rows * length * (2 * width + features),
            transcendentals=0,
        ),
    )(slot_row, seg[:, :, None], slot_mod, tokens, weight, bias[:, None])


def peers_of(seq):
    x, y = lax.rem(seq, 2), lax.div(seq, 2)
    return [seq + 1 - 2 * x, seq + 2 - 4 * y, 3 - seq]


def greet(devices):
    barrier = pltpu.get_barrier_semaphore()
    for device in devices:
        pl.semaphore_signal(barrier, inc=1, device_id=device, device_id_type=pl.DeviceIdType.MESH)
    pl.semaphore_wait(barrier, len(devices))


def send_block(source, target, sent, came, index, device):
    return pltpu.make_async_remote_copy(
        src_ref=source,
        dst_ref=target,
        send_sem=sent.at[index],
        recv_sem=came.at[index],
        device_id=device,
        device_id_type=pl.DeviceIdType.MESH,
    )


def attend_kernel(block, scale, code_col, code_row, query, key, value, out_ref, lse_ref, token_ref=None, sent=None, came=None, kept=None):
    length = query.shape[-1]
    keys = key[0, 0].astype(F32).T.astype(BF16)
    values = value[0, 0]
    codes = code_col[0]
    row, head = (pl.program_id(0), pl.program_id(1)) if sent is not None else (0, 0)
    rows, heads = out_ref.shape[:2]
    if sent is not None:
        seq = lax.axis_index("seq")
        peers = peers_of(seq)
        size = length // 4

        @pl.when((row == 0) & (head == 0))
        def _():
            greet([{"seq": peer} for peer in peers])

        def to_peer(r, h, m):
            lanes = pl.ds(m * size, size)
            place = (r * heads + h) * 3 + m - 1
            return send_block(out_ref.at[r, h, :, lanes], token_ref.at[r, seq, h], sent, came, place, {"seq": peers[m - 1]})

        def to_self(r, h):
            return pltpu.make_async_copy(out_ref.at[r, h, :, pl.ds(0, size)], token_ref.at[r, seq, h], kept.at[r * heads + h])

    for step in range(length // block):
        here = pl.ds(step * block, block)
        scores = jnp.dot(keys, query[0, 0, :, here], preferred_element_type=F32)
        scores = jnp.where(codes == code_row[0, :, here], scores * scale, -1e30)
        peak = jnp.max(scores, axis=0, keepdims=True)
        raised = jnp.exp2(scores - peak)
        total = jnp.sum(raised, axis=0, keepdims=True)
        probs = (raised * (1.0 / total)).astype(BF16)
        out_ref[row, head, :, here] = jnp.dot(values, probs, preferred_element_type=F32).astype(BF16)
        lse_ref[0, 0, :, here] = peak + jnp.log2(total)

    if sent is not None:
        to_self(row, head).start()
        for m in range(1, 4):
            to_peer(row, head, m).start()

        @pl.when((row == rows - 1) & (head == heads - 1))
        def _():
            for r in range(rows):
                for h in range(heads):
                    to_self(r, h).wait()
                    for m in range(1, 4):
                        to_peer(r, h, m).wait()


def attend(packed, col, row, block, exchange):
    rows, _, heads, size, length = packed.shape
    part = lambda j: pl.BlockSpec((1, None, 1, size, length), lambda r, h: (r, j, h, 0, 0))
    out_specs = [
        pl.BlockSpec((1, 1, size, length), lambda r, h: (r, h, 0, 0)),
        pl.BlockSpec((1, 1, 1, length), lambda r, h: (r, h, 0, 0)),
    ]
    out_shape = [
        jax.ShapeDtypeStruct((rows, heads, size, length), BF16),
        jax.ShapeDtypeStruct((rows, heads, 1, length), F32),
    ]
    scratch = []
    extra = {}
    if exchange:
        out_specs[0] = pl.BlockSpec((rows, heads, size, length), lambda r, h: (0, 0, 0, 0))
        out_specs.append(pl.BlockSpec(memory_space=pl.ANY))
        out_shape.append(jax.ShapeDtypeStruct((rows, 4, heads, size, length // 4), BF16))
        count = rows * heads
        scratch = [pltpu.SemaphoreType.DMA((3 * count,)), pltpu.SemaphoreType.DMA((3 * count,)), pltpu.SemaphoreType.DMA((count,))]
        extra = dict(collective_id=2, has_side_effects=True)
    return pl.pallas_call(
        partial(attend_kernel, block, size**-0.5 * LOG2E),
        grid=(rows, heads),
        in_specs=[
            pl.BlockSpec((1, length, 1), lambda r, h: (r, 0, 0)),
            pl.BlockSpec((1, 1, length), lambda r, h: (r, 0, 0)),
            part(0),
            part(1),
            part(2),
        ],
        out_specs=out_specs,
        out_shape=out_shape,
        scratch_shapes=scratch,
        compiler_params=pltpu.CompilerParams(vmem_limit_bytes=VMEM_LIMIT, **extra),
        cost_estimate=pl.CostEstimate(
            flops=8 * rows * heads * length * length * 128,
            bytes_accessed=8 * rows * heads * length * size,
            transcendentals=rows * heads * length * length,
        ),
    )(col, row, packed, packed, packed)


def attend_back_kernel(
    block,
    inner,
    scale,
    exchange,
    code_col,
    code_row,
    query,
    key,
    value,
    out,
    grad_out,
    lse,
    grad_ref,
    *rest,
):
    length = query.shape[-1]
    size = query.shape[-2]
    row, head = (pl.program_id(0), pl.program_id(1)) if exchange else (0, 0)
    rows, _, heads = grad_ref.shape[:3]
    if exchange:
        token_ref, key_sum, value_sum, keys, values, sent, came, kept = rest
        seq = lax.axis_index("seq")
        peers = peers_of(seq)
        local = length // 4

        @pl.when((row == 0) & (head == 0))
        def _():
            greet([{"seq": peer} for peer in peers])

        def to_peer(r, h, m):
            lanes = pl.ds(m * local, local)
            place = (r * heads + h) * 3 + m - 1
            return send_block(grad_ref.at[r, :, h, :, lanes], token_ref.at[r, :, seq, h], sent, came, place, {"seq": peers[m - 1]})

        def to_self(r, h):
            lanes = pl.ds(0, local)
            return pltpu.make_async_copy(grad_ref.at[r, :, h, :, lanes], token_ref.at[r, :, seq, h], kept.at[r * heads + h])

    else:
        key_sum, value_sum, keys, values = rest
    keys[...] = key[0, 0].astype(F32).T.astype(BF16)
    values[...] = value[0, 0].astype(F32).T.astype(BF16)
    for step in range(length // block):
        here = pl.ds(step * block, block)
        query_low = query[0, 0, :, here]
        grad_low = grad_out[0, 0, :, here]
        query_rows = query_low.astype(F32).T.astype(BF16)
        grad_rows = grad_low.astype(F32).T.astype(BF16)
        row_dot = jnp.sum(grad_low.astype(F32) * out[0, 0, :, here].astype(F32), axis=0, keepdims=True)
        grad_query = jnp.zeros((size, block), F32)
        for part in range(length // inner):
            there = pl.ds(part * inner, inner)
            scores = jnp.dot(keys[there, :], query_low, preferred_element_type=F32)
            scores = jnp.where(code_col[0, there, :] == code_row[0, :, here], scores * (scale * LOG2E), -1e30)
            probs = jnp.exp2(scores - lse[0, 0, :, here])
            grad_probs = jnp.dot(values[there, :], grad_low, preferred_element_type=F32)
            grad_raw = (probs * (grad_probs - row_dot) * scale).astype(BF16)
            value_part = jnp.dot(probs.astype(BF16), grad_rows, preferred_element_type=F32)
            key_part = jnp.dot(grad_raw, query_rows, preferred_element_type=F32)
            if step == 0:
                value_sum[there, :] = value_part
                key_sum[there, :] = key_part
            else:
                value_sum[there, :] += value_part
                key_sum[there, :] += key_part
            grad_query += jnp.dot(key[0, 0, :, there], grad_raw, preferred_element_type=F32)
        grad_ref[row, 0, head, :, here] = grad_query.astype(BF16)
    grad_ref[row, 1, head] = key_sum[...].T.astype(BF16)
    grad_ref[row, 2, head] = value_sum[...].T.astype(BF16)

    if exchange:
        to_self(row, head).start()
        for m in range(1, 4):
            to_peer(row, head, m).start()

        @pl.when((row == rows - 1) & (head == heads - 1))
        def _():
            for r in range(rows):
                for h in range(heads):
                    to_self(r, h).wait()
                    for m in range(1, 4):
                        to_peer(r, h, m).wait()


def attend_back(packed, out, grad_out, lse, col, row, block, inner, exchange):
    rows, _, heads, size, length = packed.shape
    part = lambda j: pl.BlockSpec((1, None, 1, size, length), lambda r, h: (r, j, h, 0, 0))
    whole = pl.BlockSpec((1, 1, size, length), lambda r, h: (r, h, 0, 0))
    out_specs = [pl.BlockSpec((1, 3, 1, size, length), lambda r, h: (r, 0, h, 0, 0))]
    out_shape = [jax.ShapeDtypeStruct((rows, 3, heads, size, length), BF16)]
    scratch = []
    extra = {}
    if exchange:
        out_specs = [
            pl.BlockSpec((rows, 3, heads, size, length), lambda r, h: (0, 0, 0, 0, 0)),
            pl.BlockSpec(memory_space=pl.ANY),
        ]
        out_shape.append(jax.ShapeDtypeStruct((rows, 3, 4, heads, size, length // 4), BF16))
        count = rows * heads
        scratch = [pltpu.SemaphoreType.DMA((3 * count,)), pltpu.SemaphoreType.DMA((3 * count,)), pltpu.SemaphoreType.DMA((count,))]
        extra = dict(collective_id=3, has_side_effects=True)
    return pl.pallas_call(
        partial(attend_back_kernel, block, inner, size**-0.5, exchange),
        grid=(rows, heads),
        in_specs=[
            pl.BlockSpec((1, length, 1), lambda r, h: (r, 0, 0)),
            pl.BlockSpec((1, 1, length), lambda r, h: (r, 0, 0)),
            part(0),
            part(1),
            part(2),
            whole,
            whole,
            pl.BlockSpec((1, 1, 1, length), lambda r, h: (r, h, 0, 0)),
        ],
        out_specs=out_specs,
        out_shape=out_shape,
        scratch_shapes=[
            pltpu.VMEM((length, size), F32),
            pltpu.VMEM((length, size), F32),
            pltpu.VMEM((length, size), BF16),
            pltpu.VMEM((length, size), BF16),
        ]
        + scratch,
        compiler_params=pltpu.CompilerParams(vmem_limit_bytes=VMEM_LIMIT, **extra),
        cost_estimate=pl.CostEstimate(
            flops=20 * rows * heads * length * length * 128,
            bytes_accessed=16 * rows * heads * length * size,
            transcendentals=rows * heads * length * length,
        ),
    )(col, row, packed, packed, packed, out, grad_out, lse)


def mlp_kernel(
    normed, grad_out, normed_turned, grad_turned, up, down, bias, out_sum, grad_sum, up_keep, up_send, down_keep, down_send, bias_sum
):
    step = pl.program_id(0)
    half = up_keep.shape[0]
    c0 = math.sqrt(2 / math.pi)
    c1 = c0 * 0.044715
    hidden = jnp.dot(normed[...], up[...], preferred_element_type=F32) + bias[...]
    square = hidden * hidden
    gate = 0.5 + 0.5 * jnp.tanh(hidden * (c0 + c1 * square))
    raised = hidden * gate
    slope = gate + raised * (1.0 - gate) * (2 * c0 + 6 * c1 * square)
    active = raised.astype(BF16)
    back = (((1,), (1,)), ((), ()))
    grad_active = lax.dot_general(grad_out[...], down[...], back, preferred_element_type=F32)
    grad_wide = (grad_active * slope).astype(BF16)
    out_part = jnp.dot(active, down[...], preferred_element_type=F32)
    grad_part = lax.dot_general(grad_wide, up[...], back, preferred_element_type=F32)

    @pl.when(step == 0)
    def _():
        out_sum[...] = out_part
        grad_sum[...] = grad_part

    @pl.when(step > 0)
    def _():
        out_sum[...] += out_part
        grad_sum[...] += grad_part

    bias_sum[...] = jnp.sum(grad_wide.astype(F32), axis=0, keepdims=True)
    up_keep[...] = jnp.dot(normed_turned[:half], grad_wide, preferred_element_type=F32)
    up_send[...] = jnp.dot(normed_turned[half:], grad_wide, preferred_element_type=F32).astype(BF16)
    down_keep[...] = jnp.dot(grad_turned[:half], active, preferred_element_type=F32)
    down_send[...] = jnp.dot(grad_turned[half:], active, preferred_element_type=F32).astype(BF16)


def feed_forward(normed, grad_out, normed_turned, grad_turned, up, down, bias, tile):
    count, width = normed.shape
    hidden = up.shape[1]
    half = width // 2
    fixed = lambda *shape: pl.BlockSpec(shape, lambda t: (0, 0))
    across = lambda rows: pl.BlockSpec((rows, tile), lambda t: (0, t))
    shape = jax.ShapeDtypeStruct
    return pl.pallas_call(
        mlp_kernel,
        grid=(hidden // tile,),
        in_specs=[
            fixed(count, width),
            fixed(count, width),
            fixed(width, count),
            fixed(width, count),
            across(width),
            pl.BlockSpec((tile, width), lambda t: (t, 0)),
            across(1),
        ],
        out_specs=[fixed(count, width), fixed(count, width), across(half), across(half), across(half), across(half), across(1)],
        out_shape=[
            shape((count, width), F32),
            shape((count, width), F32),
            shape((half, hidden), F32),
            shape((half, hidden), BF16),
            shape((half, hidden), F32),
            shape((half, hidden), BF16),
            shape((1, hidden), F32),
        ],
        compiler_params=pltpu.CompilerParams(vmem_limit_bytes=VMEM_LIMIT),
        cost_estimate=pl.CostEstimate(
            flops=12 * count * width * hidden,
            bytes_accessed=10 * width * hidden,
            transcendentals=count * hidden,
        ),
    )(normed, grad_out, normed_turned, grad_turned, up, down, bias)


def turn_halves(values, groups, mine):
    count, width = values.shape
    view = values.T.reshape(groups, 2, width // (2 * groups), count)
    keep = lax.dynamic_index_in_dim(view, mine, 1, keepdims=False).reshape(width // 2, count)
    send = lax.dynamic_index_in_dim(view, 1 - mine, 1, keepdims=False).reshape(width // 2, count)
    return jnp.concatenate([keep, send], axis=0)


STAGES = 2


def mlp_reduce_kernel(
    tiles,
    normed,
    grad_out,
    normed_turned,
    grad_turned,
    up0,
    up1,
    up2,
    up3,
    down0,
    down1,
    down2,
    down3,
    bias,
    out_sum,
    grad_sum,
    bias_sum,
    up_total,
    down_total,
    left_full,
    left_up,
    left_up_low,
    left_down,
    left_down_low,
    up_mine,
    down_mine,
    up_core,
    down_core,
    up_core_got,
    down_core_got,
    up_half,
    down_half,
    up_out,
    down_out,
    up_got,
    down_got,
    up_quarter,
    down_quarter,
    up_last,
    down_last,
    up_last_got,
    down_last_got,
    chip_full,
    chip_out,
    chip_got,
    core_sent,
    core_came,
    seq_sent,
    seq_came,
    last_sent,
    last_came,
    chip_sent,
    chip_came,
    bias_line,
):
    step = pl.program_id(0)
    seq, row = lax.axis_index("seq"), lax.axis_index("rows")
    half = normed_turned.shape[0] // 2
    x, y = lax.rem(seq, 2), lax.div(seq, 2)
    core_peer = {"rows": row + 1 - 2 * lax.rem(row, 2)}
    x_peer = {"seq": seq + 1 - 2 * x}
    y_peer = {"seq": seq + 2 - 4 * y}
    chip, core = lax.div(row, 2), lax.rem(row, 2)
    to_chip = [lax.rem(chip + k, 4) for k in range(4)]
    chip_peers = [{"rows": 2 * to_chip[k] + core} for k in range(4)]

    @pl.when(step == 0)
    def _():
        bias_line[...] = bias[...].astype(F32).reshape(1, bias.shape[0])
        barrier = pltpu.get_barrier_semaphore()
        for peer in (core_peer, x_peer, y_peer, *chip_peers[1:]):
            pl.semaphore_signal(barrier, inc=1, device_id=peer, device_id_type=pl.DeviceIdType.MESH)
        pl.semaphore_wait(barrier, 6)

    def copies(source, target, sent, came, slot, kind, device):
        return pltpu.make_async_remote_copy(
            src_ref=source.at[slot],
            dst_ref=target.at[slot],
            send_sem=sent.at[kind, slot],
            recv_sem=came.at[kind, slot],
            device_id=device,
            device_id_type=pl.DeviceIdType.MESH,
        )

    def to_core(slot):
        return (
            copies(up_core, up_core_got, core_sent, core_came, slot, 0, core_peer),
            copies(down_core, down_core_got, core_sent, core_came, slot, 1, core_peer),
        )

    def to_seq(slot):
        return (
            copies(up_out, up_got, seq_sent, seq_came, slot, 0, x_peer),
            copies(down_out, down_got, seq_sent, seq_came, slot, 1, y_peer),
        )

    def to_last(slot):
        return (
            copies(up_last, up_last_got, last_sent, last_came, slot, 0, y_peer),
            copies(down_last, down_last_got, last_sent, last_came, slot, 1, x_peer),
        )

    def to_chips(slot):
        return [
            pltpu.make_async_remote_copy(
                src_ref=chip_out.at[slot, to_chip[k]],
                dst_ref=chip_got.at[slot, k - 1],
                send_sem=chip_sent.at[k - 1, slot],
                recv_sem=chip_came.at[k - 1, slot],
                device_id=chip_peers[k],
                device_id_type=pl.DeviceIdType.MESH,
            )
            for k in range(1, 4)
        ]

    @pl.when(step >= 4)
    def _():
        slot = lax.rem(step, 2)
        for copy in to_chips(slot):
            copy.wait()
        for kind, total in enumerate((up_total, down_total)):
            value = chip_full[slot, chip, kind]
            for k in range(3):
                value = value + chip_got[slot, k, kind].astype(F32)
            total[...] = value

    @pl.when(step >= 3)
    def _():
        slot = lax.rem(step + 1, 2)
        for copy in to_last(slot):
            copy.wait()
        size = half // 4
        ups = up_quarter[slot] + up_last_got[slot].astype(F32)
        downs = down_quarter[slot] + down_last_got[slot].astype(F32)
        for place in range(4):
            up_block = ups[place * size : (place + 1) * size]
            down_block = downs[:, place * 128 : (place + 1) * 128]
            chip_full[slot, place, 0] = up_block
            chip_full[slot, place, 1] = down_block
            chip_out[slot, place, 0] = up_block.astype(BF16)
            chip_out[slot, place, 1] = down_block.astype(BF16)
        @pl.when(step < tiles + 1)
        def _():
            for copy in to_chips(slot):
                copy.start()

        @pl.when(step == tiles + 1)
        def _():
            left_full[...] = chip_full[slot]

    @pl.when(step >= 2)
    def _():
        slot = lax.rem(step, 2)
        for copy in to_seq(slot):
            copy.wait()
        up_quarter[slot] = up_half[slot, y] + up_got[slot, y].astype(F32)
        up_last[slot] = (up_half[slot, 1 - y] + up_got[slot, 1 - y].astype(F32)).astype(BF16)
        down_quarter[slot] = down_half[slot, x] + down_got[slot, x].astype(F32)
        down_last[slot] = (down_half[slot, 1 - x] + down_got[slot, 1 - x].astype(F32)).astype(BF16)
        @pl.when(step < tiles + 1)
        def _():
            for copy in to_last(slot):
                copy.start()

        @pl.when(step == tiles + 1)
        def _():
            left_up[...] = up_quarter[slot]
            left_up_low[...] = up_last[slot]
            left_down[...] = down_quarter[slot]
            left_down_low[...] = down_last[slot]


    @pl.when((step >= 1) & (step <= tiles))
    def _():
        slot = lax.rem(step + 1, 2)
        for copy in to_core(slot):
            copy.wait()
        for other in range(2):
            kept, gone = 2 * other + x, 2 * other + 1 - x
            up_half[slot, other] = up_mine[slot, kept] + up_core_got[slot, kept].astype(F32)
            up_out[slot, other] = (up_mine[slot, gone] + up_core_got[slot, gone].astype(F32)).astype(BF16)
            kept, gone = 2 * y + other, 2 * (1 - y) + other
            down_half[slot, other] = down_mine[slot, kept] + down_core_got[slot, kept].astype(F32)
            down_out[slot, other] = (down_mine[slot, gone] + down_core_got[slot, gone].astype(F32)).astype(BF16)
        for copy in to_seq(slot):
            copy.start()

    @pl.when(step < tiles)
    def _():
        slot = lax.rem(step, 2)
        up = jnp.concatenate([up0[...], up1[...], up2[...], up3[...]], axis=1)
        down = jnp.concatenate([down0[...], down1[...], down2[...], down3[...]], axis=0)
        hidden_part = bias.shape[0] // 4
        biases = jnp.concatenate(
            [
                bias_line[:, pl.ds(pl.multiple_of(owner * hidden_part + step * 128, 128), 128)]
                for owner in range(4)
            ],
            axis=1,
        )
        c0 = math.sqrt(2 / math.pi)
        c1 = c0 * 0.044715
        hidden = jnp.dot(normed[...], up, preferred_element_type=F32) + biases
        square = hidden * hidden
        gate = 0.5 + 0.5 * jnp.tanh(hidden * (c0 + c1 * square))
        raised = hidden * gate
        slope = gate + raised * (1.0 - gate) * (2 * c0 + 6 * c1 * square)
        active = raised.astype(BF16)
        down_part = jnp.dot(grad_turned[...], active, preferred_element_type=F32)
        for owner in range(4):
            size = half // 4
            down_mine[slot, owner] = down_part[owner * size : (owner + 1) * size]
            down_core[slot, owner] = down_part[half + owner * size : half + (owner + 1) * size].astype(BF16)
        to_core(slot)[1].start()
        back = (((1,), (1,)), ((), ()))
        grad_active = lax.dot_general(grad_out[...], down, back, preferred_element_type=F32)
        grad_wide = (grad_active * slope).astype(BF16)
        up_part = jnp.dot(normed_turned[...], grad_wide, preferred_element_type=F32)
        for owner in range(4):
            columns = slice(owner * 128, (owner + 1) * 128)
            up_mine[slot, owner] = up_part[:half, columns]
            up_core[slot, owner] = up_part[half:, columns].astype(BF16)
        to_core(slot)[0].start()
        sums = jnp.sum(grad_wide.astype(F32), axis=0, keepdims=True)
        for owner in range(4):
            bias_sum[owner] = sums[:, owner * 128 : (owner + 1) * 128]
        out_part = jnp.dot(active, down, preferred_element_type=F32)
        grad_part = lax.dot_general(grad_wide, up, back, preferred_element_type=F32)

        @pl.when(step == 0)
        def _():
            out_sum[...] = out_part
            grad_sum[...] = grad_part

        @pl.when(step > 0)
        def _():
            out_sum[...] += out_part
            grad_sum[...] += grad_part


def feed_forward_reduce(normed, grad_out, normed_turned, grad_turned, up, down, bias):
    count, width = normed.shape
    hidden = up.shape[1]
    part = hidden // 4
    tiles = part // 128
    half, quarter = width // 2, width // 8
    last = tiles - 1
    shape = jax.ShapeDtypeStruct
    fixed = lambda *dims: pl.BlockSpec(dims, lambda t: (0, 0), pipeline_mode=pl.Buffered(buffer_count=1))
    result = lambda *dims: pl.BlockSpec(dims, lambda t: (0, 0))
    done = lambda t: jnp.maximum(t - 4, 0)

    def up_block(owner):
        return pl.BlockSpec((width, 128), lambda t: (0, owner * tiles + jnp.minimum(t, last)))

    def down_block(owner):
        return pl.BlockSpec((128, width), lambda t: (owner * tiles + jnp.minimum(t, last), 0))

    bias_block = pl.BlockSpec((4, 1, 128), lambda t: (0, 0, jnp.minimum(t, last)))
    pair = lambda dtype, *dims: pltpu.VMEM((2,) + dims, dtype)
    return pl.pallas_call(
        partial(mlp_reduce_kernel, tiles),
        grid=(tiles + STAGES,),
        in_specs=[fixed(count, width), fixed(count, width), fixed(width, count), fixed(width, count)]
        + [up_block(owner) for owner in range(4)]
        + [down_block(owner) for owner in range(4)]
        + [pl.BlockSpec((hidden,), lambda t: (0,))],
        out_specs=[
            result(count, width),
            result(count, width),
            bias_block,
            pl.BlockSpec((quarter, 128), lambda t: (0, done(t))),
            pl.BlockSpec((quarter, 128), lambda t: (0, done(t))),
            pl.BlockSpec((4, 2, quarter, 128), lambda t: (0, 0, 0, 0)),
            result(half, 128),
            result(half, 128),
            result(quarter, 512),
            result(quarter, 512),
        ],
        out_shape=[
            shape((count, width), F32),
            shape((count, width), F32),
            shape((4, 1, part), F32),
            shape((quarter, part - 256), F32),
            shape((quarter, part - 256), F32),
            shape((4, 2, quarter, 128), F32),
            shape((half, 128), F32),
            shape((half, 128), BF16),
            shape((quarter, 512), F32),
            shape((quarter, 512), BF16),
        ],
        scratch_shapes=[
            pair(F32, 4, half, 128),
            pair(F32, 4, quarter, 512),
            pair(BF16, 4, half, 128),
            pair(BF16, 4, quarter, 512),
            pair(BF16, 4, half, 128),
            pair(BF16, 4, quarter, 512),
            pair(F32, 2, half, 128),
            pair(F32, 2, quarter, 512),
            pair(BF16, 2, half, 128),
            pair(BF16, 2, quarter, 512),
            pair(BF16, 2, half, 128),
            pair(BF16, 2, quarter, 512),
            pair(F32, half, 128),
            pair(F32, quarter, 512),
            pair(BF16, half, 128),
            pair(BF16, quarter, 512),
            pair(BF16, half, 128),
            pair(BF16, quarter, 512),
            pair(F32, 4, 2, quarter, 128),
            pair(BF16, 4, 2, quarter, 128),
            pair(BF16, 3, 2, quarter, 128),
        ]
        + [pltpu.SemaphoreType.DMA((2, 2))] * 6
        + [pltpu.SemaphoreType.DMA((3, 2))] * 2
        + [pltpu.VMEM((1, hidden), F32)],
        compiler_params=pltpu.CompilerParams(collective_id=1, has_side_effects=True, vmem_limit_bytes=VMEM_LIMIT),
        cost_estimate=pl.CostEstimate(
            flops=12 * count * width * hidden,
            bytes_accessed=6 * width * hidden,
            transcendentals=count * hidden,
        ),
    )(normed, grad_out, normed_turned, grad_turned, up, up, up, up, down, down, down, down, bias)


def slot_column(slots):
    return lax.rem(lax.broadcasted_iota(jnp.int32, (3 * slots, 1), 0), slots)


def split_low(values):
    high = values.astype(BF16)
    rest = values - high.astype(F32)
    middle = rest.astype(BF16)
    return high, middle, (rest - middle.astype(F32)).astype(BF16)


def per_token(slot_col, seg_row, table):
    picked = (slot_col == seg_row).astype(BF16)
    return lax.dot_general(
        picked, jnp.concatenate(split_low(table), axis=0), (((0,), (0,)), ((), ())), preferred_element_type=F32
    )


def per_slot(slot_col, seg_row, values):
    slots = slot_col.shape[0] // 3
    picked = (slot_col[:slots] == seg_row).astype(BF16)
    return sum(jnp.dot(picked, part, preferred_element_type=F32) for part in split_low(values))


def normalize(values):
    center = values - jnp.mean(values, axis=-1, keepdims=True)
    inverse = lax.rsqrt(jnp.mean(center * center, axis=-1, keepdims=True) + norm_eps)
    return center * inverse, inverse


def normalize_back(normal, inverse, grad):
    return inverse * (grad - jnp.mean(grad, axis=-1, keepdims=True) - normal * jnp.mean(grad * normal, axis=-1, keepdims=True))


def after_kernel(
    seg,
    table,
    bias,
    attended,
    weight,
    out_sum,
    grad_sum,
    middle,
    branch,
    cotangent,
    left_full,
    left_up,
    left_up_low,
    left_down,
    left_down_low,
    block_out,
    grad_middle_ref,
    view_ref,
    slot_sums,
    bias_sum,
    proj_own,
    proj_low,
    up_tail,
    down_tail,
    attended_here,
    weight_here,
    rows_here,
    cotangent_here,
    block_here,
    middle_here,
    normal_here,
    grad_here,
    heads_out,
    total,
    core_out,
    core_got,
    load_sem,
    first_sem,
    store_sem,
    sent,
    came,
    kept,
    core_sent,
    core_came,
    full_here,
    up_here,
    up_low_here,
    down_here,
    down_low_here,
    up_got,
    down_got,
    chip_out,
    chip_got,
    left_sem,
    left_sent,
    left_came,
):
    rows, length, width = cotangent_here.shape
    depth, own = width // 8, width // 4
    seq, row = lax.axis_index("seq"), lax.axis_index("rows")
    core = lax.rem(row, 2)
    core_peer = {"rows": row + 1 - 2 * core}
    peers = peers_of(seq)
    slot_col = slot_column(table.shape[1])

    def go(copies):
        for copy in copies:
            copy.start()

    def end(copies):
        for copy in copies:
            copy.wait()

    def loads(r):
        lines = pl.ds(r * length, length)
        pairs = (
            (out_sum.at[lines], rows_here.at[r, 0]),
            (grad_sum.at[lines], rows_here.at[r, 1]),
            (middle.at[r], rows_here.at[r, 2]),
            (branch.at[r], rows_here.at[r, 3]),
            (cotangent.at[r], cotangent_here.at[r]),
        )
        return [pltpu.make_async_copy(source, target, load_sem.at[r, k]) for k, (source, target) in enumerate(pairs)]

    load_weight = pltpu.make_async_copy(weight, weight_here, first_sem.at[0])
    load_attended = pltpu.make_async_copy(attended, attended_here, first_sem.at[1])
    lefts = ((left_full, full_here.at[0]), (left_up_low, up_low_here), (left_down_low, down_low_here), (left_up, up_here), (left_down, down_here))
    load_left = [pltpu.make_async_copy(source, target, left_sem.at[k]) for k, (source, target) in enumerate(lefts)]
    go(load_left + loads(0) + [load_weight] + loads(1) + [load_attended])
    chip = lax.div(row, 2)
    to_chip = [lax.rem(chip + k, 4) for k in range(4)]
    chip_peers = [{"rows": 2 * to_chip[k] + core} for k in range(4)]
    greet([{"seq": peer} for peer in peers] + [core_peer] + chip_peers[1:])

    def to_chips(tile):
        return [
            send_to(
                chip_out.at[tile, to_chip[k]],
                chip_got.at[tile, k - 1],
                left_sent.at[2 + 3 * tile + k - 1],
                left_came.at[2 + 3 * tile + k - 1],
                chip_peers[k],
            )
            for k in range(1, 4)
        ]

    left_copies = [
        send_to(up_low_here, up_got, left_sent.at[0], left_came.at[0], {"seq": peers[1]}),
        send_to(down_low_here, down_got, left_sent.at[1], left_came.at[1], {"seq": peers[0]}),
    ]
    end(load_left)
    go(left_copies)
    chip_out[0] = full_here[0].astype(BF16)
    go(to_chips(0))

    def to_peer(r, m):
        lanes = pl.ds(m * length, length)
        return send_block(
            heads_out.at[r, peers[m - 1]], view_ref.at[r, :, lanes], sent, came, r * 3 + m - 1, {"seq": peers[m - 1]}
        )

    def to_self(r):
        return pltpu.make_async_copy(heads_out.at[r, seq], view_ref.at[r, :, pl.ds(0, length)], kept.at[r])

    def stores(r):
        return [
            pltpu.make_async_copy(middle_here.at[r], grad_middle_ref.at[r], store_sem.at[r, 0]),
            pltpu.make_async_copy(block_here.at[r], block_out.at[r], store_sem.at[r, 1]),
        ]

    def mods(r, first, count):
        seg_row = seg[r : r + 1, pl.ds(pl.multiple_of(seq * length, 128), length)]
        found = per_token(slot_col, seg_row, table[r, :, first * width : (first + count) * width])
        return [found[:, k * width : (k + 1) * width] for k in range(count)]

    for r in range(rows):
        (gate_a,), (scale_b,) = mods(r, 2, 1), mods(r, 4, 1)
        end(loads(r))
        normal, inverse = normalize(rows_here[r, 2])
        normal_here[r] = normal
        grad_normed = rows_here[r, 1]
        grad_middle = cotangent_here[r].astype(F32) + normalize_back(normal, inverse, grad_normed * (1.0 + scale_b))
        middle_here[r] = grad_middle
        stores(r)[0].start()
        grad_branch = (grad_middle * gate_a).astype(BF16)
        grad_here[r] = grad_branch
        if r == 0:
            load_weight.wait()
        grad_heads = lax.dot_general(weight_here[...], grad_branch, (((1,), (1,)), ((), ())), preferred_element_type=F32)
        for owner in range(4):
            heads_out[r, owner] = grad_heads[owner * own : (owner + 1) * own].astype(BF16)
        to_self(r).start()
        for m in range(1, 4):
            to_peer(r, m).start()

    end(left_copies)
    ups = up_here[...] + up_got[...].astype(F32)
    downs = down_here[...] + down_got[...].astype(F32)
    for place in range(4):
        full_here[1, place, 0] = ups[place * depth : (place + 1) * depth]
        full_here[1, place, 1] = downs[:, place * 128 : (place + 1) * 128]
    chip_out[1] = full_here[1].astype(BF16)
    go(to_chips(1))
    load_attended.wait()
    for r in range(rows):
        part = jnp.dot(attended_here[r], grad_here[r], preferred_element_type=F32)
        sums = jnp.sum(grad_here[r].astype(F32), axis=0, keepdims=True)
        if r == 0:
            total[...] = part
            bias_sum[...] = sums
        else:
            total[...] += part
            bias_sum[...] += sums
    to_core = send_to(core_out, core_got, core_sent, core_came, core_peer)
    for place in range(4):
        other = pl.multiple_of((2 * place + 1 - core) * depth, 8)
        core_out[place] = total[pl.ds(other, depth), :].astype(BF16)
    to_core.start()

    bias_line = bias[...].astype(F32).reshape(1, width)
    for r in range(rows):
        (gate_b,) = mods(r, 5, 1)
        branch_b = rows_here[r, 0] + bias_line
        block_here[r] = (rows_here[r, 2] + gate_b * branch_b).astype(BF16)
        stores(r)[1].start()
        grad_normed = rows_here[r, 1]
        seg_row = seg[r : r + 1, pl.ds(pl.multiple_of(seq * length, 128), length)]
        pieces = (
            middle_here[r] * rows_here[r, 3],
            grad_normed,
            grad_normed * normal_here[r],
            cotangent_here[r].astype(F32) * branch_b,
        )
        for k, piece in enumerate(pieces):
            slot_sums[r, :, k * width : (k + 1) * width] = per_slot(slot_col, seg_row, piece)

    to_core.wait()
    for place in range(4):
        mine = pl.multiple_of((2 * place + core) * depth, 8)
        proj_low[place] = (total[pl.ds(mine, depth), :] + core_got[place].astype(F32)).astype(BF16)
    mine = pl.multiple_of(row * depth, 8)
    proj_own[...] = total[pl.ds(mine, depth), :] + core_got[chip].astype(F32)
    for tile in range(2):
        end(to_chips(tile))
        for kind, target in enumerate((up_tail, down_tail)):
            value = full_here[tile, chip, kind]
            for k in range(3):
                value = value + chip_got[tile, k, kind].astype(F32)
            target[:, tile * 128 : (tile + 1) * 128] = value
    for r in range(rows):
        end(stores(r))
        to_self(r).wait()
        for m in range(1, 4):
            to_peer(r, m).wait()


def after_feed_forward(seg, table, attended, weight, bias, out_sum, grad_sum, middle, branch, cotangent, left):
    rows, length, width = cotangent.shape
    slots = table.shape[1]
    depth = width // 8
    shape = jax.ShapeDtypeStruct
    vmem = lambda dtype, *dims: pltpu.VMEM(dims, dtype)
    near, far = pl.BlockSpec(memory_space=pltpu.VMEM), pl.BlockSpec(memory_space=pl.ANY)
    dma = lambda *dims: pltpu.SemaphoreType.DMA(dims)
    return pl.pallas_call(
        after_kernel,
        in_specs=[near] * 3 + [far] * 12,
        out_specs=[far] * 3 + [near] * 6,
        out_shape=[
            shape((rows, length, width), BF16),
            shape((rows, length, width), F32),
            shape((rows, width // 4, 4 * length), BF16),
            shape((rows, slots, 4 * width), F32),
            shape((1, width), F32),
            shape((depth, width), F32),
            shape((4, depth, width), BF16),
            shape((depth, 256), F32),
            shape((depth, 256), F32),
        ],
        scratch_shapes=[
            vmem(BF16, rows, width, length),
            vmem(BF16, width, width),
            vmem(F32, rows, 4, length, width),
            vmem(BF16, rows, length, width),
            vmem(BF16, rows, length, width),
            vmem(F32, rows, length, width),
            vmem(F32, rows, length, width),
            vmem(BF16, rows, length, width),
            vmem(BF16, rows, 4, width // 4, length),
            vmem(F32, width, width),
            vmem(BF16, 4, depth, width),
            vmem(BF16, 4, depth, width),
            dma(rows, 5),
            dma(2),
            dma(rows, 2),
            dma(3 * rows),
            dma(3 * rows),
            dma(rows),
            pltpu.SemaphoreType.DMA,
            pltpu.SemaphoreType.DMA,
            vmem(F32, 2, 4, 2, depth, 128),
            vmem(F32, 4 * depth, 128),
            vmem(BF16, 4 * depth, 128),
            vmem(F32, depth, 512),
            vmem(BF16, depth, 512),
            vmem(BF16, 4 * depth, 128),
            vmem(BF16, depth, 512),
            vmem(BF16, 2, 4, 2, depth, 128),
            vmem(BF16, 2, 3, 2, depth, 128),
            dma(5),
            dma(8),
            dma(8),
        ],
        compiler_params=pltpu.CompilerParams(vmem_limit_bytes=VMEM_LIMIT, collective_id=4, has_side_effects=True),
        cost_estimate=pl.CostEstimate(flops=8 * 10**9, bytes_accessed=3 * 10**7, transcendentals=0),
    )(seg, table, bias, attended, weight, out_sum, grad_sum, middle, branch, cotangent, *left)


def qkv_weight_kernel(grad, normed, keep_ref, send_ref, sum_ref, total, turned):
    step = pl.program_id(0)
    chips, depth = lax.axis_size("rows") // 2, total.shape[1] // lax.axis_size("rows")
    mine = lax.rem(lax.axis_index("rows"), 2)
    part = jnp.dot(grad[0], normed[0], preferred_element_type=F32)
    sums = jnp.sum(grad[0].astype(F32), axis=1, keepdims=True)

    @pl.when(step == 0)
    def _():
        total[...] = part
        sum_ref[...] = sums

    @pl.when(step > 0)
    def _():
        total[...] += part
        sum_ref[...] += sums

    @pl.when(step == pl.num_programs(0) - 1)
    def _():
        turned[...] = total[...].T
        for chip in range(chips):
            first = pl.multiple_of((2 * chip + mine) * depth, 8)
            other = pl.multiple_of((2 * chip + 1 - mine) * depth, 8)
            keep_ref[chip] = turned[pl.ds(first, depth), :]
            send_ref[chip] = turned[pl.ds(other, depth), :].astype(BF16)


def qkv_weight_grad(grad, normed):
    rows, features, length = grad.shape
    width = normed.shape[2]
    groups = lax.axis_size("rows")
    shape = (groups // 2, width // groups, features)
    return pl.pallas_call(
        qkv_weight_kernel,
        grid=(rows,),
        in_specs=[
            pl.BlockSpec((1, features, length), lambda r: (r, 0, 0)),
            pl.BlockSpec((1, length, width), lambda r: (r, 0, 0)),
        ],
        out_specs=[
            pl.BlockSpec(shape, lambda r: (0, 0, 0)),
            pl.BlockSpec(shape, lambda r: (0, 0, 0)),
            pl.BlockSpec((features, 1), lambda r: (0, 0)),
        ],
        out_shape=[
            jax.ShapeDtypeStruct(shape, F32),
            jax.ShapeDtypeStruct(shape, BF16),
            jax.ShapeDtypeStruct((features, 1), F32),
        ],
        scratch_shapes=[pltpu.VMEM((features, width), F32), pltpu.VMEM((width, features), F32)],
        compiler_params=pltpu.CompilerParams(vmem_limit_bytes=VMEM_LIMIT),
        cost_estimate=pl.CostEstimate(
            flops=2 * rows * length * width * features,
            bytes_accessed=2 * rows * length * (width + features) + 6 * width * features // 2,
            transcendentals=0,
        ),
    )(grad, normed)


def tail_kernel(
    images,
    mod,
    weight,
    cond,
    ada_ref,
    cond_ref,
    bias_ref,
    got,
    low_mine,
    low_got,
    row_mine,
    row_got,
    cond_mine,
    cond_got,
    column_got,
    sent,
    arrived,
):
    seq_count, row_total = lax.axis_size("seq"), lax.axis_size("rows")
    seq, row = lax.axis_index("seq"), lax.axis_index("rows")
    to_seq = [lax.rem(seq + m, seq_count) for m in range(seq_count)]
    to_row = [lax.rem(row + m, row_total) for m in range(row_total)]
    barrier = pltpu.get_barrier_semaphore()
    for m in range(1, seq_count):
        pl.semaphore_signal(barrier, inc=1, device_id={"seq": to_seq[m]}, device_id_type=pl.DeviceIdType.MESH)
    for m in range(1, row_total):
        pl.semaphore_signal(barrier, inc=1, device_id={"rows": to_row[m]}, device_id_type=pl.DeviceIdType.MESH)
    pl.semaphore_wait(barrier, seq_count + row_total - 2)

    used = [0]

    def start(source, target, device):
        copy = pltpu.make_async_remote_copy(
            src_ref=source,
            dst_ref=target,
            send_sem=sent.at[used[0]],
            recv_sem=arrived.at[used[0]],
            device_id=device,
            device_id_type=pl.DeviceIdType.MESH,
        )
        used[0] += 1
        copy.start()
        return copy

    copies = [start(mod.at[to_seq[m]], got.at[m], {"seq": to_seq[m]}) for m in range(1, seq_count)]
    column_got[0] = cond[row]
    column_copies = [start(cond.at[to_row[m]], column_got.at[m], {"rows": to_row[m]}) for m in range(1, row_total)]
    total = mod[seq]
    for m, copy in enumerate(copies):
        copy.wait()
        total = total + got[m + 1]
    low = total[:images].astype(BF16)
    low_mine[...] = low
    row_mine[...] = total[images:]
    row_mine[0:1] = jnp.sum(total[:images], axis=0, keepdims=True)
    low_got[0] = low
    copies = [start(low_mine, low_got.at[m], {"rows": to_row[m]}) for m in range(1, row_total)]
    copies += [start(row_mine, row_got.at[m], {"rows": to_row[m]}) for m in range(1, row_total)]
    term = lax.dot_general(low, weight[...], (((1,), (1,)), ((), ())), preferred_element_type=F32)
    cond_mine[...] = term
    cond_copies = [start(cond_mine, cond_got.at[m], {"seq": to_seq[m]}) for m in range(1, seq_count)]
    for copy in copies:
        copy.wait()
    sums = row_mine[...]
    for m in range(1, row_total):
        sums = sums + row_got[m]
    bias_ref[seq] = sums
    copies = [start(bias_ref.at[seq], bias_ref.at[seq], {"seq": to_seq[m]}) for m in range(1, seq_count)]
    for copy in column_copies:
        copy.wait()
    gathered = jnp.concatenate([low_got[m] for m in range(row_total)], axis=0)
    columns = jnp.concatenate([column_got[m] for m in range(row_total)], axis=0)
    ada_ref[...] = lax.dot_general(columns, gathered, (((0,), (0,)), ((), ())), preferred_element_type=F32)
    for m, copy in enumerate(cond_copies):
        copy.wait()
        term = term + cond_got[m + 1]
    cond_ref[...] = term
    for copy in copies:
        copy.wait()


def finish(mod, weight, cond, images):
    seq_count, lines, columns = mod.shape
    width, depth = weight.shape[0], cond.shape[2]
    row_total = lax.axis_size("rows")
    extra = lines - images
    copies = 3 * (seq_count - 1) + 3 * (row_total - 1)
    return pl.pallas_call(
        partial(tail_kernel, images),
        in_specs=[pl.BlockSpec(memory_space=pltpu.VMEM)] * 3,
        out_specs=[pl.BlockSpec(memory_space=pltpu.VMEM)] * 3,
        out_shape=[
            jax.ShapeDtypeStruct((depth, columns), F32),
            jax.ShapeDtypeStruct((images, width), F32),
            jax.ShapeDtypeStruct((seq_count, extra, columns), F32),
        ],
        scratch_shapes=[
            pltpu.VMEM((seq_count, lines, columns), F32),
            pltpu.VMEM((images, columns), BF16),
            pltpu.VMEM((row_total, images, columns), BF16),
            pltpu.VMEM((extra, columns), F32),
            pltpu.VMEM((row_total, extra, columns), F32),
            pltpu.VMEM((images, width), F32),
            pltpu.VMEM((seq_count, images, width), F32),
            pltpu.VMEM((row_total, images, depth), BF16),
            pltpu.SemaphoreType.DMA((copies,)),
            pltpu.SemaphoreType.DMA((copies,)),
        ],
        compiler_params=pltpu.CompilerParams(collective_id=0, has_side_effects=True, vmem_limit_bytes=VMEM_LIMIT),
        cost_estimate=pl.CostEstimate(flops=10**9, bytes_accessed=10**7, transcendentals=0),
    )(mod, weight, cond)


def send_to(source, target, sent, came, device):
    return pltpu.make_async_remote_copy(
        src_ref=source,
        dst_ref=target,
        send_sem=sent,
        recv_sem=came,
        device_id=device,
        device_id_type=pl.DeviceIdType.MESH,
    )


def back_kernel(
    block,
    inner,
    scale,
    code_col,
    code_row,
    query,
    key,
    value,
    out,
    grad_out,
    lse,
    normed,
    proj_own,
    proj_low,
    down,
    down_tail,
    seg,
    table,
    slot_sums,
    image_index,
    conditioning,
    proj_bias,
    up_bias,
    down_bias,
    tokens,
    grad_middle,
    weight,
    ada,
    grad_tokens,
    proj_ref,
    down_ref,
    ada_ref,
    cond_ref,
    ada_bias_ref,
    qv_bias_ref,
    proj_bias_ref,
    up_bias_ref,
    down_bias_ref,
    qkv_ref,
    grads,
    token_got,
    key_sum,
    value_sum,
    keys,
    values,
    total,
    spare,
    core_out,
    core_got,
    proj_got,
    seq_out,
    seq_got,
    down_out,
    down_got,
    qkv_own,
    chip_got,
    weights,
    tokens_here,
    middle_here,
    grad_here,
    features,
    image_sums,
    feature_sums,
    mod,
    got,
    lines,
    lines_got,
    low_all,
    small_core,
    small_chip,
    small_seq,
    cond_all,
    cond,
    column_got,
    piece_out,
    piece_got,
    sent,
    came,
    kept,
    load_sem,
    store_sem,
    other_sent,
    other_came,
):
    length, size = query.shape[-1], query.shape[-2]
    row, head = pl.program_id(0), pl.program_id(1)
    rows, _, heads = grads.shape[:3]
    width = normed.shape[-1]
    images, columns = mod.shape[1:]
    depth, own, local = width // 8, width // 4, length // 4
    seq, group = lax.axis_index("seq"), lax.axis_index("rows")
    chip, core = lax.div(group, 2), lax.rem(group, 2)
    seq_places = peers_of(seq)
    peers = [{"seq": place} for place in seq_places]
    row_places = [lax.rem(group + m, 8) for m in range(8)]
    row_peers = [{"rows": place} for place in row_places]
    core_peer = {"rows": group + 1 - 2 * core}
    to_chip = [lax.rem(chip + k, 4) for k in range(4)]
    from_chip = [lax.rem(chip + 4 - k, 4) for k in range(4)]
    chip_peers = [{"rows": 2 * to_chip[k] + core} for k in range(4)]
    first = (row == 0) & (head == 0)
    last = (row == rows - 1) & (head == heads - 1)
    slot_col = slot_column(table.shape[1])
    used = [0]

    def copy_to(source, target, device):
        used[0] += 1
        return send_to(source, target, other_sent.at[used[0] - 1], other_came.at[used[0] - 1], device)

    def go(copies):
        for copy in copies:
            copy.start()

    def end(copies):
        for copy in copies:
            copy.wait()

    def to_peer(r, h, m):
        place = (r * heads + h) * 3 + m - 1
        source = grads.at[r, :, h, :, pl.ds(m * local, local)]
        return send_to(source, token_got.at[r, :, seq, h], sent.at[place], came.at[place], peers[m - 1])

    def to_self(r, h):
        source = grads.at[r, :, h, :, pl.ds(0, local)]
        return pltpu.make_async_copy(source, token_got.at[r, :, seq, h], kept.at[r * heads + h])

    proj_copies = [copy_to(proj_low.at[to_chip[k]], proj_got.at[k - 1], chip_peers[k]) for k in range(1, 4)]
    seq_copies = [copy_to(seq_out.at[place], seq_got.at[m], peers[m]) for m, place in enumerate(seq_places)]
    core_copy = copy_to(core_out, core_got, core_peer)
    down_copy = copy_to(down_out.at[1 - core], down_got, core_peer)
    chip_copies = [copy_to(core_out.at[to_chip[k]], chip_got.at[k - 1], chip_peers[k]) for k in range(1, 4)]
    column_copies = [copy_to(cond.at[row_places[m]], column_got.at[group], row_peers[m]) for m in range(1, 8)]
    mod_copies = [copy_to(mod.at[place], got.at[m], peers[m]) for m, place in enumerate(seq_places)]
    line_copies = [copy_to(lines.at[place], lines_got.at[m], peers[m]) for m, place in enumerate(seq_places)]
    low_core = copy_to(low_all.at[chip, core], low_all.at[chip, core], core_peer)
    low_chips = [copy_to(low_all.at[chip, core], low_all.at[chip, core], chip_peers[k]) for k in range(1, 4)]
    low_on = [copy_to(low_all.at[from_chip[k], core], low_all.at[from_chip[k], core], core_peer) for k in range(1, 4)]
    small_over = copy_to(small_core.at[core], small_core.at[core], core_peer)
    small_chips = [copy_to(small_chip.at[chip], small_chip.at[chip], chip_peers[k]) for k in range(1, 4)]
    small_copies = [copy_to(small_seq.at[seq], small_seq.at[seq], peers[m]) for m in range(3)]
    cond_copies = [copy_to(cond_all.at[seq], cond_all.at[seq], peers[m]) for m in range(3)]
    base = used[0]

    load_weights = [
        pltpu.make_async_copy(weight.at[:, pl.ds(part * width, width)], weights.at[part], load_sem.at[part])
        for part in range(3)
    ]
    load_tokens = pltpu.make_async_copy(tokens, tokens_here, load_sem.at[3])
    load_middle = pltpu.make_async_copy(grad_middle, middle_here, load_sem.at[4])
    load_ada = [
        pltpu.make_async_copy(ada.at[pl.ds(0, width)], weights.at[0], load_sem.at[5]),
        pltpu.make_async_copy(ada.at[pl.ds(width, columns - width)], weights.at[1, pl.ds(0, columns - width)], load_sem.at[6]),
    ]

    @pl.when(first)
    def _():
        greet(peers + row_peers[1:])
        go(proj_copies)
        half = down_out.shape[2]
        down_out[0] = down[:, :half]
        down_out[1] = jnp.concatenate([down[:, half:], down_tail[...]], axis=1)
        down_copy.start()
        go(load_weights + [load_tokens, load_middle])
        value = conditioning[...].astype(F32)
        low = (value / (1.0 + jnp.exp(-value))).astype(BF16)
        for place in range(8):
            cond[place] = low[:, place * depth : (place + 1) * depth]
        column_got[group] = cond[group]
        go(column_copies)
        image_sums[...] = jnp.zeros_like(image_sums)
        feature_sums[...] = jnp.zeros_like(feature_sums)

    keys[...] = key[0, 0].astype(F32).T.astype(BF16)
    values[...] = value[0, 0].astype(F32).T.astype(BF16)

    def place_of(part):
        return pl.ds(pl.multiple_of((part * heads + head) * size, 8), size)

    for step in range(length // block):
        here = pl.ds(step * block, block)
        query_low = query[0, 0, :, here]
        grad_low = grad_out[0, 0, :, here]
        query_rows = query_low.astype(F32).T.astype(BF16)
        grad_rows = grad_low.astype(F32).T.astype(BF16)
        row_dot = jnp.sum(grad_low.astype(F32) * out[0, 0, :, here].astype(F32), axis=0, keepdims=True)
        grad_query = jnp.zeros((size, block), F32)
        for part in range(length // inner):
            there = pl.ds(part * inner, inner)
            scores = jnp.dot(keys[there, :], query_low, preferred_element_type=F32)
            scores = jnp.where(code_col[0, there, :] == code_row[0, :, here], scores * (scale * LOG2E), -1e30)
            probs = jnp.exp2(scores - lse[0, 0, :, here])
            grad_probs = jnp.dot(values[there, :], grad_low, preferred_element_type=F32)
            grad_raw = (probs * (grad_probs - row_dot) * scale).astype(BF16)
            value_part = jnp.dot(probs.astype(BF16), grad_rows, preferred_element_type=F32)
            key_part = jnp.dot(grad_raw, query_rows, preferred_element_type=F32)
            if step == 0:
                value_sum[there, :] = value_part
                key_sum[there, :] = key_part
            else:
                value_sum[there, :] += value_part
                key_sum[there, :] += key_part
            grad_query += jnp.dot(key[0, 0, :, there], grad_raw, preferred_element_type=F32)
        low = grad_query.astype(BF16)
        grads[row, 0, head, :, here] = low
        spare[place_of(0), here] = low.astype(F32)
    for part, sums in ((1, key_sum), (2, value_sum)):
        low = sums[...].T.astype(BF16)
        grads[row, part, head] = low
        spare[place_of(part), :] = low.astype(F32)

    to_self(row, head).start()
    for m in range(1, 4):
        to_peer(row, head, m).start()

    own_features = 3 * own

    @pl.when((head == heads - 1) & (row == 0))
    def _():
        total[...] = jnp.dot(spare[:own_features].astype(BF16), normed[0], preferred_element_type=F32)

    @pl.when((head == heads - 1) & (row > 0))
    def _():
        total[...] += jnp.dot(spare[:own_features].astype(BF16), normed[0], preferred_element_type=F32)

    def store_tokens(r):
        return pltpu.make_async_copy(grad_here.at[r], grad_tokens.at[r], store_sem.at[r])

    def input_grad(r):
        for h in range(heads):
            to_self(r, h).wait()
            for m in range(1, 4):
                to_peer(r, h, m).wait()
        grad_normed = jnp.zeros((width, local), F32)
        for part in range(3):
            for place in range(4):
                for h in range(heads):
                    start = (place * heads + h) * size
                    features[start : start + size] = token_got[r, part, place, h].astype(F32)
            low = features[...].astype(BF16)
            grad_normed += jnp.dot(weights[part], low, preferred_element_type=F32)
            if part != 1:
                lanes = slice(part * width, (part + 1) * width)
                ones = jnp.ones((8, local), BF16)
                feature_sums[:, lanes] += lax.dot_general(ones, low, (((1,), (1,)), ((), ())), preferred_element_type=F32)
        grad_normed = grad_normed.T
        normal, inverse = normalize(tokens_here[r].astype(F32))
        seg_row = seg[r : r + 1, pl.ds(pl.multiple_of(seq * local, 128), local)]
        scale_a = per_token(slot_col, seg_row, table[r, :, width : 2 * width])
        grad_here[r] = middle_here[r] + normalize_back(normal, inverse, grad_normed * (1.0 + scale_a))
        store_tokens(r).start()
        late = [per_slot(slot_col, seg_row, piece) for piece in (grad_normed, grad_normed * normal)]
        slots = jnp.concatenate(late + [slot_sums[r]], axis=1)
        pick = lax.broadcasted_iota(jnp.int32, (images, slots.shape[0]), 0) == image_index[r : r + 1, :]
        picks = jnp.concatenate([pick.astype(BF16)] * 3, axis=1)
        image_sums[...] += jnp.dot(picks, jnp.concatenate(split_low(slots), axis=0), preferred_element_type=F32)

    @pl.when(last)
    def _():
        spare[:, :own_features] = total[...].T
        for place in range(4):
            other = pl.multiple_of((2 * place + 1 - core) * depth, 8)
            core_out[place] = spare[pl.ds(other, depth), :own_features].astype(BF16)
        core_copy.start()
        end(proj_copies)
        mine = proj_own[...]
        for k in range(3):
            mine = mine + proj_got[k].astype(F32)
        for place in range(4):
            seq_out[place] = mine[:, place * own : (place + 1) * own].astype(BF16)
        go(seq_copies)
        for place in range(4):

            @pl.when(seq == place)
            def _():
                proj_ref[...] = mine[:, place * own : (place + 1) * own]

        down_copy.wait()
        left, right = down_out[core], down_got[...]
        left, right = jnp.where(core == 0, left, right), jnp.where(core == 0, right, left)
        down_ref[:depth] = left
        down_ref[depth:] = right
        core_copy.wait()
        for place in range(4):
            same = pl.multiple_of((2 * place + core) * depth, 8)
            core_out[place] = (spare[pl.ds(same, depth), :own_features] + core_got[place].astype(F32)).astype(BF16)
        same = pl.multiple_of(group * depth, 8)
        qkv_own[...] = spare[pl.ds(same, depth), :own_features] + core_got[chip].astype(F32)
        go(chip_copies)

        end(load_weights + [load_tokens, load_middle])
        for r in range(rows):
            input_grad(r)
        go(load_ada)

        for place in range(4):
            mod[place] = image_sums[:, place * columns : (place + 1) * columns]
        for line in range(8):
            if line < 2:
                value = feature_sums[0:1, 2 * line * width : (2 * line + 1) * width]
            else:
                value = (proj_bias[...], *(up_bias[k] for k in range(4)), down_bias[...])[line - 2]
            lines[line // 2, line % 2 : line % 2 + 1] = value
        go(mod_copies + line_copies)
        for m, copy in enumerate(seq_copies):
            copy.wait()
            proj_ref[...] += seq_got[m].astype(F32)
        sums = mod[seq]
        for m, copy in enumerate(mod_copies):
            copy.wait()
            sums = sums + got[m]
        low = sums.astype(BF16)
        low_all[chip, core] = low
        go([low_core] + low_chips)
        small = lines[seq]
        for m, copy in enumerate(line_copies):
            copy.wait()
            small = small + lines_got[m]
        small_core[core] = jnp.zeros_like(small_core[core])
        small_core[core, 0:2, :width] = small
        small_core[core, 2:3] = jnp.sum(sums, axis=0, keepdims=True)
        small_over.start()
        end(load_ada)
        term = jnp.dot(low[:, :width], weights[0], preferred_element_type=F32)
        term += jnp.dot(low[:, width:], weights[1, : columns - width], preferred_element_type=F32)
        cond_all[seq] = term
        go(cond_copies)
        end(chip_copies + column_copies)
        mine = qkv_own[...]
        for k in range(3):
            mine = mine + chip_got[k].astype(F32)
        for part in range(3):
            piece_out[part] = mine[:, part * own : (part + 1) * own]

        def piece(part):
            index = part * 4 + seq
            target, place = lax.div(index, 3), lax.rem(index, 3)
            copy = send_to(
                piece_out.at[part], piece_got.at[place], other_sent.at[base + part], other_came.at[base + place], {"seq": target}
            )
            return copy, target, place

        def arriving(place):
            source = lax.rem(3 * seq + place, 4)
            copy = send_to(
                piece_out.at[0], piece_got.at[place], other_sent.at[base], other_came.at[base + place], {"seq": source}
            )
            return copy, source

        for part in range(3):
            copy, target, place = piece(part)

            @pl.when(target != seq)
            def _():
                copy.start()

            @pl.when(target == seq)
            def _():
                piece_got[place] = piece_out[part]

        small_over.wait()
        small_chip[chip] = small_core[0] + small_core[1]
        go(small_chips)
        for came_in, going_on in zip(low_chips, low_on):
            came_in.wait()
            going_on.start()
        end(small_chips)
        small_seq[seq] = (small_chip[0] + small_chip[1]) + (small_chip[2] + small_chip[3])
        go(small_copies)
        end([low_core] + low_on)
        gathered = jnp.concatenate([low_all[m // 2, m % 2] for m in range(8)], axis=0)
        blocks = jnp.concatenate([column_got[m] for m in range(8)], axis=0)
        ada_ref[...] = lax.dot_general(blocks, gathered, (((0,), (0,)), ((), ())), preferred_element_type=F32)
        for part in range(3):
            copy, target, place = piece(part)

            @pl.when(target != seq)
            def _():
                copy.wait_send()

        for place in range(3):
            copy, source = arriving(place)

            @pl.when(source != seq)
            def _():
                copy.wait_recv()

        for place in range(3):
            qkv_ref[:, place * own : (place + 1) * own] = piece_got[place]
        end(cond_copies)
        value = conditioning[...].astype(F32)
        gate = 1.0 / (1.0 + jnp.exp(-value))
        sums = (cond_all[0] + cond_all[1]) + (cond_all[2] + cond_all[3])
        cond_ref[...] = sums * gate * (1.0 + value * (1.0 - gate))
        end(small_copies)
        for place in range(4):
            ada_bias_ref[pl.ds(place * columns, columns)] = small_seq[place, 2]
        qv_bias_ref[...] = small_seq[0, 0:2, :width]
        proj_bias_ref[...] = small_seq[1, 0, :width]
        for line in range(3, 7):
            up_bias_ref[pl.ds((line - 3) * width, width)] = small_seq[line // 2, line % 2, :width]
        down_bias_ref[...] = small_seq[3, 1, :width]
        for r in range(rows):
            store_tokens(r).wait()


def attend_back_and_finish(packed, out, grad_out, lse, col, row, normed, *rest):
    proj_own, proj_low, down, down_tail, seg, table, slot_sums, image_index, conditioning, biases, tokens, grad_middle, weight, ada = rest
    rows, _, heads, size, length = packed.shape
    width = normed.shape[2]
    depth, own, features, local = width // 8, width // 4, 3 * heads * size, length // 4
    half = (down.shape[1] + down_tail.shape[1]) // 2
    images, columns = conditioning.shape[0], ada.shape[0]
    part = lambda j: pl.BlockSpec((1, None, 1, size, length), lambda r, h: (r, j, h, 0, 0))
    whole = pl.BlockSpec((1, 1, size, length), lambda r, h: (r, h, 0, 0))
    single = pl.Buffered(buffer_count=1)
    fixed = lambda *dims: pl.BlockSpec(dims, lambda r, h: (0,) * len(dims), pipeline_mode=single)
    result = lambda *dims: pl.BlockSpec(dims, lambda r, h: (0,) * len(dims))
    far = pl.BlockSpec(memory_space=pl.ANY)
    shape = jax.ShapeDtypeStruct
    vmem = lambda dtype, *dims: pltpu.VMEM(dims, dtype)
    count = rows * heads
    copies = 3 + 3 + 1 + 1 + 3 + 7 + 3 + 3 + 1 + 3 + 3 + 1 + 3 + 3 + 3 + 3
    dma = lambda n: pltpu.SemaphoreType.DMA((n,))
    return pl.pallas_call(
        partial(back_kernel, 256, 512, size**-0.5),
        grid=(rows, heads),
        in_specs=[
            pl.BlockSpec((1, length, 1), lambda r, h: (r, 0, 0)),
            pl.BlockSpec((1, 1, length), lambda r, h: (r, 0, 0)),
            part(0),
            part(1),
            part(2),
            whole,
            whole,
            pl.BlockSpec((1, 1, 1, length), lambda r, h: (r, h, 0, 0)),
            pl.BlockSpec((1, length, width), lambda r, h: (r, 0, 0), pipeline_mode=single),
            fixed(depth, width),
            fixed(4, depth, width),
            fixed(*down.shape),
            fixed(*down_tail.shape),
            fixed(*seg.shape),
            fixed(*table.shape),
            fixed(*slot_sums.shape),
            fixed(*image_index.shape),
            fixed(images, width),
            fixed(1, width),
            fixed(4, 1, width),
            fixed(1, width),
            far,
            far,
            far,
            far,
        ],
        out_specs=[
            far,
            result(depth, own),
            result(own, half),
            result(depth, columns),
            result(images, width),
            result(4 * columns),
            result(2, width),
            result(width),
            result(4 * width),
            result(width),
            result(depth, features),
        ],
        out_shape=[
            shape((rows, local, width), F32),
            shape((depth, own), F32),
            shape((own, half), F32),
            shape((depth, columns), F32),
            shape((images, width), F32),
            shape((4 * columns,), F32),
            shape((2, width), F32),
            shape((width,), F32),
            shape((4 * width,), F32),
            shape((width,), F32),
            shape((depth, features), F32),
        ],
        scratch_shapes=[
            vmem(BF16, rows, 3, heads, size, length),
            vmem(BF16, rows, 3, 4, heads, size, local),
            vmem(F32, length, size),
            vmem(F32, length, size),
            vmem(BF16, length, size),
            vmem(BF16, length, size),
            vmem(F32, features, width),
            vmem(F32, width, length),
            vmem(BF16, 4, depth, features),
            vmem(BF16, 4, depth, features),
            vmem(BF16, 3, depth, width),
            vmem(BF16, 4, depth, own),
            vmem(BF16, 3, depth, own),
            vmem(F32, 2, depth, half),
            vmem(F32, depth, half),
            vmem(F32, depth, features),
            vmem(BF16, 3, depth, features),
            vmem(BF16, 3, width, width),
            vmem(BF16, rows, local, width),
            vmem(F32, rows, local, width),
            vmem(F32, rows, local, width),
            vmem(F32, width, local),
            vmem(F32, images, 6 * width),
            vmem(F32, 8, 3 * width),
            vmem(F32, 4, images, columns),
            vmem(F32, 3, images, columns),
            vmem(F32, 4, 2, width),
            vmem(F32, 3, 2, width),
            vmem(BF16, 4, 2, images, columns),
            vmem(F32, 2, 4, columns),
            vmem(F32, 4, 4, columns),
            vmem(F32, 4, 4, columns),
            vmem(F32, 4, images, width),
            vmem(BF16, 8, images, depth),
            vmem(BF16, 8, images, depth),
            vmem(F32, 3, depth, own),
            vmem(F32, 3, depth, own),
            dma(3 * count),
            dma(3 * count),
            dma(count),
            dma(7),
            dma(rows),
            dma(copies),
            dma(copies),
        ],
        compiler_params=pltpu.CompilerParams(vmem_limit_bytes=VMEM_LIMIT, collective_id=3, has_side_effects=True),
        cost_estimate=pl.CostEstimate(
            flops=20 * rows * heads * length * length * 128,
            bytes_accessed=16 * rows * heads * length * size,
            transcendentals=rows * heads * length * length,
        ),
    )(
        col,
        row,
        packed,
        packed,
        packed,
        out,
        grad_out,
        lse,
        normed,
        proj_own,
        proj_low,
        down,
        down_tail,
        seg,
        table,
        slot_sums,
        image_index,
        conditioning,
        *biases,
        tokens,
        grad_middle,
        weight,
        ada,
    )


def forward_kernel(
    block,
    image_index,
    seg,
    fill,
    conditioning,
    ada_bias,
    qv_bias,
    proj_bias,
    tokens,
    ada,
    weight,
    proj,
    cotangent,
    normed_ref,
    packed_ref,
    attended_ref,
    features_ref,
    branch_ref,
    middle_ref,
    inner_ref,
    grad_ref,
    inner_turned_ref,
    grad_turned_ref,
    table_ref,
    code_row,
    code_col,
    lse_ref,
    bias_sum,
    here,
    normed_all,
    packed_all,
    ada_here,
    windows,
    turned,
    own_weight,
    bias_turned,
    mod_all,
    table,
    seg_all,
    attended_all,
    attended_got,
    flat,
    features_all,
    proj_here,
    cotangent_here,
    branch_all,
    middle_all,
    inner_all,
    grad_all,
    inner_turned,
    grad_turned,
    rows_turned,
    load_sem,
    own_sem,
    mod_sent,
    mod_came,
    sent,
    came,
    forward_sent,
    forward_came,
    heads_sent,
    heads_came,
    heads_kept,
    store_sem,
    last_sem,
):
    rows, _, local, width = here.shape
    _, parts, heads, size, length = packed_all.shape
    own, depth, half = heads * size, width // 8, local // 2
    columns = ada_here.shape[0]
    images, slots = conditioning.shape[0], image_index.shape[1]
    slot_col = slot_column(slots)
    scale = size**-0.5 * LOG2E
    seq = lax.axis_index("seq")
    core = lax.rem(lax.axis_index("rows"), 2)
    places = [seq] + peers_of(seq)
    peers = [{"seq": place} for place in places]

    greet(peers[1:])

    def direct(r, m):
        index = r * 2 + m - 1
        return send_to(tokens.at[r], here.at[r, m], sent.at[index], came.at[index], peers[m])

    def forward(r, m):
        part = pl.ds(0, half) if m == 1 else pl.ds(half, half)
        index = r * 2 + m - 1
        return send_to(
            here.at[r, 3 - m, part], here.at[r, 3, part], forward_sent.at[index], forward_came.at[index], peers[m]
        )

    def go(copies):
        for copy in copies:
            copy.start()

    def end(copies):
        for copy in copies:
            copy.wait()

    go([direct(0, m) for m in (1, 2)])
    own_copies = [pltpu.make_async_copy(tokens.at[r], here.at[r, 0], own_sem.at[r]) for r in range(rows)]
    load_ada = pltpu.make_async_copy(ada, ada_here, load_sem.at[0])
    load_windows = []
    for part in range(3):
        lanes = pl.ds(pl.multiple_of(part * width + seq * 256, 128), 384)
        load_windows.append(pltpu.make_async_copy(weight.at[:, lanes], windows.at[part], load_sem.at[1 + part]))
    load_proj = pltpu.make_async_copy(proj, proj_here, load_sem.at[4])
    load_cotangent = pltpu.make_async_copy(cotangent, cotangent_here, load_sem.at[5])
    go([load_ada] + load_windows + own_copies + [load_proj, load_cotangent])

    value = conditioning[...].astype(F32)
    low = (value / (1.0 + jnp.exp(-value))).astype(BF16)
    load_ada.wait()
    mod_all[seq] = lax.dot_general(low, ada_here[...], (((1,), (1,)), ((), ())), preferred_element_type=F32)
    mod_copies = [
        send_to(mod_all.at[seq], mod_all.at[seq], mod_sent.at[m - 1], mod_came.at[m - 1], peers[m]) for m in range(1, 4)
    ]
    go(mod_copies)

    for m in range(4):
        lanes = pl.ds(pl.multiple_of(places[m] * local, 128), local)
        found = seg[:, lanes]
        where = places[m] * local + lax.broadcasted_iota(jnp.int32, (1, local), 1)
        for r in range(rows):
            code = jnp.where(where < fill[r], found[r : r + 1], -1 - where)
            seg_all[r, m] = found[r : r + 1]
            code_row[r, :, m * local : (m + 1) * local] = code
            column = jnp.broadcast_to(code.astype(F32), (128, local)).T[:, :1]
            code_col[r, m * local : (m + 1) * local] = column.astype(jnp.int32)

    for part in range(3):
        load_windows[part].wait()
        turned[...] = windows[part].astype(F32).T
        own_weight[part * own : (part + 1) * own] = turned[pl.ds(pl.multiple_of(seq * 32, 8), own), :].astype(BF16)
    window = qv_bias[:, pl.ds(pl.multiple_of(seq * 256, 128), 384)].astype(F32)
    bias_turned[...] = jnp.concatenate([window, jnp.zeros((6, 384), F32)], axis=0).T
    bias = bias_turned[pl.ds(pl.multiple_of(seq * 32, 8), own), :]
    bias = jnp.concatenate([bias[:, 0:1], jnp.zeros((own, 1), F32), bias[:, 1:2]], axis=0)

    end([direct(0, m) for m in (1, 2)])
    go([forward(0, m) for m in (1, 2)] + [direct(1, m) for m in (1, 2)])

    end(mod_copies)
    bias_all = ada_bias[...].astype(F32).reshape(1, 4 * columns)
    proj_line = proj_bias[...].astype(F32).reshape(1, width)
    for place in range(4):
        lanes = slice(place * columns, (place + 1) * columns)
        table[:, lanes] = mod_all[place] + bias_all[:, lanes]
    stacked = jnp.concatenate(split_low(table[...]), axis=0)
    image_col = lax.rem(lax.broadcasted_iota(jnp.int32, (3 * images, slots), 0), images)
    for r in range(rows):
        picked = (image_col == image_index[r : r + 1]).astype(BF16)
        table_ref[r] = lax.dot_general(picked, stacked, (((0,), (0,)), ((), ())), preferred_element_type=F32)

    def stores(r, m):
        index = r * 4 + m
        lanes = pl.ds(m * local, local)
        return (
            pltpu.make_async_copy(normed_all.at[r, m], normed_ref.at[r, m], store_sem.at[0, index]),
            pltpu.make_async_copy(packed_all.at[r, :, :, :, lanes], packed_ref.at[r, :, :, :, lanes], store_sem.at[1, index]),
        )

    def work(r, m):
        mods = per_token(slot_col, seg_all[r, m], table_ref[r, :, : 2 * width])
        normal, _ = normalize(here[r, m].astype(F32))
        normed = (normal * (1.0 + mods[:, width:]) + mods[:, :width]).astype(BF16)
        normed_all[r, m] = normed
        mixed = lax.dot_general(own_weight[...], normed, (((1,), (1,)), ((), ())), preferred_element_type=F32)
        mixed = (mixed + bias).astype(BF16)
        for part in range(parts):
            for head in range(heads):
                start = (part * heads + head) * size
                packed_all[r, part, head, :, m * local : (m + 1) * local] = mixed[start : start + size]
        go(stores(r, m))

    def to_peer(r, h, m):
        source = attended_all.at[r, h, :, pl.ds(m * local, local)]
        place = (r * heads + h) * 3 + m - 1
        return send_to(source, attended_got.at[r, seq, h], heads_sent.at[place], heads_came.at[place], peers[m])

    def to_self(r, h):
        source = attended_all.at[r, h, :, pl.ds(0, local)]
        return pltpu.make_async_copy(source, attended_got.at[r, seq, h], heads_kept.at[r * heads + h])

    def attend_head(r, h):
        keys = packed_all[r, 1, h].astype(F32).T.astype(BF16)
        values = packed_all[r, 2, h]
        codes = code_col[r]
        for step in range(length // block):
            lanes = pl.ds(step * block, block)
            scores = jnp.dot(keys, packed_all[r, 0, h, :, lanes], preferred_element_type=F32)
            scores = jnp.where(codes == code_row[r, :, lanes], scores * scale, -1e30)
            peak = jnp.max(scores, axis=0, keepdims=True)
            raised = jnp.exp2(scores - peak)
            total = jnp.sum(raised, axis=0, keepdims=True)
            probs = (raised * (1.0 / total)).astype(BF16)
            attended_all[r, h, :, lanes] = jnp.dot(values, probs, preferred_element_type=F32).astype(BF16)
            lse_ref[r, h, :, lanes] = peak + jnp.log2(total)
        to_self(r, h).start()
        for m in range(1, 4):
            to_peer(r, h, m).start()

    def attend_row(r, first, last):
        @pl.loop(first, last)
        def _(h):
            attend_head(r, h)

    def turn(values, target, r):
        rows_turned[...] = values.T
        for place in range(4):
            for order in range(2):
                first = pl.multiple_of((2 * place + (core if order == 0 else 1 - core)) * depth, 8)
                start = (4 * order + place) * depth
                target[r, start : start + depth] = rows_turned[pl.ds(first, depth), :].astype(BF16)

    end(own_copies)
    for m in range(3):
        work(0, m)
    end([load_proj, load_cotangent])
    for r in range(rows):
        gate_b = per_token(slot_col, seg_all[r, 0], table_ref[r, :, 5 * width :])
        grad = cotangent_here[r].astype(F32) * gate_b
        grad_all[r] = grad.astype(BF16)
        turn(grad, grad_turned, r)
        sums = jnp.sum(grad.astype(BF16).astype(F32), axis=0, keepdims=True)
        if r == 0:
            bias_sum[...] = sums
        else:
            bias_sum[...] += sums
    def last_stores(r):
        lines, lanes = pl.ds(r * local, local), pl.ds(r * local, local)
        pairs = (
            (attended_all.at[r], attended_ref.at[r]),
            (features_all.at[r], features_ref.at[r]),
            (branch_all.at[r], branch_ref.at[r]),
            (middle_all.at[r], middle_ref.at[r]),
            (inner_all.at[r], inner_ref.at[lines]),
            (grad_all.at[r], grad_ref.at[lines]),
            (inner_turned.at[r], inner_turned_ref.at[:, lanes]),
            (grad_turned.at[r], grad_turned_ref.at[:, lanes]),
        )
        return [pltpu.make_async_copy(source, target, last_sem.at[r, k]) for k, (source, target) in enumerate(pairs)]

    def project(r):
        for h in range(heads):
            to_self(r, h).wait()
            for m in range(1, 4):
                to_peer(r, h, m).wait()
        for place in range(4):
            for h in range(heads):
                start = (place * heads + h) * size
                flat[start : start + size] = attended_got[r, place, h].astype(F32)
        features = flat[...].astype(BF16)
        features_all[r] = features
        mods = per_token(slot_col, seg_all[r, 0], table_ref[r, :, 2 * width : 5 * width])
        gate_a, shift_b, scale_b = (mods[:, k * width : (k + 1) * width] for k in range(3))
        branch = lax.dot_general(features, proj_here[...], (((0,), (0,)), ((), ())), preferred_element_type=F32) + proj_line
        middle = here[r, 0].astype(F32) + gate_a * branch
        branch_all[r] = branch
        middle_all[r] = middle
        normed = normalize(middle)[0] * (1.0 + scale_b) + shift_b
        inner_all[r] = normed.astype(BF16)
        turn(normed, inner_turned, r)
        go(last_stores(r))
    end([forward(0, m) for m in (1, 2)])
    work(0, 3)
    attend_row(0, 0, heads // 2)
    end([direct(1, m) for m in (1, 2)])
    go([forward(1, m) for m in (1, 2)])
    attend_row(0, heads // 2, heads)
    for m in range(3):
        work(1, m)
    end([forward(1, m) for m in (1, 2)])
    work(1, 3)
    attend_row(1, 0, heads)
    project(0)
    project(1)
    for r in range(rows):
        for m in range(4):
            end(stores(r, m))
        end(last_stores(r))


def before_feed_forward(image_index, seg, fill, conditioning, ada_bias, qv_bias, proj_bias, tokens, ada, weight, proj, cotangent):
    rows, local, width = tokens.shape
    length = 4 * local
    images, slots = conditioning.shape[0], image_index.shape[1]
    heads, size = HEADS // 4, width // HEADS
    columns = ada.shape[0]
    shape = jax.ShapeDtypeStruct
    vmem = lambda dtype, *dims: pltpu.VMEM(dims, dtype)
    near, far = pl.BlockSpec(memory_space=pltpu.VMEM), pl.BlockSpec(memory_space=pl.ANY)
    dma = lambda *dims: pltpu.SemaphoreType.DMA(dims)
    return pl.pallas_call(
        partial(forward_kernel, 512),
        in_specs=[near] * 2 + [pl.BlockSpec(memory_space=pltpu.SMEM)] + [near] * 4 + [far] * 5,
        out_specs=[far] * 10 + [near] * 5,
        out_shape=[
            shape((rows, 4, local, width), BF16),
            shape((rows, 3, heads, size, length), BF16),
            shape((rows, heads, size, length), BF16),
            shape((rows, width, local), BF16),
            shape((rows, local, width), F32),
            shape((rows, local, width), F32),
            shape((rows * local, width), BF16),
            shape((rows * local, width), BF16),
            shape((width, rows * local), BF16),
            shape((width, rows * local), BF16),
            shape((rows, slots, 6 * width), F32),
            shape((rows, 1, length), jnp.int32),
            shape((rows, length, 1), jnp.int32),
            shape((rows, heads, 1, length), F32),
            shape((1, width), F32),
        ],
        scratch_shapes=[
            vmem(BF16, rows, 4, local, width),
            vmem(BF16, rows, 4, local, width),
            vmem(BF16, rows, 3, heads, size, length),
            vmem(BF16, columns, width),
            vmem(BF16, 3, width, 384),
            vmem(F32, 384, width),
            vmem(BF16, 3 * heads * size, width),
            vmem(F32, 384, 8),
            vmem(F32, 4, images, columns),
            vmem(F32, images, 6 * width),
            vmem(jnp.int32, rows, 4, 1, local),
            vmem(BF16, rows, heads, size, length),
            vmem(BF16, rows, 4, heads, size, local),
            vmem(F32, width, local),
            vmem(BF16, rows, width, local),
            vmem(BF16, width, width),
            vmem(BF16, rows, local, width),
            vmem(F32, rows, local, width),
            vmem(F32, rows, local, width),
            vmem(BF16, rows, local, width),
            vmem(BF16, rows, local, width),
            vmem(BF16, rows, width, local),
            vmem(BF16, rows, width, local),
            vmem(F32, width, local),
            dma(6),
            dma(rows),
            dma(3),
            dma(3),
            dma(2 * rows),
            dma(2 * rows),
            dma(2 * rows),
            dma(2 * rows),
            dma(3 * rows * heads),
            dma(3 * rows * heads),
            dma(rows * heads),
            dma(2, 4 * rows),
            dma(rows, 8),
        ],
        compiler_params=pltpu.CompilerParams(vmem_limit_bytes=VMEM_LIMIT, collective_id=6, has_side_effects=True),
        cost_estimate=pl.CostEstimate(flops=2 * 10**10, bytes_accessed=4 * 10**7, transcendentals=0),
    )(image_index, seg, fill, conditioning, ada_bias, qv_bias, proj_bias, tokens, ada, weight, proj, cotangent)


def hand_out_kernel(places, *refs):
    count = len(places)
    sources, targets = refs[:count], refs[count:]
    held, sems = refs[-count - 1 : -1], refs[-1]
    loads = [pltpu.make_async_copy(sources[k], held[k], sems.at[0, k]) for k in range(count)]
    stores = []
    for k, (index, first, size) in enumerate(places):
        target = targets[index] if size is None else targets[index].at[:, pl.ds(first, size)]
        stores.append(pltpu.make_async_copy(held[k], target, sems.at[1, k]))
    for copy in loads:
        copy.start()
    for load, store in zip(loads, stores):
        load.wait()
        store.start()
    for copy in stores:
        copy.wait()


def hand_out(*results):
    arrays, places, shapes = [], [], []
    for index, result in enumerate(results):
        first = 0
        pieces = result if isinstance(result, tuple) else (result,)
        for piece in pieces:
            size = piece.shape[1] if len(pieces) > 1 else None
            arrays.append(piece)
            places.append((index, first, size))
            first += size or 0
        shape = pieces[0].shape if len(pieces) == 1 else (pieces[0].shape[0], first)
        shapes.append(jax.ShapeDtypeStruct(shape, pieces[0].dtype))
    far = pl.BlockSpec(memory_space=pl.ANY)
    return pl.pallas_call(
        partial(hand_out_kernel, tuple(places)),
        in_specs=[far] * len(arrays),
        out_specs=[far] * len(shapes),
        out_shape=shapes,
        scratch_shapes=[pltpu.VMEM(array.shape, array.dtype) for array in arrays]
        + [pltpu.SemaphoreType.DMA((2, len(arrays)))],
        compiler_params=pltpu.CompilerParams(vmem_limit_bytes=VMEM_LIMIT),
    )(*arrays)


def gather_seq(values):
    count = lax.axis_size("seq")
    if count == 4:
        first, second = swap(values, "seq", 1), swap(values, "seq", 2)
        half = values.shape[0] // 2
        third = jnp.concatenate([swap(second[:half], "seq", 1), swap(first[half:], "seq", 2)], axis=0)
        return [values, first, second, third]
    return [values] + [swap(values, "seq", m) for m in range(1, count)]


def exchange_seq(blocks):
    return [blocks[0]] + [swap(blocks[m], "seq", m) for m in range(1, len(blocks))]


def in_order(blocks, axis):
    index = lax.axis_index("seq")
    stacked = jnp.stack(blocks, axis=axis)
    return flip_blocks(stacked, axis, index)


class Halving:
    def __init__(self, blocks, low_first):
        self.blocks = dict(enumerate(blocks))
        bits = [1 << k for k in range(len(blocks).bit_length() - 1)]
        self.bits = bits if low_first else bits[::-1]

    def send(self):
        self.bit = self.bits.pop(0)
        self.kept = [m for m in self.blocks if not m & self.bit]
        return jnp.stack([self.blocks[m | self.bit] for m in self.kept]).astype(BF16)

    def move(self, sent):
        return swap(sent, "seq", self.bit)

    def add(self, came):
        self.blocks = {m: self.blocks[m] + came[k].astype(F32) for k, m in enumerate(self.kept)}


class Spreading:
    def __init__(self, pick):
        chip, chips = lax.axis_index("rows") // 2, lax.axis_size("rows") // 2
        self.own = pick(chip)
        self.sent = [pick(chip ^ m).astype(BF16) for m in range(1, chips)]

    def move(self):
        self.came = [swap(block, "rows", 2 * (m + 1)) for m, block in enumerate(self.sent)]

    def total(self):
        total = self.own
        for block in self.came:
            total = total + block.astype(F32)
        return total


def columns_of(values, index, size):
    return lax.dynamic_slice_in_dim(values, index * size, size, values.ndim - 1)


def lines_of(values, index, size):
    return lax.dynamic_slice_in_dim(values, index * size, size, 0)


def tied(*values):
    return lax.optimization_barrier(values)


def on_square(
    tokens,
    conditioning,
    segment_ids,
    image_index,
    row_fill,
    ada_weight,
    ada_bias,
    qkv_weight,
    qv_bias,
    proj_weight,
    proj_bias,
    up_weight,
    up_bias,
    down_weight,
    down_bias,
    cotangent,
):
    row_count, local_len, width = tokens.shape
    seq_count, groups = lax.axis_size("seq"), lax.axis_size("rows")
    seq_index, row_index = lax.axis_index("seq"), lax.axis_index("rows")
    chips, core = groups // 2, row_index % 2
    full_len = local_len * seq_count
    token_count = row_count * local_len
    heads_dev = HEADS // seq_count
    head_size = width // HEADS
    own = heads_dev * head_size
    image_count = conditioning.shape[0]
    hidden_size = up_weight.shape[1]
    depth = width // groups

    (
        normed_all,
        packed,
        attended,
        attended_tok,
        branch_a,
        middle,
        normed_b,
        grad_out,
        normed_turned,
        grad_turned,
        slot_mod,
        code_row,
        code_col,
        log_totals,
        part_down_bias,
    ) = before_feed_forward(
        image_index,
        segment_ids,
        row_fill,
        conditioning,
        ada_bias,
        qv_bias,
        proj_bias,
        tokens,
        ada_weight.T,
        qkv_weight,
        proj_weight,
        cotangent,
    )
    normed_all = normed_all.reshape(row_count, full_len, width)
    out_sum, grad_sum, part_up_bias, up_main, down_main, *left = feed_forward_reduce(
        normed_b, grad_out, normed_turned, grad_turned, up_weight, down_weight, up_bias
    )
    block_out, grad_middle, grad_view, slot_sums, part_proj_bias, proj_own, proj_low, up_tail, down_tail = after_feed_forward(
        segment_ids,
        slot_mod,
        attended_tok,
        proj_weight,
        down_bias,
        out_sum,
        grad_sum,
        middle,
        branch_a,
        cotangent,
        left,
    )
    grad_view = grad_view.reshape(row_count, heads_dev, head_size, full_len)
    (
        grad_tokens,
        grad_proj_weight,
        grad_down_weight,
        grad_ada_weight,
        grad_cond,
        grad_ada_bias,
        grad_qv_bias,
        grad_proj_bias,
        grad_up_bias,
        grad_down_bias,
        grad_qkv_weight,
    ) = attend_back_and_finish(
        packed,
        attended,
        grad_view,
        log_totals,
        code_col,
        code_row,
        normed_all,
        proj_own,
        proj_low,
        down_main,
        down_tail,
        segment_ids,
        slot_mod,
        slot_sums,
        image_index,
        conditioning,
        (part_proj_bias, part_up_bias, part_down_bias),
        tokens,
        grad_middle,
        qkv_weight,
        ada_weight.T,
    )
    results = list(hand_out(
        block_out,
        grad_tokens,
        grad_cond,
        grad_ada_weight,
        grad_ada_bias,
        grad_qkv_weight,
        grad_qv_bias,
        grad_proj_weight,
        grad_proj_bias,
        (up_main, up_tail),
        grad_up_bias,
        grad_down_weight,
        grad_down_bias,
    ))
    results[11] = results[11].T
    return tuple(results)


def on_device(
    tokens,
    conditioning,
    segment_ids,
    image_index,
    row_fill,
    ada_weight,
    ada_bias,
    qkv_weight,
    qv_bias,
    proj_weight,
    proj_bias,
    up_weight,
    up_bias,
    down_weight,
    down_bias,
    cotangent,
):
    row_count, local_len, width = tokens.shape
    seq_count, groups = lax.axis_size("seq"), lax.axis_size("rows")
    seq_index, row_index = lax.axis_index("seq"), lax.axis_index("rows")
    chips, core = groups // 2, row_index % 2
    full_len = local_len * seq_count
    token_count = row_count * local_len
    heads_dev = HEADS // seq_count
    head_size = width // HEADS
    own = heads_dev * head_size
    image_count = conditioning.shape[0]
    hidden_size = up_weight.shape[1]
    depth = width // groups

    tokens_all = jnp.concatenate(gather_seq(tokens), axis=1)
    order = lax.iota(jnp.int32, seq_count) ^ seq_index
    seg_blocks = flip_blocks(segment_ids.reshape(row_count, seq_count, local_len), 1, seq_index)
    seg_all = seg_blocks.reshape(row_count, full_len)
    places = (order[:, None] * local_len + lax.iota(jnp.int32, local_len)).reshape(1, full_len)
    codes = jnp.where(places < row_fill[:, None], seg_all, -1 - places)
    code_col, code_row = codes[:, :, None], codes[:, None, :]

    qkv_own = jnp.concatenate(
        [lax.dynamic_slice_in_dim(qkv_weight, part * width + seq_index * own, own, 1).T for part in range(3)], axis=0
    )
    bias_own = lax.dynamic_slice_in_dim(qv_bias.astype(F32), seq_index * own, own, 1)
    bias_own = jnp.concatenate([bias_own[0], jnp.zeros((own,), F32), bias_own[1]])

    cond_wide = conditioning.astype(F32)
    cond_low = jax.nn.silu(cond_wide).astype(BF16)
    mod_part = jnp.dot(cond_low, ada_weight, preferred_element_type=F32)
    modulation = lax.all_gather(mod_part, "seq", axis=1, tiled=True) + ada_bias.astype(F32)
    cond_cols = cond_low.reshape(image_count, groups, depth).transpose(1, 0, 2)
    local_seg = lax.dynamic_slice_in_dim(segment_ids, seq_index * local_len, local_len, 1)
    slot_ids = lax.iota(jnp.int32, image_index.shape[1])
    slot_mod = jnp.take(modulation, image_index, axis=0)

    normed_all, packed = project_qkv(
        tokens_all, seg_all, slot_mod[:, :, : 2 * width], qkv_own, bias_own, heads_dev, min(256, full_len)
    )
    square = seq_count == 4 and chips == 4
    attended, log_totals, *attended_sent = attend(packed, code_col, code_row, 512, square)

    slot_pick = (local_seg[:, :, None] == slot_ids).astype(F32)
    mod_tok = jnp.einsum("rts,rse->rte", slot_pick, slot_mod, precision=lax.Precision.HIGHEST)
    shift_a, scale_a, gate_a, shift_b, scale_b, gate_b = jnp.split(mod_tok, 6, axis=-1)
    tokens_wide = tokens.astype(F32)
    upstream = cotangent.astype(F32)
    grad_branch_b = (upstream * gate_b).astype(BF16)
    part_down_bias = jnp.sum(grad_branch_b.astype(F32), axis=(0, 1))
    grad_out = grad_branch_b.reshape(token_count, width)
    grad_turned = turn_halves(grad_out, seq_count, core)

    def by_block(values):
        return [values[..., m * local_len : (m + 1) * local_len] for m in range(seq_count)]

    if square:
        attended_tok = attended_sent[0]
    else:
        attended_tok = in_order(exchange_seq(by_block(attended.reshape(row_count, own, full_len))), 1)
    attended_tok = attended_tok.reshape(row_count, width, local_len)
    branch_a = jnp.einsum(
        "rft,fe->rte", attended_tok, proj_weight, preferred_element_type=F32
    ) + proj_bias.astype(F32)
    middle = tokens_wide + gate_a * branch_a
    normed_b = modulate(middle, shift_b, scale_b).astype(BF16).reshape(token_count, width)
    normed_turned = turn_halves(normed_b, chips, core)

    if square:
        out_sum, grad_sum, part_up_bias, grad_up_weight, down_turned = feed_forward_reduce(
            normed_b, grad_out, normed_turned, grad_turned, up_weight, down_weight, up_bias.astype(F32)
        )
        part_up_bias = part_up_bias.reshape(1, hidden_size)
    else:
        out_sum, grad_sum, up_keep, up_send, down_keep, down_send, part_up_bias = feed_forward(
            normed_b, grad_out, normed_turned, grad_turned, up_weight, down_weight, up_bias.astype(F32)[None], 512
        )
        up_came, down_came = swap(up_send, "rows", 1), swap(down_send, "rows", 1)
    branch_b = out_sum.reshape(row_count, local_len, width) + down_bias.astype(F32)
    grad_normed_b = grad_sum.reshape(row_count, local_len, width)
    block_out = (middle + gate_b * branch_b).astype(BF16)
    grad_gate_b = upstream * branch_b
    _, norm_back_b = jax.vjp(modulate, middle, shift_b, scale_b)
    grad_mid_norm, grad_shift_b, grad_scale_b = norm_back_b(grad_normed_b)
    grad_middle = upstream + grad_mid_norm
    grad_branch_a = (grad_middle * gate_a).astype(BF16)
    grad_gate_a = grad_middle * branch_a
    part_proj_bias = jnp.sum(grad_branch_a.astype(F32), axis=(0, 1))
    grad_attended = jnp.einsum(
        "fe,rte->rft", proj_weight, grad_branch_a, preferred_element_type=F32
    ).astype(BF16)
    heads_blocks = [lax.dynamic_slice_in_dim(grad_attended, (seq_index ^ m) * own, own, 1) for m in range(seq_count)]
    grad_heads_in = jnp.concatenate(exchange_seq(heads_blocks), axis=2)
    grad_view = grad_heads_in.reshape(row_count, heads_dev, head_size, full_len)

    part_proj = jnp.einsum("rte,rft->ef", grad_branch_a, attended_tok, preferred_element_type=F32)
    proj_view = part_proj.reshape(seq_count, 2, depth * groups // (2 * seq_count), width)
    proj_keep = lax.dynamic_index_in_dim(proj_view, core, 1, keepdims=False)
    proj_send = lax.dynamic_index_in_dim(proj_view, 1 - core, 1, keepdims=False).astype(BF16)
    proj_came = swap(proj_send, "rows", 1).reshape(width // 2, width)
    proj_keep = proj_keep.reshape(width // 2, width)
    up_size, down_size = hidden_size // seq_count, width // (2 * seq_count)
    proj_blocks = [
        lines_of(proj_keep, seq_index ^ m, down_size) + lines_of(proj_came, seq_index ^ m, down_size).astype(F32)
        for m in range(seq_count)
    ]
    if square:
        proj_sent = [block.astype(BF16) for block in proj_blocks[1:]]
        grad_view, *proj_sent = tied(grad_view, *proj_sent)
        proj_total = proj_blocks[0]
        for m in range(1, seq_count):
            proj_total = proj_total + swap(proj_sent[m - 1], "seq", m).astype(F32)
    else:
        ups = Halving(
            [
                columns_of(up_keep, seq_index ^ m, up_size) + columns_of(up_came, seq_index ^ m, up_size).astype(F32)
                for m in range(seq_count)
            ],
            True,
        )
        downs = Halving(
            [
                jnp.concatenate(
                    [
                        lines_of(down_keep, seq_index ^ m, down_size)
                        + lines_of(down_came, seq_index ^ m, down_size).astype(F32),
                        proj_blocks[m],
                    ],
                    axis=1,
                )
                for m in range(seq_count)
            ],
            False,
        )
        up_sent, down_sent = ups.send(), downs.send()
        up_came, down_came = ups.move(up_sent), downs.move(down_sent)

    grad_heads, *grad_sent = attend_back(
        packed, attended, grad_view, log_totals, code_col, code_row, 256, 512, square
    )
    grad_own = grad_heads.reshape(row_count, 3 * own, full_len)
    if square:
        grad_flat = grad_sent[0]
    else:
        grad_blocks = exchange_seq(by_block(grad_own))
        grad_flat = in_order([block.reshape(row_count, 3, own, local_len) for block in grad_blocks], 2)
    grad_flat = grad_flat.reshape(row_count, 3 * width, local_len)

    qkv_keep, qkv_send, own_sums = qkv_weight_grad(grad_own, normed_all)
    down_part, proj_part = hidden_size // chips, width // chips
    if square:
        proj_spread = Spreading(lambda chip: columns_of(proj_total, chip, proj_part))
        grad_flat, qkv_send, *proj_spread.sent = tied(grad_flat, qkv_send, *proj_spread.sent)
        proj_spread.move()
    else:
        while ups.bits:
            ups.add(up_came)
            downs.add(down_came)
            up_came, down_came = ups.move(ups.send()), downs.move(downs.send())
        ups.add(up_came)
        downs.add(down_came)
        up_total, down_total = ups.blocks[0], downs.blocks[0][:, :hidden_size]
        proj_total = downs.blocks[0][:, hidden_size:]
        up_spread = Spreading(lambda chip: lines_of(up_total, chip, depth))
        down_spread = Spreading(
            lambda chip: jnp.concatenate(
                [columns_of(down_total, chip, down_part), columns_of(proj_total, chip, proj_part)], axis=1
            )
        )
        up_spread.move()
        down_spread.move()
    qkv_came = swap(qkv_send, "rows", 1)
    grad_normed_a = jnp.einsum("rft,df->rtd", grad_flat, qkv_weight, preferred_element_type=F32)
    _, norm_back_a = jax.vjp(modulate, tokens_wide, shift_a, scale_a)
    grad_tok_norm, grad_shift_a, grad_scale_a = norm_back_a(grad_normed_a)
    grad_tokens = grad_middle + grad_tok_norm
    grad_mod_tok = jnp.concatenate(
        [grad_shift_a, grad_scale_a, grad_gate_a, grad_shift_b, grad_scale_b, grad_gate_b], axis=-1
    )
    slot_grads = jnp.einsum("rts,rte->rse", slot_pick, grad_mod_tok, precision=lax.Precision.HIGHEST)
    image_pick = (image_index[:, :, None] == lax.iota(jnp.int32, image_count)).astype(F32)
    grad_modulation = jnp.einsum("rsi,rse->ie", image_pick, slot_grads, precision=lax.Precision.HIGHEST)

    own_sums = own_sums.reshape(3, own)
    part_qv = lax.dynamic_update_slice(
        jnp.zeros((2, width), F32), jnp.stack([own_sums[0], own_sums[2]]), (0, seq_index * own)
    )
    small = jnp.concatenate([part_qv.reshape(-1), part_proj_bias, part_up_bias[0], part_down_bias])
    columns = ada_weight.shape[1]
    lines = -(-small.size // (seq_count * columns))
    room = seq_count * columns * lines
    small = jnp.pad(small, (0, room - small.size)).reshape(seq_count, lines, columns)
    mod_view = grad_modulation.reshape(image_count, seq_count, columns).transpose(1, 0, 2)
    joined = jnp.concatenate(
        [mod_view, jnp.zeros((seq_count, 1, columns), F32), small, jnp.zeros((seq_count, 7 - lines, columns), F32)], axis=1
    )
    qkv_both = qkv_keep + qkv_came.astype(F32)
    qkv_spread = Spreading(lambda chip: lax.dynamic_index_in_dim(qkv_both, chip, 0, keepdims=False))
    joined, *qkv_spread.sent = tied(joined, *qkv_spread.sent)
    qkv_spread.move()
    if square:
        turned = jnp.concatenate([down_turned, proj_spread.total()], axis=1)
    else:
        grad_up_weight, turned = up_spread.total(), down_spread.total()
    half = down_part // 2
    cut = lambda index: jnp.concatenate(
        [columns_of(turned[:, :down_part], index, half), columns_of(turned[:, down_part:], index, proj_part // 2)], axis=1
    )
    core_keep, core_sent = cut(core), cut(1 - core)
    joined, core_sent = tied(joined, core_sent)
    core_came = swap(core_sent, "rows", 1)
    grad_ada_weight, cond_sum, bias_sums = finish(joined, ada_weight, cond_cols, image_count)
    _, silu_back = jax.vjp(jax.nn.silu, cond_wide)
    grad_cond = silu_back(cond_sum)[0]
    grad_ada_bias = bias_sums[:, 0].reshape(-1)
    small = bias_sums[:, 1 : 1 + lines].reshape(-1)
    grad_qv_bias = small[: 2 * width].reshape(2, width)
    grad_proj_bias = small[2 * width : 3 * width]
    grad_up_bias = small[3 * width : 3 * width + hidden_size]
    grad_down_bias = small[3 * width + hidden_size : 4 * width + hidden_size]

    pair = flip_blocks(jnp.stack([core_keep, core_came]), 0, core).reshape(-1, core_keep.shape[1])
    grad_down_weight, grad_proj_weight = pair[:, :half].T, pair[:, half:].T

    qkv_total = qkv_spread.total()
    pieces = []
    for place in range(3):
        pairs = [((3 * target + place) % seq_count, target) for target in range(seq_count)]
        part_of = [0] * seq_count
        for source, target in pairs:
            part_of[source] = (3 * target + place) // seq_count
        chosen = columns_of(qkv_total, jnp.array(part_of, jnp.int32)[seq_index], own)
        pieces.append(lax.ppermute(chosen, "seq", pairs))
    grad_qkv_weight = jnp.concatenate(pieces, axis=1)
    return (
        block_out,
        grad_tokens,
        grad_cond,
        grad_ada_weight,
        grad_ada_bias,
        grad_qkv_weight,
        grad_qv_bias,
        grad_proj_weight,
        grad_proj_bias,
        grad_up_weight,
        grad_up_bias,
        grad_down_weight,
        grad_down_bias,
    )


def solution(mesh):
    in_specs = (
        P("rows", "seq", None),
        P("rows", None),
        P("rows", None),
        P("rows", None),
        P("rows"),
        P(None, "seq"),
        P(),
        P(),
        P(),
        P(),
        P(),
        P(),
        P(),
        P(),
        P(),
        P("rows", "seq", None),
    )
    out_specs = (
        P("rows", "seq", None),
        P("rows", "seq", None),
        P("rows", None),
        P("rows", "seq"),
        P(),
        P("rows", "seq"),
        P(),
        P("rows", "seq"),
        P(),
        P("rows", "seq"),
        P(),
        P("rows", "seq"),
        P(),
    )
    square = mesh.shape["seq"] == 4 and mesh.shape["rows"] == 8
    return jax.shard_map(
        on_square if square else on_device, mesh=mesh, in_specs=in_specs, out_specs=out_specs, check_vma=False
    )
```

```python
from functools import partial
import math

import jax
import jax.numpy as jnp
from jax import lax
from jax.experimental import pallas as pl
from jax.experimental.pallas import tpu as pltpu
from jax.sharding import PartitionSpec as P

HEADS = 16
LOG2E = math.log2(math.e)
VMEM_LIMIT = 60 << 20
BF16 = jnp.bfloat16
F32 = jnp.float32

norm_eps = 1e-06


def modulate(values, offset, factor):
    center = values - jnp.mean(values, axis=-1, keepdims=True)
    spread = jnp.mean(center * center, axis=-1, keepdims=True)
    return center * lax.rsqrt(spread + norm_eps) * (1.0 + factor) + offset


def gelu_tanh(values):
    return jax.nn.gelu(values, approximate=True)


def swap(values, axis, mask):
    count = lax.axis_size(axis)
    return lax.ppermute(values, axis, [(i, i ^ mask) for i in range(count)])


def flip_blocks(values, axis, mask):
    return jnp.take(values, lax.iota(jnp.int32, values.shape[axis]) ^ mask, axis=axis)


def qkv_kernel(slot_row, seg, mod, tokens, weight, bias, normed_ref, qkv_ref):
    width = tokens.shape[-1]
    values = tokens[0].astype(F32)
    picked = (seg[0] == slot_row[...]).astype(BF16)
    table = mod[0]
    high = table.astype(BF16)
    rest = table - high.astype(F32)
    middle = rest.astype(BF16)
    last = (rest - middle.astype(F32)).astype(BF16)
    stacked = jnp.concatenate([high, middle, last], axis=0)
    per_token = jnp.dot(picked, stacked, preferred_element_type=F32)
    normed = modulate(values, per_token[:, :width], per_token[:, width:]).astype(BF16)
    normed_ref[0] = normed
    mixed = lax.dot_general(weight[...], normed, (((1,), (1,)), ((), ())), preferred_element_type=F32)
    mixed = (mixed + bias[...]).astype(BF16)
    _, parts, heads, size, _ = qkv_ref.shape
    for part in range(parts):
        for head in range(heads):
            start = (part * heads + head) * size
            qkv_ref[0, part, head] = mixed[start : start + size]


def project_qkv(tokens, seg, slot_mod, weight, bias, heads, block):
    rows, length, width = tokens.shape
    slots = slot_mod.shape[1]
    features = weight.shape[0]
    size = features // (3 * heads)
    slot_row = jnp.tile(lax.iota(jnp.int32, slots), 3)[None]
    return pl.pallas_call(
        qkv_kernel,
        grid=(rows, length // block),
        in_specs=[
            pl.BlockSpec((1, 3 * slots), lambda r, t: (0, 0)),
            pl.BlockSpec((1, block, 1), lambda r, t: (r, t, 0)),
            pl.BlockSpec((1, slots, 2 * width), lambda r, t: (r, 0, 0)),
            pl.BlockSpec((1, block, width), lambda r, t: (r, t, 0)),
            pl.BlockSpec((features, width), lambda r, t: (0, 0)),
            pl.BlockSpec((features, 1), lambda r, t: (0, 0)),
        ],
        out_specs=[
            pl.BlockSpec((1, block, width), lambda r, t: (r, t, 0)),
            pl.BlockSpec((1, 3, heads, size, block), lambda r, t: (r, 0, 0, 0, t)),
        ],
        out_shape=[
            jax.ShapeDtypeStruct((rows, length, width), BF16),
            jax.ShapeDtypeStruct((rows, 3, heads, size, length), BF16),
        ],
        compiler_params=pltpu.CompilerParams(vmem_limit_bytes=VMEM_LIMIT),
        cost_estimate=pl.CostEstimate(
            flops=2 * rows * length * width * features,
            bytes_accessed=2 * rows * length * (2 * width + features),
            transcendentals=0,
        ),
    )(slot_row, seg[:, :, None], slot_mod, tokens, weight, bias[:, None])


def peers_of(seq):
    x, y = lax.rem(seq, 2), lax.div(seq, 2)
    return [seq + 1 - 2 * x, seq + 2 - 4 * y, 3 - seq]


def greet(devices):
    barrier = pltpu.get_barrier_semaphore()
    for device in devices:
        pl.semaphore_signal(barrier, inc=1, device_id=device, device_id_type=pl.DeviceIdType.MESH)
    pl.semaphore_wait(barrier, len(devices))


def send_block(source, target, sent, came, index, device):
    return pltpu.make_async_remote_copy(
        src_ref=source,
        dst_ref=target,
        send_sem=sent.at[index],
        recv_sem=came.at[index],
        device_id=device,
        device_id_type=pl.DeviceIdType.MESH,
    )


def attend_kernel(block, scale, code_col, code_row, query, key, value, out_ref, lse_ref, token_ref=None, sent=None, came=None, kept=None):
    length = query.shape[-1]
    keys = key[0, 0].astype(F32).T.astype(BF16)
    values = value[0, 0]
    codes = code_col[0]
    row, head = (pl.program_id(0), pl.program_id(1)) if sent is not None else (0, 0)
    rows, heads = out_ref.shape[:2]
    if sent is not None:
        seq = lax.axis_index("seq")
        peers = peers_of(seq)
        size = length // 4

        @pl.when((row == 0) & (head == 0))
        def _():
            greet([{"seq": peer} for peer in peers])

        def to_peer(r, h, m):
            lanes = pl.ds(m * size, size)
            place = (r * heads + h) * 3 + m - 1
            return send_block(out_ref.at[r, h, :, lanes], token_ref.at[r, seq, h], sent, came, place, {"seq": peers[m - 1]})

        def to_self(r, h):
            return pltpu.make_async_copy(out_ref.at[r, h, :, pl.ds(0, size)], token_ref.at[r, seq, h], kept.at[r * heads + h])

    for step in range(length // block):
        here = pl.ds(step * block, block)
        scores = jnp.dot(keys, query[0, 0, :, here], preferred_element_type=F32)
        scores = jnp.where(codes == code_row[0, :, here], scores * scale, -1e30)
        peak = jnp.max(scores, axis=0, keepdims=True)
        raised = jnp.exp2(scores - peak)
        total = jnp.sum(raised, axis=0, keepdims=True)
        probs = (raised * (1.0 / total)).astype(BF16)
        out_ref[row, head, :, here] = jnp.dot(values, probs, preferred_element_type=F32).astype(BF16)
        lse_ref[0, 0, :, here] = peak + jnp.log2(total)

    if sent is not None:
        to_self(row, head).start()
        for m in range(1, 4):
            to_peer(row, head, m).start()

        @pl.when((row == rows - 1) & (head == heads - 1))
        def _():
            for r in range(rows):
                for h in range(heads):
                    to_self(r, h).wait()
                    for m in range(1, 4):
                        to_peer(r, h, m).wait()


def attend(packed, col, row, block, exchange):
    rows, _, heads, size, length = packed.shape
    part = lambda j: pl.BlockSpec((1, None, 1, size, length), lambda r, h: (r, j, h, 0, 0))
    out_specs = [
        pl.BlockSpec((1, 1, size, length), lambda r, h: (r, h, 0, 0)),
        pl.BlockSpec((1, 1, 1, length), lambda r, h: (r, h, 0, 0)),
    ]
    out_shape = [
        jax.ShapeDtypeStruct((rows, heads, size, length), BF16),
        jax.ShapeDtypeStruct((rows, heads, 1, length), F32),
    ]
    scratch = []
    extra = {}
    if exchange:
        out_specs[0] = pl.BlockSpec((rows, heads, size, length), lambda r, h: (0, 0, 0, 0))
        out_specs.append(pl.BlockSpec(memory_space=pl.ANY))
        out_shape.append(jax.ShapeDtypeStruct((rows, 4, heads, size, length // 4), BF16))
        count = rows * heads
        scratch = [pltpu.SemaphoreType.DMA((3 * count,)), pltpu.SemaphoreType.DMA((3 * count,)), pltpu.SemaphoreType.DMA((count,))]
        extra = dict(collective_id=2, has_side_effects=True)
    return pl.pallas_call(
        partial(attend_kernel, block, size**-0.5 * LOG2E),
        grid=(rows, heads),
        in_specs=[
            pl.BlockSpec((1, length, 1), lambda r, h: (r, 0, 0)),
            pl.BlockSpec((1, 1, length), lambda r, h: (r, 0, 0)),
            part(0),
            part(1),
            part(2),
        ],
        out_specs=out_specs,
        out_shape=out_shape,
        scratch_shapes=scratch,
        compiler_params=pltpu.CompilerParams(vmem_limit_bytes=VMEM_LIMIT, **extra),
        cost_estimate=pl.CostEstimate(
            flops=8 * rows * heads * length * length * 128,
            bytes_accessed=8 * rows * heads * length * size,
            transcendentals=rows * heads * length * length,
        ),
    )(col, row, packed, packed, packed)


def attend_back_kernel(
    block,
    inner,
    scale,
    exchange,
    code_col,
    code_row,
    query,
    key,
    value,
    out,
    grad_out,
    lse,
    grad_ref,
    *rest,
):
    length = query.shape[-1]
    size = query.shape[-2]
    row, head = (pl.program_id(0), pl.program_id(1)) if exchange else (0, 0)
    rows, _, heads = grad_ref.shape[:3]
    if exchange:
        token_ref, key_sum, value_sum, keys, values, sent, came, kept = rest
        seq = lax.axis_index("seq")
        peers = peers_of(seq)
        local = length // 4

        @pl.when((row == 0) & (head == 0))
        def _():
            greet([{"seq": peer} for peer in peers])

        def to_peer(r, h, m):
            lanes = pl.ds(m * local, local)
            place = (r * heads + h) * 3 + m - 1
            return send_block(grad_ref.at[r, :, h, :, lanes], token_ref.at[r, :, seq, h], sent, came, place, {"seq": peers[m - 1]})

        def to_self(r, h):
            lanes = pl.ds(0, local)
            return pltpu.make_async_copy(grad_ref.at[r, :, h, :, lanes], token_ref.at[r, :, seq, h], kept.at[r * heads + h])

    else:
        key_sum, value_sum, keys, values = rest
    keys[...] = key[0, 0].astype(F32).T.astype(BF16)
    values[...] = value[0, 0].astype(F32).T.astype(BF16)
    for step in range(length // block):
        here = pl.ds(step * block, block)
        query_low = query[0, 0, :, here]
        grad_low = grad_out[0, 0, :, here]
        query_rows = query_low.astype(F32).T.astype(BF16)
        grad_rows = grad_low.astype(F32).T.astype(BF16)
        row_dot = jnp.sum(grad_low.astype(F32) * out[0, 0, :, here].astype(F32), axis=0, keepdims=True)
        grad_query = jnp.zeros((size, block), F32)
        for part in range(length // inner):
            there = pl.ds(part * inner, inner)
            scores = jnp.dot(keys[there, :], query_low, preferred_element_type=F32)
            scores = jnp.where(code_col[0, there, :] == code_row[0, :, here], scores * (scale * LOG2E), -1e30)
            probs = jnp.exp2(scores - lse[0, 0, :, here])
            grad_probs = jnp.dot(values[there, :], grad_low, preferred_element_type=F32)
            grad_raw = (probs * (grad_probs - row_dot) * scale).astype(BF16)
            value_part = jnp.dot(probs.astype(BF16), grad_rows, preferred_element_type=F32)
            key_part = jnp.dot(grad_raw, query_rows, preferred_element_type=F32)
            if step == 0:
                value_sum[there, :] = value_part
                key_sum[there, :] = key_part
            else:
                value_sum[there, :] += value_part
                key_sum[there, :] += key_part
            grad_query += jnp.dot(key[0, 0, :, there], grad_raw, preferred_element_type=F32)
        grad_ref[row, 0, head, :, here] = grad_query.astype(BF16)
    grad_ref[row, 1, head] = key_sum[...].T.astype(BF16)
    grad_ref[row, 2, head] = value_sum[...].T.astype(BF16)

    if exchange:
        to_self(row, head).start()
        for m in range(1, 4):
            to_peer(row, head, m).start()

        @pl.when((row == rows - 1) & (head == heads - 1))
        def _():
            for r in range(rows):
                for h in range(heads):
                    to_self(r, h).wait()
                    for m in range(1, 4):
                        to_peer(r, h, m).wait()


def attend_back(packed, out, grad_out, lse, col, row, block, inner, exchange):
    rows, _, heads, size, length = packed.shape
    part = lambda j: pl.BlockSpec((1, None, 1, size, length), lambda r, h: (r, j, h, 0, 0))
    whole = pl.BlockSpec((1, 1, size, length), lambda r, h: (r, h, 0, 0))
    out_specs = [pl.BlockSpec((1, 3, 1, size, length), lambda r, h: (r, 0, h, 0, 0))]
    out_shape = [jax.ShapeDtypeStruct((rows, 3, heads, size, length), BF16)]
    scratch = []
    extra = {}
    if exchange:
        out_specs = [
            pl.BlockSpec((rows, 3, heads, size, length), lambda r, h: (0, 0, 0, 0, 0)),
            pl.BlockSpec(memory_space=pl.ANY),
        ]
        out_shape.append(jax.ShapeDtypeStruct((rows, 3, 4, heads, size, length // 4), BF16))
        count = rows * heads
        scratch = [pltpu.SemaphoreType.DMA((3 * count,)), pltpu.SemaphoreType.DMA((3 * count,)), pltpu.SemaphoreType.DMA((count,))]
        extra = dict(collective_id=3, has_side_effects=True)
    return pl.pallas_call(
        partial(attend_back_kernel, block, inner, size**-0.5, exchange),
        grid=(rows, heads),
        in_specs=[
            pl.BlockSpec((1, length, 1), lambda r, h: (r, 0, 0)),
            pl.BlockSpec((1, 1, length), lambda r, h: (r, 0, 0)),
            part(0),
            part(1),
            part(2),
            whole,
            whole,
            pl.BlockSpec((1, 1, 1, length), lambda r, h: (r, h, 0, 0)),
        ],
        out_specs=out_specs,
        out_shape=out_shape,
        scratch_shapes=[
            pltpu.VMEM((length, size), F32),
            pltpu.VMEM((length, size), F32),
            pltpu.VMEM((length, size), BF16),
            pltpu.VMEM((length, size), BF16),
        ]
        + scratch,
        compiler_params=pltpu.CompilerParams(vmem_limit_bytes=VMEM_LIMIT, **extra),
        cost_estimate=pl.CostEstimate(
            flops=20 * rows * heads * length * length * 128,
            bytes_accessed=16 * rows * heads * length * size,
            transcendentals=rows * heads * length * length,
        ),
    )(col, row, packed, packed, packed, out, grad_out, lse)


def mlp_kernel(
    normed, grad_out, normed_turned, grad_turned, up, down, bias, out_sum, grad_sum, up_keep, up_send, down_keep, down_send, bias_sum
):
    step = pl.program_id(0)
    half = up_keep.shape[0]
    c0 = math.sqrt(2 / math.pi)
    c1 = c0 * 0.044715
    hidden = jnp.dot(normed[...], up[...], preferred_element_type=F32) + bias[...]
    square = hidden * hidden
    gate = 0.5 + 0.5 * jnp.tanh(hidden * (c0 + c1 * square))
    raised = hidden * gate
    slope = gate + raised * (1.0 - gate) * (2 * c0 + 6 * c1 * square)
    active = raised.astype(BF16)
    back = (((1,), (1,)), ((), ()))
    grad_active = lax.dot_general(grad_out[...], down[...], back, preferred_element_type=F32)
    grad_wide = (grad_active * slope).astype(BF16)
    out_part = jnp.dot(active, down[...], preferred_element_type=F32)
    grad_part = lax.dot_general(grad_wide, up[...], back, preferred_element_type=F32)

    @pl.when(step == 0)
    def _():
        out_sum[...] = out_part
        grad_sum[...] = grad_part

    @pl.when(step > 0)
    def _():
        out_sum[...] += out_part
        grad_sum[...] += grad_part

    bias_sum[...] = jnp.sum(grad_wide.astype(F32), axis=0, keepdims=True)
    up_keep[...] = jnp.dot(normed_turned[:half], grad_wide, preferred_element_type=F32)
    up_send[...] = jnp.dot(normed_turned[half:], grad_wide, preferred_element_type=F32).astype(BF16)
    down_keep[...] = jnp.dot(grad_turned[:half], active, preferred_element_type=F32)
    down_send[...] = jnp.dot(grad_turned[half:], active, preferred_element_type=F32).astype(BF16)


def feed_forward(normed, grad_out, normed_turned, grad_turned, up, down, bias, tile):
    count, width = normed.shape
    hidden = up.shape[1]
    half = width // 2
    fixed = lambda *shape: pl.BlockSpec(shape, lambda t: (0, 0))
    across = lambda rows: pl.BlockSpec((rows, tile), lambda t: (0, t))
    shape = jax.ShapeDtypeStruct
    return pl.pallas_call(
        mlp_kernel,
        grid=(hidden // tile,),
        in_specs=[
            fixed(count, width),
            fixed(count, width),
            fixed(width, count),
            fixed(width, count),
            across(width),
            pl.BlockSpec((tile, width), lambda t: (t, 0)),
            across(1),
        ],
        out_specs=[fixed(count, width), fixed(count, width), across(half), across(half), across(half), across(half), across(1)],
        out_shape=[
            shape((count, width), F32),
            shape((count, width), F32),
            shape((half, hidden), F32),
            shape((half, hidden), BF16),
            shape((half, hidden), F32),
            shape((half, hidden), BF16),
            shape((1, hidden), F32),
        ],
        compiler_params=pltpu.CompilerParams(vmem_limit_bytes=VMEM_LIMIT),
        cost_estimate=pl.CostEstimate(
            flops=12 * count * width * hidden,
            bytes_accessed=10 * width * hidden,
            transcendentals=count * hidden,
        ),
    )(normed, grad_out, normed_turned, grad_turned, up, down, bias)


def turn_halves(values, groups, mine):
    count, width = values.shape
    view = values.T.reshape(groups, 2, width // (2 * groups), count)
    keep = lax.dynamic_index_in_dim(view, mine, 1, keepdims=False).reshape(width // 2, count)
    send = lax.dynamic_index_in_dim(view, 1 - mine, 1, keepdims=False).reshape(width // 2, count)
    return jnp.concatenate([keep, send], axis=0)


STAGES = 2


def mlp_reduce_kernel(
    tiles,
    normed,
    grad_out,
    normed_turned,
    grad_turned,
    up0,
    up1,
    up2,
    up3,
    down0,
    down1,
    down2,
    down3,
    bias,
    out_sum,
    grad_sum,
    bias_sum,
    up_total,
    down_total,
    left_full,
    left_up,
    left_up_low,
    left_down,
    left_down_low,
    up_mine,
    down_mine,
    up_core,
    down_core,
    up_core_got,
    down_core_got,
    up_half,
    down_half,
    up_out,
    down_out,
    up_got,
    down_got,
    up_quarter,
    down_quarter,
    up_last,
    down_last,
    up_last_got,
    down_last_got,
    chip_full,
    chip_out,
    chip_got,
    core_sent,
    core_came,
    seq_sent,
    seq_came,
    last_sent,
    last_came,
    chip_sent,
    chip_came,
    bias_line,
):
    step = pl.program_id(0)
    seq, row = lax.axis_index("seq"), lax.axis_index("rows")
    half = normed_turned.shape[0] // 2
    x, y = lax.rem(seq, 2), lax.div(seq, 2)
    core_peer = {"rows": row + 1 - 2 * lax.rem(row, 2)}
    x_peer = {"seq": seq + 1 - 2 * x}
    y_peer = {"seq": seq + 2 - 4 * y}
    chip, core = lax.div(row, 2), lax.rem(row, 2)
    to_chip = [lax.rem(chip + k, 4) for k in range(4)]
    chip_peers = [{"rows": 2 * to_chip[k] + core} for k in range(4)]

    @pl.when(step == 0)
    def _():
        bias_line[...] = bias[...].astype(F32).reshape(1, bias.shape[0])
        barrier = pltpu.get_barrier_semaphore()
        for peer in (core_peer, x_peer, y_peer, *chip_peers[1:]):
            pl.semaphore_signal(barrier, inc=1, device_id=peer, device_id_type=pl.DeviceIdType.MESH)
        pl.semaphore_wait(barrier, 6)

    def copies(source, target, sent, came, tile, places, kind, device):
        slot = lax.rem(tile, places)
        return pltpu.make_async_remote_copy(
            src_ref=source.at[lax.rem(tile, 2)],
            dst_ref=target.at[slot],
            send_sem=sent.at[kind, slot],
            recv_sem=came.at[kind, slot],
            device_id=device,
            device_id_type=pl.DeviceIdType.MESH,
        )

    def to_core(tile):
        return (
            copies(up_core, up_core_got, core_sent, core_came, tile, 2, 0, core_peer),
            copies(down_core, down_core_got, core_sent, core_came, tile, 2, 1, core_peer),
        )

    def to_seq(tile):
        return (
            copies(up_out, up_got, seq_sent, seq_came, tile, 3, 0, x_peer),
            copies(down_out, down_got, seq_sent, seq_came, tile, 3, 1, y_peer),
        )

    def to_last(tile):
        return (
            copies(up_last, up_last_got, last_sent, last_came, tile, 3, 0, y_peer),
            copies(down_last, down_last_got, last_sent, last_came, tile, 3, 1, x_peer),
        )

    def to_chips(slot):
        return [
            pltpu.make_async_remote_copy(
                src_ref=chip_out.at[slot, to_chip[k]],
                dst_ref=chip_got.at[slot, k - 1],
                send_sem=chip_sent.at[k - 1, slot],
                recv_sem=chip_came.at[k - 1, slot],
                device_id=chip_peers[k],
                device_id_type=pl.DeviceIdType.MESH,
            )
            for k in range(1, 4)
        ]

    @pl.when((step >= 1) & (step <= tiles))
    def _():
        slot = lax.rem(step + 1, 2)
        for copy in to_core(step - 1):
            copy.wait()
        for other in range(2):
            kept, gone = 2 * other + x, 2 * other + 1 - x
            up_half[slot, other] = up_mine[slot, kept] + up_core_got[slot, kept].astype(F32)
            up_out[slot, other] = (up_mine[slot, gone] + up_core_got[slot, gone].astype(F32)).astype(BF16)
            kept, gone = 2 * y + other, 2 * (1 - y) + other
            down_half[slot, other] = down_mine[slot, kept] + down_core_got[slot, kept].astype(F32)
            down_out[slot, other] = (down_mine[slot, gone] + down_core_got[slot, gone].astype(F32)).astype(BF16)
        for copy in to_seq(step - 1):
            copy.start()

    @pl.when(step >= 2)
    def _():
        slot = lax.rem(step, 2)
        place3 = lax.rem(step + 1, 3)
        for copy in to_seq(step - 2):
            copy.wait()
        up_quarter[slot] = up_half[slot, y] + up_got[place3, y].astype(F32)
        up_last[slot] = (up_half[slot, 1 - y] + up_got[place3, 1 - y].astype(F32)).astype(BF16)
        down_quarter[slot] = down_half[slot, x] + down_got[place3, x].astype(F32)
        down_last[slot] = (down_half[slot, 1 - x] + down_got[place3, 1 - x].astype(F32)).astype(BF16)
        @pl.when(step < tiles + 1)
        def _():
            for copy in to_last(step - 2):
                copy.start()

        @pl.when(step == tiles + 1)
        def _():
            left_up[...] = up_quarter[slot]
            left_up_low[...] = up_last[slot]
            left_down[...] = down_quarter[slot]
            left_down_low[...] = down_last[slot]


    @pl.when(step >= 4)
    def _():
        slot = lax.rem(step, 2)
        for copy in to_chips(slot):
            copy.wait()
        for kind, total in enumerate((up_total, down_total)):
            value = chip_full[slot, chip, kind]
            for k in range(3):
                value = value + chip_got[slot, k, kind].astype(F32)
            total[...] = value

    @pl.when(step >= 3)
    def _():
        slot = lax.rem(step + 1, 2)
        place3 = lax.rem(step, 3)
        for copy in to_last(step - 3):
            copy.wait()
        size = half // 4
        ups = up_quarter[slot] + up_last_got[place3].astype(F32)
        downs = down_quarter[slot] + down_last_got[place3].astype(F32)
        for place in range(4):
            up_block = ups[place * size : (place + 1) * size]
            down_block = downs[:, place * 128 : (place + 1) * 128]
            chip_full[slot, place, 0] = up_block
            chip_full[slot, place, 1] = down_block
            chip_out[slot, place, 0] = up_block.astype(BF16)
            chip_out[slot, place, 1] = down_block.astype(BF16)
        @pl.when(step < tiles + 1)
        def _():
            for copy in to_chips(slot):
                copy.start()

        @pl.when(step == tiles + 1)
        def _():
            left_full[...] = chip_full[slot]

    @pl.when(step < tiles)
    def _():
        slot = lax.rem(step, 2)
        up = jnp.concatenate([up0[...], up1[...], up2[...], up3[...]], axis=1)
        down = jnp.concatenate([down0[...], down1[...], down2[...], down3[...]], axis=0)
        hidden_part = bias.shape[0] // 4
        biases = jnp.concatenate(
            [
                bias_line[:, pl.ds(pl.multiple_of(owner * hidden_part + step * 128, 128), 128)]
                for owner in range(4)
            ],
            axis=1,
        )
        c0 = math.sqrt(2 / math.pi)
        c1 = c0 * 0.044715
        hidden = jnp.dot(normed[...], up, preferred_element_type=F32) + biases
        square = hidden * hidden
        gate = 0.5 + 0.5 * jnp.tanh(hidden * (c0 + c1 * square))
        raised = hidden * gate
        slope = gate + raised * (1.0 - gate) * (2 * c0 + 6 * c1 * square)
        active = raised.astype(BF16)
        down_part = jnp.dot(grad_turned[...], active, preferred_element_type=F32)
        for owner in range(4):
            size = half // 4
            down_mine[slot, owner] = down_part[owner * size : (owner + 1) * size]
            down_core[slot, owner] = down_part[half + owner * size : half + (owner + 1) * size].astype(BF16)
        to_core(step)[1].start()
        back = (((1,), (1,)), ((), ()))
        grad_active = lax.dot_general(grad_out[...], down, back, preferred_element_type=F32)
        grad_wide = (grad_active * slope).astype(BF16)
        up_part = jnp.dot(normed_turned[...], grad_wide, preferred_element_type=F32)
        for owner in range(4):
            columns = slice(owner * 128, (owner + 1) * 128)
            up_mine[slot, owner] = up_part[:half, columns]
            up_core[slot, owner] = up_part[half:, columns].astype(BF16)
        to_core(step)[0].start()
        sums = jnp.sum(grad_wide.astype(F32), axis=0, keepdims=True)
        for owner in range(4):
            bias_sum[owner] = sums[:, owner * 128 : (owner + 1) * 128]
        out_part = jnp.dot(active, down, preferred_element_type=F32)
        grad_part = lax.dot_general(grad_wide, up, back, preferred_element_type=F32)

        @pl.when(step == 0)
        def _():
            out_sum[...] = out_part
            grad_sum[...] = grad_part

        @pl.when(step > 0)
        def _():
            out_sum[...] += out_part
            grad_sum[...] += grad_part


def feed_forward_reduce(normed, grad_out, normed_turned, grad_turned, up, down, bias):
    count, width = normed.shape
    hidden = up.shape[1]
    part = hidden // 4
    tiles = part // 128
    half, quarter = width // 2, width // 8
    last = tiles - 1
    shape = jax.ShapeDtypeStruct
    fixed = lambda *dims: pl.BlockSpec(dims, lambda t: (0, 0), pipeline_mode=pl.Buffered(buffer_count=1))
    result = lambda *dims: pl.BlockSpec(dims, lambda t: (0, 0))
    done = lambda t: jnp.maximum(t - 4, 0)

    def up_block(owner):
        return pl.BlockSpec((width, 128), lambda t: (0, owner * tiles + jnp.minimum(t, last)))

    def down_block(owner):
        return pl.BlockSpec((128, width), lambda t: (owner * tiles + jnp.minimum(t, last), 0))

    bias_block = pl.BlockSpec((4, 1, 128), lambda t: (0, 0, jnp.minimum(t, last)))
    pair = lambda dtype, *dims: pltpu.VMEM((2,) + dims, dtype)
    triple = lambda dtype, *dims: pltpu.VMEM((3,) + dims, dtype)
    return pl.pallas_call(
        partial(mlp_reduce_kernel, tiles),
        grid=(tiles + STAGES,),
        in_specs=[fixed(count, width), fixed(count, width), fixed(width, count), fixed(width, count)]
        + [up_block(owner) for owner in range(4)]
        + [down_block(owner) for owner in range(4)]
        + [pl.BlockSpec((hidden,), lambda t: (0,))],
        out_specs=[
            result(count, width),
            result(count, width),
            bias_block,
            pl.BlockSpec((quarter, 128), lambda t: (0, done(t))),
            pl.BlockSpec((quarter, 128), lambda t: (0, done(t))),
            pl.BlockSpec((4, 2, quarter, 128), lambda t: (0, 0, 0, 0)),
            result(half, 128),
            result(half, 128),
            result(quarter, 512),
            result(quarter, 512),
        ],
        out_shape=[
            shape((count, width), F32),
            shape((count, width), F32),
            shape((4, 1, part), F32),
            shape((quarter, part - 256), F32),
            shape((quarter, part - 256), F32),
            shape((4, 2, quarter, 128), F32),
            shape((half, 128), F32),
            shape((half, 128), BF16),
            shape((quarter, 512), F32),
            shape((quarter, 512), BF16),
        ],
        scratch_shapes=[
            pair(F32, 4, half, 128),
            pair(F32, 4, quarter, 512),
            pair(BF16, 4, half, 128),
            pair(BF16, 4, quarter, 512),
            pair(BF16, 4, half, 128),
            pair(BF16, 4, quarter, 512),
            pair(F32, 2, half, 128),
            pair(F32, 2, quarter, 512),
            pair(BF16, 2, half, 128),
            pair(BF16, 2, quarter, 512),
            triple(BF16, 2, half, 128),
            triple(BF16, 2, quarter, 512),
            pair(F32, half, 128),
            pair(F32, quarter, 512),
            pair(BF16, half, 128),
            pair(BF16, quarter, 512),
            triple(BF16, half, 128),
            triple(BF16, quarter, 512),
            pair(F32, 4, 2, quarter, 128),
            pair(BF16, 4, 2, quarter, 128),
            pair(BF16, 3, 2, quarter, 128),
        ]
        + [pltpu.SemaphoreType.DMA((2, 2))] * 2
        + [pltpu.SemaphoreType.DMA((2, 3))] * 4
        + [pltpu.SemaphoreType.DMA((3, 2))] * 2
        + [pltpu.VMEM((1, hidden), F32)],
        compiler_params=pltpu.CompilerParams(collective_id=1, has_side_effects=True, vmem_limit_bytes=VMEM_LIMIT),
        cost_estimate=pl.CostEstimate(
            flops=12 * count * width * hidden,
            bytes_accessed=6 * width * hidden,
            transcendentals=count * hidden,
        ),
    )(normed, grad_out, normed_turned, grad_turned, up, up, up, up, down, down, down, down, bias)


def slot_column(slots):
    return lax.rem(lax.broadcasted_iota(jnp.int32, (3 * slots, 1), 0), slots)


def split_low(values):
    high = values.astype(BF16)
    rest = values - high.astype(F32)
    middle = rest.astype(BF16)
    return high, middle, (rest - middle.astype(F32)).astype(BF16)


def per_token(slot_col, seg_row, table):
    picked = (slot_col == seg_row).astype(BF16)
    return lax.dot_general(
        picked, jnp.concatenate(split_low(table), axis=0), (((0,), (0,)), ((), ())), preferred_element_type=F32
    )


def per_slot(slot_col, seg_row, values):
    slots = slot_col.shape[0] // 3
    picked = (slot_col[:slots] == seg_row).astype(BF16)
    return sum(jnp.dot(picked, part, preferred_element_type=F32) for part in split_low(values))


def normalize(values):
    center = values - jnp.mean(values, axis=-1, keepdims=True)
    inverse = lax.rsqrt(jnp.mean(center * center, axis=-1, keepdims=True) + norm_eps)
    return center * inverse, inverse


def normalize_back(normal, inverse, grad):
    return inverse * (grad - jnp.mean(grad, axis=-1, keepdims=True) - normal * jnp.mean(grad * normal, axis=-1, keepdims=True))


def after_kernel(
    seg,
    table,
    bias,
    attended,
    weight,
    out_sum,
    grad_sum,
    middle,
    branch,
    cotangent,
    left_full,
    left_up,
    left_up_low,
    left_down,
    left_down_low,
    block_out,
    grad_middle_ref,
    view_ref,
    slot_sums,
    bias_sum,
    proj_own,
    proj_low,
    up_tail,
    down_tail,
    attended_here,
    weight_here,
    rows_here,
    cotangent_here,
    block_here,
    middle_here,
    normal_here,
    grad_here,
    heads_out,
    total,
    core_out,
    core_got,
    load_sem,
    first_sem,
    store_sem,
    sent,
    came,
    kept,
    core_sent,
    core_came,
    full_here,
    up_here,
    up_low_here,
    down_here,
    down_low_here,
    up_got,
    down_got,
    chip_out,
    chip_got,
    left_sem,
    left_sent,
    left_came,
):
    rows, length, width = cotangent_here.shape
    depth, own = width // 8, width // 4
    seq, row = lax.axis_index("seq"), lax.axis_index("rows")
    core = lax.rem(row, 2)
    core_peer = {"rows": row + 1 - 2 * core}
    peers = peers_of(seq)
    slot_col = slot_column(table.shape[1])

    def go(copies):
        for copy in copies:
            copy.start()

    def end(copies):
        for copy in copies:
            copy.wait()

    def loads(r):
        lines = pl.ds(r * length, length)
        pairs = (
            (out_sum.at[lines], rows_here.at[r, 0]),
            (grad_sum.at[lines], rows_here.at[r, 1]),
            (middle.at[r], rows_here.at[r, 2]),
            (branch.at[r], rows_here.at[r, 3]),
            (cotangent.at[r], cotangent_here.at[r]),
        )
        return [pltpu.make_async_copy(source, target, load_sem.at[r, k]) for k, (source, target) in enumerate(pairs)]

    load_weight = pltpu.make_async_copy(weight, weight_here, first_sem.at[0])
    load_attended = pltpu.make_async_copy(attended, attended_here, first_sem.at[1])
    lefts = ((left_full, full_here.at[0]), (left_up_low, up_low_here), (left_down_low, down_low_here), (left_up, up_here), (left_down, down_here))
    load_left = [pltpu.make_async_copy(source, target, left_sem.at[k]) for k, (source, target) in enumerate(lefts)]
    go(load_left + loads(0) + [load_weight] + loads(1) + [load_attended])
    chip = lax.div(row, 2)
    to_chip = [lax.rem(chip + k, 4) for k in range(4)]
    chip_peers = [{"rows": 2 * to_chip[k] + core} for k in range(4)]

    def to_chips(tile):
        return [
            send_to(
                chip_out.at[tile, to_chip[k]],
                chip_got.at[tile, k - 1],
                left_sent.at[2 + 3 * tile + k - 1],
                left_came.at[2 + 3 * tile + k - 1],
                chip_peers[k],
            )
            for k in range(1, 4)
        ]

    left_copies = [
        send_to(up_low_here, up_got, left_sent.at[0], left_came.at[0], {"seq": peers[1]}),
        send_to(down_low_here, down_got, left_sent.at[1], left_came.at[1], {"seq": peers[0]}),
    ]

    greet([{"seq": peer} for peer in peers] + [core_peer] + chip_peers[1:])
    end(load_left)
    go(left_copies)
    chip_out[0] = full_here[0].astype(BF16)
    go(to_chips(0))

    def go_on():
        end(left_copies)
        ups = up_here[...] + up_got[...].astype(F32)
        downs = down_here[...] + down_got[...].astype(F32)
        for place in range(4):
            full_here[1, place, 0] = ups[place * depth : (place + 1) * depth]
            full_here[1, place, 1] = downs[:, place * 128 : (place + 1) * 128]
        chip_out[1] = full_here[1].astype(BF16)
        go(to_chips(1))

    def to_peer(r, m):
        lanes = pl.ds(m * length, length)
        return send_block(
            heads_out.at[r, peers[m - 1]], view_ref.at[r, :, lanes], sent, came, r * 3 + m - 1, {"seq": peers[m - 1]}
        )

    def to_self(r):
        return pltpu.make_async_copy(heads_out.at[r, seq], view_ref.at[r, :, pl.ds(0, length)], kept.at[r])

    def stores(r):
        return [
            pltpu.make_async_copy(middle_here.at[r], grad_middle_ref.at[r], store_sem.at[r, 0]),
            pltpu.make_async_copy(block_here.at[r], block_out.at[r], store_sem.at[r, 1]),
        ]

    def mods(r, first, count):
        seg_row = seg[r : r + 1, pl.ds(pl.multiple_of(seq * length, 128), length)]
        found = per_token(slot_col, seg_row, table[r, :, first * width : (first + count) * width])
        return [found[:, k * width : (k + 1) * width] for k in range(count)]

    for r in range(rows):
        (gate_a,), (scale_b,) = mods(r, 2, 1), mods(r, 4, 1)
        end(loads(r))
        normal, inverse = normalize(rows_here[r, 2])
        normal_here[r] = normal
        grad_normed = rows_here[r, 1]
        grad_middle = cotangent_here[r].astype(F32) + normalize_back(normal, inverse, grad_normed * (1.0 + scale_b))
        middle_here[r] = grad_middle
        stores(r)[0].start()
        grad_branch = (grad_middle * gate_a).astype(BF16)
        grad_here[r] = grad_branch
        if r == 0:
            load_weight.wait()
        grad_heads = lax.dot_general(weight_here[...], grad_branch, (((1,), (1,)), ((), ())), preferred_element_type=F32)
        for owner in range(4):
            heads_out[r, owner] = grad_heads[owner * own : (owner + 1) * own].astype(BF16)
        to_self(r).start()
        for m in range(1, 4):
            to_peer(r, m).start()
        if r == 0:
            go_on()

    load_attended.wait()
    for r in range(rows):
        part = jnp.dot(attended_here[r], grad_here[r], preferred_element_type=F32)
        sums = jnp.sum(grad_here[r].astype(F32), axis=0, keepdims=True)
        if r == 0:
            total[...] = part
            bias_sum[...] = sums
        else:
            total[...] += part
            bias_sum[...] += sums
    to_core = send_to(core_out, core_got, core_sent, core_came, core_peer)
    for place in range(4):
        other = pl.multiple_of((2 * place + 1 - core) * depth, 8)
        core_out[place] = total[pl.ds(other, depth), :].astype(BF16)
    to_core.start()

    bias_line = bias[...].astype(F32).reshape(1, width)
    for r in range(rows):
        (gate_b,) = mods(r, 5, 1)
        branch_b = rows_here[r, 0] + bias_line
        block_here[r] = (rows_here[r, 2] + gate_b * branch_b).astype(BF16)
        stores(r)[1].start()
        grad_normed = rows_here[r, 1]
        seg_row = seg[r : r + 1, pl.ds(pl.multiple_of(seq * length, 128), length)]
        pieces = (
            middle_here[r] * rows_here[r, 3],
            grad_normed,
            grad_normed * normal_here[r],
            cotangent_here[r].astype(F32) * branch_b,
        )
        for k, piece in enumerate(pieces):
            slot_sums[r, :, k * width : (k + 1) * width] = per_slot(slot_col, seg_row, piece)

    to_core.wait()
    for place in range(4):
        mine = pl.multiple_of((2 * place + core) * depth, 8)
        proj_low[place] = (total[pl.ds(mine, depth), :] + core_got[place].astype(F32)).astype(BF16)
    mine = pl.multiple_of(row * depth, 8)
    proj_own[...] = total[pl.ds(mine, depth), :] + core_got[chip].astype(F32)
    for tile in range(2):
        end(to_chips(tile))
        for kind, target in enumerate((up_tail, down_tail)):
            value = full_here[tile, chip, kind]
            for k in range(3):
                value = value + chip_got[tile, k, kind].astype(F32)
            target[:, tile * 128 : (tile + 1) * 128] = value
    for r in range(rows):
        end(stores(r))
        to_self(r).wait()
        for m in range(1, 4):
            to_peer(r, m).wait()


def after_feed_forward(seg, table, attended, weight, bias, out_sum, grad_sum, middle, branch, cotangent, left):
    rows, length, width = cotangent.shape
    slots = table.shape[1]
    depth = width // 8
    shape = jax.ShapeDtypeStruct
    vmem = lambda dtype, *dims: pltpu.VMEM(dims, dtype)
    near, far = pl.BlockSpec(memory_space=pltpu.VMEM), pl.BlockSpec(memory_space=pl.ANY)
    dma = lambda *dims: pltpu.SemaphoreType.DMA(dims)
    return pl.pallas_call(
        after_kernel,
        in_specs=[near] * 3 + [far] * 12,
        out_specs=[far] * 3 + [near] * 6,
        out_shape=[
            shape((rows, length, width), BF16),
            shape((rows, length, width), F32),
            shape((rows, width // 4, 4 * length), BF16),
            shape((rows, slots, 4 * width), F32),
            shape((1, width), F32),
            shape((depth, width), F32),
            shape((4, depth, width), BF16),
            shape((depth, 256), F32),
            shape((depth, 256), F32),
        ],
        scratch_shapes=[
            vmem(BF16, rows, width, length),
            vmem(BF16, width, width),
            vmem(F32, rows, 4, length, width),
            vmem(BF16, rows, length, width),
            vmem(BF16, rows, length, width),
            vmem(F32, rows, length, width),
            vmem(F32, rows, length, width),
            vmem(BF16, rows, length, width),
            vmem(BF16, rows, 4, width // 4, length),
            vmem(F32, width, width),
            vmem(BF16, 4, depth, width),
            vmem(BF16, 4, depth, width),
            dma(rows, 5),
            dma(2),
            dma(rows, 2),
            dma(3 * rows),
            dma(3 * rows),
            dma(rows),
            pltpu.SemaphoreType.DMA,
            pltpu.SemaphoreType.DMA,
            vmem(F32, 2, 4, 2, depth, 128),
            vmem(F32, 4 * depth, 128),
            vmem(BF16, 4 * depth, 128),
            vmem(F32, depth, 512),
            vmem(BF16, depth, 512),
            vmem(BF16, 4 * depth, 128),
            vmem(BF16, depth, 512),
            vmem(BF16, 2, 4, 2, depth, 128),
            vmem(BF16, 2, 3, 2, depth, 128),
            dma(5),
            dma(8),
            dma(8),
        ],
        compiler_params=pltpu.CompilerParams(vmem_limit_bytes=VMEM_LIMIT, collective_id=4, has_side_effects=True),
        cost_estimate=pl.CostEstimate(flops=8 * 10**9, bytes_accessed=3 * 10**7, transcendentals=0),
    )(seg, table, bias, attended, weight, out_sum, grad_sum, middle, branch, cotangent, *left)


def qkv_weight_kernel(grad, normed, keep_ref, send_ref, sum_ref, total, turned):
    step = pl.program_id(0)
    chips, depth = lax.axis_size("rows") // 2, total.shape[1] // lax.axis_size("rows")
    mine = lax.rem(lax.axis_index("rows"), 2)
    part = jnp.dot(grad[0], normed[0], preferred_element_type=F32)
    sums = jnp.sum(grad[0].astype(F32), axis=1, keepdims=True)

    @pl.when(step == 0)
    def _():
        total[...] = part
        sum_ref[...] = sums

    @pl.when(step > 0)
    def _():
        total[...] += part
        sum_ref[...] += sums

    @pl.when(step == pl.num_programs(0) - 1)
    def _():
        turned[...] = total[...].T
        for chip in range(chips):
            first = pl.multiple_of((2 * chip + mine) * depth, 8)
            other = pl.multiple_of((2 * chip + 1 - mine) * depth, 8)
            keep_ref[chip] = turned[pl.ds(first, depth), :]
            send_ref[chip] = turned[pl.ds(other, depth), :].astype(BF16)


def qkv_weight_grad(grad, normed):
    rows, features, length = grad.shape
    width = normed.shape[2]
    groups = lax.axis_size("rows")
    shape = (groups // 2, width // groups, features)
    return pl.pallas_call(
        qkv_weight_kernel,
        grid=(rows,),
        in_specs=[
            pl.BlockSpec((1, features, length), lambda r: (r, 0, 0)),
            pl.BlockSpec((1, length, width), lambda r: (r, 0, 0)),
        ],
        out_specs=[
            pl.BlockSpec(shape, lambda r: (0, 0, 0)),
            pl.BlockSpec(shape, lambda r: (0, 0, 0)),
            pl.BlockSpec((features, 1), lambda r: (0, 0)),
        ],
        out_shape=[
            jax.ShapeDtypeStruct(shape, F32),
            jax.ShapeDtypeStruct(shape, BF16),
            jax.ShapeDtypeStruct((features, 1), F32),
        ],
        scratch_shapes=[pltpu.VMEM((features, width), F32), pltpu.VMEM((width, features), F32)],
        compiler_params=pltpu.CompilerParams(vmem_limit_bytes=VMEM_LIMIT),
        cost_estimate=pl.CostEstimate(
            flops=2 * rows * length * width * features,
            bytes_accessed=2 * rows * length * (width + features) + 6 * width * features // 2,
            transcendentals=0,
        ),
    )(grad, normed)


def tail_kernel(
    images,
    mod,
    weight,
    cond,
    ada_ref,
    cond_ref,
    bias_ref,
    got,
    low_mine,
    low_got,
    row_mine,
    row_got,
    cond_mine,
    cond_got,
    column_got,
    sent,
    arrived,
):
    seq_count, row_total = lax.axis_size("seq"), lax.axis_size("rows")
    seq, row = lax.axis_index("seq"), lax.axis_index("rows")
    to_seq = [lax.rem(seq + m, seq_count) for m in range(seq_count)]
    to_row = [lax.rem(row + m, row_total) for m in range(row_total)]
    barrier = pltpu.get_barrier_semaphore()
    for m in range(1, seq_count):
        pl.semaphore_signal(barrier, inc=1, device_id={"seq": to_seq[m]}, device_id_type=pl.DeviceIdType.MESH)
    for m in range(1, row_total):
        pl.semaphore_signal(barrier, inc=1, device_id={"rows": to_row[m]}, device_id_type=pl.DeviceIdType.MESH)
    pl.semaphore_wait(barrier, seq_count + row_total - 2)

    used = [0]

    def start(source, target, device):
        copy = pltpu.make_async_remote_copy(
            src_ref=source,
            dst_ref=target,
            send_sem=sent.at[used[0]],
            recv_sem=arrived.at[used[0]],
            device_id=device,
            device_id_type=pl.DeviceIdType.MESH,
        )
        used[0] += 1
        copy.start()
        return copy

    copies = [start(mod.at[to_seq[m]], got.at[m], {"seq": to_seq[m]}) for m in range(1, seq_count)]
    column_got[0] = cond[row]
    column_copies = [start(cond.at[to_row[m]], column_got.at[m], {"rows": to_row[m]}) for m in range(1, row_total)]
    total = mod[seq]
    for m, copy in enumerate(copies):
        copy.wait()
        total = total + got[m + 1]
    low = total[:images].astype(BF16)
    low_mine[...] = low
    row_mine[...] = total[images:]
    row_mine[0:1] = jnp.sum(total[:images], axis=0, keepdims=True)
    low_got[0] = low
    copies = [start(low_mine, low_got.at[m], {"rows": to_row[m]}) for m in range(1, row_total)]
    copies += [start(row_mine, row_got.at[m], {"rows": to_row[m]}) for m in range(1, row_total)]
    term = lax.dot_general(low, weight[...], (((1,), (1,)), ((), ())), preferred_element_type=F32)
    cond_mine[...] = term
    cond_copies = [start(cond_mine, cond_got.at[m], {"seq": to_seq[m]}) for m in range(1, seq_count)]
    for copy in copies:
        copy.wait()
    sums = row_mine[...]
    for m in range(1, row_total):
        sums = sums + row_got[m]
    bias_ref[seq] = sums
    copies = [start(bias_ref.at[seq], bias_ref.at[seq], {"seq": to_seq[m]}) for m in range(1, seq_count)]
    for copy in column_copies:
        copy.wait()
    gathered = jnp.concatenate([low_got[m] for m in range(row_total)], axis=0)
    columns = jnp.concatenate([column_got[m] for m in range(row_total)], axis=0)
    ada_ref[...] = lax.dot_general(columns, gathered, (((0,), (0,)), ((), ())), preferred_element_type=F32)
    for m, copy in enumerate(cond_copies):
        copy.wait()
        term = term + cond_got[m + 1]
    cond_ref[...] = term
    for copy in copies:
        copy.wait()


def finish(mod, weight, cond, images):
    seq_count, lines, columns = mod.shape
    width, depth = weight.shape[0], cond.shape[2]
    row_total = lax.axis_size("rows")
    extra = lines - images
    copies = 3 * (seq_count - 1) + 3 * (row_total - 1)
    return pl.pallas_call(
        partial(tail_kernel, images),
        in_specs=[pl.BlockSpec(memory_space=pltpu.VMEM)] * 3,
        out_specs=[pl.BlockSpec(memory_space=pltpu.VMEM)] * 3,
        out_shape=[
            jax.ShapeDtypeStruct((depth, columns), F32),
            jax.ShapeDtypeStruct((images, width), F32),
            jax.ShapeDtypeStruct((seq_count, extra, columns), F32),
        ],
        scratch_shapes=[
            pltpu.VMEM((seq_count, lines, columns), F32),
            pltpu.VMEM((images, columns), BF16),
            pltpu.VMEM((row_total, images, columns), BF16),
            pltpu.VMEM((extra, columns), F32),
            pltpu.VMEM((row_total, extra, columns), F32),
            pltpu.VMEM((images, width), F32),
            pltpu.VMEM((seq_count, images, width), F32),
            pltpu.VMEM((row_total, images, depth), BF16),
            pltpu.SemaphoreType.DMA((copies,)),
            pltpu.SemaphoreType.DMA((copies,)),
        ],
        compiler_params=pltpu.CompilerParams(collective_id=0, has_side_effects=True, vmem_limit_bytes=VMEM_LIMIT),
        cost_estimate=pl.CostEstimate(flops=10**9, bytes_accessed=10**7, transcendentals=0),
    )(mod, weight, cond)


def send_to(source, target, sent, came, device):
    return pltpu.make_async_remote_copy(
        src_ref=source,
        dst_ref=target,
        send_sem=sent,
        recv_sem=came,
        device_id=device,
        device_id_type=pl.DeviceIdType.MESH,
    )


def back_kernel(
    block,
    inner,
    scale,
    code_col,
    code_row,
    query,
    key,
    value,
    out,
    grad_out,
    lse,
    normed,
    proj_own,
    proj_low,
    down,
    down_tail,
    seg,
    table,
    slot_sums,
    image_index,
    conditioning,
    proj_bias,
    up_bias,
    down_bias,
    tokens,
    grad_middle,
    weight,
    ada,
    grad_tokens,
    proj_ref,
    down_ref,
    ada_ref,
    cond_ref,
    ada_bias_ref,
    qv_bias_ref,
    proj_bias_ref,
    up_bias_ref,
    down_bias_ref,
    qkv_ref,
    grads,
    token_got,
    key_sum,
    value_sum,
    keys,
    values,
    total,
    spare,
    core_out,
    core_got,
    proj_got,
    seq_out,
    seq_got,
    down_out,
    down_got,
    qkv_own,
    chip_got,
    weights,
    tokens_here,
    middle_here,
    grad_here,
    features,
    image_sums,
    feature_sums,
    mod,
    got,
    lines,
    lines_got,
    low_all,
    small_core,
    small_chip,
    small_seq,
    cond_all,
    cond,
    column_got,
    piece_out,
    piece_got,
    sent,
    came,
    kept,
    load_sem,
    store_sem,
    other_sent,
    other_came,
    normed_here,
):
    length, size = query.shape[-1], query.shape[-2]
    row, head = pl.program_id(0), pl.program_id(1)
    rows, _, heads = grads.shape[:3]
    width = normed.shape[-1]
    images, columns = mod.shape[1:]
    depth, own, local = width // 8, width // 4, length // 4
    seq, group = lax.axis_index("seq"), lax.axis_index("rows")
    chip, core = lax.div(group, 2), lax.rem(group, 2)
    seq_places = peers_of(seq)
    peers = [{"seq": place} for place in seq_places]
    row_places = [lax.rem(group + m, 8) for m in range(8)]
    row_peers = [{"rows": place} for place in row_places]
    core_peer = {"rows": group + 1 - 2 * core}
    to_chip = [lax.rem(chip + k, 4) for k in range(4)]
    from_chip = [lax.rem(chip + 4 - k, 4) for k in range(4)]
    chip_peers = [{"rows": 2 * to_chip[k] + core} for k in range(4)]
    first = (row == 0) & (head == 0)
    last = (row == rows - 1) & (head == heads - 1)
    slot_col = slot_column(table.shape[1])
    used = [0]

    def copy_to(source, target, device):
        used[0] += 1
        return send_to(source, target, other_sent.at[used[0] - 1], other_came.at[used[0] - 1], device)

    def go(copies):
        for copy in copies:
            copy.start()

    def end(copies):
        for copy in copies:
            copy.wait()

    def to_peer(r, h, m):
        place = (r * heads + h) * 3 + m - 1
        source = grads.at[r, :, h, :, pl.ds(m * local, local)]
        return send_to(source, token_got.at[r, :, seq, h], sent.at[place], came.at[place], peers[m - 1])

    def to_self(r, h):
        source = grads.at[r, :, h, :, pl.ds(0, local)]
        return pltpu.make_async_copy(source, token_got.at[r, :, seq, h], kept.at[r * heads + h])

    proj_copies = [copy_to(proj_low.at[to_chip[k]], proj_got.at[k - 1], chip_peers[k]) for k in range(1, 4)]
    seq_copies = [copy_to(seq_out.at[place], seq_got.at[m], peers[m]) for m, place in enumerate(seq_places)]
    core_copy = copy_to(core_out, core_got, core_peer)
    down_copy = copy_to(down_out.at[1 - core], down_got, core_peer)
    chip_copies = [copy_to(core_out.at[to_chip[k]], chip_got.at[k - 1], chip_peers[k]) for k in range(1, 4)]
    column_copies = [copy_to(cond.at[row_places[m]], column_got.at[group], row_peers[m]) for m in range(1, 8)]
    mod_copies = [copy_to(mod.at[place], got.at[m], peers[m]) for m, place in enumerate(seq_places)]
    line_copies = [copy_to(lines.at[place], lines_got.at[m], peers[m]) for m, place in enumerate(seq_places)]
    low_core = copy_to(low_all.at[chip, core], low_all.at[chip, core], core_peer)
    low_chips = [copy_to(low_all.at[chip, core], low_all.at[chip, core], chip_peers[k]) for k in range(1, 4)]
    low_on = [copy_to(low_all.at[from_chip[k], core], low_all.at[from_chip[k], core], core_peer) for k in range(1, 4)]
    small_over = copy_to(small_core.at[core], small_core.at[core], core_peer)
    small_chips = [copy_to(small_chip.at[chip], small_chip.at[chip], chip_peers[k]) for k in range(1, 4)]
    small_copies = [copy_to(small_seq.at[seq], small_seq.at[seq], peers[m]) for m in range(3)]
    cond_copies = [copy_to(cond_all.at[seq], cond_all.at[seq], peers[m]) for m in range(3)]
    base = used[0]

    load_weights = [
        pltpu.make_async_copy(weight.at[:, pl.ds(part * width, width)], weights.at[part], load_sem.at[part])
        for part in range(3)
    ]
    load_normed = lambda r: pltpu.make_async_copy(normed.at[r], normed_here, load_sem.at[7])
    load_tokens = pltpu.make_async_copy(tokens, tokens_here, load_sem.at[3])
    load_middle = pltpu.make_async_copy(grad_middle, middle_here, load_sem.at[4])
    load_ada = [
        pltpu.make_async_copy(ada.at[pl.ds(0, width)], weights.at[0], load_sem.at[5]),
        pltpu.make_async_copy(ada.at[pl.ds(width, columns - width)], weights.at[1, pl.ds(0, columns - width)], load_sem.at[6]),
    ]

    @pl.when(first)
    def _():
        go(load_weights + [load_tokens, load_middle, load_normed(0)])

    keys[...] = key[0, 0].astype(F32).T.astype(BF16)
    values[...] = value[0, 0].astype(F32).T.astype(BF16)

    def place_of(part):
        return pl.ds(pl.multiple_of((part * heads + head) * size, 8), size)

    for step in range(length // block):
        here = pl.ds(step * block, block)
        query_low = query[0, 0, :, here]
        grad_low = grad_out[0, 0, :, here]
        query_rows = query_low.astype(F32).T.astype(BF16)
        grad_rows = grad_low.astype(F32).T.astype(BF16)
        row_dot = jnp.sum(grad_low.astype(F32) * out[0, 0, :, here].astype(F32), axis=0, keepdims=True)
        grad_query = jnp.zeros((size, block), F32)
        for part in range(length // inner):
            there = pl.ds(part * inner, inner)
            scores = jnp.dot(keys[there, :], query_low, preferred_element_type=F32)
            scores = jnp.where(code_col[0, there, :] == code_row[0, :, here], scores * (scale * LOG2E), -1e30)
            probs = jnp.exp2(scores - lse[0, 0, :, here])
            grad_probs = jnp.dot(values[there, :], grad_low, preferred_element_type=F32)
            grad_raw = (probs * (grad_probs - row_dot) * scale).astype(BF16)
            value_part = jnp.dot(probs.astype(BF16), grad_rows, preferred_element_type=F32)
            key_part = jnp.dot(grad_raw, query_rows, preferred_element_type=F32)
            if step == 0:
                value_sum[there, :] = value_part
                key_sum[there, :] = key_part
            else:
                value_sum[there, :] += value_part
                key_sum[there, :] += key_part
            grad_query += jnp.dot(key[0, 0, :, there], grad_raw, preferred_element_type=F32)
        low = grad_query.astype(BF16)
        grads[row, 0, head, :, here] = low
        spare[place_of(0), here] = low.astype(F32)
    for part, sums in ((1, key_sum), (2, value_sum)):
        low = sums[...].T.astype(BF16)
        grads[row, part, head] = low
        spare[place_of(part), :] = low.astype(F32)

    @pl.when(first)
    def _():
        greet(peers + row_peers[1:])
        go(proj_copies)
        half = down_out.shape[2]
        down_out[0] = down[:, :half]
        down_out[1] = jnp.concatenate([down[:, half:], down_tail[...]], axis=1)
        down_copy.start()
        value = conditioning[...].astype(F32)
        low = (value / (1.0 + jnp.exp(-value))).astype(BF16)
        for place in range(8):
            cond[place] = low[:, place * depth : (place + 1) * depth]
        column_got[group] = cond[group]
        go(column_copies)
        image_sums[...] = jnp.zeros_like(image_sums)
        feature_sums[...] = jnp.zeros_like(feature_sums)

    to_self(row, head).start()
    for m in range(1, 4):
        to_peer(row, head, m).start()

    own_features = 3 * own

    @pl.when((head == heads - 1) & (row == 0))
    def _():
        load_normed(0).wait()
        total[...] = jnp.dot(spare[:own_features].astype(BF16), normed_here[...], preferred_element_type=F32)
        load_normed(1).start()

    @pl.when((head == heads - 1) & (row > 0))
    def _():
        load_normed(1).wait()
        total[...] += jnp.dot(spare[:own_features].astype(BF16), normed_here[...], preferred_element_type=F32)

    def store_tokens(r):
        return pltpu.make_async_copy(grad_here.at[r], grad_tokens.at[r], store_sem.at[r])

    def input_grad(r):
        for h in range(heads):
            to_self(r, h).wait()
            for m in range(1, 4):
                to_peer(r, h, m).wait()
        grad_normed = jnp.zeros((width, local), F32)
        for part in range(3):
            for place in range(4):
                for h in range(heads):
                    start = (place * heads + h) * size
                    features[start : start + size] = token_got[r, part, place, h].astype(F32)
            low = features[...].astype(BF16)
            grad_normed += jnp.dot(weights[part], low, preferred_element_type=F32)
            if part != 1:
                lanes = slice(part * width, (part + 1) * width)
                ones = jnp.ones((8, local), BF16)
                feature_sums[:, lanes] += lax.dot_general(ones, low, (((1,), (1,)), ((), ())), preferred_element_type=F32)
        grad_normed = grad_normed.T
        normal, inverse = normalize(tokens_here[r].astype(F32))
        seg_row = seg[r : r + 1, pl.ds(pl.multiple_of(seq * local, 128), local)]
        scale_a = per_token(slot_col, seg_row, table[r, :, width : 2 * width])
        grad_here[r] = middle_here[r] + normalize_back(normal, inverse, grad_normed * (1.0 + scale_a))
        store_tokens(r).start()
        late = [per_slot(slot_col, seg_row, piece) for piece in (grad_normed, grad_normed * normal)]
        slots = jnp.concatenate(late + [slot_sums[r]], axis=1)
        pick = lax.broadcasted_iota(jnp.int32, (images, slots.shape[0]), 0) == image_index[r : r + 1, :]
        picks = jnp.concatenate([pick.astype(BF16)] * 3, axis=1)
        image_sums[...] += jnp.dot(picks, jnp.concatenate(split_low(slots), axis=0), preferred_element_type=F32)

    @pl.when(last)
    def _():
        spare[:, :own_features] = total[...].T
        for place in range(4):
            other = pl.multiple_of((2 * place + 1 - core) * depth, 8)
            core_out[place] = spare[pl.ds(other, depth), :own_features].astype(BF16)
        core_copy.start()
        end(proj_copies)
        mine = proj_own[...]
        for k in range(3):
            mine = mine + proj_got[k].astype(F32)
        for place in range(4):
            seq_out[place] = mine[:, place * own : (place + 1) * own].astype(BF16)
        go(seq_copies)
        for place in range(4):

            @pl.when(seq == place)
            def _():
                proj_ref[...] = mine[:, place * own : (place + 1) * own]

        down_copy.wait()
        left, right = down_out[core], down_got[...]
        left, right = jnp.where(core == 0, left, right), jnp.where(core == 0, right, left)
        down_ref[:depth] = left
        down_ref[depth:] = right
        core_copy.wait()
        for place in range(4):
            same = pl.multiple_of((2 * place + core) * depth, 8)
            core_out[place] = (spare[pl.ds(same, depth), :own_features] + core_got[place].astype(F32)).astype(BF16)
        same = pl.multiple_of(group * depth, 8)
        qkv_own[...] = spare[pl.ds(same, depth), :own_features] + core_got[chip].astype(F32)
        go(chip_copies)

        end(load_weights + [load_tokens, load_middle])
        for r in range(rows):
            input_grad(r)
        go(load_ada)

        for place in range(4):
            mod[place] = image_sums[:, place * columns : (place + 1) * columns]
        for line in range(8):
            if line < 2:
                value = feature_sums[0:1, 2 * line * width : (2 * line + 1) * width]
            else:
                value = (proj_bias[...], *(up_bias[k] for k in range(4)), down_bias[...])[line - 2]
            lines[line // 2, line % 2 : line % 2 + 1] = value
        go(mod_copies + line_copies)
        for m, copy in enumerate(seq_copies):
            copy.wait()
            proj_ref[...] += seq_got[m].astype(F32)
        sums = mod[seq]
        for m, copy in enumerate(mod_copies):
            copy.wait()
            sums = sums + got[m]
        low = sums.astype(BF16)
        low_all[chip, core] = low
        go([low_core] + low_chips)
        small = lines[seq]
        for m, copy in enumerate(line_copies):
            copy.wait()
            small = small + lines_got[m]
        small_core[core] = jnp.zeros_like(small_core[core])
        small_core[core, 0:2, :width] = small
        small_core[core, 2:3] = jnp.sum(sums, axis=0, keepdims=True)
        small_over.start()
        end(load_ada)
        term = jnp.dot(low[:, :width], weights[0], preferred_element_type=F32)
        term += jnp.dot(low[:, width:], weights[1, : columns - width], preferred_element_type=F32)
        cond_all[seq] = term
        go(cond_copies)
        end(chip_copies + column_copies)
        mine = qkv_own[...]
        for k in range(3):
            mine = mine + chip_got[k].astype(F32)
        for part in range(3):
            piece_out[part] = mine[:, part * own : (part + 1) * own]

        def piece(part):
            index = part * 4 + seq
            target, place = lax.div(index, 3), lax.rem(index, 3)
            copy = send_to(
                piece_out.at[part], piece_got.at[place], other_sent.at[base + part], other_came.at[base + place], {"seq": target}
            )
            return copy, target, place

        def arriving(place):
            source = lax.rem(3 * seq + place, 4)
            copy = send_to(
                piece_out.at[0], piece_got.at[place], other_sent.at[base], other_came.at[base + place], {"seq": source}
            )
            return copy, source

        for part in range(3):
            copy, target, place = piece(part)

            @pl.when(target != seq)
            def _():
                copy.start()

            @pl.when(target == seq)
            def _():
                piece_got[place] = piece_out[part]

        small_over.wait()
        small_chip[chip] = small_core[0] + small_core[1]
        go(small_chips)
        for came_in, going_on in zip(low_chips, low_on):
            came_in.wait()
            going_on.start()
        end(small_chips)
        small_seq[seq] = (small_chip[0] + small_chip[1]) + (small_chip[2] + small_chip[3])
        go(small_copies)
        end([low_core] + low_on)
        gathered = jnp.concatenate([low_all[m // 2, m % 2] for m in range(8)], axis=0)
        blocks = jnp.concatenate([column_got[m] for m in range(8)], axis=0)
        ada_ref[...] = lax.dot_general(blocks, gathered, (((0,), (0,)), ((), ())), preferred_element_type=F32)
        for part in range(3):
            copy, target, place = piece(part)

            @pl.when(target != seq)
            def _():
                copy.wait_send()

        for place in range(3):
            copy, source = arriving(place)

            @pl.when(source != seq)
            def _():
                copy.wait_recv()

        for place in range(3):
            qkv_ref[:, place * own : (place + 1) * own] = piece_got[place]
        end(cond_copies)
        value = conditioning[...].astype(F32)
        gate = 1.0 / (1.0 + jnp.exp(-value))
        sums = (cond_all[0] + cond_all[1]) + (cond_all[2] + cond_all[3])
        cond_ref[...] = sums * gate * (1.0 + value * (1.0 - gate))
        end(small_copies)
        for place in range(4):
            ada_bias_ref[pl.ds(place * columns, columns)] = small_seq[place, 2]
        qv_bias_ref[...] = small_seq[0, 0:2, :width]
        proj_bias_ref[...] = small_seq[1, 0, :width]
        for line in range(3, 7):
            up_bias_ref[pl.ds((line - 3) * width, width)] = small_seq[line // 2, line % 2, :width]
        down_bias_ref[...] = small_seq[3, 1, :width]
        for r in range(rows):
            store_tokens(r).wait()


def attend_back_and_finish(packed, out, grad_out, lse, col, row, normed, *rest):
    proj_own, proj_low, down, down_tail, seg, table, slot_sums, image_index, conditioning, biases, tokens, grad_middle, weight, ada = rest
    rows, _, heads, size, length = packed.shape
    width = normed.shape[2]
    depth, own, features, local = width // 8, width // 4, 3 * heads * size, length // 4
    half = (down.shape[1] + down_tail.shape[1]) // 2
    images, columns = conditioning.shape[0], ada.shape[0]
    part = lambda j: pl.BlockSpec((1, None, 1, size, length), lambda r, h: (r, j, h, 0, 0))
    whole = pl.BlockSpec((1, 1, size, length), lambda r, h: (r, h, 0, 0))
    single = pl.Buffered(buffer_count=1)
    fixed = lambda *dims: pl.BlockSpec(dims, lambda r, h: (0,) * len(dims), pipeline_mode=single)
    result = lambda *dims: pl.BlockSpec(dims, lambda r, h: (0,) * len(dims))
    far = pl.BlockSpec(memory_space=pl.ANY)
    shape = jax.ShapeDtypeStruct
    vmem = lambda dtype, *dims: pltpu.VMEM(dims, dtype)
    count = rows * heads
    copies = 3 + 3 + 1 + 1 + 3 + 7 + 3 + 3 + 1 + 3 + 3 + 1 + 3 + 3 + 3 + 3
    dma = lambda n: pltpu.SemaphoreType.DMA((n,))
    return pl.pallas_call(
        partial(back_kernel, 256, 512, size**-0.5),
        grid=(rows, heads),
        in_specs=[
            pl.BlockSpec((1, length, 1), lambda r, h: (r, 0, 0)),
            pl.BlockSpec((1, 1, length), lambda r, h: (r, 0, 0)),
            part(0),
            part(1),
            part(2),
            whole,
            whole,
            pl.BlockSpec((1, 1, 1, length), lambda r, h: (r, h, 0, 0)),
            far,
            fixed(depth, width),
            fixed(4, depth, width),
            fixed(*down.shape),
            fixed(*down_tail.shape),
            fixed(*seg.shape),
            fixed(*table.shape),
            fixed(*slot_sums.shape),
            fixed(*image_index.shape),
            fixed(images, width),
            fixed(1, width),
            fixed(4, 1, width),
            fixed(1, width),
            far,
            far,
            far,
            far,
        ],
        out_specs=[
            far,
            result(depth, own),
            result(own, half),
            result(depth, columns),
            result(images, width),
            result(4 * columns),
            result(2, width),
            result(width),
            result(4 * width),
            result(width),
            result(depth, features),
        ],
        out_shape=[
            shape((rows, local, width), F32),
            shape((depth, own), F32),
            shape((own, half), F32),
            shape((depth, columns), F32),
            shape((images, width), F32),
            shape((4 * columns,), F32),
            shape((2, width), F32),
            shape((width,), F32),
            shape((4 * width,), F32),
            shape((width,), F32),
            shape((depth, features), F32),
        ],
        scratch_shapes=[
            vmem(BF16, rows, 3, heads, size, length),
            vmem(BF16, rows, 3, 4, heads, size, local),
            vmem(F32, length, size),
            vmem(F32, length, size),
            vmem(BF16, length, size),
            vmem(BF16, length, size),
            vmem(F32, features, width),
            vmem(F32, width, length),
            vmem(BF16, 4, depth, features),
            vmem(BF16, 4, depth, features),
            vmem(BF16, 3, depth, width),
            vmem(BF16, 4, depth, own),
            vmem(BF16, 3, depth, own),
            vmem(F32, 2, depth, half),
            vmem(F32, depth, half),
            vmem(F32, depth, features),
            vmem(BF16, 3, depth, features),
            vmem(BF16, 3, width, width),
            vmem(BF16, rows, local, width),
            vmem(F32, rows, local, width),
            vmem(F32, rows, local, width),
            vmem(F32, width, local),
            vmem(F32, images, 6 * width),
            vmem(F32, 8, 3 * width),
            vmem(F32, 4, images, columns),
            vmem(F32, 3, images, columns),
            vmem(F32, 4, 2, width),
            vmem(F32, 3, 2, width),
            vmem(BF16, 4, 2, images, columns),
            vmem(F32, 2, 4, columns),
            vmem(F32, 4, 4, columns),
            vmem(F32, 4, 4, columns),
            vmem(F32, 4, images, width),
            vmem(BF16, 8, images, depth),
            vmem(BF16, 8, images, depth),
            vmem(F32, 3, depth, own),
            vmem(F32, 3, depth, own),
            dma(3 * count),
            dma(3 * count),
            dma(count),
            dma(8),
            dma(rows),
            dma(copies),
            dma(copies),
            vmem(BF16, length, width),
        ],
        compiler_params=pltpu.CompilerParams(vmem_limit_bytes=VMEM_LIMIT, collective_id=3, has_side_effects=True),
        cost_estimate=pl.CostEstimate(
            flops=20 * rows * heads * length * length * 128,
            bytes_accessed=16 * rows * heads * length * size,
            transcendentals=rows * heads * length * length,
        ),
    )(
        col,
        row,
        packed,
        packed,
        packed,
        out,
        grad_out,
        lse,
        normed,
        proj_own,
        proj_low,
        down,
        down_tail,
        seg,
        table,
        slot_sums,
        image_index,
        conditioning,
        *biases,
        tokens,
        grad_middle,
        weight,
        ada,
    )


def forward_kernel(
    block,
    image_index,
    seg,
    fill,
    conditioning,
    ada_bias,
    qv_bias,
    proj_bias,
    tokens,
    ada,
    weight,
    proj,
    cotangent,
    normed_ref,
    packed_ref,
    attended_ref,
    features_ref,
    branch_ref,
    middle_ref,
    inner_ref,
    grad_ref,
    inner_turned_ref,
    grad_turned_ref,
    table_ref,
    code_row,
    code_col,
    lse_ref,
    bias_sum,
    here,
    normed_all,
    packed_all,
    ada_here,
    windows,
    turned,
    own_weight,
    bias_turned,
    mod_all,
    table,
    seg_all,
    attended_all,
    attended_got,
    flat,
    features_all,
    proj_here,
    cotangent_here,
    branch_all,
    middle_all,
    inner_all,
    grad_all,
    inner_turned,
    grad_turned,
    rows_turned,
    load_sem,
    own_sem,
    mod_sent,
    mod_came,
    sent,
    came,
    forward_sent,
    forward_came,
    heads_sent,
    heads_came,
    heads_kept,
    store_sem,
    last_sem,
):
    rows, _, local, width = here.shape
    _, parts, heads, size, length = packed_all.shape
    own, depth, half = heads * size, width // 8, local // 2
    columns = ada_here.shape[0]
    images, slots = conditioning.shape[0], image_index.shape[1]
    slot_col = slot_column(slots)
    scale = size**-0.5 * LOG2E
    seq = lax.axis_index("seq")
    core = lax.rem(lax.axis_index("rows"), 2)
    places = [seq] + peers_of(seq)
    peers = [{"seq": place} for place in places]


    def direct(r, m):
        index = r * 2 + m - 1
        return send_to(tokens.at[r], here.at[r, m], sent.at[index], came.at[index], peers[m])

    def forward(r, m):
        part = pl.ds(0, half) if m == 1 else pl.ds(half, half)
        index = r * 2 + m - 1
        return send_to(
            here.at[r, 3 - m, part], here.at[r, 3, part], forward_sent.at[index], forward_came.at[index], peers[m]
        )

    def go(copies):
        for copy in copies:
            copy.start()

    def end(copies):
        for copy in copies:
            copy.wait()

    own_copies = [pltpu.make_async_copy(tokens.at[r], here.at[r, 0], own_sem.at[r]) for r in range(rows)]
    load_ada = pltpu.make_async_copy(ada, ada_here, load_sem.at[0])
    load_windows = []
    for part in range(3):
        lanes = pl.ds(pl.multiple_of(part * width + seq * 256, 128), 384)
        load_windows.append(pltpu.make_async_copy(weight.at[:, lanes], windows.at[part], load_sem.at[1 + part]))
    load_proj = pltpu.make_async_copy(proj, proj_here, load_sem.at[4])
    load_cotangent = pltpu.make_async_copy(cotangent, cotangent_here, load_sem.at[5])
    go([load_ada] + load_windows + own_copies + [load_proj, load_cotangent])
    greet(peers[1:])
    go([direct(0, m) for m in (1, 2)])

    value = conditioning[...].astype(F32)
    low = (value / (1.0 + jnp.exp(-value))).astype(BF16)
    load_ada.wait()
    mod_all[seq] = lax.dot_general(low, ada_here[...], (((1,), (1,)), ((), ())), preferred_element_type=F32)
    mod_copies = [
        send_to(mod_all.at[seq], mod_all.at[seq], mod_sent.at[m - 1], mod_came.at[m - 1], peers[m]) for m in range(1, 4)
    ]
    go(mod_copies)

    for m in range(4):
        lanes = pl.ds(pl.multiple_of(places[m] * local, 128), local)
        found = seg[:, lanes]
        where = places[m] * local + lax.broadcasted_iota(jnp.int32, (1, local), 1)
        for r in range(rows):
            code = jnp.where(where < fill[r], found[r : r + 1], -1 - where)
            seg_all[r, m] = found[r : r + 1]
            code_row[r, :, m * local : (m + 1) * local] = code
            column = jnp.broadcast_to(code.astype(F32), (128, local)).T[:, :1]
            code_col[r, m * local : (m + 1) * local] = column.astype(jnp.int32)

    for part in range(3):
        load_windows[part].wait()
        turned[...] = windows[part].astype(F32).T
        own_weight[part * own : (part + 1) * own] = turned[pl.ds(pl.multiple_of(seq * 32, 8), own), :].astype(BF16)
    window = qv_bias[:, pl.ds(pl.multiple_of(seq * 256, 128), 384)].astype(F32)
    bias_turned[...] = jnp.concatenate([window, jnp.zeros((6, 384), F32)], axis=0).T
    bias = bias_turned[pl.ds(pl.multiple_of(seq * 32, 8), own), :]
    bias = jnp.concatenate([bias[:, 0:1], jnp.zeros((own, 1), F32), bias[:, 1:2]], axis=0)

    end([direct(0, m) for m in (1, 2)])
    go([forward(0, m) for m in (1, 2)] + [direct(1, m) for m in (1, 2)])

    end(mod_copies)
    bias_all = ada_bias[...].astype(F32).reshape(1, 4 * columns)
    proj_line = proj_bias[...].astype(F32).reshape(1, width)
    for place in range(4):
        lanes = slice(place * columns, (place + 1) * columns)
        table[:, lanes] = mod_all[place] + bias_all[:, lanes]
    stacked = jnp.concatenate(split_low(table[...]), axis=0)
    image_col = lax.rem(lax.broadcasted_iota(jnp.int32, (3 * images, slots), 0), images)
    for r in range(rows):
        picked = (image_col == image_index[r : r + 1]).astype(BF16)
        table_ref[r] = lax.dot_general(picked, stacked, (((0,), (0,)), ((), ())), preferred_element_type=F32)

    def stores(r, m):
        index = r * 4 + m
        lanes = pl.ds(m * local, local)
        return (
            pltpu.make_async_copy(normed_all.at[r, m], normed_ref.at[r, m], store_sem.at[0, index]),
            pltpu.make_async_copy(packed_all.at[r, :, :, :, lanes], packed_ref.at[r, :, :, :, lanes], store_sem.at[1, index]),
        )

    def work(r, m):
        mods = per_token(slot_col, seg_all[r, m], table_ref[r, :, : 2 * width])
        normal, _ = normalize(here[r, m].astype(F32))
        normed = (normal * (1.0 + mods[:, width:]) + mods[:, :width]).astype(BF16)
        normed_all[r, m] = normed
        mixed = lax.dot_general(own_weight[...], normed, (((1,), (1,)), ((), ())), preferred_element_type=F32)
        mixed = (mixed + bias).astype(BF16)
        for part in range(parts):
            for head in range(heads):
                start = (part * heads + head) * size
                packed_all[r, part, head, :, m * local : (m + 1) * local] = mixed[start : start + size]
        go(stores(r, m))

    def to_peer(r, h, m):
        source = attended_all.at[r, h, :, pl.ds(m * local, local)]
        place = (r * heads + h) * 3 + m - 1
        return send_to(source, attended_got.at[r, seq, h], heads_sent.at[place], heads_came.at[place], peers[m])

    def to_self(r, h):
        source = attended_all.at[r, h, :, pl.ds(0, local)]
        return pltpu.make_async_copy(source, attended_got.at[r, seq, h], heads_kept.at[r * heads + h])

    def attend_head(r, h):
        keys = packed_all[r, 1, h].astype(F32).T.astype(BF16)
        values = packed_all[r, 2, h]
        codes = code_col[r]
        for step in range(length // block):
            lanes = pl.ds(step * block, block)
            scores = jnp.dot(keys, packed_all[r, 0, h, :, lanes], preferred_element_type=F32)
            scores = jnp.where(codes == code_row[r, :, lanes], scores * scale, -1e30)
            peak = jnp.max(scores, axis=0, keepdims=True)
            raised = jnp.exp2(scores - peak)
            total = jnp.sum(raised, axis=0, keepdims=True)
            probs = (raised * (1.0 / total)).astype(BF16)
            attended_all[r, h, :, lanes] = jnp.dot(values, probs, preferred_element_type=F32).astype(BF16)
            lse_ref[r, h, :, lanes] = peak + jnp.log2(total)
        to_self(r, h).start()
        for m in range(1, 4):
            to_peer(r, h, m).start()

    def attend_row(r, first, last):
        @pl.loop(first, last)
        def _(h):
            attend_head(r, h)

    def last_stores(r):
        lines, lanes = pl.ds(r * local, local), pl.ds(r * local, local)
        pairs = (
            (grad_all.at[r], grad_ref.at[lines]),
            (grad_turned.at[r], grad_turned_ref.at[:, lanes]),
            (attended_all.at[r], attended_ref.at[r]),
            (features_all.at[r], features_ref.at[r]),
            (branch_all.at[r], branch_ref.at[r]),
            (middle_all.at[r], middle_ref.at[r]),
            (inner_all.at[r], inner_ref.at[lines]),
            (inner_turned.at[r], inner_turned_ref.at[:, lanes]),
        )
        return [pltpu.make_async_copy(source, target, last_sem.at[r, k]) for k, (source, target) in enumerate(pairs)]

    def turn(values, target, r):
        rows_turned[...] = values.T
        for place in range(4):
            for order in range(2):
                first = pl.multiple_of((2 * place + (core if order == 0 else 1 - core)) * depth, 8)
                start = (4 * order + place) * depth
                target[r, start : start + depth] = rows_turned[pl.ds(first, depth), :].astype(BF16)

    end(own_copies)
    for m in range(3):
        work(0, m)
    end([load_proj, load_cotangent])
    for r in range(rows):
        gate_b = per_token(slot_col, seg_all[r, 0], table_ref[r, :, 5 * width :])
        grad = cotangent_here[r].astype(F32) * gate_b
        grad_all[r] = grad.astype(BF16)
        turn(grad, grad_turned, r)
        sums = jnp.sum(grad.astype(BF16).astype(F32), axis=0, keepdims=True)
        if r == 0:
            bias_sum[...] = sums
        else:
            bias_sum[...] += sums
        go(last_stores(r)[:2])
    def project(r):
        for h in range(heads):
            to_self(r, h).wait()
            for m in range(1, 4):
                to_peer(r, h, m).wait()
        for place in range(4):
            for h in range(heads):
                start = (place * heads + h) * size
                flat[start : start + size] = attended_got[r, place, h].astype(F32)
        features = flat[...].astype(BF16)
        features_all[r] = features
        go(last_stores(r)[2:4])
        mods = per_token(slot_col, seg_all[r, 0], table_ref[r, :, 2 * width : 5 * width])
        gate_a, shift_b, scale_b = (mods[:, k * width : (k + 1) * width] for k in range(3))
        branch = lax.dot_general(features, proj_here[...], (((0,), (0,)), ((), ())), preferred_element_type=F32) + proj_line
        middle = here[r, 0].astype(F32) + gate_a * branch
        branch_all[r] = branch
        middle_all[r] = middle
        go(last_stores(r)[4:6])
        normed = normalize(middle)[0] * (1.0 + scale_b) + shift_b
        inner_all[r] = normed.astype(BF16)
        turn(normed, inner_turned, r)
        go(last_stores(r)[6:])
    end([forward(0, m) for m in (1, 2)])
    work(0, 3)
    attend_row(0, 0, heads // 2)
    end([direct(1, m) for m in (1, 2)])
    go([forward(1, m) for m in (1, 2)])
    attend_row(0, heads // 2, heads)
    for m in range(3):
        work(1, m)
    end([forward(1, m) for m in (1, 2)])
    work(1, 3)
    attend_row(1, 0, heads)
    project(0)
    project(1)
    for r in range(rows):
        for m in range(4):
            end(stores(r, m))
        end(last_stores(r))


def before_feed_forward(image_index, seg, fill, conditioning, ada_bias, qv_bias, proj_bias, tokens, ada, weight, proj, cotangent):
    rows, local, width = tokens.shape
    length = 4 * local
    images, slots = conditioning.shape[0], image_index.shape[1]
    heads, size = HEADS // 4, width // HEADS
    columns = ada.shape[0]
    shape = jax.ShapeDtypeStruct
    vmem = lambda dtype, *dims: pltpu.VMEM(dims, dtype)
    near, far = pl.BlockSpec(memory_space=pltpu.VMEM), pl.BlockSpec(memory_space=pl.ANY)
    dma = lambda *dims: pltpu.SemaphoreType.DMA(dims)
    return pl.pallas_call(
        partial(forward_kernel, 512),
        in_specs=[near] * 2 + [pl.BlockSpec(memory_space=pltpu.SMEM)] + [near] * 4 + [far] * 5,
        out_specs=[far] * 10 + [near] * 5,
        out_shape=[
            shape((rows, 4, local, width), BF16),
            shape((rows, 3, heads, size, length), BF16),
            shape((rows, heads, size, length), BF16),
            shape((rows, width, local), BF16),
            shape((rows, local, width), F32),
            shape((rows, local, width), F32),
            shape((rows * local, width), BF16),
            shape((rows * local, width), BF16),
            shape((width, rows * local), BF16),
            shape((width, rows * local), BF16),
            shape((rows, slots, 6 * width), F32),
            shape((rows, 1, length), jnp.int32),
            shape((rows, length, 1), jnp.int32),
            shape((rows, heads, 1, length), F32),
            shape((1, width), F32),
        ],
        scratch_shapes=[
            vmem(BF16, rows, 4, local, width),
            vmem(BF16, rows, 4, local, width),
            vmem(BF16, rows, 3, heads, size, length),
            vmem(BF16, columns, width),
            vmem(BF16, 3, width, 384),
            vmem(F32, 384, width),
            vmem(BF16, 3 * heads * size, width),
            vmem(F32, 384, 8),
            vmem(F32, 4, images, columns),
            vmem(F32, images, 6 * width),
            vmem(jnp.int32, rows, 4, 1, local),
            vmem(BF16, rows, heads, size, length),
            vmem(BF16, rows, 4, heads, size, local),
            vmem(F32, width, local),
            vmem(BF16, rows, width, local),
            vmem(BF16, width, width),
            vmem(BF16, rows, local, width),
            vmem(F32, rows, local, width),
            vmem(F32, rows, local, width),
            vmem(BF16, rows, local, width),
            vmem(BF16, rows, local, width),
            vmem(BF16, rows, width, local),
            vmem(BF16, rows, width, local),
            vmem(F32, width, local),
            dma(6),
            dma(rows),
            dma(3),
            dma(3),
            dma(2 * rows),
            dma(2 * rows),
            dma(2 * rows),
            dma(2 * rows),
            dma(3 * rows * heads),
            dma(3 * rows * heads),
            dma(rows * heads),
            dma(2, 4 * rows),
            dma(rows, 8),
        ],
        compiler_params=pltpu.CompilerParams(vmem_limit_bytes=VMEM_LIMIT, collective_id=6, has_side_effects=True),
        cost_estimate=pl.CostEstimate(flops=2 * 10**10, bytes_accessed=4 * 10**7, transcendentals=0),
    )(image_index, seg, fill, conditioning, ada_bias, qv_bias, proj_bias, tokens, ada, weight, proj, cotangent)


def hand_out_kernel(places, *refs):
    count = len(places)
    sources, targets = refs[:count], refs[count:]
    held, sems = refs[-count - 1 : -1], refs[-1]
    loads = [pltpu.make_async_copy(sources[k], held[k], sems.at[0, k]) for k in range(count)]
    stores = []
    for k, (index, first, size) in enumerate(places):
        target = targets[index] if size is None else targets[index].at[:, pl.ds(first, size)]
        stores.append(pltpu.make_async_copy(held[k], target, sems.at[1, k]))
    for copy in loads:
        copy.start()
    for load, store in zip(loads, stores):
        load.wait()
        store.start()
    for copy in stores:
        copy.wait()


def hand_out(*results):
    arrays, places, shapes = [], [], []
    for index, result in enumerate(results):
        first = 0
        pieces = result if isinstance(result, tuple) else (result,)
        for piece in pieces:
            size = piece.shape[1] if len(pieces) > 1 else None
            arrays.append(piece)
            places.append((index, first, size))
            first += size or 0
        shape = pieces[0].shape if len(pieces) == 1 else (pieces[0].shape[0], first)
        shapes.append(jax.ShapeDtypeStruct(shape, pieces[0].dtype))
    far = pl.BlockSpec(memory_space=pl.ANY)
    return pl.pallas_call(
        partial(hand_out_kernel, tuple(places)),
        in_specs=[far] * len(arrays),
        out_specs=[far] * len(shapes),
        out_shape=shapes,
        scratch_shapes=[pltpu.VMEM(array.shape, array.dtype) for array in arrays]
        + [pltpu.SemaphoreType.DMA((2, len(arrays)))],
        compiler_params=pltpu.CompilerParams(vmem_limit_bytes=VMEM_LIMIT),
    )(*arrays)


def gather_seq(values):
    count = lax.axis_size("seq")
    if count == 4:
        first, second = swap(values, "seq", 1), swap(values, "seq", 2)
        half = values.shape[0] // 2
        third = jnp.concatenate([swap(second[:half], "seq", 1), swap(first[half:], "seq", 2)], axis=0)
        return [values, first, second, third]
    return [values] + [swap(values, "seq", m) for m in range(1, count)]


def exchange_seq(blocks):
    return [blocks[0]] + [swap(blocks[m], "seq", m) for m in range(1, len(blocks))]


def in_order(blocks, axis):
    index = lax.axis_index("seq")
    stacked = jnp.stack(blocks, axis=axis)
    return flip_blocks(stacked, axis, index)


class Halving:
    def __init__(self, blocks, low_first):
        self.blocks = dict(enumerate(blocks))
        bits = [1 << k for k in range(len(blocks).bit_length() - 1)]
        self.bits = bits if low_first else bits[::-1]

    def send(self):
        self.bit = self.bits.pop(0)
        self.kept = [m for m in self.blocks if not m & self.bit]
        return jnp.stack([self.blocks[m | self.bit] for m in self.kept]).astype(BF16)

    def move(self, sent):
        return swap(sent, "seq", self.bit)

    def add(self, came):
        self.blocks = {m: self.blocks[m] + came[k].astype(F32) for k, m in enumerate(self.kept)}


class Spreading:
    def __init__(self, pick):
        chip, chips = lax.axis_index("rows") // 2, lax.axis_size("rows") // 2
        self.own = pick(chip)
        self.sent = [pick(chip ^ m).astype(BF16) for m in range(1, chips)]

    def move(self):
        self.came = [swap(block, "rows", 2 * (m + 1)) for m, block in enumerate(self.sent)]

    def total(self):
        total = self.own
        for block in self.came:
            total = total + block.astype(F32)
        return total


def columns_of(values, index, size):
    return lax.dynamic_slice_in_dim(values, index * size, size, values.ndim - 1)


def lines_of(values, index, size):
    return lax.dynamic_slice_in_dim(values, index * size, size, 0)


def tied(*values):
    return lax.optimization_barrier(values)


def on_square(
    tokens,
    conditioning,
    segment_ids,
    image_index,
    row_fill,
    ada_weight,
    ada_bias,
    qkv_weight,
    qv_bias,
    proj_weight,
    proj_bias,
    up_weight,
    up_bias,
    down_weight,
    down_bias,
    cotangent,
):
    row_count, local_len, width = tokens.shape
    seq_count, groups = lax.axis_size("seq"), lax.axis_size("rows")
    seq_index, row_index = lax.axis_index("seq"), lax.axis_index("rows")
    chips, core = groups // 2, row_index % 2
    full_len = local_len * seq_count
    token_count = row_count * local_len
    heads_dev = HEADS // seq_count
    head_size = width // HEADS
    own = heads_dev * head_size
    image_count = conditioning.shape[0]
    hidden_size = up_weight.shape[1]
    depth = width // groups

    (
        normed_all,
        packed,
        attended,
        attended_tok,
        branch_a,
        middle,
        normed_b,
        grad_out,
        normed_turned,
        grad_turned,
        slot_mod,
        code_row,
        code_col,
        log_totals,
        part_down_bias,
    ) = before_feed_forward(
        image_index,
        segment_ids,
        row_fill,
        conditioning,
        ada_bias,
        qv_bias,
        proj_bias,
        tokens,
        ada_weight.T,
        qkv_weight,
        proj_weight,
        cotangent,
    )
    normed_all = normed_all.reshape(row_count, full_len, width)
    out_sum, grad_sum, part_up_bias, up_main, down_main, *left = feed_forward_reduce(
        normed_b, grad_out, normed_turned, grad_turned, up_weight, down_weight, up_bias
    )
    block_out, grad_middle, grad_view, slot_sums, part_proj_bias, proj_own, proj_low, up_tail, down_tail = after_feed_forward(
        segment_ids,
        slot_mod,
        attended_tok,
        proj_weight,
        down_bias,
        out_sum,
        grad_sum,
        middle,
        branch_a,
        cotangent,
        left,
    )
    grad_view = grad_view.reshape(row_count, heads_dev, head_size, full_len)
    (
        grad_tokens,
        grad_proj_weight,
        grad_down_weight,
        grad_ada_weight,
        grad_cond,
        grad_ada_bias,
        grad_qv_bias,
        grad_proj_bias,
        grad_up_bias,
        grad_down_bias,
        grad_qkv_weight,
    ) = attend_back_and_finish(
        packed,
        attended,
        grad_view,
        log_totals,
        code_col,
        code_row,
        normed_all,
        proj_own,
        proj_low,
        down_main,
        down_tail,
        segment_ids,
        slot_mod,
        slot_sums,
        image_index,
        conditioning,
        (part_proj_bias, part_up_bias, part_down_bias),
        tokens,
        grad_middle,
        qkv_weight,
        ada_weight.T,
    )
    results = list(hand_out(
        block_out,
        grad_tokens,
        grad_cond,
        grad_ada_weight,
        grad_ada_bias,
        grad_qkv_weight,
        grad_qv_bias,
        grad_proj_weight,
        grad_proj_bias,
        (up_main, up_tail),
        grad_up_bias,
        grad_down_weight,
        grad_down_bias,
    ))
    results[11] = results[11].T
    return tuple(results)


def on_device(
    tokens,
    conditioning,
    segment_ids,
    image_index,
    row_fill,
    ada_weight,
    ada_bias,
    qkv_weight,
    qv_bias,
    proj_weight,
    proj_bias,
    up_weight,
    up_bias,
    down_weight,
    down_bias,
    cotangent,
):
    row_count, local_len, width = tokens.shape
    seq_count, groups = lax.axis_size("seq"), lax.axis_size("rows")
    seq_index, row_index = lax.axis_index("seq"), lax.axis_index("rows")
    chips, core = groups // 2, row_index % 2
    full_len = local_len * seq_count
    token_count = row_count * local_len
    heads_dev = HEADS // seq_count
    head_size = width // HEADS
    own = heads_dev * head_size
    image_count = conditioning.shape[0]
    hidden_size = up_weight.shape[1]
    depth = width // groups

    tokens_all = jnp.concatenate(gather_seq(tokens), axis=1)
    order = lax.iota(jnp.int32, seq_count) ^ seq_index
    seg_blocks = flip_blocks(segment_ids.reshape(row_count, seq_count, local_len), 1, seq_index)
    seg_all = seg_blocks.reshape(row_count, full_len)
    places = (order[:, None] * local_len + lax.iota(jnp.int32, local_len)).reshape(1, full_len)
    codes = jnp.where(places < row_fill[:, None], seg_all, -1 - places)
    code_col, code_row = codes[:, :, None], codes[:, None, :]

    qkv_own = jnp.concatenate(
        [lax.dynamic_slice_in_dim(qkv_weight, part * width + seq_index * own, own, 1).T for part in range(3)], axis=0
    )
    bias_own = lax.dynamic_slice_in_dim(qv_bias.astype(F32), seq_index * own, own, 1)
    bias_own = jnp.concatenate([bias_own[0], jnp.zeros((own,), F32), bias_own[1]])

    cond_wide = conditioning.astype(F32)
    cond_low = jax.nn.silu(cond_wide).astype(BF16)
    mod_part = jnp.dot(cond_low, ada_weight, preferred_element_type=F32)
    modulation = lax.all_gather(mod_part, "seq", axis=1, tiled=True) + ada_bias.astype(F32)
    cond_cols = cond_low.reshape(image_count, groups, depth).transpose(1, 0, 2)
    local_seg = lax.dynamic_slice_in_dim(segment_ids, seq_index * local_len, local_len, 1)
    slot_ids = lax.iota(jnp.int32, image_index.shape[1])
    slot_mod = jnp.take(modulation, image_index, axis=0)

    normed_all, packed = project_qkv(
        tokens_all, seg_all, slot_mod[:, :, : 2 * width], qkv_own, bias_own, heads_dev, min(256, full_len)
    )
    square = seq_count == 4 and chips == 4
    attended, log_totals, *attended_sent = attend(packed, code_col, code_row, 512, square)

    slot_pick = (local_seg[:, :, None] == slot_ids).astype(F32)
    mod_tok = jnp.einsum("rts,rse->rte", slot_pick, slot_mod, precision=lax.Precision.HIGHEST)
    shift_a, scale_a, gate_a, shift_b, scale_b, gate_b = jnp.split(mod_tok, 6, axis=-1)
    tokens_wide = tokens.astype(F32)
    upstream = cotangent.astype(F32)
    grad_branch_b = (upstream * gate_b).astype(BF16)
    part_down_bias = jnp.sum(grad_branch_b.astype(F32), axis=(0, 1))
    grad_out = grad_branch_b.reshape(token_count, width)
    grad_turned = turn_halves(grad_out, seq_count, core)

    def by_block(values):
        return [values[..., m * local_len : (m + 1) * local_len] for m in range(seq_count)]

    if square:
        attended_tok = attended_sent[0]
    else:
        attended_tok = in_order(exchange_seq(by_block(attended.reshape(row_count, own, full_len))), 1)
    attended_tok = attended_tok.reshape(row_count, width, local_len)
    branch_a = jnp.einsum(
        "rft,fe->rte", attended_tok, proj_weight, preferred_element_type=F32
    ) + proj_bias.astype(F32)
    middle = tokens_wide + gate_a * branch_a
    normed_b = modulate(middle, shift_b, scale_b).astype(BF16).reshape(token_count, width)
    normed_turned = turn_halves(normed_b, chips, core)

    if square:
        out_sum, grad_sum, part_up_bias, grad_up_weight, down_turned = feed_forward_reduce(
            normed_b, grad_out, normed_turned, grad_turned, up_weight, down_weight, up_bias.astype(F32)
        )
        part_up_bias = part_up_bias.reshape(1, hidden_size)
    else:
        out_sum, grad_sum, up_keep, up_send, down_keep, down_send, part_up_bias = feed_forward(
            normed_b, grad_out, normed_turned, grad_turned, up_weight, down_weight, up_bias.astype(F32)[None], 512
        )
        up_came, down_came = swap(up_send, "rows", 1), swap(down_send, "rows", 1)
    branch_b = out_sum.reshape(row_count, local_len, width) + down_bias.astype(F32)
    grad_normed_b = grad_sum.reshape(row_count, local_len, width)
    block_out = (middle + gate_b * branch_b).astype(BF16)
    grad_gate_b = upstream * branch_b
    _, norm_back_b = jax.vjp(modulate, middle, shift_b, scale_b)
    grad_mid_norm, grad_shift_b, grad_scale_b = norm_back_b(grad_normed_b)
    grad_middle = upstream + grad_mid_norm
    grad_branch_a = (grad_middle * gate_a).astype(BF16)
    grad_gate_a = grad_middle * branch_a
    part_proj_bias = jnp.sum(grad_branch_a.astype(F32), axis=(0, 1))
    grad_attended = jnp.einsum(
        "fe,rte->rft", proj_weight, grad_branch_a, preferred_element_type=F32
    ).astype(BF16)
    heads_blocks = [lax.dynamic_slice_in_dim(grad_attended, (seq_index ^ m) * own, own, 1) for m in range(seq_count)]
    grad_heads_in = jnp.concatenate(exchange_seq(heads_blocks), axis=2)
    grad_view = grad_heads_in.reshape(row_count, heads_dev, head_size, full_len)

    part_proj = jnp.einsum("rte,rft->ef", grad_branch_a, attended_tok, preferred_element_type=F32)
    proj_view = part_proj.reshape(seq_count, 2, depth * groups // (2 * seq_count), width)
    proj_keep = lax.dynamic_index_in_dim(proj_view, core, 1, keepdims=False)
    proj_send = lax.dynamic_index_in_dim(proj_view, 1 - core, 1, keepdims=False).astype(BF16)
    proj_came = swap(proj_send, "rows", 1).reshape(width // 2, width)
    proj_keep = proj_keep.reshape(width // 2, width)
    up_size, down_size = hidden_size // seq_count, width // (2 * seq_count)
    proj_blocks = [
        lines_of(proj_keep, seq_index ^ m, down_size) + lines_of(proj_came, seq_index ^ m, down_size).astype(F32)
        for m in range(seq_count)
    ]
    if square:
        proj_sent = [block.astype(BF16) for block in proj_blocks[1:]]
        grad_view, *proj_sent = tied(grad_view, *proj_sent)
        proj_total = proj_blocks[0]
        for m in range(1, seq_count):
            proj_total = proj_total + swap(proj_sent[m - 1], "seq", m).astype(F32)
    else:
        ups = Halving(
            [
                columns_of(up_keep, seq_index ^ m, up_size) + columns_of(up_came, seq_index ^ m, up_size).astype(F32)
                for m in range(seq_count)
            ],
            True,
        )
        downs = Halving(
            [
                jnp.concatenate(
                    [
                        lines_of(down_keep, seq_index ^ m, down_size)
                        + lines_of(down_came, seq_index ^ m, down_size).astype(F32),
                        proj_blocks[m],
                    ],
                    axis=1,
                )
                for m in range(seq_count)
            ],
            False,
        )
        up_sent, down_sent = ups.send(), downs.send()
        up_came, down_came = ups.move(up_sent), downs.move(down_sent)

    grad_heads, *grad_sent = attend_back(
        packed, attended, grad_view, log_totals, code_col, code_row, 256, 512, square
    )
    grad_own = grad_heads.reshape(row_count, 3 * own, full_len)
    if square:
        grad_flat = grad_sent[0]
    else:
        grad_blocks = exchange_seq(by_block(grad_own))
        grad_flat = in_order([block.reshape(row_count, 3, own, local_len) for block in grad_blocks], 2)
    grad_flat = grad_flat.reshape(row_count, 3 * width, local_len)

    qkv_keep, qkv_send, own_sums = qkv_weight_grad(grad_own, normed_all)
    down_part, proj_part = hidden_size // chips, width // chips
    if square:
        proj_spread = Spreading(lambda chip: columns_of(proj_total, chip, proj_part))
        grad_flat, qkv_send, *proj_spread.sent = tied(grad_flat, qkv_send, *proj_spread.sent)
        proj_spread.move()
    else:
        while ups.bits:
            ups.add(up_came)
            downs.add(down_came)
            up_came, down_came = ups.move(ups.send()), downs.move(downs.send())
        ups.add(up_came)
        downs.add(down_came)
        up_total, down_total = ups.blocks[0], downs.blocks[0][:, :hidden_size]
        proj_total = downs.blocks[0][:, hidden_size:]
        up_spread = Spreading(lambda chip: lines_of(up_total, chip, depth))
        down_spread = Spreading(
            lambda chip: jnp.concatenate(
                [columns_of(down_total, chip, down_part), columns_of(proj_total, chip, proj_part)], axis=1
            )
        )
        up_spread.move()
        down_spread.move()
    qkv_came = swap(qkv_send, "rows", 1)
    grad_normed_a = jnp.einsum("rft,df->rtd", grad_flat, qkv_weight, preferred_element_type=F32)
    _, norm_back_a = jax.vjp(modulate, tokens_wide, shift_a, scale_a)
    grad_tok_norm, grad_shift_a, grad_scale_a = norm_back_a(grad_normed_a)
    grad_tokens = grad_middle + grad_tok_norm
    grad_mod_tok = jnp.concatenate(
        [grad_shift_a, grad_scale_a, grad_gate_a, grad_shift_b, grad_scale_b, grad_gate_b], axis=-1
    )
    slot_grads = jnp.einsum("rts,rte->rse", slot_pick, grad_mod_tok, precision=lax.Precision.HIGHEST)
    image_pick = (image_index[:, :, None] == lax.iota(jnp.int32, image_count)).astype(F32)
    grad_modulation = jnp.einsum("rsi,rse->ie", image_pick, slot_grads, precision=lax.Precision.HIGHEST)

    own_sums = own_sums.reshape(3, own)
    part_qv = lax.dynamic_update_slice(
        jnp.zeros((2, width), F32), jnp.stack([own_sums[0], own_sums[2]]), (0, seq_index * own)
    )
    small = jnp.concatenate([part_qv.reshape(-1), part_proj_bias, part_up_bias[0], part_down_bias])
    columns = ada_weight.shape[1]
    lines = -(-small.size // (seq_count * columns))
    room = seq_count * columns * lines
    small = jnp.pad(small, (0, room - small.size)).reshape(seq_count, lines, columns)
    mod_view = grad_modulation.reshape(image_count, seq_count, columns).transpose(1, 0, 2)
    joined = jnp.concatenate(
        [mod_view, jnp.zeros((seq_count, 1, columns), F32), small, jnp.zeros((seq_count, 7 - lines, columns), F32)], axis=1
    )
    qkv_both = qkv_keep + qkv_came.astype(F32)
    qkv_spread = Spreading(lambda chip: lax.dynamic_index_in_dim(qkv_both, chip, 0, keepdims=False))
    joined, *qkv_spread.sent = tied(joined, *qkv_spread.sent)
    qkv_spread.move()
    if square:
        turned = jnp.concatenate([down_turned, proj_spread.total()], axis=1)
    else:
        grad_up_weight, turned = up_spread.total(), down_spread.total()
    half = down_part // 2
    cut = lambda index: jnp.concatenate(
        [columns_of(turned[:, :down_part], index, half), columns_of(turned[:, down_part:], index, proj_part // 2)], axis=1
    )
    core_keep, core_sent = cut(core), cut(1 - core)
    joined, core_sent = tied(joined, core_sent)
    core_came = swap(core_sent, "rows", 1)
    grad_ada_weight, cond_sum, bias_sums = finish(joined, ada_weight, cond_cols, image_count)
    _, silu_back = jax.vjp(jax.nn.silu, cond_wide)
    grad_cond = silu_back(cond_sum)[0]
    grad_ada_bias = bias_sums[:, 0].reshape(-1)
    small = bias_sums[:, 1 : 1 + lines].reshape(-1)
    grad_qv_bias = small[: 2 * width].reshape(2, width)
    grad_proj_bias = small[2 * width : 3 * width]
    grad_up_bias = small[3 * width : 3 * width + hidden_size]
    grad_down_bias = small[3 * width + hidden_size : 4 * width + hidden_size]

    pair = flip_blocks(jnp.stack([core_keep, core_came]), 0, core).reshape(-1, core_keep.shape[1])
    grad_down_weight, grad_proj_weight = pair[:, :half].T, pair[:, half:].T

    qkv_total = qkv_spread.total()
    pieces = []
    for place in range(3):
        pairs = [((3 * target + place) % seq_count, target) for target in range(seq_count)]
        part_of = [0] * seq_count
        for source, target in pairs:
            part_of[source] = (3 * target + place) // seq_count
        chosen = columns_of(qkv_total, jnp.array(part_of, jnp.int32)[seq_index], own)
        pieces.append(lax.ppermute(chosen, "seq", pairs))
    grad_qkv_weight = jnp.concatenate(pieces, axis=1)
    return (
        block_out,
        grad_tokens,
        grad_cond,
        grad_ada_weight,
        grad_ada_bias,
        grad_qkv_weight,
        grad_qv_bias,
        grad_proj_weight,
        grad_proj_bias,
        grad_up_weight,
        grad_up_bias,
        grad_down_weight,
        grad_down_bias,
    )


def solution(mesh):
    in_specs = (
        P("rows", "seq", None),
        P("rows", None),
        P("rows", None),
        P("rows", None),
        P("rows"),
        P(None, "seq"),
        P(),
        P(),
        P(),
        P(),
        P(),
        P(),
        P(),
        P(),
        P(),
        P("rows", "seq", None),
    )
    out_specs = (
        P("rows", "seq", None),
        P("rows", "seq", None),
        P("rows", None),
        P("rows", "seq"),
        P(),
        P("rows", "seq"),
        P(),
        P("rows", "seq"),
        P(),
        P("rows", "seq"),
        P(),
        P("rows", "seq"),
        P(),
    )
    square = mesh.shape["seq"] == 4 and mesh.shape["rows"] == 8
    return jax.shard_map(
        on_square if square else on_device, mesh=mesh, in_specs=in_specs, out_specs=out_specs, check_vma=False
    )
```

```python
from functools import partial
import math

import jax
import jax.numpy as jnp
from jax import lax
from jax.experimental import pallas as pl
from jax.experimental.pallas import tpu as pltpu
from jax.sharding import PartitionSpec as P

HEADS = 16
LOG2E = math.log2(math.e)
VMEM_LIMIT = 60 << 20
BF16 = jnp.bfloat16
F32 = jnp.float32

norm_eps = 1e-06


def modulate(values, offset, factor):
    center = values - jnp.mean(values, axis=-1, keepdims=True)
    spread = jnp.mean(center * center, axis=-1, keepdims=True)
    return center * lax.rsqrt(spread + norm_eps) * (1.0 + factor) + offset


def gelu_tanh(values):
    return jax.nn.gelu(values, approximate=True)


def swap(values, axis, mask):
    count = lax.axis_size(axis)
    return lax.ppermute(values, axis, [(i, i ^ mask) for i in range(count)])


def flip_blocks(values, axis, mask):
    return jnp.take(values, lax.iota(jnp.int32, values.shape[axis]) ^ mask, axis=axis)


def qkv_kernel(slot_row, seg, mod, tokens, weight, bias, normed_ref, qkv_ref):
    width = tokens.shape[-1]
    values = tokens[0].astype(F32)
    picked = (seg[0] == slot_row[...]).astype(BF16)
    table = mod[0]
    high = table.astype(BF16)
    rest = table - high.astype(F32)
    middle = rest.astype(BF16)
    last = (rest - middle.astype(F32)).astype(BF16)
    stacked = jnp.concatenate([high, middle, last], axis=0)
    per_token = jnp.dot(picked, stacked, preferred_element_type=F32)
    normed = modulate(values, per_token[:, :width], per_token[:, width:]).astype(BF16)
    normed_ref[0] = normed
    mixed = lax.dot_general(weight[...], normed, (((1,), (1,)), ((), ())), preferred_element_type=F32)
    mixed = (mixed + bias[...]).astype(BF16)
    _, parts, heads, size, _ = qkv_ref.shape
    for part in range(parts):
        for head in range(heads):
            start = (part * heads + head) * size
            qkv_ref[0, part, head] = mixed[start : start + size]


def project_qkv(tokens, seg, slot_mod, weight, bias, heads, block):
    rows, length, width = tokens.shape
    slots = slot_mod.shape[1]
    features = weight.shape[0]
    size = features // (3 * heads)
    slot_row = jnp.tile(lax.iota(jnp.int32, slots), 3)[None]
    return pl.pallas_call(
        qkv_kernel,
        grid=(rows, length // block),
        in_specs=[
            pl.BlockSpec((1, 3 * slots), lambda r, t: (0, 0)),
            pl.BlockSpec((1, block, 1), lambda r, t: (r, t, 0)),
            pl.BlockSpec((1, slots, 2 * width), lambda r, t: (r, 0, 0)),
            pl.BlockSpec((1, block, width), lambda r, t: (r, t, 0)),
            pl.BlockSpec((features, width), lambda r, t: (0, 0)),
            pl.BlockSpec((features, 1), lambda r, t: (0, 0)),
        ],
        out_specs=[
            pl.BlockSpec((1, block, width), lambda r, t: (r, t, 0)),
            pl.BlockSpec((1, 3, heads, size, block), lambda r, t: (r, 0, 0, 0, t)),
        ],
        out_shape=[
            jax.ShapeDtypeStruct((rows, length, width), BF16),
            jax.ShapeDtypeStruct((rows, 3, heads, size, length), BF16),
        ],
        compiler_params=pltpu.CompilerParams(vmem_limit_bytes=VMEM_LIMIT),
        cost_estimate=pl.CostEstimate(
            flops=2 * rows * length * width * features,
            bytes_accessed=2 * rows * length * (2 * width + features),
            transcendentals=0,
        ),
    )(slot_row, seg[:, :, None], slot_mod, tokens, weight, bias[:, None])


def peers_of(seq):
    x, y = lax.rem(seq, 2), lax.div(seq, 2)
    return [seq + 1 - 2 * x, seq + 2 - 4 * y, 3 - seq]


def call(devices):
    barrier = pltpu.get_barrier_semaphore()
    for device in devices:
        pl.semaphore_signal(barrier, inc=1, device_id=device, device_id_type=pl.DeviceIdType.MESH)


def meet(devices):
    pl.semaphore_wait(pltpu.get_barrier_semaphore(), len(devices))


def greet(devices):
    call(devices)
    meet(devices)


def send_block(source, target, sent, came, index, device):
    return pltpu.make_async_remote_copy(
        src_ref=source,
        dst_ref=target,
        send_sem=sent.at[index],
        recv_sem=came.at[index],
        device_id=device,
        device_id_type=pl.DeviceIdType.MESH,
    )


def attend_kernel(block, scale, code_col, code_row, query, key, value, out_ref, lse_ref, token_ref=None, sent=None, came=None, kept=None):
    length = query.shape[-1]
    keys = key[0, 0].astype(F32).T.astype(BF16)
    values = value[0, 0]
    codes = code_col[0]
    row, head = (pl.program_id(0), pl.program_id(1)) if sent is not None else (0, 0)
    rows, heads = out_ref.shape[:2]
    if sent is not None:
        seq = lax.axis_index("seq")
        peers = peers_of(seq)
        size = length // 4

        @pl.when((row == 0) & (head == 0))
        def _():
            greet([{"seq": peer} for peer in peers])

        def to_peer(r, h, m):
            lanes = pl.ds(m * size, size)
            place = (r * heads + h) * 3 + m - 1
            return send_block(out_ref.at[r, h, :, lanes], token_ref.at[r, seq, h], sent, came, place, {"seq": peers[m - 1]})

        def to_self(r, h):
            return pltpu.make_async_copy(out_ref.at[r, h, :, pl.ds(0, size)], token_ref.at[r, seq, h], kept.at[r * heads + h])

    for step in range(length // block):
        here = pl.ds(step * block, block)
        scores = jnp.dot(keys, query[0, 0, :, here], preferred_element_type=F32)
        scores = jnp.where(codes == code_row[0, :, here], scores * scale, -1e30)
        peak = jnp.max(scores, axis=0, keepdims=True)
        raised = jnp.exp2(scores - peak)
        total = jnp.sum(raised, axis=0, keepdims=True)
        probs = (raised * (1.0 / total)).astype(BF16)
        out_ref[row, head, :, here] = jnp.dot(values, probs, preferred_element_type=F32).astype(BF16)
        lse_ref[0, 0, :, here] = peak + jnp.log2(total)

    if sent is not None:
        to_self(row, head).start()
        for m in range(1, 4):
            to_peer(row, head, m).start()

        @pl.when((row == rows - 1) & (head == heads - 1))
        def _():
            for r in range(rows):
                for h in range(heads):
                    to_self(r, h).wait()
                    for m in range(1, 4):
                        to_peer(r, h, m).wait()


def attend(packed, col, row, block, exchange):
    rows, _, heads, size, length = packed.shape
    part = lambda j: pl.BlockSpec((1, None, 1, size, length), lambda r, h: (r, j, h, 0, 0))
    out_specs = [
        pl.BlockSpec((1, 1, size, length), lambda r, h: (r, h, 0, 0)),
        pl.BlockSpec((1, 1, 1, length), lambda r, h: (r, h, 0, 0)),
    ]
    out_shape = [
        jax.ShapeDtypeStruct((rows, heads, size, length), BF16),
        jax.ShapeDtypeStruct((rows, heads, 1, length), F32),
    ]
    scratch = []
    extra = {}
    if exchange:
        out_specs[0] = pl.BlockSpec((rows, heads, size, length), lambda r, h: (0, 0, 0, 0))
        out_specs.append(pl.BlockSpec(memory_space=pl.ANY))
        out_shape.append(jax.ShapeDtypeStruct((rows, 4, heads, size, length // 4), BF16))
        count = rows * heads
        scratch = [pltpu.SemaphoreType.DMA((3 * count,)), pltpu.SemaphoreType.DMA((3 * count,)), pltpu.SemaphoreType.DMA((count,))]
        extra = dict(collective_id=2, has_side_effects=True)
    return pl.pallas_call(
        partial(attend_kernel, block, size**-0.5 * LOG2E),
        grid=(rows, heads),
        in_specs=[
            pl.BlockSpec((1, length, 1), lambda r, h: (r, 0, 0)),
            pl.BlockSpec((1, 1, length), lambda r, h: (r, 0, 0)),
            part(0),
            part(1),
            part(2),
        ],
        out_specs=out_specs,
        out_shape=out_shape,
        scratch_shapes=scratch,
        compiler_params=pltpu.CompilerParams(vmem_limit_bytes=VMEM_LIMIT, **extra),
        cost_estimate=pl.CostEstimate(
            flops=8 * rows * heads * length * length * 128,
            bytes_accessed=8 * rows * heads * length * size,
            transcendentals=rows * heads * length * length,
        ),
    )(col, row, packed, packed, packed)


def attend_back_kernel(
    block,
    inner,
    scale,
    exchange,
    code_col,
    code_row,
    query,
    key,
    value,
    out,
    grad_out,
    lse,
    grad_ref,
    *rest,
):
    length = query.shape[-1]
    size = query.shape[-2]
    row, head = (pl.program_id(0), pl.program_id(1)) if exchange else (0, 0)
    rows, _, heads = grad_ref.shape[:3]
    if exchange:
        token_ref, key_sum, value_sum, keys, values, sent, came, kept = rest
        seq = lax.axis_index("seq")
        peers = peers_of(seq)
        local = length // 4

        @pl.when((row == 0) & (head == 0))
        def _():
            greet([{"seq": peer} for peer in peers])

        def to_peer(r, h, m):
            lanes = pl.ds(m * local, local)
            place = (r * heads + h) * 3 + m - 1
            return send_block(grad_ref.at[r, :, h, :, lanes], token_ref.at[r, :, seq, h], sent, came, place, {"seq": peers[m - 1]})

        def to_self(r, h):
            lanes = pl.ds(0, local)
            return pltpu.make_async_copy(grad_ref.at[r, :, h, :, lanes], token_ref.at[r, :, seq, h], kept.at[r * heads + h])

    else:
        key_sum, value_sum, keys, values = rest
    keys[...] = key[0, 0].astype(F32).T.astype(BF16)
    values[...] = value[0, 0].astype(F32).T.astype(BF16)
    for step in range(length // block):
        here = pl.ds(step * block, block)
        query_low = query[0, 0, :, here]
        grad_low = grad_out[0, 0, :, here]
        query_rows = query_low.astype(F32).T.astype(BF16)
        grad_rows = grad_low.astype(F32).T.astype(BF16)
        row_dot = jnp.sum(grad_low.astype(F32) * out[0, 0, :, here].astype(F32), axis=0, keepdims=True)
        grad_query = jnp.zeros((size, block), F32)
        for part in range(length // inner):
            there = pl.ds(part * inner, inner)
            scores = jnp.dot(keys[there, :], query_low, preferred_element_type=F32)
            scores = jnp.where(code_col[0, there, :] == code_row[0, :, here], scores * (scale * LOG2E), -1e30)
            probs = jnp.exp2(scores - lse[0, 0, :, here])
            grad_probs = jnp.dot(values[there, :], grad_low, preferred_element_type=F32)
            grad_raw = (probs * (grad_probs - row_dot) * scale).astype(BF16)
            value_part = jnp.dot(probs.astype(BF16), grad_rows, preferred_element_type=F32)
            key_part = jnp.dot(grad_raw, query_rows, preferred_element_type=F32)
            if step == 0:
                value_sum[there, :] = value_part
                key_sum[there, :] = key_part
            else:
                value_sum[there, :] += value_part
                key_sum[there, :] += key_part
            grad_query += jnp.dot(key[0, 0, :, there], grad_raw, preferred_element_type=F32)
        grad_ref[row, 0, head, :, here] = grad_query.astype(BF16)
    grad_ref[row, 1, head] = key_sum[...].T.astype(BF16)
    grad_ref[row, 2, head] = value_sum[...].T.astype(BF16)

    if exchange:
        to_self(row, head).start()
        for m in range(1, 4):
            to_peer(row, head, m).start()

        @pl.when((row == rows - 1) & (head == heads - 1))
        def _():
            for r in range(rows):
                for h in range(heads):
                    to_self(r, h).wait()
                    for m in range(1, 4):
                        to_peer(r, h, m).wait()


def attend_back(packed, out, grad_out, lse, col, row, block, inner, exchange):
    rows, _, heads, size, length = packed.shape
    part = lambda j: pl.BlockSpec((1, None, 1, size, length), lambda r, h: (r, j, h, 0, 0))
    whole = pl.BlockSpec((1, 1, size, length), lambda r, h: (r, h, 0, 0))
    out_specs = [pl.BlockSpec((1, 3, 1, size, length), lambda r, h: (r, 0, h, 0, 0))]
    out_shape = [jax.ShapeDtypeStruct((rows, 3, heads, size, length), BF16)]
    scratch = []
    extra = {}
    if exchange:
        out_specs = [
            pl.BlockSpec((rows, 3, heads, size, length), lambda r, h: (0, 0, 0, 0, 0)),
            pl.BlockSpec(memory_space=pl.ANY),
        ]
        out_shape.append(jax.ShapeDtypeStruct((rows, 3, 4, heads, size, length // 4), BF16))
        count = rows * heads
        scratch = [pltpu.SemaphoreType.DMA((3 * count,)), pltpu.SemaphoreType.DMA((3 * count,)), pltpu.SemaphoreType.DMA((count,))]
        extra = dict(collective_id=3, has_side_effects=True)
    return pl.pallas_call(
        partial(attend_back_kernel, block, inner, size**-0.5, exchange),
        grid=(rows, heads),
        in_specs=[
            pl.BlockSpec((1, length, 1), lambda r, h: (r, 0, 0)),
            pl.BlockSpec((1, 1, length), lambda r, h: (r, 0, 0)),
            part(0),
            part(1),
            part(2),
            whole,
            whole,
            pl.BlockSpec((1, 1, 1, length), lambda r, h: (r, h, 0, 0)),
        ],
        out_specs=out_specs,
        out_shape=out_shape,
        scratch_shapes=[
            pltpu.VMEM((length, size), F32),
            pltpu.VMEM((length, size), F32),
            pltpu.VMEM((length, size), BF16),
            pltpu.VMEM((length, size), BF16),
        ]
        + scratch,
        compiler_params=pltpu.CompilerParams(vmem_limit_bytes=VMEM_LIMIT, **extra),
        cost_estimate=pl.CostEstimate(
            flops=20 * rows * heads * length * length * 128,
            bytes_accessed=16 * rows * heads * length * size,
            transcendentals=rows * heads * length * length,
        ),
    )(col, row, packed, packed, packed, out, grad_out, lse)


def mlp_kernel(
    normed, grad_out, normed_turned, grad_turned, up, down, bias, out_sum, grad_sum, up_keep, up_send, down_keep, down_send, bias_sum
):
    step = pl.program_id(0)
    half = up_keep.shape[0]
    c0 = math.sqrt(2 / math.pi)
    c1 = c0 * 0.044715
    hidden = jnp.dot(normed[...], up[...], preferred_element_type=F32) + bias[...]
    square = hidden * hidden
    gate = 0.5 + 0.5 * jnp.tanh(hidden * (c0 + c1 * square))
    raised = hidden * gate
    slope = gate + raised * (1.0 - gate) * (2 * c0 + 6 * c1 * square)
    active = raised.astype(BF16)
    back = (((1,), (1,)), ((), ()))
    grad_active = lax.dot_general(grad_out[...], down[...], back, preferred_element_type=F32)
    grad_wide = (grad_active * slope).astype(BF16)
    out_part = jnp.dot(active, down[...], preferred_element_type=F32)
    grad_part = lax.dot_general(grad_wide, up[...], back, preferred_element_type=F32)

    @pl.when(step == 0)
    def _():
        out_sum[...] = out_part
        grad_sum[...] = grad_part

    @pl.when(step > 0)
    def _():
        out_sum[...] += out_part
        grad_sum[...] += grad_part

    bias_sum[...] = jnp.sum(grad_wide.astype(F32), axis=0, keepdims=True)
    up_keep[...] = jnp.dot(normed_turned[:half], grad_wide, preferred_element_type=F32)
    up_send[...] = jnp.dot(normed_turned[half:], grad_wide, preferred_element_type=F32).astype(BF16)
    down_keep[...] = jnp.dot(grad_turned[:half], active, preferred_element_type=F32)
    down_send[...] = jnp.dot(grad_turned[half:], active, preferred_element_type=F32).astype(BF16)


def feed_forward(normed, grad_out, normed_turned, grad_turned, up, down, bias, tile):
    count, width = normed.shape
    hidden = up.shape[1]
    half = width // 2
    fixed = lambda *shape: pl.BlockSpec(shape, lambda t: (0, 0))
    across = lambda rows: pl.BlockSpec((rows, tile), lambda t: (0, t))
    shape = jax.ShapeDtypeStruct
    return pl.pallas_call(
        mlp_kernel,
        grid=(hidden // tile,),
        in_specs=[
            fixed(count, width),
            fixed(count, width),
            fixed(width, count),
            fixed(width, count),
            across(width),
            pl.BlockSpec((tile, width), lambda t: (t, 0)),
            across(1),
        ],
        out_specs=[fixed(count, width), fixed(count, width), across(half), across(half), across(half), across(half), across(1)],
        out_shape=[
            shape((count, width), F32),
            shape((count, width), F32),
            shape((half, hidden), F32),
            shape((half, hidden), BF16),
            shape((half, hidden), F32),
            shape((half, hidden), BF16),
            shape((1, hidden), F32),
        ],
        compiler_params=pltpu.CompilerParams(vmem_limit_bytes=VMEM_LIMIT),
        cost_estimate=pl.CostEstimate(
            flops=12 * count * width * hidden,
            bytes_accessed=10 * width * hidden,
            transcendentals=count * hidden,
        ),
    )(normed, grad_out, normed_turned, grad_turned, up, down, bias)


def turn_halves(values, groups, mine):
    count, width = values.shape
    view = values.T.reshape(groups, 2, width // (2 * groups), count)
    keep = lax.dynamic_index_in_dim(view, mine, 1, keepdims=False).reshape(width // 2, count)
    send = lax.dynamic_index_in_dim(view, 1 - mine, 1, keepdims=False).reshape(width // 2, count)
    return jnp.concatenate([keep, send], axis=0)


STAGES = 2


def mlp_reduce_kernel(
    tiles,
    normed,
    grad_out,
    normed_turned,
    grad_turned,
    up0,
    up1,
    up2,
    up3,
    down0,
    down1,
    down2,
    down3,
    bias,
    out_sum,
    grad_sum,
    bias_sum,
    up_total,
    down_total,
    left_full,
    left_up,
    left_up_low,
    left_down,
    left_down_low,
    up_mine,
    down_mine,
    up_core,
    down_core,
    up_core_got,
    down_core_got,
    up_half,
    down_half,
    up_out,
    down_out,
    up_got,
    down_got,
    up_quarter,
    down_quarter,
    up_last,
    down_last,
    up_last_got,
    down_last_got,
    chip_full,
    chip_out,
    chip_got,
    core_sent,
    core_came,
    seq_sent,
    seq_came,
    last_sent,
    last_came,
    chip_sent,
    chip_came,
    bias_line,
):
    step = pl.program_id(0)
    seq, row = lax.axis_index("seq"), lax.axis_index("rows")
    half = normed_turned.shape[0] // 2
    x, y = lax.rem(seq, 2), lax.div(seq, 2)
    core_peer = {"rows": row + 1 - 2 * lax.rem(row, 2)}
    x_peer = {"seq": seq + 1 - 2 * x}
    y_peer = {"seq": seq + 2 - 4 * y}
    chip, core = lax.div(row, 2), lax.rem(row, 2)
    to_chip = [lax.rem(chip + k, 4) for k in range(4)]
    chip_peers = [{"rows": 2 * to_chip[k] + core} for k in range(4)]

    @pl.when(step == 0)
    def _():
        bias_line[...] = bias[...].astype(F32).reshape(1, bias.shape[0])
        barrier = pltpu.get_barrier_semaphore()
        for peer in (core_peer, x_peer, y_peer, *chip_peers[1:]):
            pl.semaphore_signal(barrier, inc=1, device_id=peer, device_id_type=pl.DeviceIdType.MESH)
        pl.semaphore_wait(barrier, 6)

    def copies(source, target, sent, came, tile, places, kind, device):
        slot = lax.rem(tile, places)
        return pltpu.make_async_remote_copy(
            src_ref=source.at[lax.rem(tile, 2)],
            dst_ref=target.at[slot],
            send_sem=sent.at[kind, slot],
            recv_sem=came.at[kind, slot],
            device_id=device,
            device_id_type=pl.DeviceIdType.MESH,
        )

    def to_core(tile):
        return (
            copies(up_core, up_core_got, core_sent, core_came, tile, 2, 0, core_peer),
            copies(down_core, down_core_got, core_sent, core_came, tile, 2, 1, core_peer),
        )

    def to_seq(tile):
        return (
            copies(up_out, up_got, seq_sent, seq_came, tile, 3, 0, x_peer),
            copies(down_out, down_got, seq_sent, seq_came, tile, 3, 1, y_peer),
        )

    def to_last(tile):
        return (
            copies(up_last, up_last_got, last_sent, last_came, tile, 3, 0, y_peer),
            copies(down_last, down_last_got, last_sent, last_came, tile, 3, 1, x_peer),
        )

    def to_chips(slot):
        return [
            pltpu.make_async_remote_copy(
                src_ref=chip_out.at[slot, to_chip[k]],
                dst_ref=chip_got.at[slot, k - 1],
                send_sem=chip_sent.at[k - 1, slot],
                recv_sem=chip_came.at[k - 1, slot],
                device_id=chip_peers[k],
                device_id_type=pl.DeviceIdType.MESH,
            )
            for k in range(1, 4)
        ]

    @pl.when((step >= 1) & (step <= tiles))
    def _():
        slot = lax.rem(step + 1, 2)
        for copy in to_core(step - 1):
            copy.wait()
        for other in range(2):
            kept, gone = 2 * other + x, 2 * other + 1 - x
            up_half[slot, other] = up_mine[slot, kept] + up_core_got[slot, kept].astype(F32)
            up_out[slot, other] = (up_mine[slot, gone] + up_core_got[slot, gone].astype(F32)).astype(BF16)
            kept, gone = 2 * y + other, 2 * (1 - y) + other
            down_half[slot, other] = down_mine[slot, kept] + down_core_got[slot, kept].astype(F32)
            down_out[slot, other] = (down_mine[slot, gone] + down_core_got[slot, gone].astype(F32)).astype(BF16)
        for copy in to_seq(step - 1):
            copy.start()

    @pl.when(step >= 2)
    def _():
        slot = lax.rem(step, 2)
        place3 = lax.rem(step + 1, 3)
        for copy in to_seq(step - 2):
            copy.wait()
        up_quarter[slot] = up_half[slot, y] + up_got[place3, y].astype(F32)
        up_last[slot] = (up_half[slot, 1 - y] + up_got[place3, 1 - y].astype(F32)).astype(BF16)
        down_quarter[slot] = down_half[slot, x] + down_got[place3, x].astype(F32)
        down_last[slot] = (down_half[slot, 1 - x] + down_got[place3, 1 - x].astype(F32)).astype(BF16)
        @pl.when(step < tiles + 1)
        def _():
            for copy in to_last(step - 2):
                copy.start()

        @pl.when(step == tiles + 1)
        def _():
            left_up[...] = up_quarter[slot]
            left_up_low[...] = up_last[slot]
            left_down[...] = down_quarter[slot]
            left_down_low[...] = down_last[slot]


    @pl.when(step >= 4)
    def _():
        slot = lax.rem(step, 2)
        for copy in to_chips(slot):
            copy.wait()
        for kind, total in enumerate((up_total, down_total)):
            value = chip_full[slot, chip, kind]
            for k in range(3):
                value = value + chip_got[slot, k, kind].astype(F32)
            total[...] = value

    @pl.when(step >= 3)
    def _():
        slot = lax.rem(step + 1, 2)
        place3 = lax.rem(step, 3)
        for copy in to_last(step - 3):
            copy.wait()
        size = half // 4
        ups = up_quarter[slot] + up_last_got[place3].astype(F32)
        downs = down_quarter[slot] + down_last_got[place3].astype(F32)
        for place in range(4):
            up_block = ups[place * size : (place + 1) * size]
            down_block = downs[:, place * 128 : (place + 1) * 128]
            chip_full[slot, place, 0] = up_block
            chip_full[slot, place, 1] = down_block
            chip_out[slot, place, 0] = up_block.astype(BF16)
            chip_out[slot, place, 1] = down_block.astype(BF16)
        @pl.when(step < tiles + 1)
        def _():
            for copy in to_chips(slot):
                copy.start()

        @pl.when(step == tiles + 1)
        def _():
            left_full[...] = chip_full[slot]

    @pl.when(step < tiles)
    def _():
        slot = lax.rem(step, 2)
        up = jnp.concatenate([up0[...], up1[...], up2[...], up3[...]], axis=1)
        down = jnp.concatenate([down0[...], down1[...], down2[...], down3[...]], axis=0)
        hidden_part = bias.shape[0] // 4
        biases = jnp.concatenate(
            [
                bias_line[:, pl.ds(pl.multiple_of(owner * hidden_part + step * 128, 128), 128)]
                for owner in range(4)
            ],
            axis=1,
        )
        c0 = math.sqrt(2 / math.pi)
        c1 = c0 * 0.044715
        hidden = jnp.dot(normed[...], up, preferred_element_type=F32) + biases
        square = hidden * hidden
        gate = 0.5 + 0.5 * jnp.tanh(hidden * (c0 + c1 * square))
        raised = hidden * gate
        slope = gate + raised * (1.0 - gate) * (2 * c0 + 6 * c1 * square)
        active = raised.astype(BF16)
        down_part = jnp.dot(grad_turned[...], active, preferred_element_type=F32)
        for owner in range(4):
            size = half // 4
            down_mine[slot, owner] = down_part[owner * size : (owner + 1) * size]
            down_core[slot, owner] = down_part[half + owner * size : half + (owner + 1) * size].astype(BF16)
        to_core(step)[1].start()
        back = (((1,), (1,)), ((), ()))
        grad_active = lax.dot_general(grad_out[...], down, back, preferred_element_type=F32)
        grad_wide = (grad_active * slope).astype(BF16)
        up_part = jnp.dot(normed_turned[...], grad_wide, preferred_element_type=F32)
        for owner in range(4):
            columns = slice(owner * 128, (owner + 1) * 128)
            up_mine[slot, owner] = up_part[:half, columns]
            up_core[slot, owner] = up_part[half:, columns].astype(BF16)
        to_core(step)[0].start()
        sums = jnp.sum(grad_wide.astype(F32), axis=0, keepdims=True)
        for owner in range(4):
            bias_sum[owner] = sums[:, owner * 128 : (owner + 1) * 128]
        out_part = jnp.dot(active, down, preferred_element_type=F32)
        grad_part = lax.dot_general(grad_wide, up, back, preferred_element_type=F32)

        @pl.when(step == 0)
        def _():
            out_sum[...] = out_part
            grad_sum[...] = grad_part

        @pl.when(step > 0)
        def _():
            out_sum[...] += out_part
            grad_sum[...] += grad_part


def feed_forward_reduce(normed, grad_out, normed_turned, grad_turned, up, down, bias):
    count, width = normed.shape
    hidden = up.shape[1]
    part = hidden // 4
    tiles = part // 128
    half, quarter = width // 2, width // 8
    last = tiles - 1
    shape = jax.ShapeDtypeStruct
    fixed = lambda *dims: pl.BlockSpec(dims, lambda t: (0, 0), pipeline_mode=pl.Buffered(buffer_count=1))
    result = lambda *dims: pl.BlockSpec(dims, lambda t: (0, 0))
    done = lambda t: jnp.maximum(t - 4, 0)

    def up_block(owner):
        return pl.BlockSpec((width, 128), lambda t: (0, owner * tiles + jnp.minimum(t, last)))

    def down_block(owner):
        return pl.BlockSpec((128, width), lambda t: (owner * tiles + jnp.minimum(t, last), 0))

    bias_block = pl.BlockSpec((4, 1, 128), lambda t: (0, 0, jnp.minimum(t, last)))
    pair = lambda dtype, *dims: pltpu.VMEM((2,) + dims, dtype)
    triple = lambda dtype, *dims: pltpu.VMEM((3,) + dims, dtype)
    return pl.pallas_call(
        partial(mlp_reduce_kernel, tiles),
        grid=(tiles + STAGES,),
        in_specs=[fixed(count, width), fixed(count, width), fixed(width, count), fixed(width, count)]
        + [up_block(owner) for owner in range(4)]
        + [down_block(owner) for owner in range(4)]
        + [pl.BlockSpec((hidden,), lambda t: (0,))],
        out_specs=[
            result(count, width),
            result(count, width),
            bias_block,
            pl.BlockSpec((quarter, 128), lambda t: (0, done(t))),
            pl.BlockSpec((quarter, 128), lambda t: (0, done(t))),
            pl.BlockSpec((4, 2, quarter, 128), lambda t: (0, 0, 0, 0)),
            result(half, 128),
            result(half, 128),
            result(quarter, 512),
            result(quarter, 512),
        ],
        out_shape=[
            shape((count, width), F32),
            shape((count, width), F32),
            shape((4, 1, part), F32),
            shape((quarter, part - 256), F32),
            shape((quarter, part - 256), F32),
            shape((4, 2, quarter, 128), F32),
            shape((half, 128), F32),
            shape((half, 128), BF16),
            shape((quarter, 512), F32),
            shape((quarter, 512), BF16),
        ],
        scratch_shapes=[
            pair(F32, 4, half, 128),
            pair(F32, 4, quarter, 512),
            pair(BF16, 4, half, 128),
            pair(BF16, 4, quarter, 512),
            pair(BF16, 4, half, 128),
            pair(BF16, 4, quarter, 512),
            pair(F32, 2, half, 128),
            pair(F32, 2, quarter, 512),
            pair(BF16, 2, half, 128),
            pair(BF16, 2, quarter, 512),
            triple(BF16, 2, half, 128),
            triple(BF16, 2, quarter, 512),
            pair(F32, half, 128),
            pair(F32, quarter, 512),
            pair(BF16, half, 128),
            pair(BF16, quarter, 512),
            triple(BF16, half, 128),
            triple(BF16, quarter, 512),
            pair(F32, 4, 2, quarter, 128),
            pair(BF16, 4, 2, quarter, 128),
            pair(BF16, 3, 2, quarter, 128),
        ]
        + [pltpu.SemaphoreType.DMA((2, 2))] * 2
        + [pltpu.SemaphoreType.DMA((2, 3))] * 4
        + [pltpu.SemaphoreType.DMA((3, 2))] * 2
        + [pltpu.VMEM((1, hidden), F32)],
        compiler_params=pltpu.CompilerParams(collective_id=1, has_side_effects=True, vmem_limit_bytes=VMEM_LIMIT),
        cost_estimate=pl.CostEstimate(
            flops=12 * count * width * hidden,
            bytes_accessed=6 * width * hidden,
            transcendentals=count * hidden,
        ),
    )(normed, grad_out, normed_turned, grad_turned, up, up, up, up, down, down, down, down, bias)


def slot_column(slots):
    return lax.rem(lax.broadcasted_iota(jnp.int32, (3 * slots, 1), 0), slots)


def split_low(values):
    high = values.astype(BF16)
    rest = values - high.astype(F32)
    middle = rest.astype(BF16)
    return high, middle, (rest - middle.astype(F32)).astype(BF16)


def per_token(slot_col, seg_row, table):
    picked = (slot_col == seg_row).astype(BF16)
    return lax.dot_general(
        picked, jnp.concatenate(split_low(table), axis=0), (((0,), (0,)), ((), ())), preferred_element_type=F32
    )


def per_slot(slot_col, seg_row, values):
    slots = slot_col.shape[0] // 3
    picked = (slot_col[:slots] == seg_row).astype(BF16)
    return sum(jnp.dot(picked, part, preferred_element_type=F32) for part in split_low(values))


def normalize(values):
    center = values - jnp.mean(values, axis=-1, keepdims=True)
    inverse = lax.rsqrt(jnp.mean(center * center, axis=-1, keepdims=True) + norm_eps)
    return center * inverse, inverse


def normalize_back(normal, inverse, grad):
    return inverse * (grad - jnp.mean(grad, axis=-1, keepdims=True) - normal * jnp.mean(grad * normal, axis=-1, keepdims=True))


def after_kernel(
    seg,
    table,
    bias,
    attended,
    weight,
    out_sum,
    grad_sum,
    middle,
    branch,
    cotangent,
    left_full,
    left_up,
    left_up_low,
    left_down,
    left_down_low,
    block_out,
    grad_middle_ref,
    view_ref,
    slot_sums,
    bias_sum,
    proj_own,
    proj_low,
    up_tail,
    down_tail,
    attended_here,
    weight_here,
    rows_here,
    cotangent_here,
    block_here,
    middle_here,
    normal_here,
    grad_here,
    heads_out,
    total,
    core_out,
    core_got,
    load_sem,
    first_sem,
    store_sem,
    sent,
    came,
    kept,
    core_sent,
    core_came,
    full_here,
    up_here,
    up_low_here,
    down_here,
    down_low_here,
    up_got,
    down_got,
    chip_out,
    chip_got,
    left_sem,
    left_sent,
    left_came,
):
    rows, length, width = cotangent_here.shape
    depth, own = width // 8, width // 4
    seq, row = lax.axis_index("seq"), lax.axis_index("rows")
    core = lax.rem(row, 2)
    core_peer = {"rows": row + 1 - 2 * core}
    peers = peers_of(seq)
    slot_col = slot_column(table.shape[1])

    def go(copies):
        for copy in copies:
            copy.start()

    def end(copies):
        for copy in copies:
            copy.wait()

    def loads(r):
        lines = pl.ds(r * length, length)
        pairs = (
            (out_sum.at[lines], rows_here.at[r, 0]),
            (grad_sum.at[lines], rows_here.at[r, 1]),
            (middle.at[r], rows_here.at[r, 2]),
            (branch.at[r], rows_here.at[r, 3]),
            (cotangent.at[r], cotangent_here.at[r]),
        )
        return [pltpu.make_async_copy(source, target, load_sem.at[r, k]) for k, (source, target) in enumerate(pairs)]

    load_weight = pltpu.make_async_copy(weight, weight_here, first_sem.at[0])
    load_attended = pltpu.make_async_copy(attended, attended_here, first_sem.at[1])
    lefts = ((left_full, full_here.at[0]), (left_up_low, up_low_here), (left_down_low, down_low_here), (left_up, up_here), (left_down, down_here))
    load_left = [pltpu.make_async_copy(source, target, left_sem.at[k]) for k, (source, target) in enumerate(lefts)]
    go(load_left + loads(0) + [load_weight] + loads(1) + [load_attended])
    chip = lax.div(row, 2)
    to_chip = [lax.rem(chip + k, 4) for k in range(4)]
    chip_peers = [{"rows": 2 * to_chip[k] + core} for k in range(4)]

    def to_chips(tile):
        return [
            send_to(
                chip_out.at[tile, to_chip[k]],
                chip_got.at[tile, k - 1],
                left_sent.at[2 + 3 * tile + k - 1],
                left_came.at[2 + 3 * tile + k - 1],
                chip_peers[k],
            )
            for k in range(1, 4)
        ]

    left_copies = [
        send_to(up_low_here, up_got, left_sent.at[0], left_came.at[0], {"seq": peers[1]}),
        send_to(down_low_here, down_got, left_sent.at[1], left_came.at[1], {"seq": peers[0]}),
    ]

    greet([{"seq": peer} for peer in peers] + [core_peer] + chip_peers[1:])
    end(load_left)
    go(left_copies)
    chip_out[0] = full_here[0].astype(BF16)
    go(to_chips(0))

    def go_on():
        end(left_copies)
        ups = up_here[...] + up_got[...].astype(F32)
        downs = down_here[...] + down_got[...].astype(F32)
        for place in range(4):
            full_here[1, place, 0] = ups[place * depth : (place + 1) * depth]
            full_here[1, place, 1] = downs[:, place * 128 : (place + 1) * 128]
        chip_out[1] = full_here[1].astype(BF16)
        go(to_chips(1))

    def to_peer(r, m):
        lanes = pl.ds(m * length, length)
        return send_block(
            heads_out.at[r, peers[m - 1]], view_ref.at[r, :, lanes], sent, came, r * 3 + m - 1, {"seq": peers[m - 1]}
        )

    def to_self(r):
        return pltpu.make_async_copy(heads_out.at[r, seq], view_ref.at[r, :, pl.ds(0, length)], kept.at[r])

    def stores(r):
        return [
            pltpu.make_async_copy(middle_here.at[r], grad_middle_ref.at[r], store_sem.at[r, 0]),
            pltpu.make_async_copy(block_here.at[r], block_out.at[r], store_sem.at[r, 1]),
        ]

    def mods(r, first, count):
        seg_row = seg[r : r + 1, pl.ds(pl.multiple_of(seq * length, 128), length)]
        found = per_token(slot_col, seg_row, table[r, :, first * width : (first + count) * width])
        return [found[:, k * width : (k + 1) * width] for k in range(count)]

    for r in range(rows):
        (gate_a,), (scale_b,) = mods(r, 2, 1), mods(r, 4, 1)
        end(loads(r))
        normal, inverse = normalize(rows_here[r, 2])
        normal_here[r] = normal
        grad_normed = rows_here[r, 1]
        grad_middle = cotangent_here[r].astype(F32) + normalize_back(normal, inverse, grad_normed * (1.0 + scale_b))
        middle_here[r] = grad_middle
        stores(r)[0].start()
        grad_branch = (grad_middle * gate_a).astype(BF16)
        grad_here[r] = grad_branch
        if r == 0:
            load_weight.wait()
        grad_heads = lax.dot_general(weight_here[...], grad_branch, (((1,), (1,)), ((), ())), preferred_element_type=F32)
        for owner in range(4):
            heads_out[r, owner] = grad_heads[owner * own : (owner + 1) * own].astype(BF16)
        to_self(r).start()
        for m in range(1, 4):
            to_peer(r, m).start()
        if r == 0:
            go_on()

    load_attended.wait()
    for r in range(rows):
        part = jnp.dot(attended_here[r], grad_here[r], preferred_element_type=F32)
        sums = jnp.sum(grad_here[r].astype(F32), axis=0, keepdims=True)
        if r == 0:
            total[...] = part
            bias_sum[...] = sums
        else:
            total[...] += part
            bias_sum[...] += sums
    to_core = send_to(core_out, core_got, core_sent, core_came, core_peer)
    for place in range(4):
        other = pl.multiple_of((2 * place + 1 - core) * depth, 8)
        core_out[place] = total[pl.ds(other, depth), :].astype(BF16)
    to_core.start()

    bias_line = bias[...].astype(F32).reshape(1, width)
    for r in range(rows):
        (gate_b,) = mods(r, 5, 1)
        branch_b = rows_here[r, 0] + bias_line
        block_here[r] = (rows_here[r, 2] + gate_b * branch_b).astype(BF16)
        stores(r)[1].start()
        grad_normed = rows_here[r, 1]
        seg_row = seg[r : r + 1, pl.ds(pl.multiple_of(seq * length, 128), length)]
        pieces = (
            middle_here[r] * rows_here[r, 3],
            grad_normed,
            grad_normed * normal_here[r],
            cotangent_here[r].astype(F32) * branch_b,
        )
        for k, piece in enumerate(pieces):
            slot_sums[r, :, k * width : (k + 1) * width] = per_slot(slot_col, seg_row, piece)

    to_core.wait()
    for place in range(4):
        mine = pl.multiple_of((2 * place + core) * depth, 8)
        proj_low[place] = (total[pl.ds(mine, depth), :] + core_got[place].astype(F32)).astype(BF16)
    mine = pl.multiple_of(row * depth, 8)
    proj_own[...] = total[pl.ds(mine, depth), :] + core_got[chip].astype(F32)
    for tile in range(2):
        end(to_chips(tile))
        for kind, target in enumerate((up_tail, down_tail)):
            value = full_here[tile, chip, kind]
            for k in range(3):
                value = value + chip_got[tile, k, kind].astype(F32)
            target[:, tile * 128 : (tile + 1) * 128] = value
    for r in range(rows):
        end(stores(r))
        to_self(r).wait()
        for m in range(1, 4):
            to_peer(r, m).wait()


def after_feed_forward(seg, table, attended, weight, bias, out_sum, grad_sum, middle, branch, cotangent, left):
    rows, length, width = cotangent.shape
    slots = table.shape[1]
    depth = width // 8
    shape = jax.ShapeDtypeStruct
    vmem = lambda dtype, *dims: pltpu.VMEM(dims, dtype)
    near, far = pl.BlockSpec(memory_space=pltpu.VMEM), pl.BlockSpec(memory_space=pl.ANY)
    dma = lambda *dims: pltpu.SemaphoreType.DMA(dims)
    return pl.pallas_call(
        after_kernel,
        in_specs=[near] * 3 + [far] * 12,
        out_specs=[far] * 3 + [near] * 6,
        out_shape=[
            shape((rows, length, width), BF16),
            shape((rows, length, width), F32),
            shape((rows, width // 4, 4 * length), BF16),
            shape((rows, slots, 4 * width), F32),
            shape((1, width), F32),
            shape((depth, width), F32),
            shape((4, depth, width), BF16),
            shape((depth, 256), F32),
            shape((depth, 256), F32),
        ],
        scratch_shapes=[
            vmem(BF16, rows, width, length),
            vmem(BF16, width, width),
            vmem(F32, rows, 4, length, width),
            vmem(BF16, rows, length, width),
            vmem(BF16, rows, length, width),
            vmem(F32, rows, length, width),
            vmem(F32, rows, length, width),
            vmem(BF16, rows, length, width),
            vmem(BF16, rows, 4, width // 4, length),
            vmem(F32, width, width),
            vmem(BF16, 4, depth, width),
            vmem(BF16, 4, depth, width),
            dma(rows, 5),
            dma(2),
            dma(rows, 2),
            dma(3 * rows),
            dma(3 * rows),
            dma(rows),
            pltpu.SemaphoreType.DMA,
            pltpu.SemaphoreType.DMA,
            vmem(F32, 2, 4, 2, depth, 128),
            vmem(F32, 4 * depth, 128),
            vmem(BF16, 4 * depth, 128),
            vmem(F32, depth, 512),
            vmem(BF16, depth, 512),
            vmem(BF16, 4 * depth, 128),
            vmem(BF16, depth, 512),
            vmem(BF16, 2, 4, 2, depth, 128),
            vmem(BF16, 2, 3, 2, depth, 128),
            dma(5),
            dma(8),
            dma(8),
        ],
        compiler_params=pltpu.CompilerParams(vmem_limit_bytes=VMEM_LIMIT, collective_id=4, has_side_effects=True),
        cost_estimate=pl.CostEstimate(flops=8 * 10**9, bytes_accessed=3 * 10**7, transcendentals=0),
    )(seg, table, bias, attended, weight, out_sum, grad_sum, middle, branch, cotangent, *left)


def qkv_weight_kernel(grad, normed, keep_ref, send_ref, sum_ref, total, turned):
    step = pl.program_id(0)
    chips, depth = lax.axis_size("rows") // 2, total.shape[1] // lax.axis_size("rows")
    mine = lax.rem(lax.axis_index("rows"), 2)
    part = jnp.dot(grad[0], normed[0], preferred_element_type=F32)
    sums = jnp.sum(grad[0].astype(F32), axis=1, keepdims=True)

    @pl.when(step == 0)
    def _():
        total[...] = part
        sum_ref[...] = sums

    @pl.when(step > 0)
    def _():
        total[...] += part
        sum_ref[...] += sums

    @pl.when(step == pl.num_programs(0) - 1)
    def _():
        turned[...] = total[...].T
        for chip in range(chips):
            first = pl.multiple_of((2 * chip + mine) * depth, 8)
            other = pl.multiple_of((2 * chip + 1 - mine) * depth, 8)
            keep_ref[chip] = turned[pl.ds(first, depth), :]
            send_ref[chip] = turned[pl.ds(other, depth), :].astype(BF16)


def qkv_weight_grad(grad, normed):
    rows, features, length = grad.shape
    width = normed.shape[2]
    groups = lax.axis_size("rows")
    shape = (groups // 2, width // groups, features)
    return pl.pallas_call(
        qkv_weight_kernel,
        grid=(rows,),
        in_specs=[
            pl.BlockSpec((1, features, length), lambda r: (r, 0, 0)),
            pl.BlockSpec((1, length, width), lambda r: (r, 0, 0)),
        ],
        out_specs=[
            pl.BlockSpec(shape, lambda r: (0, 0, 0)),
            pl.BlockSpec(shape, lambda r: (0, 0, 0)),
            pl.BlockSpec((features, 1), lambda r: (0, 0)),
        ],
        out_shape=[
            jax.ShapeDtypeStruct(shape, F32),
            jax.ShapeDtypeStruct(shape, BF16),
            jax.ShapeDtypeStruct((features, 1), F32),
        ],
        scratch_shapes=[pltpu.VMEM((features, width), F32), pltpu.VMEM((width, features), F32)],
        compiler_params=pltpu.CompilerParams(vmem_limit_bytes=VMEM_LIMIT),
        cost_estimate=pl.CostEstimate(
            flops=2 * rows * length * width * features,
            bytes_accessed=2 * rows * length * (width + features) + 6 * width * features // 2,
            transcendentals=0,
        ),
    )(grad, normed)


def tail_kernel(
    images,
    mod,
    weight,
    cond,
    ada_ref,
    cond_ref,
    bias_ref,
    got,
    low_mine,
    low_got,
    row_mine,
    row_got,
    cond_mine,
    cond_got,
    column_got,
    sent,
    arrived,
):
    seq_count, row_total = lax.axis_size("seq"), lax.axis_size("rows")
    seq, row = lax.axis_index("seq"), lax.axis_index("rows")
    to_seq = [lax.rem(seq + m, seq_count) for m in range(seq_count)]
    to_row = [lax.rem(row + m, row_total) for m in range(row_total)]
    barrier = pltpu.get_barrier_semaphore()
    for m in range(1, seq_count):
        pl.semaphore_signal(barrier, inc=1, device_id={"seq": to_seq[m]}, device_id_type=pl.DeviceIdType.MESH)
    for m in range(1, row_total):
        pl.semaphore_signal(barrier, inc=1, device_id={"rows": to_row[m]}, device_id_type=pl.DeviceIdType.MESH)
    pl.semaphore_wait(barrier, seq_count + row_total - 2)

    used = [0]

    def start(source, target, device):
        copy = pltpu.make_async_remote_copy(
            src_ref=source,
            dst_ref=target,
            send_sem=sent.at[used[0]],
            recv_sem=arrived.at[used[0]],
            device_id=device,
            device_id_type=pl.DeviceIdType.MESH,
        )
        used[0] += 1
        copy.start()
        return copy

    copies = [start(mod.at[to_seq[m]], got.at[m], {"seq": to_seq[m]}) for m in range(1, seq_count)]
    column_got[0] = cond[row]
    column_copies = [start(cond.at[to_row[m]], column_got.at[m], {"rows": to_row[m]}) for m in range(1, row_total)]
    total = mod[seq]
    for m, copy in enumerate(copies):
        copy.wait()
        total = total + got[m + 1]
    low = total[:images].astype(BF16)
    low_mine[...] = low
    row_mine[...] = total[images:]
    row_mine[0:1] = jnp.sum(total[:images], axis=0, keepdims=True)
    low_got[0] = low
    copies = [start(low_mine, low_got.at[m], {"rows": to_row[m]}) for m in range(1, row_total)]
    copies += [start(row_mine, row_got.at[m], {"rows": to_row[m]}) for m in range(1, row_total)]
    term = lax.dot_general(low, weight[...], (((1,), (1,)), ((), ())), preferred_element_type=F32)
    cond_mine[...] = term
    cond_copies = [start(cond_mine, cond_got.at[m], {"seq": to_seq[m]}) for m in range(1, seq_count)]
    for copy in copies:
        copy.wait()
    sums = row_mine[...]
    for m in range(1, row_total):
        sums = sums + row_got[m]
    bias_ref[seq] = sums
    copies = [start(bias_ref.at[seq], bias_ref.at[seq], {"seq": to_seq[m]}) for m in range(1, seq_count)]
    for copy in column_copies:
        copy.wait()
    gathered = jnp.concatenate([low_got[m] for m in range(row_total)], axis=0)
    columns = jnp.concatenate([column_got[m] for m in range(row_total)], axis=0)
    ada_ref[...] = lax.dot_general(columns, gathered, (((0,), (0,)), ((), ())), preferred_element_type=F32)
    for m, copy in enumerate(cond_copies):
        copy.wait()
        term = term + cond_got[m + 1]
    cond_ref[...] = term
    for copy in copies:
        copy.wait()


def finish(mod, weight, cond, images):
    seq_count, lines, columns = mod.shape
    width, depth = weight.shape[0], cond.shape[2]
    row_total = lax.axis_size("rows")
    extra = lines - images
    copies = 3 * (seq_count - 1) + 3 * (row_total - 1)
    return pl.pallas_call(
        partial(tail_kernel, images),
        in_specs=[pl.BlockSpec(memory_space=pltpu.VMEM)] * 3,
        out_specs=[pl.BlockSpec(memory_space=pltpu.VMEM)] * 3,
        out_shape=[
            jax.ShapeDtypeStruct((depth, columns), F32),
            jax.ShapeDtypeStruct((images, width), F32),
            jax.ShapeDtypeStruct((seq_count, extra, columns), F32),
        ],
        scratch_shapes=[
            pltpu.VMEM((seq_count, lines, columns), F32),
            pltpu.VMEM((images, columns), BF16),
            pltpu.VMEM((row_total, images, columns), BF16),
            pltpu.VMEM((extra, columns), F32),
            pltpu.VMEM((row_total, extra, columns), F32),
            pltpu.VMEM((images, width), F32),
            pltpu.VMEM((seq_count, images, width), F32),
            pltpu.VMEM((row_total, images, depth), BF16),
            pltpu.SemaphoreType.DMA((copies,)),
            pltpu.SemaphoreType.DMA((copies,)),
        ],
        compiler_params=pltpu.CompilerParams(collective_id=0, has_side_effects=True, vmem_limit_bytes=VMEM_LIMIT),
        cost_estimate=pl.CostEstimate(flops=10**9, bytes_accessed=10**7, transcendentals=0),
    )(mod, weight, cond)


def send_to(source, target, sent, came, device):
    return pltpu.make_async_remote_copy(
        src_ref=source,
        dst_ref=target,
        send_sem=sent,
        recv_sem=came,
        device_id=device,
        device_id_type=pl.DeviceIdType.MESH,
    )


def back_kernel(
    block,
    inner,
    scale,
    code_col,
    code_row,
    query,
    key,
    value,
    out,
    grad_out,
    lse,
    normed,
    proj_own,
    proj_low,
    down,
    down_tail,
    seg,
    table,
    slot_sums,
    image_index,
    conditioning,
    proj_bias,
    up_bias,
    down_bias,
    tokens,
    grad_middle,
    weight,
    ada,
    grad_tokens,
    proj_ref,
    down_ref,
    ada_ref,
    cond_ref,
    ada_bias_ref,
    qv_bias_ref,
    proj_bias_ref,
    up_bias_ref,
    down_bias_ref,
    qkv_ref,
    grads,
    token_got,
    key_sum,
    value_sum,
    keys,
    values,
    total,
    spare,
    core_out,
    core_got,
    proj_got,
    seq_out,
    seq_got,
    down_out,
    down_got,
    qkv_own,
    chip_got,
    weights,
    tokens_here,
    middle_here,
    grad_here,
    features,
    image_sums,
    feature_sums,
    mod,
    got,
    lines,
    lines_got,
    low_all,
    small_core,
    small_chip,
    small_seq,
    cond_all,
    cond,
    column_got,
    piece_out,
    piece_got,
    sent,
    came,
    kept,
    load_sem,
    store_sem,
    other_sent,
    other_came,
    normed_here,
):
    length, size = query.shape[-1], query.shape[-2]
    row, head = pl.program_id(0), pl.program_id(1)
    rows, _, heads = grads.shape[:3]
    width = normed.shape[-1]
    images, columns = mod.shape[1:]
    depth, own, local = width // 8, width // 4, length // 4
    seq, group = lax.axis_index("seq"), lax.axis_index("rows")
    chip, core = lax.div(group, 2), lax.rem(group, 2)
    seq_places = peers_of(seq)
    peers = [{"seq": place} for place in seq_places]
    row_places = [lax.rem(group + m, 8) for m in range(8)]
    row_peers = [{"rows": place} for place in row_places]
    core_peer = {"rows": group + 1 - 2 * core}
    to_chip = [lax.rem(chip + k, 4) for k in range(4)]
    from_chip = [lax.rem(chip + 4 - k, 4) for k in range(4)]
    chip_peers = [{"rows": 2 * to_chip[k] + core} for k in range(4)]
    first = (row == 0) & (head == 0)
    last = (row == rows - 1) & (head == heads - 1)
    slot_col = slot_column(table.shape[1])
    used = [0]

    def copy_to(source, target, device):
        used[0] += 1
        return send_to(source, target, other_sent.at[used[0] - 1], other_came.at[used[0] - 1], device)

    def go(copies):
        for copy in copies:
            copy.start()

    def end(copies):
        for copy in copies:
            copy.wait()

    def to_peer(r, h, m):
        place = (r * heads + h) * 3 + m - 1
        source = grads.at[r, :, h, :, pl.ds(m * local, local)]
        return send_to(source, token_got.at[r, :, seq, h], sent.at[place], came.at[place], peers[m - 1])

    def to_self(r, h):
        source = grads.at[r, :, h, :, pl.ds(0, local)]
        return pltpu.make_async_copy(source, token_got.at[r, :, seq, h], kept.at[r * heads + h])

    proj_copies = [copy_to(proj_low.at[to_chip[k]], proj_got.at[k - 1], chip_peers[k]) for k in range(1, 4)]
    seq_copies = [copy_to(seq_out.at[place], seq_got.at[m], peers[m]) for m, place in enumerate(seq_places)]
    core_copy = copy_to(core_out, core_got, core_peer)
    down_copy = copy_to(down_out.at[1 - core], down_got, core_peer)
    chip_copies = [copy_to(core_out.at[to_chip[k]], chip_got.at[k - 1], chip_peers[k]) for k in range(1, 4)]
    column_copies = [copy_to(cond.at[row_places[m]], column_got.at[group], row_peers[m]) for m in range(1, 8)]
    mod_copies = [copy_to(mod.at[place], got.at[m], peers[m]) for m, place in enumerate(seq_places)]
    line_copies = [copy_to(lines.at[place], lines_got.at[m], peers[m]) for m, place in enumerate(seq_places)]
    low_core = copy_to(low_all.at[chip, core], low_all.at[chip, core], core_peer)
    low_chips = [copy_to(low_all.at[chip, core], low_all.at[chip, core], chip_peers[k]) for k in range(1, 4)]
    low_on = [copy_to(low_all.at[from_chip[k], core], low_all.at[from_chip[k], core], core_peer) for k in range(1, 4)]
    small_over = copy_to(small_core.at[core], small_core.at[core], core_peer)
    small_chips = [copy_to(small_chip.at[chip], small_chip.at[chip], chip_peers[k]) for k in range(1, 4)]
    small_copies = [copy_to(small_seq.at[seq], small_seq.at[seq], peers[m]) for m in range(3)]
    cond_copies = [copy_to(cond_all.at[seq], cond_all.at[seq], peers[m]) for m in range(3)]
    base = used[0]

    load_weights = [
        pltpu.make_async_copy(weight.at[:, pl.ds(part * width, width)], weights.at[part], load_sem.at[part])
        for part in range(3)
    ]
    load_normed = lambda r: pltpu.make_async_copy(normed.at[r], normed_here, load_sem.at[7])
    load_tokens = pltpu.make_async_copy(tokens, tokens_here, load_sem.at[3])
    load_middle = pltpu.make_async_copy(grad_middle, middle_here, load_sem.at[4])
    load_ada = [
        pltpu.make_async_copy(ada.at[pl.ds(0, width)], weights.at[0], load_sem.at[5]),
        pltpu.make_async_copy(ada.at[pl.ds(width, columns - width)], weights.at[1, pl.ds(0, columns - width)], load_sem.at[6]),
    ]

    @pl.when(first)
    def _():
        call(peers + row_peers[1:])
        go(load_weights + [load_tokens, load_middle, load_normed(0)])

    keys[...] = key[0, 0].astype(F32).T.astype(BF16)
    values[...] = value[0, 0].astype(F32).T.astype(BF16)

    def place_of(part):
        return pl.ds(pl.multiple_of((part * heads + head) * size, 8), size)

    for step in range(length // block):
        here = pl.ds(step * block, block)
        query_low = query[0, 0, :, here]
        grad_low = grad_out[0, 0, :, here]
        query_rows = query_low.astype(F32).T.astype(BF16)
        grad_rows = grad_low.astype(F32).T.astype(BF16)
        row_dot = jnp.sum(grad_low.astype(F32) * out[0, 0, :, here].astype(F32), axis=0, keepdims=True)
        grad_query = jnp.zeros((size, block), F32)
        for part in range(length // inner):
            there = pl.ds(part * inner, inner)
            scores = jnp.dot(keys[there, :], query_low, preferred_element_type=F32)
            scores = jnp.where(code_col[0, there, :] == code_row[0, :, here], scores * (scale * LOG2E), -1e30)
            probs = jnp.exp2(scores - lse[0, 0, :, here])
            grad_probs = jnp.dot(values[there, :], grad_low, preferred_element_type=F32)
            grad_raw = (probs * (grad_probs - row_dot) * scale).astype(BF16)
            value_part = jnp.dot(probs.astype(BF16), grad_rows, preferred_element_type=F32)
            key_part = jnp.dot(grad_raw, query_rows, preferred_element_type=F32)
            if step == 0:
                value_sum[there, :] = value_part
                key_sum[there, :] = key_part
            else:
                value_sum[there, :] += value_part
                key_sum[there, :] += key_part
            grad_query += jnp.dot(key[0, 0, :, there], grad_raw, preferred_element_type=F32)
        low = grad_query.astype(BF16)
        grads[row, 0, head, :, here] = low
        spare[place_of(0), here] = low.astype(F32)
    for part, sums in ((1, key_sum), (2, value_sum)):
        low = sums[...].T.astype(BF16)
        grads[row, part, head] = low
        spare[place_of(part), :] = low.astype(F32)

    @pl.when(first)
    def _():
        meet(peers + row_peers[1:])
        go(proj_copies)
        half = down_out.shape[2]
        down_out[0] = down[:, :half]
        down_out[1] = jnp.concatenate([down[:, half:], down_tail[...]], axis=1)
        down_copy.start()
        value = conditioning[...].astype(F32)
        low = (value / (1.0 + jnp.exp(-value))).astype(BF16)
        for place in range(8):
            cond[place] = low[:, place * depth : (place + 1) * depth]
        column_got[group] = cond[group]
        go(column_copies)
        image_sums[...] = jnp.zeros_like(image_sums)
        feature_sums[...] = jnp.zeros_like(feature_sums)

    to_self(row, head).start()
    for m in range(1, 4):
        to_peer(row, head, m).start()

    own_features = 3 * own

    @pl.when((head == heads - 1) & (row == 0))
    def _():
        load_normed(0).wait()
        total[...] = jnp.dot(spare[:own_features].astype(BF16), normed_here[...], preferred_element_type=F32)
        load_normed(1).start()

    @pl.when((head == heads - 1) & (row > 0))
    def _():
        load_normed(1).wait()
        total[...] += jnp.dot(spare[:own_features].astype(BF16), normed_here[...], preferred_element_type=F32)

    def store_tokens(r):
        return pltpu.make_async_copy(grad_here.at[r], grad_tokens.at[r], store_sem.at[r])

    def input_grad(r):
        for h in range(heads):
            to_self(r, h).wait()
            for m in range(1, 4):
                to_peer(r, h, m).wait()
        grad_normed = jnp.zeros((width, local), F32)
        for part in range(3):
            for place in range(4):
                for h in range(heads):
                    start = (place * heads + h) * size
                    features[start : start + size] = token_got[r, part, place, h].astype(F32)
            low = features[...].astype(BF16)
            grad_normed += jnp.dot(weights[part], low, preferred_element_type=F32)
            if part != 1:
                lanes = slice(part * width, (part + 1) * width)
                ones = jnp.ones((8, local), BF16)
                feature_sums[:, lanes] += lax.dot_general(ones, low, (((1,), (1,)), ((), ())), preferred_element_type=F32)
        grad_normed = grad_normed.T
        normal, inverse = normalize(tokens_here[r].astype(F32))
        seg_row = seg[r : r + 1, pl.ds(pl.multiple_of(seq * local, 128), local)]
        scale_a = per_token(slot_col, seg_row, table[r, :, width : 2 * width])
        grad_here[r] = middle_here[r] + normalize_back(normal, inverse, grad_normed * (1.0 + scale_a))
        store_tokens(r).start()
        late = [per_slot(slot_col, seg_row, piece) for piece in (grad_normed, grad_normed * normal)]
        slots = jnp.concatenate(late + [slot_sums[r]], axis=1)
        pick = lax.broadcasted_iota(jnp.int32, (images, slots.shape[0]), 0) == image_index[r : r + 1, :]
        picks = jnp.concatenate([pick.astype(BF16)] * 3, axis=1)
        image_sums[...] += jnp.dot(picks, jnp.concatenate(split_low(slots), axis=0), preferred_element_type=F32)

    @pl.when(last)
    def _():
        spare[:, :own_features] = total[...].T
        for place in range(4):
            other = pl.multiple_of((2 * place + 1 - core) * depth, 8)
            core_out[place] = spare[pl.ds(other, depth), :own_features].astype(BF16)
        core_copy.start()
        end(proj_copies)
        mine = proj_own[...]
        for k in range(3):
            mine = mine + proj_got[k].astype(F32)
        for place in range(4):
            seq_out[place] = mine[:, place * own : (place + 1) * own].astype(BF16)
        go(seq_copies)
        for place in range(4):

            @pl.when(seq == place)
            def _():
                proj_ref[...] = mine[:, place * own : (place + 1) * own]

        down_copy.wait()
        left, right = down_out[core], down_got[...]
        left, right = jnp.where(core == 0, left, right), jnp.where(core == 0, right, left)
        down_ref[:depth] = left
        down_ref[depth:] = right
        core_copy.wait()
        for place in range(4):
            same = pl.multiple_of((2 * place + core) * depth, 8)
            core_out[place] = (spare[pl.ds(same, depth), :own_features] + core_got[place].astype(F32)).astype(BF16)
        same = pl.multiple_of(group * depth, 8)
        qkv_own[...] = spare[pl.ds(same, depth), :own_features] + core_got[chip].astype(F32)
        go(chip_copies)

        end(load_weights + [load_tokens, load_middle])
        for r in range(rows):
            input_grad(r)
        go(load_ada)

        for place in range(4):
            mod[place] = image_sums[:, place * columns : (place + 1) * columns]
        for line in range(8):
            if line < 2:
                value = feature_sums[0:1, 2 * line * width : (2 * line + 1) * width]
            else:
                value = (proj_bias[...], *(up_bias[k] for k in range(4)), down_bias[...])[line - 2]
            lines[line // 2, line % 2 : line % 2 + 1] = value
        go(mod_copies + line_copies)
        for m, copy in enumerate(seq_copies):
            copy.wait()
            proj_ref[...] += seq_got[m].astype(F32)
        sums = mod[seq]
        for m, copy in enumerate(mod_copies):
            copy.wait()
            sums = sums + got[m]
        low = sums.astype(BF16)
        low_all[chip, core] = low
        go([low_core] + low_chips)
        small = lines[seq]
        for m, copy in enumerate(line_copies):
            copy.wait()
            small = small + lines_got[m]
        small_core[core] = jnp.zeros_like(small_core[core])
        small_core[core, 0:2, :width] = small
        small_core[core, 2:3] = jnp.sum(sums, axis=0, keepdims=True)
        small_over.start()
        end(load_ada)
        term = jnp.dot(low[:, :width], weights[0], preferred_element_type=F32)
        term += jnp.dot(low[:, width:], weights[1, : columns - width], preferred_element_type=F32)
        cond_all[seq] = term
        go(cond_copies)
        end(chip_copies + column_copies)
        mine = qkv_own[...]
        for k in range(3):
            mine = mine + chip_got[k].astype(F32)
        for part in range(3):
            piece_out[part] = mine[:, part * own : (part + 1) * own]

        def piece(part):
            index = part * 4 + seq
            target, place = lax.div(index, 3), lax.rem(index, 3)
            copy = send_to(
                piece_out.at[part], piece_got.at[place], other_sent.at[base + part], other_came.at[base + place], {"seq": target}
            )
            return copy, target, place

        def arriving(place):
            source = lax.rem(3 * seq + place, 4)
            copy = send_to(
                piece_out.at[0], piece_got.at[place], other_sent.at[base], other_came.at[base + place], {"seq": source}
            )
            return copy, source

        for part in range(3):
            copy, target, place = piece(part)

            @pl.when(target != seq)
            def _():
                copy.start()

            @pl.when(target == seq)
            def _():
                piece_got[place] = piece_out[part]

        small_over.wait()
        small_chip[chip] = small_core[0] + small_core[1]
        go(small_chips)
        for came_in, going_on in zip(low_chips, low_on):
            came_in.wait()
            going_on.start()
        end(small_chips)
        small_seq[seq] = (small_chip[0] + small_chip[1]) + (small_chip[2] + small_chip[3])
        go(small_copies)
        end([low_core] + low_on)
        gathered = jnp.concatenate([low_all[m // 2, m % 2] for m in range(8)], axis=0)
        blocks = jnp.concatenate([column_got[m] for m in range(8)], axis=0)
        ada_ref[...] = lax.dot_general(blocks, gathered, (((0,), (0,)), ((), ())), preferred_element_type=F32)
        for part in range(3):
            copy, target, place = piece(part)

            @pl.when(target != seq)
            def _():
                copy.wait_send()

        for place in range(3):
            copy, source = arriving(place)

            @pl.when(source != seq)
            def _():
                copy.wait_recv()

        for place in range(3):
            qkv_ref[:, place * own : (place + 1) * own] = piece_got[place]
        end(cond_copies)
        value = conditioning[...].astype(F32)
        gate = 1.0 / (1.0 + jnp.exp(-value))
        sums = (cond_all[0] + cond_all[1]) + (cond_all[2] + cond_all[3])
        cond_ref[...] = sums * gate * (1.0 + value * (1.0 - gate))
        end(small_copies)
        for place in range(4):
            ada_bias_ref[pl.ds(place * columns, columns)] = small_seq[place, 2]
        qv_bias_ref[...] = small_seq[0, 0:2, :width]
        proj_bias_ref[...] = small_seq[1, 0, :width]
        for line in range(3, 7):
            up_bias_ref[pl.ds((line - 3) * width, width)] = small_seq[line // 2, line % 2, :width]
        down_bias_ref[...] = small_seq[3, 1, :width]
        for r in range(rows):
            store_tokens(r).wait()


def attend_back_and_finish(packed, out, grad_out, lse, col, row, normed, *rest):
    proj_own, proj_low, down, down_tail, seg, table, slot_sums, image_index, conditioning, biases, tokens, grad_middle, weight, ada = rest
    rows, _, heads, size, length = packed.shape
    width = normed.shape[2]
    depth, own, features, local = width // 8, width // 4, 3 * heads * size, length // 4
    half = (down.shape[1] + down_tail.shape[1]) // 2
    images, columns = conditioning.shape[0], ada.shape[0]
    part = lambda j: pl.BlockSpec((1, None, 1, size, length), lambda r, h: (r, j, h, 0, 0))
    whole = pl.BlockSpec((1, 1, size, length), lambda r, h: (r, h, 0, 0))
    single = pl.Buffered(buffer_count=1)
    fixed = lambda *dims: pl.BlockSpec(dims, lambda r, h: (0,) * len(dims), pipeline_mode=single)
    result = lambda *dims: pl.BlockSpec(dims, lambda r, h: (0,) * len(dims))
    far = pl.BlockSpec(memory_space=pl.ANY)
    shape = jax.ShapeDtypeStruct
    vmem = lambda dtype, *dims: pltpu.VMEM(dims, dtype)
    count = rows * heads
    copies = 3 + 3 + 1 + 1 + 3 + 7 + 3 + 3 + 1 + 3 + 3 + 1 + 3 + 3 + 3 + 3
    dma = lambda n: pltpu.SemaphoreType.DMA((n,))
    return pl.pallas_call(
        partial(back_kernel, 256, 512, size**-0.5),
        grid=(rows, heads),
        in_specs=[
            pl.BlockSpec((1, length, 1), lambda r, h: (r, 0, 0)),
            pl.BlockSpec((1, 1, length), lambda r, h: (r, 0, 0)),
            part(0),
            part(1),
            part(2),
            whole,
            whole,
            pl.BlockSpec((1, 1, 1, length), lambda r, h: (r, h, 0, 0)),
            far,
            fixed(depth, width),
            fixed(4, depth, width),
            fixed(*down.shape),
            fixed(*down_tail.shape),
            fixed(*seg.shape),
            fixed(*table.shape),
            fixed(*slot_sums.shape),
            fixed(*image_index.shape),
            fixed(images, width),
            fixed(1, width),
            fixed(4, 1, width),
            fixed(1, width),
            far,
            far,
            far,
            far,
        ],
        out_specs=[
            far,
            result(depth, own),
            result(own, half),
            result(depth, columns),
            result(images, width),
            result(4 * columns),
            result(2, width),
            result(width),
            result(4 * width),
            result(width),
            result(depth, features),
        ],
        out_shape=[
            shape((rows, local, width), F32),
            shape((depth, own), F32),
            shape((own, half), F32),
            shape((depth, columns), F32),
            shape((images, width), F32),
            shape((4 * columns,), F32),
            shape((2, width), F32),
            shape((width,), F32),
            shape((4 * width,), F32),
            shape((width,), F32),
            shape((depth, features), F32),
        ],
        scratch_shapes=[
            vmem(BF16, rows, 3, heads, size, length),
            vmem(BF16, rows, 3, 4, heads, size, local),
            vmem(F32, length, size),
            vmem(F32, length, size),
            vmem(BF16, length, size),
            vmem(BF16, length, size),
            vmem(F32, features, width),
            vmem(F32, width, length),
            vmem(BF16, 4, depth, features),
            vmem(BF16, 4, depth, features),
            vmem(BF16, 3, depth, width),
            vmem(BF16, 4, depth, own),
            vmem(BF16, 3, depth, own),
            vmem(F32, 2, depth, half),
            vmem(F32, depth, half),
            vmem(F32, depth, features),
            vmem(BF16, 3, depth, features),
            vmem(BF16, 3, width, width),
            vmem(BF16, rows, local, width),
            vmem(F32, rows, local, width),
            vmem(F32, rows, local, width),
            vmem(F32, width, local),
            vmem(F32, images, 6 * width),
            vmem(F32, 8, 3 * width),
            vmem(F32, 4, images, columns),
            vmem(F32, 3, images, columns),
            vmem(F32, 4, 2, width),
            vmem(F32, 3, 2, width),
            vmem(BF16, 4, 2, images, columns),
            vmem(F32, 2, 4, columns),
            vmem(F32, 4, 4, columns),
            vmem(F32, 4, 4, columns),
            vmem(F32, 4, images, width),
            vmem(BF16, 8, images, depth),
            vmem(BF16, 8, images, depth),
            vmem(F32, 3, depth, own),
            vmem(F32, 3, depth, own),
            dma(3 * count),
            dma(3 * count),
            dma(count),
            dma(8),
            dma(rows),
            dma(copies),
            dma(copies),
            vmem(BF16, length, width),
        ],
        compiler_params=pltpu.CompilerParams(vmem_limit_bytes=VMEM_LIMIT, collective_id=3, has_side_effects=True),
        cost_estimate=pl.CostEstimate(
            flops=20 * rows * heads * length * length * 128,
            bytes_accessed=16 * rows * heads * length * size,
            transcendentals=rows * heads * length * length,
        ),
    )(
        col,
        row,
        packed,
        packed,
        packed,
        out,
        grad_out,
        lse,
        normed,
        proj_own,
        proj_low,
        down,
        down_tail,
        seg,
        table,
        slot_sums,
        image_index,
        conditioning,
        *biases,
        tokens,
        grad_middle,
        weight,
        ada,
    )


def forward_kernel(
    block,
    image_index,
    seg,
    fill,
    conditioning,
    ada_bias,
    qv_bias,
    proj_bias,
    tokens,
    ada,
    weight,
    proj,
    cotangent,
    normed_ref,
    packed_ref,
    attended_ref,
    features_ref,
    branch_ref,
    middle_ref,
    inner_ref,
    grad_ref,
    inner_turned_ref,
    grad_turned_ref,
    table_ref,
    code_row,
    code_col,
    lse_ref,
    bias_sum,
    here,
    normed_all,
    packed_all,
    ada_here,
    windows,
    turned,
    own_weight,
    bias_turned,
    mod_all,
    table,
    seg_all,
    attended_all,
    attended_got,
    flat,
    features_all,
    proj_here,
    cotangent_here,
    branch_all,
    middle_all,
    inner_all,
    grad_all,
    inner_turned,
    grad_turned,
    rows_turned,
    load_sem,
    own_sem,
    mod_sent,
    mod_came,
    sent,
    came,
    forward_sent,
    forward_came,
    heads_sent,
    heads_came,
    heads_kept,
    store_sem,
    last_sem,
):
    rows, _, local, width = here.shape
    _, parts, heads, size, length = packed_all.shape
    own, depth, half = heads * size, width // 8, local // 2
    columns = ada_here.shape[0]
    images, slots = conditioning.shape[0], image_index.shape[1]
    slot_col = slot_column(slots)
    scale = size**-0.5 * LOG2E
    seq = lax.axis_index("seq")
    core = lax.rem(lax.axis_index("rows"), 2)
    places = [seq] + peers_of(seq)
    peers = [{"seq": place} for place in places]


    def direct(r, m):
        index = r * 2 + m - 1
        return send_to(tokens.at[r], here.at[r, m], sent.at[index], came.at[index], peers[m])

    def forward(r, m):
        part = pl.ds(0, half) if m == 1 else pl.ds(half, half)
        index = r * 2 + m - 1
        return send_to(
            here.at[r, 3 - m, part], here.at[r, 3, part], forward_sent.at[index], forward_came.at[index], peers[m]
        )

    def go(copies):
        for copy in copies:
            copy.start()

    def end(copies):
        for copy in copies:
            copy.wait()

    own_copies = [pltpu.make_async_copy(tokens.at[r], here.at[r, 0], own_sem.at[r]) for r in range(rows)]
    load_ada = pltpu.make_async_copy(ada, ada_here, load_sem.at[0])
    load_windows = []
    for part in range(3):
        lanes = pl.ds(pl.multiple_of(part * width + seq * 256, 128), 384)
        load_windows.append(pltpu.make_async_copy(weight.at[:, lanes], windows.at[part], load_sem.at[1 + part]))
    load_proj = pltpu.make_async_copy(proj, proj_here, load_sem.at[4])
    load_cotangent = pltpu.make_async_copy(cotangent, cotangent_here, load_sem.at[5])
    go([load_ada] + load_windows + own_copies + [load_proj, load_cotangent])
    greet(peers[1:])
    go([direct(0, m) for m in (1, 2)])

    value = conditioning[...].astype(F32)
    low = (value / (1.0 + jnp.exp(-value))).astype(BF16)
    load_ada.wait()
    mod_all[seq] = lax.dot_general(low, ada_here[...], (((1,), (1,)), ((), ())), preferred_element_type=F32)
    mod_copies = [
        send_to(mod_all.at[seq], mod_all.at[seq], mod_sent.at[m - 1], mod_came.at[m - 1], peers[m]) for m in range(1, 4)
    ]
    go(mod_copies)

    for m in range(4):
        lanes = pl.ds(pl.multiple_of(places[m] * local, 128), local)
        found = seg[:, lanes]
        where = places[m] * local + lax.broadcasted_iota(jnp.int32, (1, local), 1)
        for r in range(rows):
            code = jnp.where(where < fill[r], found[r : r + 1], -1 - where)
            seg_all[r, m] = found[r : r + 1]
            code_row[r, :, m * local : (m + 1) * local] = code
            column = jnp.broadcast_to(code.astype(F32), (128, local)).T[:, :1]
            code_col[r, m * local : (m + 1) * local] = column.astype(jnp.int32)

    for part in range(3):
        load_windows[part].wait()
        turned[...] = windows[part].astype(F32).T
        own_weight[part * own : (part + 1) * own] = turned[pl.ds(pl.multiple_of(seq * 32, 8), own), :].astype(BF16)
    window = qv_bias[:, pl.ds(pl.multiple_of(seq * 256, 128), 384)].astype(F32)
    bias_turned[...] = jnp.concatenate([window, jnp.zeros((6, 384), F32)], axis=0).T
    bias = bias_turned[pl.ds(pl.multiple_of(seq * 32, 8), own), :]
    bias = jnp.concatenate([bias[:, 0:1], jnp.zeros((own, 1), F32), bias[:, 1:2]], axis=0)

    end([direct(0, m) for m in (1, 2)])
    go([forward(0, m) for m in (1, 2)] + [direct(1, m) for m in (1, 2)])

    end(mod_copies)
    bias_all = ada_bias[...].astype(F32).reshape(1, 4 * columns)
    proj_line = proj_bias[...].astype(F32).reshape(1, width)
    for place in range(4):
        lanes = slice(place * columns, (place + 1) * columns)
        table[:, lanes] = mod_all[place] + bias_all[:, lanes]
    stacked = jnp.concatenate(split_low(table[...]), axis=0)
    image_col = lax.rem(lax.broadcasted_iota(jnp.int32, (3 * images, slots), 0), images)
    for r in range(rows):
        picked = (image_col == image_index[r : r + 1]).astype(BF16)
        table_ref[r] = lax.dot_general(picked, stacked, (((0,), (0,)), ((), ())), preferred_element_type=F32)

    def stores(r, m):
        index = r * 4 + m
        lanes = pl.ds(m * local, local)
        return (
            pltpu.make_async_copy(normed_all.at[r, m], normed_ref.at[r, m], store_sem.at[0, index]),
            pltpu.make_async_copy(packed_all.at[r, :, :, :, lanes], packed_ref.at[r, :, :, :, lanes], store_sem.at[1, index]),
        )

    def work(r, m):
        mods = per_token(slot_col, seg_all[r, m], table_ref[r, :, : 2 * width])
        normal, _ = normalize(here[r, m].astype(F32))
        normed = (normal * (1.0 + mods[:, width:]) + mods[:, :width]).astype(BF16)
        normed_all[r, m] = normed
        mixed = lax.dot_general(own_weight[...], normed, (((1,), (1,)), ((), ())), preferred_element_type=F32)
        mixed = (mixed + bias).astype(BF16)
        for part in range(parts):
            for head in range(heads):
                start = (part * heads + head) * size
                packed_all[r, part, head, :, m * local : (m + 1) * local] = mixed[start : start + size]
        go(stores(r, m))

    def to_peer(r, h, m):
        source = attended_all.at[r, h, :, pl.ds(m * local, local)]
        place = (r * heads + h) * 3 + m - 1
        return send_to(source, attended_got.at[r, seq, h], heads_sent.at[place], heads_came.at[place], peers[m])

    def to_self(r, h):
        source = attended_all.at[r, h, :, pl.ds(0, local)]
        return pltpu.make_async_copy(source, attended_got.at[r, seq, h], heads_kept.at[r * heads + h])

    def attend_head(r, h):
        keys = packed_all[r, 1, h].astype(F32).T.astype(BF16)
        values = packed_all[r, 2, h]
        codes = code_col[r]
        for step in range(length // block):
            lanes = pl.ds(step * block, block)
            scores = jnp.dot(keys, packed_all[r, 0, h, :, lanes], preferred_element_type=F32)
            scores = jnp.where(codes == code_row[r, :, lanes], scores * scale, -1e30)
            peak = jnp.max(scores, axis=0, keepdims=True)
            raised = jnp.exp2(scores - peak)
            total = jnp.sum(raised, axis=0, keepdims=True)
            probs = (raised * (1.0 / total)).astype(BF16)
            attended_all[r, h, :, lanes] = jnp.dot(values, probs, preferred_element_type=F32).astype(BF16)
            lse_ref[r, h, :, lanes] = peak + jnp.log2(total)

    def send_head(r, h):
        to_self(r, h).start()
        for m in range(1, 4):
            to_peer(r, h, m).start()

    def attend_row(r, first, last):
        @pl.loop(first, last)
        def _(h):
            attend_head(r, h)
            if r > 0:
                send_head(r, h)

    def last_stores(r):
        lines, lanes = pl.ds(r * local, local), pl.ds(r * local, local)
        pairs = (
            (grad_all.at[r], grad_ref.at[lines]),
            (grad_turned.at[r], grad_turned_ref.at[:, lanes]),
            (attended_all.at[r], attended_ref.at[r]),
            (features_all.at[r], features_ref.at[r]),
            (branch_all.at[r], branch_ref.at[r]),
            (middle_all.at[r], middle_ref.at[r]),
            (inner_all.at[r], inner_ref.at[lines]),
            (inner_turned.at[r], inner_turned_ref.at[:, lanes]),
        )
        return [pltpu.make_async_copy(source, target, last_sem.at[r, k]) for k, (source, target) in enumerate(pairs)]

    def turn(values, target, r):
        rows_turned[...] = values.T
        for place in range(4):
            for order in range(2):
                first = pl.multiple_of((2 * place + (core if order == 0 else 1 - core)) * depth, 8)
                start = (4 * order + place) * depth
                target[r, start : start + depth] = rows_turned[pl.ds(first, depth), :].astype(BF16)

    end(own_copies)
    for m in range(3):
        work(0, m)
    end([load_proj, load_cotangent])
    for r in range(rows):
        gate_b = per_token(slot_col, seg_all[r, 0], table_ref[r, :, 5 * width :])
        grad = cotangent_here[r].astype(F32) * gate_b
        grad_all[r] = grad.astype(BF16)
        turn(grad, grad_turned, r)
        sums = jnp.sum(grad.astype(BF16).astype(F32), axis=0, keepdims=True)
        if r == 0:
            bias_sum[...] = sums
        else:
            bias_sum[...] += sums
        go(last_stores(r)[:2])
    def project(r):
        for h in range(heads):
            to_self(r, h).wait()
            for m in range(1, 4):
                to_peer(r, h, m).wait()
        for place in range(4):
            for h in range(heads):
                start = (place * heads + h) * size
                flat[start : start + size] = attended_got[r, place, h].astype(F32)
        features = flat[...].astype(BF16)
        features_all[r] = features
        go(last_stores(r)[2:4])
        mods = per_token(slot_col, seg_all[r, 0], table_ref[r, :, 2 * width : 5 * width])
        gate_a, shift_b, scale_b = (mods[:, k * width : (k + 1) * width] for k in range(3))
        branch = lax.dot_general(features, proj_here[...], (((0,), (0,)), ((), ())), preferred_element_type=F32) + proj_line
        middle = here[r, 0].astype(F32) + gate_a * branch
        branch_all[r] = branch
        middle_all[r] = middle
        go(last_stores(r)[4:6])
        normed = normalize(middle)[0] * (1.0 + scale_b) + shift_b
        inner_all[r] = normed.astype(BF16)
        turn(normed, inner_turned, r)
        go(last_stores(r)[6:])
    end([forward(0, m) for m in (1, 2)])
    work(0, 3)
    attend_row(0, 0, heads // 2)
    end([direct(1, m) for m in (1, 2)])
    go([forward(1, m) for m in (1, 2)])
    attend_row(0, heads // 2, heads)
    for m in range(3):
        work(1, m)
    end([forward(1, m) for m in (1, 2)])
    for h in range(heads):
        send_head(0, h)
    work(1, 3)
    attend_row(1, 0, heads)
    project(0)
    project(1)
    for r in range(rows):
        for m in range(4):
            end(stores(r, m))
        end(last_stores(r))


def before_feed_forward(image_index, seg, fill, conditioning, ada_bias, qv_bias, proj_bias, tokens, ada, weight, proj, cotangent):
    rows, local, width = tokens.shape
    length = 4 * local
    images, slots = conditioning.shape[0], image_index.shape[1]
    heads, size = HEADS // 4, width // HEADS
    columns = ada.shape[0]
    shape = jax.ShapeDtypeStruct
    vmem = lambda dtype, *dims: pltpu.VMEM(dims, dtype)
    near, far = pl.BlockSpec(memory_space=pltpu.VMEM), pl.BlockSpec(memory_space=pl.ANY)
    dma = lambda *dims: pltpu.SemaphoreType.DMA(dims)
    return pl.pallas_call(
        partial(forward_kernel, 512),
        in_specs=[near] * 2 + [pl.BlockSpec(memory_space=pltpu.SMEM)] + [near] * 4 + [far] * 5,
        out_specs=[far] * 10 + [near] * 5,
        out_shape=[
            shape((rows, 4, local, width), BF16),
            shape((rows, 3, heads, size, length), BF16),
            shape((rows, heads, size, length), BF16),
            shape((rows, width, local), BF16),
            shape((rows, local, width), F32),
            shape((rows, local, width), F32),
            shape((rows * local, width), BF16),
            shape((rows * local, width), BF16),
            shape((width, rows * local), BF16),
            shape((width, rows * local), BF16),
            shape((rows, slots, 6 * width), F32),
            shape((rows, 1, length), jnp.int32),
            shape((rows, length, 1), jnp.int32),
            shape((rows, heads, 1, length), F32),
            shape((1, width), F32),
        ],
        scratch_shapes=[
            vmem(BF16, rows, 4, local, width),
            vmem(BF16, rows, 4, local, width),
            vmem(BF16, rows, 3, heads, size, length),
            vmem(BF16, columns, width),
            vmem(BF16, 3, width, 384),
            vmem(F32, 384, width),
            vmem(BF16, 3 * heads * size, width),
            vmem(F32, 384, 8),
            vmem(F32, 4, images, columns),
            vmem(F32, images, 6 * width),
            vmem(jnp.int32, rows, 4, 1, local),
            vmem(BF16, rows, heads, size, length),
            vmem(BF16, rows, 4, heads, size, local),
            vmem(F32, width, local),
            vmem(BF16, rows, width, local),
            vmem(BF16, width, width),
            vmem(BF16, rows, local, width),
            vmem(F32, rows, local, width),
            vmem(F32, rows, local, width),
            vmem(BF16, rows, local, width),
            vmem(BF16, rows, local, width),
            vmem(BF16, rows, width, local),
            vmem(BF16, rows, width, local),
            vmem(F32, width, local),
            dma(6),
            dma(rows),
            dma(3),
            dma(3),
            dma(2 * rows),
            dma(2 * rows),
            dma(2 * rows),
            dma(2 * rows),
            dma(3 * rows * heads),
            dma(3 * rows * heads),
            dma(rows * heads),
            dma(2, 4 * rows),
            dma(rows, 8),
        ],
        compiler_params=pltpu.CompilerParams(vmem_limit_bytes=VMEM_LIMIT, collective_id=6, has_side_effects=True),
        cost_estimate=pl.CostEstimate(flops=2 * 10**10, bytes_accessed=4 * 10**7, transcendentals=0),
    )(image_index, seg, fill, conditioning, ada_bias, qv_bias, proj_bias, tokens, ada, weight, proj, cotangent)


def hand_out_kernel(places, *refs):
    count = len(places)
    sources, targets = refs[:count], refs[count:]
    held, sems = refs[-count - 1 : -1], refs[-1]
    loads = [pltpu.make_async_copy(sources[k], held[k], sems.at[0, k]) for k in range(count)]
    stores = []
    for k, (index, first, size) in enumerate(places):
        target = targets[index] if size is None else targets[index].at[:, pl.ds(first, size)]
        stores.append(pltpu.make_async_copy(held[k], target, sems.at[1, k]))
    for copy in loads:
        copy.start()
    for load, store in zip(loads, stores):
        load.wait()
        store.start()
    for copy in stores:
        copy.wait()


def hand_out(*results):
    arrays, places, shapes = [], [], []
    for index, result in enumerate(results):
        first = 0
        pieces = result if isinstance(result, tuple) else (result,)
        for piece in pieces:
            size = piece.shape[1] if len(pieces) > 1 else None
            arrays.append(piece)
            places.append((index, first, size))
            first += size or 0
        shape = pieces[0].shape if len(pieces) == 1 else (pieces[0].shape[0], first)
        shapes.append(jax.ShapeDtypeStruct(shape, pieces[0].dtype))
    far = pl.BlockSpec(memory_space=pl.ANY)
    return pl.pallas_call(
        partial(hand_out_kernel, tuple(places)),
        in_specs=[far] * len(arrays),
        out_specs=[far] * len(shapes),
        out_shape=shapes,
        scratch_shapes=[pltpu.VMEM(array.shape, array.dtype) for array in arrays]
        + [pltpu.SemaphoreType.DMA((2, len(arrays)))],
        compiler_params=pltpu.CompilerParams(vmem_limit_bytes=VMEM_LIMIT),
    )(*arrays)


def gather_seq(values):
    count = lax.axis_size("seq")
    if count == 4:
        first, second = swap(values, "seq", 1), swap(values, "seq", 2)
        half = values.shape[0] // 2
        third = jnp.concatenate([swap(second[:half], "seq", 1), swap(first[half:], "seq", 2)], axis=0)
        return [values, first, second, third]
    return [values] + [swap(values, "seq", m) for m in range(1, count)]


def exchange_seq(blocks):
    return [blocks[0]] + [swap(blocks[m], "seq", m) for m in range(1, len(blocks))]


def in_order(blocks, axis):
    index = lax.axis_index("seq")
    stacked = jnp.stack(blocks, axis=axis)
    return flip_blocks(stacked, axis, index)


class Halving:
    def __init__(self, blocks, low_first):
        self.blocks = dict(enumerate(blocks))
        bits = [1 << k for k in range(len(blocks).bit_length() - 1)]
        self.bits = bits if low_first else bits[::-1]

    def send(self):
        self.bit = self.bits.pop(0)
        self.kept = [m for m in self.blocks if not m & self.bit]
        return jnp.stack([self.blocks[m | self.bit] for m in self.kept]).astype(BF16)

    def move(self, sent):
        return swap(sent, "seq", self.bit)

    def add(self, came):
        self.blocks = {m: self.blocks[m] + came[k].astype(F32) for k, m in enumerate(self.kept)}


class Spreading:
    def __init__(self, pick):
        chip, chips = lax.axis_index("rows") // 2, lax.axis_size("rows") // 2
        self.own = pick(chip)
        self.sent = [pick(chip ^ m).astype(BF16) for m in range(1, chips)]

    def move(self):
        self.came = [swap(block, "rows", 2 * (m + 1)) for m, block in enumerate(self.sent)]

    def total(self):
        total = self.own
        for block in self.came:
            total = total + block.astype(F32)
        return total


def columns_of(values, index, size):
    return lax.dynamic_slice_in_dim(values, index * size, size, values.ndim - 1)


def lines_of(values, index, size):
    return lax.dynamic_slice_in_dim(values, index * size, size, 0)


def tied(*values):
    return lax.optimization_barrier(values)


def on_square(
    tokens,
    conditioning,
    segment_ids,
    image_index,
    row_fill,
    ada_weight,
    ada_bias,
    qkv_weight,
    qv_bias,
    proj_weight,
    proj_bias,
    up_weight,
    up_bias,
    down_weight,
    down_bias,
    cotangent,
):
    row_count, local_len, width = tokens.shape
    seq_count, groups = lax.axis_size("seq"), lax.axis_size("rows")
    seq_index, row_index = lax.axis_index("seq"), lax.axis_index("rows")
    chips, core = groups // 2, row_index % 2
    full_len = local_len * seq_count
    token_count = row_count * local_len
    heads_dev = HEADS // seq_count
    head_size = width // HEADS
    own = heads_dev * head_size
    image_count = conditioning.shape[0]
    hidden_size = up_weight.shape[1]
    depth = width // groups

    (
        normed_all,
        packed,
        attended,
        attended_tok,
        branch_a,
        middle,
        normed_b,
        grad_out,
        normed_turned,
        grad_turned,
        slot_mod,
        code_row,
        code_col,
        log_totals,
        part_down_bias,
    ) = before_feed_forward(
        image_index,
        segment_ids,
        row_fill,
        conditioning,
        ada_bias,
        qv_bias,
        proj_bias,
        tokens,
        ada_weight.T,
        qkv_weight,
        proj_weight,
        cotangent,
    )
    normed_all = normed_all.reshape(row_count, full_len, width)
    out_sum, grad_sum, part_up_bias, up_main, down_main, *left = feed_forward_reduce(
        normed_b, grad_out, normed_turned, grad_turned, up_weight, down_weight, up_bias
    )
    block_out, grad_middle, grad_view, slot_sums, part_proj_bias, proj_own, proj_low, up_tail, down_tail = after_feed_forward(
        segment_ids,
        slot_mod,
        attended_tok,
        proj_weight,
        down_bias,
        out_sum,
        grad_sum,
        middle,
        branch_a,
        cotangent,
        left,
    )
    grad_view = grad_view.reshape(row_count, heads_dev, head_size, full_len)
    (
        grad_tokens,
        grad_proj_weight,
        grad_down_weight,
        grad_ada_weight,
        grad_cond,
        grad_ada_bias,
        grad_qv_bias,
        grad_proj_bias,
        grad_up_bias,
        grad_down_bias,
        grad_qkv_weight,
    ) = attend_back_and_finish(
        packed,
        attended,
        grad_view,
        log_totals,
        code_col,
        code_row,
        normed_all,
        proj_own,
        proj_low,
        down_main,
        down_tail,
        segment_ids,
        slot_mod,
        slot_sums,
        image_index,
        conditioning,
        (part_proj_bias, part_up_bias, part_down_bias),
        tokens,
        grad_middle,
        qkv_weight,
        ada_weight.T,
    )
    results = list(hand_out(
        block_out,
        grad_tokens,
        grad_cond,
        grad_ada_weight,
        grad_ada_bias,
        grad_qkv_weight,
        grad_qv_bias,
        grad_proj_weight,
        grad_proj_bias,
        (up_main, up_tail),
        grad_up_bias,
        grad_down_weight,
        grad_down_bias,
    ))
    results[11] = results[11].T
    return tuple(results)


def on_device(
    tokens,
    conditioning,
    segment_ids,
    image_index,
    row_fill,
    ada_weight,
    ada_bias,
    qkv_weight,
    qv_bias,
    proj_weight,
    proj_bias,
    up_weight,
    up_bias,
    down_weight,
    down_bias,
    cotangent,
):
    row_count, local_len, width = tokens.shape
    seq_count, groups = lax.axis_size("seq"), lax.axis_size("rows")
    seq_index, row_index = lax.axis_index("seq"), lax.axis_index("rows")
    chips, core = groups // 2, row_index % 2
    full_len = local_len * seq_count
    token_count = row_count * local_len
    heads_dev = HEADS // seq_count
    head_size = width // HEADS
    own = heads_dev * head_size
    image_count = conditioning.shape[0]
    hidden_size = up_weight.shape[1]
    depth = width // groups

    tokens_all = jnp.concatenate(gather_seq(tokens), axis=1)
    order = lax.iota(jnp.int32, seq_count) ^ seq_index
    seg_blocks = flip_blocks(segment_ids.reshape(row_count, seq_count, local_len), 1, seq_index)
    seg_all = seg_blocks.reshape(row_count, full_len)
    places = (order[:, None] * local_len + lax.iota(jnp.int32, local_len)).reshape(1, full_len)
    codes = jnp.where(places < row_fill[:, None], seg_all, -1 - places)
    code_col, code_row = codes[:, :, None], codes[:, None, :]

    qkv_own = jnp.concatenate(
        [lax.dynamic_slice_in_dim(qkv_weight, part * width + seq_index * own, own, 1).T for part in range(3)], axis=0
    )
    bias_own = lax.dynamic_slice_in_dim(qv_bias.astype(F32), seq_index * own, own, 1)
    bias_own = jnp.concatenate([bias_own[0], jnp.zeros((own,), F32), bias_own[1]])

    cond_wide = conditioning.astype(F32)
    cond_low = jax.nn.silu(cond_wide).astype(BF16)
    mod_part = jnp.dot(cond_low, ada_weight, preferred_element_type=F32)
    modulation = lax.all_gather(mod_part, "seq", axis=1, tiled=True) + ada_bias.astype(F32)
    cond_cols = cond_low.reshape(image_count, groups, depth).transpose(1, 0, 2)
    local_seg = lax.dynamic_slice_in_dim(segment_ids, seq_index * local_len, local_len, 1)
    slot_ids = lax.iota(jnp.int32, image_index.shape[1])
    slot_mod = jnp.take(modulation, image_index, axis=0)

    normed_all, packed = project_qkv(
        tokens_all, seg_all, slot_mod[:, :, : 2 * width], qkv_own, bias_own, heads_dev, min(256, full_len)
    )
    square = seq_count == 4 and chips == 4
    attended, log_totals, *attended_sent = attend(packed, code_col, code_row, 512, square)

    slot_pick = (local_seg[:, :, None] == slot_ids).astype(F32)
    mod_tok = jnp.einsum("rts,rse->rte", slot_pick, slot_mod, precision=lax.Precision.HIGHEST)
    shift_a, scale_a, gate_a, shift_b, scale_b, gate_b = jnp.split(mod_tok, 6, axis=-1)
    tokens_wide = tokens.astype(F32)
    upstream = cotangent.astype(F32)
    grad_branch_b = (upstream * gate_b).astype(BF16)
    part_down_bias = jnp.sum(grad_branch_b.astype(F32), axis=(0, 1))
    grad_out = grad_branch_b.reshape(token_count, width)
    grad_turned = turn_halves(grad_out, seq_count, core)

    def by_block(values):
        return [values[..., m * local_len : (m + 1) * local_len] for m in range(seq_count)]

    if square:
        attended_tok = attended_sent[0]
    else:
        attended_tok = in_order(exchange_seq(by_block(attended.reshape(row_count, own, full_len))), 1)
    attended_tok = attended_tok.reshape(row_count, width, local_len)
    branch_a = jnp.einsum(
        "rft,fe->rte", attended_tok, proj_weight, preferred_element_type=F32
    ) + proj_bias.astype(F32)
    middle = tokens_wide + gate_a * branch_a
    normed_b = modulate(middle, shift_b, scale_b).astype(BF16).reshape(token_count, width)
    normed_turned = turn_halves(normed_b, chips, core)

    if square:
        out_sum, grad_sum, part_up_bias, grad_up_weight, down_turned = feed_forward_reduce(
            normed_b, grad_out, normed_turned, grad_turned, up_weight, down_weight, up_bias.astype(F32)
        )
        part_up_bias = part_up_bias.reshape(1, hidden_size)
    else:
        out_sum, grad_sum, up_keep, up_send, down_keep, down_send, part_up_bias = feed_forward(
            normed_b, grad_out, normed_turned, grad_turned, up_weight, down_weight, up_bias.astype(F32)[None], 512
        )
        up_came, down_came = swap(up_send, "rows", 1), swap(down_send, "rows", 1)
    branch_b = out_sum.reshape(row_count, local_len, width) + down_bias.astype(F32)
    grad_normed_b = grad_sum.reshape(row_count, local_len, width)
    block_out = (middle + gate_b * branch_b).astype(BF16)
    grad_gate_b = upstream * branch_b
    _, norm_back_b = jax.vjp(modulate, middle, shift_b, scale_b)
    grad_mid_norm, grad_shift_b, grad_scale_b = norm_back_b(grad_normed_b)
    grad_middle = upstream + grad_mid_norm
    grad_branch_a = (grad_middle * gate_a).astype(BF16)
    grad_gate_a = grad_middle * branch_a
    part_proj_bias = jnp.sum(grad_branch_a.astype(F32), axis=(0, 1))
    grad_attended = jnp.einsum(
        "fe,rte->rft", proj_weight, grad_branch_a, preferred_element_type=F32
    ).astype(BF16)
    heads_blocks = [lax.dynamic_slice_in_dim(grad_attended, (seq_index ^ m) * own, own, 1) for m in range(seq_count)]
    grad_heads_in = jnp.concatenate(exchange_seq(heads_blocks), axis=2)
    grad_view = grad_heads_in.reshape(row_count, heads_dev, head_size, full_len)

    part_proj = jnp.einsum("rte,rft->ef", grad_branch_a, attended_tok, preferred_element_type=F32)
    proj_view = part_proj.reshape(seq_count, 2, depth * groups // (2 * seq_count), width)
    proj_keep = lax.dynamic_index_in_dim(proj_view, core, 1, keepdims=False)
    proj_send = lax.dynamic_index_in_dim(proj_view, 1 - core, 1, keepdims=False).astype(BF16)
    proj_came = swap(proj_send, "rows", 1).reshape(width // 2, width)
    proj_keep = proj_keep.reshape(width // 2, width)
    up_size, down_size = hidden_size // seq_count, width // (2 * seq_count)
    proj_blocks = [
        lines_of(proj_keep, seq_index ^ m, down_size) + lines_of(proj_came, seq_index ^ m, down_size).astype(F32)
        for m in range(seq_count)
    ]
    if square:
        proj_sent = [block.astype(BF16) for block in proj_blocks[1:]]
        grad_view, *proj_sent = tied(grad_view, *proj_sent)
        proj_total = proj_blocks[0]
        for m in range(1, seq_count):
            proj_total = proj_total + swap(proj_sent[m - 1], "seq", m).astype(F32)
    else:
        ups = Halving(
            [
                columns_of(up_keep, seq_index ^ m, up_size) + columns_of(up_came, seq_index ^ m, up_size).astype(F32)
                for m in range(seq_count)
            ],
            True,
        )
        downs = Halving(
            [
                jnp.concatenate(
                    [
                        lines_of(down_keep, seq_index ^ m, down_size)
                        + lines_of(down_came, seq_index ^ m, down_size).astype(F32),
                        proj_blocks[m],
                    ],
                    axis=1,
                )
                for m in range(seq_count)
            ],
            False,
        )
        up_sent, down_sent = ups.send(), downs.send()
        up_came, down_came = ups.move(up_sent), downs.move(down_sent)

    grad_heads, *grad_sent = attend_back(
        packed, attended, grad_view, log_totals, code_col, code_row, 256, 512, square
    )
    grad_own = grad_heads.reshape(row_count, 3 * own, full_len)
    if square:
        grad_flat = grad_sent[0]
    else:
        grad_blocks = exchange_seq(by_block(grad_own))
        grad_flat = in_order([block.reshape(row_count, 3, own, local_len) for block in grad_blocks], 2)
    grad_flat = grad_flat.reshape(row_count, 3 * width, local_len)

    qkv_keep, qkv_send, own_sums = qkv_weight_grad(grad_own, normed_all)
    down_part, proj_part = hidden_size // chips, width // chips
    if square:
        proj_spread = Spreading(lambda chip: columns_of(proj_total, chip, proj_part))
        grad_flat, qkv_send, *proj_spread.sent = tied(grad_flat, qkv_send, *proj_spread.sent)
        proj_spread.move()
    else:
        while ups.bits:
            ups.add(up_came)
            downs.add(down_came)
            up_came, down_came = ups.move(ups.send()), downs.move(downs.send())
        ups.add(up_came)
        downs.add(down_came)
        up_total, down_total = ups.blocks[0], downs.blocks[0][:, :hidden_size]
        proj_total = downs.blocks[0][:, hidden_size:]
        up_spread = Spreading(lambda chip: lines_of(up_total, chip, depth))
        down_spread = Spreading(
            lambda chip: jnp.concatenate(
                [columns_of(down_total, chip, down_part), columns_of(proj_total, chip, proj_part)], axis=1
            )
        )
        up_spread.move()
        down_spread.move()
    qkv_came = swap(qkv_send, "rows", 1)
    grad_normed_a = jnp.einsum("rft,df->rtd", grad_flat, qkv_weight, preferred_element_type=F32)
    _, norm_back_a = jax.vjp(modulate, tokens_wide, shift_a, scale_a)
    grad_tok_norm, grad_shift_a, grad_scale_a = norm_back_a(grad_normed_a)
    grad_tokens = grad_middle + grad_tok_norm
    grad_mod_tok = jnp.concatenate(
        [grad_shift_a, grad_scale_a, grad_gate_a, grad_shift_b, grad_scale_b, grad_gate_b], axis=-1
    )
    slot_grads = jnp.einsum("rts,rte->rse", slot_pick, grad_mod_tok, precision=lax.Precision.HIGHEST)
    image_pick = (image_index[:, :, None] == lax.iota(jnp.int32, image_count)).astype(F32)
    grad_modulation = jnp.einsum("rsi,rse->ie", image_pick, slot_grads, precision=lax.Precision.HIGHEST)

    own_sums = own_sums.reshape(3, own)
    part_qv = lax.dynamic_update_slice(
        jnp.zeros((2, width), F32), jnp.stack([own_sums[0], own_sums[2]]), (0, seq_index * own)
    )
    small = jnp.concatenate([part_qv.reshape(-1), part_proj_bias, part_up_bias[0], part_down_bias])
    columns = ada_weight.shape[1]
    lines = -(-small.size // (seq_count * columns))
    room = seq_count * columns * lines
    small = jnp.pad(small, (0, room - small.size)).reshape(seq_count, lines, columns)
    mod_view = grad_modulation.reshape(image_count, seq_count, columns).transpose(1, 0, 2)
    joined = jnp.concatenate(
        [mod_view, jnp.zeros((seq_count, 1, columns), F32), small, jnp.zeros((seq_count, 7 - lines, columns), F32)], axis=1
    )
    qkv_both = qkv_keep + qkv_came.astype(F32)
    qkv_spread = Spreading(lambda chip: lax.dynamic_index_in_dim(qkv_both, chip, 0, keepdims=False))
    joined, *qkv_spread.sent = tied(joined, *qkv_spread.sent)
    qkv_spread.move()
    if square:
        turned = jnp.concatenate([down_turned, proj_spread.total()], axis=1)
    else:
        grad_up_weight, turned = up_spread.total(), down_spread.total()
    half = down_part // 2
    cut = lambda index: jnp.concatenate(
        [columns_of(turned[:, :down_part], index, half), columns_of(turned[:, down_part:], index, proj_part // 2)], axis=1
    )
    core_keep, core_sent = cut(core), cut(1 - core)
    joined, core_sent = tied(joined, core_sent)
    core_came = swap(core_sent, "rows", 1)
    grad_ada_weight, cond_sum, bias_sums = finish(joined, ada_weight, cond_cols, image_count)
    _, silu_back = jax.vjp(jax.nn.silu, cond_wide)
    grad_cond = silu_back(cond_sum)[0]
    grad_ada_bias = bias_sums[:, 0].reshape(-1)
    small = bias_sums[:, 1 : 1 + lines].reshape(-1)
    grad_qv_bias = small[: 2 * width].reshape(2, width)
    grad_proj_bias = small[2 * width : 3 * width]
    grad_up_bias = small[3 * width : 3 * width + hidden_size]
    grad_down_bias = small[3 * width + hidden_size : 4 * width + hidden_size]

    pair = flip_blocks(jnp.stack([core_keep, core_came]), 0, core).reshape(-1, core_keep.shape[1])
    grad_down_weight, grad_proj_weight = pair[:, :half].T, pair[:, half:].T

    qkv_total = qkv_spread.total()
    pieces = []
    for place in range(3):
        pairs = [((3 * target + place) % seq_count, target) for target in range(seq_count)]
        part_of = [0] * seq_count
        for source, target in pairs:
            part_of[source] = (3 * target + place) // seq_count
        chosen = columns_of(qkv_total, jnp.array(part_of, jnp.int32)[seq_index], own)
        pieces.append(lax.ppermute(chosen, "seq", pairs))
    grad_qkv_weight = jnp.concatenate(pieces, axis=1)
    return (
        block_out,
        grad_tokens,
        grad_cond,
        grad_ada_weight,
        grad_ada_bias,
        grad_qkv_weight,
        grad_qv_bias,
        grad_proj_weight,
        grad_proj_bias,
        grad_up_weight,
        grad_up_bias,
        grad_down_weight,
        grad_down_bias,
    )


def solution(mesh):
    in_specs = (
        P("rows", "seq", None),
        P("rows", None),
        P("rows", None),
        P("rows", None),
        P("rows"),
        P(None, "seq"),
        P(),
        P(),
        P(),
        P(),
        P(),
        P(),
        P(),
        P(),
        P(),
        P("rows", "seq", None),
    )
    out_specs = (
        P("rows", "seq", None),
        P("rows", "seq", None),
        P("rows", None),
        P("rows", "seq"),
        P(),
        P("rows", "seq"),
        P(),
        P("rows", "seq"),
        P(),
        P("rows", "seq"),
        P(),
        P("rows", "seq"),
        P(),
    )
    square = mesh.shape["seq"] == 4 and mesh.shape["rows"] == 8
    return jax.shard_map(
        on_square if square else on_device, mesh=mesh, in_specs=in_specs, out_specs=out_specs, check_vma=False
    )
```

```python
from functools import partial
import math

import jax
import jax.numpy as jnp
from jax import lax
from jax.experimental import pallas as pl
from jax.experimental.pallas import tpu as pltpu
from jax.sharding import PartitionSpec as P

HEADS = 16
LOG2E = math.log2(math.e)
VMEM_LIMIT = 60 << 20
BF16 = jnp.bfloat16
F32 = jnp.float32

norm_eps = 1e-06


def modulate(values, offset, factor):
    center = values - jnp.mean(values, axis=-1, keepdims=True)
    spread = jnp.mean(center * center, axis=-1, keepdims=True)
    return center * lax.rsqrt(spread + norm_eps) * (1.0 + factor) + offset


def gelu_tanh(values):
    return jax.nn.gelu(values, approximate=True)


def swap(values, axis, mask):
    count = lax.axis_size(axis)
    return lax.ppermute(values, axis, [(i, i ^ mask) for i in range(count)])


def flip_blocks(values, axis, mask):
    return jnp.take(values, lax.iota(jnp.int32, values.shape[axis]) ^ mask, axis=axis)


def qkv_kernel(slot_row, seg, mod, tokens, weight, bias, normed_ref, qkv_ref):
    width = tokens.shape[-1]
    values = tokens[0].astype(F32)
    picked = (seg[0] == slot_row[...]).astype(BF16)
    table = mod[0]
    high = table.astype(BF16)
    rest = table - high.astype(F32)
    middle = rest.astype(BF16)
    last = (rest - middle.astype(F32)).astype(BF16)
    stacked = jnp.concatenate([high, middle, last], axis=0)
    per_token = jnp.dot(picked, stacked, preferred_element_type=F32)
    normed = modulate(values, per_token[:, :width], per_token[:, width:]).astype(BF16)
    normed_ref[0] = normed
    mixed = lax.dot_general(weight[...], normed, (((1,), (1,)), ((), ())), preferred_element_type=F32)
    mixed = (mixed + bias[...]).astype(BF16)
    _, parts, heads, size, _ = qkv_ref.shape
    for part in range(parts):
        for head in range(heads):
            start = (part * heads + head) * size
            qkv_ref[0, part, head] = mixed[start : start + size]


def project_qkv(tokens, seg, slot_mod, weight, bias, heads, block):
    rows, length, width = tokens.shape
    slots = slot_mod.shape[1]
    features = weight.shape[0]
    size = features // (3 * heads)
    slot_row = jnp.tile(lax.iota(jnp.int32, slots), 3)[None]
    return pl.pallas_call(
        qkv_kernel,
        grid=(rows, length // block),
        in_specs=[
            pl.BlockSpec((1, 3 * slots), lambda r, t: (0, 0)),
            pl.BlockSpec((1, block, 1), lambda r, t: (r, t, 0)),
            pl.BlockSpec((1, slots, 2 * width), lambda r, t: (r, 0, 0)),
            pl.BlockSpec((1, block, width), lambda r, t: (r, t, 0)),
            pl.BlockSpec((features, width), lambda r, t: (0, 0)),
            pl.BlockSpec((features, 1), lambda r, t: (0, 0)),
        ],
        out_specs=[
            pl.BlockSpec((1, block, width), lambda r, t: (r, t, 0)),
            pl.BlockSpec((1, 3, heads, size, block), lambda r, t: (r, 0, 0, 0, t)),
        ],
        out_shape=[
            jax.ShapeDtypeStruct((rows, length, width), BF16),
            jax.ShapeDtypeStruct((rows, 3, heads, size, length), BF16),
        ],
        compiler_params=pltpu.CompilerParams(vmem_limit_bytes=VMEM_LIMIT),
        cost_estimate=pl.CostEstimate(
            flops=2 * rows * length * width * features,
            bytes_accessed=2 * rows * length * (2 * width + features),
            transcendentals=0,
        ),
    )(slot_row, seg[:, :, None], slot_mod, tokens, weight, bias[:, None])


def peers_of(seq):
    x, y = lax.rem(seq, 2), lax.div(seq, 2)
    return [seq + 1 - 2 * x, seq + 2 - 4 * y, 3 - seq]


def call(devices):
    barrier = pltpu.get_barrier_semaphore()
    for device in devices:
        pl.semaphore_signal(barrier, inc=1, device_id=device, device_id_type=pl.DeviceIdType.MESH)


def meet(devices):
    pl.semaphore_wait(pltpu.get_barrier_semaphore(), len(devices))


def greet(devices):
    call(devices)
    meet(devices)


def send_block(source, target, sent, came, index, device):
    return pltpu.make_async_remote_copy(
        src_ref=source,
        dst_ref=target,
        send_sem=sent.at[index],
        recv_sem=came.at[index],
        device_id=device,
        device_id_type=pl.DeviceIdType.MESH,
    )


def attend_kernel(block, scale, code_col, code_row, query, key, value, out_ref, lse_ref, token_ref=None, sent=None, came=None, kept=None):
    length = query.shape[-1]
    keys = key[0, 0].astype(F32).T.astype(BF16)
    values = value[0, 0]
    codes = code_col[0]
    row, head = (pl.program_id(0), pl.program_id(1)) if sent is not None else (0, 0)
    rows, heads = out_ref.shape[:2]
    if sent is not None:
        seq = lax.axis_index("seq")
        peers = peers_of(seq)
        size = length // 4

        @pl.when((row == 0) & (head == 0))
        def _():
            greet([{"seq": peer} for peer in peers])

        def to_peer(r, h, m):
            lanes = pl.ds(m * size, size)
            place = (r * heads + h) * 3 + m - 1
            return send_block(out_ref.at[r, h, :, lanes], token_ref.at[r, seq, h], sent, came, place, {"seq": peers[m - 1]})

        def to_self(r, h):
            return pltpu.make_async_copy(out_ref.at[r, h, :, pl.ds(0, size)], token_ref.at[r, seq, h], kept.at[r * heads + h])

    for step in range(length // block):
        here = pl.ds(step * block, block)
        scores = jnp.dot(keys, query[0, 0, :, here], preferred_element_type=F32)
        scores = jnp.where(codes == code_row[0, :, here], scores * scale, -1e30)
        peak = jnp.max(scores, axis=0, keepdims=True)
        raised = jnp.exp2(scores - peak)
        total = jnp.sum(raised, axis=0, keepdims=True)
        probs = (raised * (1.0 / total)).astype(BF16)
        out_ref[row, head, :, here] = jnp.dot(values, probs, preferred_element_type=F32).astype(BF16)
        lse_ref[0, 0, :, here] = peak + jnp.log2(total)

    if sent is not None:
        to_self(row, head).start()
        for m in range(1, 4):
            to_peer(row, head, m).start()

        @pl.when((row == rows - 1) & (head == heads - 1))
        def _():
            for r in range(rows):
                for h in range(heads):
                    to_self(r, h).wait()
                    for m in range(1, 4):
                        to_peer(r, h, m).wait()


def attend(packed, col, row, block, exchange):
    rows, _, heads, size, length = packed.shape
    part = lambda j: pl.BlockSpec((1, None, 1, size, length), lambda r, h: (r, j, h, 0, 0))
    out_specs = [
        pl.BlockSpec((1, 1, size, length), lambda r, h: (r, h, 0, 0)),
        pl.BlockSpec((1, 1, 1, length), lambda r, h: (r, h, 0, 0)),
    ]
    out_shape = [
        jax.ShapeDtypeStruct((rows, heads, size, length), BF16),
        jax.ShapeDtypeStruct((rows, heads, 1, length), F32),
    ]
    scratch = []
    extra = {}
    if exchange:
        out_specs[0] = pl.BlockSpec((rows, heads, size, length), lambda r, h: (0, 0, 0, 0))
        out_specs.append(pl.BlockSpec(memory_space=pl.ANY))
        out_shape.append(jax.ShapeDtypeStruct((rows, 4, heads, size, length // 4), BF16))
        count = rows * heads
        scratch = [pltpu.SemaphoreType.DMA((3 * count,)), pltpu.SemaphoreType.DMA((3 * count,)), pltpu.SemaphoreType.DMA((count,))]
        extra = dict(collective_id=2, has_side_effects=True)
    return pl.pallas_call(
        partial(attend_kernel, block, size**-0.5 * LOG2E),
        grid=(rows, heads),
        in_specs=[
            pl.BlockSpec((1, length, 1), lambda r, h: (r, 0, 0)),
            pl.BlockSpec((1, 1, length), lambda r, h: (r, 0, 0)),
            part(0),
            part(1),
            part(2),
        ],
        out_specs=out_specs,
        out_shape=out_shape,
        scratch_shapes=scratch,
        compiler_params=pltpu.CompilerParams(vmem_limit_bytes=VMEM_LIMIT, **extra),
        cost_estimate=pl.CostEstimate(
            flops=8 * rows * heads * length * length * 128,
            bytes_accessed=8 * rows * heads * length * size,
            transcendentals=rows * heads * length * length,
        ),
    )(col, row, packed, packed, packed)


def attend_back_kernel(
    block,
    inner,
    scale,
    exchange,
    code_col,
    code_row,
    query,
    key,
    value,
    out,
    grad_out,
    lse,
    grad_ref,
    *rest,
):
    length = query.shape[-1]
    size = query.shape[-2]
    row, head = (pl.program_id(0), pl.program_id(1)) if exchange else (0, 0)
    rows, _, heads = grad_ref.shape[:3]
    if exchange:
        token_ref, key_sum, value_sum, keys, values, sent, came, kept = rest
        seq = lax.axis_index("seq")
        peers = peers_of(seq)
        local = length // 4

        @pl.when((row == 0) & (head == 0))
        def _():
            greet([{"seq": peer} for peer in peers])

        def to_peer(r, h, m):
            lanes = pl.ds(m * local, local)
            place = (r * heads + h) * 3 + m - 1
            return send_block(grad_ref.at[r, :, h, :, lanes], token_ref.at[r, :, seq, h], sent, came, place, {"seq": peers[m - 1]})

        def to_self(r, h):
            lanes = pl.ds(0, local)
            return pltpu.make_async_copy(grad_ref.at[r, :, h, :, lanes], token_ref.at[r, :, seq, h], kept.at[r * heads + h])

    else:
        key_sum, value_sum, keys, values = rest
    keys[...] = key[0, 0].astype(F32).T.astype(BF16)
    values[...] = value[0, 0].astype(F32).T.astype(BF16)
    for step in range(length // block):
        here = pl.ds(step * block, block)
        query_low = query[0, 0, :, here]
        grad_low = grad_out[0, 0, :, here]
        query_rows = query_low.astype(F32).T.astype(BF16)
        grad_rows = grad_low.astype(F32).T.astype(BF16)
        row_dot = jnp.sum(grad_low.astype(F32) * out[0, 0, :, here].astype(F32), axis=0, keepdims=True)
        grad_query = jnp.zeros((size, block), F32)
        for part in range(length // inner):
            there = pl.ds(part * inner, inner)
            scores = jnp.dot(keys[there, :], query_low, preferred_element_type=F32)
            scores = jnp.where(code_col[0, there, :] == code_row[0, :, here], scores * (scale * LOG2E), -1e30)
            probs = jnp.exp2(scores - lse[0, 0, :, here])
            grad_probs = jnp.dot(values[there, :], grad_low, preferred_element_type=F32)
            grad_raw = (probs * (grad_probs - row_dot) * scale).astype(BF16)
            value_part = jnp.dot(probs.astype(BF16), grad_rows, preferred_element_type=F32)
            key_part = jnp.dot(grad_raw, query_rows, preferred_element_type=F32)
            if step == 0:
                value_sum[there, :] = value_part
                key_sum[there, :] = key_part
            else:
                value_sum[there, :] += value_part
                key_sum[there, :] += key_part
            grad_query += jnp.dot(key[0, 0, :, there], grad_raw, preferred_element_type=F32)
        grad_ref[row, 0, head, :, here] = grad_query.astype(BF16)
    grad_ref[row, 1, head] = key_sum[...].T.astype(BF16)
    grad_ref[row, 2, head] = value_sum[...].T.astype(BF16)

    if exchange:
        to_self(row, head).start()
        for m in range(1, 4):
            to_peer(row, head, m).start()

        @pl.when((row == rows - 1) & (head == heads - 1))
        def _():
            for r in range(rows):
                for h in range(heads):
                    to_self(r, h).wait()
                    for m in range(1, 4):
                        to_peer(r, h, m).wait()


def attend_back(packed, out, grad_out, lse, col, row, block, inner, exchange):
    rows, _, heads, size, length = packed.shape
    part = lambda j: pl.BlockSpec((1, None, 1, size, length), lambda r, h: (r, j, h, 0, 0))
    whole = pl.BlockSpec((1, 1, size, length), lambda r, h: (r, h, 0, 0))
    out_specs = [pl.BlockSpec((1, 3, 1, size, length), lambda r, h: (r, 0, h, 0, 0))]
    out_shape = [jax.ShapeDtypeStruct((rows, 3, heads, size, length), BF16)]
    scratch = []
    extra = {}
    if exchange:
        out_specs = [
            pl.BlockSpec((rows, 3, heads, size, length), lambda r, h: (0, 0, 0, 0, 0)),
            pl.BlockSpec(memory_space=pl.ANY),
        ]
        out_shape.append(jax.ShapeDtypeStruct((rows, 3, 4, heads, size, length // 4), BF16))
        count = rows * heads
        scratch = [pltpu.SemaphoreType.DMA((3 * count,)), pltpu.SemaphoreType.DMA((3 * count,)), pltpu.SemaphoreType.DMA((count,))]
        extra = dict(collective_id=3, has_side_effects=True)
    return pl.pallas_call(
        partial(attend_back_kernel, block, inner, size**-0.5, exchange),
        grid=(rows, heads),
        in_specs=[
            pl.BlockSpec((1, length, 1), lambda r, h: (r, 0, 0)),
            pl.BlockSpec((1, 1, length), lambda r, h: (r, 0, 0)),
            part(0),
            part(1),
            part(2),
            whole,
            whole,
            pl.BlockSpec((1, 1, 1, length), lambda r, h: (r, h, 0, 0)),
        ],
        out_specs=out_specs,
        out_shape=out_shape,
        scratch_shapes=[
            pltpu.VMEM((length, size), F32),
            pltpu.VMEM((length, size), F32),
            pltpu.VMEM((length, size), BF16),
            pltpu.VMEM((length, size), BF16),
        ]
        + scratch,
        compiler_params=pltpu.CompilerParams(vmem_limit_bytes=VMEM_LIMIT, **extra),
        cost_estimate=pl.CostEstimate(
            flops=20 * rows * heads * length * length * 128,
            bytes_accessed=16 * rows * heads * length * size,
            transcendentals=rows * heads * length * length,
        ),
    )(col, row, packed, packed, packed, out, grad_out, lse)


def mlp_kernel(
    normed, grad_out, normed_turned, grad_turned, up, down, bias, out_sum, grad_sum, up_keep, up_send, down_keep, down_send, bias_sum
):
    step = pl.program_id(0)
    half = up_keep.shape[0]
    c0 = math.sqrt(2 / math.pi)
    c1 = c0 * 0.044715
    hidden = jnp.dot(normed[...], up[...], preferred_element_type=F32) + bias[...]
    square = hidden * hidden
    gate = 0.5 + 0.5 * jnp.tanh(hidden * (c0 + c1 * square))
    raised = hidden * gate
    slope = gate + raised * (1.0 - gate) * (2 * c0 + 6 * c1 * square)
    active = raised.astype(BF16)
    back = (((1,), (1,)), ((), ()))
    grad_active = lax.dot_general(grad_out[...], down[...], back, preferred_element_type=F32)
    grad_wide = (grad_active * slope).astype(BF16)
    out_part = jnp.dot(active, down[...], preferred_element_type=F32)
    grad_part = lax.dot_general(grad_wide, up[...], back, preferred_element_type=F32)

    @pl.when(step == 0)
    def _():
        out_sum[...] = out_part
        grad_sum[...] = grad_part

    @pl.when(step > 0)
    def _():
        out_sum[...] += out_part
        grad_sum[...] += grad_part

    bias_sum[...] = jnp.sum(grad_wide.astype(F32), axis=0, keepdims=True)
    up_keep[...] = jnp.dot(normed_turned[:half], grad_wide, preferred_element_type=F32)
    up_send[...] = jnp.dot(normed_turned[half:], grad_wide, preferred_element_type=F32).astype(BF16)
    down_keep[...] = jnp.dot(grad_turned[:half], active, preferred_element_type=F32)
    down_send[...] = jnp.dot(grad_turned[half:], active, preferred_element_type=F32).astype(BF16)


def feed_forward(normed, grad_out, normed_turned, grad_turned, up, down, bias, tile):
    count, width = normed.shape
    hidden = up.shape[1]
    half = width // 2
    fixed = lambda *shape: pl.BlockSpec(shape, lambda t: (0, 0))
    across = lambda rows: pl.BlockSpec((rows, tile), lambda t: (0, t))
    shape = jax.ShapeDtypeStruct
    return pl.pallas_call(
        mlp_kernel,
        grid=(hidden // tile,),
        in_specs=[
            fixed(count, width),
            fixed(count, width),
            fixed(width, count),
            fixed(width, count),
            across(width),
            pl.BlockSpec((tile, width), lambda t: (t, 0)),
            across(1),
        ],
        out_specs=[fixed(count, width), fixed(count, width), across(half), across(half), across(half), across(half), across(1)],
        out_shape=[
            shape((count, width), F32),
            shape((count, width), F32),
            shape((half, hidden), F32),
            shape((half, hidden), BF16),
            shape((half, hidden), F32),
            shape((half, hidden), BF16),
            shape((1, hidden), F32),
        ],
        compiler_params=pltpu.CompilerParams(vmem_limit_bytes=VMEM_LIMIT),
        cost_estimate=pl.CostEstimate(
            flops=12 * count * width * hidden,
            bytes_accessed=10 * width * hidden,
            transcendentals=count * hidden,
        ),
    )(normed, grad_out, normed_turned, grad_turned, up, down, bias)


def turn_halves(values, groups, mine):
    count, width = values.shape
    view = values.T.reshape(groups, 2, width // (2 * groups), count)
    keep = lax.dynamic_index_in_dim(view, mine, 1, keepdims=False).reshape(width // 2, count)
    send = lax.dynamic_index_in_dim(view, 1 - mine, 1, keepdims=False).reshape(width // 2, count)
    return jnp.concatenate([keep, send], axis=0)


STAGES = 2


def mlp_reduce_kernel(
    tiles,
    normed,
    grad_out,
    normed_turned,
    grad_turned,
    up0,
    up1,
    up2,
    up3,
    down0,
    down1,
    down2,
    down3,
    bias,
    out_sum,
    grad_sum,
    bias_sum,
    up_total,
    down_total,
    left_full,
    left_up,
    left_up_low,
    left_down,
    left_down_low,
    up_mine,
    down_mine,
    up_core,
    down_core,
    up_core_got,
    down_core_got,
    up_half,
    down_half,
    up_out,
    down_out,
    up_got,
    down_got,
    up_quarter,
    down_quarter,
    up_last,
    down_last,
    up_last_got,
    down_last_got,
    chip_full,
    chip_out,
    chip_got,
    core_sent,
    core_came,
    seq_sent,
    seq_came,
    last_sent,
    last_came,
    chip_sent,
    chip_came,
    bias_line,
):
    step = pl.program_id(0)
    seq, row = lax.axis_index("seq"), lax.axis_index("rows")
    half = normed_turned.shape[0] // 2
    x, y = lax.rem(seq, 2), lax.div(seq, 2)
    core_peer = {"rows": row + 1 - 2 * lax.rem(row, 2)}
    x_peer = {"seq": seq + 1 - 2 * x}
    y_peer = {"seq": seq + 2 - 4 * y}
    chip, core = lax.div(row, 2), lax.rem(row, 2)
    to_chip = [lax.rem(chip + k, 4) for k in range(4)]
    chip_peers = [{"rows": 2 * to_chip[k] + core} for k in range(4)]

    @pl.when(step == 0)
    def _():
        bias_line[...] = bias[...].astype(F32).reshape(1, bias.shape[0])
        barrier = pltpu.get_barrier_semaphore()
        for peer in (core_peer, x_peer, y_peer, *chip_peers[1:]):
            pl.semaphore_signal(barrier, inc=1, device_id=peer, device_id_type=pl.DeviceIdType.MESH)
        pl.semaphore_wait(barrier, 6)

    def copies(source, target, sent, came, tile, places, kind, device):
        slot = lax.rem(tile, places)
        return pltpu.make_async_remote_copy(
            src_ref=source.at[lax.rem(tile, 2)],
            dst_ref=target.at[slot],
            send_sem=sent.at[kind, slot],
            recv_sem=came.at[kind, slot],
            device_id=device,
            device_id_type=pl.DeviceIdType.MESH,
        )

    def to_core(tile):
        return (
            copies(up_core, up_core_got, core_sent, core_came, tile, 2, 0, core_peer),
            copies(down_core, down_core_got, core_sent, core_came, tile, 2, 1, core_peer),
        )

    def to_seq(tile):
        return (
            copies(up_out, up_got, seq_sent, seq_came, tile, 3, 0, x_peer),
            copies(down_out, down_got, seq_sent, seq_came, tile, 3, 1, y_peer),
        )

    def to_last(tile):
        return (
            copies(up_last, up_last_got, last_sent, last_came, tile, 3, 0, y_peer),
            copies(down_last, down_last_got, last_sent, last_came, tile, 3, 1, x_peer),
        )

    def to_chips(slot):
        return [
            pltpu.make_async_remote_copy(
                src_ref=chip_out.at[slot, to_chip[k]],
                dst_ref=chip_got.at[slot, k - 1],
                send_sem=chip_sent.at[k - 1, slot],
                recv_sem=chip_came.at[k - 1, slot],
                device_id=chip_peers[k],
                device_id_type=pl.DeviceIdType.MESH,
            )
            for k in range(1, 4)
        ]

    @pl.when((step >= 1) & (step <= tiles))
    def _():
        slot = lax.rem(step + 1, 2)
        for copy in to_core(step - 1):
            copy.wait()
        for other in range(2):
            kept, gone = 2 * other + x, 2 * other + 1 - x
            up_half[slot, other] = up_mine[slot, kept] + up_core_got[slot, kept].astype(F32)
            up_out[slot, other] = (up_mine[slot, gone] + up_core_got[slot, gone].astype(F32)).astype(BF16)
            kept, gone = 2 * y + other, 2 * (1 - y) + other
            down_half[slot, other] = down_mine[slot, kept] + down_core_got[slot, kept].astype(F32)
            down_out[slot, other] = (down_mine[slot, gone] + down_core_got[slot, gone].astype(F32)).astype(BF16)
        for copy in to_seq(step - 1):
            copy.start()

    @pl.when(step >= 2)
    def _():
        slot = lax.rem(step, 2)
        place3 = lax.rem(step + 1, 3)
        for copy in to_seq(step - 2):
            copy.wait()
        up_quarter[slot] = up_half[slot, y] + up_got[place3, y].astype(F32)
        up_last[slot] = (up_half[slot, 1 - y] + up_got[place3, 1 - y].astype(F32)).astype(BF16)
        down_quarter[slot] = down_half[slot, x] + down_got[place3, x].astype(F32)
        down_last[slot] = (down_half[slot, 1 - x] + down_got[place3, 1 - x].astype(F32)).astype(BF16)
        @pl.when(step < tiles + 1)
        def _():
            for copy in to_last(step - 2):
                copy.start()

        @pl.when(step == tiles + 1)
        def _():
            left_up[...] = up_quarter[slot]
            left_up_low[...] = up_last[slot]
            left_down[...] = down_quarter[slot]
            left_down_low[...] = down_last[slot]


    @pl.when(step >= 4)
    def _():
        slot = lax.rem(step, 2)
        for copy in to_chips(slot):
            copy.wait()
        for kind, total in enumerate((up_total, down_total)):
            value = chip_full[slot, chip, kind]
            for k in range(3):
                value = value + chip_got[slot, k, kind].astype(F32)
            total[...] = value

    @pl.when(step >= 3)
    def _():
        slot = lax.rem(step + 1, 2)
        place3 = lax.rem(step, 3)
        for copy in to_last(step - 3):
            copy.wait()
        size = half // 4
        ups = up_quarter[slot] + up_last_got[place3].astype(F32)
        downs = down_quarter[slot] + down_last_got[place3].astype(F32)
        for place in range(4):
            up_block = ups[place * size : (place + 1) * size]
            down_block = downs[:, place * 128 : (place + 1) * 128]
            chip_full[slot, place, 0] = up_block
            chip_full[slot, place, 1] = down_block
            chip_out[slot, place, 0] = up_block.astype(BF16)
            chip_out[slot, place, 1] = down_block.astype(BF16)
        @pl.when(step < tiles + 1)
        def _():
            for copy in to_chips(slot):
                copy.start()

        @pl.when(step == tiles + 1)
        def _():
            left_full[...] = chip_full[slot]

    @pl.when(step < tiles)
    def _():
        slot = lax.rem(step, 2)
        up = jnp.concatenate([up0[...], up1[...], up2[...], up3[...]], axis=1)
        down = jnp.concatenate([down0[...], down1[...], down2[...], down3[...]], axis=0)
        hidden_part = bias.shape[0] // 4
        biases = jnp.concatenate(
            [
                bias_line[:, pl.ds(pl.multiple_of(owner * hidden_part + step * 128, 128), 128)]
                for owner in range(4)
            ],
            axis=1,
        )
        c0 = math.sqrt(2 / math.pi)
        c1 = c0 * 0.044715
        hidden = jnp.dot(normed[...], up, preferred_element_type=F32) + biases
        square = hidden * hidden
        gate = 0.5 + 0.5 * jnp.tanh(hidden * (c0 + c1 * square))
        raised = hidden * gate
        slope = gate + raised * (1.0 - gate) * (2 * c0 + 6 * c1 * square)
        active = raised.astype(BF16)
        down_part = jnp.dot(grad_turned[...], active, preferred_element_type=F32)
        for owner in range(4):
            size = half // 4
            down_mine[slot, owner] = down_part[owner * size : (owner + 1) * size]
            down_core[slot, owner] = down_part[half + owner * size : half + (owner + 1) * size].astype(BF16)
        to_core(step)[1].start()
        back = (((1,), (1,)), ((), ()))
        grad_active = lax.dot_general(grad_out[...], down, back, preferred_element_type=F32)
        grad_wide = (grad_active * slope).astype(BF16)
        up_part = jnp.dot(normed_turned[...], grad_wide, preferred_element_type=F32)
        for owner in range(4):
            columns = slice(owner * 128, (owner + 1) * 128)
            up_mine[slot, owner] = up_part[:half, columns]
            up_core[slot, owner] = up_part[half:, columns].astype(BF16)
        to_core(step)[0].start()
        sums = jnp.sum(grad_wide.astype(F32), axis=0, keepdims=True)
        for owner in range(4):
            bias_sum[owner] = sums[:, owner * 128 : (owner + 1) * 128]
        out_part = jnp.dot(active, down, preferred_element_type=F32)
        grad_part = lax.dot_general(grad_wide, up, back, preferred_element_type=F32)

        @pl.when(step == 0)
        def _():
            out_sum[...] = out_part
            grad_sum[...] = grad_part

        @pl.when(step > 0)
        def _():
            out_sum[...] += out_part
            grad_sum[...] += grad_part


def feed_forward_reduce(normed, grad_out, normed_turned, grad_turned, up, down, bias):
    count, width = normed.shape
    hidden = up.shape[1]
    part = hidden // 4
    tiles = part // 128
    half, quarter = width // 2, width // 8
    last = tiles - 1
    shape = jax.ShapeDtypeStruct
    fixed = lambda *dims: pl.BlockSpec(dims, lambda t: (0, 0), pipeline_mode=pl.Buffered(buffer_count=1))
    result = lambda *dims: pl.BlockSpec(dims, lambda t: (0, 0))
    done = lambda t: jnp.maximum(t - 4, 0)

    def up_block(owner):
        return pl.BlockSpec((width, 128), lambda t: (0, owner * tiles + jnp.minimum(t, last)))

    def down_block(owner):
        return pl.BlockSpec((128, width), lambda t: (owner * tiles + jnp.minimum(t, last), 0))

    bias_block = pl.BlockSpec((4, 1, 128), lambda t: (0, 0, jnp.minimum(t, last)))
    pair = lambda dtype, *dims: pltpu.VMEM((2,) + dims, dtype)
    triple = lambda dtype, *dims: pltpu.VMEM((3,) + dims, dtype)
    return pl.pallas_call(
        partial(mlp_reduce_kernel, tiles),
        grid=(tiles + STAGES,),
        in_specs=[fixed(count, width), fixed(count, width), fixed(width, count), fixed(width, count)]
        + [up_block(owner) for owner in range(4)]
        + [down_block(owner) for owner in range(4)]
        + [pl.BlockSpec((hidden,), lambda t: (0,))],
        out_specs=[
            result(count, width),
            result(count, width),
            bias_block,
            pl.BlockSpec((quarter, 128), lambda t: (0, done(t))),
            pl.BlockSpec((quarter, 128), lambda t: (0, done(t))),
            pl.BlockSpec((4, 2, quarter, 128), lambda t: (0, 0, 0, 0)),
            result(half, 128),
            result(half, 128),
            result(quarter, 512),
            result(quarter, 512),
        ],
        out_shape=[
            shape((count, width), F32),
            shape((count, width), F32),
            shape((4, 1, part), F32),
            shape((quarter, part - 256), F32),
            shape((quarter, part - 256), F32),
            shape((4, 2, quarter, 128), F32),
            shape((half, 128), F32),
            shape((half, 128), BF16),
            shape((quarter, 512), F32),
            shape((quarter, 512), BF16),
        ],
        scratch_shapes=[
            pair(F32, 4, half, 128),
            pair(F32, 4, quarter, 512),
            pair(BF16, 4, half, 128),
            pair(BF16, 4, quarter, 512),
            pair(BF16, 4, half, 128),
            pair(BF16, 4, quarter, 512),
            pair(F32, 2, half, 128),
            pair(F32, 2, quarter, 512),
            pair(BF16, 2, half, 128),
            pair(BF16, 2, quarter, 512),
            triple(BF16, 2, half, 128),
            triple(BF16, 2, quarter, 512),
            pair(F32, half, 128),
            pair(F32, quarter, 512),
            pair(BF16, half, 128),
            pair(BF16, quarter, 512),
            triple(BF16, half, 128),
            triple(BF16, quarter, 512),
            pair(F32, 4, 2, quarter, 128),
            pair(BF16, 4, 2, quarter, 128),
            pair(BF16, 3, 2, quarter, 128),
        ]
        + [pltpu.SemaphoreType.DMA((2, 2))] * 2
        + [pltpu.SemaphoreType.DMA((2, 3))] * 4
        + [pltpu.SemaphoreType.DMA((3, 2))] * 2
        + [pltpu.VMEM((1, hidden), F32)],
        compiler_params=pltpu.CompilerParams(collective_id=1, has_side_effects=True, vmem_limit_bytes=VMEM_LIMIT),
        cost_estimate=pl.CostEstimate(
            flops=12 * count * width * hidden,
            bytes_accessed=6 * width * hidden,
            transcendentals=count * hidden,
        ),
    )(normed, grad_out, normed_turned, grad_turned, up, up, up, up, down, down, down, down, bias)


def slot_column(slots):
    return lax.rem(lax.broadcasted_iota(jnp.int32, (3 * slots, 1), 0), slots)


def split_low(values):
    high = values.astype(BF16)
    rest = values - high.astype(F32)
    middle = rest.astype(BF16)
    return high, middle, (rest - middle.astype(F32)).astype(BF16)


def per_token(slot_col, seg_row, table):
    picked = (slot_col == seg_row).astype(BF16)
    return lax.dot_general(
        picked, jnp.concatenate(split_low(table), axis=0), (((0,), (0,)), ((), ())), preferred_element_type=F32
    )


def per_slot(slot_col, seg_row, values):
    slots = slot_col.shape[0] // 3
    picked = (slot_col[:slots] == seg_row).astype(BF16)
    return sum(jnp.dot(picked, part, preferred_element_type=F32) for part in split_low(values))


def normalize(values):
    center = values - jnp.mean(values, axis=-1, keepdims=True)
    inverse = lax.rsqrt(jnp.mean(center * center, axis=-1, keepdims=True) + norm_eps)
    return center * inverse, inverse


def normalize_back(normal, inverse, grad):
    return inverse * (grad - jnp.mean(grad, axis=-1, keepdims=True) - normal * jnp.mean(grad * normal, axis=-1, keepdims=True))


def after_kernel(
    seg,
    table,
    bias,
    attended,
    weight,
    out_sum,
    grad_sum,
    middle,
    branch,
    cotangent,
    left_full,
    left_up,
    left_up_low,
    left_down,
    left_down_low,
    block_out,
    grad_middle_ref,
    view_ref,
    slot_sums,
    bias_sum,
    proj_own,
    proj_low,
    up_tail,
    down_tail,
    attended_here,
    weight_here,
    rows_here,
    cotangent_here,
    block_here,
    middle_here,
    normal_here,
    grad_here,
    heads_out,
    total,
    core_out,
    core_got,
    load_sem,
    first_sem,
    store_sem,
    sent,
    came,
    kept,
    core_sent,
    core_came,
    full_here,
    up_here,
    up_low_here,
    down_here,
    down_low_here,
    up_got,
    down_got,
    chip_out,
    chip_got,
    left_sem,
    left_sent,
    left_came,
):
    rows, length, width = cotangent_here.shape
    depth, own = width // 8, width // 4
    seq, row = lax.axis_index("seq"), lax.axis_index("rows")
    core = lax.rem(row, 2)
    core_peer = {"rows": row + 1 - 2 * core}
    peers = peers_of(seq)
    slot_col = slot_column(table.shape[1])

    def go(copies):
        for copy in copies:
            copy.start()

    def end(copies):
        for copy in copies:
            copy.wait()

    def loads(r):
        lines = pl.ds(r * length, length)
        pairs = (
            (out_sum.at[lines], rows_here.at[r, 0]),
            (grad_sum.at[lines], rows_here.at[r, 1]),
            (middle.at[r], rows_here.at[r, 2]),
            (branch.at[r], rows_here.at[r, 3]),
            (cotangent.at[r], cotangent_here.at[r]),
        )
        return [pltpu.make_async_copy(source, target, load_sem.at[r, k]) for k, (source, target) in enumerate(pairs)]

    load_weight = pltpu.make_async_copy(weight, weight_here, first_sem.at[0])
    load_attended = pltpu.make_async_copy(attended, attended_here, first_sem.at[1])
    lefts = ((left_full, full_here.at[0]), (left_up_low, up_low_here), (left_down_low, down_low_here), (left_up, up_here), (left_down, down_here))
    load_left = [pltpu.make_async_copy(source, target, left_sem.at[k]) for k, (source, target) in enumerate(lefts)]
    go(load_left + loads(0) + [load_weight] + loads(1) + [load_attended])
    chip = lax.div(row, 2)
    to_chip = [lax.rem(chip + k, 4) for k in range(4)]
    chip_peers = [{"rows": 2 * to_chip[k] + core} for k in range(4)]

    def to_chips(tile):
        return [
            send_to(
                chip_out.at[tile, to_chip[k]],
                chip_got.at[tile, k - 1],
                left_sent.at[2 + 3 * tile + k - 1],
                left_came.at[2 + 3 * tile + k - 1],
                chip_peers[k],
            )
            for k in range(1, 4)
        ]

    left_copies = [
        send_to(up_low_here, up_got, left_sent.at[0], left_came.at[0], {"seq": peers[1]}),
        send_to(down_low_here, down_got, left_sent.at[1], left_came.at[1], {"seq": peers[0]}),
    ]

    greet([{"seq": peer} for peer in peers] + [core_peer] + chip_peers[1:])
    end(load_left)
    go(left_copies)
    chip_out[0] = full_here[0].astype(BF16)
    go(to_chips(0))

    def go_on():
        end(left_copies)
        ups = up_here[...] + up_got[...].astype(F32)
        downs = down_here[...] + down_got[...].astype(F32)
        for place in range(4):
            full_here[1, place, 0] = ups[place * depth : (place + 1) * depth]
            full_here[1, place, 1] = downs[:, place * 128 : (place + 1) * 128]
        chip_out[1] = full_here[1].astype(BF16)
        go(to_chips(1))

    def to_peer(r, m):
        lanes = pl.ds(m * length, length)
        return send_block(
            heads_out.at[r, peers[m - 1]], view_ref.at[r, :, lanes], sent, came, r * 3 + m - 1, {"seq": peers[m - 1]}
        )

    def to_self(r):
        return pltpu.make_async_copy(heads_out.at[r, seq], view_ref.at[r, :, pl.ds(0, length)], kept.at[r])

    def stores(r):
        return [
            pltpu.make_async_copy(middle_here.at[r], grad_middle_ref.at[r], store_sem.at[r, 0]),
            pltpu.make_async_copy(block_here.at[r], block_out.at[r], store_sem.at[r, 1]),
        ]

    def mods(r, first, count):
        seg_row = seg[r : r + 1, pl.ds(pl.multiple_of(seq * length, 128), length)]
        found = per_token(slot_col, seg_row, table[r, :, first * width : (first + count) * width])
        return [found[:, k * width : (k + 1) * width] for k in range(count)]

    for r in range(rows):
        (gate_a,), (scale_b,) = mods(r, 2, 1), mods(r, 4, 1)
        end(loads(r))
        normal, inverse = normalize(rows_here[r, 2])
        normal_here[r] = normal
        grad_normed = rows_here[r, 1]
        grad_middle = cotangent_here[r].astype(F32) + normalize_back(normal, inverse, grad_normed * (1.0 + scale_b))
        middle_here[r] = grad_middle
        stores(r)[0].start()
        grad_branch = (grad_middle * gate_a).astype(BF16)
        grad_here[r] = grad_branch
        if r == 0:
            load_weight.wait()
        grad_heads = lax.dot_general(weight_here[...], grad_branch, (((1,), (1,)), ((), ())), preferred_element_type=F32)
        for owner in range(4):
            heads_out[r, owner] = grad_heads[owner * own : (owner + 1) * own].astype(BF16)
        to_self(r).start()
        for m in range(1, 4):
            to_peer(r, m).start()
        if r == 0:
            go_on()

    load_attended.wait()
    for r in range(rows):
        part = jnp.dot(attended_here[r], grad_here[r], preferred_element_type=F32)
        sums = jnp.sum(grad_here[r].astype(F32), axis=0, keepdims=True)
        if r == 0:
            total[...] = part
            bias_sum[...] = sums
        else:
            total[...] += part
            bias_sum[...] += sums
    to_core = send_to(core_out, core_got, core_sent, core_came, core_peer)
    for place in range(4):
        other = pl.multiple_of((2 * place + 1 - core) * depth, 8)
        core_out[place] = total[pl.ds(other, depth), :].astype(BF16)
    to_core.start()

    bias_line = bias[...].astype(F32).reshape(1, width)
    for r in range(rows):
        (gate_b,) = mods(r, 5, 1)
        branch_b = rows_here[r, 0] + bias_line
        block_here[r] = (rows_here[r, 2] + gate_b * branch_b).astype(BF16)
        stores(r)[1].start()
        grad_normed = rows_here[r, 1]
        seg_row = seg[r : r + 1, pl.ds(pl.multiple_of(seq * length, 128), length)]
        pieces = (
            middle_here[r] * rows_here[r, 3],
            grad_normed,
            grad_normed * normal_here[r],
            cotangent_here[r].astype(F32) * branch_b,
        )
        for k, piece in enumerate(pieces):
            slot_sums[r, :, k * width : (k + 1) * width] = per_slot(slot_col, seg_row, piece)

    to_core.wait()
    for place in range(4):
        mine = pl.multiple_of((2 * place + core) * depth, 8)
        proj_low[place] = (total[pl.ds(mine, depth), :] + core_got[place].astype(F32)).astype(BF16)
    mine = pl.multiple_of(row * depth, 8)
    proj_own[...] = total[pl.ds(mine, depth), :] + core_got[chip].astype(F32)
    for tile in range(2):
        end(to_chips(tile))
        for kind, target in enumerate((up_tail, down_tail)):
            value = full_here[tile, chip, kind]
            for k in range(3):
                value = value + chip_got[tile, k, kind].astype(F32)
            target[:, tile * 128 : (tile + 1) * 128] = value
    for r in range(rows):
        end(stores(r))
        to_self(r).wait()
        for m in range(1, 4):
            to_peer(r, m).wait()


def after_feed_forward(seg, table, attended, weight, bias, out_sum, grad_sum, middle, branch, cotangent, left):
    rows, length, width = cotangent.shape
    slots = table.shape[1]
    depth = width // 8
    shape = jax.ShapeDtypeStruct
    vmem = lambda dtype, *dims: pltpu.VMEM(dims, dtype)
    near, far = pl.BlockSpec(memory_space=pltpu.VMEM), pl.BlockSpec(memory_space=pl.ANY)
    dma = lambda *dims: pltpu.SemaphoreType.DMA(dims)
    return pl.pallas_call(
        after_kernel,
        in_specs=[near] * 3 + [far] * 12,
        out_specs=[far] * 3 + [near] * 6,
        out_shape=[
            shape((rows, length, width), BF16),
            shape((rows, length, width), F32),
            shape((rows, width // 4, 4 * length), BF16),
            shape((rows, slots, 4 * width), F32),
            shape((1, width), F32),
            shape((depth, width), F32),
            shape((4, depth, width), BF16),
            shape((depth, 256), F32),
            shape((depth, 256), F32),
        ],
        scratch_shapes=[
            vmem(BF16, rows, width, length),
            vmem(BF16, width, width),
            vmem(F32, rows, 4, length, width),
            vmem(BF16, rows, length, width),
            vmem(BF16, rows, length, width),
            vmem(F32, rows, length, width),
            vmem(F32, rows, length, width),
            vmem(BF16, rows, length, width),
            vmem(BF16, rows, 4, width // 4, length),
            vmem(F32, width, width),
            vmem(BF16, 4, depth, width),
            vmem(BF16, 4, depth, width),
            dma(rows, 5),
            dma(2),
            dma(rows, 2),
            dma(3 * rows),
            dma(3 * rows),
            dma(rows),
            pltpu.SemaphoreType.DMA,
            pltpu.SemaphoreType.DMA,
            vmem(F32, 2, 4, 2, depth, 128),
            vmem(F32, 4 * depth, 128),
            vmem(BF16, 4 * depth, 128),
            vmem(F32, depth, 512),
            vmem(BF16, depth, 512),
            vmem(BF16, 4 * depth, 128),
            vmem(BF16, depth, 512),
            vmem(BF16, 2, 4, 2, depth, 128),
            vmem(BF16, 2, 3, 2, depth, 128),
            dma(5),
            dma(8),
            dma(8),
        ],
        compiler_params=pltpu.CompilerParams(vmem_limit_bytes=VMEM_LIMIT, collective_id=4, has_side_effects=True),
        cost_estimate=pl.CostEstimate(flops=8 * 10**9, bytes_accessed=3 * 10**7, transcendentals=0),
    )(seg, table, bias, attended, weight, out_sum, grad_sum, middle, branch, cotangent, *left)


def qkv_weight_kernel(grad, normed, keep_ref, send_ref, sum_ref, total, turned):
    step = pl.program_id(0)
    chips, depth = lax.axis_size("rows") // 2, total.shape[1] // lax.axis_size("rows")
    mine = lax.rem(lax.axis_index("rows"), 2)
    part = jnp.dot(grad[0], normed[0], preferred_element_type=F32)
    sums = jnp.sum(grad[0].astype(F32), axis=1, keepdims=True)

    @pl.when(step == 0)
    def _():
        total[...] = part
        sum_ref[...] = sums

    @pl.when(step > 0)
    def _():
        total[...] += part
        sum_ref[...] += sums

    @pl.when(step == pl.num_programs(0) - 1)
    def _():
        turned[...] = total[...].T
        for chip in range(chips):
            first = pl.multiple_of((2 * chip + mine) * depth, 8)
            other = pl.multiple_of((2 * chip + 1 - mine) * depth, 8)
            keep_ref[chip] = turned[pl.ds(first, depth), :]
            send_ref[chip] = turned[pl.ds(other, depth), :].astype(BF16)


def qkv_weight_grad(grad, normed):
    rows, features, length = grad.shape
    width = normed.shape[2]
    groups = lax.axis_size("rows")
    shape = (groups // 2, width // groups, features)
    return pl.pallas_call(
        qkv_weight_kernel,
        grid=(rows,),
        in_specs=[
            pl.BlockSpec((1, features, length), lambda r: (r, 0, 0)),
            pl.BlockSpec((1, length, width), lambda r: (r, 0, 0)),
        ],
        out_specs=[
            pl.BlockSpec(shape, lambda r: (0, 0, 0)),
            pl.BlockSpec(shape, lambda r: (0, 0, 0)),
            pl.BlockSpec((features, 1), lambda r: (0, 0)),
        ],
        out_shape=[
            jax.ShapeDtypeStruct(shape, F32),
            jax.ShapeDtypeStruct(shape, BF16),
            jax.ShapeDtypeStruct((features, 1), F32),
        ],
        scratch_shapes=[pltpu.VMEM((features, width), F32), pltpu.VMEM((width, features), F32)],
        compiler_params=pltpu.CompilerParams(vmem_limit_bytes=VMEM_LIMIT),
        cost_estimate=pl.CostEstimate(
            flops=2 * rows * length * width * features,
            bytes_accessed=2 * rows * length * (width + features) + 6 * width * features // 2,
            transcendentals=0,
        ),
    )(grad, normed)


def tail_kernel(
    images,
    mod,
    weight,
    cond,
    ada_ref,
    cond_ref,
    bias_ref,
    got,
    low_mine,
    low_got,
    row_mine,
    row_got,
    cond_mine,
    cond_got,
    column_got,
    sent,
    arrived,
):
    seq_count, row_total = lax.axis_size("seq"), lax.axis_size("rows")
    seq, row = lax.axis_index("seq"), lax.axis_index("rows")
    to_seq = [lax.rem(seq + m, seq_count) for m in range(seq_count)]
    to_row = [lax.rem(row + m, row_total) for m in range(row_total)]
    barrier = pltpu.get_barrier_semaphore()
    for m in range(1, seq_count):
        pl.semaphore_signal(barrier, inc=1, device_id={"seq": to_seq[m]}, device_id_type=pl.DeviceIdType.MESH)
    for m in range(1, row_total):
        pl.semaphore_signal(barrier, inc=1, device_id={"rows": to_row[m]}, device_id_type=pl.DeviceIdType.MESH)
    pl.semaphore_wait(barrier, seq_count + row_total - 2)

    used = [0]

    def start(source, target, device):
        copy = pltpu.make_async_remote_copy(
            src_ref=source,
            dst_ref=target,
            send_sem=sent.at[used[0]],
            recv_sem=arrived.at[used[0]],
            device_id=device,
            device_id_type=pl.DeviceIdType.MESH,
        )
        used[0] += 1
        copy.start()
        return copy

    copies = [start(mod.at[to_seq[m]], got.at[m], {"seq": to_seq[m]}) for m in range(1, seq_count)]
    column_got[0] = cond[row]
    column_copies = [start(cond.at[to_row[m]], column_got.at[m], {"rows": to_row[m]}) for m in range(1, row_total)]
    total = mod[seq]
    for m, copy in enumerate(copies):
        copy.wait()
        total = total + got[m + 1]
    low = total[:images].astype(BF16)
    low_mine[...] = low
    row_mine[...] = total[images:]
    row_mine[0:1] = jnp.sum(total[:images], axis=0, keepdims=True)
    low_got[0] = low
    copies = [start(low_mine, low_got.at[m], {"rows": to_row[m]}) for m in range(1, row_total)]
    copies += [start(row_mine, row_got.at[m], {"rows": to_row[m]}) for m in range(1, row_total)]
    term = lax.dot_general(low, weight[...], (((1,), (1,)), ((), ())), preferred_element_type=F32)
    cond_mine[...] = term
    cond_copies = [start(cond_mine, cond_got.at[m], {"seq": to_seq[m]}) for m in range(1, seq_count)]
    for copy in copies:
        copy.wait()
    sums = row_mine[...]
    for m in range(1, row_total):
        sums = sums + row_got[m]
    bias_ref[seq] = sums
    copies = [start(bias_ref.at[seq], bias_ref.at[seq], {"seq": to_seq[m]}) for m in range(1, seq_count)]
    for copy in column_copies:
        copy.wait()
    gathered = jnp.concatenate([low_got[m] for m in range(row_total)], axis=0)
    columns = jnp.concatenate([column_got[m] for m in range(row_total)], axis=0)
    ada_ref[...] = lax.dot_general(columns, gathered, (((0,), (0,)), ((), ())), preferred_element_type=F32)
    for m, copy in enumerate(cond_copies):
        copy.wait()
        term = term + cond_got[m + 1]
    cond_ref[...] = term
    for copy in copies:
        copy.wait()


def finish(mod, weight, cond, images):
    seq_count, lines, columns = mod.shape
    width, depth = weight.shape[0], cond.shape[2]
    row_total = lax.axis_size("rows")
    extra = lines - images
    copies = 3 * (seq_count - 1) + 3 * (row_total - 1)
    return pl.pallas_call(
        partial(tail_kernel, images),
        in_specs=[pl.BlockSpec(memory_space=pltpu.VMEM)] * 3,
        out_specs=[pl.BlockSpec(memory_space=pltpu.VMEM)] * 3,
        out_shape=[
            jax.ShapeDtypeStruct((depth, columns), F32),
            jax.ShapeDtypeStruct((images, width), F32),
            jax.ShapeDtypeStruct((seq_count, extra, columns), F32),
        ],
        scratch_shapes=[
            pltpu.VMEM((seq_count, lines, columns), F32),
            pltpu.VMEM((images, columns), BF16),
            pltpu.VMEM((row_total, images, columns), BF16),
            pltpu.VMEM((extra, columns), F32),
            pltpu.VMEM((row_total, extra, columns), F32),
            pltpu.VMEM((images, width), F32),
            pltpu.VMEM((seq_count, images, width), F32),
            pltpu.VMEM((row_total, images, depth), BF16),
            pltpu.SemaphoreType.DMA((copies,)),
            pltpu.SemaphoreType.DMA((copies,)),
        ],
        compiler_params=pltpu.CompilerParams(collective_id=0, has_side_effects=True, vmem_limit_bytes=VMEM_LIMIT),
        cost_estimate=pl.CostEstimate(flops=10**9, bytes_accessed=10**7, transcendentals=0),
    )(mod, weight, cond)


def send_to(source, target, sent, came, device):
    return pltpu.make_async_remote_copy(
        src_ref=source,
        dst_ref=target,
        send_sem=sent,
        recv_sem=came,
        device_id=device,
        device_id_type=pl.DeviceIdType.MESH,
    )


def back_kernel(
    block,
    inner,
    scale,
    code_col,
    code_row,
    query,
    key,
    value,
    out,
    grad_out,
    lse,
    normed,
    proj_own,
    proj_low,
    down,
    down_tail,
    seg,
    table,
    slot_sums,
    image_index,
    conditioning,
    proj_bias,
    up_bias,
    down_bias,
    tokens,
    grad_middle,
    weight,
    ada,
    grad_tokens,
    proj_ref,
    down_ref,
    ada_ref,
    cond_ref,
    ada_bias_ref,
    qv_bias_ref,
    proj_bias_ref,
    up_bias_ref,
    down_bias_ref,
    qkv_ref,
    grads,
    token_got,
    key_sum,
    value_sum,
    keys,
    values,
    total,
    spare,
    core_out,
    core_got,
    proj_got,
    seq_out,
    seq_got,
    down_out,
    down_got,
    qkv_own,
    chip_got,
    weights,
    tokens_here,
    middle_here,
    grad_here,
    features,
    image_sums,
    feature_sums,
    mod,
    got,
    lines,
    lines_got,
    low_all,
    small_core,
    small_chip,
    small_seq,
    cond_all,
    cond,
    column_got,
    piece_out,
    piece_got,
    sent,
    came,
    kept,
    load_sem,
    store_sem,
    other_sent,
    other_came,
    normed_here,
):
    length, size = query.shape[-1], query.shape[-2]
    row, head = pl.program_id(0), pl.program_id(1)
    rows, _, heads = grads.shape[:3]
    width = normed.shape[-1]
    images, columns = mod.shape[1:]
    depth, own, local = width // 8, width // 4, length // 4
    seq, group = lax.axis_index("seq"), lax.axis_index("rows")
    chip, core = lax.div(group, 2), lax.rem(group, 2)
    seq_places = peers_of(seq)
    peers = [{"seq": place} for place in seq_places]
    row_places = [lax.rem(group + m, 8) for m in range(8)]
    row_peers = [{"rows": place} for place in row_places]
    core_peer = {"rows": group + 1 - 2 * core}
    to_chip = [lax.rem(chip + k, 4) for k in range(4)]
    from_chip = [lax.rem(chip + 4 - k, 4) for k in range(4)]
    chip_peers = [{"rows": 2 * to_chip[k] + core} for k in range(4)]
    first = (row == 0) & (head == 0)
    last = (row == rows - 1) & (head == heads - 1)
    slot_col = slot_column(table.shape[1])
    used = [0]

    def copy_to(source, target, device):
        used[0] += 1
        return send_to(source, target, other_sent.at[used[0] - 1], other_came.at[used[0] - 1], device)

    def go(copies):
        for copy in copies:
            copy.start()

    def end(copies):
        for copy in copies:
            copy.wait()

    def to_peer(r, h, m):
        place = (r * heads + h) * 3 + m - 1
        source = grads.at[r, :, h, :, pl.ds(m * local, local)]
        return send_to(source, token_got.at[r, :, seq, h], sent.at[place], came.at[place], peers[m - 1])

    def to_self(r, h):
        source = grads.at[r, :, h, :, pl.ds(0, local)]
        return pltpu.make_async_copy(source, token_got.at[r, :, seq, h], kept.at[r * heads + h])

    proj_copies = [copy_to(proj_low.at[to_chip[k]], proj_got.at[k - 1], chip_peers[k]) for k in range(1, 4)]
    seq_copies = [copy_to(seq_out.at[place], seq_got.at[m], peers[m]) for m, place in enumerate(seq_places)]
    core_copy = copy_to(core_out, core_got, core_peer)
    down_copy = copy_to(down_out.at[1 - core], down_got, core_peer)
    chip_copies = [copy_to(core_out.at[to_chip[k]], chip_got.at[k - 1], chip_peers[k]) for k in range(1, 4)]
    column_copies = [copy_to(cond.at[row_places[m]], column_got.at[group], row_peers[m]) for m in range(1, 8)]
    mod_copies = [copy_to(mod.at[place], got.at[m], peers[m]) for m, place in enumerate(seq_places)]
    line_copies = [copy_to(lines.at[place], lines_got.at[m], peers[m]) for m, place in enumerate(seq_places)]
    low_core = copy_to(low_all.at[chip, core], low_all.at[chip, core], core_peer)
    low_chips = [copy_to(low_all.at[chip, core], low_all.at[chip, core], chip_peers[k]) for k in range(1, 4)]
    low_on = [copy_to(low_all.at[from_chip[k], core], low_all.at[from_chip[k], core], core_peer) for k in range(1, 4)]
    small_over = copy_to(small_core.at[core], small_core.at[core], core_peer)
    small_chips = [copy_to(small_chip.at[chip], small_chip.at[chip], chip_peers[k]) for k in range(1, 4)]
    small_copies = [copy_to(small_seq.at[seq], small_seq.at[seq], peers[m]) for m in range(3)]
    cond_copies = [copy_to(cond_all.at[seq], cond_all.at[seq], peers[m]) for m in range(3)]
    base = used[0]

    load_weights = [
        pltpu.make_async_copy(weight.at[:, pl.ds(part * width, width)], weights.at[part], load_sem.at[part])
        for part in range(3)
    ]
    load_normed = lambda r: pltpu.make_async_copy(normed.at[r], normed_here, load_sem.at[7])
    load_tokens = pltpu.make_async_copy(tokens, tokens_here, load_sem.at[3])
    load_middle = pltpu.make_async_copy(grad_middle, middle_here, load_sem.at[4])
    load_ada = [
        pltpu.make_async_copy(ada.at[pl.ds(0, width)], weights.at[0], load_sem.at[5]),
        pltpu.make_async_copy(ada.at[pl.ds(width, columns - width)], weights.at[1, pl.ds(0, columns - width)], load_sem.at[6]),
    ]

    @pl.when(first)
    def _():
        call(peers + row_peers[1:])
        go(load_weights + [load_tokens, load_middle, load_normed(0)])

    keys[...] = key[0, 0].astype(F32).T.astype(BF16)
    values[...] = value[0, 0].astype(F32).T.astype(BF16)

    def place_of(part):
        return pl.ds(pl.multiple_of((part * heads + head) * size, 8), size)

    for step in range(length // block):
        here = pl.ds(step * block, block)
        query_low = query[0, 0, :, here]
        grad_low = grad_out[0, 0, :, here]
        query_rows = query_low.astype(F32).T.astype(BF16)
        grad_rows = grad_low.astype(F32).T.astype(BF16)
        row_dot = jnp.sum(grad_low.astype(F32) * out[0, 0, :, here].astype(F32), axis=0, keepdims=True)
        grad_query = jnp.zeros((size, block), F32)
        for part in range(length // inner):
            there = pl.ds(part * inner, inner)
            scores = jnp.dot(keys[there, :], query_low, preferred_element_type=F32)
            scores = jnp.where(code_col[0, there, :] == code_row[0, :, here], scores * (scale * LOG2E), -1e30)
            probs = jnp.exp2(scores - lse[0, 0, :, here])
            grad_probs = jnp.dot(values[there, :], grad_low, preferred_element_type=F32)
            grad_raw = (probs * (grad_probs - row_dot) * scale).astype(BF16)
            value_part = jnp.dot(probs.astype(BF16), grad_rows, preferred_element_type=F32)
            key_part = jnp.dot(grad_raw, query_rows, preferred_element_type=F32)
            if step == 0:
                value_sum[there, :] = value_part
                key_sum[there, :] = key_part
            else:
                value_sum[there, :] += value_part
                key_sum[there, :] += key_part
            grad_query += jnp.dot(key[0, 0, :, there], grad_raw, preferred_element_type=F32)
        low = grad_query.astype(BF16)
        grads[row, 0, head, :, here] = low
        spare[place_of(0), here] = low.astype(F32)
    for part, sums in ((1, key_sum), (2, value_sum)):
        low = sums[...].T.astype(BF16)
        grads[row, part, head] = low
        spare[place_of(part), :] = low.astype(F32)

    @pl.when(first)
    def _():
        meet(peers + row_peers[1:])
        go(proj_copies)
        half = down_out.shape[2]
        down_out[0] = down[:, :half]
        down_out[1] = jnp.concatenate([down[:, half:], down_tail[...]], axis=1)
        down_copy.start()
        value = conditioning[...].astype(F32)
        low = (value / (1.0 + jnp.exp(-value))).astype(BF16)
        for place in range(8):
            cond[place] = low[:, place * depth : (place + 1) * depth]
        column_got[group] = cond[group]
        go(column_copies)
        image_sums[...] = jnp.zeros_like(image_sums)
        feature_sums[...] = jnp.zeros_like(feature_sums)

    to_self(row, head).start()
    for m in range(1, 4):
        to_peer(row, head, m).start()

    own_features = 3 * own

    @pl.when((head == heads - 1) & (row == 0))
    def _():
        load_normed(0).wait()
        total[...] = jnp.dot(spare[:own_features].astype(BF16), normed_here[...], preferred_element_type=F32)
        load_normed(1).start()

    @pl.when((head == heads - 1) & (row > 0))
    def _():
        load_normed(1).wait()
        total[...] += jnp.dot(spare[:own_features].astype(BF16), normed_here[...], preferred_element_type=F32)

    def store_tokens(r):
        return pltpu.make_async_copy(grad_here.at[r], grad_tokens.at[r], store_sem.at[r])

    def input_grad(r):
        for h in range(heads):
            to_self(r, h).wait()
            for m in range(1, 4):
                to_peer(r, h, m).wait()
        grad_normed = jnp.zeros((width, local), F32)
        for part in range(3):
            for place in range(4):
                for h in range(heads):
                    start = (place * heads + h) * size
                    features[start : start + size] = token_got[r, part, place, h].astype(F32)
            low = features[...].astype(BF16)
            grad_normed += jnp.dot(weights[part], low, preferred_element_type=F32)
            if part != 1:
                lanes = slice(part * width, (part + 1) * width)
                ones = jnp.ones((8, local), BF16)
                feature_sums[:, lanes] += lax.dot_general(ones, low, (((1,), (1,)), ((), ())), preferred_element_type=F32)
        grad_normed = grad_normed.T
        normal, inverse = normalize(tokens_here[r].astype(F32))
        seg_row = seg[r : r + 1, pl.ds(pl.multiple_of(seq * local, 128), local)]
        scale_a = per_token(slot_col, seg_row, table[r, :, width : 2 * width])
        grad_here[r] = middle_here[r] + normalize_back(normal, inverse, grad_normed * (1.0 + scale_a))
        store_tokens(r).start()
        late = [per_slot(slot_col, seg_row, piece) for piece in (grad_normed, grad_normed * normal)]
        slots = jnp.concatenate(late + [slot_sums[r]], axis=1)
        pick = lax.broadcasted_iota(jnp.int32, (images, slots.shape[0]), 0) == image_index[r : r + 1, :]
        picks = jnp.concatenate([pick.astype(BF16)] * 3, axis=1)
        image_sums[...] += jnp.dot(picks, jnp.concatenate(split_low(slots), axis=0), preferred_element_type=F32)

    @pl.when(last)
    def _():
        spare[:, :own_features] = total[...].T
        for place in range(4):
            other = pl.multiple_of((2 * place + 1 - core) * depth, 8)
            core_out[place] = spare[pl.ds(other, depth), :own_features].astype(BF16)
        core_copy.start()
        down_copy.wait()
        left, right = down_out[core], down_got[...]
        left, right = jnp.where(core == 0, left, right), jnp.where(core == 0, right, left)
        down_ref[:depth] = left
        down_ref[depth:] = right
        core_copy.wait()
        for place in range(4):
            same = pl.multiple_of((2 * place + core) * depth, 8)
            core_out[place] = (spare[pl.ds(same, depth), :own_features] + core_got[place].astype(F32)).astype(BF16)
        same = pl.multiple_of(group * depth, 8)
        qkv_own[...] = spare[pl.ds(same, depth), :own_features] + core_got[chip].astype(F32)
        go(chip_copies)
        end(proj_copies)
        mine = proj_own[...]
        for k in range(3):
            mine = mine + proj_got[k].astype(F32)
        for place in range(4):
            seq_out[place] = mine[:, place * own : (place + 1) * own].astype(BF16)
        go(seq_copies)
        for place in range(4):

            @pl.when(seq == place)
            def _():
                proj_ref[...] = mine[:, place * own : (place + 1) * own]

        end(load_weights + [load_tokens, load_middle])
        for r in range(rows):
            input_grad(r)
        go(load_ada)

        for place in range(4):
            mod[place] = image_sums[:, place * columns : (place + 1) * columns]
        for line in range(8):
            if line < 2:
                value = feature_sums[0:1, 2 * line * width : (2 * line + 1) * width]
            else:
                value = (proj_bias[...], *(up_bias[k] for k in range(4)), down_bias[...])[line - 2]
            lines[line // 2, line % 2 : line % 2 + 1] = value
        go(mod_copies + line_copies)
        for m, copy in enumerate(seq_copies):
            copy.wait()
            proj_ref[...] += seq_got[m].astype(F32)
        sums = mod[seq]
        for m, copy in enumerate(mod_copies):
            copy.wait()
            sums = sums + got[m]
        low = sums.astype(BF16)
        low_all[chip, core] = low
        go([low_core] + low_chips)
        small = lines[seq]
        for m, copy in enumerate(line_copies):
            copy.wait()
            small = small + lines_got[m]
        small_core[core] = jnp.zeros_like(small_core[core])
        small_core[core, 0:2, :width] = small
        small_core[core, 2:3] = jnp.sum(sums, axis=0, keepdims=True)
        small_over.start()
        end(load_ada)
        term = jnp.dot(low[:, :width], weights[0], preferred_element_type=F32)
        term += jnp.dot(low[:, width:], weights[1, : columns - width], preferred_element_type=F32)
        cond_all[seq] = term
        go(cond_copies)
        end(chip_copies + column_copies)
        mine = qkv_own[...]
        for k in range(3):
            mine = mine + chip_got[k].astype(F32)
        for part in range(3):
            piece_out[part] = mine[:, part * own : (part + 1) * own]

        def piece(part):
            index = part * 4 + seq
            target, place = lax.div(index, 3), lax.rem(index, 3)
            copy = send_to(
                piece_out.at[part], piece_got.at[place], other_sent.at[base + part], other_came.at[base + place], {"seq": target}
            )
            return copy, target, place

        def arriving(place):
            source = lax.rem(3 * seq + place, 4)
            copy = send_to(
                piece_out.at[0], piece_got.at[place], other_sent.at[base], other_came.at[base + place], {"seq": source}
            )
            return copy, source

        for part in range(3):
            copy, target, place = piece(part)

            @pl.when(target != seq)
            def _():
                copy.start()

            @pl.when(target == seq)
            def _():
                piece_got[place] = piece_out[part]

        small_over.wait()
        small_chip[chip] = small_core[0] + small_core[1]
        go(small_chips)
        for came_in, going_on in zip(low_chips, low_on):
            came_in.wait()
            going_on.start()
        end(small_chips)
        small_seq[seq] = (small_chip[0] + small_chip[1]) + (small_chip[2] + small_chip[3])
        go(small_copies)
        end([low_core] + low_on)
        gathered = jnp.concatenate([low_all[m // 2, m % 2] for m in range(8)], axis=0)
        blocks = jnp.concatenate([column_got[m] for m in range(8)], axis=0)
        ada_ref[...] = lax.dot_general(blocks, gathered, (((0,), (0,)), ((), ())), preferred_element_type=F32)
        for part in range(3):
            copy, target, place = piece(part)

            @pl.when(target != seq)
            def _():
                copy.wait_send()

        for place in range(3):
            copy, source = arriving(place)

            @pl.when(source != seq)
            def _():
                copy.wait_recv()

        for place in range(3):
            qkv_ref[:, place * own : (place + 1) * own] = piece_got[place]
        end(cond_copies)
        value = conditioning[...].astype(F32)
        gate = 1.0 / (1.0 + jnp.exp(-value))
        sums = (cond_all[0] + cond_all[1]) + (cond_all[2] + cond_all[3])
        cond_ref[...] = sums * gate * (1.0 + value * (1.0 - gate))
        end(small_copies)
        for place in range(4):
            ada_bias_ref[pl.ds(place * columns, columns)] = small_seq[place, 2]
        qv_bias_ref[...] = small_seq[0, 0:2, :width]
        proj_bias_ref[...] = small_seq[1, 0, :width]
        for line in range(3, 7):
            up_bias_ref[pl.ds((line - 3) * width, width)] = small_seq[line // 2, line % 2, :width]
        down_bias_ref[...] = small_seq[3, 1, :width]
        for r in range(rows):
            store_tokens(r).wait()


def attend_back_and_finish(packed, out, grad_out, lse, col, row, normed, *rest):
    proj_own, proj_low, down, down_tail, seg, table, slot_sums, image_index, conditioning, biases, tokens, grad_middle, weight, ada = rest
    rows, _, heads, size, length = packed.shape
    width = normed.shape[2]
    depth, own, features, local = width // 8, width // 4, 3 * heads * size, length // 4
    half = (down.shape[1] + down_tail.shape[1]) // 2
    images, columns = conditioning.shape[0], ada.shape[0]
    part = lambda j: pl.BlockSpec((1, None, 1, size, length), lambda r, h: (r, j, h, 0, 0))
    whole = pl.BlockSpec((1, 1, size, length), lambda r, h: (r, h, 0, 0))
    single = pl.Buffered(buffer_count=1)
    fixed = lambda *dims: pl.BlockSpec(dims, lambda r, h: (0,) * len(dims), pipeline_mode=single)
    result = lambda *dims: pl.BlockSpec(dims, lambda r, h: (0,) * len(dims))
    far = pl.BlockSpec(memory_space=pl.ANY)
    shape = jax.ShapeDtypeStruct
    vmem = lambda dtype, *dims: pltpu.VMEM(dims, dtype)
    count = rows * heads
    copies = 3 + 3 + 1 + 1 + 3 + 7 + 3 + 3 + 1 + 3 + 3 + 1 + 3 + 3 + 3 + 3
    dma = lambda n: pltpu.SemaphoreType.DMA((n,))
    return pl.pallas_call(
        partial(back_kernel, 256, 512, size**-0.5),
        grid=(rows, heads),
        in_specs=[
            pl.BlockSpec((1, length, 1), lambda r, h: (r, 0, 0)),
            pl.BlockSpec((1, 1, length), lambda r, h: (r, 0, 0)),
            part(0),
            part(1),
            part(2),
            whole,
            whole,
            pl.BlockSpec((1, 1, 1, length), lambda r, h: (r, h, 0, 0)),
            far,
            fixed(depth, width),
            fixed(4, depth, width),
            fixed(*down.shape),
            fixed(*down_tail.shape),
            fixed(*seg.shape),
            fixed(*table.shape),
            fixed(*slot_sums.shape),
            fixed(*image_index.shape),
            fixed(images, width),
            fixed(1, width),
            fixed(4, 1, width),
            fixed(1, width),
            far,
            far,
            far,
            far,
        ],
        out_specs=[
            far,
            result(depth, own),
            result(own, half),
            result(depth, columns),
            result(images, width),
            result(4 * columns),
            result(2, width),
            result(width),
            result(4 * width),
            result(width),
            result(depth, features),
        ],
        out_shape=[
            shape((rows, local, width), F32),
            shape((depth, own), F32),
            shape((own, half), F32),
            shape((depth, columns), F32),
            shape((images, width), F32),
            shape((4 * columns,), F32),
            shape((2, width), F32),
            shape((width,), F32),
            shape((4 * width,), F32),
            shape((width,), F32),
            shape((depth, features), F32),
        ],
        scratch_shapes=[
            vmem(BF16, rows, 3, heads, size, length),
            vmem(BF16, rows, 3, 4, heads, size, local),
            vmem(F32, length, size),
            vmem(F32, length, size),
            vmem(BF16, length, size),
            vmem(BF16, length, size),
            vmem(F32, features, width),
            vmem(F32, width, length),
            vmem(BF16, 4, depth, features),
            vmem(BF16, 4, depth, features),
            vmem(BF16, 3, depth, width),
            vmem(BF16, 4, depth, own),
            vmem(BF16, 3, depth, own),
            vmem(F32, 2, depth, half),
            vmem(F32, depth, half),
            vmem(F32, depth, features),
            vmem(BF16, 3, depth, features),
            vmem(BF16, 3, width, width),
            vmem(BF16, rows, local, width),
            vmem(F32, rows, local, width),
            vmem(F32, rows, local, width),
            vmem(F32, width, local),
            vmem(F32, images, 6 * width),
            vmem(F32, 8, 3 * width),
            vmem(F32, 4, images, columns),
            vmem(F32, 3, images, columns),
            vmem(F32, 4, 2, width),
            vmem(F32, 3, 2, width),
            vmem(BF16, 4, 2, images, columns),
            vmem(F32, 2, 4, columns),
            vmem(F32, 4, 4, columns),
            vmem(F32, 4, 4, columns),
            vmem(F32, 4, images, width),
            vmem(BF16, 8, images, depth),
            vmem(BF16, 8, images, depth),
            vmem(F32, 3, depth, own),
            vmem(F32, 3, depth, own),
            dma(3 * count),
            dma(3 * count),
            dma(count),
            dma(8),
            dma(rows),
            dma(copies),
            dma(copies),
            vmem(BF16, length, width),
        ],
        compiler_params=pltpu.CompilerParams(vmem_limit_bytes=VMEM_LIMIT, collective_id=3, has_side_effects=True),
        cost_estimate=pl.CostEstimate(
            flops=20 * rows * heads * length * length * 128,
            bytes_accessed=16 * rows * heads * length * size,
            transcendentals=rows * heads * length * length,
        ),
    )(
        col,
        row,
        packed,
        packed,
        packed,
        out,
        grad_out,
        lse,
        normed,
        proj_own,
        proj_low,
        down,
        down_tail,
        seg,
        table,
        slot_sums,
        image_index,
        conditioning,
        *biases,
        tokens,
        grad_middle,
        weight,
        ada,
    )


def forward_kernel(
    block,
    image_index,
    seg,
    fill,
    conditioning,
    ada_bias,
    qv_bias,
    proj_bias,
    tokens,
    ada,
    weight,
    proj,
    cotangent,
    normed_ref,
    packed_ref,
    attended_ref,
    features_ref,
    branch_ref,
    middle_ref,
    inner_ref,
    grad_ref,
    inner_turned_ref,
    grad_turned_ref,
    table_ref,
    code_row,
    code_col,
    lse_ref,
    bias_sum,
    here,
    normed_all,
    packed_all,
    ada_here,
    windows,
    turned,
    own_weight,
    bias_turned,
    mod_all,
    table,
    seg_all,
    attended_all,
    attended_got,
    flat,
    features_all,
    proj_here,
    cotangent_here,
    branch_all,
    middle_all,
    inner_all,
    grad_all,
    inner_turned,
    grad_turned,
    rows_turned,
    load_sem,
    own_sem,
    mod_sent,
    mod_came,
    sent,
    came,
    forward_sent,
    forward_came,
    heads_sent,
    heads_came,
    heads_kept,
    store_sem,
    last_sem,
):
    rows, _, local, width = here.shape
    _, parts, heads, size, length = packed_all.shape
    own, depth, half = heads * size, width // 8, local // 2
    columns = ada_here.shape[0]
    images, slots = conditioning.shape[0], image_index.shape[1]
    slot_col = slot_column(slots)
    scale = size**-0.5 * LOG2E
    seq = lax.axis_index("seq")
    core = lax.rem(lax.axis_index("rows"), 2)
    places = [seq] + peers_of(seq)
    peers = [{"seq": place} for place in places]


    def direct(r, m):
        index = r * 2 + m - 1
        return send_to(tokens.at[r], here.at[r, m], sent.at[index], came.at[index], peers[m])

    def forward(r, m):
        part = pl.ds(0, half) if m == 1 else pl.ds(half, half)
        index = r * 2 + m - 1
        return send_to(
            here.at[r, 3 - m, part], here.at[r, 3, part], forward_sent.at[index], forward_came.at[index], peers[m]
        )

    def go(copies):
        for copy in copies:
            copy.start()

    def end(copies):
        for copy in copies:
            copy.wait()

    own_copies = [pltpu.make_async_copy(tokens.at[r], here.at[r, 0], own_sem.at[r]) for r in range(rows)]
    load_ada = pltpu.make_async_copy(ada, ada_here, load_sem.at[0])
    load_windows = []
    for part in range(3):
        lanes = pl.ds(pl.multiple_of(part * width + seq * 256, 128), 384)
        load_windows.append(pltpu.make_async_copy(weight.at[:, lanes], windows.at[part], load_sem.at[1 + part]))
    load_proj = pltpu.make_async_copy(proj, proj_here, load_sem.at[4])
    load_cotangent = pltpu.make_async_copy(cotangent, cotangent_here, load_sem.at[5])
    go([load_ada] + load_windows + own_copies + [load_proj, load_cotangent])
    greet(peers[1:])
    go([direct(0, m) for m in (1, 2)])

    value = conditioning[...].astype(F32)
    low = (value / (1.0 + jnp.exp(-value))).astype(BF16)
    load_ada.wait()
    mod_all[seq] = lax.dot_general(low, ada_here[...], (((1,), (1,)), ((), ())), preferred_element_type=F32)
    mod_copies = [
        send_to(mod_all.at[seq], mod_all.at[seq], mod_sent.at[m - 1], mod_came.at[m - 1], peers[m]) for m in range(1, 4)
    ]
    go(mod_copies)

    for m in range(4):
        lanes = pl.ds(pl.multiple_of(places[m] * local, 128), local)
        found = seg[:, lanes]
        where = places[m] * local + lax.broadcasted_iota(jnp.int32, (1, local), 1)
        for r in range(rows):
            code = jnp.where(where < fill[r], found[r : r + 1], -1 - where)
            seg_all[r, m] = found[r : r + 1]
            code_row[r, :, m * local : (m + 1) * local] = code
            column = jnp.broadcast_to(code.astype(F32), (128, local)).T[:, :1]
            code_col[r, m * local : (m + 1) * local] = column.astype(jnp.int32)

    for part in range(3):
        load_windows[part].wait()
        turned[...] = windows[part].astype(F32).T
        own_weight[part * own : (part + 1) * own] = turned[pl.ds(pl.multiple_of(seq * 32, 8), own), :].astype(BF16)
    window = qv_bias[:, pl.ds(pl.multiple_of(seq * 256, 128), 384)].astype(F32)
    bias_turned[...] = jnp.concatenate([window, jnp.zeros((6, 384), F32)], axis=0).T
    bias = bias_turned[pl.ds(pl.multiple_of(seq * 32, 8), own), :]
    bias = jnp.concatenate([bias[:, 0:1], jnp.zeros((own, 1), F32), bias[:, 1:2]], axis=0)

    end([direct(0, m) for m in (1, 2)])
    go([forward(0, m) for m in (1, 2)] + [direct(1, m) for m in (1, 2)])

    end(mod_copies)
    bias_all = ada_bias[...].astype(F32).reshape(1, 4 * columns)
    proj_line = proj_bias[...].astype(F32).reshape(1, width)
    for place in range(4):
        lanes = slice(place * columns, (place + 1) * columns)
        table[:, lanes] = mod_all[place] + bias_all[:, lanes]
    stacked = jnp.concatenate(split_low(table[...]), axis=0)
    image_col = lax.rem(lax.broadcasted_iota(jnp.int32, (3 * images, slots), 0), images)
    for r in range(rows):
        picked = (image_col == image_index[r : r + 1]).astype(BF16)
        table_ref[r] = lax.dot_general(picked, stacked, (((0,), (0,)), ((), ())), preferred_element_type=F32)

    def stores(r, m):
        index = r * 4 + m
        lanes = pl.ds(m * local, local)
        return (
            pltpu.make_async_copy(normed_all.at[r, m], normed_ref.at[r, m], store_sem.at[0, index]),
            pltpu.make_async_copy(packed_all.at[r, :, :, :, lanes], packed_ref.at[r, :, :, :, lanes], store_sem.at[1, index]),
        )

    def work(r, m):
        mods = per_token(slot_col, seg_all[r, m], table_ref[r, :, : 2 * width])
        normal, _ = normalize(here[r, m].astype(F32))
        normed = (normal * (1.0 + mods[:, width:]) + mods[:, :width]).astype(BF16)
        normed_all[r, m] = normed
        mixed = lax.dot_general(own_weight[...], normed, (((1,), (1,)), ((), ())), preferred_element_type=F32)
        mixed = (mixed + bias).astype(BF16)
        for part in range(parts):
            for head in range(heads):
                start = (part * heads + head) * size
                packed_all[r, part, head, :, m * local : (m + 1) * local] = mixed[start : start + size]
        go(stores(r, m))

    def to_peer(r, h, m):
        source = attended_all.at[r, h, :, pl.ds(m * local, local)]
        place = (r * heads + h) * 3 + m - 1
        return send_to(source, attended_got.at[r, seq, h], heads_sent.at[place], heads_came.at[place], peers[m])

    def to_self(r, h):
        source = attended_all.at[r, h, :, pl.ds(0, local)]
        return pltpu.make_async_copy(source, attended_got.at[r, seq, h], heads_kept.at[r * heads + h])

    def attend_head(r, h):
        keys = packed_all[r, 1, h].astype(F32).T.astype(BF16)
        values = packed_all[r, 2, h]
        codes = code_col[r]
        for step in range(length // block):
            lanes = pl.ds(step * block, block)
            scores = jnp.dot(keys, packed_all[r, 0, h, :, lanes], preferred_element_type=F32)
            scores = jnp.where(codes == code_row[r, :, lanes], scores * scale, -1e30)
            peak = jnp.max(scores, axis=0, keepdims=True)
            raised = jnp.exp2(scores - peak)
            total = jnp.sum(raised, axis=0, keepdims=True)
            probs = (raised * (1.0 / total)).astype(BF16)
            attended_all[r, h, :, lanes] = jnp.dot(values, probs, preferred_element_type=F32).astype(BF16)
            lse_ref[r, h, :, lanes] = peak + jnp.log2(total)

    def send_head(r, h):
        to_self(r, h).start()
        for m in range(1, 4):
            to_peer(r, h, m).start()

    def attend_row(r, first, last):
        @pl.loop(first, last)
        def _(h):
            attend_head(r, h)
            if r > 0:
                send_head(r, h)

    def last_stores(r):
        lines, lanes = pl.ds(r * local, local), pl.ds(r * local, local)
        pairs = (
            (grad_all.at[r], grad_ref.at[lines]),
            (grad_turned.at[r], grad_turned_ref.at[:, lanes]),
            (attended_all.at[r], attended_ref.at[r]),
            (features_all.at[r], features_ref.at[r]),
            (branch_all.at[r], branch_ref.at[r]),
            (middle_all.at[r], middle_ref.at[r]),
            (inner_all.at[r], inner_ref.at[lines]),
            (inner_turned.at[r], inner_turned_ref.at[:, lanes]),
        )
        return [pltpu.make_async_copy(source, target, last_sem.at[r, k]) for k, (source, target) in enumerate(pairs)]

    def turn(values, target, r):
        rows_turned[...] = values.T
        for place in range(4):
            for order in range(2):
                first = pl.multiple_of((2 * place + (core if order == 0 else 1 - core)) * depth, 8)
                start = (4 * order + place) * depth
                target[r, start : start + depth] = rows_turned[pl.ds(first, depth), :].astype(BF16)

    end(own_copies)
    for m in range(3):
        work(0, m)
    end([load_proj, load_cotangent])
    for r in range(rows):
        gate_b = per_token(slot_col, seg_all[r, 0], table_ref[r, :, 5 * width :])
        grad = cotangent_here[r].astype(F32) * gate_b
        grad_all[r] = grad.astype(BF16)
        turn(grad, grad_turned, r)
        sums = jnp.sum(grad.astype(BF16).astype(F32), axis=0, keepdims=True)
        if r == 0:
            bias_sum[...] = sums
        else:
            bias_sum[...] += sums
        go(last_stores(r)[:2])
    def project(r):
        for h in range(heads):
            to_self(r, h).wait()
            for m in range(1, 4):
                to_peer(r, h, m).wait()
        for place in range(4):
            for h in range(heads):
                start = (place * heads + h) * size
                flat[start : start + size] = attended_got[r, place, h].astype(F32)
        features = flat[...].astype(BF16)
        features_all[r] = features
        go(last_stores(r)[2:4])
        mods = per_token(slot_col, seg_all[r, 0], table_ref[r, :, 2 * width : 5 * width])
        gate_a, shift_b, scale_b = (mods[:, k * width : (k + 1) * width] for k in range(3))
        branch = lax.dot_general(features, proj_here[...], (((0,), (0,)), ((), ())), preferred_element_type=F32) + proj_line
        middle = here[r, 0].astype(F32) + gate_a * branch
        branch_all[r] = branch
        middle_all[r] = middle
        go(last_stores(r)[4:6])
        normed = normalize(middle)[0] * (1.0 + scale_b) + shift_b
        inner_all[r] = normed.astype(BF16)
        turn(normed, inner_turned, r)
        go(last_stores(r)[6:])
    end([forward(0, m) for m in (1, 2)])
    work(0, 3)
    attend_row(0, 0, heads // 2)
    end([direct(1, m) for m in (1, 2)])
    go([forward(1, m) for m in (1, 2)])
    attend_row(0, heads // 2, heads)
    for m in range(3):
        work(1, m)
    end([forward(1, m) for m in (1, 2)])
    for h in range(heads):
        send_head(0, h)
    work(1, 3)
    attend_row(1, 0, heads)
    project(0)
    project(1)
    for r in range(rows):
        for m in range(4):
            end(stores(r, m))
        end(last_stores(r))


def before_feed_forward(image_index, seg, fill, conditioning, ada_bias, qv_bias, proj_bias, tokens, ada, weight, proj, cotangent):
    rows, local, width = tokens.shape
    length = 4 * local
    images, slots = conditioning.shape[0], image_index.shape[1]
    heads, size = HEADS // 4, width // HEADS
    columns = ada.shape[0]
    shape = jax.ShapeDtypeStruct
    vmem = lambda dtype, *dims: pltpu.VMEM(dims, dtype)
    near, far = pl.BlockSpec(memory_space=pltpu.VMEM), pl.BlockSpec(memory_space=pl.ANY)
    dma = lambda *dims: pltpu.SemaphoreType.DMA(dims)
    return pl.pallas_call(
        partial(forward_kernel, 512),
        in_specs=[near] * 2 + [pl.BlockSpec(memory_space=pltpu.SMEM)] + [near] * 4 + [far] * 5,
        out_specs=[far] * 10 + [near] * 5,
        out_shape=[
            shape((rows, 4, local, width), BF16),
            shape((rows, 3, heads, size, length), BF16),
            shape((rows, heads, size, length), BF16),
            shape((rows, width, local), BF16),
            shape((rows, local, width), F32),
            shape((rows, local, width), F32),
            shape((rows * local, width), BF16),
            shape((rows * local, width), BF16),
            shape((width, rows * local), BF16),
            shape((width, rows * local), BF16),
            shape((rows, slots, 6 * width), F32),
            shape((rows, 1, length), jnp.int32),
            shape((rows, length, 1), jnp.int32),
            shape((rows, heads, 1, length), F32),
            shape((1, width), F32),
        ],
        scratch_shapes=[
            vmem(BF16, rows, 4, local, width),
            vmem(BF16, rows, 4, local, width),
            vmem(BF16, rows, 3, heads, size, length),
            vmem(BF16, columns, width),
            vmem(BF16, 3, width, 384),
            vmem(F32, 384, width),
            vmem(BF16, 3 * heads * size, width),
            vmem(F32, 384, 8),
            vmem(F32, 4, images, columns),
            vmem(F32, images, 6 * width),
            vmem(jnp.int32, rows, 4, 1, local),
            vmem(BF16, rows, heads, size, length),
            vmem(BF16, rows, 4, heads, size, local),
            vmem(F32, width, local),
            vmem(BF16, rows, width, local),
            vmem(BF16, width, width),
            vmem(BF16, rows, local, width),
            vmem(F32, rows, local, width),
            vmem(F32, rows, local, width),
            vmem(BF16, rows, local, width),
            vmem(BF16, rows, local, width),
            vmem(BF16, rows, width, local),
            vmem(BF16, rows, width, local),
            vmem(F32, width, local),
            dma(6),
            dma(rows),
            dma(3),
            dma(3),
            dma(2 * rows),
            dma(2 * rows),
            dma(2 * rows),
            dma(2 * rows),
            dma(3 * rows * heads),
            dma(3 * rows * heads),
            dma(rows * heads),
            dma(2, 4 * rows),
            dma(rows, 8),
        ],
        compiler_params=pltpu.CompilerParams(vmem_limit_bytes=VMEM_LIMIT, collective_id=6, has_side_effects=True),
        cost_estimate=pl.CostEstimate(flops=2 * 10**10, bytes_accessed=4 * 10**7, transcendentals=0),
    )(image_index, seg, fill, conditioning, ada_bias, qv_bias, proj_bias, tokens, ada, weight, proj, cotangent)


def hand_out_kernel(places, *refs):
    count = len(places)
    sources, targets = refs[:count], refs[count:]
    held, sems = refs[-count - 1 : -1], refs[-1]
    loads = [pltpu.make_async_copy(sources[k], held[k], sems.at[0, k]) for k in range(count)]
    stores = []
    for k, (index, first, size) in enumerate(places):
        target = targets[index] if size is None else targets[index].at[:, pl.ds(first, size)]
        stores.append(pltpu.make_async_copy(held[k], target, sems.at[1, k]))
    for copy in loads:
        copy.start()
    for load, store in zip(loads, stores):
        load.wait()
        store.start()
    for copy in stores:
        copy.wait()


def hand_out(*results):
    arrays, places, shapes = [], [], []
    for index, result in enumerate(results):
        first = 0
        pieces = result if isinstance(result, tuple) else (result,)
        for piece in pieces:
            size = piece.shape[1] if len(pieces) > 1 else None
            arrays.append(piece)
            places.append((index, first, size))
            first += size or 0
        shape = pieces[0].shape if len(pieces) == 1 else (pieces[0].shape[0], first)
        shapes.append(jax.ShapeDtypeStruct(shape, pieces[0].dtype))
    far = pl.BlockSpec(memory_space=pl.ANY)
    return pl.pallas_call(
        partial(hand_out_kernel, tuple(places)),
        in_specs=[far] * len(arrays),
        out_specs=[far] * len(shapes),
        out_shape=shapes,
        scratch_shapes=[pltpu.VMEM(array.shape, array.dtype) for array in arrays]
        + [pltpu.SemaphoreType.DMA((2, len(arrays)))],
        compiler_params=pltpu.CompilerParams(vmem_limit_bytes=VMEM_LIMIT),
    )(*arrays)


def gather_seq(values):
    count = lax.axis_size("seq")
    if count == 4:
        first, second = swap(values, "seq", 1), swap(values, "seq", 2)
        half = values.shape[0] // 2
        third = jnp.concatenate([swap(second[:half], "seq", 1), swap(first[half:], "seq", 2)], axis=0)
        return [values, first, second, third]
    return [values] + [swap(values, "seq", m) for m in range(1, count)]


def exchange_seq(blocks):
    return [blocks[0]] + [swap(blocks[m], "seq", m) for m in range(1, len(blocks))]


def in_order(blocks, axis):
    index = lax.axis_index("seq")
    stacked = jnp.stack(blocks, axis=axis)
    return flip_blocks(stacked, axis, index)


class Halving:
    def __init__(self, blocks, low_first):
        self.blocks = dict(enumerate(blocks))
        bits = [1 << k for k in range(len(blocks).bit_length() - 1)]
        self.bits = bits if low_first else bits[::-1]

    def send(self):
        self.bit = self.bits.pop(0)
        self.kept = [m for m in self.blocks if not m & self.bit]
        return jnp.stack([self.blocks[m | self.bit] for m in self.kept]).astype(BF16)

    def move(self, sent):
        return swap(sent, "seq", self.bit)

    def add(self, came):
        self.blocks = {m: self.blocks[m] + came[k].astype(F32) for k, m in enumerate(self.kept)}


class Spreading:
    def __init__(self, pick):
        chip, chips = lax.axis_index("rows") // 2, lax.axis_size("rows") // 2
        self.own = pick(chip)
        self.sent = [pick(chip ^ m).astype(BF16) for m in range(1, chips)]

    def move(self):
        self.came = [swap(block, "rows", 2 * (m + 1)) for m, block in enumerate(self.sent)]

    def total(self):
        total = self.own
        for block in self.came:
            total = total + block.astype(F32)
        return total


def columns_of(values, index, size):
    return lax.dynamic_slice_in_dim(values, index * size, size, values.ndim - 1)


def lines_of(values, index, size):
    return lax.dynamic_slice_in_dim(values, index * size, size, 0)


def tied(*values):
    return lax.optimization_barrier(values)


def on_square(
    tokens,
    conditioning,
    segment_ids,
    image_index,
    row_fill,
    ada_weight,
    ada_bias,
    qkv_weight,
    qv_bias,
    proj_weight,
    proj_bias,
    up_weight,
    up_bias,
    down_weight,
    down_bias,
    cotangent,
):
    row_count, local_len, width = tokens.shape
    seq_count, groups = lax.axis_size("seq"), lax.axis_size("rows")
    seq_index, row_index = lax.axis_index("seq"), lax.axis_index("rows")
    chips, core = groups // 2, row_index % 2
    full_len = local_len * seq_count
    token_count = row_count * local_len
    heads_dev = HEADS // seq_count
    head_size = width // HEADS
    own = heads_dev * head_size
    image_count = conditioning.shape[0]
    hidden_size = up_weight.shape[1]
    depth = width // groups

    (
        normed_all,
        packed,
        attended,
        attended_tok,
        branch_a,
        middle,
        normed_b,
        grad_out,
        normed_turned,
        grad_turned,
        slot_mod,
        code_row,
        code_col,
        log_totals,
        part_down_bias,
    ) = before_feed_forward(
        image_index,
        segment_ids,
        row_fill,
        conditioning,
        ada_bias,
        qv_bias,
        proj_bias,
        tokens,
        ada_weight.T,
        qkv_weight,
        proj_weight,
        cotangent,
    )
    normed_all = normed_all.reshape(row_count, full_len, width)
    out_sum, grad_sum, part_up_bias, up_main, down_main, *left = feed_forward_reduce(
        normed_b, grad_out, normed_turned, grad_turned, up_weight, down_weight, up_bias
    )
    block_out, grad_middle, grad_view, slot_sums, part_proj_bias, proj_own, proj_low, up_tail, down_tail = after_feed_forward(
        segment_ids,
        slot_mod,
        attended_tok,
        proj_weight,
        down_bias,
        out_sum,
        grad_sum,
        middle,
        branch_a,
        cotangent,
        left,
    )
    grad_view = grad_view.reshape(row_count, heads_dev, head_size, full_len)
    (
        grad_tokens,
        grad_proj_weight,
        grad_down_weight,
        grad_ada_weight,
        grad_cond,
        grad_ada_bias,
        grad_qv_bias,
        grad_proj_bias,
        grad_up_bias,
        grad_down_bias,
        grad_qkv_weight,
    ) = attend_back_and_finish(
        packed,
        attended,
        grad_view,
        log_totals,
        code_col,
        code_row,
        normed_all,
        proj_own,
        proj_low,
        down_main,
        down_tail,
        segment_ids,
        slot_mod,
        slot_sums,
        image_index,
        conditioning,
        (part_proj_bias, part_up_bias, part_down_bias),
        tokens,
        grad_middle,
        qkv_weight,
        ada_weight.T,
    )
    results = list(hand_out(
        block_out,
        grad_tokens,
        grad_cond,
        grad_ada_weight,
        grad_ada_bias,
        grad_qkv_weight,
        grad_qv_bias,
        grad_proj_weight,
        grad_proj_bias,
        (up_main, up_tail),
        grad_up_bias,
        grad_down_weight,
        grad_down_bias,
    ))
    results[11] = results[11].T
    return tuple(results)


def on_device(
    tokens,
    conditioning,
    segment_ids,
    image_index,
    row_fill,
    ada_weight,
    ada_bias,
    qkv_weight,
    qv_bias,
    proj_weight,
    proj_bias,
    up_weight,
    up_bias,
    down_weight,
    down_bias,
    cotangent,
):
    row_count, local_len, width = tokens.shape
    seq_count, groups = lax.axis_size("seq"), lax.axis_size("rows")
    seq_index, row_index = lax.axis_index("seq"), lax.axis_index("rows")
    chips, core = groups // 2, row_index % 2
    full_len = local_len * seq_count
    token_count = row_count * local_len
    heads_dev = HEADS // seq_count
    head_size = width // HEADS
    own = heads_dev * head_size
    image_count = conditioning.shape[0]
    hidden_size = up_weight.shape[1]
    depth = width // groups

    tokens_all = jnp.concatenate(gather_seq(tokens), axis=1)
    order = lax.iota(jnp.int32, seq_count) ^ seq_index
    seg_blocks = flip_blocks(segment_ids.reshape(row_count, seq_count, local_len), 1, seq_index)
    seg_all = seg_blocks.reshape(row_count, full_len)
    places = (order[:, None] * local_len + lax.iota(jnp.int32, local_len)).reshape(1, full_len)
    codes = jnp.where(places < row_fill[:, None], seg_all, -1 - places)
    code_col, code_row = codes[:, :, None], codes[:, None, :]

    qkv_own = jnp.concatenate(
        [lax.dynamic_slice_in_dim(qkv_weight, part * width + seq_index * own, own, 1).T for part in range(3)], axis=0
    )
    bias_own = lax.dynamic_slice_in_dim(qv_bias.astype(F32), seq_index * own, own, 1)
    bias_own = jnp.concatenate([bias_own[0], jnp.zeros((own,), F32), bias_own[1]])

    cond_wide = conditioning.astype(F32)
    cond_low = jax.nn.silu(cond_wide).astype(BF16)
    mod_part = jnp.dot(cond_low, ada_weight, preferred_element_type=F32)
    modulation = lax.all_gather(mod_part, "seq", axis=1, tiled=True) + ada_bias.astype(F32)
    cond_cols = cond_low.reshape(image_count, groups, depth).transpose(1, 0, 2)
    local_seg = lax.dynamic_slice_in_dim(segment_ids, seq_index * local_len, local_len, 1)
    slot_ids = lax.iota(jnp.int32, image_index.shape[1])
    slot_mod = jnp.take(modulation, image_index, axis=0)

    normed_all, packed = project_qkv(
        tokens_all, seg_all, slot_mod[:, :, : 2 * width], qkv_own, bias_own, heads_dev, min(256, full_len)
    )
    square = seq_count == 4 and chips == 4
    attended, log_totals, *attended_sent = attend(packed, code_col, code_row, 512, square)

    slot_pick = (local_seg[:, :, None] == slot_ids).astype(F32)
    mod_tok = jnp.einsum("rts,rse->rte", slot_pick, slot_mod, precision=lax.Precision.HIGHEST)
    shift_a, scale_a, gate_a, shift_b, scale_b, gate_b = jnp.split(mod_tok, 6, axis=-1)
    tokens_wide = tokens.astype(F32)
    upstream = cotangent.astype(F32)
    grad_branch_b = (upstream * gate_b).astype(BF16)
    part_down_bias = jnp.sum(grad_branch_b.astype(F32), axis=(0, 1))
    grad_out = grad_branch_b.reshape(token_count, width)
    grad_turned = turn_halves(grad_out, seq_count, core)

    def by_block(values):
        return [values[..., m * local_len : (m + 1) * local_len] for m in range(seq_count)]

    if square:
        attended_tok = attended_sent[0]
    else:
        attended_tok = in_order(exchange_seq(by_block(attended.reshape(row_count, own, full_len))), 1)
    attended_tok = attended_tok.reshape(row_count, width, local_len)
    branch_a = jnp.einsum(
        "rft,fe->rte", attended_tok, proj_weight, preferred_element_type=F32
    ) + proj_bias.astype(F32)
    middle = tokens_wide + gate_a * branch_a
    normed_b = modulate(middle, shift_b, scale_b).astype(BF16).reshape(token_count, width)
    normed_turned = turn_halves(normed_b, chips, core)

    if square:
        out_sum, grad_sum, part_up_bias, grad_up_weight, down_turned = feed_forward_reduce(
            normed_b, grad_out, normed_turned, grad_turned, up_weight, down_weight, up_bias.astype(F32)
        )
        part_up_bias = part_up_bias.reshape(1, hidden_size)
    else:
        out_sum, grad_sum, up_keep, up_send, down_keep, down_send, part_up_bias = feed_forward(
            normed_b, grad_out, normed_turned, grad_turned, up_weight, down_weight, up_bias.astype(F32)[None], 512
        )
        up_came, down_came = swap(up_send, "rows", 1), swap(down_send, "rows", 1)
    branch_b = out_sum.reshape(row_count, local_len, width) + down_bias.astype(F32)
    grad_normed_b = grad_sum.reshape(row_count, local_len, width)
    block_out = (middle + gate_b * branch_b).astype(BF16)
    grad_gate_b = upstream * branch_b
    _, norm_back_b = jax.vjp(modulate, middle, shift_b, scale_b)
    grad_mid_norm, grad_shift_b, grad_scale_b = norm_back_b(grad_normed_b)
    grad_middle = upstream + grad_mid_norm
    grad_branch_a = (grad_middle * gate_a).astype(BF16)
    grad_gate_a = grad_middle * branch_a
    part_proj_bias = jnp.sum(grad_branch_a.astype(F32), axis=(0, 1))
    grad_attended = jnp.einsum(
        "fe,rte->rft", proj_weight, grad_branch_a, preferred_element_type=F32
    ).astype(BF16)
    heads_blocks = [lax.dynamic_slice_in_dim(grad_attended, (seq_index ^ m) * own, own, 1) for m in range(seq_count)]
    grad_heads_in = jnp.concatenate(exchange_seq(heads_blocks), axis=2)
    grad_view = grad_heads_in.reshape(row_count, heads_dev, head_size, full_len)

    part_proj = jnp.einsum("rte,rft->ef", grad_branch_a, attended_tok, preferred_element_type=F32)
    proj_view = part_proj.reshape(seq_count, 2, depth * groups // (2 * seq_count), width)
    proj_keep = lax.dynamic_index_in_dim(proj_view, core, 1, keepdims=False)
    proj_send = lax.dynamic_index_in_dim(proj_view, 1 - core, 1, keepdims=False).astype(BF16)
    proj_came = swap(proj_send, "rows", 1).reshape(width // 2, width)
    proj_keep = proj_keep.reshape(width // 2, width)
    up_size, down_size = hidden_size // seq_count, width // (2 * seq_count)
    proj_blocks = [
        lines_of(proj_keep, seq_index ^ m, down_size) + lines_of(proj_came, seq_index ^ m, down_size).astype(F32)
        for m in range(seq_count)
    ]
    if square:
        proj_sent = [block.astype(BF16) for block in proj_blocks[1:]]
        grad_view, *proj_sent = tied(grad_view, *proj_sent)
        proj_total = proj_blocks[0]
        for m in range(1, seq_count):
            proj_total = proj_total + swap(proj_sent[m - 1], "seq", m).astype(F32)
    else:
        ups = Halving(
            [
                columns_of(up_keep, seq_index ^ m, up_size) + columns_of(up_came, seq_index ^ m, up_size).astype(F32)
                for m in range(seq_count)
            ],
            True,
        )
        downs = Halving(
            [
                jnp.concatenate(
                    [
                        lines_of(down_keep, seq_index ^ m, down_size)
                        + lines_of(down_came, seq_index ^ m, down_size).astype(F32),
                        proj_blocks[m],
                    ],
                    axis=1,
                )
                for m in range(seq_count)
            ],
            False,
        )
        up_sent, down_sent = ups.send(), downs.send()
        up_came, down_came = ups.move(up_sent), downs.move(down_sent)

    grad_heads, *grad_sent = attend_back(
        packed, attended, grad_view, log_totals, code_col, code_row, 256, 512, square
    )
    grad_own = grad_heads.reshape(row_count, 3 * own, full_len)
    if square:
        grad_flat = grad_sent[0]
    else:
        grad_blocks = exchange_seq(by_block(grad_own))
        grad_flat = in_order([block.reshape(row_count, 3, own, local_len) for block in grad_blocks], 2)
    grad_flat = grad_flat.reshape(row_count, 3 * width, local_len)

    qkv_keep, qkv_send, own_sums = qkv_weight_grad(grad_own, normed_all)
    down_part, proj_part = hidden_size // chips, width // chips
    if square:
        proj_spread = Spreading(lambda chip: columns_of(proj_total, chip, proj_part))
        grad_flat, qkv_send, *proj_spread.sent = tied(grad_flat, qkv_send, *proj_spread.sent)
        proj_spread.move()
    else:
        while ups.bits:
            ups.add(up_came)
            downs.add(down_came)
            up_came, down_came = ups.move(ups.send()), downs.move(downs.send())
        ups.add(up_came)
        downs.add(down_came)
        up_total, down_total = ups.blocks[0], downs.blocks[0][:, :hidden_size]
        proj_total = downs.blocks[0][:, hidden_size:]
        up_spread = Spreading(lambda chip: lines_of(up_total, chip, depth))
        down_spread = Spreading(
            lambda chip: jnp.concatenate(
                [columns_of(down_total, chip, down_part), columns_of(proj_total, chip, proj_part)], axis=1
            )
        )
        up_spread.move()
        down_spread.move()
    qkv_came = swap(qkv_send, "rows", 1)
    grad_normed_a = jnp.einsum("rft,df->rtd", grad_flat, qkv_weight, preferred_element_type=F32)
    _, norm_back_a = jax.vjp(modulate, tokens_wide, shift_a, scale_a)
    grad_tok_norm, grad_shift_a, grad_scale_a = norm_back_a(grad_normed_a)
    grad_tokens = grad_middle + grad_tok_norm
    grad_mod_tok = jnp.concatenate(
        [grad_shift_a, grad_scale_a, grad_gate_a, grad_shift_b, grad_scale_b, grad_gate_b], axis=-1
    )
    slot_grads = jnp.einsum("rts,rte->rse", slot_pick, grad_mod_tok, precision=lax.Precision.HIGHEST)
    image_pick = (image_index[:, :, None] == lax.iota(jnp.int32, image_count)).astype(F32)
    grad_modulation = jnp.einsum("rsi,rse->ie", image_pick, slot_grads, precision=lax.Precision.HIGHEST)

    own_sums = own_sums.reshape(3, own)
    part_qv = lax.dynamic_update_slice(
        jnp.zeros((2, width), F32), jnp.stack([own_sums[0], own_sums[2]]), (0, seq_index * own)
    )
    small = jnp.concatenate([part_qv.reshape(-1), part_proj_bias, part_up_bias[0], part_down_bias])
    columns = ada_weight.shape[1]
    lines = -(-small.size // (seq_count * columns))
    room = seq_count * columns * lines
    small = jnp.pad(small, (0, room - small.size)).reshape(seq_count, lines, columns)
    mod_view = grad_modulation.reshape(image_count, seq_count, columns).transpose(1, 0, 2)
    joined = jnp.concatenate(
        [mod_view, jnp.zeros((seq_count, 1, columns), F32), small, jnp.zeros((seq_count, 7 - lines, columns), F32)], axis=1
    )
    qkv_both = qkv_keep + qkv_came.astype(F32)
    qkv_spread = Spreading(lambda chip: lax.dynamic_index_in_dim(qkv_both, chip, 0, keepdims=False))
    joined, *qkv_spread.sent = tied(joined, *qkv_spread.sent)
    qkv_spread.move()
    if square:
        turned = jnp.concatenate([down_turned, proj_spread.total()], axis=1)
    else:
        grad_up_weight, turned = up_spread.total(), down_spread.total()
    half = down_part // 2
    cut = lambda index: jnp.concatenate(
        [columns_of(turned[:, :down_part], index, half), columns_of(turned[:, down_part:], index, proj_part // 2)], axis=1
    )
    core_keep, core_sent = cut(core), cut(1 - core)
    joined, core_sent = tied(joined, core_sent)
    core_came = swap(core_sent, "rows", 1)
    grad_ada_weight, cond_sum, bias_sums = finish(joined, ada_weight, cond_cols, image_count)
    _, silu_back = jax.vjp(jax.nn.silu, cond_wide)
    grad_cond = silu_back(cond_sum)[0]
    grad_ada_bias = bias_sums[:, 0].reshape(-1)
    small = bias_sums[:, 1 : 1 + lines].reshape(-1)
    grad_qv_bias = small[: 2 * width].reshape(2, width)
    grad_proj_bias = small[2 * width : 3 * width]
    grad_up_bias = small[3 * width : 3 * width + hidden_size]
    grad_down_bias = small[3 * width + hidden_size : 4 * width + hidden_size]

    pair = flip_blocks(jnp.stack([core_keep, core_came]), 0, core).reshape(-1, core_keep.shape[1])
    grad_down_weight, grad_proj_weight = pair[:, :half].T, pair[:, half:].T

    qkv_total = qkv_spread.total()
    pieces = []
    for place in range(3):
        pairs = [((3 * target + place) % seq_count, target) for target in range(seq_count)]
        part_of = [0] * seq_count
        for source, target in pairs:
            part_of[source] = (3 * target + place) // seq_count
        chosen = columns_of(qkv_total, jnp.array(part_of, jnp.int32)[seq_index], own)
        pieces.append(lax.ppermute(chosen, "seq", pairs))
    grad_qkv_weight = jnp.concatenate(pieces, axis=1)
    return (
        block_out,
        grad_tokens,
        grad_cond,
        grad_ada_weight,
        grad_ada_bias,
        grad_qkv_weight,
        grad_qv_bias,
        grad_proj_weight,
        grad_proj_bias,
        grad_up_weight,
        grad_up_bias,
        grad_down_weight,
        grad_down_bias,
    )


def solution(mesh):
    in_specs = (
        P("rows", "seq", None),
        P("rows", None),
        P("rows", None),
        P("rows", None),
        P("rows"),
        P(None, "seq"),
        P(),
        P(),
        P(),
        P(),
        P(),
        P(),
        P(),
        P(),
        P(),
        P("rows", "seq", None),
    )
    out_specs = (
        P("rows", "seq", None),
        P("rows", "seq", None),
        P("rows", None),
        P("rows", "seq"),
        P(),
        P("rows", "seq"),
        P(),
        P("rows", "seq"),
        P(),
        P("rows", "seq"),
        P(),
        P("rows", "seq"),
        P(),
    )
    square = mesh.shape["seq"] == 4 and mesh.shape["rows"] == 8
    return jax.shard_map(
        on_square if square else on_device, mesh=mesh, in_specs=in_specs, out_specs=out_specs, check_vma=False
    )
```
